32 devices in a mesh: seq: 8 (over y, x, core), fsdp: 4 (over z).
Axes of the slice: x: 2, y: 2, z: 4, core: 2. Of those that a mesh axis runs over, the one named last changes fastest.
Arguments:
- tokens: bfloat16 [8, 1024, 2048], P('fsdp', 'seq'), may hold values from -6 to 6
- doc_starts: int32 [8, 4], P('fsdp'), may hold values from 0 to 1023, as said below
- w_query: bfloat16 [2048, 2048], P(('seq', 'fsdp')), may hold values from -0.1875 to 0.1875
- w_kv: bfloat16 [2048, 256], P(('seq', 'fsdp')), may hold values from -0.125 to 0.125
- w_out: bfloat16 [2048, 2048], P(('seq', 'fsdp')), may hold values from -1.5 to 1.5
- w_fc: bfloat16 [2048, 8192], P(('seq', 'fsdp')), may hold values from -0.125 to 0.125
- w_proj: bfloat16 [8192, 2048], P(('seq', 'fsdp')), may hold values from -0.0625 to 0.0625
- ln1_gain: float32 [2048], replicated, may hold values from 0.5 to 1.5
- ln1_bias: float32 [2048], replicated, may hold values from -1.2 to 1.2
- b_query: float32 [2048], replicated, may hold values from -3 to 3
- b_value: float32 [128], replicated, may hold values from -0.12 to 0.12
- b_out: float32 [2048], replicated, may hold values from -1.2 to 1.2
- ln2_gain: float32 [2048], replicated, may hold values from 0.5 to 1.5
- ln2_bias: float32 [2048], replicated, may hold values from -1.2 to 1.2
- b_fc: float32 [8192], replicated, may hold values from -3 to 3
- b_proj: float32 [2048], replicated, may hold values from -1.2 to 1.2
- cotangent: bfloat16 [8, 1024, 2048], P('fsdp', 'seq'), may hold values from -6 to 6
Outputs:
- output: float32 [8, 1024, 2048], P('fsdp', 'seq')
- input_grad: float32 [8, 1024, 2048], P('fsdp', 'seq')
- grad_w_query: float32 [2048, 2048], P(('seq', 'fsdp'))
- grad_w_kv: float32 [2048, 256], P(('seq', 'fsdp'))
- grad_w_out: float32 [2048, 2048], P(('seq', 'fsdp'))
- grad_w_fc: float32 [2048, 8192], P(('seq', 'fsdp'))
- grad_w_proj: float32 [8192, 2048], P(('seq', 'fsdp'))
- grad_ln1_gain: float32 [2048], replicated
- grad_ln1_bias: float32 [2048], replicated
- grad_b_query: float32 [2048], replicated
- grad_b_value: float32 [128], replicated
- grad_b_out: float32 [2048], replicated
- grad_ln2_gain: float32 [2048], replicated
- grad_ln2_bias: float32 [2048], replicated
- grad_b_fc: float32 [8192], replicated
- grad_b_proj: float32 [2048], replicated
The draws below stay inside these ranges and needn't reach their ends.
Inputs may be any that keep to these rules, and one draw needn't show every extreme that they name: `doc_starts`: positions at which documents of a stream start, in any order, repeats allowed; position 0 and position 1023 are always listed. Token t of stream b belongs to the document begun by the latest listed start at or before t.
All inputs are finite; a program needn't handle non-finite values.
Results may differ from the reference program's by a relative error of at most 0.02.
Values may be sent and summed in bfloat16 or wider, within the bound.
A program may use at most 384 MiB of HBM per device.

```python
import jax
import jax.numpy as jnp
from jax import lax

D = 2048
HEADS = 16
HD = 128
FF = 8192
TOK_DEV = 128
STREAMS_DEV = 2
DOCS = 4
STREAMS = 8
SEQLEN = 1024
QBLOCK = 512


def draw_doc_starts(key, part):
    key = jax.random.fold_in(key, 11)
    keys = jax.random.split(key, 8)
    first_start = jax.random.randint(keys[0], (STREAMS, 1), 1, TOK_DEV)
    last_start = jax.random.randint(keys[1], (STREAMS, 1), SEQLEN - TOK_DEV + 1, SEQLEN)
    lower_extra = jax.random.randint(keys[2], (STREAMS, DOCS - 3), 0, first_start)
    upper_extra = jax.random.randint(keys[3], (STREAMS, DOCS - 3), last_start, SEQLEN)
    side_pick = jax.random.randint(keys[4], (STREAMS, DOCS - 3), 0, 2)
    extra_starts = jnp.where(side_pick == 1, upper_extra, lower_extra)
    column = jnp.arange(DOCS - 3, dtype=jnp.int32)[None, :]
    extra_starts = jnp.where(column == 0, SEQLEN - 1, extra_starts)
    zero_start = jnp.zeros((STREAMS, 1), jnp.int32)
    spanning = jnp.concatenate([zero_start, first_start, last_start, extra_starts], axis=1)
    middle_start = jnp.clip(jax.random.randint(keys[5], (STREAMS, 1), TOK_DEV, SEQLEN - TOK_DEV), 1, SEQLEN - 2)
    free_starts = jax.random.randint(keys[6], (STREAMS, DOCS - 3), 1, SEQLEN - 1)
    final_start = jnp.full((STREAMS, 1), SEQLEN - 1, jnp.int32)
    cut = jnp.concatenate([zero_start, middle_start, final_start, free_starts], axis=1)
    pair_pick = jax.random.randint(keys[7], (STREAMS // STREAMS_DEV, 1), 0, STREAMS_DEV)
    which_one = jnp.repeat(pair_pick, STREAMS_DEV, axis=0)
    local_index = (jnp.arange(STREAMS, dtype=jnp.int32) % STREAMS_DEV)[:, None]
    return jnp.where(local_index == which_one, spanning, cut).astype(jnp.int32)


def with_spikes(values, own_key, source, target, blocks, factor):
    owner, partner = [(jnp.arange(values.shape[axis_at]) // (values.shape[axis_at] // blocks)).reshape([-1 if axis == axis_at else 1 for axis in range(values.ndim)]) for axis_at in (source, target)]
    chosen = jax.random.permutation(own_key, blocks)[partner]
    strong = (owner == chosen) | (owner == (partner + blocks // 2) % blocks)
    return jnp.where(strong, factor * values, values)


def levels(key, extent, cuts, smallest, high):
    loudness, own = 1.0, jax.random.fold_in(key, 6)
    for axis_at, blocks in cuts:
        heights = jnp.exp(jax.random.uniform(jax.random.fold_in(own, axis_at), (blocks,), jnp.float32, smallest / len(cuts), high / len(cuts)))
        loudness = loudness * jnp.repeat(heights, extent[axis_at] // blocks).reshape([-1 if axis == axis_at else 1 for axis in range(len(extent))])
    return loudness


def gaussian(own_key, extent, width, reach, cuts=(), held_as=jnp.bfloat16):
    factor_of = levels(own_key, extent, cuts, -0.22, 0.18) if cuts else 1.0
    values = jax.random.normal(own_key, extent, jnp.float32) * width * factor_of
    return jnp.minimum(jnp.maximum(values, -reach), reach).astype(held_as)


def noise_with(rng, shape, scale, most, shards, heavy, kind=jnp.bfloat16):
    values = scale * jax.random.normal(rng, shape, jnp.float32)
    if shards:
        values = values * levels(rng, shape, shards, -0.22, 0.18)
    return jnp.clip(with_spikes(values, jax.random.fold_in(rng, 3), *heavy), -most, most).astype(kind)


def setup_inputs(seed: int = 0) -> dict:
    arg_keys = jax.random.split(jax.random.key(seed), 18)
    return {
        "tokens": noise_with(arg_keys[0], (STREAMS, SEQLEN, D), 1.0, 6.0, ((0, 4), (1, 8)), (1, 2, 8, 2.0)),
        "doc_starts": draw_doc_starts(jax.random.fold_in(arg_keys[17], 71), 0),
        "w_query": gaussian(arg_keys[2], (D, D), (D // 2) ** -0.5, 0.1875, ((0, 32),)),
        "w_kv": gaussian(arg_keys[3], (D, 2 * HD), D ** -0.5, 0.125, ((0, 32),)),
        "w_out": gaussian(arg_keys[4], (D, D), (max(1, (8 * D) // SEQLEN)) ** -0.5, 1.5, ((0, 32),)),
        "w_fc": gaussian(arg_keys[5], (D, FF), D ** -0.5, 0.125, ((0, 32),)),
        "w_proj": gaussian(arg_keys[6], (FF, D), FF ** -0.5, 0.0625, ((0, 32),)),
        "ln1_gain": jnp.clip(1.0 + 0.1 * jax.random.normal(arg_keys[7], (D,), jnp.float32), 0.5, 1.5),
        "ln1_bias": gaussian(arg_keys[8], (D,), 0.2, 1.2, (), jnp.float32),
        "b_query": gaussian(arg_keys[9], (D,), 0.5, 3.0, (), jnp.float32),
        "b_value": gaussian(arg_keys[10], (HD,), 0.02, 0.12, (), jnp.float32),
        "b_out": gaussian(arg_keys[11], (D,), 0.2, 1.2, (), jnp.float32),
        "ln2_gain": jnp.clip(1.0 + 0.1 * jax.random.normal(arg_keys[12], (D,), jnp.float32), 0.5, 1.5),
        "ln2_bias": gaussian(arg_keys[13], (D,), 0.2, 1.2, (), jnp.float32),
        "b_fc": gaussian(arg_keys[14], (FF,), 0.5, 3.0, (), jnp.float32),
        "b_proj": gaussian(arg_keys[15], (D,), 0.2, 1.2, (), jnp.float32),
        "cotangent": gaussian(arg_keys[16], (STREAMS, SEQLEN, D), 1.0, 6.0, ((0, 4), (1, 8))),
    }


@jax.custom_vjp
def low(v):
    return lax.optimization_barrier(v.astype(jnp.bfloat16)).astype(jnp.float32)

@jax.custom_vjp
def low_back(v):
    return v

def low_keep(v):
    return (low(v), None)

def low_pass(kept, grad):
    return (grad,)

def back_keep(v):
    return (v, None)

def back_low(kept, grad):
    return (low(grad),)
low.defvjp(low_keep, low_pass)
low_back.defvjp(back_keep, back_low)
highest = lax.Precision.HIGHEST

def layer_norm(values, gain_row, shift_row):
    center = values - lax.optimization_barrier(jnp.mean(values, axis=-1, keepdims=True))
    variance = lax.optimization_barrier(jnp.mean(center * center, axis=-1, keepdims=True))
    return center * lax.rsqrt(variance + 1e-05) * gain_row + shift_row

def gelu_tanh(values):
    return 0.5 * values * (1.0 + jnp.tanh(0.7978845608028654 * (values + 0.044715 * values * values * values)))

def stream_forward(params, inputs, segment):
    w_query, w_kv, w_out, w_fc, w_proj, ln1_gain, ln1_bias, b_query, b_value, b_out, ln2_gain, ln2_bias, b_fc, b_proj = params
    length = inputs.shape[0]
    score_scale = HD ** (-0.5)
    hidden1 = low(layer_norm(inputs, ln1_gain, ln1_bias))
    queries = low(low_back(jnp.dot(hidden1, w_query, precision=highest) + b_query))
    value_shift = jnp.concatenate([jnp.zeros((HD,), jnp.float32), b_value])
    keyval = low(low_back(jnp.dot(hidden1, w_kv, precision=highest) + value_shift))
    key_rows = keyval[:, :HD]
    value_rows = keyval[:, HD:]
    head_queries = queries.reshape(length, HEADS, HD)
    position = jnp.arange(length, dtype=jnp.int32)

    def attend(row_start):
        query_block = lax.dynamic_slice_in_dim(head_queries, row_start, QBLOCK, 0)
        query_pos = row_start + jnp.arange(QBLOCK, dtype=jnp.int32)
        query_seg = lax.dynamic_slice_in_dim(segment, row_start, QBLOCK, 0)
        raw_scores = jnp.einsum('thd,ud->htu', query_block, key_rows, precision=highest) * score_scale
        scores = low_back(raw_scores)
        allowed = (position[None, :] <= query_pos[:, None]) & (segment[None, :] == query_seg[:, None])
        scores = jnp.where(allowed[None], scores, -1e+30)
        row_max = lax.optimization_barrier(jnp.max(scores, axis=-1, keepdims=True))
        weights = jnp.exp(scores - row_max)
        probs = weights / lax.optimization_barrier(jnp.sum(weights, axis=-1, keepdims=True))
        return jnp.einsum('htu,ud->thd', low(probs), value_rows, precision=highest)
    block_starts = jnp.arange(0, length, QBLOCK, dtype=jnp.int32)
    mixed_blocks = lax.map(jax.checkpoint(attend), block_starts)
    mixed = low(low_back(mixed_blocks.reshape(length, HEADS * HD)))
    attn_out = low_back(jnp.dot(mixed, w_out, precision=highest) + b_out)
    residual = inputs + attn_out
    hidden2 = low(layer_norm(residual, ln2_gain, ln2_bias))
    pre_act = low_back(jnp.dot(hidden2, w_fc, precision=highest) + b_fc)
    act_low = low(gelu_tanh(pre_act))
    return residual + jnp.dot(act_low, w_proj, precision=highest) + b_proj

def reference(tokens, doc_starts, w_query, w_kv, w_out, w_fc, w_proj, ln1_gain, ln1_bias, b_query, b_value, b_out, ln2_gain, ln2_bias, b_fc, b_proj, cotangent):
    params = tuple((item.astype(jnp.float32) for item in (w_query, w_kv, w_out, w_fc, w_proj, ln1_gain, ln1_bias, b_query, b_value, b_out, ln2_gain, ln2_bias, b_fc, b_proj)))
    position = jnp.arange(SEQLEN, dtype=jnp.int32)

    def one_stream(totals, stream_item):
        stream_tokens, stream_starts, stream_cot = stream_item
        segment = lax.optimization_barrier(jnp.sum((stream_starts[None, :] <= position[:, None]).astype(jnp.int32), axis=1)).astype(jnp.int32)
        inputs = stream_tokens.astype(jnp.float32)
        result, pullback = jax.vjp(lambda prm, inp: stream_forward(prm, inp, segment), params, inputs)
        grad_params, grad_inputs = pullback(stream_cot.astype(jnp.float32))
        totals = jax.tree.map(jnp.add, totals, grad_params)
        return (totals, (result, grad_inputs))
    zero_totals = jax.tree.map(jnp.zeros_like, params)
    totals, (output, input_grad) = lax.scan(one_stream, zero_totals, (tokens, doc_starts, cotangent))
    return (output, input_grad, totals[0], totals[1], totals[2], totals[3], totals[4], totals[5], totals[6], totals[7], totals[8], totals[9], totals[10], totals[11], totals[12], totals[13])
```

```python
import jax
import jax.numpy as jnp
from jax import lax
from jax.sharding import PartitionSpec as P

HEADS = 16
HD = 128

root_two_pi = 0.7978845608028654
cubic_coef = 0.044715
epsilon = 1e-05
f32 = jnp.float32
bf16 = jnp.bfloat16


def normalize(values, gain_row, shift_row):
    center = values - jnp.mean(values, axis=-1, keepdims=True)
    inverse = lax.rsqrt(jnp.mean(center * center, axis=-1, keepdims=True) + epsilon)
    normed = center * inverse
    return (normed * gain_row + shift_row, normed, inverse)


def normalize_back(grad_out, normed, inverse, gain_row):
    scaled = grad_out * gain_row
    grad_in = inverse * (
        scaled
        - jnp.mean(scaled, axis=-1, keepdims=True)
        - normed * jnp.mean(scaled * normed, axis=-1, keepdims=True)
    )
    return (grad_in, jnp.sum(grad_out * normed, axis=0), jnp.sum(grad_out, axis=0))


def gelu_pair(inputs):
    tangent = jnp.tanh(root_two_pi * (inputs + cubic_coef * inputs * inputs * inputs))
    activated = 0.5 * inputs * (1.0 + tangent)
    gradient_slope = 0.5 * (1.0 + tangent) + 0.5 * inputs * (
        1.0 - tangent * tangent
    ) * root_two_pi * (1.0 + 3.0 * cubic_coef * inputs * inputs)
    return (activated, gradient_slope)


def dot(a, b):
    return jnp.dot(a, b, preferred_element_type=f32)


def dot_nt(a, b):
    return lax.dot_general(a, b, (((1,), (1,)), ((), ())), preferred_element_type=f32)


def dot_tn(a, b):
    return lax.dot_general(a, b, (((0,), (0,)), ((), ())), preferred_element_type=f32)


def gather_seq(block):
    return lax.all_gather(block, "seq", axis=0, tiled=True)


def scatter_seq(partial):
    return lax.psum_scatter(partial.astype(bf16), "seq", scatter_dimension=0, tiled=True).astype(f32)


def columns_to_rows(part, groups):
    rows = part.shape[0]
    spread = part.reshape(rows, groups, part.shape[1] // groups).transpose(1, 0, 2)
    return lax.all_to_all(spread, "seq", split_axis=0, concat_axis=0, tiled=True)


def column_weight(shard, groups):
    pieces = columns_to_rows(shard, groups)
    full = lax.all_gather(pieces, "fsdp", axis=1, tiled=True)
    return full.reshape(-1, full.shape[2])


def column_weight_grad(grad, groups):
    rows, cols = grad.shape
    kept = lax.psum_scatter(
        grad.astype(bf16).reshape(groups, rows // groups, cols), "fsdp", scatter_dimension=1, tiled=True
    )
    moved = lax.all_to_all(kept, "seq", split_axis=0, concat_axis=0, tiled=True)
    return moved.transpose(1, 0, 2).reshape(moved.shape[1], groups * cols).astype(f32)


def row_weight_grad(grad):
    return lax.psum_scatter(grad.astype(bf16), "fsdp", scatter_dimension=0, tiled=True).astype(f32)


def attend(queries, keyval, starts, groups, streams, rows, heads):
    length = groups * rows
    scale = HD ** (-0.5)
    position = jnp.arange(length, dtype=jnp.int32)
    mixed_list, lse_list = [], []
    for stream in range(streams):
        q = queries[:, stream].reshape(length, heads, HD)
        k = keyval[:, stream, :, :HD].reshape(length, HD)
        v = keyval[:, stream, :, HD:].reshape(length, HD)
        segment = jnp.sum((starts[stream][None, :] <= position[:, None]).astype(jnp.int32), axis=1)
        allowed = (position[None, :] <= position[:, None]) & (segment[None, :] == segment[:, None])
        scores = jnp.einsum("thd,ud->htu", q, k, preferred_element_type=f32) * scale
        scores = jnp.where(allowed[None], scores, -1e30)
        top = jnp.max(scores, axis=-1, keepdims=True)
        lse = top + jnp.log(jnp.sum(jnp.exp(scores - top), axis=-1, keepdims=True))
        probs = jnp.exp(scores - lse).astype(bf16)
        mixed = jnp.einsum("htu,ud->thd", probs, v, preferred_element_type=f32)
        mixed_list.append(mixed.astype(bf16).reshape(groups, rows, heads * HD))
        lse_list.append(lse)
    return jnp.stack(mixed_list, axis=1), lse_list


def attend_back(queries, keyval, grads, lse_list, starts, groups, streams, rows, heads):
    length = groups * rows
    scale = HD ** (-0.5)
    position = jnp.arange(length, dtype=jnp.int32)
    gq_list, gkv_list = [], []
    for stream in range(streams):
        q = queries[:, stream].reshape(length, heads, HD)
        g = grads[:, stream].reshape(length, heads, HD)
        k = keyval[:, stream, :, :HD].reshape(length, HD)
        v = keyval[:, stream, :, HD:].reshape(length, HD)
        segment = jnp.sum((starts[stream][None, :] <= position[:, None]).astype(jnp.int32), axis=1)
        allowed = (position[None, :] <= position[:, None]) & (segment[None, :] == segment[:, None])
        scores = jnp.einsum("thd,ud->htu", q, k, preferred_element_type=f32) * scale
        probs = jnp.exp(jnp.where(allowed[None], scores, -1e30) - lse_list[stream])
        grad_probs = jnp.einsum("thd,ud->htu", g, v, preferred_element_type=f32)
        delta = jnp.sum(probs * grad_probs, axis=-1, keepdims=True)
        gs = (probs * (grad_probs - delta)).astype(bf16)
        gq = jnp.einsum("htu,ud->thd", gs, k, preferred_element_type=f32) * scale
        gk = jnp.einsum("htu,thd->ud", gs, q, preferred_element_type=f32) * scale
        gv = jnp.einsum("htu,thd->ud", probs.astype(bf16), g, preferred_element_type=f32)
        gq_list.append(gq.astype(bf16).reshape(groups, rows, heads * HD))
        gkv_list.append(jnp.concatenate([gk, gv], axis=1).reshape(groups, rows, 2 * HD))
    return jnp.stack(gq_list, axis=1), jnp.stack(gkv_list, axis=1)


def shards(
    tokens,
    doc_starts,
    w_query,
    w_kv,
    w_out,
    w_fc,
    w_proj,
    ln1_gain,
    ln1_bias,
    b_query,
    b_value,
    b_out,
    ln2_gain,
    ln2_bias,
    b_fc,
    b_proj,
    cotangent,
):
    groups = lax.axis_size("seq")
    me = lax.axis_index("seq")
    streams, rows, width = tokens.shape
    own = streams * rows
    heads = HEADS // groups
    hidden = b_fc.shape[0]
    my_cols = heads * HD
    my_hidden = hidden // groups

    wq = column_weight(w_query, groups)
    w_kv_all = gather_seq(lax.all_gather(w_kv, "fsdp", axis=0, tiled=True))
    wo = lax.all_gather(w_out, "fsdp", axis=0, tiled=True)
    wf = column_weight(w_fc, groups)
    wp = lax.all_gather(w_proj, "fsdp", axis=0, tiled=True)
    my_bq = lax.dynamic_slice_in_dim(b_query, me * my_cols, my_cols, 0)
    my_bf = lax.dynamic_slice_in_dim(b_fc, me * my_hidden, my_hidden, 0)

    inputs = tokens.reshape(own, width).astype(f32)
    cot_low = cotangent.reshape(own, width)
    cot_full = cot_low.astype(f32)
    shifted1, normed1, inverse1 = normalize(inputs, ln1_gain, ln1_bias)
    hidden1 = gather_seq(shifted1.astype(bf16))
    queries = (dot(hidden1, wq) + my_bq).astype(bf16).reshape(groups, streams, rows, my_cols)
    value_shift = jnp.concatenate([jnp.zeros((HD,), f32), b_value])
    keyval = (dot(hidden1, w_kv_all) + value_shift).astype(bf16).reshape(groups, streams, rows, 2 * HD)
    mixed, lse = attend(queries, keyval, doc_starts, groups, streams, rows, heads)
    mixed_rows = mixed.reshape(groups * own, my_cols)
    residual = inputs + scatter_seq(dot(mixed_rows, wo)) + b_out
    shifted2, normed2, inverse2 = normalize(residual, ln2_gain, ln2_bias)
    hidden2 = gather_seq(shifted2.astype(bf16))
    cot_all = gather_seq(cot_low)
    pre_act = dot(hidden2, wf) + my_bf
    activated, slope = gelu_pair(pre_act)
    act_low = activated.astype(bf16)
    output = residual + scatter_seq(dot(act_low, wp)) + b_proj

    grad_b_proj = jnp.sum(cot_full, axis=0)
    shard_proj = row_weight_grad(dot_tn(act_low, cot_all))
    grad_pre = (dot_nt(cot_all, wp) * slope).astype(bf16)
    my_grad_b_fc = jnp.sum(grad_pre.astype(f32), axis=0)
    shard_fc = column_weight_grad(dot_tn(hidden2, grad_pre), groups)
    grad_hidden2 = scatter_seq(dot_nt(grad_pre, wf))
    back_second, grad_ln2_gain, grad_ln2_bias = normalize_back(
        grad_hidden2, normed2, inverse2, ln2_gain
    )
    grad_residual = cot_full + back_second
    grad_attn = grad_residual.astype(bf16)
    grad_b_out = jnp.sum(grad_attn.astype(f32), axis=0)
    grad_attn_all = gather_seq(grad_attn)
    shard_out = row_weight_grad(dot_tn(mixed_rows, grad_attn_all))
    grad_mixed = dot_nt(grad_attn_all, wo).astype(bf16).reshape(groups, streams, rows, my_cols)
    gq, gkv = attend_back(
        queries, keyval, grad_mixed, lse, doc_starts, groups, streams, rows, heads
    )
    gq_rows = gq.reshape(groups * own, my_cols)
    gkv_rows = gkv.reshape(groups * own, 2 * HD)
    my_grad_b_query = jnp.sum(gq_rows.astype(f32), axis=0)
    grad_b_value = jnp.sum(gkv_rows[:, HD:], axis=0)
    gkv_low = gkv_rows.astype(bf16)
    shard_query = column_weight_grad(dot_tn(hidden1, gq_rows), groups)
    shard_kv = row_weight_grad(scatter_seq(dot_tn(hidden1, gkv_low)))
    grad_hidden1 = scatter_seq(dot_nt(gq_rows, wq) + dot_nt(gkv_low, w_kv_all))
    back_first, grad_ln1_gain, grad_ln1_bias = normalize_back(
        grad_hidden1, normed1, inverse1, ln1_gain
    )
    input_grad = grad_residual + back_first

    zero = jnp.zeros_like
    grad_b_query = lax.dynamic_update_slice_in_dim(zero(b_query), my_grad_b_query, me * my_cols, 0)
    grad_b_fc = lax.dynamic_update_slice_in_dim(zero(b_fc), my_grad_b_fc, me * my_hidden, 0)
    vectors = (
        grad_ln1_gain,
        grad_ln1_bias,
        grad_b_query,
        grad_b_value,
        grad_b_out,
        grad_ln2_gain,
        grad_ln2_bias,
        grad_b_fc,
        grad_b_proj,
    )
    sums = lax.psum(vectors, ("seq", "fsdp"))
    return (
        output.reshape(streams, rows, width),
        input_grad.reshape(streams, rows, width),
        shard_query,
        shard_kv,
        shard_out,
        shard_fc,
        shard_proj,
        *sums,
    )


def solution(mesh):
    acts = P("fsdp", "seq", None)
    weight = P(("seq", "fsdp"), None)
    return jax.shard_map(
        shards,
        mesh=mesh,
        in_specs=(acts, P("fsdp", None)) + (weight,) * 5 + (P(),) * 9 + (acts,),
        out_specs=(acts, acts) + (weight,) * 5 + (P(),) * 9,
        check_vma=False,
    )
```

```python
import functools

import jax
import jax.numpy as jnp
from jax import lax
from jax.experimental import pallas as pl
from jax.experimental.pallas import tpu as pltpu
from jax.sharding import PartitionSpec as P

HEADS = 16
HD = 128

root_two_pi = 0.7978845608028654
cubic_coef = 0.044715
epsilon = 1e-05
f32 = jnp.float32
bf16 = jnp.bfloat16
MESH = pl.DeviceIdType.MESH
ANY = pl.BlockSpec(memory_space=pl.ANY)
WHOLE = pl.BlockSpec(memory_space=pltpu.VMEM)
VMEM_LIMIT = 56 * 1024 * 1024
PLANE = 8


def normalize(values, gain_row, shift_row):
    center = values - jnp.mean(values, axis=-1, keepdims=True)
    inverse = lax.rsqrt(jnp.mean(center * center, axis=-1, keepdims=True) + epsilon)
    normed = center * inverse
    return (normed * gain_row + shift_row, normed, inverse)


def normalize_back(grad_out, normed, inverse, gain_row):
    scaled = grad_out * gain_row
    grad_in = inverse * (
        scaled
        - jnp.mean(scaled, axis=-1, keepdims=True)
        - normed * jnp.mean(scaled * normed, axis=-1, keepdims=True)
    )
    return (grad_in, jnp.sum(grad_out * normed, axis=0), jnp.sum(grad_out, axis=0))


def gelu_pair(inputs):
    tangent = jnp.tanh(root_two_pi * (inputs + cubic_coef * inputs * inputs * inputs))
    activated = 0.5 * inputs * (1.0 + tangent)
    gradient_slope = 0.5 * (1.0 + tangent) + 0.5 * inputs * (
        1.0 - tangent * tangent
    ) * root_two_pi * (1.0 + 3.0 * cubic_coef * inputs * inputs)
    return (activated, gradient_slope)


def dot(a, b):
    return jnp.dot(a, b, preferred_element_type=f32)


def dot_nt(a, b):
    return lax.dot_general(a, b, (((1,), (1,)), ((), ())), preferred_element_type=f32)


def dot_tn(a, b):
    return lax.dot_general(a, b, (((0,), (0,)), ((), ())), preferred_element_type=f32)


def push(src, dst, send, recv, to):
    return pltpu.make_async_remote_copy(
        src_ref=src, dst_ref=dst, send_sem=send, recv_sem=recv, device_id=to, device_id_type=MESH
    )


class Place:
    def __init__(self):
        me = lax.axis_index("seq")
        self.me = me
        self.core = lax.rem(me, 2)
        x = lax.rem(lax.div(me, 2), 2)
        y = lax.div(me, 4)
        self.sib = me + 1 - 2 * self.core
        self.xn = me + 2 - 4 * x
        self.yn = me + 4 - 8 * y
        self.dg = me + 2 - 4 * x + 4 - 8 * y
        turn = 1 - 2 * self.core
        self.xs, self.ys, self.ds = self.xn + turn, self.yn + turn, self.dg + turn

    def greet(self):
        barrier = pltpu.get_barrier_semaphore()
        for other in (self.sib, self.xn, self.yn):
            pl.semaphore_signal(barrier, inc=1, device_id={"seq": other}, device_id_type=MESH)
        pl.semaphore_wait(barrier, 3)


class Gather:
    sends = 14

    def __init__(self, place, buf, rows, send, recv):
        self.p, self.buf, self.rows, self.half = place, buf, rows, rows // 2
        self.send_sem, self.recv_sem = send, recv
        self.copies = []

    def piece(self, dev, half):
        start = pl.multiple_of(dev * self.rows + half * self.half, self.half)
        return self.buf.at[pl.ds(start, self.half), :]

    def pair(self, dev):
        start = pl.multiple_of(lax.div(dev, 2) * (2 * self.rows), 2 * self.rows)
        return pl.ds(start, 2 * self.rows)

    def send(self, dev, half, to, src=None):
        k = len(self.copies)
        piece = self.piece(dev, half)
        copy = push(
            piece if src is None else src,
            piece,
            self.send_sem.at[k],
            self.recv_sem.at[dev, half],
            {"seq": to},
        )
        copy.start()
        self.copies.append(copy)

    def arrived(self, dev, half):
        piece = self.piece(dev, half)
        push(
            piece, piece, self.send_sem.at[0], self.recv_sem.at[dev, half], {"seq": self.p.sib}
        ).wait_recv()

    def start(self, own):
        p = self.p
        parts = [own.at[pl.ds(h * self.half, self.half), :] for h in range(2)]
        self.send(p.me, 0, p.yn, parts[0])
        self.send(p.me, 1, p.xn, parts[1])
        self.send(p.me, 1, p.yn, parts[1])
        self.send(p.me, 0, p.xn, parts[0])
        for h in range(2):
            self.send(p.me, h, p.sib, parts[h])

    def relay(self):
        p = self.p
        self.arrived(p.yn, 0)
        self.send(p.yn, 0, p.xn)
        self.arrived(p.xn, 1)
        self.send(p.xn, 1, p.yn)
        self.send(p.yn, 0, p.sib)
        self.send(p.xn, 1, p.sib)
        self.arrived(p.xn, 0)
        self.send(p.xn, 0, p.sib)
        self.arrived(p.yn, 1)
        self.send(p.yn, 1, p.sib)

    def have(self, dev):
        self.arrived(dev, 0)
        self.arrived(dev, 1)

    def relay_corner(self):
        p = self.p
        for h in range(2):
            self.arrived(p.dg, h)
            self.send(p.dg, h, p.sib)

    def finish(self):
        for copy in self.copies:
            copy.wait_send()


def gather_sems():
    return [pltpu.SemaphoreType.DMA((Gather.sends,)), pltpu.SemaphoreType.DMA((PLANE, 2))]


def gather_plane(blocks, number):
    count = len(blocks)

    def kernel(*refs):
        ins, outs = refs[:count], refs[count : 2 * count]
        sems = refs[2 * count :]
        p = Place()
        locals_ = []
        for i in range(count):
            rows = ins[i].shape[0]
            start = pl.multiple_of(p.me * rows, rows)
            copy = pltpu.make_async_copy(
                ins[i], outs[i].at[pl.ds(start, rows), :], sems[2 * count].at[i]
            )
            copy.start()
            locals_.append(copy)
        p.greet()
        gathers = [
            Gather(p, outs[i], ins[i].shape[0], sems[2 * i], sems[2 * i + 1]) for i in range(count)
        ]
        gathers[0].start(ins[0])
        for i in range(count):
            if i + 1 < count:
                gathers[i + 1].start(ins[i + 1])
            gathers[i].relay()
        for i in range(count):
            gathers[i].relay_corner()
        for i in range(count):
            for dev in (p.sib, p.xs, p.ys, p.ds):
                gathers[i].have(dev)
            gathers[i].finish()
            locals_[i].wait()

    scratch = []
    for _ in blocks:
        scratch += gather_sems()
    scratch.append(pltpu.SemaphoreType.DMA((count,)))
    return pl.pallas_call(
        kernel,
        out_shape=[
            jax.ShapeDtypeStruct((PLANE * b.shape[0], b.shape[1]), b.dtype) for b in blocks
        ],
        in_specs=[ANY] * count,
        out_specs=[ANY] * count,
        scratch_shapes=scratch,
        compiler_params=pltpu.CompilerParams(collective_id=number, has_side_effects=True),
        name="gather_plane",
    )(*blocks)


def gather_matmul(own, weight, extras, outs, epilogue, number, nt=False, name="gather_matmul"):
    rows, depth = own.shape
    wide = weight.shape[0] if nt else weight.shape[1]
    tile = 256
    n_ex, n_out = len(extras), len(outs)

    def kernel(own_ref, w_ref, *refs):
        ex = refs[:n_ex]
        all_ref = refs[n_ex]
        out_refs = refs[n_ex + 1 : n_ex + 1 + n_out]
        buf, w_buf = refs[n_ex + 1 + n_out : n_ex + 3 + n_out]
        stage = refs[n_ex + 3 + n_out : n_ex + 3 + 2 * n_out]
        send, recv, local = refs[n_ex + 3 + 2 * n_out :]
        p = Place()
        mine = pl.ds(pl.multiple_of(p.me * rows, rows), rows)
        load_own = pltpu.make_async_copy(own_ref, buf.at[mine, :], local.at[0])
        load_w = pltpu.make_async_copy(w_ref, w_buf, local.at[1])
        load_own.start()
        load_w.start()
        p.greet()
        g = Gather(p, buf, rows, send, recv)
        g.start(own_ref)
        stores = []

        def work(dev, k):
            block = g.pair(dev)
            copy = pltpu.make_async_copy(
                buf.at[block, :], all_ref.at[block, :], local.at[2 + k * (1 + n_out)]
            )
            copy.start()
            stores.append(copy)

            @pl.loop(0, wide // tile)
            def _(j):
                cols = pl.ds(pl.multiple_of(j * tile, tile), tile)
                if nt:
                    acc = dot_nt(buf[block, :], w_buf[cols, :])
                else:
                    acc = dot(buf[block, :], w_buf[:, cols])
                for ref, value in zip(stage, epilogue(acc, cols, ex)):
                    ref[block, cols] = value.astype(ref.dtype)

            for i in range(n_out):
                copy = pltpu.make_async_copy(
                    stage[i].at[block, :],
                    out_refs[i].at[block, :],
                    local.at[2 + k * (1 + n_out) + 1 + i],
                )
                copy.start()
                stores.append(copy)

        load_own.wait()
        load_w.wait()
        g.have(p.sib)
        work(p.me, 0)
        g.relay()
        g.have(p.xs)
        work(p.xn, 1)
        g.have(p.ys)
        work(p.yn, 2)
        g.relay_corner()
        g.have(p.ds)
        work(p.dg, 3)
        g.finish()
        for copy in stores:
            copy.wait()

    total = PLANE * rows
    return pl.pallas_call(
        kernel,
        out_shape=[jax.ShapeDtypeStruct((total, depth), own.dtype)]
        + [jax.ShapeDtypeStruct((total, wide), t) for t in outs],
        in_specs=[ANY, ANY] + [WHOLE] * n_ex,
        out_specs=[ANY] * (1 + n_out),
        scratch_shapes=[
            pltpu.VMEM((total, depth), own.dtype),
            pltpu.VMEM(weight.shape, weight.dtype),
        ]
        + [pltpu.VMEM((total, wide), t) for t in outs]
        + gather_sems()
        + [pltpu.SemaphoreType.DMA((2 + 4 * (1 + n_out),))],
        compiler_params=pltpu.CompilerParams(
            collective_id=number, has_side_effects=True, vmem_limit_bytes=VMEM_LIMIT
        ),
        cost_estimate=pl.CostEstimate(
            flops=2 * total * depth * wide, bytes_accessed=40 * 1024 * 1024, transcendentals=0
        ),
        name=name,
    )(own, weight, *extras)


def matmul_scatter(pairs, number, name="matmul_scatter"):
    count = len(pairs)
    total = pairs[0][0].shape[0]
    rows = total // PLANE
    half = rows // 2
    wide = pairs[0][1].shape[0] if pairs[0][2] else pairs[0][1].shape[1]
    tile = 512
    lines = 32

    def kernel(*refs):
        a_refs, w_refs = refs[:count], refs[count : 2 * count]
        out_ref = refs[2 * count]
        a_bufs = refs[2 * count + 1 : 3 * count + 1]
        w_bufs = refs[3 * count + 1 : 4 * count + 1]
        part, sib_out, sib_in, out_d, out_x, out_y, in_d, in_x, in_y = refs[
            4 * count + 1 : 4 * count + 10
        ]
        sib_send, sib_recv, send, recv, local = refs[4 * count + 10 :]
        p = Place()
        loads = []
        for i in range(count):
            for k, (src, dst) in enumerate(((a_refs[i], a_bufs[i]), (w_refs[i], w_bufs[i]))):
                copy = pltpu.make_async_copy(src, dst, local.at[2 * i + k])
                copy.start()
                loads.append(copy)
        p.greet()
        for copy in loads:
            copy.wait()
        copies = []

        def product(role, dev):
            chip = lax.div(dev, 2) * (2 * rows)
            theirs = pl.ds(pl.multiple_of(chip + (1 - p.core) * rows, rows), rows)
            ours = pl.ds(pl.multiple_of(chip + p.core * rows, rows), rows)

            @pl.loop(0, wide // tile)
            def _(j):
                cols = pl.ds(pl.multiple_of(j * tile, tile), tile)

                def sum_of(where):
                    acc = None
                    for i in range(count):
                        if pairs[i][2]:
                            term = dot_nt(a_bufs[i][where, :], w_bufs[i][cols, :])
                        else:
                            term = dot(a_bufs[i][where, :], w_bufs[i][:, cols])
                        acc = term if acc is None else acc + term
                    return acc

                sib_out[role, :, cols] = sum_of(theirs).astype(bf16)
                part[role, :, cols] = sum_of(ours)

            copy = push(
                sib_out.at[role],
                sib_in.at[role],
                sib_send.at[role],
                sib_recv.at[role],
                {"seq": p.sib},
            )
            copy.start()
            copies.append(copy)
            return copy

        def add_into(dst, role, first, size, more=()):
            @pl.loop(0, size // lines)
            def _(i):
                line = pl.ds(pl.multiple_of(first + i * lines, lines), lines)
                value = part[role, line, :] + sib_in[role, line, :].astype(f32)
                for ref in more:
                    value = value + ref[line, :].astype(f32)
                dst[line, :] = value.astype(dst.dtype)

        def ship(src, dst, h, k, to):
            part_rows = pl.ds(h * half, half)
            copy = push(
                src.at[part_rows, :], dst.at[part_rows, :], send.at[k], recv.at[k], {"seq": to}
            )
            copy.start()
            copies.append(copy)
            return copy

        to_d = product(0, p.dg)
        to_x = product(1, p.xn)
        to_d.wait_recv()
        add_into(out_d, 0, 0, rows)
        dx = ship(out_d, in_d, 0, 0, p.xn)
        dy = ship(out_d, in_d, 1, 1, p.yn)
        to_y = product(2, p.yn)
        to_x.wait_recv()
        add_into(out_x, 1, 0, half)
        x0 = ship(out_x, in_x, 0, 2, p.xn)
        to_y.wait_recv()
        add_into(out_y, 2, half, half)
        y1 = ship(out_y, in_y, 1, 3, p.yn)
        to_me = product(3, p.me)
        dy.wait_recv()
        add_into(out_x, 1, half, half, (in_d,))
        x1 = ship(out_x, in_x, 1, 4, p.xn)
        dx.wait_recv()
        add_into(out_y, 2, 0, half, (in_d,))
        y0 = ship(out_y, in_y, 0, 5, p.yn)
        to_me.wait_recv()
        x0.wait_recv()
        y0.wait_recv()
        add_into(out_ref, 3, 0, half, (in_x, in_y))
        y1.wait_recv()
        x1.wait_recv()
        add_into(out_ref, 3, half, half, (in_x, in_y))
        for copy in copies:
            copy.wait_send()

    flops = sum(2 * total * a.shape[1] * wide for a, _, _ in pairs)
    return pl.pallas_call(
        kernel,
        out_shape=jax.ShapeDtypeStruct((rows, wide), f32),
        in_specs=[ANY] * (2 * count),
        out_specs=WHOLE,
        scratch_shapes=[pltpu.VMEM(a.shape, a.dtype) for a, _, _ in pairs]
        + [pltpu.VMEM(w.shape, w.dtype) for _, w, _ in pairs]
        + [pltpu.VMEM((4, rows, wide), f32)]
        + [pltpu.VMEM((4, rows, wide), bf16)] * 2
        + [pltpu.VMEM((rows, wide), bf16)] * 6
        + [pltpu.SemaphoreType.DMA((4,))] * 2
        + [pltpu.SemaphoreType.DMA((6,))] * 2
        + [pltpu.SemaphoreType.DMA((2 * count,))],
        compiler_params=pltpu.CompilerParams(
            collective_id=number, has_side_effects=True, vmem_limit_bytes=VMEM_LIMIT
        ),
        cost_estimate=pl.CostEstimate(
            flops=flops, bytes_accessed=40 * 1024 * 1024, transcendentals=0
        ),
        name=name,
    )(*[a for a, _, _ in pairs], *[w for _, w, _ in pairs])


def greet_all(groups, layers):
    me, layer = lax.axis_index("seq"), lax.axis_index("fsdp")
    barrier = pltpu.get_barrier_semaphore()
    for step in range(1, groups):
        other = lax.rem(me + step, groups)
        pl.semaphore_signal(barrier, inc=1, device_id={"seq": other}, device_id_type=MESH)
    for step in range(1, layers):
        other = lax.rem(layer + step, layers)
        pl.semaphore_signal(barrier, inc=1, device_id={"fsdp": other}, device_id_type=MESH)
    pl.semaphore_wait(barrier, groups - 1 + layers - 1)


def split_columns(arrays, groups, number):
    count = len(arrays)

    def kernel(*refs):
        ins, outs = refs[:count], refs[count : 2 * count]
        send, recv, local = refs[2 * count :]
        me = lax.axis_index("seq")
        greet_all(groups, 1)
        copies, own = [], []
        for i in range(count):
            cols = ins[i].shape[1] // groups

            def block(dev, i=i, cols=cols):
                return ins[i].at[:, pl.ds(pl.multiple_of(dev * cols, cols), cols)]

            copy = pltpu.make_async_copy(block(me), outs[i].at[me], local.at[i])
            copy.start()
            own.append(copy)
            for step in range(1, groups):
                to = lax.rem(me + step, groups)
                copy = push(
                    block(to), outs[i].at[me], send.at[i, step], recv.at[i, step], {"seq": to}
                )
                copy.start()
                copies.append(copy)
        for copy in own:
            copy.wait()
        for copy in copies:
            copy.wait()

    return pl.pallas_call(
        kernel,
        out_shape=[
            jax.ShapeDtypeStruct((groups, a.shape[0], a.shape[1] // groups), a.dtype)
            for a in arrays
        ],
        in_specs=[ANY] * count,
        out_specs=[ANY] * count,
        scratch_shapes=[
            pltpu.SemaphoreType.DMA((count, groups)),
            pltpu.SemaphoreType.DMA((count, groups)),
            pltpu.SemaphoreType.DMA((count,)),
        ],
        compiler_params=pltpu.CompilerParams(collective_id=number, has_side_effects=True),
        name="split_columns",
    )(*arrays)


def last_exchange(vector, arrays, groups, layers, number):
    count = len(arrays)
    lines = vector.shape[1]

    def kernel(vec, *refs):
        ins = refs[:count]
        vec_out = refs[count]
        outs = refs[count + 1 : 2 * count + 1]
        box, plane_sum, zbox, vsend, vrecv, zsend, zrecv, gsend, grecv, send, recv, local = refs[
            2 * count + 1 :
        ]
        me, layer = lax.axis_index("seq"), lax.axis_index("fsdp")
        greet_all(groups, layers)
        first, copies, own = [], [], []
        for step in range(1, groups):
            to = lax.rem(me + step, groups)
            copy = push(vec.at[to], box.at[step], vsend.at[step], vrecv.at[step], {"seq": to})
            copy.start()
            first.append(copy)
        for i in range(count):
            cols = ins[i].shape[2]
            place = pl.ds(pl.multiple_of(me * cols, cols), cols)
            copy = pltpu.make_async_copy(ins[i].at[me], outs[i].at[:, place], local.at[i])
            copy.start()
            own.append(copy)
            for step in range(1, groups):
                to = lax.rem(me + step, groups)
                copy = push(
                    ins[i].at[to],
                    outs[i].at[:, place],
                    send.at[i, step],
                    recv.at[i, step],
                    {"seq": to},
                )
                copy.start()
                copies.append(copy)
        total = vec[me]
        for step in range(1, groups):
            first[step - 1].wait_recv()
            total = total + box[step]
        plane_sum[...] = total
        across = []
        for step in range(1, layers):
            to = lax.rem(layer + step, layers)
            copy = push(plane_sum, zbox.at[step], zsend.at[step], zrecv.at[step], {"fsdp": to})
            copy.start()
            across.append(copy)
        for step in range(1, layers):
            across[step - 1].wait_recv()
        zbox[0] = total
        total = None
        for k in range(layers):
            term = zbox[lax.rem(k - layer + layers, layers)]
            total = term if total is None else total + term
        vec_out[me] = total
        for copy in across:
            copy.wait_send()
        last = []
        for step in range(1, groups):
            to = lax.rem(me + step, groups)
            copy = push(
                vec_out.at[me], vec_out.at[me], gsend.at[step], grecv.at[step], {"seq": to}
            )
            copy.start()
            last.append(copy)
        for copy in last:
            copy.wait()
        for copy in first:
            copy.wait_send()
        for copy in own + copies:
            copy.wait()

    sem = pltpu.SemaphoreType.DMA
    return pl.pallas_call(
        kernel,
        out_shape=[jax.ShapeDtypeStruct(vector.shape, f32)]
        + [
            jax.ShapeDtypeStruct((a.shape[1], groups * a.shape[2]), a.dtype) for a in arrays
        ],
        in_specs=[WHOLE] + [ANY] * count,
        out_specs=[WHOLE] + [ANY] * count,
        scratch_shapes=[
            pltpu.VMEM((groups, lines, 128), f32),
            pltpu.VMEM((lines, 128), f32),
            pltpu.VMEM((layers, lines, 128), f32),
            sem((groups,)),
            sem((groups,)),
            sem((layers,)),
            sem((layers,)),
            sem((groups,)),
            sem((groups,)),
            sem((max(count, 1), groups)),
            sem((max(count, 1), groups)),
            sem((max(count, 1),)),
        ],
        compiler_params=pltpu.CompilerParams(collective_id=number, has_side_effects=True),
        name="last_exchange",
    )(vector, *arrays)


def starts_of(docs, stream, positions):
    start = jnp.zeros_like(positions)
    for j in range(docs.shape[1]):
        here = docs[stream, j]
        start = jnp.maximum(start, jnp.where(here <= positions, here, 0))
    return start


def masked_scores(docs, stream, keys, q, first, limit):
    scores = dot_nt(keys, q) * (HD**-0.5)
    t = first + lax.broadcasted_iota(jnp.int32, (1, q.shape[0]), 1)
    u = lax.broadcasted_iota(jnp.int32, scores.shape, 0)
    return scores, (u >= starts_of(docs, stream, t)) & (u <= t)


QROWS = 256


def attention_forward(docs, queries, keyval, heads):
    groups, streams, rows, cols = queries.shape
    length = groups * rows
    block = min(QROWS, length)

    def kernel(docs_ref, q_ref, kv_ref, mixed_ref, lse_ref):
        stream = pl.program_id(0)
        kv = kv_ref[...].reshape(length, 2 * HD)
        keys = kv[:, :HD]
        values_t = kv[:, HD:].T
        per = block // rows
        for b in range(length // block):
            limit = (b + 1) * block
            q_rows = q_ref[b * per : (b + 1) * per].reshape(block, cols)
            for h in range(heads):
                q = q_rows[:, h * HD : (h + 1) * HD]
                scores, allowed = masked_scores(
                    docs_ref, stream, keys[:limit], q, b * block, limit
                )
                scores = jnp.where(allowed, scores, -1e30)
                top = jnp.max(scores, axis=0, keepdims=True)
                weights = jnp.exp(scores - top)
                total = jnp.sum(weights, axis=0, keepdims=True)
                mixed = dot(values_t[:, :limit], weights.astype(bf16)) / total
                mixed_ref[b * per : (b + 1) * per, :, h * HD : (h + 1) * HD] = (
                    mixed.T.astype(bf16).reshape(per, rows, HD)
                )
                lse_ref[h : h + 1, b * block : (b + 1) * block] = top + jnp.log(total)

    spec = pl.BlockSpec((groups, None, rows, cols), lambda s: (0, s, 0, 0))
    spec_kv = pl.BlockSpec((groups, None, rows, 2 * HD), lambda s: (0, s, 0, 0))
    return pl.pallas_call(
        kernel,
        grid=(streams,),
        out_shape=[
            jax.ShapeDtypeStruct(queries.shape, bf16),
            jax.ShapeDtypeStruct((streams, heads, length), f32),
        ],
        in_specs=[pl.BlockSpec(memory_space=pltpu.SMEM), spec, spec_kv],
        out_specs=[spec, pl.BlockSpec((None, heads, length), lambda s: (s, 0, 0))],
        compiler_params=pltpu.CompilerParams(vmem_limit_bytes=VMEM_LIMIT),
        cost_estimate=pl.CostEstimate(
            flops=4 * streams * heads * length * length * HD,
            bytes_accessed=8 * 1024 * 1024,
            transcendentals=streams * heads * length * length,
        ),
        name="attention_forward",
    )(docs, queries, keyval)


def attention_backward(docs, queries, keyval, grads, lse, heads):
    groups, streams, rows, cols = queries.shape
    length = groups * rows
    block = min(QROWS, length)

    def kernel(docs_ref, q_ref, kv_ref, g_ref, lse_ref, gq_ref, gkv_ref, gk, gv):
        stream = pl.program_id(0)
        kv = kv_ref[...].reshape(length, 2 * HD)
        keys, values = kv[:, :HD], kv[:, HD:]
        keys_t = keys.T
        per = block // rows
        gk[...] = jnp.zeros_like(gk)
        gv[...] = jnp.zeros_like(gv)
        for b in range(length // block):
            limit = (b + 1) * block
            q_rows = q_ref[b * per : (b + 1) * per].reshape(block, cols)
            g_rows = g_ref[b * per : (b + 1) * per].reshape(block, cols)
            for h in range(heads):
                q = q_rows[:, h * HD : (h + 1) * HD]
                g = g_rows[:, h * HD : (h + 1) * HD]
                scores, allowed = masked_scores(
                    docs_ref, stream, keys[:limit], q, b * block, limit
                )
                shift = lse_ref[h : h + 1, b * block : (b + 1) * block]
                probs = jnp.where(allowed, jnp.exp(scores - shift), 0.0)
                grad_probs = dot_nt(values[:limit], g)
                weighted = probs * grad_probs
                delta = jnp.sum(weighted, axis=0, keepdims=True)
                grad_scores = (weighted - probs * delta).astype(bf16)
                gq = dot(keys_t[:, :limit], grad_scores) * (HD**-0.5)
                gq_ref[b * per : (b + 1) * per, :, h * HD : (h + 1) * HD] = (
                    gq.T.astype(bf16).reshape(per, rows, HD)
                )
                gk[:limit, :] += dot(grad_scores, q)
                gv[:limit, :] += dot(probs.astype(bf16), g)
        gkv_ref[:, :, :HD] = (gk[...] * (HD**-0.5)).astype(bf16).reshape(groups, rows, HD)
        gkv_ref[:, :, HD:] = gv[...].astype(bf16).reshape(groups, rows, HD)

    spec = pl.BlockSpec((groups, None, rows, cols), lambda s: (0, s, 0, 0))
    spec_kv = pl.BlockSpec((groups, None, rows, 2 * HD), lambda s: (0, s, 0, 0))
    return pl.pallas_call(
        kernel,
        grid=(streams,),
        out_shape=[
            jax.ShapeDtypeStruct(queries.shape, bf16),
            jax.ShapeDtypeStruct(keyval.shape, bf16),
        ],
        in_specs=[
            pl.BlockSpec(memory_space=pltpu.SMEM),
            spec,
            spec_kv,
            spec,
            pl.BlockSpec((None, heads, length), lambda s: (s, 0, 0)),
        ],
        out_specs=[spec, spec_kv],
        scratch_shapes=[pltpu.VMEM((length, HD), f32)] * 2,
        compiler_params=pltpu.CompilerParams(vmem_limit_bytes=VMEM_LIMIT),
        cost_estimate=pl.CostEstimate(
            flops=10 * streams * heads * length * length * HD,
            bytes_accessed=8 * 1024 * 1024,
            transcendentals=streams * heads * length * length,
        ),
        name="attention_backward",
    )(docs, queries, keyval, grads, lse)


def columns_to_rows(part, groups):
    rows = part.shape[0]
    spread = part.reshape(rows, groups, part.shape[1] // groups).transpose(1, 0, 2)
    return lax.all_to_all(spread, "seq", split_axis=0, concat_axis=0, tiled=True)


def column_weight(pieces):
    full = lax.all_gather(pieces, "fsdp", axis=1, tiled=True)
    return full.reshape(-1, full.shape[2])


def column_weight_grad(grad, groups):
    rows, cols = grad.shape
    return lax.psum_scatter(
        grad.astype(bf16).reshape(groups, rows // groups, cols),
        "fsdp",
        scatter_dimension=1,
        tiled=True,
    )


def row_weight_grad(grad):
    return lax.psum_scatter(grad.astype(bf16), "fsdp", scatter_dimension=0, tiled=True).astype(f32)


def shards(
    tokens,
    doc_starts,
    w_query,
    w_kv,
    w_out,
    w_fc,
    w_proj,
    ln1_gain,
    ln1_bias,
    b_query,
    b_value,
    b_out,
    ln2_gain,
    ln2_bias,
    b_fc,
    b_proj,
    cotangent,
):
    groups = lax.axis_size("seq")
    layers = lax.axis_size("fsdp")
    me = lax.axis_index("seq")
    streams, rows, width = tokens.shape
    own = streams * rows
    heads = HEADS // groups
    hidden = b_fc.shape[0]
    my_cols = heads * HD
    my_hidden = hidden // groups
    kernels = groups == PLANE

    def gather(*blocks, number):
        if kernels:
            return gather_plane(blocks, number)
        return [lax.all_gather(b, "seq", axis=0, tiled=True) for b in blocks]

    def scatter(*pairs, number, name):
        if kernels:
            return matmul_scatter(pairs, number, name)
        total = sum((dot_nt if nt else dot)(a, w) for a, w, nt in pairs)
        return lax.psum_scatter(
            total.astype(bf16), "seq", scatter_dimension=0, tiled=True
        ).astype(f32)

    inputs = tokens.reshape(own, width).astype(f32)
    cot_low = cotangent.reshape(own, width)
    cot_full = cot_low.astype(f32)

    if kernels:
        wq_pieces, wf_pieces = split_columns((w_query, w_fc), groups, 1)
    else:
        wq_pieces, wf_pieces = columns_to_rows(w_query, groups), columns_to_rows(w_fc, groups)
    low_kv = lax.all_gather(w_kv, "fsdp", axis=0, tiled=True)
    wo = lax.all_gather(w_out, "fsdp", axis=0, tiled=True)
    wq = column_weight(wq_pieces)
    wf = column_weight(wf_pieces)
    wp = lax.all_gather(w_proj, "fsdp", axis=0, tiled=True)
    my_bq = lax.dynamic_slice_in_dim(b_query, me * my_cols, my_cols, 0)
    my_bf = lax.dynamic_slice_in_dim(b_fc, me * my_hidden, my_hidden, 0)

    shifted1, normed1, inverse1 = normalize(inputs, ln1_gain, ln1_bias)
    hidden1, cot_all, w_kv_all = gather(shifted1.astype(bf16), cot_low, low_kv, number=2)
    queries = (dot(hidden1, wq) + my_bq).astype(bf16).reshape(groups, streams, rows, my_cols)
    value_shift = jnp.concatenate([jnp.zeros((HD,), f32), b_value])
    keyval = (
        (dot(hidden1, w_kv_all) + value_shift).astype(bf16).reshape(groups, streams, rows, 2 * HD)
    )
    mixed, lse = attention_forward(doc_starts, queries, keyval, heads)
    mixed_rows = mixed.reshape(groups * own, my_cols)
    residual = inputs + scatter((mixed_rows, wo, False), number=3, name="scatter_attn") + b_out
    shifted2, normed2, inverse2 = normalize(residual, ln2_gain, ln2_bias)
    if kernels:
        hidden2, act_low, slope = gather_matmul(
            shifted2.astype(bf16),
            wf,
            [my_bf.reshape(1, my_hidden)],
            [bf16, bf16],
            lambda acc, cols, ex: gelu_pair(acc + ex[0][:, cols]),
            4,
            name="gather_fc",
        )
    else:
        (hidden2,) = gather(shifted2.astype(bf16), number=4)
        activated, slope = gelu_pair(dot(hidden2, wf) + my_bf)
        act_low = activated.astype(bf16)

    grad_b_proj = jnp.sum(cot_full, axis=0)
    shard_proj = row_weight_grad(dot_tn(act_low, cot_all))
    grad_pre = (dot_nt(cot_all, wp) * slope.astype(f32)).astype(bf16)
    my_grad_b_fc = jnp.sum(grad_pre.astype(f32), axis=0)
    fc_part = column_weight_grad(dot_tn(hidden2, grad_pre), groups)
    grad_hidden2 = scatter((grad_pre, wf, True), number=5, name="scatter_fc")
    output = residual + scatter((act_low, wp, False), number=6, name="scatter_proj") + b_proj
    back_second, grad_ln2_gain, grad_ln2_bias = normalize_back(
        grad_hidden2, normed2, inverse2, ln2_gain
    )
    grad_residual = cot_full + back_second
    grad_attn = grad_residual.astype(bf16)
    grad_b_out = jnp.sum(grad_attn.astype(f32), axis=0)
    if kernels:
        grad_attn_all, grad_mixed = gather_matmul(
            grad_attn, wo, [], [bf16], lambda acc, cols, ex: (acc,), 7, nt=True, name="gather_out"
        )
    else:
        (grad_attn_all,) = gather(grad_attn, number=7)
        grad_mixed = dot_nt(grad_attn_all, wo).astype(bf16)
    shard_out = row_weight_grad(dot_tn(mixed_rows, grad_attn_all))
    gq, gkv = attention_backward(
        doc_starts,
        queries,
        keyval,
        grad_mixed.reshape(groups, streams, rows, my_cols),
        lse,
        heads,
    )
    gq_rows = gq.reshape(groups * own, my_cols)
    gkv_rows = gkv.reshape(groups * own, 2 * HD)
    my_grad_b_query = jnp.sum(gq_rows.astype(f32), axis=0)
    grad_b_value = jnp.sum(gkv_rows[:, HD:].astype(f32), axis=0)
    query_part = column_weight_grad(dot_tn(hidden1, gq_rows), groups)
    shard_kv = row_weight_grad(
        lax.psum_scatter(
            dot_tn(hidden1, gkv_rows).astype(bf16), "seq", scatter_dimension=0, tiled=True
        )
    )
    grad_hidden1 = scatter(
        (gq_rows, wq, True), (gkv_rows, w_kv_all, True), number=8, name="scatter_query"
    )
    back_first, grad_ln1_gain, grad_ln1_bias = normalize_back(
        grad_hidden1, normed1, inverse1, ln1_gain
    )
    input_grad = grad_residual + back_first

    zero = jnp.zeros_like
    grad_b_query = lax.dynamic_update_slice_in_dim(zero(b_query), my_grad_b_query, me * my_cols, 0)
    grad_b_fc = lax.dynamic_update_slice_in_dim(zero(b_fc), my_grad_b_fc, me * my_hidden, 0)
    vectors = (
        grad_ln1_gain,
        grad_ln1_bias,
        grad_b_query,
        grad_b_value,
        grad_b_out,
        grad_ln2_gain,
        grad_ln2_bias,
        grad_b_fc,
        grad_b_proj,
    )
    if kernels:
        sizes = [v.shape[0] for v in vectors]
        lines = -(-sum(sizes) // (groups * 8 * 128)) * 8
        pad = groups * lines * 128 - sum(sizes)
        packed = jnp.concatenate(vectors + (jnp.zeros((pad,), f32),)).reshape(groups, lines, 128)
        packed, shard_fc, shard_query = last_exchange(
            packed, (fc_part, query_part), groups, layers, 9
        )
        flat = packed.reshape(-1)
        sums, at = [], 0
        for size in sizes:
            sums.append(flat[at : at + size])
            at += size
        shard_fc, shard_query = shard_fc.astype(f32), shard_query.astype(f32)
    else:
        sums = lax.psum(vectors, ("seq", "fsdp"))

        def side_by_side(part):
            moved = lax.all_to_all(part, "seq", split_axis=0, concat_axis=0, tiled=True)
            return moved.transpose(1, 0, 2).reshape(moved.shape[1], -1).astype(f32)

        shard_fc, shard_query = side_by_side(fc_part), side_by_side(query_part)
    return (
        output.reshape(streams, rows, width),
        input_grad.reshape(streams, rows, width),
        shard_query,
        shard_kv,
        shard_out,
        shard_fc,
        shard_proj,
        *sums,
    )


def solution(mesh):
    acts = P("fsdp", "seq", None)
    weight = P(("seq", "fsdp"), None)
    return jax.shard_map(
        shards,
        mesh=mesh,
        in_specs=(acts, P("fsdp", None)) + (weight,) * 5 + (P(),) * 9 + (acts,),
        out_specs=(acts, acts) + (weight,) * 5 + (P(),) * 9,
        check_vma=False,
    )
```

```python
import functools

import jax
import jax.numpy as jnp
from jax import lax
from jax.experimental import pallas as pl
from jax.experimental.pallas import tpu as pltpu
from jax.sharding import PartitionSpec as P

HEADS = 16
HD = 128

root_two_pi = 0.7978845608028654
cubic_coef = 0.044715
epsilon = 1e-05
f32 = jnp.float32
bf16 = jnp.bfloat16
MESH = pl.DeviceIdType.MESH
ANY = pl.BlockSpec(memory_space=pl.ANY)
WHOLE = pl.BlockSpec(memory_space=pltpu.VMEM)
VMEM_LIMIT = 56 * 1024 * 1024
PLANE = 8


def normalize(values, gain_row, shift_row):
    center = values - jnp.mean(values, axis=-1, keepdims=True)
    inverse = lax.rsqrt(jnp.mean(center * center, axis=-1, keepdims=True) + epsilon)
    normed = center * inverse
    return (normed * gain_row + shift_row, normed, inverse)


def normalize_back(grad_out, normed, inverse, gain_row):
    scaled = grad_out * gain_row
    grad_in = inverse * (
        scaled
        - jnp.mean(scaled, axis=-1, keepdims=True)
        - normed * jnp.mean(scaled * normed, axis=-1, keepdims=True)
    )
    return (grad_in, jnp.sum(grad_out * normed, axis=0), jnp.sum(grad_out, axis=0))


def gelu_pair(inputs):
    tangent = jnp.tanh(root_two_pi * (inputs + cubic_coef * inputs * inputs * inputs))
    activated = 0.5 * inputs * (1.0 + tangent)
    gradient_slope = 0.5 * (1.0 + tangent) + 0.5 * inputs * (
        1.0 - tangent * tangent
    ) * root_two_pi * (1.0 + 3.0 * cubic_coef * inputs * inputs)
    return (activated, gradient_slope)


def dot(a, b):
    return jnp.dot(a, b, preferred_element_type=f32)


def dot_nt(a, b):
    return lax.dot_general(a, b, (((1,), (1,)), ((), ())), preferred_element_type=f32)


def dot_tn(a, b):
    return lax.dot_general(a, b, (((0,), (0,)), ((), ())), preferred_element_type=f32)


def push(src, dst, send, recv, to):
    return pltpu.make_async_remote_copy(
        src_ref=src, dst_ref=dst, send_sem=send, recv_sem=recv, device_id=to, device_id_type=MESH
    )


def sems(*shape):
    return pltpu.SemaphoreType.DMA(shape)


def rows_at(start, size):
    return pl.ds(pl.multiple_of(start, size), size)


class Place:
    def __init__(self):
        me = lax.axis_index("seq")
        self.me = me
        self.core = lax.rem(me, 2)
        x = lax.rem(lax.div(me, 2), 2)
        y = lax.div(me, 4)
        self.sib = me + 1 - 2 * self.core
        self.xn = me + 2 - 4 * x
        self.yn = me + 4 - 8 * y
        self.dg = me + 2 - 4 * x + 4 - 8 * y
        turn = 1 - 2 * self.core
        self.xs, self.ys, self.ds = self.xn + turn, self.yn + turn, self.dg + turn
        self.layer = lax.axis_index("fsdp")

    def plane_peer(self, step):
        return lax.rem(self.me + step, PLANE)

    def line_peer(self, step, layers):
        return lax.rem(self.layer + step, layers)

    def greet(self, whole_plane=False, layers=1):
        barrier = pltpu.get_barrier_semaphore()
        if whole_plane:
            others = [self.plane_peer(step) for step in range(1, PLANE)]
        else:
            others = [self.sib, self.xn, self.yn]
        for other in others:
            pl.semaphore_signal(barrier, inc=1, device_id={"seq": other}, device_id_type=MESH)
        for step in range(1, layers):
            other = self.line_peer(step, layers)
            pl.semaphore_signal(barrier, inc=1, device_id={"fsdp": other}, device_id_type=MESH)
        pl.semaphore_wait(barrier, len(others) + layers - 1)


class Gather:
    sends = 14
    scratch = [sems(14), sems(PLANE, 2)]

    def __init__(self, place, buf, rows, send, recv):
        self.p, self.buf, self.rows, self.half = place, buf, rows, rows // 2
        self.send_sem, self.recv_sem = send, recv
        self.copies = []

    def piece(self, dev, half):
        return self.buf.at[rows_at(dev * self.rows + half * self.half, self.half), :]

    def pair(self, dev):
        return rows_at(lax.div(dev, 2) * (2 * self.rows), 2 * self.rows)

    def send(self, dev, half, to, src=None):
        k = len(self.copies)
        piece = self.piece(dev, half)
        copy = push(
            piece if src is None else src,
            piece,
            self.send_sem.at[k],
            self.recv_sem.at[dev, half],
            {"seq": to},
        )
        copy.start()
        self.copies.append(copy)

    def arrived(self, dev, half):
        piece = self.piece(dev, half)
        push(
            piece, piece, self.send_sem.at[0], self.recv_sem.at[dev, half], {"seq": self.p.sib}
        ).wait_recv()

    def start(self, own):
        p = self.p
        parts = [own.at[pl.ds(h * self.half, self.half), :] for h in range(2)]
        self.send(p.me, 0, p.yn, parts[0])
        self.send(p.me, 1, p.xn, parts[1])
        self.send(p.me, 1, p.yn, parts[1])
        self.send(p.me, 0, p.xn, parts[0])
        for h in range(2):
            self.send(p.me, h, p.sib, parts[h])

    def relay_first(self):
        p = self.p
        self.arrived(p.yn, 0)
        self.send(p.yn, 0, p.xn)
        self.arrived(p.xn, 1)
        self.send(p.xn, 1, p.yn)
        self.send(p.yn, 0, p.sib)
        self.send(p.xn, 1, p.sib)

    def relay_rest(self):
        p = self.p
        self.arrived(p.xn, 0)
        self.send(p.xn, 0, p.sib)
        self.arrived(p.yn, 1)
        self.send(p.yn, 1, p.sib)

    def relay(self):
        self.relay_first()
        self.relay_rest()

    def have(self, dev):
        self.arrived(dev, 0)
        self.arrived(dev, 1)

    def relay_corner(self):
        p = self.p
        for h in range(2):
            self.arrived(p.dg, h)
            self.send(p.dg, h, p.sib)

    def finish(self):
        for copy in self.copies:
            copy.wait_send()


class Scatter:
    def __init__(self, place, rows, part, sib_out, sib_in, boxes, sib_send, sib_recv, send, recv):
        self.p, self.rows, self.half = place, rows, rows // 2
        self.part, self.sib_out, self.sib_in = part, sib_out, sib_in
        self.out_d, self.out_x, self.out_y, self.in_d, self.in_x, self.in_y = boxes
        self.sib_send, self.sib_recv, self.send, self.recv = sib_send, sib_recv, send, recv
        self.copies = []

    @staticmethod
    def scratch(rows, wide):
        return [
            pltpu.VMEM((4, rows, wide), f32),
            pltpu.VMEM((4, rows, wide), bf16),
            pltpu.VMEM((4, rows, wide), bf16),
            *[pltpu.VMEM((rows, wide), bf16)] * 6,
            sems(4),
            sems(4),
            sems(6),
            sems(6),
        ]

    @classmethod
    def take(cls, place, rows, refs):
        return cls(place, rows, refs[0], refs[1], refs[2], refs[3:9], *refs[9:13])

    def swap(self, role, dev, product):
        p = self.p
        chip = lax.div(dev, 2) * (2 * self.rows)

        def store_out(cols, value):
            self.sib_out[role, :, cols] = value.astype(bf16)

        def store_part(cols, value):
            self.part[role, :, cols] = value

        product(
            rows_at(chip + (1 - p.core) * self.rows, self.rows),
            rows_at(chip + p.core * self.rows, self.rows),
            store_out,
            store_part,
        )
        copy = push(
            self.sib_out.at[role],
            self.sib_in.at[role],
            self.sib_send.at[role],
            self.sib_recv.at[role],
            {"seq": p.sib},
        )
        copy.start()
        self.copies.append(copy)
        return copy

    def add_into(self, dst, role, first, size, more=()):
        lines = 32

        @pl.loop(0, size // lines)
        def _(i):
            line = rows_at(first + i * lines, lines)
            value = self.part[role, line, :] + self.sib_in[role, line, :].astype(f32)
            for ref in more:
                value = value + ref[line, :].astype(f32)
            dst[line, :] = value.astype(dst.dtype)

    def ship(self, src, dst, h, k, to):
        lines = pl.ds(h * self.half, self.half)
        copy = push(
            src.at[lines, :], dst.at[lines, :], self.send.at[k], self.recv.at[k], {"seq": to}
        )
        copy.start()
        self.copies.append(copy)
        return copy

    def run(self, product, out_ref, idle=None):
        p, rows, half = self.p, self.rows, self.half
        to_d = self.swap(0, p.dg, product)
        to_x = self.swap(1, p.xn, product)
        to_d.wait_recv()
        self.add_into(self.out_d, 0, 0, rows)
        dx = self.ship(self.out_d, self.in_d, 0, 0, p.xn)
        dy = self.ship(self.out_d, self.in_d, 1, 1, p.yn)
        to_y = self.swap(2, p.yn, product)
        to_x.wait_recv()
        self.add_into(self.out_x, 1, 0, half)
        x0 = self.ship(self.out_x, self.in_x, 0, 2, p.xn)
        to_y.wait_recv()
        self.add_into(self.out_y, 2, half, half)
        y1 = self.ship(self.out_y, self.in_y, 1, 3, p.yn)
        to_me = self.swap(3, p.me, product)
        dy.wait_recv()
        self.add_into(self.out_x, 1, half, half, (self.in_d,))
        x1 = self.ship(self.out_x, self.in_x, 1, 4, p.xn)
        dx.wait_recv()
        self.add_into(self.out_y, 2, 0, half, (self.in_d,))
        y0 = self.ship(self.out_y, self.in_y, 0, 5, p.yn)
        if idle is not None:
            idle()
        to_me.wait_recv()
        x0.wait_recv()
        y0.wait_recv()
        self.add_into(out_ref, 3, 0, half, (self.in_x, self.in_y))
        y1.wait_recv()
        x1.wait_recv()
        self.add_into(out_ref, 3, half, half, (self.in_x, self.in_y))
        for copy in self.copies:
            copy.wait_send()


def params(number, vmem=True):
    return pltpu.CompilerParams(
        collective_id=number,
        has_side_effects=True,
        vmem_limit_bytes=VMEM_LIMIT if vmem else None,
    )


def cost(flops, mib=40):
    return pl.CostEstimate(flops=flops, bytes_accessed=mib * 1024 * 1024, transcendentals=0)


def load(src, dst, sem):
    copy = pltpu.make_async_copy(src, dst, sem)
    copy.start()
    return copy


def split_weights(w_query, w_fc, w_kv, layers, number):
    arrays = (w_query, w_fc)

    def kernel(wq_ref, wf_ref, kv_ref, wq_out, wf_out, kv_out, send, recv, zsend, zrecv, local):
        p = Place()
        kv_rows = kv_ref.shape[0]
        mine = kv_out.at[rows_at(p.layer * kv_rows, kv_rows), :]
        ins, outs = (wq_ref, wf_ref), (wq_out, wf_out)

        def block(i, dev):
            cols = ins[i].shape[1] // PLANE
            return ins[i].at[:, rows_at(dev * cols, cols)]

        own = [load(kv_ref, mine, local.at[2])]
        for i in range(2):
            own.append(load(block(i, p.me), outs[i].at[p.me], local.at[i]))
        p.greet(True, layers)
        copies = []
        for step in range(1, layers):
            to = p.line_peer(step, layers)
            copies.append(push(kv_ref, mine, zsend.at[step], zrecv.at[step], {"fsdp": to}))
            copies[-1].start()
        for i in range(2):
            for step in range(1, PLANE):
                to = p.plane_peer(step)
                copies.append(
                    push(
                        block(i, to),
                        outs[i].at[p.me],
                        send.at[i, step],
                        recv.at[i, step],
                        {"seq": to},
                    )
                )
                copies[-1].start()
        for copy in own + copies:
            copy.wait()

    return pl.pallas_call(
        kernel,
        out_shape=[
            jax.ShapeDtypeStruct((PLANE, a.shape[0], a.shape[1] // PLANE), a.dtype)
            for a in arrays
        ]
        + [jax.ShapeDtypeStruct((layers * w_kv.shape[0], w_kv.shape[1]), w_kv.dtype)],
        in_specs=[ANY] * 3,
        out_specs=[ANY] * 3,
        scratch_shapes=[
            sems(2, PLANE),
            sems(2, PLANE),
            sems(layers),
            sems(layers),
            sems(3),
        ],
        compiler_params=params(number, False),
        name="split_weights",
    )(w_query, w_fc, w_kv)


def gather_hidden1(hidden1, low_kv, wq_pieces, layers, number):
    def kernel(h_ref, kv_ref, wq_ref, h_all, kv_all, wq_all, *refs):
        hs, hr, ks, kr, zsend, zrecv, local = refs
        p = Place()
        h_rows, kv_rows = h_ref.shape[0], kv_ref.shape[0]
        wq_mine = wq_all.at[:, p.layer]
        own = [
            load(h_ref, h_all.at[rows_at(p.me * h_rows, h_rows), :], local.at[0]),
            load(kv_ref, kv_all.at[rows_at(p.me * kv_rows, kv_rows), :], local.at[1]),
            load(wq_ref, wq_mine, local.at[2]),
        ]
        p.greet(False, layers)
        kv = Gather(p, kv_all, kv_rows, ks, kr)
        h = Gather(p, h_all, h_rows, hs, hr)
        kv.start(kv_ref)
        h.start(h_ref)
        across = []
        for step in range(1, layers):
            to = p.line_peer(step, layers)
            across.append(push(wq_ref, wq_mine, zsend.at[step], zrecv.at[step], {"fsdp": to}))
            across[-1].start()
        kv.relay()
        kv.relay_corner()
        h.relay()
        h.relay_corner()
        for g in (kv, h):
            for dev in (p.sib, p.xs, p.ys, p.ds):
                g.have(dev)
            g.finish()
        for copy in own + across:
            copy.wait()

    groups, piece_rows, cols = wq_pieces.shape
    return pl.pallas_call(
        kernel,
        out_shape=[
            jax.ShapeDtypeStruct((PLANE * hidden1.shape[0], hidden1.shape[1]), bf16),
            jax.ShapeDtypeStruct((PLANE * low_kv.shape[0], low_kv.shape[1]), bf16),
            jax.ShapeDtypeStruct((groups, layers, piece_rows, cols), bf16),
        ],
        in_specs=[ANY] * 3,
        out_specs=[ANY] * 3,
        scratch_shapes=Gather.scratch * 2 + [sems(layers), sems(layers), sems(3)],
        compiler_params=params(number, False),
        name="gather_hidden1",
    )(hidden1, low_kv, wq_pieces)


def project_attend(docs, hidden1, wq, w_kv, bq, bkv, cot, w_out, streams, heads, layers, number):
    total, depth = hidden1.shape
    cols, kv_cols = wq.shape[1], w_kv.shape[1]
    rows = total // PLANE // streams
    length = PLANE * rows
    block = min(QROWS, length)
    chunk = total // 4

    def kernel(docs_ref, h_ref, wq_ref, wkv_ref, bq_ref, bkv_ref, cot_ref, wo_ref, *refs):
        cot_all, wo_all, q_out, kv_out, mixed_out, lse_ref = refs[:6]
        h_buf, wq_buf, wkv_buf, q_buf, kv_buf, mixed_buf = refs[6:12]
        send, recv, zsend, zrecv, local = refs[12:]
        p = Place()
        own_rows = cot_ref.shape[0]
        wo_rows = wo_ref.shape[0]
        wo_mine = wo_all.at[rows_at(p.layer * wo_rows, wo_rows), :]

        def fetch(k):
            return load(
                h_ref.at[pl.ds(k * chunk, chunk), :], h_buf.at[k % 2], local.at[k % 2]
            )

        fetches = [fetch(0)]
        weights = [load(wq_ref, wq_buf, local.at[2]), load(wkv_ref, wkv_buf, local.at[3])]
        own = [
            load(cot_ref, cot_all.at[rows_at(p.me * own_rows, own_rows), :], local.at[4]),
            load(wo_ref, wo_mine, local.at[8]),
        ]
        p.greet(False, layers)
        g = Gather(p, cot_all, own_rows, send, recv)
        g.start(cot_ref)
        for step in range(1, layers):
            to = p.line_peer(step, layers)
            own.append(push(wo_ref, wo_mine, zsend.at[step], zrecv.at[step], {"fsdp": to}))
            own[-1].start()
        for copy in weights:
            copy.wait()
        per = chunk // (streams * rows)
        for k in range(4):
            fetches[k].wait()
            if k < 3:
                fetches.append(fetch(k + 1))
            where = pl.ds(k * per, per)
            q = dot(h_buf[k % 2], wq_buf[...]) + bq_ref[...]
            q_buf[where] = q.astype(bf16).reshape(per, streams, rows, cols)
            kv = dot(h_buf[k % 2], wkv_buf[...]) + bkv_ref[...]
            kv_buf[where] = kv.astype(bf16).reshape(per, streams, rows, kv_cols)
        stores = [load(q_buf, q_out, local.at[5]), load(kv_buf, kv_out, local.at[6])]
        g.relay_first()
        for stream in range(streams):
            attend_stream(
                docs_ref,
                stream,
                q_buf.at[:, stream],
                kv_buf.at[:, stream],
                mixed_buf.at[:, stream],
                lse_ref.at[stream],
                block,
                heads,
            )
        stores.append(load(mixed_buf, mixed_out, local.at[7]))
        g.relay_rest()
        g.relay_corner()
        for dev in (p.sib, p.xs, p.ys, p.ds):
            g.have(dev)
        g.finish()
        for copy in own + stores:
            copy.wait()

    q_shape = (PLANE, streams, rows, cols)
    kv_shape = (PLANE, streams, rows, kv_cols)
    return pl.pallas_call(
        kernel,
        out_shape=[
            jax.ShapeDtypeStruct((PLANE * cot.shape[0], cot.shape[1]), bf16),
            jax.ShapeDtypeStruct((layers * w_out.shape[0], w_out.shape[1]), bf16),
            jax.ShapeDtypeStruct(q_shape, bf16),
            jax.ShapeDtypeStruct(kv_shape, bf16),
            jax.ShapeDtypeStruct(q_shape, bf16),
            jax.ShapeDtypeStruct((streams, heads, length), f32),
        ],
        in_specs=[pl.BlockSpec(memory_space=pltpu.SMEM)] + [ANY] * 3 + [WHOLE] * 2 + [ANY] * 2,
        out_specs=[ANY] * 5 + [WHOLE],
        scratch_shapes=[
            pltpu.VMEM((2, chunk, depth), bf16),
            pltpu.VMEM(wq.shape, bf16),
            pltpu.VMEM(w_kv.shape, bf16),
            pltpu.VMEM(q_shape, bf16),
            pltpu.VMEM(kv_shape, bf16),
            pltpu.VMEM(q_shape, bf16),
        ]
        + Gather.scratch
        + [sems(layers), sems(layers), sems(9)],
        compiler_params=params(number),
        cost_estimate=cost(2 * total * depth * (cols + kv_cols)),
        name="project_attend",
    )(docs, hidden1, wq, w_kv, bq, bkv, cot, w_out)


def gather_fc(hidden2, wf, bf, cot_all, number):
    rows, depth = hidden2.shape
    wide = wf.shape[1]
    total = PLANE * rows
    out_wide = cot_all.shape[1]
    tile = 256

    def kernel(own_ref, w_ref, b_ref, cot_ref, all_ref, act_ref, slope_ref, dw_ref, *refs):
        buf, w_buf, act, slope, cot, acc, dw, send, recv, local = refs
        p = Place()
        load_own = load(own_ref, buf.at[rows_at(p.me * rows, rows), :], local.at[0])
        load_w = load(w_ref, w_buf, local.at[1])
        p.greet()
        g = Gather(p, buf, rows, send, recv)
        g.start(own_ref)
        stores = []
        cots = {}

        def fetch(k, dev):
            cots[k] = load(cot_ref.at[g.pair(dev), :], cot.at[k % 2], local.at[2 + k % 2])

        def work(k, dev):
            block = g.pair(dev)
            stores.append(load(buf.at[block, :], all_ref.at[block, :], local.at[4 + 3 * k]))

            @pl.loop(0, wide // tile)
            def _(j):
                cols = rows_at(j * tile, tile)
                acc_fc = dot(buf[block, :], w_buf[:, cols]) + b_ref[:, cols]
                activated, gradient = gelu_pair(acc_fc)
                act[block, cols] = activated.astype(bf16)
                slope[block, cols] = gradient.astype(bf16)

            for i, (src, dst) in enumerate(((act, act_ref), (slope, slope_ref))):
                stores.append(
                    load(src.at[block, :], dst.at[block, :], local.at[4 + 3 * k + 1 + i])
                )

        def grads(k, dev):
            block = g.pair(dev)
            cots[k].wait()

            @pl.loop(0, wide // tile)
            def _(j):
                cols = rows_at(j * tile, tile)
                term = dot_tn(act[block, cols], cot[k % 2])
                if k == 0:
                    acc[cols, :] = term
                elif k < 3:
                    acc[cols, :] += term
                else:
                    dw[cols, :] = (acc[cols, :] + term).astype(bf16)

        fetch(0, p.me)
        fetch(1, p.xn)
        load_own.wait()
        load_w.wait()
        g.have(p.sib)
        work(0, p.me)
        g.relay_first()
        grads(0, p.me)
        fetch(2, p.yn)
        g.relay_rest()
        g.have(p.xs)
        work(1, p.xn)
        g.have(p.ys)
        work(2, p.yn)
        grads(1, p.xn)
        fetch(3, p.dg)
        g.relay_corner()
        grads(2, p.yn)
        g.have(p.ds)
        work(3, p.dg)
        grads(3, p.dg)
        stores.append(load(dw, dw_ref, local.at[16]))
        g.finish()
        for copy in stores:
            copy.wait()

    return pl.pallas_call(
        kernel,
        out_shape=[
            jax.ShapeDtypeStruct((total, depth), bf16),
            jax.ShapeDtypeStruct((total, wide), bf16),
            jax.ShapeDtypeStruct((total, wide), bf16),
            jax.ShapeDtypeStruct((wide, out_wide), bf16),
        ],
        in_specs=[ANY, ANY, WHOLE, ANY],
        out_specs=[ANY] * 4,
        scratch_shapes=[
            pltpu.VMEM((total, depth), bf16),
            pltpu.VMEM(wf.shape, bf16),
            pltpu.VMEM((total, wide), bf16),
            pltpu.VMEM((total, wide), bf16),
            pltpu.VMEM((2, 2 * rows, out_wide), bf16),
            pltpu.VMEM((wide, out_wide), f32),
            pltpu.VMEM((wide, out_wide), bf16),
        ]
        + Gather.scratch
        + [sems(17)],
        compiler_params=params(number),
        cost_estimate=cost(4 * total * depth * wide),
        name="gather_fc",
    )(hidden2, wf, bf, cot_all)


def gather_out(grad_attn, wo, mixed, number):
    rows, depth = grad_attn.shape
    wide = wo.shape[0]
    total = PLANE * rows

    def kernel(own_ref, w_ref, mixed_ref, gm_ref, dw_ref, *refs):
        buf, w_buf, mixed_buf, gm, acc, dw, send, recv, local = refs
        p = Place()
        load_own = load(own_ref, buf.at[rows_at(p.me * rows, rows), :], local.at[0])
        loads = [load(w_ref, w_buf, local.at[1]), load(mixed_ref, mixed_buf, local.at[2])]
        p.greet()
        g = Gather(p, buf, rows, send, recv)
        g.start(own_ref)

        def work(dev):
            block = g.pair(dev)
            gm[block, :] = dot_nt(buf[block, :], w_buf[...]).astype(bf16)

        def grads(k, dev):
            block = g.pair(dev)
            term = dot_tn(mixed_buf[block, :], buf[block, :])
            if k == 0:
                acc[...] = term
            elif k < 3:
                acc[...] += term
            else:
                dw[...] = (acc[...] + term).astype(bf16)

        load_own.wait()
        for copy in loads:
            copy.wait()
        g.have(p.sib)
        work(p.me)
        grads(0, p.me)
        g.relay()
        g.have(p.xs)
        work(p.xn)
        g.have(p.ys)
        work(p.yn)
        grads(1, p.xn)
        g.relay_corner()
        grads(2, p.yn)
        g.have(p.ds)
        work(p.dg)
        store = load(gm, gm_ref, local.at[3])
        grads(3, p.dg)
        store_dw = load(dw, dw_ref, local.at[4])
        g.finish()
        store.wait()
        store_dw.wait()

    return pl.pallas_call(
        kernel,
        out_shape=[
            jax.ShapeDtypeStruct((total, wide), bf16),
            jax.ShapeDtypeStruct((wide, depth), bf16),
        ],
        in_specs=[ANY] * 3,
        out_specs=[ANY] * 2,
        scratch_shapes=[
            pltpu.VMEM((total, depth), bf16),
            pltpu.VMEM(wo.shape, bf16),
            pltpu.VMEM(mixed.shape, bf16),
            pltpu.VMEM((total, wide), bf16),
            pltpu.VMEM((wide, depth), f32),
            pltpu.VMEM((wide, depth), bf16),
        ]
        + Gather.scratch
        + [sems(5)],
        compiler_params=params(number),
        cost_estimate=cost(4 * total * depth * wide),
        name="gather_out",
    )(grad_attn, wo, mixed)


TILE = 512


def scatter_attn(a, weight, number):
    total, depth = a.shape
    rows = total // PLANE
    wide = weight.shape[1]

    def kernel(a_ref, w_ref, out_ref, a_buf, w_buf, *refs):
        s, local = refs[:13], refs[13]
        p = Place()
        loads = [load(a_ref, a_buf, local.at[0]), load(w_ref, w_buf, local.at[1])]
        p.greet()
        for copy in loads:
            copy.wait()
        Scatter.take(p, rows, s).run(plain_product(a_buf, w_buf), out_ref)

    return pl.pallas_call(
        kernel,
        out_shape=jax.ShapeDtypeStruct((rows, wide), f32),
        in_specs=[ANY] * 2,
        out_specs=WHOLE,
        scratch_shapes=[pltpu.VMEM(a.shape, bf16), pltpu.VMEM(weight.shape, bf16)]
        + Scatter.scratch(rows, wide)
        + [sems(2)],
        compiler_params=params(number),
        cost_estimate=cost(2 * total * depth * wide),
        name="scatter_attn",
    )(a, weight)


def plain_product(a_buf, w_buf):
    def product(theirs, ours, store_out, store_part):
        @pl.loop(0, w_buf.shape[1] // TILE)
        def _(j):
            cols = rows_at(j * TILE, TILE)
            store_out(cols, dot(a_buf[theirs, :], w_buf[:, cols]))
            store_part(cols, dot(a_buf[ours, :], w_buf[:, cols]))

    return product


def scatter_fc(cot_all, slope, wp, wf, hidden2, number):
    total, depth = cot_all.shape
    rows = total // PLANE
    wide = wp.shape[0]
    tile = 256

    def kernel(cot_ref, slope_ref, wp_ref, wf_ref, h_ref, out_ref, bias_ref, dw_ref, *refs):
        cot, slopes, wp_buf, wf_buf, gp, h_buf, dw_buf = refs[:7]
        s = refs[7:20]
        (local,) = refs[20:]
        p = Place()
        order = (p.dg, p.xn, p.yn, p.me)

        def chip(dev):
            return rows_at(lax.div(dev, 2) * (2 * rows), 2 * rows)

        def fetch(k):
            here = chip(order[k])
            return (
                load(cot_ref.at[here, :], cot.at[k % 2], local.at[k % 2]),
                load(slope_ref.at[here, :], slopes.at[k % 2], local.at[2 + k % 2]),
            )

        fetches = [fetch(0)]
        load_wp = load(wp_ref, wp_buf, local.at[4])
        load_wf = load(wf_ref, wf_buf, local.at[5])
        bias_ref[...] = jnp.zeros_like(bias_ref)
        p.greet()
        load_wp.wait()
        count = []

        def product(theirs, ours, store_out, store_part):
            k = len(count)
            count.append(k)
            for copy in fetches[k]:
                copy.wait()
            if k < 3:
                fetches.append(fetch(k + 1))
            here = chip(order[k])

            @pl.loop(0, wide // tile)
            def _(j):
                cols = rows_at(j * tile, tile)
                grad_act = dot_nt(cot[k % 2], wp_buf[cols, :])
                grad_pre = (grad_act * slopes[k % 2, :, cols].astype(f32)).astype(bf16)
                gp[here, cols] = grad_pre
                bias_ref[:, cols] += jnp.sum(grad_pre.astype(f32), axis=0, keepdims=True)

            if k == 0:
                load_wf.wait()

            @pl.loop(0, depth // TILE)
            def _(j):
                cols = rows_at(j * TILE, TILE)
                store_out(cols, dot_nt(gp[theirs, :], wf_buf[cols, :]))
                store_part(cols, dot_nt(gp[ours, :], wf_buf[cols, :]))

        steps = depth // tile

        def h_fetch(i):
            return load(
                h_ref.at[:, pl.ds(i * tile, tile)], h_buf.at[i % 2], local.at[6 + i % 2]
            )

        def idle():
            tiles = [h_fetch(0)]
            stores = []
            for i in range(steps):
                tiles[i].wait()
                if i + 1 < steps:
                    tiles.append(h_fetch(i + 1))
                if i >= 2:
                    stores[i - 2].wait()
                dw_buf[i % 2] = dot_tn(h_buf[i % 2], gp[...]).astype(bf16)
                stores.append(
                    load(
                        dw_buf.at[i % 2],
                        dw_ref.at[pl.ds(i * tile, tile), :],
                        local.at[8 + i % 2],
                    )
                )
            for copy in stores[-2:]:
                copy.wait()

        Scatter.take(p, rows, s).run(product, out_ref, idle)

    return pl.pallas_call(
        kernel,
        out_shape=[
            jax.ShapeDtypeStruct((rows, depth), f32),
            jax.ShapeDtypeStruct((1, wide), f32),
            jax.ShapeDtypeStruct((depth, wide), bf16),
        ],
        in_specs=[ANY] * 5,
        out_specs=[WHOLE, WHOLE, ANY],
        scratch_shapes=[
            pltpu.VMEM((2, 2 * rows, depth), bf16),
            pltpu.VMEM((2, 2 * rows, wide), bf16),
            pltpu.VMEM(wp.shape, bf16),
            pltpu.VMEM(wf.shape, bf16),
            pltpu.VMEM((total, wide), bf16),
            pltpu.VMEM((2, total, tile), bf16),
            pltpu.VMEM((2, tile, wide), bf16),
        ]
        + Scatter.scratch(rows, depth)
        + [sems(10)],
        compiler_params=params(number),
        cost_estimate=cost(6 * total * depth * wide),
        name="scatter_fc",
    )(cot_all, slope, wp, wf, hidden2)


class LineSum:
    def __init__(self, place, block, box, layers, send, recv):
        self.copies = []
        self.box = box
        for step in range(1, layers):
            to = place.line_peer(step, layers)
            copy = push(block(to), box.at[step - 1], send.at[step], recv.at[step], {"fsdp": to})
            copy.start()
            self.copies.append(copy)

    def arrived(self):
        for copy in self.copies:
            copy.wait_recv()

    def total(self, own, where):
        value = own.astype(f32)
        for k in range(len(self.copies)):
            value = value + self.box[(k, *where)].astype(f32)
        return value

    def finish(self):
        for copy in self.copies:
            copy.wait_send()


def scatter_query(gq, gkv, wq, w_kv, hidden1, grad_w_out, layers, number):
    total, cols = gq.shape
    kv_cols = gkv.shape[1]
    rows = total // PLANE
    depth = wq.shape[0]
    part_rows = depth // PLANE
    out_rows = grad_w_out.shape[0] // layers
    out_wide = grad_w_out.shape[1]

    def kernel(gq_ref, gkv_ref, wq_ref, wkv_ref, h_ref, dwo_ref, *refs):
        out_ref, dwq_ref, dwkv_ref, dwo_out = refs[:4]
        g_buf, wq_buf, wkv_buf, h_buf, dwq_buf, dkv, box, dwo_own, dwo_box = refs[4:13]
        s = refs[13:26]
        ksend, krecv, zsend, zrecv, local = refs[26:]
        p = Place()

        def dwo_block(layer):
            return dwo_ref.at[rows_at(layer * out_rows, out_rows), :]

        load_dwo = load(dwo_block(p.layer), dwo_own, local.at[7])
        q_part, kv_part = pl.ds(0, cols), pl.ds(cols, kv_cols)
        loads = [
            load(gq_ref, g_buf.at[:, q_part], local.at[0]),
            load(gkv_ref, g_buf.at[:, kv_part], local.at[1]),
            load(wq_ref, wq_buf, local.at[2]),
            load(wkv_ref, wkv_buf, local.at[3]),
        ]

        def h_fetch(i):
            dev = p.plane_peer((i + 1) % PLANE)
            return load(
                h_ref.at[:, rows_at(dev * part_rows, part_rows)],
                h_buf.at[i % 2],
                local.at[4 + i % 2],
            )

        tiles = [h_fetch(0)]
        p.greet(True, layers)
        line = LineSum(p, dwo_block, dwo_box, layers, zsend, zrecv)
        for copy in loads:
            copy.wait()

        def product(theirs, ours, store_out, store_part):
            @pl.loop(0, depth // TILE)
            def _(j):
                where = rows_at(j * TILE, TILE)
                for rows_of, store in ((theirs, store_out), (ours, store_part)):
                    store(
                        where,
                        dot_nt(g_buf[rows_of, q_part], wq_buf[where, :])
                        + dot_nt(g_buf[rows_of, kv_part], wkv_buf[where, :]),
                    )

        sent = []

        def idle():
            for i in range(PLANE):
                step = (i + 1) % PLANE
                dev = p.plane_peer(step)
                tiles[i].wait()
                if i + 1 < PLANE:
                    tiles.append(h_fetch(i + 1))
                term = dot_tn(h_buf[i % 2], g_buf[...]).astype(bf16)
                dwq_buf[rows_at(dev * part_rows, part_rows), :] = term[:, :cols]
                dkv[step] = term[:, cols:]
                if step:
                    copy = push(
                        dkv.at[step], box.at[step], ksend.at[step], krecv.at[step], {"seq": dev}
                    )
                    copy.start()
                    sent.append(copy)

        Scatter.take(p, rows, s).run(product, out_ref, idle)
        store = load(dwq_buf, dwq_ref, local.at[6])
        sum_kv = dkv[0].astype(f32)
        for i, copy in enumerate(sent):
            copy.wait_recv()
            sum_kv = sum_kv + box[i + 1].astype(f32)
        dwkv_ref[...] = sum_kv.astype(bf16)
        load_dwo.wait()
        line.arrived()

        @pl.loop(0, out_rows // 16)
        def _(i):
            lines = rows_at(i * 16, 16)
            dwo_out[lines, :] = line.total(dwo_own[lines, :], (lines, slice(None)))

        for copy in sent:
            copy.wait_send()
        line.finish()
        store.wait()

    return pl.pallas_call(
        kernel,
        out_shape=[
            jax.ShapeDtypeStruct((rows, depth), f32),
            jax.ShapeDtypeStruct((depth, cols), bf16),
            jax.ShapeDtypeStruct((part_rows, kv_cols), bf16),
            jax.ShapeDtypeStruct((out_rows, out_wide), f32),
        ],
        in_specs=[ANY] * 6,
        out_specs=[WHOLE, ANY, WHOLE, WHOLE],
        scratch_shapes=[
            pltpu.VMEM((total, cols + kv_cols), bf16),
            pltpu.VMEM(wq.shape, bf16),
            pltpu.VMEM(w_kv.shape, bf16),
            pltpu.VMEM((2, total, part_rows), bf16),
            pltpu.VMEM((depth, cols), bf16),
            pltpu.VMEM((PLANE, part_rows, kv_cols), bf16),
            pltpu.VMEM((PLANE, part_rows, kv_cols), bf16),
            pltpu.VMEM((out_rows, out_wide), bf16),
            pltpu.VMEM((layers - 1, out_rows, out_wide), bf16),
        ]
        + Scatter.scratch(rows, depth)
        + [sems(PLANE), sems(PLANE), sems(layers), sems(layers), sems(8)],
        compiler_params=params(number),
        cost_estimate=cost(4 * total * depth * (cols + kv_cols)),
        name="scatter_query",
    )(gq, gkv, wq, w_kv, hidden1, grad_w_out)


def scatter_proj(act, wp, fc_pieces, grad_w_query, grad_w_kv, vector, layers, number):
    total, depth = act.shape
    rows = total // PLANE
    wide = wp.shape[1]
    lines = vector.shape[1]
    q_rows, q_cols = grad_w_query.shape[2:]
    kv_rows, kv_cols = grad_w_kv.shape[0] // layers, grad_w_kv.shape[1]
    fc_rows, fc_cols = fc_pieces.shape[1:]

    def kernel(act_ref, wp_ref, fc_ref, dwq_ref, dwkv_ref, vec, *refs):
        out_ref, fc_out, q_out, kv_out, vec_out = refs[:5]
        a_buf, w_buf, q_own, q_box, q_sum, kv_own, kv_box, box, plane_sum, zbox = refs[5:15]
        s = refs[15:28]
        (fsend, frecv, qsend, qrecv, qzsend, qzrecv, kzsend, kzrecv, vsend, vrecv, zsend, zrecv) = (
            refs[28:40]
        )
        gsend, grecv, local = refs[40:]
        p = Place()

        def q_block(layer):
            return dwq_ref.at[:, layer]

        def kv_block(layer):
            return dwkv_ref.at[rows_at(layer * kv_rows, kv_rows), :]

        fc_place = fc_out.at[:, rows_at(p.me * fc_cols, fc_cols)]
        q_place = q_out.at[:, rows_at(p.me * q_cols, q_cols)]
        loads = [load(act_ref, a_buf, local.at[0]), load(wp_ref, w_buf, local.at[1])]
        own_q = load(q_block(p.layer), q_own, local.at[2])
        own_kv = load(kv_block(p.layer), kv_own, local.at[3])
        ends = [load(fc_ref.at[p.me], fc_place, local.at[4])]
        p.greet(True, layers)
        first = []
        for step in range(1, PLANE):
            to = p.plane_peer(step)
            copy = push(vec.at[to], box.at[step], vsend.at[step], vrecv.at[step], {"seq": to})
            copy.start()
            first.append(copy)
        line_q = LineSum(p, q_block, q_box, layers, qzsend, qzrecv)
        line_kv = LineSum(p, kv_block, kv_box, layers, kzsend, kzrecv)
        for copy in loads:
            copy.wait()
        sent = []

        def spread(src, dst, send, recv):
            for step in range(1, PLANE):
                to = p.plane_peer(step)
                copy = push(src.at[to], dst, send.at[step], recv.at[step], {"seq": to})
                copy.start()
                ends.append(copy)

        def idle():
            spread(fc_ref, fc_place, fsend, frecv)
            total_vec = vec[p.me]
            for step in range(1, PLANE):
                first[step - 1].wait_recv()
                total_vec = total_vec + box[step]
            plane_sum[...] = total_vec
            zbox[0] = total_vec
            for step in range(1, layers):
                to = p.line_peer(step, layers)
                copy = push(plane_sum, zbox.at[step], zsend.at[step], zrecv.at[step], {"fsdp": to})
                copy.start()
                sent.append(copy)
            own_q.wait()
            line_q.arrived()

            @pl.loop(0, PLANE)
            def _(i):
                q_sum[i] = line_q.total(q_own[i], (i,)).astype(bf16)

            ends.append(load(q_sum.at[p.me], q_place, local.at[5]))
            spread(q_sum, q_place, qsend, qrecv)
            own_kv.wait()
            line_kv.arrived()
            kv_out[...] = line_kv.total(kv_own[...], ())
            for copy in sent:
                copy.wait_recv()
            total_vec = None
            for k in range(layers):
                term = zbox[lax.rem(p.layer - k + layers, layers)]
                total_vec = term if total_vec is None else total_vec + term
            vec_out[p.me] = total_vec
            for step in range(1, PLANE):
                to = p.plane_peer(step)
                mine = vec_out.at[p.me]
                copy = push(mine, mine, gsend.at[step], grecv.at[step], {"seq": to})
                copy.start()
                ends.append(copy)

        Scatter.take(p, rows, s).run(plain_product(a_buf, w_buf), out_ref, idle)
        for copy in first + sent:
            copy.wait_send()
        line_q.finish()
        line_kv.finish()
        for copy in ends:
            copy.wait()

    return pl.pallas_call(
        kernel,
        out_shape=[
            jax.ShapeDtypeStruct((rows, wide), f32),
            jax.ShapeDtypeStruct((fc_rows, PLANE * fc_cols), bf16),
            jax.ShapeDtypeStruct((q_rows, PLANE * q_cols), bf16),
            jax.ShapeDtypeStruct((kv_rows, kv_cols), f32),
            jax.ShapeDtypeStruct(vector.shape, f32),
        ],
        in_specs=[ANY] * 5 + [WHOLE],
        out_specs=[WHOLE, ANY, ANY, WHOLE, WHOLE],
        scratch_shapes=[
            pltpu.VMEM(act.shape, bf16),
            pltpu.VMEM(wp.shape, bf16),
            pltpu.VMEM((PLANE, q_rows, q_cols), bf16),
            pltpu.VMEM((layers - 1, PLANE, q_rows, q_cols), bf16),
            pltpu.VMEM((PLANE, q_rows, q_cols), bf16),
            pltpu.VMEM((kv_rows, kv_cols), bf16),
            pltpu.VMEM((layers - 1, kv_rows, kv_cols), bf16),
            pltpu.VMEM((PLANE, lines, 128), f32),
            pltpu.VMEM((lines, 128), f32),
            pltpu.VMEM((layers, lines, 128), f32),
        ]
        + Scatter.scratch(rows, wide)
        + [sems(PLANE)] * 4
        + [sems(layers)] * 4
        + [sems(PLANE)] * 2
        + [sems(layers)] * 2
        + [sems(PLANE)] * 2
        + [sems(6)],
        compiler_params=params(number),
        cost_estimate=cost(2 * total * depth * wide),
        name="scatter_proj",
    )(act, wp, fc_pieces, grad_w_query, grad_w_kv, vector)


def starts_of(docs, stream, positions):
    start = jnp.zeros_like(positions)
    for j in range(docs.shape[1]):
        here = docs[stream, j]
        start = jnp.maximum(start, jnp.where(here <= positions, here, 0))
    return start


def masked_scores(docs, stream, keys, q, first, limit):
    scores = dot_nt(keys, q) * (HD**-0.5)
    t = first + lax.broadcasted_iota(jnp.int32, (1, q.shape[0]), 1)
    u = lax.broadcasted_iota(jnp.int32, scores.shape, 0)
    return scores, (u >= starts_of(docs, stream, t)) & (u <= t)


QROWS = 256


def attend_stream(docs, stream, q_ref, kv_ref, mixed_ref, lse_ref, block, heads):
    groups, rows, cols = q_ref.shape
    length = groups * rows
    kv = kv_ref[...].reshape(length, 2 * HD)
    keys = kv[:, :HD]
    values_t = kv[:, HD:].T
    per = block // rows
    for b in range(length // block):
        limit = (b + 1) * block
        q_rows = q_ref[b * per : (b + 1) * per].reshape(block, cols)
        for h in range(heads):
            q = q_rows[:, h * HD : (h + 1) * HD]
            scores, allowed = masked_scores(docs, stream, keys[:limit], q, b * block, limit)
            scores = jnp.where(allowed, scores, -1e30)
            top = jnp.max(scores, axis=0, keepdims=True)
            weights = jnp.exp(scores - top)
            total = jnp.sum(weights, axis=0, keepdims=True)
            mixed = dot(values_t[:, :limit], weights.astype(bf16)) / total
            mixed_ref[b * per : (b + 1) * per, :, h * HD : (h + 1) * HD] = (
                mixed.T.astype(bf16).reshape(per, rows, HD)
            )
            lse_ref[h : h + 1, b * block : (b + 1) * block] = top + jnp.log(total)


def attention_backward(docs, queries, keyval, grads, lse, heads):
    groups, streams, rows, cols = queries.shape
    length = groups * rows
    block = min(QROWS, length)

    def kernel(docs_ref, q_ref, kv_ref, g_ref, lse_ref, gq_ref, gkv_ref, gk, gv):
        stream = pl.program_id(0)
        kv = kv_ref[...].reshape(length, 2 * HD)
        keys, values = kv[:, :HD], kv[:, HD:]
        keys_t = keys.T
        per = block // rows
        gk[...] = jnp.zeros_like(gk)
        gv[...] = jnp.zeros_like(gv)
        for b in range(length // block):
            limit = (b + 1) * block
            q_rows = q_ref[b * per : (b + 1) * per].reshape(block, cols)
            g_rows = g_ref[b * per : (b + 1) * per].reshape(block, cols)
            for h in range(heads):
                q = q_rows[:, h * HD : (h + 1) * HD]
                g = g_rows[:, h * HD : (h + 1) * HD]
                scores, allowed = masked_scores(
                    docs_ref, stream, keys[:limit], q, b * block, limit
                )
                shift = lse_ref[h : h + 1, b * block : (b + 1) * block]
                probs = jnp.where(allowed, jnp.exp(scores - shift), 0.0)
                grad_probs = dot_nt(values[:limit], g)
                weighted = probs * grad_probs
                delta = jnp.sum(weighted, axis=0, keepdims=True)
                grad_scores = (weighted - probs * delta).astype(bf16)
                gq = dot(keys_t[:, :limit], grad_scores) * (HD**-0.5)
                gq_ref[b * per : (b + 1) * per, :, h * HD : (h + 1) * HD] = (
                    gq.T.astype(bf16).reshape(per, rows, HD)
                )
                gk[:limit, :] += dot(grad_scores, q)
                gv[:limit, :] += dot(probs.astype(bf16), g)
        gkv_ref[:, :, :HD] = (gk[...] * (HD**-0.5)).astype(bf16).reshape(groups, rows, HD)
        gkv_ref[:, :, HD:] = gv[...].astype(bf16).reshape(groups, rows, HD)

    spec = pl.BlockSpec((groups, None, rows, cols), lambda s: (0, s, 0, 0))
    spec_kv = pl.BlockSpec((groups, None, rows, 2 * HD), lambda s: (0, s, 0, 0))
    return pl.pallas_call(
        kernel,
        grid=(streams,),
        out_shape=[
            jax.ShapeDtypeStruct(queries.shape, bf16),
            jax.ShapeDtypeStruct(keyval.shape, bf16),
        ],
        in_specs=[
            pl.BlockSpec(memory_space=pltpu.SMEM),
            spec,
            spec_kv,
            spec,
            pl.BlockSpec((None, heads, length), lambda s: (s, 0, 0)),
        ],
        out_specs=[spec, spec_kv],
        scratch_shapes=[pltpu.VMEM((length, HD), f32)] * 2,
        compiler_params=pltpu.CompilerParams(vmem_limit_bytes=VMEM_LIMIT),
        cost_estimate=pl.CostEstimate(
            flops=10 * streams * heads * length * length * HD,
            bytes_accessed=8 * 1024 * 1024,
            transcendentals=streams * heads * length * length,
        ),
        name="attention_backward",
    )(docs, queries, keyval, grads, lse)


def pack_vectors(vectors):
    sizes = [v.shape[0] for v in vectors]
    lines = -(-sum(sizes) // (PLANE * 8 * 128)) * 8
    pad = PLANE * lines * 128 - sum(sizes)
    return jnp.concatenate(vectors + (jnp.zeros((pad,), f32),)).reshape(PLANE, lines, 128)


def unpack_vectors(packed, vectors):
    flat = packed.reshape(-1)
    sums, at = [], 0
    for v in vectors:
        sums.append(flat[at : at + v.shape[0]])
        at += v.shape[0]
    return sums


def after(value, *earlier):
    return lax.optimization_barrier((value, *earlier))[0]


def line_gather(shard, axis=0):
    return lax.all_gather(shard, "fsdp", axis=axis, tiled=True)


def line_scatter(grad, axis=0):
    return lax.psum_scatter(grad.astype(bf16), "fsdp", scatter_dimension=axis, tiled=True)


def column_weight_grad(grad, groups):
    rows, cols = grad.shape
    return line_scatter(grad.reshape(groups, rows // groups, cols), 1)


def shards(
    tokens,
    doc_starts,
    w_query,
    w_kv,
    w_out,
    w_fc,
    w_proj,
    ln1_gain,
    ln1_bias,
    b_query,
    b_value,
    b_out,
    ln2_gain,
    ln2_bias,
    b_fc,
    b_proj,
    cotangent,
):
    layers = lax.axis_size("fsdp")
    me = lax.axis_index("seq")
    streams, rows, width = tokens.shape
    own = streams * rows
    heads = HEADS // PLANE
    hidden = b_fc.shape[0]
    my_cols = heads * HD
    my_hidden = hidden // PLANE
    total = PLANE * own

    inputs = tokens.reshape(own, width).astype(f32)
    cot_low = cotangent.reshape(own, width)
    cot_full = cot_low.astype(f32)

    wq_pieces, wf_pieces, low_kv = split_weights(w_query, w_fc, w_kv, layers, 1)
    wf = line_gather(wf_pieces, 1).reshape(width, my_hidden)
    wp = line_gather(w_proj)
    my_bq = lax.dynamic_slice_in_dim(b_query, me * my_cols, my_cols, 0).reshape(1, my_cols)
    my_bf = lax.dynamic_slice_in_dim(b_fc, me * my_hidden, my_hidden, 0).reshape(1, my_hidden)
    bkv = jnp.concatenate([jnp.zeros((HD,), f32), b_value]).reshape(1, 2 * HD)

    shifted1, normed1, inverse1 = normalize(inputs, ln1_gain, ln1_bias)
    hidden1, w_kv_all, wq = gather_hidden1(shifted1.astype(bf16), low_kv, wq_pieces, layers, 2)
    wq = wq.reshape(width, my_cols)
    cot_all, wo, queries, keyval, mixed, lse = project_attend(
        doc_starts, hidden1, wq, w_kv_all, my_bq, bkv, cot_low, w_out, streams, heads, layers, 3
    )
    mixed_rows = mixed.reshape(total, my_cols)
    residual = inputs + scatter_attn(mixed_rows, wo, 4) + b_out
    shifted2, normed2, inverse2 = normalize(residual, ln2_gain, ln2_bias)
    hidden2, act_low, slope, grad_w_proj = gather_fc(shifted2.astype(bf16), wf, my_bf, cot_all, 5)
    shard_proj = line_scatter(grad_w_proj)
    grad_b_proj = jnp.sum(cot_full, axis=0)

    grad_hidden2, my_grad_b_fc, grad_w_fc = scatter_fc(cot_all, slope, wp, wf, hidden2, 6)
    fc_pieces = column_weight_grad(grad_w_fc, PLANE)
    back_second, grad_ln2_gain, grad_ln2_bias = normalize_back(
        grad_hidden2, normed2, inverse2, ln2_gain
    )
    grad_residual = cot_full + back_second
    grad_attn = grad_residual.astype(bf16)
    grad_b_out = jnp.sum(grad_attn.astype(f32), axis=0)
    grad_mixed, grad_w_out = gather_out(grad_attn, wo, mixed_rows, 7)
    gq, gkv = attention_backward(
        doc_starts,
        queries,
        keyval,
        after(grad_mixed, shard_proj).reshape(PLANE, streams, rows, my_cols),
        lse,
        heads,
    )
    gq_rows = gq.reshape(total, my_cols)
    gkv_rows = gkv.reshape(total, 2 * HD)
    grad_hidden1, grad_w_query, grad_w_kv, shard_out = scatter_query(
        gq_rows, gkv_rows, wq, w_kv_all, hidden1, grad_w_out, layers, 8
    )
    my_grad_b_query = jnp.sum(gq_rows.astype(f32), axis=0)
    grad_b_value = jnp.sum(gkv_rows[:, HD:].astype(f32), axis=0)
    back_first, grad_ln1_gain, grad_ln1_bias = normalize_back(
        grad_hidden1, normed1, inverse1, ln1_gain
    )
    input_grad = grad_residual + back_first
    zero = jnp.zeros_like
    grad_b_query = lax.dynamic_update_slice_in_dim(zero(b_query), my_grad_b_query, me * my_cols, 0)
    grad_b_fc = lax.dynamic_update_slice_in_dim(
        zero(b_fc), my_grad_b_fc.reshape(-1), me * my_hidden, 0
    )
    vectors = (
        grad_ln1_gain,
        grad_ln1_bias,
        grad_b_query,
        grad_b_value,
        grad_b_out,
        grad_ln2_gain,
        grad_ln2_bias,
        grad_b_fc,
        grad_b_proj,
    )
    mlp, shard_fc, shard_query, shard_kv, packed = scatter_proj(
        act_low,
        wp,
        fc_pieces,
        grad_w_query.reshape(PLANE, layers, -1, my_cols),
        grad_w_kv,
        pack_vectors(vectors),
        layers,
        9,
    )
    output = residual + mlp + b_proj
    sums = unpack_vectors(packed, vectors)
    return (
        output.reshape(streams, rows, width),
        input_grad.reshape(streams, rows, width),
        shard_query.astype(f32),
        shard_kv,
        shard_out,
        shard_fc.astype(f32),
        shard_proj.astype(f32),
        *sums,
    )


def gather_seq(block):
    return lax.all_gather(block, "seq", axis=0, tiled=True)


def scatter_seq(partial):
    return lax.psum_scatter(partial.astype(bf16), "seq", scatter_dimension=0, tiled=True).astype(f32)


def columns_to_rows(part, groups):
    rows = part.shape[0]
    spread = part.reshape(rows, groups, part.shape[1] // groups).transpose(1, 0, 2)
    return lax.all_to_all(spread, "seq", split_axis=0, concat_axis=0, tiled=True)


def column_weight(shard, groups):
    pieces = columns_to_rows(shard, groups)
    full = lax.all_gather(pieces, "fsdp", axis=1, tiled=True)
    return full.reshape(-1, full.shape[2])


def plain_column_grad(grad, groups):
    rows, cols = grad.shape
    kept = lax.psum_scatter(
        grad.astype(bf16).reshape(groups, rows // groups, cols), "fsdp", scatter_dimension=1, tiled=True
    )
    moved = lax.all_to_all(kept, "seq", split_axis=0, concat_axis=0, tiled=True)
    return moved.transpose(1, 0, 2).reshape(moved.shape[1], groups * cols).astype(f32)


def row_weight_grad(grad):
    return lax.psum_scatter(grad.astype(bf16), "fsdp", scatter_dimension=0, tiled=True).astype(f32)


def plain_attend(queries, keyval, starts, groups, streams, rows, heads):
    length = groups * rows
    scale = HD ** (-0.5)
    position = jnp.arange(length, dtype=jnp.int32)
    mixed_list, lse_list = [], []
    for stream in range(streams):
        q = queries[:, stream].reshape(length, heads, HD)
        k = keyval[:, stream, :, :HD].reshape(length, HD)
        v = keyval[:, stream, :, HD:].reshape(length, HD)
        segment = jnp.sum((starts[stream][None, :] <= position[:, None]).astype(jnp.int32), axis=1)
        allowed = (position[None, :] <= position[:, None]) & (segment[None, :] == segment[:, None])
        scores = jnp.einsum("thd,ud->htu", q, k, preferred_element_type=f32) * scale
        scores = jnp.where(allowed[None], scores, -1e30)
        top = jnp.max(scores, axis=-1, keepdims=True)
        lse = top + jnp.log(jnp.sum(jnp.exp(scores - top), axis=-1, keepdims=True))
        probs = jnp.exp(scores - lse).astype(bf16)
        mixed = jnp.einsum("htu,ud->thd", probs, v, preferred_element_type=f32)
        mixed_list.append(mixed.astype(bf16).reshape(groups, rows, heads * HD))
        lse_list.append(lse)
    return jnp.stack(mixed_list, axis=1), lse_list


def plain_attend_back(queries, keyval, grads, lse_list, starts, groups, streams, rows, heads):
    length = groups * rows
    scale = HD ** (-0.5)
    position = jnp.arange(length, dtype=jnp.int32)
    gq_list, gkv_list = [], []
    for stream in range(streams):
        q = queries[:, stream].reshape(length, heads, HD)
        g = grads[:, stream].reshape(length, heads, HD)
        k = keyval[:, stream, :, :HD].reshape(length, HD)
        v = keyval[:, stream, :, HD:].reshape(length, HD)
        segment = jnp.sum((starts[stream][None, :] <= position[:, None]).astype(jnp.int32), axis=1)
        allowed = (position[None, :] <= position[:, None]) & (segment[None, :] == segment[:, None])
        scores = jnp.einsum("thd,ud->htu", q, k, preferred_element_type=f32) * scale
        probs = jnp.exp(jnp.where(allowed[None], scores, -1e30) - lse_list[stream])
        grad_probs = jnp.einsum("thd,ud->htu", g, v, preferred_element_type=f32)
        delta = jnp.sum(probs * grad_probs, axis=-1, keepdims=True)
        gs = (probs * (grad_probs - delta)).astype(bf16)
        gq = jnp.einsum("htu,ud->thd", gs, k, preferred_element_type=f32) * scale
        gk = jnp.einsum("htu,thd->ud", gs, q, preferred_element_type=f32) * scale
        gv = jnp.einsum("htu,thd->ud", probs.astype(bf16), g, preferred_element_type=f32)
        gq_list.append(gq.astype(bf16).reshape(groups, rows, heads * HD))
        gkv_list.append(jnp.concatenate([gk, gv], axis=1).reshape(groups, rows, 2 * HD))
    return jnp.stack(gq_list, axis=1), jnp.stack(gkv_list, axis=1)


def plain_shards(
    tokens,
    doc_starts,
    w_query,
    w_kv,
    w_out,
    w_fc,
    w_proj,
    ln1_gain,
    ln1_bias,
    b_query,
    b_value,
    b_out,
    ln2_gain,
    ln2_bias,
    b_fc,
    b_proj,
    cotangent,
):
    groups = lax.axis_size("seq")
    me = lax.axis_index("seq")
    streams, rows, width = tokens.shape
    own = streams * rows
    heads = HEADS // groups
    hidden = b_fc.shape[0]
    my_cols = heads * HD
    my_hidden = hidden // groups

    wq = column_weight(w_query, groups)
    w_kv_all = gather_seq(lax.all_gather(w_kv, "fsdp", axis=0, tiled=True))
    wo = lax.all_gather(w_out, "fsdp", axis=0, tiled=True)
    wf = column_weight(w_fc, groups)
    wp = lax.all_gather(w_proj, "fsdp", axis=0, tiled=True)
    my_bq = lax.dynamic_slice_in_dim(b_query, me * my_cols, my_cols, 0)
    my_bf = lax.dynamic_slice_in_dim(b_fc, me * my_hidden, my_hidden, 0)

    inputs = tokens.reshape(own, width).astype(f32)
    cot_low = cotangent.reshape(own, width)
    cot_full = cot_low.astype(f32)
    shifted1, normed1, inverse1 = normalize(inputs, ln1_gain, ln1_bias)
    hidden1 = gather_seq(shifted1.astype(bf16))
    queries = (dot(hidden1, wq) + my_bq).astype(bf16).reshape(groups, streams, rows, my_cols)
    value_shift = jnp.concatenate([jnp.zeros((HD,), f32), b_value])
    keyval = (dot(hidden1, w_kv_all) + value_shift).astype(bf16).reshape(groups, streams, rows, 2 * HD)
    mixed, lse = plain_attend(queries, keyval, doc_starts, groups, streams, rows, heads)
    mixed_rows = mixed.reshape(groups * own, my_cols)
    residual = inputs + scatter_seq(dot(mixed_rows, wo)) + b_out
    shifted2, normed2, inverse2 = normalize(residual, ln2_gain, ln2_bias)
    hidden2 = gather_seq(shifted2.astype(bf16))
    cot_all = gather_seq(cot_low)
    pre_act = dot(hidden2, wf) + my_bf
    activated, slope = gelu_pair(pre_act)
    act_low = activated.astype(bf16)
    output = residual + scatter_seq(dot(act_low, wp)) + b_proj

    grad_b_proj = jnp.sum(cot_full, axis=0)
    shard_proj = row_weight_grad(dot_tn(act_low, cot_all))
    grad_pre = (dot_nt(cot_all, wp) * slope).astype(bf16)
    my_grad_b_fc = jnp.sum(grad_pre.astype(f32), axis=0)
    shard_fc = plain_column_grad(dot_tn(hidden2, grad_pre), groups)
    grad_hidden2 = scatter_seq(dot_nt(grad_pre, wf))
    back_second, grad_ln2_gain, grad_ln2_bias = normalize_back(
        grad_hidden2, normed2, inverse2, ln2_gain
    )
    grad_residual = cot_full + back_second
    grad_attn = grad_residual.astype(bf16)
    grad_b_out = jnp.sum(grad_attn.astype(f32), axis=0)
    grad_attn_all = gather_seq(grad_attn)
    shard_out = row_weight_grad(dot_tn(mixed_rows, grad_attn_all))
    grad_mixed = dot_nt(grad_attn_all, wo).astype(bf16).reshape(groups, streams, rows, my_cols)
    gq, gkv = plain_attend_back(
        queries, keyval, grad_mixed, lse, doc_starts, groups, streams, rows, heads
    )
    gq_rows = gq.reshape(groups * own, my_cols)
    gkv_rows = gkv.reshape(groups * own, 2 * HD)
    my_grad_b_query = jnp.sum(gq_rows.astype(f32), axis=0)
    grad_b_value = jnp.sum(gkv_rows[:, HD:], axis=0)
    gkv_low = gkv_rows.astype(bf16)
    shard_query = plain_column_grad(dot_tn(hidden1, gq_rows), groups)
    shard_kv = row_weight_grad(scatter_seq(dot_tn(hidden1, gkv_low)))
    grad_hidden1 = scatter_seq(dot_nt(gq_rows, wq) + dot_nt(gkv_low, w_kv_all))
    back_first, grad_ln1_gain, grad_ln1_bias = normalize_back(
        grad_hidden1, normed1, inverse1, ln1_gain
    )
    input_grad = grad_residual + back_first

    zero = jnp.zeros_like
    grad_b_query = lax.dynamic_update_slice_in_dim(zero(b_query), my_grad_b_query, me * my_cols, 0)
    grad_b_fc = lax.dynamic_update_slice_in_dim(zero(b_fc), my_grad_b_fc, me * my_hidden, 0)
    vectors = (
        grad_ln1_gain,
        grad_ln1_bias,
        grad_b_query,
        grad_b_value,
        grad_b_out,
        grad_ln2_gain,
        grad_ln2_bias,
        grad_b_fc,
        grad_b_proj,
    )
    sums = lax.psum(vectors, ("seq", "fsdp"))
    return (
        output.reshape(streams, rows, width),
        input_grad.reshape(streams, rows, width),
        shard_query,
        shard_kv,
        shard_out,
        shard_fc,
        shard_proj,
        *sums,
    )


def solution(mesh):
    acts = P("fsdp", "seq", None)
    weight = P(("seq", "fsdp"), None)
    return jax.shard_map(
        shards if mesh.shape["seq"] == PLANE else plain_shards,
        mesh=mesh,
        in_specs=(acts, P("fsdp", None)) + (weight,) * 5 + (P(),) * 9 + (acts,),
        out_specs=(acts, acts) + (weight,) * 5 + (P(),) * 9,
        check_vma=False,
    )
```

```python
import functools

import jax
import jax.numpy as jnp
from jax import lax
from jax.experimental import pallas as pl
from jax.experimental.pallas import tpu as pltpu
from jax.sharding import PartitionSpec as P

HEADS = 16
HD = 128

root_two_pi = 0.7978845608028654
cubic_coef = 0.044715
epsilon = 1e-05
f32 = jnp.float32
bf16 = jnp.bfloat16
MESH = pl.DeviceIdType.MESH
ANY = pl.BlockSpec(memory_space=pl.ANY)
WHOLE = pl.BlockSpec(memory_space=pltpu.VMEM)
VMEM_LIMIT = 56 * 1024 * 1024
PLANE = 8


def normalize(values, gain_row, shift_row):
    center = values - jnp.mean(values, axis=-1, keepdims=True)
    inverse = lax.rsqrt(jnp.mean(center * center, axis=-1, keepdims=True) + epsilon)
    normed = center * inverse
    return (normed * gain_row + shift_row, normed, inverse)


def normalize_back(grad_out, normed, inverse, gain_row):
    scaled = grad_out * gain_row
    grad_in = inverse * (
        scaled
        - jnp.mean(scaled, axis=-1, keepdims=True)
        - normed * jnp.mean(scaled * normed, axis=-1, keepdims=True)
    )
    return (grad_in, jnp.sum(grad_out * normed, axis=0), jnp.sum(grad_out, axis=0))


def gelu_pair(inputs):
    tangent = jnp.tanh(root_two_pi * (inputs + cubic_coef * inputs * inputs * inputs))
    activated = 0.5 * inputs * (1.0 + tangent)
    gradient_slope = 0.5 * (1.0 + tangent) + 0.5 * inputs * (
        1.0 - tangent * tangent
    ) * root_two_pi * (1.0 + 3.0 * cubic_coef * inputs * inputs)
    return (activated, gradient_slope)


def dot(a, b):
    return jnp.dot(a, b, preferred_element_type=f32)


def dot_nt(a, b):
    return lax.dot_general(a, b, (((1,), (1,)), ((), ())), preferred_element_type=f32)


def dot_tn(a, b):
    return lax.dot_general(a, b, (((0,), (0,)), ((), ())), preferred_element_type=f32)


def push(src, dst, send, recv, to):
    return pltpu.make_async_remote_copy(
        src_ref=src, dst_ref=dst, send_sem=send, recv_sem=recv, device_id=to, device_id_type=MESH
    )


def sems(*shape):
    return pltpu.SemaphoreType.DMA(shape)


def rows_at(start, size):
    return pl.ds(pl.multiple_of(start, size), size)


class Place:
    def __init__(self):
        me = lax.axis_index("seq")
        self.me = me
        self.core = lax.rem(me, 2)
        x = lax.rem(lax.div(me, 2), 2)
        y = lax.div(me, 4)
        self.sib = me + 1 - 2 * self.core
        self.xn = me + 2 - 4 * x
        self.yn = me + 4 - 8 * y
        self.dg = me + 2 - 4 * x + 4 - 8 * y
        turn = 1 - 2 * self.core
        self.xs, self.ys, self.ds = self.xn + turn, self.yn + turn, self.dg + turn
        self.layer = lax.axis_index("fsdp")

    def plane_peer(self, step):
        return lax.rem(self.me + step, PLANE)

    def line_peer(self, step, layers):
        return lax.rem(self.layer + step, layers)

    def greet(self, whole_plane=False, layers=1):
        barrier = pltpu.get_barrier_semaphore()
        if whole_plane:
            others = [self.plane_peer(step) for step in range(1, PLANE)]
        else:
            others = [self.sib, self.xn, self.yn]
        for other in others:
            pl.semaphore_signal(barrier, inc=1, device_id={"seq": other}, device_id_type=MESH)
        for step in range(1, layers):
            other = self.line_peer(step, layers)
            pl.semaphore_signal(barrier, inc=1, device_id={"fsdp": other}, device_id_type=MESH)
        pl.semaphore_wait(barrier, len(others) + layers - 1)


class Gather:
    sends = 14
    scratch = [sems(14), sems(PLANE, 2)]

    def __init__(self, place, buf, rows, send, recv):
        self.p, self.buf, self.rows, self.half = place, buf, rows, rows // 2
        self.send_sem, self.recv_sem = send, recv
        self.copies = []

    def piece(self, dev, half):
        return self.buf.at[rows_at(dev * self.rows + half * self.half, self.half), :]

    def pair(self, dev):
        return rows_at(lax.div(dev, 2) * (2 * self.rows), 2 * self.rows)

    def send(self, dev, half, to, src=None):
        k = len(self.copies)
        piece = self.piece(dev, half)
        copy = push(
            piece if src is None else src,
            piece,
            self.send_sem.at[k],
            self.recv_sem.at[dev, half],
            {"seq": to},
        )
        copy.start()
        self.copies.append(copy)

    def arrived(self, dev, half):
        piece = self.piece(dev, half)
        push(
            piece, piece, self.send_sem.at[0], self.recv_sem.at[dev, half], {"seq": self.p.sib}
        ).wait_recv()

    def start(self, own):
        p = self.p
        parts = [own.at[pl.ds(h * self.half, self.half), :] for h in range(2)]
        self.send(p.me, 0, p.yn, parts[0])
        self.send(p.me, 1, p.xn, parts[1])
        self.send(p.me, 1, p.yn, parts[1])
        self.send(p.me, 0, p.xn, parts[0])
        for h in range(2):
            self.send(p.me, h, p.sib, parts[h])

    def relay_first(self):
        p = self.p
        self.arrived(p.yn, 0)
        self.send(p.yn, 0, p.xn)
        self.arrived(p.xn, 1)
        self.send(p.xn, 1, p.yn)
        self.send(p.yn, 0, p.sib)
        self.send(p.xn, 1, p.sib)

    def relay_rest(self):
        p = self.p
        self.arrived(p.xn, 0)
        self.send(p.xn, 0, p.sib)
        self.arrived(p.yn, 1)
        self.send(p.yn, 1, p.sib)

    def relay(self):
        self.relay_first()
        self.relay_rest()

    def have(self, dev):
        self.arrived(dev, 0)
        self.arrived(dev, 1)

    def relay_corner(self):
        p = self.p
        for h in range(2):
            self.arrived(p.dg, h)
            self.send(p.dg, h, p.sib)

    def finish(self):
        for copy in self.copies:
            copy.wait_send()


class Scatter:
    def __init__(self, place, rows, part, sib_out, sib_in, boxes, sib_send, sib_recv, send, recv):
        self.p, self.rows, self.half = place, rows, rows // 2
        self.part, self.sib_out, self.sib_in = part, sib_out, sib_in
        self.out_d, self.out_x, self.out_y, self.in_d, self.in_x, self.in_y = boxes
        self.sib_send, self.sib_recv, self.send, self.recv = sib_send, sib_recv, send, recv
        self.copies = []

    @staticmethod
    def scratch(rows, wide):
        return [
            pltpu.VMEM((4, rows, wide), f32),
            pltpu.VMEM((4, rows, wide), bf16),
            pltpu.VMEM((4, rows, wide), bf16),
            *[pltpu.VMEM((rows, wide), bf16)] * 6,
            sems(4),
            sems(4),
            sems(6),
            sems(6),
        ]

    @classmethod
    def take(cls, place, rows, refs):
        return cls(place, rows, refs[0], refs[1], refs[2], refs[3:9], *refs[9:13])

    def swap(self, role, dev, product):
        p = self.p
        chip = lax.div(dev, 2) * (2 * self.rows)

        def store_out(cols, value):
            self.sib_out[role, :, cols] = value.astype(bf16)

        def store_part(cols, value):
            self.part[role, :, cols] = value

        product(
            rows_at(chip + (1 - p.core) * self.rows, self.rows),
            rows_at(chip + p.core * self.rows, self.rows),
            store_out,
            store_part,
        )
        copy = push(
            self.sib_out.at[role],
            self.sib_in.at[role],
            self.sib_send.at[role],
            self.sib_recv.at[role],
            {"seq": p.sib},
        )
        copy.start()
        self.copies.append(copy)
        return copy

    def add_into(self, dst, role, first, size, more=()):
        lines = 32

        @pl.loop(0, size // lines)
        def _(i):
            line = rows_at(first + i * lines, lines)
            value = self.part[role, line, :] + self.sib_in[role, line, :].astype(f32)
            for ref in more:
                value = value + ref[line, :].astype(f32)
            dst[line, :] = value.astype(dst.dtype)

    def ship(self, src, dst, h, k, to):
        lines = pl.ds(h * self.half, self.half)
        copy = push(
            src.at[lines, :], dst.at[lines, :], self.send.at[k], self.recv.at[k], {"seq": to}
        )
        copy.start()
        self.copies.append(copy)
        return copy

    def run(self, product, out_ref, idle=None):
        p, rows, half = self.p, self.rows, self.half
        to_d = self.swap(0, p.dg, product)
        to_x = self.swap(1, p.xn, product)
        to_d.wait_recv()
        self.add_into(self.out_d, 0, 0, rows)
        dx = self.ship(self.out_d, self.in_d, 0, 0, p.xn)
        dy = self.ship(self.out_d, self.in_d, 1, 1, p.yn)
        to_y = self.swap(2, p.yn, product)
        to_x.wait_recv()
        self.add_into(self.out_x, 1, 0, half)
        x0 = self.ship(self.out_x, self.in_x, 0, 2, p.xn)
        to_y.wait_recv()
        self.add_into(self.out_y, 2, half, half)
        y1 = self.ship(self.out_y, self.in_y, 1, 3, p.yn)
        to_me = self.swap(3, p.me, product)
        dy.wait_recv()
        self.add_into(self.out_x, 1, half, half, (self.in_d,))
        x1 = self.ship(self.out_x, self.in_x, 1, 4, p.xn)
        dx.wait_recv()
        self.add_into(self.out_y, 2, 0, half, (self.in_d,))
        y0 = self.ship(self.out_y, self.in_y, 0, 5, p.yn)
        if idle is not None:
            idle()
        to_me.wait_recv()
        x0.wait_recv()
        y0.wait_recv()
        self.add_into(out_ref, 3, 0, half, (self.in_x, self.in_y))
        y1.wait_recv()
        x1.wait_recv()
        self.add_into(out_ref, 3, half, half, (self.in_x, self.in_y))
        for copy in self.copies:
            copy.wait_send()


def params(number, vmem=True):
    return pltpu.CompilerParams(
        collective_id=number,
        has_side_effects=True,
        vmem_limit_bytes=VMEM_LIMIT if vmem else None,
    )


def cost(flops, mib=40):
    return pl.CostEstimate(flops=flops, bytes_accessed=mib * 1024 * 1024, transcendentals=0)


def load(src, dst, sem):
    copy = pltpu.make_async_copy(src, dst, sem)
    copy.start()
    return copy


def split_weights(w_query, w_fc, w_kv, w_out, layers, number):
    arrays, lined = (w_query, w_fc), (w_kv, w_out)

    def kernel(wq_ref, wf_ref, kv_ref, wo_ref, wq_out, wf_out, kv_out, wo_out, *refs):
        send, recv, zsend, zrecv, local = refs
        p = Place()
        ins, outs = (wq_ref, wf_ref), (wq_out, wf_out)
        line_ins = (kv_ref, wo_ref)
        mine = [
            out.at[rows_at(p.layer * src.shape[0], src.shape[0]), :]
            for src, out in zip(line_ins, (kv_out, wo_out))
        ]

        def block(i, dev):
            cols = ins[i].shape[1] // PLANE
            return ins[i].at[:, rows_at(dev * cols, cols)]

        own = []
        for i in range(2):
            own.append(load(line_ins[i], mine[i], local.at[2 + i]))
            own.append(load(block(i, p.me), outs[i].at[p.me], local.at[i]))
        p.greet(True, layers)
        copies = []
        for i in range(2):
            for step in range(1, layers):
                to = p.line_peer(step, layers)
                copies.append(
                    push(
                        line_ins[i], mine[i], zsend.at[i, step], zrecv.at[i, step], {"fsdp": to}
                    )
                )
                copies[-1].start()
        for i in range(2):
            for step in range(1, PLANE):
                to = p.plane_peer(step)
                copies.append(
                    push(
                        block(i, to),
                        outs[i].at[p.me],
                        send.at[i, step],
                        recv.at[i, step],
                        {"seq": to},
                    )
                )
                copies[-1].start()
        for copy in own + copies:
            copy.wait()

    return pl.pallas_call(
        kernel,
        out_shape=[
            jax.ShapeDtypeStruct((PLANE, a.shape[0], a.shape[1] // PLANE), a.dtype)
            for a in arrays
        ]
        + [jax.ShapeDtypeStruct((layers * a.shape[0], a.shape[1]), a.dtype) for a in lined],
        in_specs=[ANY] * 4,
        out_specs=[ANY] * 4,
        scratch_shapes=[
            sems(2, PLANE),
            sems(2, PLANE),
            sems(2, layers),
            sems(2, layers),
            sems(4),
        ],
        compiler_params=params(number, False),
        name="split_weights",
    )(w_query, w_fc, w_kv, w_out)


def gather_hidden1(hidden1, low_kv, wq_pieces, layers, number):
    def kernel(h_ref, kv_ref, wq_ref, h_all, kv_all, wq_all, *refs):
        hs, hr, ks, kr, zsend, zrecv, local = refs
        p = Place()
        h_rows, kv_rows = h_ref.shape[0], kv_ref.shape[0]
        wq_mine = wq_all.at[:, p.layer]
        own = [
            load(h_ref, h_all.at[rows_at(p.me * h_rows, h_rows), :], local.at[0]),
            load(kv_ref, kv_all.at[rows_at(p.me * kv_rows, kv_rows), :], local.at[1]),
            load(wq_ref, wq_mine, local.at[2]),
        ]
        p.greet(False, layers)
        kv = Gather(p, kv_all, kv_rows, ks, kr)
        h = Gather(p, h_all, h_rows, hs, hr)
        kv.start(kv_ref)
        h.start(h_ref)
        across = []
        for step in range(1, layers):
            to = p.line_peer(step, layers)
            across.append(push(wq_ref, wq_mine, zsend.at[step], zrecv.at[step], {"fsdp": to}))
            across[-1].start()
        kv.relay()
        kv.relay_corner()
        h.relay()
        h.relay_corner()
        for g in (kv, h):
            for dev in (p.sib, p.xs, p.ys, p.ds):
                g.have(dev)
            g.finish()
        for copy in own + across:
            copy.wait()

    groups, piece_rows, cols = wq_pieces.shape
    return pl.pallas_call(
        kernel,
        out_shape=[
            jax.ShapeDtypeStruct((PLANE * hidden1.shape[0], hidden1.shape[1]), bf16),
            jax.ShapeDtypeStruct((PLANE * low_kv.shape[0], low_kv.shape[1]), bf16),
            jax.ShapeDtypeStruct((groups, layers, piece_rows, cols), bf16),
        ],
        in_specs=[ANY] * 3,
        out_specs=[ANY] * 3,
        scratch_shapes=Gather.scratch * 2 + [sems(layers), sems(layers), sems(3)],
        compiler_params=params(number, False),
        name="gather_hidden1",
    )(hidden1, low_kv, wq_pieces)


def project_attend(docs, hidden1, wq, w_kv, bq, bkv, cot, streams, heads, number):
    total, depth = hidden1.shape
    cols, kv_cols = wq.shape[1], w_kv.shape[1]
    rows = total // PLANE // streams
    length = PLANE * rows
    block = min(QROWS, length)
    chunk = total // 4

    def kernel(docs_ref, h_ref, wq_ref, wkv_ref, bq_ref, bkv_ref, cot_ref, *refs):
        cot_all, q_out, kv_out, mixed_out, lse_ref = refs[:5]
        h_buf, wq_buf, wkv_buf, q_buf, kv_buf, mixed_buf, send, recv, local = refs[5:]
        p = Place()
        own_rows = cot_ref.shape[0]

        def fetch(k):
            return load(
                h_ref.at[pl.ds(k * chunk, chunk), :], h_buf.at[k % 2], local.at[k % 2]
            )

        fetches = [fetch(0)]
        weights = [load(wq_ref, wq_buf, local.at[2]), load(wkv_ref, wkv_buf, local.at[3])]
        own = load(cot_ref, cot_all.at[rows_at(p.me * own_rows, own_rows), :], local.at[4])
        p.greet()
        g = Gather(p, cot_all, own_rows, send, recv)
        g.start(cot_ref)
        for copy in weights:
            copy.wait()
        per = chunk // (streams * rows)
        for k in range(4):
            fetches[k].wait()
            if k < 3:
                fetches.append(fetch(k + 1))
            where = pl.ds(k * per, per)
            q = dot(h_buf[k % 2], wq_buf[...]) + bq_ref[...]
            q_buf[where] = q.astype(bf16).reshape(per, streams, rows, cols)
            kv = dot(h_buf[k % 2], wkv_buf[...]) + bkv_ref[...]
            kv_buf[where] = kv.astype(bf16).reshape(per, streams, rows, kv_cols)
        stores = [load(q_buf, q_out, local.at[5]), load(kv_buf, kv_out, local.at[6])]
        g.relay_first()
        for stream in range(streams):
            attend_stream(
                docs_ref,
                stream,
                q_buf.at[:, stream],
                kv_buf.at[:, stream],
                mixed_buf.at[:, stream],
                lse_ref.at[stream],
                block,
                heads,
            )
        stores.append(load(mixed_buf, mixed_out, local.at[7]))
        g.relay_rest()
        g.relay_corner()
        for dev in (p.sib, p.xs, p.ys, p.ds):
            g.have(dev)
        g.finish()
        own.wait()
        for copy in stores:
            copy.wait()

    q_shape = (PLANE, streams, rows, cols)
    kv_shape = (PLANE, streams, rows, kv_cols)
    return pl.pallas_call(
        kernel,
        out_shape=[
            jax.ShapeDtypeStruct((PLANE * cot.shape[0], cot.shape[1]), bf16),
            jax.ShapeDtypeStruct(q_shape, bf16),
            jax.ShapeDtypeStruct(kv_shape, bf16),
            jax.ShapeDtypeStruct(q_shape, bf16),
            jax.ShapeDtypeStruct((streams, heads, length), f32),
        ],
        in_specs=[pl.BlockSpec(memory_space=pltpu.SMEM)] + [ANY] * 3 + [WHOLE] * 2 + [ANY],
        out_specs=[ANY] * 4 + [WHOLE],
        scratch_shapes=[
            pltpu.VMEM((2, chunk, depth), bf16),
            pltpu.VMEM(wq.shape, bf16),
            pltpu.VMEM(w_kv.shape, bf16),
            pltpu.VMEM(q_shape, bf16),
            pltpu.VMEM(kv_shape, bf16),
            pltpu.VMEM(q_shape, bf16),
        ]
        + Gather.scratch
        + [sems(8)],
        compiler_params=params(number),
        cost_estimate=cost(2 * total * depth * (cols + kv_cols)),
        name="project_attend",
    )(docs, hidden1, wq, w_kv, bq, bkv, cot)


def gather_fc(hidden2, wf, bf, cot_all, number):
    rows, depth = hidden2.shape
    wide = wf.shape[1]
    total = PLANE * rows
    out_wide = cot_all.shape[1]
    tile = 256

    def kernel(own_ref, w_ref, b_ref, cot_ref, all_ref, act_ref, slope_ref, dw_ref, *refs):
        buf, w_buf, act, slope, cot, acc, dw, send, recv, local = refs
        p = Place()
        load_own = load(own_ref, buf.at[rows_at(p.me * rows, rows), :], local.at[0])
        load_w = load(w_ref, w_buf, local.at[1])
        p.greet()
        g = Gather(p, buf, rows, send, recv)
        g.start(own_ref)
        stores = []
        cots = {}

        def fetch(k, dev):
            cots[k] = load(cot_ref.at[g.pair(dev), :], cot.at[k % 2], local.at[2 + k % 2])

        def work(k, dev):
            block = g.pair(dev)
            stores.append(load(buf.at[block, :], all_ref.at[block, :], local.at[4 + 3 * k]))

            @pl.loop(0, wide // tile)
            def _(j):
                cols = rows_at(j * tile, tile)
                acc_fc = dot(buf[block, :], w_buf[:, cols]) + b_ref[:, cols]
                activated, gradient = gelu_pair(acc_fc)
                act[block, cols] = activated.astype(bf16)
                slope[block, cols] = gradient.astype(bf16)

            for i, (src, dst) in enumerate(((act, act_ref), (slope, slope_ref))):
                stores.append(
                    load(src.at[block, :], dst.at[block, :], local.at[4 + 3 * k + 1 + i])
                )

        def grads(k, dev):
            block = g.pair(dev)
            cots[k].wait()

            @pl.loop(0, wide // tile)
            def _(j):
                cols = rows_at(j * tile, tile)
                term = dot_tn(act[block, cols], cot[k % 2])
                if k == 0:
                    acc[cols, :] = term
                elif k < 3:
                    acc[cols, :] += term
                else:
                    dw[cols, :] = (acc[cols, :] + term).astype(bf16)

        fetch(0, p.me)
        fetch(1, p.xn)
        load_own.wait()
        load_w.wait()
        g.have(p.sib)
        work(0, p.me)
        g.relay_first()
        grads(0, p.me)
        fetch(2, p.yn)
        g.relay_rest()
        g.have(p.xs)
        work(1, p.xn)
        g.have(p.ys)
        work(2, p.yn)
        grads(1, p.xn)
        fetch(3, p.dg)
        g.relay_corner()
        grads(2, p.yn)
        g.have(p.ds)
        work(3, p.dg)
        grads(3, p.dg)
        stores.append(load(dw, dw_ref, local.at[16]))
        g.finish()
        for copy in stores:
            copy.wait()

    return pl.pallas_call(
        kernel,
        out_shape=[
            jax.ShapeDtypeStruct((total, depth), bf16),
            jax.ShapeDtypeStruct((total, wide), bf16),
            jax.ShapeDtypeStruct((total, wide), bf16),
            jax.ShapeDtypeStruct((wide, out_wide), bf16),
        ],
        in_specs=[ANY, ANY, WHOLE, ANY],
        out_specs=[ANY] * 4,
        scratch_shapes=[
            pltpu.VMEM((total, depth), bf16),
            pltpu.VMEM(wf.shape, bf16),
            pltpu.VMEM((total, wide), bf16),
            pltpu.VMEM((total, wide), bf16),
            pltpu.VMEM((2, 2 * rows, out_wide), bf16),
            pltpu.VMEM((wide, out_wide), f32),
            pltpu.VMEM((wide, out_wide), bf16),
        ]
        + Gather.scratch
        + [sems(17)],
        compiler_params=params(number),
        cost_estimate=cost(4 * total * depth * wide),
        name="gather_fc",
    )(hidden2, wf, bf, cot_all)


def gather_out(grad_attn, wo, mixed, number):
    rows, depth = grad_attn.shape
    wide = wo.shape[0]
    total = PLANE * rows

    def kernel(own_ref, w_ref, mixed_ref, gm_ref, dw_ref, *refs):
        buf, w_buf, mixed_buf, gm, acc, dw, send, recv, local = refs
        p = Place()
        load_own = load(own_ref, buf.at[rows_at(p.me * rows, rows), :], local.at[0])
        loads = [load(w_ref, w_buf, local.at[1]), load(mixed_ref, mixed_buf, local.at[2])]
        p.greet()
        g = Gather(p, buf, rows, send, recv)
        g.start(own_ref)

        def work(dev):
            block = g.pair(dev)
            gm[block, :] = dot_nt(buf[block, :], w_buf[...]).astype(bf16)

        def grads(k, dev):
            block = g.pair(dev)
            term = dot_tn(mixed_buf[block, :], buf[block, :])
            if k == 0:
                acc[...] = term
            elif k < 3:
                acc[...] += term
            else:
                dw[...] = (acc[...] + term).astype(bf16)

        load_own.wait()
        for copy in loads:
            copy.wait()
        g.have(p.sib)
        work(p.me)
        grads(0, p.me)
        g.relay()
        g.have(p.xs)
        work(p.xn)
        g.have(p.ys)
        work(p.yn)
        grads(1, p.xn)
        g.relay_corner()
        grads(2, p.yn)
        g.have(p.ds)
        work(p.dg)
        store = load(gm, gm_ref, local.at[3])
        grads(3, p.dg)
        store_dw = load(dw, dw_ref, local.at[4])
        g.finish()
        store.wait()
        store_dw.wait()

    return pl.pallas_call(
        kernel,
        out_shape=[
            jax.ShapeDtypeStruct((total, wide), bf16),
            jax.ShapeDtypeStruct((wide, depth), bf16),
        ],
        in_specs=[ANY] * 3,
        out_specs=[ANY] * 2,
        scratch_shapes=[
            pltpu.VMEM((total, depth), bf16),
            pltpu.VMEM(wo.shape, bf16),
            pltpu.VMEM(mixed.shape, bf16),
            pltpu.VMEM((total, wide), bf16),
            pltpu.VMEM((wide, depth), f32),
            pltpu.VMEM((wide, depth), bf16),
        ]
        + Gather.scratch
        + [sems(5)],
        compiler_params=params(number),
        cost_estimate=cost(4 * total * depth * wide),
        name="gather_out",
    )(grad_attn, wo, mixed)


TILE = 512


def scatter_attn(a, weight, number):
    total, depth = a.shape
    rows = total // PLANE
    wide = weight.shape[1]

    def kernel(a_ref, w_ref, out_ref, a_buf, w_buf, *refs):
        s, local = refs[:13], refs[13]
        p = Place()
        loads = [load(a_ref, a_buf, local.at[0]), load(w_ref, w_buf, local.at[1])]
        p.greet()
        for copy in loads:
            copy.wait()
        Scatter.take(p, rows, s).run(plain_product(a_buf, w_buf), out_ref)

    return pl.pallas_call(
        kernel,
        out_shape=jax.ShapeDtypeStruct((rows, wide), f32),
        in_specs=[ANY] * 2,
        out_specs=WHOLE,
        scratch_shapes=[pltpu.VMEM(a.shape, bf16), pltpu.VMEM(weight.shape, bf16)]
        + Scatter.scratch(rows, wide)
        + [sems(2)],
        compiler_params=params(number),
        cost_estimate=cost(2 * total * depth * wide),
        name="scatter_attn",
    )(a, weight)


def plain_product(a_buf, w_buf):
    def product(theirs, ours, store_out, store_part):
        @pl.loop(0, w_buf.shape[1] // TILE)
        def _(j):
            cols = rows_at(j * TILE, TILE)
            store_out(cols, dot(a_buf[theirs, :], w_buf[:, cols]))
            store_part(cols, dot(a_buf[ours, :], w_buf[:, cols]))

    return product


def scatter_fc(cot_all, slope, wp, wf, hidden2, number):
    total, depth = cot_all.shape
    rows = total // PLANE
    wide = wp.shape[0]
    tile = 256

    def kernel(cot_ref, slope_ref, wp_ref, wf_ref, h_ref, out_ref, bias_ref, dw_ref, *refs):
        cot, slopes, wp_buf, wf_buf, gp, h_buf, dw_buf = refs[:7]
        s = refs[7:20]
        (local,) = refs[20:]
        p = Place()
        order = (p.dg, p.xn, p.yn, p.me)

        def chip(dev):
            return rows_at(lax.div(dev, 2) * (2 * rows), 2 * rows)

        def fetch(k):
            here = chip(order[k])
            return (
                load(cot_ref.at[here, :], cot.at[k % 2], local.at[k % 2]),
                load(slope_ref.at[here, :], slopes.at[k % 2], local.at[2 + k % 2]),
            )

        fetches = [fetch(0)]
        load_wp = load(wp_ref, wp_buf, local.at[4])
        load_wf = load(wf_ref, wf_buf, local.at[5])
        bias_ref[...] = jnp.zeros_like(bias_ref)
        p.greet()
        load_wp.wait()
        count = []

        def product(theirs, ours, store_out, store_part):
            k = len(count)
            count.append(k)
            for copy in fetches[k]:
                copy.wait()
            if k < 3:
                fetches.append(fetch(k + 1))
            here = chip(order[k])

            @pl.loop(0, wide // tile)
            def _(j):
                cols = rows_at(j * tile, tile)
                grad_act = dot_nt(cot[k % 2], wp_buf[cols, :])
                grad_pre = (grad_act * slopes[k % 2, :, cols].astype(f32)).astype(bf16)
                gp[here, cols] = grad_pre
                bias_ref[:, cols] += jnp.sum(grad_pre.astype(f32), axis=0, keepdims=True)

            if k == 0:
                load_wf.wait()

            @pl.loop(0, depth // TILE)
            def _(j):
                cols = rows_at(j * TILE, TILE)
                store_out(cols, dot_nt(gp[theirs, :], wf_buf[cols, :]))
                store_part(cols, dot_nt(gp[ours, :], wf_buf[cols, :]))

        steps = depth // tile

        def h_fetch(i):
            return load(
                h_ref.at[:, pl.ds(i * tile, tile)], h_buf.at[i % 2], local.at[6 + i % 2]
            )

        def idle():
            tiles = [h_fetch(0)]
            stores = []
            for i in range(steps):
                tiles[i].wait()
                if i + 1 < steps:
                    tiles.append(h_fetch(i + 1))
                if i >= 2:
                    stores[i - 2].wait()
                dw_buf[i % 2] = dot_tn(h_buf[i % 2], gp[...]).astype(bf16)
                stores.append(
                    load(
                        dw_buf.at[i % 2],
                        dw_ref.at[pl.ds(i * tile, tile), :],
                        local.at[8 + i % 2],
                    )
                )
            for copy in stores[-2:]:
                copy.wait()

        Scatter.take(p, rows, s).run(product, out_ref, idle)

    return pl.pallas_call(
        kernel,
        out_shape=[
            jax.ShapeDtypeStruct((rows, depth), f32),
            jax.ShapeDtypeStruct((1, wide), f32),
            jax.ShapeDtypeStruct((depth, wide), bf16),
        ],
        in_specs=[ANY] * 5,
        out_specs=[WHOLE, WHOLE, ANY],
        scratch_shapes=[
            pltpu.VMEM((2, 2 * rows, depth), bf16),
            pltpu.VMEM((2, 2 * rows, wide), bf16),
            pltpu.VMEM(wp.shape, bf16),
            pltpu.VMEM(wf.shape, bf16),
            pltpu.VMEM((total, wide), bf16),
            pltpu.VMEM((2, total, tile), bf16),
            pltpu.VMEM((2, tile, wide), bf16),
        ]
        + Scatter.scratch(rows, depth)
        + [sems(10)],
        compiler_params=params(number),
        cost_estimate=cost(6 * total * depth * wide),
        name="scatter_fc",
    )(cot_all, slope, wp, wf, hidden2)


class LineSum:
    def __init__(self, place, block, box, layers, send, recv):
        self.copies = []
        self.box = box
        for step in range(1, layers):
            to = place.line_peer(step, layers)
            copy = push(block(to), box.at[step - 1], send.at[step], recv.at[step], {"fsdp": to})
            copy.start()
            self.copies.append(copy)

    def arrived(self):
        for copy in self.copies:
            copy.wait_recv()

    def total(self, own, where):
        value = own.astype(f32)
        for k in range(len(self.copies)):
            value = value + self.box[(k, *where)].astype(f32)
        return value

    def finish(self):
        for copy in self.copies:
            copy.wait_send()


def scatter_query(gq, gkv, wq, w_kv, hidden1, grad_w_out, layers, number):
    total, cols = gq.shape
    kv_cols = gkv.shape[1]
    rows = total // PLANE
    depth = wq.shape[0]
    part_rows = depth // PLANE
    line_rows = part_rows // layers
    out_rows = grad_w_out.shape[0] // layers
    out_wide = grad_w_out.shape[1]

    def kernel(gq_ref, gkv_ref, wq_ref, wkv_ref, h_ref, dwo_ref, *refs):
        out_ref, dwq_ref, dwkv_ref, dwo_out = refs[:4]
        g_buf, wq_buf, wkv_buf, h_buf, dwq_buf, dwq_box, dkv, box, dwo_own, dwo_box = refs[4:14]
        s = refs[14:27]
        ksend, krecv, zsend, zrecv, qsend, qrecv, local = refs[27:]
        p = Place()

        def dwo_block(layer):
            return dwo_ref.at[rows_at(layer * out_rows, out_rows), :]

        load_dwo = load(dwo_block(p.layer), dwo_own, local.at[7])
        q_part, kv_part = pl.ds(0, cols), pl.ds(cols, kv_cols)
        loads = [
            load(gq_ref, g_buf.at[:, q_part], local.at[0]),
            load(gkv_ref, g_buf.at[:, kv_part], local.at[1]),
            load(wq_ref, wq_buf, local.at[2]),
            load(wkv_ref, wkv_buf, local.at[3]),
        ]

        def h_fetch(i):
            dev = p.plane_peer((i + 1) % PLANE)
            return load(
                h_ref.at[:, rows_at(dev * part_rows, part_rows)],
                h_buf.at[i % 2],
                local.at[4 + i % 2],
            )

        tiles = [h_fetch(0)]
        p.greet(True, layers)
        line = LineSum(p, dwo_block, dwo_box, layers, zsend, zrecv)
        for copy in loads:
            copy.wait()

        def product(theirs, ours, store_out, store_part):
            @pl.loop(0, depth // TILE)
            def _(j):
                where = rows_at(j * TILE, TILE)
                for rows_of, store in ((theirs, store_out), (ours, store_part)):
                    store(
                        where,
                        dot_nt(g_buf[rows_of, q_part], wq_buf[where, :])
                        + dot_nt(g_buf[rows_of, kv_part], wkv_buf[where, :]),
                    )

        sent = []
        lines_q = []

        def idle():
            for i in range(PLANE):
                step = (i + 1) % PLANE
                dev = p.plane_peer(step)
                tiles[i].wait()
                if i + 1 < PLANE:
                    tiles.append(h_fetch(i + 1))
                term = dot_tn(h_buf[i % 2], g_buf[...]).astype(bf16)
                dwq_buf[dev] = term[:, :cols].reshape(layers, line_rows, cols)
                dkv[step] = term[:, cols:]
                if step:
                    copy = push(
                        dkv.at[step], box.at[step], ksend.at[step], krecv.at[step], {"seq": dev}
                    )
                    copy.start()
                    sent.append(copy)
            lines_q.append(
                LineSum(p, lambda layer: dwq_buf.at[:, layer], dwq_box, layers, qsend, qrecv)
            )

        Scatter.take(p, rows, s).run(product, out_ref, idle)
        sum_kv = dkv[0].astype(f32)
        for i, copy in enumerate(sent):
            copy.wait_recv()
            sum_kv = sum_kv + box[i + 1].astype(f32)
        dwkv_ref[...] = sum_kv.astype(bf16)
        load_dwo.wait()
        line.arrived()

        @pl.loop(0, out_rows // 16)
        def _(i):
            lines = rows_at(i * 16, 16)
            dwo_out[lines, :] = line.total(dwo_own[lines, :], (lines, slice(None)))

        (line_q,) = lines_q
        line_q.arrived()

        @pl.loop(0, PLANE)
        def _(i):
            dwq_ref[i] = line_q.total(dwq_buf[i, p.layer], (i,)).astype(bf16)

        for copy in sent:
            copy.wait_send()
        line.finish()
        line_q.finish()

    return pl.pallas_call(
        kernel,
        out_shape=[
            jax.ShapeDtypeStruct((rows, depth), f32),
            jax.ShapeDtypeStruct((PLANE, line_rows, cols), bf16),
            jax.ShapeDtypeStruct((part_rows, kv_cols), bf16),
            jax.ShapeDtypeStruct((out_rows, out_wide), f32),
        ],
        in_specs=[ANY] * 6,
        out_specs=[WHOLE] * 4,
        scratch_shapes=[
            pltpu.VMEM((total, cols + kv_cols), bf16),
            pltpu.VMEM(wq.shape, bf16),
            pltpu.VMEM(w_kv.shape, bf16),
            pltpu.VMEM((2, total, part_rows), bf16),
            pltpu.VMEM((PLANE, layers, line_rows, cols), bf16),
            pltpu.VMEM((layers - 1, PLANE, line_rows, cols), bf16),
            pltpu.VMEM((PLANE, part_rows, kv_cols), bf16),
            pltpu.VMEM((PLANE, part_rows, kv_cols), bf16),
            pltpu.VMEM((out_rows, out_wide), bf16),
            pltpu.VMEM((layers - 1, out_rows, out_wide), bf16),
        ]
        + Scatter.scratch(rows, depth)
        + [sems(PLANE)] * 2
        + [sems(layers)] * 4
        + [sems(8)],
        compiler_params=params(number),
        cost_estimate=cost(4 * total * depth * (cols + kv_cols)),
        name="scatter_query",
    )(gq, gkv, wq, w_kv, hidden1, grad_w_out)


def last_exchange(vector, fc_pieces, q_pieces, grad_w_kv, layers, number):
    lines = vector.shape[1]
    pieces = (fc_pieces, q_pieces)
    kv_rows, kv_cols = grad_w_kv.shape[0] // layers, grad_w_kv.shape[1]

    def kernel(vec, kv_ref, fc_ref, q_ref, vec_out, kv_out, fc_out, q_out, *refs):
        box, plane_sum, zbox, kv_box = refs[:4]
        vsend, vrecv, zsend, zrecv, kzsend, kzrecv, gsend, grecv, send, recv, local = refs[4:]
        p = Place()

        def kv_block(layer):
            return kv_ref.at[rows_at(layer * kv_rows, kv_rows), :]

        p.greet(True, layers)
        first, copies = [], []
        for step in range(1, PLANE):
            to = p.plane_peer(step)
            copy = push(vec.at[to], box.at[step], vsend.at[step], vrecv.at[step], {"seq": to})
            copy.start()
            first.append(copy)
        line_kv = LineSum(p, kv_block, kv_box, layers, kzsend, kzrecv)
        for i, (src, out) in enumerate(((fc_ref, fc_out), (q_ref, q_out))):
            cols = src.shape[2]
            place = out.at[:, rows_at(p.me * cols, cols)]
            copies.append(load(src.at[p.me], place, local.at[i]))
            for step in range(1, PLANE):
                to = p.plane_peer(step)
                copies.append(
                    push(src.at[to], place, send.at[i, step], recv.at[i, step], {"seq": to})
                )
                copies[-1].start()
        total = vec[p.me]
        for step in range(1, PLANE):
            first[step - 1].wait_recv()
            total = total + box[step]
        plane_sum[...] = total
        zbox[0] = total
        across = []
        for step in range(1, layers):
            to = p.line_peer(step, layers)
            copy = push(plane_sum, zbox.at[step], zsend.at[step], zrecv.at[step], {"fsdp": to})
            copy.start()
            across.append(copy)
        line_kv.arrived()
        kv_out[...] = line_kv.total(kv_ref[rows_at(p.layer * kv_rows, kv_rows), :], ())
        for copy in across:
            copy.wait_recv()
        total = None
        for k in range(layers):
            term = zbox[lax.rem(p.layer - k + layers, layers)]
            total = term if total is None else total + term
        vec_out[p.me] = total
        for step in range(1, PLANE):
            to = p.plane_peer(step)
            mine = vec_out.at[p.me]
            copies.append(push(mine, mine, gsend.at[step], grecv.at[step], {"seq": to}))
            copies[-1].start()
        for copy in copies:
            copy.wait()
        for copy in first + across:
            copy.wait_send()
        line_kv.finish()

    return pl.pallas_call(
        kernel,
        out_shape=[
            jax.ShapeDtypeStruct(vector.shape, f32),
            jax.ShapeDtypeStruct((kv_rows, kv_cols), f32),
        ]
        + [jax.ShapeDtypeStruct((a.shape[1], PLANE * a.shape[2]), a.dtype) for a in pieces],
        in_specs=[WHOLE, WHOLE, ANY, ANY],
        out_specs=[WHOLE, WHOLE, ANY, ANY],
        scratch_shapes=[
            pltpu.VMEM((PLANE, lines, 128), f32),
            pltpu.VMEM((lines, 128), f32),
            pltpu.VMEM((layers, lines, 128), f32),
            pltpu.VMEM((layers - 1, kv_rows, kv_cols), bf16),
        ]
        + [sems(PLANE)] * 2
        + [sems(layers)] * 4
        + [sems(PLANE)] * 2
        + [sems(2, PLANE)] * 2
        + [sems(2)],
        compiler_params=params(number, False),
        name="last_exchange",
    )(vector, grad_w_kv, *pieces)


def starts_of(docs, stream, positions):
    start = jnp.zeros_like(positions)
    for j in range(docs.shape[1]):
        here = docs[stream, j]
        start = jnp.maximum(start, jnp.where(here <= positions, here, 0))
    return start


def masked_scores(docs, stream, keys, q, first, limit):
    scores = dot_nt(keys, q) * (HD**-0.5)
    t = first + lax.broadcasted_iota(jnp.int32, (1, q.shape[0]), 1)
    u = lax.broadcasted_iota(jnp.int32, scores.shape, 0)
    return scores, (u >= starts_of(docs, stream, t)) & (u <= t)


QROWS = 256


def attend_stream(docs, stream, q_ref, kv_ref, mixed_ref, lse_ref, block, heads):
    groups, rows, cols = q_ref.shape
    length = groups * rows
    kv = kv_ref[...].reshape(length, 2 * HD)
    keys = kv[:, :HD]
    values_t = kv[:, HD:].T
    per = block // rows
    for b in range(length // block):
        limit = (b + 1) * block
        q_rows = q_ref[b * per : (b + 1) * per].reshape(block, cols)
        for h in range(heads):
            q = q_rows[:, h * HD : (h + 1) * HD]
            scores, allowed = masked_scores(docs, stream, keys[:limit], q, b * block, limit)
            scores = jnp.where(allowed, scores, -1e30)
            top = jnp.max(scores, axis=0, keepdims=True)
            weights = jnp.exp(scores - top)
            total = jnp.sum(weights, axis=0, keepdims=True)
            mixed = dot(values_t[:, :limit], weights.astype(bf16)) / total
            mixed_ref[b * per : (b + 1) * per, :, h * HD : (h + 1) * HD] = (
                mixed.T.astype(bf16).reshape(per, rows, HD)
            )
            lse_ref[h : h + 1, b * block : (b + 1) * block] = top + jnp.log(total)


def attend_stream_back(docs, stream, q_ref, kv_ref, g_ref, lse_ref, gq_ref, gkv_ref, gk, gv, heads):
    groups, rows, cols = q_ref.shape
    length = groups * rows
    block = min(QROWS, length)
    kv = kv_ref[...].reshape(length, 2 * HD)
    keys, values = kv[:, :HD], kv[:, HD:]
    keys_t = keys.T
    per = block // rows
    gk[...] = jnp.zeros_like(gk)
    gv[...] = jnp.zeros_like(gv)
    for b in range(length // block):
        limit = (b + 1) * block
        q_rows = q_ref[b * per : (b + 1) * per].reshape(block, cols)
        g_rows = g_ref[b * per : (b + 1) * per].reshape(block, cols)
        for h in range(heads):
            q = q_rows[:, h * HD : (h + 1) * HD]
            g = g_rows[:, h * HD : (h + 1) * HD]
            scores, allowed = masked_scores(docs, stream, keys[:limit], q, b * block, limit)
            shift = lse_ref[h : h + 1, b * block : (b + 1) * block]
            probs = jnp.where(allowed, jnp.exp(scores - shift), 0.0)
            grad_probs = dot_nt(values[:limit], g)
            weighted = probs * grad_probs
            delta = jnp.sum(weighted, axis=0, keepdims=True)
            grad_scores = (weighted - probs * delta).astype(bf16)
            gq = dot(keys_t[:, :limit], grad_scores) * (HD**-0.5)
            gq_ref[b * per : (b + 1) * per, :, h * HD : (h + 1) * HD] = (
                gq.T.astype(bf16).reshape(per, rows, HD)
            )
            gk[:limit, :] += dot(grad_scores, q)
            gv[:limit, :] += dot(probs.astype(bf16), g)
    gkv_ref[:, :, :HD] = (gk[...] * (HD**-0.5)).astype(bf16).reshape(groups, rows, HD)
    gkv_ref[:, :, HD:] = gv[...].astype(bf16).reshape(groups, rows, HD)


def attend_back_scatter_proj(docs, queries, keyval, grads, lse, act, wp, heads, number):
    groups, streams, rows, cols = queries.shape
    length = groups * rows
    total, depth = act.shape
    own = total // PLANE
    wide = wp.shape[1]

    def kernel(docs_ref, q_ref, kv_ref, g_ref, lse_ref, act_ref, wp_ref, *refs):
        gq_out, gkv_out, out_ref = refs[:3]
        a_buf, w_buf, q_buf, kv_buf, g_buf, gq_buf, gkv_buf, gk, gv = refs[3:12]
        s, local = refs[12:25], refs[25]
        p = Place()
        loads = [load(act_ref, a_buf, local.at[0]), load(wp_ref, w_buf, local.at[1])]
        ins = [
            load(q_ref, q_buf, local.at[2]),
            load(kv_ref, kv_buf, local.at[3]),
            load(g_ref, g_buf, local.at[4]),
        ]
        p.greet()
        for copy in loads:
            copy.wait()

        def idle(stream):
            if stream == 0:
                for copy in ins:
                    copy.wait()
            attend_stream_back(
                docs_ref,
                stream,
                q_buf.at[:, stream],
                kv_buf.at[:, stream],
                g_buf.at[:, stream],
                lse_ref.at[stream],
                gq_buf.at[:, stream],
                gkv_buf.at[:, stream],
                gk,
                gv,
                heads,
            )

        def idle_all():
            for stream in range(streams):
                idle(stream)

        Scatter.take(p, own, s).run(plain_product(a_buf, w_buf), out_ref, idle_all)
        stores = [load(gq_buf, gq_out, local.at[5]), load(gkv_buf, gkv_out, local.at[6])]
        for copy in stores:
            copy.wait()

    return pl.pallas_call(
        kernel,
        out_shape=[
            jax.ShapeDtypeStruct(queries.shape, bf16),
            jax.ShapeDtypeStruct(keyval.shape, bf16),
            jax.ShapeDtypeStruct((own, wide), f32),
        ],
        in_specs=[pl.BlockSpec(memory_space=pltpu.SMEM)] + [ANY] * 3 + [WHOLE] + [ANY] * 2,
        out_specs=[ANY, ANY, WHOLE],
        scratch_shapes=[
            pltpu.VMEM(act.shape, bf16),
            pltpu.VMEM(wp.shape, bf16),
            pltpu.VMEM(queries.shape, bf16),
            pltpu.VMEM(keyval.shape, bf16),
            pltpu.VMEM(grads.shape, bf16),
            pltpu.VMEM(queries.shape, bf16),
            pltpu.VMEM(keyval.shape, bf16),
            pltpu.VMEM((length, HD), f32),
            pltpu.VMEM((length, HD), f32),
        ]
        + Scatter.scratch(own, wide)
        + [sems(7)],
        compiler_params=params(number),
        cost_estimate=cost(2 * total * depth * wide),
        name="attend_back_scatter_proj",
    )(docs, queries, keyval, grads, lse, act, wp)


def pack_vectors(vectors):
    sizes = [v.shape[0] for v in vectors]
    lines = -(-sum(sizes) // (PLANE * 8 * 128)) * 8
    pad = PLANE * lines * 128 - sum(sizes)
    return jnp.concatenate(vectors + (jnp.zeros((pad,), f32),)).reshape(PLANE, lines, 128)


def unpack_vectors(packed, vectors):
    flat = packed.reshape(-1)
    sums, at = [], 0
    for v in vectors:
        sums.append(flat[at : at + v.shape[0]])
        at += v.shape[0]
    return sums


def after(value, *earlier):
    return lax.optimization_barrier((value, *earlier))[0]


def line_gather(shard, axis=0):
    return lax.all_gather(shard, "fsdp", axis=axis, tiled=True)


def line_scatter(grad, axis=0):
    return lax.psum_scatter(grad.astype(bf16), "fsdp", scatter_dimension=axis, tiled=True)


def column_weight_grad(grad, groups):
    rows, cols = grad.shape
    return line_scatter(grad.reshape(groups, rows // groups, cols), 1)


def shards(
    tokens,
    doc_starts,
    w_query,
    w_kv,
    w_out,
    w_fc,
    w_proj,
    ln1_gain,
    ln1_bias,
    b_query,
    b_value,
    b_out,
    ln2_gain,
    ln2_bias,
    b_fc,
    b_proj,
    cotangent,
):
    layers = lax.axis_size("fsdp")
    me = lax.axis_index("seq")
    streams, rows, width = tokens.shape
    own = streams * rows
    heads = HEADS // PLANE
    hidden = b_fc.shape[0]
    my_cols = heads * HD
    my_hidden = hidden // PLANE
    total = PLANE * own

    inputs = tokens.reshape(own, width).astype(f32)
    cot_low = cotangent.reshape(own, width)
    cot_full = cot_low.astype(f32)

    wq_pieces, wf_pieces, low_kv, wo = split_weights(w_query, w_fc, w_kv, w_out, layers, 1)
    wf = line_gather(wf_pieces, 1).reshape(width, my_hidden)
    wp = line_gather(w_proj)
    my_bq = lax.dynamic_slice_in_dim(b_query, me * my_cols, my_cols, 0).reshape(1, my_cols)
    my_bf = lax.dynamic_slice_in_dim(b_fc, me * my_hidden, my_hidden, 0).reshape(1, my_hidden)
    bkv = jnp.concatenate([jnp.zeros((HD,), f32), b_value]).reshape(1, 2 * HD)

    shifted1, normed1, inverse1 = normalize(inputs, ln1_gain, ln1_bias)
    hidden1, w_kv_all, wq = gather_hidden1(shifted1.astype(bf16), low_kv, wq_pieces, layers, 2)
    wq = wq.reshape(width, my_cols)
    cot_all, queries, keyval, mixed, lse = project_attend(
        doc_starts, hidden1, wq, w_kv_all, my_bq, bkv, cot_low, streams, heads, 3
    )
    mixed_rows = mixed.reshape(total, my_cols)
    residual = inputs + scatter_attn(mixed_rows, wo, 4) + b_out
    shifted2, normed2, inverse2 = normalize(residual, ln2_gain, ln2_bias)
    hidden2, act_low, slope, grad_w_proj = gather_fc(shifted2.astype(bf16), wf, my_bf, cot_all, 5)
    shard_proj = line_scatter(grad_w_proj)
    grad_b_proj = jnp.sum(cot_full, axis=0)

    grad_hidden2, my_grad_b_fc, grad_w_fc = scatter_fc(cot_all, slope, wp, wf, hidden2, 6)
    fc_pieces = column_weight_grad(grad_w_fc, PLANE)
    back_second, grad_ln2_gain, grad_ln2_bias = normalize_back(
        grad_hidden2, normed2, inverse2, ln2_gain
    )
    grad_residual = cot_full + back_second
    grad_attn = grad_residual.astype(bf16)
    grad_b_out = jnp.sum(grad_attn.astype(f32), axis=0)
    grad_mixed, grad_w_out = gather_out(grad_attn, wo, mixed_rows, 7)
    gq, gkv, mlp = attend_back_scatter_proj(
        doc_starts,
        queries,
        keyval,
        after(grad_mixed, shard_proj).reshape(PLANE, streams, rows, my_cols),
        lse,
        act_low,
        wp,
        heads,
        8,
    )
    output = residual + mlp + b_proj
    gq_rows = gq.reshape(total, my_cols)
    gkv_rows = gkv.reshape(total, 2 * HD)
    grad_hidden1, query_pieces, grad_w_kv, shard_out = scatter_query(
        gq_rows, gkv_rows, wq, w_kv_all, hidden1, grad_w_out, layers, 9
    )
    my_grad_b_query = jnp.sum(gq_rows.astype(f32), axis=0)
    grad_b_value = jnp.sum(gkv_rows[:, HD:].astype(f32), axis=0)
    back_first, grad_ln1_gain, grad_ln1_bias = normalize_back(
        grad_hidden1, normed1, inverse1, ln1_gain
    )
    input_grad = grad_residual + back_first
    zero = jnp.zeros_like
    grad_b_query = lax.dynamic_update_slice_in_dim(zero(b_query), my_grad_b_query, me * my_cols, 0)
    grad_b_fc = lax.dynamic_update_slice_in_dim(
        zero(b_fc), my_grad_b_fc.reshape(-1), me * my_hidden, 0
    )
    vectors = (
        grad_ln1_gain,
        grad_ln1_bias,
        grad_b_query,
        grad_b_value,
        grad_b_out,
        grad_ln2_gain,
        grad_ln2_bias,
        grad_b_fc,
        grad_b_proj,
    )
    packed, shard_kv, shard_fc, shard_query = last_exchange(
        pack_vectors(vectors), fc_pieces, query_pieces, grad_w_kv, layers, 10
    )
    sums = unpack_vectors(packed, vectors)
    return (
        output.reshape(streams, rows, width),
        input_grad.reshape(streams, rows, width),
        shard_query.astype(f32),
        shard_kv,
        shard_out,
        shard_fc.astype(f32),
        shard_proj.astype(f32),
        *sums,
    )


def gather_seq(block):
    return lax.all_gather(block, "seq", axis=0, tiled=True)


def scatter_seq(partial):
    return lax.psum_scatter(partial.astype(bf16), "seq", scatter_dimension=0, tiled=True).astype(f32)


def columns_to_rows(part, groups):
    rows = part.shape[0]
    spread = part.reshape(rows, groups, part.shape[1] // groups).transpose(1, 0, 2)
    return lax.all_to_all(spread, "seq", split_axis=0, concat_axis=0, tiled=True)


def column_weight(shard, groups):
    pieces = columns_to_rows(shard, groups)
    full = lax.all_gather(pieces, "fsdp", axis=1, tiled=True)
    return full.reshape(-1, full.shape[2])


def plain_column_grad(grad, groups):
    rows, cols = grad.shape
    kept = lax.psum_scatter(
        grad.astype(bf16).reshape(groups, rows // groups, cols), "fsdp", scatter_dimension=1, tiled=True
    )
    moved = lax.all_to_all(kept, "seq", split_axis=0, concat_axis=0, tiled=True)
    return moved.transpose(1, 0, 2).reshape(moved.shape[1], groups * cols).astype(f32)


def row_weight_grad(grad):
    return lax.psum_scatter(grad.astype(bf16), "fsdp", scatter_dimension=0, tiled=True).astype(f32)


def plain_attend(queries, keyval, starts, groups, streams, rows, heads):
    length = groups * rows
    scale = HD ** (-0.5)
    position = jnp.arange(length, dtype=jnp.int32)
    mixed_list, lse_list = [], []
    for stream in range(streams):
        q = queries[:, stream].reshape(length, heads, HD)
        k = keyval[:, stream, :, :HD].reshape(length, HD)
        v = keyval[:, stream, :, HD:].reshape(length, HD)
        segment = jnp.sum((starts[stream][None, :] <= position[:, None]).astype(jnp.int32), axis=1)
        allowed = (position[None, :] <= position[:, None]) & (segment[None, :] == segment[:, None])
        scores = jnp.einsum("thd,ud->htu", q, k, preferred_element_type=f32) * scale
        scores = jnp.where(allowed[None], scores, -1e30)
        top = jnp.max(scores, axis=-1, keepdims=True)
        lse = top + jnp.log(jnp.sum(jnp.exp(scores - top), axis=-1, keepdims=True))
        probs = jnp.exp(scores - lse).astype(bf16)
        mixed = jnp.einsum("htu,ud->thd", probs, v, preferred_element_type=f32)
        mixed_list.append(mixed.astype(bf16).reshape(groups, rows, heads * HD))
        lse_list.append(lse)
    return jnp.stack(mixed_list, axis=1), lse_list


def plain_attend_back(queries, keyval, grads, lse_list, starts, groups, streams, rows, heads):
    length = groups * rows
    scale = HD ** (-0.5)
    position = jnp.arange(length, dtype=jnp.int32)
    gq_list, gkv_list = [], []
    for stream in range(streams):
        q = queries[:, stream].reshape(length, heads, HD)
        g = grads[:, stream].reshape(length, heads, HD)
        k = keyval[:, stream, :, :HD].reshape(length, HD)
        v = keyval[:, stream, :, HD:].reshape(length, HD)
        segment = jnp.sum((starts[stream][None, :] <= position[:, None]).astype(jnp.int32), axis=1)
        allowed = (position[None, :] <= position[:, None]) & (segment[None, :] == segment[:, None])
        scores = jnp.einsum("thd,ud->htu", q, k, preferred_element_type=f32) * scale
        probs = jnp.exp(jnp.where(allowed[None], scores, -1e30) - lse_list[stream])
        grad_probs = jnp.einsum("thd,ud->htu", g, v, preferred_element_type=f32)
        delta = jnp.sum(probs * grad_probs, axis=-1, keepdims=True)
        gs = (probs * (grad_probs - delta)).astype(bf16)
        gq = jnp.einsum("htu,ud->thd", gs, k, preferred_element_type=f32) * scale
        gk = jnp.einsum("htu,thd->ud", gs, q, preferred_element_type=f32) * scale
        gv = jnp.einsum("htu,thd->ud", probs.astype(bf16), g, preferred_element_type=f32)
        gq_list.append(gq.astype(bf16).reshape(groups, rows, heads * HD))
        gkv_list.append(jnp.concatenate([gk, gv], axis=1).reshape(groups, rows, 2 * HD))
    return jnp.stack(gq_list, axis=1), jnp.stack(gkv_list, axis=1)


def plain_shards(
    tokens,
    doc_starts,
    w_query,
    w_kv,
    w_out,
    w_fc,
    w_proj,
    ln1_gain,
    ln1_bias,
    b_query,
    b_value,
    b_out,
    ln2_gain,
    ln2_bias,
    b_fc,
    b_proj,
    cotangent,
):
    groups = lax.axis_size("seq")
    me = lax.axis_index("seq")
    streams, rows, width = tokens.shape
    own = streams * rows
    heads = HEADS // groups
    hidden = b_fc.shape[0]
    my_cols = heads * HD
    my_hidden = hidden // groups

    wq = column_weight(w_query, groups)
    w_kv_all = gather_seq(lax.all_gather(w_kv, "fsdp", axis=0, tiled=True))
    wo = lax.all_gather(w_out, "fsdp", axis=0, tiled=True)
    wf = column_weight(w_fc, groups)
    wp = lax.all_gather(w_proj, "fsdp", axis=0, tiled=True)
    my_bq = lax.dynamic_slice_in_dim(b_query, me * my_cols, my_cols, 0)
    my_bf = lax.dynamic_slice_in_dim(b_fc, me * my_hidden, my_hidden, 0)

    inputs = tokens.reshape(own, width).astype(f32)
    cot_low = cotangent.reshape(own, width)
    cot_full = cot_low.astype(f32)
    shifted1, normed1, inverse1 = normalize(inputs, ln1_gain, ln1_bias)
    hidden1 = gather_seq(shifted1.astype(bf16))
    queries = (dot(hidden1, wq) + my_bq).astype(bf16).reshape(groups, streams, rows, my_cols)
    value_shift = jnp.concatenate([jnp.zeros((HD,), f32), b_value])
    keyval = (dot(hidden1, w_kv_all) + value_shift).astype(bf16).reshape(groups, streams, rows, 2 * HD)
    mixed, lse = plain_attend(queries, keyval, doc_starts, groups, streams, rows, heads)
    mixed_rows = mixed.reshape(groups * own, my_cols)
    residual = inputs + scatter_seq(dot(mixed_rows, wo)) + b_out
    shifted2, normed2, inverse2 = normalize(residual, ln2_gain, ln2_bias)
    hidden2 = gather_seq(shifted2.astype(bf16))
    cot_all = gather_seq(cot_low)
    pre_act = dot(hidden2, wf) + my_bf
    activated, slope = gelu_pair(pre_act)
    act_low = activated.astype(bf16)
    output = residual + scatter_seq(dot(act_low, wp)) + b_proj

    grad_b_proj = jnp.sum(cot_full, axis=0)
    shard_proj = row_weight_grad(dot_tn(act_low, cot_all))
    grad_pre = (dot_nt(cot_all, wp) * slope).astype(bf16)
    my_grad_b_fc = jnp.sum(grad_pre.astype(f32), axis=0)
    shard_fc = plain_column_grad(dot_tn(hidden2, grad_pre), groups)
    grad_hidden2 = scatter_seq(dot_nt(grad_pre, wf))
    back_second, grad_ln2_gain, grad_ln2_bias = normalize_back(
        grad_hidden2, normed2, inverse2, ln2_gain
    )
    grad_residual = cot_full + back_second
    grad_attn = grad_residual.astype(bf16)
    grad_b_out = jnp.sum(grad_attn.astype(f32), axis=0)
    grad_attn_all = gather_seq(grad_attn)
    shard_out = row_weight_grad(dot_tn(mixed_rows, grad_attn_all))
    grad_mixed = dot_nt(grad_attn_all, wo).astype(bf16).reshape(groups, streams, rows, my_cols)
    gq, gkv = plain_attend_back(
        queries, keyval, grad_mixed, lse, doc_starts, groups, streams, rows, heads
    )
    gq_rows = gq.reshape(groups * own, my_cols)
    gkv_rows = gkv.reshape(groups * own, 2 * HD)
    my_grad_b_query = jnp.sum(gq_rows.astype(f32), axis=0)
    grad_b_value = jnp.sum(gkv_rows[:, HD:], axis=0)
    gkv_low = gkv_rows.astype(bf16)
    shard_query = plain_column_grad(dot_tn(hidden1, gq_rows), groups)
    shard_kv = row_weight_grad(scatter_seq(dot_tn(hidden1, gkv_low)))
    grad_hidden1 = scatter_seq(dot_nt(gq_rows, wq) + dot_nt(gkv_low, w_kv_all))
    back_first, grad_ln1_gain, grad_ln1_bias = normalize_back(
        grad_hidden1, normed1, inverse1, ln1_gain
    )
    input_grad = grad_residual + back_first

    zero = jnp.zeros_like
    grad_b_query = lax.dynamic_update_slice_in_dim(zero(b_query), my_grad_b_query, me * my_cols, 0)
    grad_b_fc = lax.dynamic_update_slice_in_dim(zero(b_fc), my_grad_b_fc, me * my_hidden, 0)
    vectors = (
        grad_ln1_gain,
        grad_ln1_bias,
        grad_b_query,
        grad_b_value,
        grad_b_out,
        grad_ln2_gain,
        grad_ln2_bias,
        grad_b_fc,
        grad_b_proj,
    )
    sums = lax.psum(vectors, ("seq", "fsdp"))
    return (
        output.reshape(streams, rows, width),
        input_grad.reshape(streams, rows, width),
        shard_query,
        shard_kv,
        shard_out,
        shard_fc,
        shard_proj,
        *sums,
    )


def solution(mesh):
    acts = P("fsdp", "seq", None)
    weight = P(("seq", "fsdp"), None)
    return jax.shard_map(
        shards if mesh.shape["seq"] == PLANE else plain_shards,
        mesh=mesh,
        in_specs=(acts, P("fsdp", None)) + (weight,) * 5 + (P(),) * 9 + (acts,),
        out_specs=(acts, acts) + (weight,) * 5 + (P(),) * 9,
        check_vma=False,
    )
```

```python
import functools

import jax
import jax.numpy as jnp
from jax import lax
from jax.experimental import pallas as pl
from jax.experimental.pallas import tpu as pltpu
from jax.sharding import PartitionSpec as P

HEADS = 16
HD = 128

root_two_pi = 0.7978845608028654
cubic_coef = 0.044715
epsilon = 1e-05
f32 = jnp.float32
bf16 = jnp.bfloat16
MESH = pl.DeviceIdType.MESH
ANY = pl.BlockSpec(memory_space=pl.ANY)
WHOLE = pl.BlockSpec(memory_space=pltpu.VMEM)
VMEM_LIMIT = 56 * 1024 * 1024
PLANE = 8


def normalize(values, gain_row, shift_row):
    center = values - jnp.mean(values, axis=-1, keepdims=True)
    inverse = lax.rsqrt(jnp.mean(center * center, axis=-1, keepdims=True) + epsilon)
    normed = center * inverse
    return (normed * gain_row + shift_row, normed, inverse)


def normalize_back(grad_out, normed, inverse, gain_row):
    scaled = grad_out * gain_row
    grad_in = inverse * (
        scaled
        - jnp.mean(scaled, axis=-1, keepdims=True)
        - normed * jnp.mean(scaled * normed, axis=-1, keepdims=True)
    )
    return (grad_in, jnp.sum(grad_out * normed, axis=0), jnp.sum(grad_out, axis=0))


def norm_stats(values):
    mean = jnp.mean(values, axis=-1, keepdims=True)
    center = values - mean
    return mean, lax.rsqrt(jnp.mean(center * center, axis=-1, keepdims=True) + epsilon)


def norm_back(grad_out, normed, inverse, gain_row):
    scaled = grad_out * gain_row
    return inverse * (
        scaled
        - jnp.mean(scaled, axis=-1, keepdims=True)
        - normed * jnp.mean(scaled * normed, axis=-1, keepdims=True)
    )


def gelu_pair(inputs):
    tangent = jnp.tanh(root_two_pi * (inputs + cubic_coef * inputs * inputs * inputs))
    activated = 0.5 * inputs * (1.0 + tangent)
    gradient_slope = 0.5 * (1.0 + tangent) + 0.5 * inputs * (
        1.0 - tangent * tangent
    ) * root_two_pi * (1.0 + 3.0 * cubic_coef * inputs * inputs)
    return (activated, gradient_slope)


def dot(a, b):
    return jnp.dot(a, b, preferred_element_type=f32)


def dot_nt(a, b):
    return lax.dot_general(a, b, (((1,), (1,)), ((), ())), preferred_element_type=f32)


def dot_tn(a, b):
    return lax.dot_general(a, b, (((0,), (0,)), ((), ())), preferred_element_type=f32)


def push(src, dst, send, recv, to):
    return pltpu.make_async_remote_copy(
        src_ref=src, dst_ref=dst, send_sem=send, recv_sem=recv, device_id=to, device_id_type=MESH
    )


def sems(*shape):
    return pltpu.SemaphoreType.DMA(shape)


def rows_at(start, size):
    return pl.ds(pl.multiple_of(start, size), size)


class Place:
    def __init__(self):
        me = lax.axis_index("seq")
        self.me = me
        self.core = lax.rem(me, 2)
        x = lax.rem(lax.div(me, 2), 2)
        y = lax.div(me, 4)
        self.sib = me + 1 - 2 * self.core
        self.xn = me + 2 - 4 * x
        self.yn = me + 4 - 8 * y
        self.dg = me + 2 - 4 * x + 4 - 8 * y
        turn = 1 - 2 * self.core
        self.xs, self.ys, self.ds = self.xn + turn, self.yn + turn, self.dg + turn
        self.layer = lax.axis_index("fsdp")

    def plane_peer(self, step):
        return lax.rem(self.me + step, PLANE)

    def line_peer(self, step, layers):
        return lax.rem(self.layer + step, layers)

    def greet(self, whole_plane=False, layers=1):
        barrier = pltpu.get_barrier_semaphore()
        if whole_plane:
            others = [self.plane_peer(step) for step in range(1, PLANE)]
        else:
            others = [self.sib, self.xn, self.yn]
        for other in others:
            pl.semaphore_signal(barrier, inc=1, device_id={"seq": other}, device_id_type=MESH)
        for step in range(1, layers):
            other = self.line_peer(step, layers)
            pl.semaphore_signal(barrier, inc=1, device_id={"fsdp": other}, device_id_type=MESH)
        pl.semaphore_wait(barrier, len(others) + layers - 1)


class Gather:
    sends = 14
    scratch = [sems(14), sems(PLANE, 2)]

    def __init__(self, place, buf, rows, send, recv):
        self.p, self.buf, self.rows, self.half = place, buf, rows, rows // 2
        self.send_sem, self.recv_sem = send, recv
        self.copies = []

    def piece(self, dev, half):
        return self.buf.at[rows_at(dev * self.rows + half * self.half, self.half), :]

    def pair(self, dev):
        return rows_at(lax.div(dev, 2) * (2 * self.rows), 2 * self.rows)

    def send(self, dev, half, to, src=None):
        k = len(self.copies)
        piece = self.piece(dev, half)
        copy = push(
            piece if src is None else src,
            piece,
            self.send_sem.at[k],
            self.recv_sem.at[dev, half],
            {"seq": to},
        )
        copy.start()
        self.copies.append(copy)

    def arrived(self, dev, half):
        piece = self.piece(dev, half)
        push(
            piece, piece, self.send_sem.at[0], self.recv_sem.at[dev, half], {"seq": self.p.sib}
        ).wait_recv()

    def start(self, own):
        p = self.p
        parts = [own.at[pl.ds(h * self.half, self.half), :] for h in range(2)]
        self.send(p.me, 0, p.yn, parts[0])
        self.send(p.me, 1, p.xn, parts[1])
        self.send(p.me, 1, p.yn, parts[1])
        self.send(p.me, 0, p.xn, parts[0])
        for h in range(2):
            self.send(p.me, h, p.sib, parts[h])

    def relay_first(self):
        p = self.p
        self.arrived(p.yn, 0)
        self.send(p.yn, 0, p.xn)
        self.arrived(p.xn, 1)
        self.send(p.xn, 1, p.yn)
        self.send(p.yn, 0, p.sib)
        self.send(p.xn, 1, p.sib)

    def relay_rest(self):
        p = self.p
        self.arrived(p.xn, 0)
        self.send(p.xn, 0, p.sib)
        self.arrived(p.yn, 1)
        self.send(p.yn, 1, p.sib)

    def relay(self):
        self.relay_first()
        self.relay_rest()

    def have(self, dev):
        self.arrived(dev, 0)
        self.arrived(dev, 1)

    def relay_corner(self):
        p = self.p
        for h in range(2):
            self.arrived(p.dg, h)
            self.send(p.dg, h, p.sib)

    def finish(self):
        for copy in self.copies:
            copy.wait_send()


class Scatter:
    LINES = 32

    def __init__(self, place, rows, part, sib_out, sib_in, boxes, sib_send, sib_recv, send, recv):
        self.p, self.rows, self.half = place, rows, rows // 2
        self.wide = part.shape[2]
        self.part, self.sib_out, self.sib_in = part, sib_out, sib_in
        self.out_d, self.out_x, self.out_y, self.in_d, self.in_x, self.in_y = boxes
        self.sib_send, self.sib_recv, self.send, self.recv = sib_send, sib_recv, send, recv
        self.copies = []

    @staticmethod
    def scratch(rows, wide):
        return [
            pltpu.VMEM((4, rows, wide), f32),
            pltpu.VMEM((4, rows, wide), bf16),
            pltpu.VMEM((4, rows, wide), bf16),
            *[pltpu.VMEM((rows, wide), bf16)] * 6,
            sems(4, 2),
            sems(4, 2),
            sems(8),
            sems(8),
        ]

    @classmethod
    def take(cls, place, rows, refs):
        return cls(place, rows, refs[0], refs[1], refs[2], refs[3:9], *refs[9:13])

    def cols(self, c):
        return pl.ds(c * (self.wide // 2), self.wide // 2)

    def swap(self, role, dev, product, c):
        p = self.p
        chip = lax.div(dev, 2) * (2 * self.rows)

        def store_out(cols, value):
            self.sib_out[role, :, cols] = value.astype(bf16)

        def store_part(cols, value):
            self.part[role, :, cols] = value

        product(
            role,
            rows_at(chip + (1 - p.core) * self.rows, self.rows),
            rows_at(chip + p.core * self.rows, self.rows),
            store_out,
            store_part,
            c,
        )
        copy = push(
            self.sib_out.at[role, :, self.cols(c)],
            self.sib_in.at[role, :, self.cols(c)],
            self.sib_send.at[role, c],
            self.sib_recv.at[role, c],
            {"seq": p.sib},
        )
        copy.start()
        self.copies.append(copy)
        return copy

    def swap_all(self, role, dev, product):
        return [self.swap(role, dev, product, c) for c in range(2)]

    def add_into(self, dst, role, first, size, more=(), cols=slice(None)):
        lines = self.LINES

        @pl.loop(0, size // lines)
        def _(i):
            line = rows_at(first + i * lines, lines)
            value = self.part[role, line, cols] + self.sib_in[role, line, cols].astype(f32)
            for ref in more:
                value = value + ref[line, cols].astype(f32)
            if dst is None:
                self.emit(line, value)
            else:
                dst[line, cols] = value.astype(dst.dtype)

    def ship(self, src, dst, h, k, to, cols=slice(None)):
        lines = pl.ds(h * self.half, self.half)
        copy = push(
            src.at[lines, cols], dst.at[lines, cols], self.send.at[k], self.recv.at[k], {"seq": to}
        )
        copy.start()
        self.copies.append(copy)
        return copy

    def ship_corner(self, c):
        cols = self.cols(c)
        self.add_into(self.out_d, 0, 0, self.rows, (), cols)
        return (
            self.ship(self.out_d, self.in_d, 0, 2 * c, self.p.xn, cols),
            self.ship(self.out_d, self.in_d, 1, 2 * c + 1, self.p.yn, cols),
        )

    def run(self, product, emit, idle=None):
        p, rows, half = self.p, self.rows, self.half
        self.emit = emit
        d0 = self.swap(0, p.dg, product, 0)
        d1 = self.swap(0, p.dg, product, 1)
        d0.wait_recv()
        dx0, dy0 = self.ship_corner(0)
        to_x = [self.swap(1, p.xn, product, 0)]
        d1.wait_recv()
        dx1, dy1 = self.ship_corner(1)
        to_x.append(self.swap(1, p.xn, product, 1))
        to_y = self.swap_all(2, p.yn, product)
        for copy in to_x:
            copy.wait_recv()
        self.add_into(self.out_x, 1, 0, half)
        x0 = self.ship(self.out_x, self.in_x, 0, 4, p.xn)
        for copy in to_y:
            copy.wait_recv()
        self.add_into(self.out_y, 2, half, half)
        y1 = self.ship(self.out_y, self.in_y, 1, 5, p.yn)
        to_me = self.swap_all(3, p.me, product)
        dy0.wait_recv()
        dy1.wait_recv()
        self.add_into(self.out_x, 1, half, half, (self.in_d,))
        x1 = self.ship(self.out_x, self.in_x, 1, 6, p.xn)
        dx0.wait_recv()
        dx1.wait_recv()
        self.add_into(self.out_y, 2, 0, half, (self.in_d,))
        y0 = self.ship(self.out_y, self.in_y, 0, 7, p.yn)
        if idle is not None:
            idle()
        for copy in to_me:
            copy.wait_recv()
        x0.wait_recv()
        y0.wait_recv()
        self.add_into(None, 3, 0, half, (self.in_x, self.in_y))
        y1.wait_recv()
        x1.wait_recv()
        self.add_into(None, 3, half, half, (self.in_x, self.in_y))
        for copy in self.copies:
            copy.wait_send()


class LineGather:
    def __init__(self, place, src, out, layers, send, recv):
        self.p, self.src, self.out, self.layers = place, src, out, layers
        self.send, self.recv = send, recv
        self.moves = [d for d in (2, -2, 1, -1) if abs(d) < layers]

    def block(self, layer):
        rows = self.src.shape[0]
        return self.out.at[rows_at(layer * rows, rows), :]

    def copy(self, src, layer, k, to):
        return push(src, self.block(layer), self.send.at[k], self.recv.at[layer], {"fsdp": to})

    def inside(self, layer):
        return (layer >= 0) & (layer < self.layers)

    def start(self):
        me = self.p.layer
        for k, d in enumerate(self.moves):

            @pl.when(self.inside(me + d))
            def _(k=k, d=d):
                self.copy(self.src, me, k, me + d).start()

    def wait_from(self, layer):
        block = self.block(layer)
        other = lax.rem(self.p.layer + 1, self.layers)
        push(block, block, self.send.at[0], self.recv.at[layer], {"fsdp": other}).wait_recv()

    def passing(self):
        me = self.p.layer
        found = []
        for far in range(3, self.layers):
            for sign in (1, -1):
                source, to = me - sign * (far - 1), me + sign
                found.append((self.inside(source) & self.inside(to), source, to))
        return found

    def relay(self):
        for k, (here, source, to) in enumerate(self.passing()):

            @pl.when(here)
            def _(k=k, source=source, to=to):
                self.wait_from(source)
                self.copy(self.block(source), source, len(self.moves) + k, to).start()

    def finish(self):
        me = self.p.layer
        passed = self.passing()
        for step in range(1, self.layers):
            source = lax.rem(me + step, self.layers)
            waited = None
            for here, whose, _ in passed:
                hit = here & (whose == source)
                waited = hit if waited is None else waited | hit
            if waited is None:
                self.wait_from(source)
            else:
                pl.when(jnp.logical_not(waited))(lambda source=source: self.wait_from(source))
        for k, d in enumerate(self.moves):

            @pl.when(self.inside(me + d))
            def _(k=k, d=d):
                self.copy(self.src, me, k, me + d).wait_send()

        for k, (here, source, to) in enumerate(passed):

            @pl.when(here)
            def _(k=k, source=source, to=to):
                self.copy(self.block(source), source, len(self.moves) + k, to).wait_send()

    @staticmethod
    def scratch(layers):
        return [sems(4 + 2 * max(0, layers - 3)), sems(layers)]


class LineSum:
    def __init__(self, place, block, box, layers, send, recv):
        self.copies = []
        self.box = box
        for step in range(1, layers):
            to = place.line_peer(step, layers)
            copy = push(block(to), box.at[step - 1], send.at[step], recv.at[step], {"fsdp": to})
            copy.start()
            self.copies.append(copy)

    def arrived(self):
        for copy in self.copies:
            copy.wait_recv()

    def total(self, own, where):
        value = own.astype(f32)
        for k in range(len(self.copies)):
            value = value + self.box[(k, *where)].astype(f32)
        return value

    def finish(self):
        for copy in self.copies:
            copy.wait_send()


class PlaneSum:
    def __init__(self, place, src, box, send, recv):
        self.p, self.src, self.box = place, src, box
        self.copies = []
        for step in range(1, PLANE):
            to = place.plane_peer(step)
            copy = push(src.at[to], box.at[step], send.at[step], recv.at[step], {"seq": to})
            copy.start()
            self.copies.append(copy)

    def total(self):
        value = self.src[self.p.me].astype(f32)
        for step, copy in enumerate(self.copies):
            copy.wait_recv()
            value = value + self.box[step + 1].astype(f32)
        return value

    def finish(self):
        for copy in self.copies:
            copy.wait_send()


class Spread:
    def __init__(self, place, src, out, send, recv, local):
        cols = src.shape[2]
        spot = out.at[:, rows_at(place.me * cols, cols)]
        self.copies = [load(src.at[place.me], spot, local)]
        for step in range(1, PLANE):
            to = place.plane_peer(step)
            copy = push(src.at[to], spot, send.at[step], recv.at[step], {"seq": to})
            copy.start()
            self.copies.append(copy)

    def finish(self):
        for copy in self.copies:
            copy.wait()


def fold(ref, first, value):
    rows, wide = value.shape
    total = jnp.sum(value.reshape(rows // 8, 8, wide), axis=0)

    @pl.when(first)
    def _():
        ref[...] = total

    @pl.when(jnp.logical_not(first))
    def _():
        ref[...] += total


def params(number, vmem=True):
    return pltpu.CompilerParams(
        collective_id=number,
        has_side_effects=True,
        vmem_limit_bytes=VMEM_LIMIT if vmem else None,
    )


def cost(flops, mib=40):
    return pl.CostEstimate(flops=flops, bytes_accessed=mib * 1024 * 1024, transcendentals=0)


def load(src, dst, sem):
    copy = pltpu.make_async_copy(src, dst, sem)
    copy.start()
    return copy


def split_weights(tokens, gain, shift, w_query, w_fc, w_kv, w_out, layers, number):
    arrays, lined = (w_query, w_fc), (w_kv, w_out)
    own_rows, width = tokens.shape

    def kernel(tok_ref, gain_ref, shift_ref, wq_ref, wf_ref, kv_ref, wo_ref, *refs):
        wq_out, wf_out, kv_out, wo_out, hidden, mean_out, inverse_out = refs[:7]
        send, recv, kv_send, kv_recv, wo_send, wo_recv, local = refs[7:]
        p = Place()
        ins, outs = (wq_ref, wf_ref), (wq_out, wf_out)
        lines = (
            LineGather(p, kv_ref, kv_out, layers, kv_send, kv_recv),
            LineGather(p, wo_ref, wo_out, layers, wo_send, wo_recv),
        )

        def block(i, dev):
            cols = ins[i].shape[1] // PLANE
            return ins[i].at[:, rows_at(dev * cols, cols)]

        own = []
        for i in range(2):
            own.append(load(lines[i].src, lines[i].block(p.layer), local.at[2 + i]))
            own.append(load(block(i, p.me), outs[i].at[p.me], local.at[i]))
        p.greet(True, layers)
        for line in lines:
            line.start()
        copies = []
        for i in (1, 0):
            for step in range(1, PLANE):
                to = p.plane_peer(step)
                copies.append(
                    push(
                        block(i, to),
                        outs[i].at[p.me],
                        send.at[i, step],
                        recv.at[i, step],
                        {"seq": to},
                    )
                )
                copies[-1].start()

        @pl.loop(0, own_rows // 32)
        def _(i):
            here = rows_at(i * 32, 32)
            values = tok_ref[here, :].astype(f32)
            mean, inverse = norm_stats(values)
            hidden[here, :] = (
                (values - mean) * inverse * gain_ref[...] + shift_ref[...]
            ).astype(bf16)
            mean_out[here, :] = mean
            inverse_out[here, :] = inverse

        for line in lines:
            line.relay()
        for copy in own + copies:
            copy.wait()
        for line in lines:
            line.finish()

    return pl.pallas_call(
        kernel,
        out_shape=[
            jax.ShapeDtypeStruct((PLANE, a.shape[0], a.shape[1] // PLANE), a.dtype)
            for a in arrays
        ]
        + [jax.ShapeDtypeStruct((layers * a.shape[0], a.shape[1]), a.dtype) for a in lined]
        + [jax.ShapeDtypeStruct((own_rows, width), bf16)]
        + [jax.ShapeDtypeStruct((own_rows, 1), f32)] * 2,
        in_specs=[WHOLE] * 3 + [ANY] * 4,
        out_specs=[ANY] * 4 + [WHOLE] * 3,
        scratch_shapes=[sems(2, PLANE), sems(2, PLANE)]
        + LineGather.scratch(layers) * 2
        + [sems(4)],
        compiler_params=params(number),
        name="split_weights",
    )(tokens, gain, shift, w_query, w_fc, w_kv, w_out)


def gather_hidden1(hidden1, low_kv, wq_pieces, layers, number):
    def kernel(h_ref, kv_ref, wq_ref, h_all, kv_all, wq_all, *refs):
        hs, hr, ks, kr, zsend, zrecv, local = refs
        p = Place()
        h_rows, kv_rows = h_ref.shape[0], kv_ref.shape[0]
        wq_mine = wq_all.at[:, p.layer]
        own = [
            load(h_ref, h_all.at[rows_at(p.me * h_rows, h_rows), :], local.at[0]),
            load(kv_ref, kv_all.at[rows_at(p.me * kv_rows, kv_rows), :], local.at[1]),
            load(wq_ref, wq_mine, local.at[2]),
        ]
        p.greet(False, layers)
        kv = Gather(p, kv_all, kv_rows, ks, kr)
        h = Gather(p, h_all, h_rows, hs, hr)
        kv.start(kv_ref)
        h.start(h_ref)
        across = []
        for step in range(1, layers):
            to = p.line_peer(step, layers)
            across.append(push(wq_ref, wq_mine, zsend.at[step], zrecv.at[step], {"fsdp": to}))
            across[-1].start()
        kv.relay()
        kv.relay_corner()
        h.relay()
        h.relay_corner()
        for g in (kv, h):
            for dev in (p.sib, p.xs, p.ys, p.ds):
                g.have(dev)
            g.finish()
        for copy in own + across:
            copy.wait()

    groups, piece_rows, cols = wq_pieces.shape
    return pl.pallas_call(
        kernel,
        out_shape=[
            jax.ShapeDtypeStruct((PLANE * hidden1.shape[0], hidden1.shape[1]), bf16),
            jax.ShapeDtypeStruct((PLANE * low_kv.shape[0], low_kv.shape[1]), bf16),
            jax.ShapeDtypeStruct((groups, layers, piece_rows, cols), bf16),
        ],
        in_specs=[ANY] * 3,
        out_specs=[ANY] * 3,
        scratch_shapes=Gather.scratch * 2 + [sems(layers), sems(layers), sems(3)],
        compiler_params=params(number, False),
        name="gather_hidden1",
    )(hidden1, low_kv, wq_pieces)


def project_attend(docs, hidden1, wq, w_kv, bq, bkv, cot, streams, heads, number):
    total, depth = hidden1.shape
    cols, kv_cols = wq.shape[1], w_kv.shape[1]
    rows = total // PLANE // streams
    length = PLANE * rows
    block = min(QROWS, length)
    chunk = total // 4

    def kernel(docs_ref, h_ref, wq_ref, wkv_ref, bq_ref, bkv_ref, cot_ref, *refs):
        cot_all, q_out, kv_out, mixed_out, lse_ref = refs[:5]
        h_buf, wq_buf, wkv_buf, q_buf, kv_buf, mixed_buf, send, recv, local = refs[5:]
        p = Place()
        own_rows = cot_ref.shape[0]

        def fetch(k):
            return load(
                h_ref.at[pl.ds(k * chunk, chunk), :], h_buf.at[k % 2], local.at[k % 2]
            )

        fetches = [fetch(0)]
        weights = [load(wq_ref, wq_buf, local.at[2]), load(wkv_ref, wkv_buf, local.at[3])]
        own = load(cot_ref, cot_all.at[rows_at(p.me * own_rows, own_rows), :], local.at[4])
        p.greet()
        g = Gather(p, cot_all, own_rows, send, recv)
        g.start(cot_ref)
        for copy in weights:
            copy.wait()
        per = chunk // (streams * rows)
        for k in range(4):
            fetches[k].wait()
            if k < 3:
                fetches.append(fetch(k + 1))
            where = pl.ds(k * per, per)
            q = dot(h_buf[k % 2], wq_buf[...]) + bq_ref[...]
            q_buf[where] = q.astype(bf16).reshape(per, streams, rows, cols)
            kv = dot(h_buf[k % 2], wkv_buf[...]) + bkv_ref[...]
            kv_buf[where] = kv.astype(bf16).reshape(per, streams, rows, kv_cols)
        stores = [load(q_buf, q_out, local.at[5]), load(kv_buf, kv_out, local.at[6])]
        g.relay_first()
        for stream in range(streams):
            attend_stream(
                docs_ref,
                stream,
                q_buf.at[:, stream],
                kv_buf.at[:, stream],
                mixed_buf.at[:, stream],
                lse_ref.at[stream],
                block,
                heads,
            )
        stores.append(load(mixed_buf, mixed_out, local.at[7]))
        g.relay_rest()
        g.relay_corner()
        for dev in (p.sib, p.xs, p.ys, p.ds):
            g.have(dev)
        g.finish()
        own.wait()
        for copy in stores:
            copy.wait()

    q_shape = (PLANE, streams, rows, cols)
    kv_shape = (PLANE, streams, rows, kv_cols)
    return pl.pallas_call(
        kernel,
        out_shape=[
            jax.ShapeDtypeStruct((PLANE * cot.shape[0], cot.shape[1]), bf16),
            jax.ShapeDtypeStruct(q_shape, bf16),
            jax.ShapeDtypeStruct(kv_shape, bf16),
            jax.ShapeDtypeStruct(q_shape, bf16),
            jax.ShapeDtypeStruct((streams, heads, length), f32),
        ],
        in_specs=[pl.BlockSpec(memory_space=pltpu.SMEM)] + [ANY] * 3 + [WHOLE] * 2 + [ANY],
        out_specs=[ANY] * 4 + [WHOLE],
        scratch_shapes=[
            pltpu.VMEM((2, chunk, depth), bf16),
            pltpu.VMEM(wq.shape, bf16),
            pltpu.VMEM(w_kv.shape, bf16),
            pltpu.VMEM(q_shape, bf16),
            pltpu.VMEM(kv_shape, bf16),
            pltpu.VMEM(q_shape, bf16),
        ]
        + Gather.scratch
        + [sems(8)],
        compiler_params=params(number),
        cost_estimate=cost(2 * total * depth * (cols + kv_cols)),
        name="project_attend",
    )(docs, hidden1, wq, w_kv, bq, bkv, cot)


def gather_fc(hidden2, wf, bf, cot_all, number):
    rows, depth = hidden2.shape
    wide = wf.shape[1]
    total = PLANE * rows
    out_wide = cot_all.shape[1]
    tile = 256

    def kernel(own_ref, w_ref, b_ref, cot_ref, all_ref, act_ref, slope_ref, dw_ref, *refs):
        buf, w_buf, act, slope, cot, acc, dw, send, recv, local = refs
        p = Place()
        load_own = load(own_ref, buf.at[rows_at(p.me * rows, rows), :], local.at[0])
        load_w = load(w_ref, w_buf, local.at[1])
        p.greet()
        g = Gather(p, buf, rows, send, recv)
        g.start(own_ref)
        stores = []
        cots = {}

        def fetch(k, dev):
            cots[k] = load(cot_ref.at[g.pair(dev), :], cot.at[k % 2], local.at[2 + k % 2])

        def work(k, dev):
            block = g.pair(dev)
            stores.append(load(buf.at[block, :], all_ref.at[block, :], local.at[4 + 3 * k]))

            @pl.loop(0, wide // tile)
            def _(j):
                cols = rows_at(j * tile, tile)
                acc_fc = dot(buf[block, :], w_buf[:, cols]) + b_ref[:, cols]
                activated, gradient = gelu_pair(acc_fc)
                act[block, cols] = activated.astype(bf16)
                slope[block, cols] = gradient.astype(bf16)

            for i, (src, dst) in enumerate(((act, act_ref), (slope, slope_ref))):
                stores.append(
                    load(src.at[block, :], dst.at[block, :], local.at[4 + 3 * k + 1 + i])
                )

        def grads(k, dev):
            block = g.pair(dev)
            cots[k].wait()

            @pl.loop(0, wide // tile)
            def _(j):
                cols = rows_at(j * tile, tile)
                term = dot_tn(act[block, cols], cot[k % 2])
                if k == 0:
                    acc[cols, :] = term
                elif k < 3:
                    acc[cols, :] += term
                else:
                    dw[cols, :] = (acc[cols, :] + term).astype(bf16)

        fetch(0, p.me)
        fetch(1, p.xn)
        load_own.wait()
        load_w.wait()
        g.have(p.sib)
        work(0, p.me)
        g.relay_first()
        grads(0, p.me)
        fetch(2, p.yn)
        g.relay_rest()
        g.have(p.xs)
        work(1, p.xn)
        g.have(p.ys)
        work(2, p.yn)
        grads(1, p.xn)
        fetch(3, p.dg)
        g.relay_corner()
        grads(2, p.yn)
        g.have(p.ds)
        work(3, p.dg)
        grads(3, p.dg)
        stores.append(load(dw, dw_ref, local.at[16]))
        g.finish()
        for copy in stores:
            copy.wait()

    return pl.pallas_call(
        kernel,
        out_shape=[
            jax.ShapeDtypeStruct((total, depth), bf16),
            jax.ShapeDtypeStruct((total, wide), bf16),
            jax.ShapeDtypeStruct((total, wide), bf16),
            jax.ShapeDtypeStruct((wide, out_wide), bf16),
        ],
        in_specs=[ANY, ANY, WHOLE, ANY],
        out_specs=[ANY] * 4,
        scratch_shapes=[
            pltpu.VMEM((total, depth), bf16),
            pltpu.VMEM(wf.shape, bf16),
            pltpu.VMEM((total, wide), bf16),
            pltpu.VMEM((total, wide), bf16),
            pltpu.VMEM((2, 2 * rows, out_wide), bf16),
            pltpu.VMEM((wide, out_wide), f32),
            pltpu.VMEM((wide, out_wide), bf16),
        ]
        + Gather.scratch
        + [sems(17)],
        compiler_params=params(number),
        cost_estimate=cost(4 * total * depth * wide),
        name="gather_fc",
    )(hidden2, wf, bf, cot_all)


def gather_out(grad_attn, wo, mixed, number):
    rows, depth = grad_attn.shape
    wide = wo.shape[0]
    total = PLANE * rows

    def kernel(own_ref, w_ref, mixed_ref, gm_ref, dw_ref, *refs):
        buf, w_buf, mixed_buf, gm, acc, dw, send, recv, local = refs
        p = Place()
        load_own = load(own_ref, buf.at[rows_at(p.me * rows, rows), :], local.at[0])
        loads = [load(w_ref, w_buf, local.at[1]), load(mixed_ref, mixed_buf, local.at[2])]
        p.greet()
        g = Gather(p, buf, rows, send, recv)
        g.start(own_ref)

        def work(dev):
            block = g.pair(dev)
            gm[block, :] = dot_nt(buf[block, :], w_buf[...]).astype(bf16)

        def grads(k, dev):
            block = g.pair(dev)
            term = dot_tn(mixed_buf[block, :], buf[block, :])
            if k == 0:
                acc[...] = term
            elif k < 3:
                acc[...] += term
            else:
                dw[...] = (acc[...] + term).astype(bf16)

        load_own.wait()
        for copy in loads:
            copy.wait()
        g.have(p.sib)
        work(p.me)
        grads(0, p.me)
        g.relay()
        g.have(p.xs)
        work(p.xn)
        g.have(p.ys)
        work(p.yn)
        grads(1, p.xn)
        g.relay_corner()
        grads(2, p.yn)
        g.have(p.ds)
        work(p.dg)
        store = load(gm, gm_ref, local.at[3])
        grads(3, p.dg)
        store_dw = load(dw, dw_ref, local.at[4])
        g.finish()
        store.wait()
        store_dw.wait()

    return pl.pallas_call(
        kernel,
        out_shape=[
            jax.ShapeDtypeStruct((total, wide), bf16),
            jax.ShapeDtypeStruct((wide, depth), bf16),
        ],
        in_specs=[ANY] * 3,
        out_specs=[ANY] * 2,
        scratch_shapes=[
            pltpu.VMEM((total, depth), bf16),
            pltpu.VMEM(wo.shape, bf16),
            pltpu.VMEM(mixed.shape, bf16),
            pltpu.VMEM((total, wide), bf16),
            pltpu.VMEM((wide, depth), f32),
            pltpu.VMEM((wide, depth), bf16),
        ]
        + Gather.scratch
        + [sems(5)],
        compiler_params=params(number),
        cost_estimate=cost(4 * total * depth * wide),
        name="gather_out",
    )(grad_attn, wo, mixed)


TILE = 512


def scatter_attn(mixed, wo, tokens, b_out, gain, shift, number):
    total, depth = mixed.shape
    rows = total // PLANE
    wide = wo.shape[1]

    def kernel(a_ref, w_ref, tok_ref, bias_ref, gain_ref, shift_ref, *refs):
        residual, hidden, mean_out, inverse_out = refs[:4]
        a_buf, w_buf = refs[4:6]
        s, local = refs[6:19], refs[19]
        p = Place()
        loads = [load(a_ref, a_buf, local.at[0]), load(w_ref, w_buf, local.at[1])]
        p.greet()
        for copy in loads:
            copy.wait()

        def emit(line, value):
            values = tok_ref[line, :].astype(f32) + value + bias_ref[...]
            mean, inverse = norm_stats(values)
            residual[line, :] = values
            hidden[line, :] = (
                (values - mean) * inverse * gain_ref[...] + shift_ref[...]
            ).astype(bf16)
            mean_out[line, :] = mean
            inverse_out[line, :] = inverse

        Scatter.take(p, rows, s).run(plain_product(a_buf, w_buf), emit)

    return pl.pallas_call(
        kernel,
        out_shape=[
            jax.ShapeDtypeStruct((rows, wide), f32),
            jax.ShapeDtypeStruct((rows, wide), bf16),
            jax.ShapeDtypeStruct((rows, 1), f32),
            jax.ShapeDtypeStruct((rows, 1), f32),
        ],
        in_specs=[ANY] * 2 + [WHOLE] * 4,
        out_specs=[WHOLE] * 4,
        scratch_shapes=[pltpu.VMEM(mixed.shape, bf16), pltpu.VMEM(wo.shape, bf16)]
        + Scatter.scratch(rows, wide)
        + [sems(2)],
        compiler_params=params(number),
        cost_estimate=cost(2 * total * depth * wide),
        name="scatter_attn",
    )(mixed, wo, tokens, b_out, gain, shift)


def plain_product(a_buf, w_buf):
    steps = w_buf.shape[1] // 2 // TILE

    def product(role, theirs, ours, store_out, store_part, c):
        @pl.loop(0, steps)
        def _(j):
            cols = rows_at((c * steps + j) * TILE, TILE)
            store_out(cols, dot(a_buf[theirs, :], w_buf[:, cols]))
            store_part(cols, dot(a_buf[ours, :], w_buf[:, cols]))

    return product


def scatter_fc(cot_all, slope, wp, wf, hidden2, cot, residual, mean, inverse, gain, number):
    total, depth = cot_all.shape
    rows = total // PLANE
    wide = wp.shape[0]
    tile = 256

    def kernel(cot_ref, slope_ref, wp_ref, wf_ref, h_ref, *refs):
        cot_own, residual_ref, mean_ref, inverse_ref, gain_ref = refs[:5]
        grad_residual, grad_attn, sums_ref, bias_ref, dw_ref = refs[5:10]
        cot, slopes, wp_buf, wf_buf, gp, h_buf, dw_buf, folds = refs[10:18]
        s = refs[18:31]
        (local,) = refs[31:]
        p = Place()
        order = (p.dg, p.xn, p.yn, p.me)

        def chip(dev):
            return rows_at(lax.div(dev, 2) * (2 * rows), 2 * rows)

        def fetch(k):
            here = chip(order[k])
            return (
                load(cot_ref.at[here, :], cot.at[k % 2], local.at[k % 2]),
                load(slope_ref.at[here, :], slopes.at[k % 2], local.at[2 + k % 2]),
            )

        fetches = [fetch(0)]
        load_wp = load(wp_ref, wp_buf, local.at[4])
        load_wf = load(wf_ref, wf_buf, local.at[5])
        bias_ref[...] = jnp.zeros_like(bias_ref)
        p.greet()
        load_wp.wait()
        halves = depth // 2 // TILE

        def back_through_gelu(k):
            for copy in fetches[k]:
                copy.wait()
            if k < 3:
                fetches.append(fetch(k + 1))
            here = chip(order[k])

            @pl.loop(0, wide // tile)
            def _(j):
                cols = rows_at(j * tile, tile)
                grad_act = dot_nt(cot[k % 2], wp_buf[cols, :])
                grad_pre = (grad_act * slopes[k % 2, :, cols].astype(f32)).astype(bf16)
                gp[here, cols] = grad_pre
                bias_ref[:, cols] += jnp.sum(grad_pre.astype(f32), axis=0, keepdims=True)

            if k == 0:
                load_wf.wait()

        def product(role, theirs, ours, store_out, store_part, c):
            if c == 0:
                back_through_gelu(role)

            @pl.loop(0, halves)
            def _(j):
                cols = rows_at((c * halves + j) * TILE, TILE)
                store_out(cols, dot_nt(gp[theirs, :], wf_buf[cols, :]))
                store_part(cols, dot_nt(gp[ours, :], wf_buf[cols, :]))

        def emit(line, value):
            first = line.start == 0
            grad_out = cot_own[line, :].astype(f32)
            back = inverse_ref[line, :]
            normed = (residual_ref[line, :] - mean_ref[line, :]) * back
            result = grad_out + norm_back(value, normed, back, gain_ref[...])
            low = result.astype(bf16)
            grad_residual[line, :] = result
            grad_attn[line, :] = low
            for i, term in enumerate((value * normed, value, low.astype(f32), grad_out)):
                fold(folds.at[i], first, term)

        steps = depth // tile

        def h_fetch(i):
            return load(
                h_ref.at[:, pl.ds(i * tile, tile)], h_buf.at[i % 2], local.at[6 + i % 2]
            )

        def idle():
            tiles = [h_fetch(0)]
            stores = []
            for i in range(steps):
                tiles[i].wait()
                if i + 1 < steps:
                    tiles.append(h_fetch(i + 1))
                if i >= 2:
                    stores[i - 2].wait()
                dw_buf[i % 2] = dot_tn(h_buf[i % 2], gp[...]).astype(bf16)
                stores.append(
                    load(
                        dw_buf.at[i % 2],
                        dw_ref.at[pl.ds(i * tile, tile), :],
                        local.at[8 + i % 2],
                    )
                )
            for copy in stores[-2:]:
                copy.wait()

        Scatter.take(p, rows, s).run(product, emit, idle)
        sums_ref[...] = jnp.sum(folds[...], axis=1)

    return pl.pallas_call(
        kernel,
        out_shape=[
            jax.ShapeDtypeStruct((rows, depth), f32),
            jax.ShapeDtypeStruct((rows, depth), bf16),
            jax.ShapeDtypeStruct((4, depth), f32),
            jax.ShapeDtypeStruct((1, wide), f32),
            jax.ShapeDtypeStruct((depth, wide), bf16),
        ],
        in_specs=[ANY] * 5 + [WHOLE] * 5,
        out_specs=[WHOLE] * 4 + [ANY],
        scratch_shapes=[
            pltpu.VMEM((2, 2 * rows, depth), bf16),
            pltpu.VMEM((2, 2 * rows, wide), bf16),
            pltpu.VMEM(wp.shape, bf16),
            pltpu.VMEM(wf.shape, bf16),
            pltpu.VMEM((total, wide), bf16),
            pltpu.VMEM((2, total, tile), bf16),
            pltpu.VMEM((2, tile, wide), bf16),
            pltpu.VMEM((4, 8, depth), f32),
        ]
        + Scatter.scratch(rows, depth)
        + [sems(10)],
        compiler_params=params(number),
        cost_estimate=cost(6 * total * depth * wide),
        name="scatter_fc",
    )(cot_all, slope, wp, wf, hidden2, cot, residual, mean, inverse, gain)


def scatter_query(
    gq, gkv, wq, w_kv, grad_w_out, grad_w_query, grad_w_kv, back, layers, number
):
    total, cols = gq.shape
    kv_cols = gkv.shape[1]
    rows = total // PLANE
    depth = wq.shape[0]
    out_rows, out_wide = grad_w_out.shape[0] // layers, grad_w_out.shape[1]
    q_rows, q_cols = grad_w_query.shape[2:]
    kv_part = grad_w_kv.shape[1]
    kv_rows = kv_part // layers

    def kernel(gq_ref, gkv_ref, wq_ref, wkv_ref, dwo_ref, dwq_ref, dwkv_ref, *refs):
        tok_ref, mean_ref, inverse_ref, gain_ref, residual_ref = refs[:5]
        out_ref, sums_ref, dwo_out, dwq_out, dwkv_out = refs[5:10]
        g_buf, wq_buf, wkv_buf, folds = refs[10:14]
        dwo_own, dwo_box, q_own, q_box, q_sum, kv_box, kv_sum, kvz_box = refs[14:22]
        s = refs[22:35]
        (osend, orecv, qzsend, qzrecv, qsend, qrecv, ksend, krecv, kzsend, kzrecv, local) = refs[
            35:
        ]
        p = Place()
        q_side, kv_side = pl.ds(0, cols), pl.ds(cols, kv_cols)
        loads = [
            load(gq_ref, g_buf.at[:, q_side], local.at[0]),
            load(gkv_ref, g_buf.at[:, kv_side], local.at[1]),
            load(wq_ref, wq_buf, local.at[2]),
            load(wkv_ref, wkv_buf, local.at[3]),
        ]

        def dwo_block(layer):
            return dwo_ref.at[rows_at(layer * out_rows, out_rows), :]

        def dwq_block(layer):
            return dwq_ref.at[:, layer]

        own = [
            load(dwo_block(p.layer), dwo_own, local.at[4]),
            load(dwq_block(p.layer), q_own, local.at[5]),
        ]
        p.greet(True, layers)
        plane_kv = PlaneSum(p, dwkv_ref, kv_box, ksend, krecv)
        line_q = LineSum(p, dwq_block, q_box, layers, qzsend, qzrecv)
        line_o = LineSum(p, dwo_block, dwo_box, layers, osend, orecv)
        for copy in loads:
            copy.wait()
        halves = depth // 2 // TILE

        def product(role, theirs, ours, store_out, store_part, c):
            @pl.loop(0, halves)
            def _(j):
                where = rows_at((c * halves + j) * TILE, TILE)
                for rows_of, store in ((theirs, store_out), (ours, store_part)):
                    store(
                        where,
                        dot_nt(g_buf[rows_of, q_side], wq_buf[where, :])
                        + dot_nt(g_buf[rows_of, kv_side], wkv_buf[where, :]),
                    )

        later = []

        def idle():
            for copy in own:
                copy.wait()
            kv_sum[...] = plane_kv.total().astype(bf16).reshape(layers, kv_rows, kv_cols)
            line_kv = LineSum(p, lambda layer: kv_sum.at[layer], kvz_box, layers, kzsend, kzrecv)
            line_q.arrived()

            @pl.loop(0, PLANE)
            def _(i):
                q_sum[i] = line_q.total(q_own[i], (i,)).astype(bf16)

            later.append(Spread(p, q_sum, dwq_out, qsend, qrecv, local.at[6]))
            line_kv.arrived()
            dwkv_out[...] = line_kv.total(kv_sum[p.layer], ())
            later.append(line_kv)
            line_o.arrived()

            @pl.loop(0, out_rows // 16)
            def _(i):
                lines = rows_at(i * 16, 16)
                dwo_out[lines, :] = line_o.total(dwo_own[lines, :], (lines, slice(None)))

        def emit(line, value):
            first = line.start == 0
            normed = (tok_ref[line, :].astype(f32) - mean_ref[line, :]) * inverse_ref[line, :]
            out_ref[line, :] = residual_ref[line, :] + norm_back(
                value, normed, inverse_ref[line, :], gain_ref[...]
            )
            fold(folds.at[0], first, value * normed)
            fold(folds.at[1], first, value)

        Scatter.take(p, rows, s).run(product, emit, idle)
        sums_ref[...] = jnp.sum(folds[...], axis=1)
        plane_kv.finish()
        line_q.finish()
        line_o.finish()
        for item in later:
            item.finish()

    return pl.pallas_call(
        kernel,
        out_shape=[
            jax.ShapeDtypeStruct((rows, depth), f32),
            jax.ShapeDtypeStruct((2, depth), f32),
            jax.ShapeDtypeStruct((out_rows, out_wide), f32),
            jax.ShapeDtypeStruct((q_rows, PLANE * q_cols), bf16),
            jax.ShapeDtypeStruct((kv_rows, kv_cols), f32),
        ],
        in_specs=[ANY] * 6 + [WHOLE] * 6,
        out_specs=[WHOLE] * 3 + [ANY, WHOLE],
        scratch_shapes=[
            pltpu.VMEM((total, cols + kv_cols), bf16),
            pltpu.VMEM(wq.shape, bf16),
            pltpu.VMEM(w_kv.shape, bf16),
            pltpu.VMEM((2, 8, depth), f32),
            pltpu.VMEM((out_rows, out_wide), bf16),
            pltpu.VMEM((layers - 1, out_rows, out_wide), bf16),
            pltpu.VMEM((PLANE, q_rows, q_cols), bf16),
            pltpu.VMEM((layers - 1, PLANE, q_rows, q_cols), bf16),
            pltpu.VMEM((PLANE, q_rows, q_cols), bf16),
            pltpu.VMEM((PLANE, kv_part, kv_cols), bf16),
            pltpu.VMEM((layers, kv_rows, kv_cols), bf16),
            pltpu.VMEM((layers - 1, kv_rows, kv_cols), bf16),
        ]
        + Scatter.scratch(rows, depth)
        + [sems(layers)] * 4
        + [sems(PLANE)] * 4
        + [sems(layers)] * 2
        + [sems(7)],
        compiler_params=params(number),
        cost_estimate=cost(2 * total * depth * (cols + kv_cols)),
        name="scatter_query",
    )(gq, gkv, wq, w_kv, grad_w_out, grad_w_query, grad_w_kv, *back)


def last_exchange(vector, fc_pieces, layers, number):
    lines = vector.shape[1]

    def kernel(vec, fc_ref, vec_out, fc_out, *refs):
        box, plane_sum, zbox = refs[:3]
        vsend, vrecv, zsend, zrecv, gsend, grecv, send, recv, local = refs[3:]
        p = Place()
        p.greet(True, layers)
        plane = PlaneSum(p, vec, box, vsend, vrecv)
        spread = Spread(p, fc_ref, fc_out, send, recv, local.at[0])
        total = plane.total()
        plane_sum[...] = total
        zbox[0] = total
        across = []
        for step in range(1, layers):
            to = p.line_peer(step, layers)
            copy = push(plane_sum, zbox.at[step], zsend.at[step], zrecv.at[step], {"fsdp": to})
            copy.start()
            across.append(copy)
        for copy in across:
            copy.wait_recv()
        total = None
        for k in range(layers):
            term = zbox[lax.rem(p.layer - k + layers, layers)]
            total = term if total is None else total + term
        vec_out[p.me] = total
        last = []
        for step in range(1, PLANE):
            to = p.plane_peer(step)
            mine = vec_out.at[p.me]
            last.append(push(mine, mine, gsend.at[step], grecv.at[step], {"seq": to}))
            last[-1].start()
        for copy in last:
            copy.wait()
        spread.finish()
        plane.finish()
        for copy in across:
            copy.wait_send()

    return pl.pallas_call(
        kernel,
        out_shape=[
            jax.ShapeDtypeStruct(vector.shape, f32),
            jax.ShapeDtypeStruct((fc_pieces.shape[1], PLANE * fc_pieces.shape[2]), bf16),
        ],
        in_specs=[WHOLE, ANY],
        out_specs=[WHOLE, ANY],
        scratch_shapes=[
            pltpu.VMEM((PLANE, lines, 128), f32),
            pltpu.VMEM((lines, 128), f32),
            pltpu.VMEM((layers, lines, 128), f32),
        ]
        + [sems(PLANE)] * 2
        + [sems(layers)] * 2
        + [sems(PLANE)] * 4
        + [sems(1)],
        compiler_params=params(number, False),
        name="last_exchange",
    )(vector, fc_pieces)


def starts_of(docs, stream, positions):
    start = jnp.zeros_like(positions)
    for j in range(docs.shape[1]):
        here = docs[stream, j]
        start = jnp.maximum(start, jnp.where(here <= positions, here, 0))
    return start


def masked_scores(docs, stream, keys, q, first, limit):
    scores = dot_nt(keys, q) * (HD**-0.5)
    t = first + lax.broadcasted_iota(jnp.int32, (1, q.shape[0]), 1)
    u = lax.broadcasted_iota(jnp.int32, scores.shape, 0)
    return scores, (u >= starts_of(docs, stream, t)) & (u <= t)


QROWS = 256


def attend_stream(docs, stream, q_ref, kv_ref, mixed_ref, lse_ref, block, heads):
    groups, rows, cols = q_ref.shape
    length = groups * rows
    kv = kv_ref[...].reshape(length, 2 * HD)
    keys = kv[:, :HD]
    values_t = kv[:, HD:].T
    per = block // rows
    for b in range(length // block):
        limit = (b + 1) * block
        q_rows = q_ref[b * per : (b + 1) * per].reshape(block, cols)
        for h in range(heads):
            q = q_rows[:, h * HD : (h + 1) * HD]
            scores, allowed = masked_scores(docs, stream, keys[:limit], q, b * block, limit)
            scores = jnp.where(allowed, scores, -1e30)
            top = jnp.max(scores, axis=0, keepdims=True)
            weights = jnp.exp(scores - top)
            total = jnp.sum(weights, axis=0, keepdims=True)
            mixed = dot(values_t[:, :limit], weights.astype(bf16)) / total
            mixed_ref[b * per : (b + 1) * per, :, h * HD : (h + 1) * HD] = (
                mixed.T.astype(bf16).reshape(per, rows, HD)
            )
            lse_ref[h : h + 1, b * block : (b + 1) * block] = top + jnp.log(total)


def attend_stream_back(docs, stream, q_ref, kv_ref, g_ref, lse_ref, gq_ref, gkv_ref, gk, gv, heads):
    groups, rows, cols = q_ref.shape
    length = groups * rows
    block = min(QROWS, length)
    kv = kv_ref[...].reshape(length, 2 * HD)
    keys, values = kv[:, :HD], kv[:, HD:]
    keys_t = keys.T
    per = block // rows
    gk[...] = jnp.zeros_like(gk)
    gv[...] = jnp.zeros_like(gv)
    for b in range(length // block):
        limit = (b + 1) * block
        q_rows = q_ref[b * per : (b + 1) * per].reshape(block, cols)
        g_rows = g_ref[b * per : (b + 1) * per].reshape(block, cols)
        for h in range(heads):
            q = q_rows[:, h * HD : (h + 1) * HD]
            g = g_rows[:, h * HD : (h + 1) * HD]
            scores, allowed = masked_scores(docs, stream, keys[:limit], q, b * block, limit)
            shift = lse_ref[h : h + 1, b * block : (b + 1) * block]
            probs = jnp.where(allowed, jnp.exp(scores - shift), 0.0)
            grad_probs = dot_nt(values[:limit], g)
            weighted = probs * grad_probs
            delta = jnp.sum(weighted, axis=0, keepdims=True)
            grad_scores = (weighted - probs * delta).astype(bf16)
            gq = dot(keys_t[:, :limit], grad_scores) * (HD**-0.5)
            gq_ref[b * per : (b + 1) * per, :, h * HD : (h + 1) * HD] = (
                gq.T.astype(bf16).reshape(per, rows, HD)
            )
            gk[:limit, :] += dot(grad_scores, q)
            gv[:limit, :] += dot(probs.astype(bf16), g)
    gkv_ref[:, :, :HD] = (gk[...] * (HD**-0.5)).astype(bf16).reshape(groups, rows, HD)
    gkv_ref[:, :, HD:] = gv[...].astype(bf16).reshape(groups, rows, HD)


def attend_back_scatter_proj(
    docs, queries, keyval, grads, lse, act, wp, hidden1, residual, b_proj, layers, heads, number
):
    groups, streams, rows, cols = queries.shape
    kv_cols = keyval.shape[3]
    length = groups * rows
    total, depth = act.shape
    own = total // PLANE
    wide = wp.shape[1]
    part = hidden1.shape[1] // PLANE

    def kernel(docs_ref, q_ref, kv_ref, g_ref, lse_ref, act_ref, wp_ref, h_ref, *refs):
        residual_ref, bias_ref = refs[:2]
        gq_out, gkv_out, gq_sum, gkv_sum, dwq_out, dwkv_out, out_ref = refs[2:9]
        a_buf, w_buf, q_buf, kv_buf, g_buf, grad_buf, gk, gv, h_buf = refs[9:18]
        dwq_buf, dwkv_buf = refs[18:20]
        s, local = refs[20:33], refs[33]
        p = Place()
        loads = [load(act_ref, a_buf, local.at[0]), load(wp_ref, w_buf, local.at[1])]
        ins = [
            load(q_ref, q_buf, local.at[2]),
            load(kv_ref, kv_buf, local.at[3]),
            load(g_ref, g_buf, local.at[4]),
        ]

        def h_fetch(i):
            return load(h_ref.at[:, pl.ds(i * part, part)], h_buf.at[i % 2], local.at[5 + i % 2])

        tiles = [h_fetch(0)]
        p.greet()
        for copy in loads:
            copy.wait()
        stores = []

        def idle():
            for copy in ins:
                copy.wait()
            for stream in range(streams):
                attend_stream_back(
                    docs_ref,
                    stream,
                    q_buf.at[:, stream],
                    kv_buf.at[:, stream],
                    g_buf.at[:, stream],
                    lse_ref.at[stream],
                    grad_buf.at[:, stream, :, pl.ds(0, cols)],
                    grad_buf.at[:, stream, :, pl.ds(cols, kv_cols)],
                    gk,
                    gv,
                    heads,
                )
            stores.append(load(grad_buf.at[:, :, :, pl.ds(0, cols)], gq_out, local.at[7]))
            stores.append(load(grad_buf.at[:, :, :, pl.ds(cols, kv_cols)], gkv_out, local.at[8]))
            grad = grad_buf[...].reshape(total, cols + kv_cols)
            sums = jnp.sum(grad.astype(f32), axis=0, keepdims=True)
            gq_sum[...] = sums[:, :cols]
            gkv_sum[...] = sums[:, cols:]
            for i in range(PLANE):
                tiles[i].wait()
                if i + 1 < PLANE:
                    tiles.append(h_fetch(i + 1))
                term = dot_tn(h_buf[i % 2], grad).astype(bf16)
                dwq_buf[i] = term[:, :cols].reshape(layers, part // layers, cols)
                dwkv_buf[i] = term[:, cols:]
            stores.append(load(dwq_buf, dwq_out, local.at[9]))
            stores.append(load(dwkv_buf, dwkv_out, local.at[10]))

        def emit(line, value):
            out_ref[line, :] = residual_ref[line, :] + value + bias_ref[...]

        Scatter.take(p, own, s).run(plain_product(a_buf, w_buf), emit, idle)
        for copy in stores:
            copy.wait()

    return pl.pallas_call(
        kernel,
        out_shape=[
            jax.ShapeDtypeStruct(queries.shape, bf16),
            jax.ShapeDtypeStruct(keyval.shape, bf16),
            jax.ShapeDtypeStruct((1, cols), f32),
            jax.ShapeDtypeStruct((1, kv_cols), f32),
            jax.ShapeDtypeStruct((PLANE, layers, part // layers, cols), bf16),
            jax.ShapeDtypeStruct((PLANE, part, kv_cols), bf16),
            jax.ShapeDtypeStruct((own, wide), f32),
        ],
        in_specs=[pl.BlockSpec(memory_space=pltpu.SMEM)]
        + [ANY] * 3
        + [WHOLE]
        + [ANY] * 3
        + [WHOLE] * 2,
        out_specs=[ANY, ANY, WHOLE, WHOLE, ANY, ANY, WHOLE],
        scratch_shapes=[
            pltpu.VMEM(act.shape, bf16),
            pltpu.VMEM(wp.shape, bf16),
            pltpu.VMEM(queries.shape, bf16),
            pltpu.VMEM(keyval.shape, bf16),
            pltpu.VMEM(grads.shape, bf16),
            pltpu.VMEM((groups, streams, rows, cols + kv_cols), bf16),
            pltpu.VMEM((length, HD), f32),
            pltpu.VMEM((length, HD), f32),
            pltpu.VMEM((2, total, part), bf16),
            pltpu.VMEM((PLANE, layers, part // layers, cols), bf16),
            pltpu.VMEM((PLANE, part, kv_cols), bf16),
        ]
        + Scatter.scratch(own, wide)
        + [sems(11)],
        compiler_params=params(number),
        cost_estimate=cost(2 * total * depth * wide),
        name="attend_back_scatter_proj",
    )(docs, queries, keyval, grads, lse, act, wp, hidden1, residual, b_proj)


def pack_vectors(vectors):
    sizes = [v.shape[0] for v in vectors]
    lines = -(-sum(sizes) // (PLANE * 8 * 128)) * 8
    pad = PLANE * lines * 128 - sum(sizes)
    return jnp.concatenate(vectors + (jnp.zeros((pad,), f32),)).reshape(PLANE, lines, 128)


def unpack_vectors(packed, vectors):
    flat = packed.reshape(-1)
    sums, at = [], 0
    for v in vectors:
        sums.append(flat[at : at + v.shape[0]])
        at += v.shape[0]
    return sums


def after(value, *earlier):
    return lax.optimization_barrier((value, *earlier))[0]


def line_gather(shard, axis=0):
    return lax.all_gather(shard, "fsdp", axis=axis, tiled=True)


def line_scatter(grad, axis=0):
    return lax.psum_scatter(grad.astype(bf16), "fsdp", scatter_dimension=axis, tiled=True)


def column_weight_grad(grad, groups):
    rows, cols = grad.shape
    return line_scatter(grad.reshape(groups, rows // groups, cols), 1)


def shards(
    tokens,
    doc_starts,
    w_query,
    w_kv,
    w_out,
    w_fc,
    w_proj,
    ln1_gain,
    ln1_bias,
    b_query,
    b_value,
    b_out,
    ln2_gain,
    ln2_bias,
    b_fc,
    b_proj,
    cotangent,
):
    layers = lax.axis_size("fsdp")
    me = lax.axis_index("seq")
    streams, rows, width = tokens.shape
    own = streams * rows
    heads = HEADS // PLANE
    hidden = b_fc.shape[0]
    my_cols = heads * HD
    my_hidden = hidden // PLANE
    total = PLANE * own

    own_tokens = tokens.reshape(own, width)
    cot_low = cotangent.reshape(own, width)

    def row(vector):
        return vector.reshape(1, -1)

    wq_pieces, wf_pieces, low_kv, wo, low_hidden1, mean1, inverse1 = split_weights(
        own_tokens, row(ln1_gain), row(ln1_bias), w_query, w_fc, w_kv, w_out, layers, 1
    )
    wf = line_gather(wf_pieces, 1).reshape(width, my_hidden)
    wp = line_gather(w_proj)
    my_bq = row(lax.dynamic_slice_in_dim(b_query, me * my_cols, my_cols, 0))
    my_bf = row(lax.dynamic_slice_in_dim(b_fc, me * my_hidden, my_hidden, 0))
    bkv = row(jnp.concatenate([jnp.zeros((HD,), f32), b_value]))

    hidden1, w_kv_all, wq = gather_hidden1(low_hidden1, low_kv, wq_pieces, layers, 2)
    wq = wq.reshape(width, my_cols)
    cot_all, queries, keyval, mixed, lse = project_attend(
        doc_starts, hidden1, wq, w_kv_all, my_bq, bkv, cot_low, streams, heads, 3
    )
    mixed_rows = mixed.reshape(total, my_cols)
    residual, low_hidden2, mean2, inverse2 = scatter_attn(
        mixed_rows, wo, own_tokens, row(b_out), row(ln2_gain), row(ln2_bias), 4
    )
    hidden2, act_low, slope, grad_w_proj = gather_fc(low_hidden2, wf, my_bf, cot_all, 5)
    shard_proj = line_scatter(grad_w_proj)

    grad_residual, grad_attn, sums2, my_grad_b_fc, grad_w_fc = scatter_fc(
        cot_all, slope, wp, wf, hidden2, cot_low, residual, mean2, inverse2, row(ln2_gain), 6
    )
    fc_pieces = column_weight_grad(grad_w_fc, PLANE)
    grad_mixed, grad_w_out = gather_out(grad_attn, wo, mixed_rows, 7)
    gq, gkv, my_grad_b_query, sums_kv, grad_w_query, grad_w_kv, output = attend_back_scatter_proj(
        doc_starts,
        queries,
        keyval,
        after(grad_mixed, shard_proj).reshape(PLANE, streams, rows, my_cols),
        lse,
        act_low,
        wp,
        hidden1,
        residual,
        row(b_proj),
        layers,
        heads,
        8,
    )
    input_grad, sums1, shard_out, shard_query, shard_kv = scatter_query(
        gq.reshape(total, my_cols),
        gkv.reshape(total, 2 * HD),
        wq,
        w_kv_all,
        grad_w_out,
        grad_w_query,
        grad_w_kv,
        (own_tokens, mean1, inverse1, row(ln1_gain), grad_residual),
        layers,
        9,
    )

    zero = jnp.zeros_like
    grad_b_query = lax.dynamic_update_slice_in_dim(
        zero(b_query), my_grad_b_query.reshape(-1), me * my_cols, 0
    )
    grad_b_fc = lax.dynamic_update_slice_in_dim(
        zero(b_fc), my_grad_b_fc.reshape(-1), me * my_hidden, 0
    )
    vectors = (
        sums1[0],
        sums1[1],
        grad_b_query,
        sums_kv[0, HD:],
        sums2[2],
        sums2[0],
        sums2[1],
        grad_b_fc,
        sums2[3],
    )
    packed, shard_fc = last_exchange(pack_vectors(vectors), fc_pieces, layers, 10)
    sums = unpack_vectors(packed, vectors)
    return (
        output.reshape(streams, rows, width),
        input_grad.reshape(streams, rows, width),
        shard_query.astype(f32),
        shard_kv,
        shard_out,
        shard_fc.astype(f32),
        shard_proj.astype(f32),
        *sums,
    )


def gather_seq(block):
    return lax.all_gather(block, "seq", axis=0, tiled=True)


def scatter_seq(partial):
    return lax.psum_scatter(partial.astype(bf16), "seq", scatter_dimension=0, tiled=True).astype(f32)


def columns_to_rows(part, groups):
    rows = part.shape[0]
    spread = part.reshape(rows, groups, part.shape[1] // groups).transpose(1, 0, 2)
    return lax.all_to_all(spread, "seq", split_axis=0, concat_axis=0, tiled=True)


def column_weight(shard, groups):
    pieces = columns_to_rows(shard, groups)
    full = lax.all_gather(pieces, "fsdp", axis=1, tiled=True)
    return full.reshape(-1, full.shape[2])


def plain_column_grad(grad, groups):
    rows, cols = grad.shape
    kept = lax.psum_scatter(
        grad.astype(bf16).reshape(groups, rows // groups, cols), "fsdp", scatter_dimension=1, tiled=True
    )
    moved = lax.all_to_all(kept, "seq", split_axis=0, concat_axis=0, tiled=True)
    return moved.transpose(1, 0, 2).reshape(moved.shape[1], groups * cols).astype(f32)


def row_weight_grad(grad):
    return lax.psum_scatter(grad.astype(bf16), "fsdp", scatter_dimension=0, tiled=True).astype(f32)


def plain_attend(queries, keyval, starts, groups, streams, rows, heads):
    length = groups * rows
    scale = HD ** (-0.5)
    position = jnp.arange(length, dtype=jnp.int32)
    mixed_list, lse_list = [], []
    for stream in range(streams):
        q = queries[:, stream].reshape(length, heads, HD)
        k = keyval[:, stream, :, :HD].reshape(length, HD)
        v = keyval[:, stream, :, HD:].reshape(length, HD)
        segment = jnp.sum((starts[stream][None, :] <= position[:, None]).astype(jnp.int32), axis=1)
        allowed = (position[None, :] <= position[:, None]) & (segment[None, :] == segment[:, None])
        scores = jnp.einsum("thd,ud->htu", q, k, preferred_element_type=f32) * scale
        scores = jnp.where(allowed[None], scores, -1e30)
        top = jnp.max(scores, axis=-1, keepdims=True)
        lse = top + jnp.log(jnp.sum(jnp.exp(scores - top), axis=-1, keepdims=True))
        probs = jnp.exp(scores - lse).astype(bf16)
        mixed = jnp.einsum("htu,ud->thd", probs, v, preferred_element_type=f32)
        mixed_list.append(mixed.astype(bf16).reshape(groups, rows, heads * HD))
        lse_list.append(lse)
    return jnp.stack(mixed_list, axis=1), lse_list


def plain_attend_back(queries, keyval, grads, lse_list, starts, groups, streams, rows, heads):
    length = groups * rows
    scale = HD ** (-0.5)
    position = jnp.arange(length, dtype=jnp.int32)
    gq_list, gkv_list = [], []
    for stream in range(streams):
        q = queries[:, stream].reshape(length, heads, HD)
        g = grads[:, stream].reshape(length, heads, HD)
        k = keyval[:, stream, :, :HD].reshape(length, HD)
        v = keyval[:, stream, :, HD:].reshape(length, HD)
        segment = jnp.sum((starts[stream][None, :] <= position[:, None]).astype(jnp.int32), axis=1)
        allowed = (position[None, :] <= position[:, None]) & (segment[None, :] == segment[:, None])
        scores = jnp.einsum("thd,ud->htu", q, k, preferred_element_type=f32) * scale
        probs = jnp.exp(jnp.where(allowed[None], scores, -1e30) - lse_list[stream])
        grad_probs = jnp.einsum("thd,ud->htu", g, v, preferred_element_type=f32)
        delta = jnp.sum(probs * grad_probs, axis=-1, keepdims=True)
        gs = (probs * (grad_probs - delta)).astype(bf16)
        gq = jnp.einsum("htu,ud->thd", gs, k, preferred_element_type=f32) * scale
        gk = jnp.einsum("htu,thd->ud", gs, q, preferred_element_type=f32) * scale
        gv = jnp.einsum("htu,thd->ud", probs.astype(bf16), g, preferred_element_type=f32)
        gq_list.append(gq.astype(bf16).reshape(groups, rows, heads * HD))
        gkv_list.append(jnp.concatenate([gk, gv], axis=1).reshape(groups, rows, 2 * HD))
    return jnp.stack(gq_list, axis=1), jnp.stack(gkv_list, axis=1)


def plain_shards(
    tokens,
    doc_starts,
    w_query,
    w_kv,
    w_out,
    w_fc,
    w_proj,
    ln1_gain,
    ln1_bias,
    b_query,
    b_value,
    b_out,
    ln2_gain,
    ln2_bias,
    b_fc,
    b_proj,
    cotangent,
):
    groups = lax.axis_size("seq")
    me = lax.axis_index("seq")
    streams, rows, width = tokens.shape
    own = streams * rows
    heads = HEADS // groups
    hidden = b_fc.shape[0]
    my_cols = heads * HD
    my_hidden = hidden // groups

    wq = column_weight(w_query, groups)
    w_kv_all = gather_seq(lax.all_gather(w_kv, "fsdp", axis=0, tiled=True))
    wo = lax.all_gather(w_out, "fsdp", axis=0, tiled=True)
    wf = column_weight(w_fc, groups)
    wp = lax.all_gather(w_proj, "fsdp", axis=0, tiled=True)
    my_bq = lax.dynamic_slice_in_dim(b_query, me * my_cols, my_cols, 0)
    my_bf = lax.dynamic_slice_in_dim(b_fc, me * my_hidden, my_hidden, 0)

    inputs = tokens.reshape(own, width).astype(f32)
    cot_low = cotangent.reshape(own, width)
    cot_full = cot_low.astype(f32)
    shifted1, normed1, inverse1 = normalize(inputs, ln1_gain, ln1_bias)
    hidden1 = gather_seq(shifted1.astype(bf16))
    queries = (dot(hidden1, wq) + my_bq).astype(bf16).reshape(groups, streams, rows, my_cols)
    value_shift = jnp.concatenate([jnp.zeros((HD,), f32), b_value])
    keyval = (dot(hidden1, w_kv_all) + value_shift).astype(bf16).reshape(groups, streams, rows, 2 * HD)
    mixed, lse = plain_attend(queries, keyval, doc_starts, groups, streams, rows, heads)
    mixed_rows = mixed.reshape(groups * own, my_cols)
    residual = inputs + scatter_seq(dot(mixed_rows, wo)) + b_out
    shifted2, normed2, inverse2 = normalize(residual, ln2_gain, ln2_bias)
    hidden2 = gather_seq(shifted2.astype(bf16))
    cot_all = gather_seq(cot_low)
    pre_act = dot(hidden2, wf) + my_bf
    activated, slope = gelu_pair(pre_act)
    act_low = activated.astype(bf16)
    output = residual + scatter_seq(dot(act_low, wp)) + b_proj

    grad_b_proj = jnp.sum(cot_full, axis=0)
    shard_proj = row_weight_grad(dot_tn(act_low, cot_all))
    grad_pre = (dot_nt(cot_all, wp) * slope).astype(bf16)
    my_grad_b_fc = jnp.sum(grad_pre.astype(f32), axis=0)
    shard_fc = plain_column_grad(dot_tn(hidden2, grad_pre), groups)
    grad_hidden2 = scatter_seq(dot_nt(grad_pre, wf))
    back_second, grad_ln2_gain, grad_ln2_bias = normalize_back(
        grad_hidden2, normed2, inverse2, ln2_gain
    )
    grad_residual = cot_full + back_second
    grad_attn = grad_residual.astype(bf16)
    grad_b_out = jnp.sum(grad_attn.astype(f32), axis=0)
    grad_attn_all = gather_seq(grad_attn)
    shard_out = row_weight_grad(dot_tn(mixed_rows, grad_attn_all))
    grad_mixed = dot_nt(grad_attn_all, wo).astype(bf16).reshape(groups, streams, rows, my_cols)
    gq, gkv = plain_attend_back(
        queries, keyval, grad_mixed, lse, doc_starts, groups, streams, rows, heads
    )
    gq_rows = gq.reshape(groups * own, my_cols)
    gkv_rows = gkv.reshape(groups * own, 2 * HD)
    my_grad_b_query = jnp.sum(gq_rows.astype(f32), axis=0)
    grad_b_value = jnp.sum(gkv_rows[:, HD:], axis=0)
    gkv_low = gkv_rows.astype(bf16)
    shard_query = plain_column_grad(dot_tn(hidden1, gq_rows), groups)
    shard_kv = row_weight_grad(scatter_seq(dot_tn(hidden1, gkv_low)))
    grad_hidden1 = scatter_seq(dot_nt(gq_rows, wq) + dot_nt(gkv_low, w_kv_all))
    back_first, grad_ln1_gain, grad_ln1_bias = normalize_back(
        grad_hidden1, normed1, inverse1, ln1_gain
    )
    input_grad = grad_residual + back_first

    zero = jnp.zeros_like
    grad_b_query = lax.dynamic_update_slice_in_dim(zero(b_query), my_grad_b_query, me * my_cols, 0)
    grad_b_fc = lax.dynamic_update_slice_in_dim(zero(b_fc), my_grad_b_fc, me * my_hidden, 0)
    vectors = (
        grad_ln1_gain,
        grad_ln1_bias,
        grad_b_query,
        grad_b_value,
        grad_b_out,
        grad_ln2_gain,
        grad_ln2_bias,
        grad_b_fc,
        grad_b_proj,
    )
    sums = lax.psum(vectors, ("seq", "fsdp"))
    return (
        output.reshape(streams, rows, width),
        input_grad.reshape(streams, rows, width),
        shard_query,
        shard_kv,
        shard_out,
        shard_fc,
        shard_proj,
        *sums,
    )


def solution(mesh):
    acts = P("fsdp", "seq", None)
    weight = P(("seq", "fsdp"), None)
    return jax.shard_map(
        shards if mesh.shape["seq"] == PLANE else plain_shards,
        mesh=mesh,
        in_specs=(acts, P("fsdp", None)) + (weight,) * 5 + (P(),) * 9 + (acts,),
        out_specs=(acts, acts) + (weight,) * 5 + (P(),) * 9,
        check_vma=False,
    )
```

```python
import functools

import jax
import jax.numpy as jnp
from jax import lax
from jax.experimental import pallas as pl
from jax.experimental.pallas import tpu as pltpu
from jax.sharding import PartitionSpec as P

HEADS = 16
HD = 128

root_two_pi = 0.7978845608028654
cubic_coef = 0.044715
epsilon = 1e-05
f32 = jnp.float32
bf16 = jnp.bfloat16
MESH = pl.DeviceIdType.MESH
ANY = pl.BlockSpec(memory_space=pl.ANY)
WHOLE = pl.BlockSpec(memory_space=pltpu.VMEM)
VMEM_LIMIT = 56 * 1024 * 1024
PLANE = 8


def normalize(values, gain_row, shift_row):
    center = values - jnp.mean(values, axis=-1, keepdims=True)
    inverse = lax.rsqrt(jnp.mean(center * center, axis=-1, keepdims=True) + epsilon)
    normed = center * inverse
    return (normed * gain_row + shift_row, normed, inverse)


def normalize_back(grad_out, normed, inverse, gain_row):
    scaled = grad_out * gain_row
    grad_in = inverse * (
        scaled
        - jnp.mean(scaled, axis=-1, keepdims=True)
        - normed * jnp.mean(scaled * normed, axis=-1, keepdims=True)
    )
    return (grad_in, jnp.sum(grad_out * normed, axis=0), jnp.sum(grad_out, axis=0))


def norm_stats(values):
    mean = jnp.mean(values, axis=-1, keepdims=True)
    center = values - mean
    return mean, lax.rsqrt(jnp.mean(center * center, axis=-1, keepdims=True) + epsilon)


def norm_back(grad_out, normed, inverse, gain_row):
    scaled = grad_out * gain_row
    return inverse * (
        scaled
        - jnp.mean(scaled, axis=-1, keepdims=True)
        - normed * jnp.mean(scaled * normed, axis=-1, keepdims=True)
    )


def gelu_pair(inputs):
    tangent = jnp.tanh(root_two_pi * (inputs + cubic_coef * inputs * inputs * inputs))
    activated = 0.5 * inputs * (1.0 + tangent)
    gradient_slope = 0.5 * (1.0 + tangent) + 0.5 * inputs * (
        1.0 - tangent * tangent
    ) * root_two_pi * (1.0 + 3.0 * cubic_coef * inputs * inputs)
    return (activated, gradient_slope)


def dot(a, b):
    return jnp.dot(a, b, preferred_element_type=f32)


def dot_nt(a, b):
    return lax.dot_general(a, b, (((1,), (1,)), ((), ())), preferred_element_type=f32)


def dot_tn(a, b):
    return lax.dot_general(a, b, (((0,), (0,)), ((), ())), preferred_element_type=f32)


def push(src, dst, send, recv, to):
    return pltpu.make_async_remote_copy(
        src_ref=src, dst_ref=dst, send_sem=send, recv_sem=recv, device_id=to, device_id_type=MESH
    )


def sems(*shape):
    return pltpu.SemaphoreType.DMA(shape)


def rows_at(start, size):
    return pl.ds(pl.multiple_of(start, size), size)


class Place:
    def __init__(self):
        me = lax.axis_index("seq")
        self.me = me
        self.core = lax.rem(me, 2)
        x = lax.rem(lax.div(me, 2), 2)
        y = lax.div(me, 4)
        self.sib = me + 1 - 2 * self.core
        self.xn = me + 2 - 4 * x
        self.yn = me + 4 - 8 * y
        self.dg = me + 2 - 4 * x + 4 - 8 * y
        turn = 1 - 2 * self.core
        self.xs, self.ys, self.ds = self.xn + turn, self.yn + turn, self.dg + turn
        self.layer = lax.axis_index("fsdp")

    def plane_peer(self, step):
        return lax.rem(self.me + step, PLANE)

    def line_peer(self, step, layers):
        return lax.rem(self.layer + step, layers)

    def greet(self, whole_plane=False, layers=1):
        barrier = pltpu.get_barrier_semaphore()
        if whole_plane:
            others = [self.plane_peer(step) for step in range(1, PLANE)]
        else:
            others = [self.sib, self.xn, self.yn]
        for other in others:
            pl.semaphore_signal(barrier, inc=1, device_id={"seq": other}, device_id_type=MESH)
        for step in range(1, layers):
            other = self.line_peer(step, layers)
            pl.semaphore_signal(barrier, inc=1, device_id={"fsdp": other}, device_id_type=MESH)
        pl.semaphore_wait(barrier, len(others) + layers - 1)


class Gather:
    sends = 14
    scratch = [sems(14), sems(PLANE, 2)]

    def __init__(self, place, buf, rows, send, recv):
        self.p, self.buf, self.rows, self.half = place, buf, rows, rows // 2
        self.send_sem, self.recv_sem = send, recv
        self.copies = []

    def piece(self, dev, half):
        return self.buf.at[rows_at(dev * self.rows + half * self.half, self.half), :]

    def pair(self, dev):
        return rows_at(lax.div(dev, 2) * (2 * self.rows), 2 * self.rows)

    def send(self, dev, half, to, src=None):
        k = len(self.copies)
        piece = self.piece(dev, half)
        copy = push(
            piece if src is None else src,
            piece,
            self.send_sem.at[k],
            self.recv_sem.at[dev, half],
            {"seq": to},
        )
        copy.start()
        self.copies.append(copy)

    def arrived(self, dev, half):
        piece = self.piece(dev, half)
        push(
            piece, piece, self.send_sem.at[0], self.recv_sem.at[dev, half], {"seq": self.p.sib}
        ).wait_recv()

    def start(self, own):
        p = self.p
        parts = [own.at[pl.ds(h * self.half, self.half), :] for h in range(2)]
        self.send(p.me, 0, p.yn, parts[0])
        self.send(p.me, 1, p.xn, parts[1])
        self.send(p.me, 1, p.yn, parts[1])
        self.send(p.me, 0, p.xn, parts[0])
        for h in range(2):
            self.send(p.me, h, p.sib, parts[h])

    def relay_first(self):
        p = self.p
        self.arrived(p.yn, 0)
        self.send(p.yn, 0, p.xn)
        self.arrived(p.xn, 1)
        self.send(p.xn, 1, p.yn)
        self.send(p.yn, 0, p.sib)
        self.send(p.xn, 1, p.sib)

    def relay_rest(self):
        p = self.p
        self.arrived(p.xn, 0)
        self.send(p.xn, 0, p.sib)
        self.arrived(p.yn, 1)
        self.send(p.yn, 1, p.sib)

    def relay(self):
        self.relay_first()
        self.relay_rest()

    def have(self, dev):
        self.arrived(dev, 0)
        self.arrived(dev, 1)

    def relay_corner(self):
        p = self.p
        for h in range(2):
            self.arrived(p.dg, h)
            self.send(p.dg, h, p.sib)

    def finish(self):
        for copy in self.copies:
            copy.wait_send()


class Scatter:
    LINES = 32

    def __init__(
        self, place, rows, acc, part, sib_out, sib_in, boxes, sib_send, sib_recv, send, recv
    ):
        self.p, self.rows, self.half = place, rows, rows // 2
        self.wide = part.shape[2]
        self.acc, self.part, self.sib_out, self.sib_in = acc, part, sib_out, sib_in
        self.out_d, self.out_x, self.out_y, self.in_d, self.in_x, self.in_y = boxes
        self.sib_send, self.sib_recv, self.send, self.recv = sib_send, sib_recv, send, recv
        self.copies = []

    @staticmethod
    def scratch(rows, wide):
        return [
            pltpu.VMEM((2 * rows, wide // 2), f32),
            pltpu.VMEM((4, rows, wide), f32),
            pltpu.VMEM((4, rows, wide), bf16),
            pltpu.VMEM((4, rows, wide), bf16),
            *[pltpu.VMEM((rows, wide), bf16)] * 6,
            sems(4, 2),
            sems(4, 2),
            sems(8),
            sems(8),
        ]

    @classmethod
    def take(cls, place, rows, refs):
        return cls(place, rows, *refs[:4], refs[4:10], *refs[10:14])

    refs = 14

    def cols(self, c):
        return pl.ds(c * (self.wide // 2), self.wide // 2)

    def swap(self, role, dev, product, c):
        p = self.p
        self.acc[...] = product(role, rows_at(lax.div(dev, 2) * (2 * self.rows), 2 * self.rows), c)
        theirs = rows_at((1 - p.core) * self.rows, self.rows)
        ours = rows_at(p.core * self.rows, self.rows)
        self.sib_out[role, :, self.cols(c)] = self.acc[theirs, :].astype(bf16)
        copy = push(
            self.sib_out.at[role, :, self.cols(c)],
            self.sib_in.at[role, :, self.cols(c)],
            self.sib_send.at[role, c],
            self.sib_recv.at[role, c],
            {"seq": p.sib},
        )
        copy.start()
        self.copies.append(copy)
        self.part[role, :, self.cols(c)] = self.acc[ours, :]
        return copy

    def swap_all(self, role, dev, product):
        return [self.swap(role, dev, product, c) for c in range(2)]

    def add_into(self, dst, role, first, size, more=(), cols=slice(None)):
        lines = self.LINES

        @pl.loop(0, size // lines)
        def _(i):
            line = rows_at(first + i * lines, lines)
            value = self.part[role, line, cols] + self.sib_in[role, line, cols].astype(f32)
            for ref in more:
                value = value + ref[line, cols].astype(f32)
            if dst is None:
                self.emit(line, value)
            else:
                dst[line, cols] = value.astype(dst.dtype)

    def ship(self, src, dst, h, k, to, cols=slice(None)):
        lines = pl.ds(h * self.half, self.half)
        copy = push(
            src.at[lines, cols], dst.at[lines, cols], self.send.at[k], self.recv.at[k], {"seq": to}
        )
        copy.start()
        self.copies.append(copy)
        return copy

    def ship_corner(self, c):
        cols = self.cols(c)
        self.add_into(self.out_d, 0, 0, self.rows, (), cols)
        return (
            self.ship(self.out_d, self.in_d, 0, 2 * c, self.p.xn, cols),
            self.ship(self.out_d, self.in_d, 1, 2 * c + 1, self.p.yn, cols),
        )

    def run(self, product, emit, idle=None, early=None):
        p, rows, half = self.p, self.rows, self.half
        self.emit = emit
        d0 = self.swap(0, p.dg, product, 0)
        d1 = self.swap(0, p.dg, product, 1)
        d0.wait_recv()
        dx0, dy0 = self.ship_corner(0)
        to_x = [self.swap(1, p.xn, product, 0)]
        d1.wait_recv()
        dx1, dy1 = self.ship_corner(1)
        to_x.append(self.swap(1, p.xn, product, 1))
        to_y = self.swap_all(2, p.yn, product)
        for copy in to_x:
            copy.wait_recv()
        self.add_into(self.out_x, 1, 0, half)
        x0 = self.ship(self.out_x, self.in_x, 0, 4, p.xn)
        for copy in to_y:
            copy.wait_recv()
        self.add_into(self.out_y, 2, half, half)
        y1 = self.ship(self.out_y, self.in_y, 1, 5, p.yn)
        to_me = self.swap_all(3, p.me, product)
        if early is not None:
            early()
        dy0.wait_recv()
        dy1.wait_recv()
        self.add_into(self.out_x, 1, half, half, (self.in_d,))
        x1 = self.ship(self.out_x, self.in_x, 1, 6, p.xn)
        dx0.wait_recv()
        dx1.wait_recv()
        self.add_into(self.out_y, 2, 0, half, (self.in_d,))
        y0 = self.ship(self.out_y, self.in_y, 0, 7, p.yn)
        if idle is not None:
            idle()
        for copy in to_me:
            copy.wait_recv()
        x0.wait_recv()
        y0.wait_recv()
        self.add_into(None, 3, 0, half, (self.in_x, self.in_y))
        y1.wait_recv()
        x1.wait_recv()
        self.add_into(None, 3, half, half, (self.in_x, self.in_y))
        for copy in self.copies:
            copy.wait_send()


class LineGather:
    def __init__(self, place, src, out, layers, send, recv):
        self.p, self.src, self.out, self.layers = place, src, out, layers
        self.send, self.recv = send, recv
        self.moves = [d for d in (2, -2, 1, -1) if abs(d) < layers]

    def block(self, layer):
        rows = self.src.shape[0]
        return self.out.at[rows_at(layer * rows, rows), :]

    def copy(self, src, layer, k, to):
        return push(src, self.block(layer), self.send.at[k], self.recv.at[layer], {"fsdp": to})

    def inside(self, layer):
        return (layer >= 0) & (layer < self.layers)

    def start(self):
        me = self.p.layer
        for k, d in enumerate(self.moves):

            @pl.when(self.inside(me + d))
            def _(k=k, d=d):
                self.copy(self.src, me, k, me + d).start()

    def wait_from(self, layer):
        block = self.block(layer)
        other = lax.rem(self.p.layer + 1, self.layers)
        push(block, block, self.send.at[0], self.recv.at[layer], {"fsdp": other}).wait_recv()

    def passing(self):
        me = self.p.layer
        found = []
        for far in range(3, self.layers):
            for sign in (1, -1):
                source, to = me - sign * (far - 1), me + sign
                found.append((self.inside(source) & self.inside(to), source, to))
        return found

    def relay(self):
        for k, (here, source, to) in enumerate(self.passing()):

            @pl.when(here)
            def _(k=k, source=source, to=to):
                self.wait_from(source)
                self.copy(self.block(source), source, len(self.moves) + k, to).start()

    def finish(self):
        me = self.p.layer
        passed = self.passing()
        for step in range(1, self.layers):
            source = lax.rem(me + step, self.layers)
            waited = None
            for here, whose, _ in passed:
                hit = here & (whose == source)
                waited = hit if waited is None else waited | hit
            if waited is None:
                self.wait_from(source)
            else:
                pl.when(jnp.logical_not(waited))(lambda source=source: self.wait_from(source))
        for k, d in enumerate(self.moves):

            @pl.when(self.inside(me + d))
            def _(k=k, d=d):
                self.copy(self.src, me, k, me + d).wait_send()

        for k, (here, source, to) in enumerate(passed):

            @pl.when(here)
            def _(k=k, source=source, to=to):
                self.copy(self.block(source), source, len(self.moves) + k, to).wait_send()

    @staticmethod
    def scratch(layers):
        return [sems(4 + 2 * max(0, layers - 3)), sems(layers)]


class LineSum:
    def __init__(self, place, block, box, layers, send, recv, room=None, local=None):
        self.box, self.send, self.recv, self.room, self.local = box, send, recv, room, local
        self.block = block
        self.passing = room is not None and layers == 4
        if not self.passing:
            self.copies = []
            for step in range(1, layers):
                to = place.line_peer(step, layers)
                copy = push(
                    block(to), box.at[step - 1], send.at[step], recv.at[step], {"fsdp": to}
                )
                copy.start()
                self.copies.append(copy)
            return
        side = lax.div(place.layer, 2)
        self.end, self.mid = 3 * side, 1 + side
        self.far_end, self.far_mid = 3 - 3 * side, 2 - side
        self.is_end = place.layer == self.end
        self.is_mid = jnp.logical_not(self.is_end)

        @pl.when(self.is_end)
        def _():
            box[2] = jnp.zeros(box.shape[1:], box.dtype)
            for copy in self.end_sends():
                copy.start()

        @pl.when(self.is_mid)
        def _():
            self.own_far().start()
            for copy in self.mid_sends():
                copy.start()

    def move(self, src, dst, k, slot, to):
        return push(src, dst, self.send.at[k], self.recv.at[slot], {"fsdp": to})

    def end_sends(self):
        return (
            self.move(self.block(self.far_end), self.room.at[0], 0, 3, self.mid),
            self.move(self.block(self.far_mid), self.box.at[2], 2, 2, self.far_mid),
            self.move(self.block(self.mid), self.box.at[0], 1, 0, self.mid),
        )

    def mid_sends(self):
        return (
            self.move(self.block(self.far_mid), self.box.at[1], 1, 1, self.far_mid),
            self.move(self.block(self.end), self.box.at[0], 0, 0, self.end),
        )

    def own_far(self):
        return pltpu.make_async_copy(self.block(self.far_end), self.room.at[1], self.local)

    def passed_on(self):
        return self.move(self.room.at[1], self.box.at[1], 2, 1, self.far_end)

    def relay(self):
        if not self.passing:
            return

        @pl.when(self.is_mid)
        def _():
            self.own_far().wait()
            self.move(self.room.at[0], self.room.at[0], 0, 3, self.end).wait_recv()
            total = self.room[0].astype(f32) + self.room[1].astype(f32)
            self.room[1] = total.astype(bf16)
            self.passed_on().start()

    def arrived(self):
        if not self.passing:
            for copy in self.copies:
                copy.wait_recv()
            return
        for slot in range(2):
            here = self.box.at[slot]
            self.move(here, here, 0, slot, self.far_mid).wait_recv()

        @pl.when(self.is_mid)
        def _():
            here = self.box.at[2]
            self.move(here, here, 0, 2, self.far_mid).wait_recv()

    def total(self, own, where):
        value = own.astype(f32)
        for k in range(self.box.shape[0]):
            value = value + self.box[(k, *where)].astype(f32)
        return value

    def finish(self):
        if not self.passing:
            for copy in self.copies:
                copy.wait_send()
            return

        @pl.when(self.is_end)
        def _():
            for copy in self.end_sends():
                copy.wait_send()

        @pl.when(self.is_mid)
        def _():
            for copy in (*self.mid_sends(), self.passed_on()):
                copy.wait_send()


class PlaneSum:
    def __init__(self, place, src, box, send, recv):
        self.p, self.src, self.box = place, src, box
        self.copies = []
        for step in range(1, PLANE):
            to = place.plane_peer(step)
            copy = push(src.at[to], box.at[step], send.at[step], recv.at[step], {"seq": to})
            copy.start()
            self.copies.append(copy)

    def total(self):
        value = self.src[self.p.me].astype(f32)
        for step, copy in enumerate(self.copies):
            copy.wait_recv()
            value = value + self.box[step + 1].astype(f32)
        return value

    def finish(self):
        for copy in self.copies:
            copy.wait_send()


class Spread:
    def __init__(self, place, src, out, send, recv, local, room=None):
        cols = src.shape[2]
        spot = out.at[:, rows_at(place.me * cols, cols)]
        if room is None:
            self.copies = [load(src.at[place.me], spot, local)]
        else:
            self.copies = [Through(src.at[place.me], room, spot, local)]
        for step in range(1, PLANE):
            to = place.plane_peer(step)
            copy = push(src.at[to], spot, send.at[step], recv.at[step], {"seq": to})
            copy.start()
            self.copies.append(copy)

    def finish(self):
        for copy in self.copies:
            copy.wait()


def fold(ref, first, value):
    rows, wide = value.shape
    total = jnp.sum(value.reshape(rows // 8, 8, wide), axis=0)

    @pl.when(first)
    def _():
        ref[...] = total

    @pl.when(jnp.logical_not(first))
    def _():
        ref[...] += total


def params(number, vmem=True):
    return pltpu.CompilerParams(
        collective_id=number,
        has_side_effects=True,
        vmem_limit_bytes=VMEM_LIMIT if vmem else None,
    )


def cost(flops, mib=40):
    return pl.CostEstimate(flops=flops, bytes_accessed=mib * 1024 * 1024, transcendentals=0)


def load(src, dst, sem):
    copy = pltpu.make_async_copy(src, dst, sem)
    copy.start()
    return copy


class Through:
    def __init__(self, src, room, dst, sem):
        self.room, self.dst, self.sem = room, dst, sem
        self.copy = load(src, room, sem)

    def put(self):
        self.copy.wait()
        self.copy = load(self.room, self.dst, self.sem)

    def wait(self):
        self.copy.wait()


def split_weights(tokens, gain, shift, w_query, w_fc, w_kv, w_out, layers, number):
    arrays, lined = (w_query, w_fc), (w_kv, w_out)
    own_rows, width = tokens.shape

    def kernel(tok_ref, gain_ref, shift_ref, wq_ref, wf_ref, kv_ref, wo_ref, *refs):
        wq_out, wf_out, kv_out, wo_out, hidden, mean_out, inverse_out = refs[:7]
        send, recv, kv_send, kv_recv, wo_send, wo_recv, local = refs[7:14]
        rooms = refs[14:]
        p = Place()
        ins, outs = (wq_ref, wf_ref), (wq_out, wf_out)
        lines = (
            LineGather(p, kv_ref, kv_out, layers, kv_send, kv_recv),
            LineGather(p, wo_ref, wo_out, layers, wo_send, wo_recv),
        )

        def block(i, dev):
            cols = ins[i].shape[1] // PLANE
            return ins[i].at[:, rows_at(dev * cols, cols)]

        own = []
        for i in range(2):
            own.append(Through(block(i, p.me), rooms[i], outs[i].at[p.me], local.at[i]))
            own.append(Through(lines[i].src, rooms[2 + i], lines[i].block(p.layer), local.at[2 + i]))
        p.greet(True, layers)
        for line in lines:
            line.start()
        copies = []
        for i in (1, 0):
            for step in range(1, PLANE):
                to = p.plane_peer(step)
                copies.append(
                    push(
                        block(i, to),
                        outs[i].at[p.me],
                        send.at[i, step],
                        recv.at[i, step],
                        {"seq": to},
                    )
                )
                copies[-1].start()

        for copy in own:
            copy.put()

        @pl.loop(0, own_rows // 32)
        def _(i):
            here = rows_at(i * 32, 32)
            values = tok_ref[here, :].astype(f32)
            mean, inverse = norm_stats(values)
            hidden[here, :] = (
                (values - mean) * inverse * gain_ref[...] + shift_ref[...]
            ).astype(bf16)
            mean_out[here, :] = mean
            inverse_out[here, :] = inverse

        for line in lines:
            line.relay()
        for copy in own + copies:
            copy.wait()
        for line in lines:
            line.finish()

    return pl.pallas_call(
        kernel,
        out_shape=[
            jax.ShapeDtypeStruct((PLANE, a.shape[0], a.shape[1] // PLANE), a.dtype)
            for a in arrays
        ]
        + [jax.ShapeDtypeStruct((layers * a.shape[0], a.shape[1]), a.dtype) for a in lined]
        + [jax.ShapeDtypeStruct((own_rows, width), bf16)]
        + [jax.ShapeDtypeStruct((own_rows, 1), f32)] * 2,
        in_specs=[WHOLE] * 3 + [ANY] * 4,
        out_specs=[ANY] * 4 + [WHOLE] * 3,
        scratch_shapes=[sems(2, PLANE), sems(2, PLANE)]
        + LineGather.scratch(layers) * 2
        + [sems(4)]
        + [pltpu.VMEM((a.shape[0], a.shape[1] // PLANE), bf16) for a in arrays]
        + [pltpu.VMEM(a.shape, bf16) for a in lined],
        compiler_params=params(number),
        name="split_weights",
    )(tokens, gain, shift, w_query, w_fc, w_kv, w_out)


def gather_hidden1(hidden1, low_kv, wq_pieces, layers, number):
    def kernel(h_ref, kv_ref, wq_ref, h_all, kv_all, wq_all, *refs):
        hs, hr, ks, kr, zsend, zrecv, local, h_room, kv_room, wq_room = refs
        p = Place()
        h_rows, kv_rows = h_ref.shape[0], kv_ref.shape[0]
        wq_mine = wq_all.at[:, p.layer]
        own = [
            Through(h_ref, h_room, h_all.at[rows_at(p.me * h_rows, h_rows), :], local.at[0]),
            Through(kv_ref, kv_room, kv_all.at[rows_at(p.me * kv_rows, kv_rows), :], local.at[1]),
            Through(wq_ref, wq_room, wq_mine, local.at[2]),
        ]
        p.greet(False, layers)
        kv = Gather(p, kv_all, kv_rows, ks, kr)
        h = Gather(p, h_all, h_rows, hs, hr)
        kv.start(kv_ref)
        h.start(h_ref)
        across = []
        for step in range(1, layers):
            to = p.line_peer(step, layers)
            across.append(push(wq_ref, wq_mine, zsend.at[step], zrecv.at[step], {"fsdp": to}))
            across[-1].start()
        for copy in own:
            copy.put()
        kv.relay()
        kv.relay_corner()
        h.relay()
        h.relay_corner()
        for g in (kv, h):
            for dev in (p.sib, p.xs, p.ys, p.ds):
                g.have(dev)
            g.finish()
        for copy in own + across:
            copy.wait()

    groups, piece_rows, cols = wq_pieces.shape
    return pl.pallas_call(
        kernel,
        out_shape=[
            jax.ShapeDtypeStruct((PLANE * hidden1.shape[0], hidden1.shape[1]), bf16),
            jax.ShapeDtypeStruct((PLANE * low_kv.shape[0], low_kv.shape[1]), bf16),
            jax.ShapeDtypeStruct((groups, layers, piece_rows, cols), bf16),
        ],
        in_specs=[ANY] * 3,
        out_specs=[ANY] * 3,
        scratch_shapes=Gather.scratch * 2
        + [sems(layers), sems(layers), sems(3)]
        + [pltpu.VMEM(a.shape, bf16) for a in (hidden1, low_kv, wq_pieces)],
        compiler_params=params(number),
        name="gather_hidden1",
    )(hidden1, low_kv, wq_pieces)


def project_attend(docs, hidden1, wq, w_kv, bq, bkv, cot, streams, heads, number):
    total, depth = hidden1.shape
    cols, kv_cols = wq.shape[1], w_kv.shape[1]
    rows = total // PLANE // streams
    length = PLANE * rows
    block = min(QROWS, length)
    chunk = total // 4

    def kernel(docs_ref, h_ref, wq_ref, wkv_ref, bq_ref, bkv_ref, cot_ref, *refs):
        cot_all, q_out, kv_out, mixed_out, lse_ref = refs[:5]
        h_buf, wq_buf, wkv_buf, q_buf, kv_buf, mixed_buf, room, send, recv, local = refs[5:]
        p = Place()
        own_rows = cot_ref.shape[0]

        def fetch(k):
            return load(
                h_ref.at[pl.ds(k * chunk, chunk), :], h_buf.at[k % 2], local.at[k % 2]
            )

        fetches = [fetch(0)]
        weights = [load(wq_ref, wq_buf, local.at[2]), load(wkv_ref, wkv_buf, local.at[3])]
        own = Through(
            cot_ref, room, cot_all.at[rows_at(p.me * own_rows, own_rows), :], local.at[4]
        )
        p.greet()
        g = Gather(p, cot_all, own_rows, send, recv)
        g.start(cot_ref)
        own.put()
        for copy in weights:
            copy.wait()
        per = chunk // (streams * rows)
        for k in range(4):
            fetches[k].wait()
            if k < 3:
                fetches.append(fetch(k + 1))
            where = pl.ds(k * per, per)
            q = dot(h_buf[k % 2], wq_buf[...]) + bq_ref[...]
            q_buf[where] = q.astype(bf16).reshape(per, streams, rows, cols)
            kv = dot(h_buf[k % 2], wkv_buf[...]) + bkv_ref[...]
            kv_buf[where] = kv.astype(bf16).reshape(per, streams, rows, kv_cols)
        stores = [load(q_buf, q_out, local.at[5]), load(kv_buf, kv_out, local.at[6])]
        g.relay_first()
        for stream in range(streams):
            attend_stream(
                docs_ref,
                stream,
                q_buf.at[:, stream],
                kv_buf.at[:, stream],
                mixed_buf.at[:, stream],
                lse_ref.at[stream],
                block,
                heads,
            )
        stores.append(load(mixed_buf, mixed_out, local.at[7]))
        g.relay_rest()
        g.relay_corner()
        for dev in (p.sib, p.xs, p.ys, p.ds):
            g.have(dev)
        g.finish()
        own.wait()
        for copy in stores:
            copy.wait()

    q_shape = (PLANE, streams, rows, cols)
    kv_shape = (PLANE, streams, rows, kv_cols)
    return pl.pallas_call(
        kernel,
        out_shape=[
            jax.ShapeDtypeStruct((PLANE * cot.shape[0], cot.shape[1]), bf16),
            jax.ShapeDtypeStruct(q_shape, bf16),
            jax.ShapeDtypeStruct(kv_shape, bf16),
            jax.ShapeDtypeStruct(q_shape, bf16),
            jax.ShapeDtypeStruct((streams, heads, length), f32),
        ],
        in_specs=[pl.BlockSpec(memory_space=pltpu.SMEM)] + [ANY] * 3 + [WHOLE] * 2 + [ANY],
        out_specs=[ANY] * 4 + [WHOLE],
        scratch_shapes=[
            pltpu.VMEM((2, chunk, depth), bf16),
            pltpu.VMEM(wq.shape, bf16),
            pltpu.VMEM(w_kv.shape, bf16),
            pltpu.VMEM(q_shape, bf16),
            pltpu.VMEM(kv_shape, bf16),
            pltpu.VMEM(q_shape, bf16),
            pltpu.VMEM(cot.shape, bf16),
        ]
        + Gather.scratch
        + [sems(8)],
        compiler_params=params(number),
        cost_estimate=cost(2 * total * depth * (cols + kv_cols)),
        name="project_attend",
    )(docs, hidden1, wq, w_kv, bq, bkv, cot)


def gather_fc(hidden2, wf, bf, cot_all, number):
    rows, depth = hidden2.shape
    wide = wf.shape[1]
    total = PLANE * rows
    out_wide = cot_all.shape[1]
    tile = 256

    def kernel(own_ref, w_ref, b_ref, cot_ref, all_ref, act_ref, slope_ref, dw_ref, *refs):
        buf, w_buf, act, slope, cot, acc, dw, send, recv, local = refs
        p = Place()
        load_own = load(own_ref, buf.at[rows_at(p.me * rows, rows), :], local.at[0])
        load_w = load(w_ref, w_buf, local.at[1])
        p.greet()
        g = Gather(p, buf, rows, send, recv)
        g.start(own_ref)
        stores = []
        cots = {}

        def fetch(k, dev):
            cots[k] = load(cot_ref.at[g.pair(dev), :], cot.at[k % 2], local.at[2 + k % 2])

        def work(k, dev):
            block = g.pair(dev)
            stores.append(load(buf.at[block, :], all_ref.at[block, :], local.at[4 + 3 * k]))

            @pl.loop(0, wide // 512)
            def _(j):
                cols = rows_at(j * 512, 512)
                acc_fc = dot(buf[block, :], w_buf[:, cols]) + b_ref[:, cols]
                activated, gradient = gelu_pair(acc_fc)
                act[block, cols] = activated.astype(bf16)
                slope[block, cols] = gradient.astype(bf16)

            for i, (src, dst) in enumerate(((act, act_ref), (slope, slope_ref))):
                stores.append(
                    load(src.at[block, :], dst.at[block, :], local.at[4 + 3 * k + 1 + i])
                )

        def grads(k, dev):
            block = g.pair(dev)
            cots[k].wait()

            for j in range(wide // tile):
                cols = pl.ds(j * tile, tile)
                term = dot_tn(act[block, cols], cot[k % 2])
                if k == 0:
                    acc[cols, :] = term
                elif k < 3:
                    acc[cols, :] += term
                else:
                    dw[cols, :] = (acc[cols, :] + term).astype(bf16)
                    stores.append(load(dw.at[cols, :], dw_ref.at[cols, :], local.at[16 + j]))

        fetch(0, p.me)
        fetch(1, p.xn)
        load_own.wait()
        load_w.wait()
        g.have(p.sib)
        work(0, p.me)
        g.relay_first()
        grads(0, p.me)
        fetch(2, p.yn)
        g.relay_rest()
        g.have(p.xs)
        work(1, p.xn)
        g.have(p.ys)
        work(2, p.yn)
        grads(1, p.xn)
        fetch(3, p.dg)
        g.relay_corner()
        grads(2, p.yn)
        g.have(p.ds)
        work(3, p.dg)
        grads(3, p.dg)
        g.finish()
        for copy in stores:
            copy.wait()

    return pl.pallas_call(
        kernel,
        out_shape=[
            jax.ShapeDtypeStruct((total, depth), bf16),
            jax.ShapeDtypeStruct((total, wide), bf16),
            jax.ShapeDtypeStruct((total, wide), bf16),
            jax.ShapeDtypeStruct((wide, out_wide), bf16),
        ],
        in_specs=[ANY, ANY, WHOLE, ANY],
        out_specs=[ANY] * 4,
        scratch_shapes=[
            pltpu.VMEM((total, depth), bf16),
            pltpu.VMEM(wf.shape, bf16),
            pltpu.VMEM((total, wide), bf16),
            pltpu.VMEM((total, wide), bf16),
            pltpu.VMEM((2, 2 * rows, out_wide), bf16),
            pltpu.VMEM((wide, out_wide), f32),
            pltpu.VMEM((wide, out_wide), bf16),
        ]
        + Gather.scratch
        + [sems(16 + wide // tile)],
        compiler_params=params(number),
        cost_estimate=cost(4 * total * depth * wide),
        name="gather_fc",
    )(hidden2, wf, bf, cot_all)


def gather_out(grad_attn, wo, mixed, number):
    rows, depth = grad_attn.shape
    wide = wo.shape[0]
    total = PLANE * rows

    def kernel(own_ref, w_ref, mixed_ref, gm_ref, dw_ref, *refs):
        buf, w_buf, mixed_buf, gm, acc, dw, send, recv, local = refs
        p = Place()
        load_own = load(own_ref, buf.at[rows_at(p.me * rows, rows), :], local.at[0])
        loads = [load(w_ref, w_buf, local.at[1]), load(mixed_ref, mixed_buf, local.at[2])]
        p.greet()
        g = Gather(p, buf, rows, send, recv)
        g.start(own_ref)

        def work(dev):
            block = g.pair(dev)
            gm[block, :] = dot_nt(buf[block, :], w_buf[...]).astype(bf16)

        def grads(k, dev):
            block = g.pair(dev)
            term = dot_tn(mixed_buf[block, :], buf[block, :])
            if k == 0:
                acc[...] = term
            elif k < 3:
                acc[...] += term
            else:
                dw[...] = (acc[...] + term).astype(bf16)

        load_own.wait()
        for copy in loads:
            copy.wait()
        g.have(p.sib)
        work(p.me)
        grads(0, p.me)
        g.relay()
        g.have(p.xs)
        work(p.xn)
        g.have(p.ys)
        work(p.yn)
        grads(1, p.xn)
        g.relay_corner()
        grads(2, p.yn)
        g.have(p.ds)
        work(p.dg)
        store = load(gm, gm_ref, local.at[3])
        grads(3, p.dg)
        store_dw = load(dw, dw_ref, local.at[4])
        g.finish()
        store.wait()
        store_dw.wait()

    return pl.pallas_call(
        kernel,
        out_shape=[
            jax.ShapeDtypeStruct((total, wide), bf16),
            jax.ShapeDtypeStruct((wide, depth), bf16),
        ],
        in_specs=[ANY] * 3,
        out_specs=[ANY] * 2,
        scratch_shapes=[
            pltpu.VMEM((total, depth), bf16),
            pltpu.VMEM(wo.shape, bf16),
            pltpu.VMEM(mixed.shape, bf16),
            pltpu.VMEM((total, wide), bf16),
            pltpu.VMEM((wide, depth), f32),
            pltpu.VMEM((wide, depth), bf16),
        ]
        + Gather.scratch
        + [sems(5)],
        compiler_params=params(number),
        cost_estimate=cost(4 * total * depth * wide),
        name="gather_out",
    )(grad_attn, wo, mixed)


def scatter_attn(mixed, wo, tokens, b_out, gain, shift, number):
    total, depth = mixed.shape
    rows = total // PLANE
    wide = wo.shape[1]

    def kernel(a_ref, w_ref, tok_ref, bias_ref, gain_ref, shift_ref, *refs):
        residual, hidden, mean_out, inverse_out = refs[:4]
        a_buf, w_buf = refs[4:6]
        s, local = refs[6:20], refs[20]
        p = Place()
        loads = [load(a_ref, a_buf, local.at[0]), load(w_ref, w_buf, local.at[1])]
        p.greet()
        for copy in loads:
            copy.wait()

        def emit(line, value):
            values = tok_ref[line, :].astype(f32) + value + bias_ref[...]
            mean, inverse = norm_stats(values)
            residual[line, :] = values
            hidden[line, :] = (
                (values - mean) * inverse * gain_ref[...] + shift_ref[...]
            ).astype(bf16)
            mean_out[line, :] = mean
            inverse_out[line, :] = inverse

        Scatter.take(p, rows, s).run(plain_product(a_buf, w_buf), emit)

    return pl.pallas_call(
        kernel,
        out_shape=[
            jax.ShapeDtypeStruct((rows, wide), f32),
            jax.ShapeDtypeStruct((rows, wide), bf16),
            jax.ShapeDtypeStruct((rows, 1), f32),
            jax.ShapeDtypeStruct((rows, 1), f32),
        ],
        in_specs=[ANY] * 2 + [WHOLE] * 4,
        out_specs=[WHOLE] * 4,
        scratch_shapes=[pltpu.VMEM(mixed.shape, bf16), pltpu.VMEM(wo.shape, bf16)]
        + Scatter.scratch(rows, wide)
        + [sems(2)],
        compiler_params=params(number),
        cost_estimate=cost(2 * total * depth * wide),
        name="scatter_attn",
    )(mixed, wo, tokens, b_out, gain, shift)


def plain_product(a_buf, w_buf):
    half = w_buf.shape[1] // 2

    def product(role, here, c):
        return dot(a_buf[here, :], w_buf[:, pl.ds(c * half, half)])

    return product


def scatter_fc(cot_all, slope, wp, wf, hidden2, cot, residual, mean, inverse, gain, number):
    total, depth = cot_all.shape
    rows = total // PLANE
    wide = wp.shape[0]
    tile = 256

    def kernel(cot_ref, slope_ref, wp_ref, wf_ref, h_ref, *refs):
        cot_own, residual_ref, mean_ref, inverse_ref, gain_ref = refs[:5]
        grad_residual, grad_attn, sums_ref, bias_ref, dw_ref = refs[5:10]
        cot, slopes, wp_buf, wf_buf, gp, h_buf, dw_buf, folds = refs[10:18]
        s = refs[18:32]
        (local,) = refs[32:]
        p = Place()
        order = (p.dg, p.xn, p.yn, p.me)

        def chip(dev):
            return rows_at(lax.div(dev, 2) * (2 * rows), 2 * rows)

        def fetch(k):
            here = chip(order[k])
            return (
                load(cot_ref.at[here, :], cot.at[k % 2], local.at[k % 2]),
                load(slope_ref.at[here, :], slopes.at[k % 2], local.at[2 + k % 2]),
            )

        fetches = [fetch(0)]
        load_wp = load(wp_ref, wp_buf, local.at[4])
        load_wf = load(wf_ref, wf_buf, local.at[5])
        bias_ref[...] = jnp.zeros_like(bias_ref)
        p.greet()
        load_wp.wait()
        half = depth // 2

        def back_through_gelu(k):
            for copy in fetches[k]:
                copy.wait()
            if k < 3:
                fetches.append(fetch(k + 1))
            here = chip(order[k])

            @pl.loop(0, wide // 512)
            def _(j):
                cols = rows_at(j * 512, 512)
                grad_act = dot_nt(cot[k % 2], wp_buf[cols, :])
                grad_pre = (grad_act * slopes[k % 2, :, cols].astype(f32)).astype(bf16)
                gp[here, cols] = grad_pre
                bias_ref[:, cols] += jnp.sum(grad_pre.astype(f32), axis=0, keepdims=True)

            if k == 0:
                load_wf.wait()

        def product(role, here, c):
            if c == 0:
                back_through_gelu(role)
            return dot_nt(gp[here, :], wf_buf[pl.ds(c * half, half), :])

        def emit(line, value):
            first = line.start == 0
            grad_out = cot_own[line, :].astype(f32)
            back = inverse_ref[line, :]
            normed = (residual_ref[line, :] - mean_ref[line, :]) * back
            result = grad_out + norm_back(value, normed, back, gain_ref[...])
            low = result.astype(bf16)
            grad_residual[line, :] = result
            grad_attn[line, :] = low
            for i, term in enumerate((value * normed, value, low.astype(f32), grad_out)):
                fold(folds.at[i], first, term)

        steps = depth // tile

        def h_fetch(i):
            return load(
                h_ref.at[:, pl.ds(i * tile, tile)], h_buf.at[i % 2], local.at[6 + i % 2]
            )

        def idle():
            tiles = [h_fetch(0)]
            stores = []
            for i in range(steps):
                tiles[i].wait()
                if i + 1 < steps:
                    tiles.append(h_fetch(i + 1))
                if i >= 2:
                    stores[i - 2].wait()
                dw_buf[i % 2] = dot_tn(h_buf[i % 2], gp[...]).astype(bf16)
                stores.append(
                    load(
                        dw_buf.at[i % 2],
                        dw_ref.at[pl.ds(i * tile, tile), :],
                        local.at[8 + i % 2],
                    )
                )
            for copy in stores[-2:]:
                copy.wait()

        Scatter.take(p, rows, s).run(product, emit, idle)
        sums_ref[...] = jnp.sum(folds[...], axis=1)

    return pl.pallas_call(
        kernel,
        out_shape=[
            jax.ShapeDtypeStruct((rows, depth), f32),
            jax.ShapeDtypeStruct((rows, depth), bf16),
            jax.ShapeDtypeStruct((4, depth), f32),
            jax.ShapeDtypeStruct((1, wide), f32),
            jax.ShapeDtypeStruct((depth, wide), bf16),
        ],
        in_specs=[ANY] * 5 + [WHOLE] * 5,
        out_specs=[WHOLE] * 4 + [ANY],
        scratch_shapes=[
            pltpu.VMEM((2, 2 * rows, depth), bf16),
            pltpu.VMEM((2, 2 * rows, wide), bf16),
            pltpu.VMEM(wp.shape, bf16),
            pltpu.VMEM(wf.shape, bf16),
            pltpu.VMEM((total, wide), bf16),
            pltpu.VMEM((2, total, tile), bf16),
            pltpu.VMEM((2, tile, wide), bf16),
            pltpu.VMEM((4, 8, depth), f32),
        ]
        + Scatter.scratch(rows, depth)
        + [sems(10)],
        compiler_params=params(number),
        cost_estimate=cost(6 * total * depth * wide),
        name="scatter_fc",
    )(cot_all, slope, wp, wf, hidden2, cot, residual, mean, inverse, gain)


def scatter_query(
    gq, gkv, wq, w_kv, grad_w_out, grad_w_query, grad_w_kv, back, layers, number
):
    total, cols = gq.shape
    kv_cols = gkv.shape[1]
    rows = total // PLANE
    depth = wq.shape[0]
    out_rows, out_wide = grad_w_out.shape[0] // layers, grad_w_out.shape[1]
    q_rows, q_cols = grad_w_query.shape[2:]
    kv_part = grad_w_kv.shape[1]
    kv_rows = kv_part // layers

    def kernel(gq_ref, gkv_ref, wq_ref, wkv_ref, dwo_ref, dwq_ref, dwkv_ref, *refs):
        tok_ref, mean_ref, inverse_ref, gain_ref, residual_ref = refs[:5]
        out_ref, sums_ref, dwo_out, dwq_out, dwkv_out = refs[5:10]
        g_buf, wq_buf, wkv_buf, folds = refs[10:14]
        dwo_own, dwo_box, q_own, q_box, q_sum, kv_box, kv_sum, kvz_box = refs[14:22]
        q_pass, o_pass = refs[22:24]
        s = refs[24:38]
        (osend, orecv, qzsend, qzrecv, qsend, qrecv, ksend, krecv, kzsend, kzrecv, local) = refs[
            38:
        ]
        p = Place()
        q_side, kv_side = pl.ds(0, cols), pl.ds(cols, kv_cols)
        loads = [
            load(gq_ref, g_buf.at[:, q_side], local.at[0]),
            load(gkv_ref, g_buf.at[:, kv_side], local.at[1]),
            load(wq_ref, wq_buf, local.at[2]),
            load(wkv_ref, wkv_buf, local.at[3]),
        ]

        def dwo_block(layer):
            return dwo_ref.at[rows_at(layer * out_rows, out_rows), :]

        def dwq_block(layer):
            return dwq_ref.at[:, layer]

        own = [
            load(dwo_block(p.layer), dwo_own, local.at[4]),
            load(dwq_block(p.layer), q_own, local.at[5]),
        ]
        p.greet(True, layers)
        plane_kv = PlaneSum(p, dwkv_ref, kv_box, ksend, krecv)
        line_q = LineSum(p, dwq_block, q_box, layers, qzsend, qzrecv, q_pass, local.at[7])
        line_o = LineSum(p, dwo_block, dwo_box, layers, osend, orecv, o_pass, local.at[8])
        for copy in loads:
            copy.wait()
        half = depth // 2

        def product(role, here, c):
            where = pl.ds(c * half, half)
            return dot_nt(g_buf[here, q_side], wq_buf[where, :]) + dot_nt(
                g_buf[here, kv_side], wkv_buf[where, :]
            )

        later = []

        def early():
            line_q.relay()
            line_o.relay()

        def idle():
            for copy in own:
                copy.wait()
            kv_sum[...] = plane_kv.total().astype(bf16).reshape(layers, kv_rows, kv_cols)
            line_kv = LineSum(
                p, lambda layer: kv_sum.at[layer], kvz_box, layers, kzsend, kzrecv
            )
            line_q.arrived()

            @pl.loop(0, PLANE)
            def _(i):
                q_sum[i] = line_q.total(q_own[i], (i,)).astype(bf16)

            later.append(Spread(p, q_sum, dwq_out, qsend, qrecv, local.at[6]))
            line_kv.arrived()
            dwkv_out[...] = line_kv.total(kv_sum[p.layer], ())
            later.append(line_kv)
            line_o.arrived()

            @pl.loop(0, out_rows // 16)
            def _(i):
                lines = rows_at(i * 16, 16)
                dwo_out[lines, :] = line_o.total(dwo_own[lines, :], (lines, slice(None)))

        def emit(line, value):
            first = line.start == 0
            normed = (tok_ref[line, :].astype(f32) - mean_ref[line, :]) * inverse_ref[line, :]
            out_ref[line, :] = residual_ref[line, :] + norm_back(
                value, normed, inverse_ref[line, :], gain_ref[...]
            )
            fold(folds.at[0], first, value * normed)
            fold(folds.at[1], first, value)

        Scatter.take(p, rows, s).run(product, emit, idle, early)
        sums_ref[...] = jnp.sum(folds[...], axis=1)
        plane_kv.finish()
        line_q.finish()
        line_o.finish()
        for item in later:
            item.finish()

    return pl.pallas_call(
        kernel,
        out_shape=[
            jax.ShapeDtypeStruct((rows, depth), f32),
            jax.ShapeDtypeStruct((2, depth), f32),
            jax.ShapeDtypeStruct((out_rows, out_wide), f32),
            jax.ShapeDtypeStruct((q_rows, PLANE * q_cols), bf16),
            jax.ShapeDtypeStruct((kv_rows, kv_cols), f32),
        ],
        in_specs=[ANY] * 6 + [WHOLE] * 6,
        out_specs=[WHOLE] * 3 + [ANY, WHOLE],
        scratch_shapes=[
            pltpu.VMEM((total, cols + kv_cols), bf16),
            pltpu.VMEM(wq.shape, bf16),
            pltpu.VMEM(w_kv.shape, bf16),
            pltpu.VMEM((2, 8, depth), f32),
            pltpu.VMEM((out_rows, out_wide), bf16),
            pltpu.VMEM((layers - 1, out_rows, out_wide), bf16),
            pltpu.VMEM((PLANE, q_rows, q_cols), bf16),
            pltpu.VMEM((layers - 1, PLANE, q_rows, q_cols), bf16),
            pltpu.VMEM((PLANE, q_rows, q_cols), bf16),
            pltpu.VMEM((PLANE, kv_part, kv_cols), bf16),
            pltpu.VMEM((layers, kv_rows, kv_cols), bf16),
            pltpu.VMEM((layers - 1, kv_rows, kv_cols), bf16),
            pltpu.VMEM((2, PLANE, q_rows, q_cols), bf16),
            pltpu.VMEM((2, out_rows, out_wide), bf16),
        ]
        + Scatter.scratch(rows, depth)
        + [sems(layers)] * 4
        + [sems(PLANE)] * 4
        + [sems(layers)] * 2
        + [sems(9)],
        compiler_params=params(number),
        cost_estimate=cost(2 * total * depth * (cols + kv_cols)),
        name="scatter_query",
    )(gq, gkv, wq, w_kv, grad_w_out, grad_w_query, grad_w_kv, *back)


def last_exchange(vector, fc_pieces, layers, number):
    lines = vector.shape[1]

    def kernel(vec, fc_ref, vec_out, fc_out, *refs):
        box, plane_sum, zbox, room = refs[:4]
        vsend, vrecv, zsend, zrecv, gsend, grecv, send, recv, local = refs[4:]
        p = Place()
        p.greet(True, layers)
        plane = PlaneSum(p, vec, box, vsend, vrecv)
        spread = Spread(p, fc_ref, fc_out, send, recv, local.at[0], room)
        spread.copies[0].put()
        total = plane.total()
        plane_sum[...] = total
        zbox[0] = total
        across = []
        for step in range(1, layers):
            to = p.line_peer(step, layers)
            copy = push(plane_sum, zbox.at[step], zsend.at[step], zrecv.at[step], {"fsdp": to})
            copy.start()
            across.append(copy)
        for copy in across:
            copy.wait_recv()
        total = None
        for k in range(layers):
            term = zbox[lax.rem(p.layer - k + layers, layers)]
            total = term if total is None else total + term
        vec_out[p.me] = total
        last = []
        for step in range(1, PLANE):
            to = p.plane_peer(step)
            mine = vec_out.at[p.me]
            last.append(push(mine, mine, gsend.at[step], grecv.at[step], {"seq": to}))
            last[-1].start()
        for copy in last:
            copy.wait()
        spread.finish()
        plane.finish()
        for copy in across:
            copy.wait_send()

    return pl.pallas_call(
        kernel,
        out_shape=[
            jax.ShapeDtypeStruct(vector.shape, f32),
            jax.ShapeDtypeStruct((fc_pieces.shape[1], PLANE * fc_pieces.shape[2]), bf16),
        ],
        in_specs=[WHOLE, ANY],
        out_specs=[WHOLE, ANY],
        scratch_shapes=[
            pltpu.VMEM((PLANE, lines, 128), f32),
            pltpu.VMEM((lines, 128), f32),
            pltpu.VMEM((layers, lines, 128), f32),
            pltpu.VMEM(fc_pieces.shape[1:], bf16),
        ]
        + [sems(PLANE)] * 2
        + [sems(layers)] * 2
        + [sems(PLANE)] * 4
        + [sems(1)],
        compiler_params=params(number, False),
        name="last_exchange",
    )(vector, fc_pieces)


def starts_of(docs, stream, positions):
    start = jnp.zeros_like(positions)
    for j in range(docs.shape[1]):
        here = docs[stream, j]
        start = jnp.maximum(start, jnp.where(here <= positions, here, 0))
    return start


def masked_scores(docs, stream, keys, q, first, limit):
    scores = dot_nt(keys, q) * (HD**-0.5)
    t = first + lax.broadcasted_iota(jnp.int32, (1, q.shape[0]), 1)
    u = lax.broadcasted_iota(jnp.int32, scores.shape, 0)
    return scores, (u >= starts_of(docs, stream, t)) & (u <= t)


QROWS = 256


def attend_stream(docs, stream, q_ref, kv_ref, mixed_ref, lse_ref, block, heads):
    groups, rows, cols = q_ref.shape
    length = groups * rows
    kv = kv_ref[...].reshape(length, 2 * HD)
    keys = kv[:, :HD]
    values_t = kv[:, HD:].T
    per = block // rows
    for b in range(length // block):
        limit = (b + 1) * block
        q_rows = q_ref[b * per : (b + 1) * per].reshape(block, cols)
        for h in range(heads):
            q = q_rows[:, h * HD : (h + 1) * HD]
            scores, allowed = masked_scores(docs, stream, keys[:limit], q, b * block, limit)
            scores = jnp.where(allowed, scores, -1e30)
            top = jnp.max(scores, axis=0, keepdims=True)
            weights = jnp.exp(scores - top)
            total = jnp.sum(weights, axis=0, keepdims=True)
            mixed = dot(values_t[:, :limit], weights.astype(bf16)) / total
            mixed_ref[b * per : (b + 1) * per, :, h * HD : (h + 1) * HD] = (
                mixed.T.astype(bf16).reshape(per, rows, HD)
            )
            lse_ref[h : h + 1, b * block : (b + 1) * block] = top + jnp.log(total)


def attend_stream_back(docs, stream, q_ref, kv_ref, g_ref, lse_ref, gq_ref, gkv_ref, gk, gv, heads):
    groups, rows, cols = q_ref.shape
    length = groups * rows
    block = min(QROWS, length)
    kv = kv_ref[...].reshape(length, 2 * HD)
    keys, values = kv[:, :HD], kv[:, HD:]
    keys_t = keys.T
    per = block // rows
    gk[...] = jnp.zeros_like(gk)
    gv[...] = jnp.zeros_like(gv)
    for b in range(length // block):
        limit = (b + 1) * block
        q_rows = q_ref[b * per : (b + 1) * per].reshape(block, cols)
        g_rows = g_ref[b * per : (b + 1) * per].reshape(block, cols)
        for h in range(heads):
            q = q_rows[:, h * HD : (h + 1) * HD]
            g = g_rows[:, h * HD : (h + 1) * HD]
            scores, allowed = masked_scores(docs, stream, keys[:limit], q, b * block, limit)
            shift = lse_ref[h : h + 1, b * block : (b + 1) * block]
            probs = jnp.where(allowed, jnp.exp(scores - shift), 0.0)
            grad_probs = dot_nt(values[:limit], g)
            weighted = probs * grad_probs
            delta = jnp.sum(weighted, axis=0, keepdims=True)
            grad_scores = (weighted - probs * delta).astype(bf16)
            gq = dot(keys_t[:, :limit], grad_scores) * (HD**-0.5)
            gq_ref[b * per : (b + 1) * per, :, h * HD : (h + 1) * HD] = (
                gq.T.astype(bf16).reshape(per, rows, HD)
            )
            gk[:limit, :] += dot(grad_scores, q)
            gv[:limit, :] += dot(probs.astype(bf16), g)
    gkv_ref[:, :, :HD] = (gk[...] * (HD**-0.5)).astype(bf16).reshape(groups, rows, HD)
    gkv_ref[:, :, HD:] = gv[...].astype(bf16).reshape(groups, rows, HD)


def attend_back_scatter_proj(
    docs, queries, keyval, grads, lse, act, wp, hidden1, residual, b_proj, layers, heads, number
):
    groups, streams, rows, cols = queries.shape
    kv_cols = keyval.shape[3]
    length = groups * rows
    total, depth = act.shape
    own = total // PLANE
    wide = wp.shape[1]
    part = hidden1.shape[1] // PLANE

    def kernel(docs_ref, q_ref, kv_ref, g_ref, lse_ref, act_ref, wp_ref, h_ref, *refs):
        residual_ref, bias_ref = refs[:2]
        gq_out, gkv_out, gq_sum, gkv_sum, dwq_out, dwkv_out, out_ref = refs[2:9]
        a_buf, w_buf, q_buf, kv_buf, g_buf, grad_buf, gk, gv, h_buf = refs[9:18]
        dwq_buf, dwkv_buf = refs[18:20]
        s, local = refs[20:34], refs[34]
        p = Place()
        loads = [load(act_ref, a_buf, local.at[0]), load(wp_ref, w_buf, local.at[1])]
        ins = [
            load(q_ref, q_buf, local.at[2]),
            load(kv_ref, kv_buf, local.at[3]),
            load(g_ref, g_buf, local.at[4]),
        ]

        def h_fetch(i):
            here = pl.ds(2 * i * part, 2 * part)
            return load(h_ref.at[:, here], h_buf.at[i % 2], local.at[5 + i % 2])

        tiles = [h_fetch(0)]
        p.greet()
        for copy in loads:
            copy.wait()
        stores = []

        def idle():
            for copy in ins:
                copy.wait()
            for stream in range(streams):
                attend_stream_back(
                    docs_ref,
                    stream,
                    q_buf.at[:, stream],
                    kv_buf.at[:, stream],
                    g_buf.at[:, stream],
                    lse_ref.at[stream],
                    grad_buf.at[:, stream, :, pl.ds(0, cols)],
                    grad_buf.at[:, stream, :, pl.ds(cols, kv_cols)],
                    gk,
                    gv,
                    heads,
                )
            stores.append(load(grad_buf.at[:, :, :, pl.ds(0, cols)], gq_out, local.at[7]))
            stores.append(load(grad_buf.at[:, :, :, pl.ds(cols, kv_cols)], gkv_out, local.at[8]))
            grad = grad_buf[...].reshape(total, cols + kv_cols)
            sums = jnp.sum(grad.astype(f32), axis=0, keepdims=True)
            gq_sum[...] = sums[:, :cols]
            gkv_sum[...] = sums[:, cols:]
            for i in range(PLANE // 2):
                tiles[i].wait()
                if i + 1 < PLANE // 2:
                    tiles.append(h_fetch(i + 1))
                term = dot_tn(h_buf[i % 2], grad).astype(bf16)
                for k in range(2):
                    lines = term[k * part : (k + 1) * part]
                    dwq_buf[2 * i + k] = lines[:, :cols].reshape(layers, part // layers, cols)
                    dwkv_buf[2 * i + k] = lines[:, cols:]
            stores.append(load(dwq_buf, dwq_out, local.at[9]))
            stores.append(load(dwkv_buf, dwkv_out, local.at[10]))

        def emit(line, value):
            out_ref[line, :] = residual_ref[line, :] + value + bias_ref[...]

        Scatter.take(p, own, s).run(plain_product(a_buf, w_buf), emit, idle)
        for copy in stores:
            copy.wait()

    return pl.pallas_call(
        kernel,
        out_shape=[
            jax.ShapeDtypeStruct(queries.shape, bf16),
            jax.ShapeDtypeStruct(keyval.shape, bf16),
            jax.ShapeDtypeStruct((1, cols), f32),
            jax.ShapeDtypeStruct((1, kv_cols), f32),
            jax.ShapeDtypeStruct((PLANE, layers, part // layers, cols), bf16),
            jax.ShapeDtypeStruct((PLANE, part, kv_cols), bf16),
            jax.ShapeDtypeStruct((own, wide), f32),
        ],
        in_specs=[pl.BlockSpec(memory_space=pltpu.SMEM)]
        + [ANY] * 3
        + [WHOLE]
        + [ANY] * 3
        + [WHOLE] * 2,
        out_specs=[ANY, ANY, WHOLE, WHOLE, ANY, ANY, WHOLE],
        scratch_shapes=[
            pltpu.VMEM(act.shape, bf16),
            pltpu.VMEM(wp.shape, bf16),
            pltpu.VMEM(queries.shape, bf16),
            pltpu.VMEM(keyval.shape, bf16),
            pltpu.VMEM(grads.shape, bf16),
            pltpu.VMEM((groups, streams, rows, cols + kv_cols), bf16),
            pltpu.VMEM((length, HD), f32),
            pltpu.VMEM((length, HD), f32),
            pltpu.VMEM((2, total, 2 * part), bf16),
            pltpu.VMEM((PLANE, layers, part // layers, cols), bf16),
            pltpu.VMEM((PLANE, part, kv_cols), bf16),
        ]
        + Scatter.scratch(own, wide)
        + [sems(11)],
        compiler_params=params(number),
        cost_estimate=cost(2 * total * depth * wide),
        name="attend_back_scatter_proj",
    )(docs, queries, keyval, grads, lse, act, wp, hidden1, residual, b_proj)


def pack_vectors(vectors):
    sizes = [v.shape[0] for v in vectors]
    lines = -(-sum(sizes) // (PLANE * 8 * 128)) * 8
    pad = PLANE * lines * 128 - sum(sizes)
    return jnp.concatenate(vectors + (jnp.zeros((pad,), f32),)).reshape(PLANE, lines, 128)


def unpack_vectors(packed, vectors):
    flat = packed.reshape(-1)
    sums, at = [], 0
    for v in vectors:
        sums.append(flat[at : at + v.shape[0]])
        at += v.shape[0]
    return sums


def after(value, *earlier):
    return lax.optimization_barrier((value, *earlier))[0]


def line_gather(shard, axis=0):
    return lax.all_gather(shard, "fsdp", axis=axis, tiled=True)


def line_scatter(grad, axis=0):
    return lax.psum_scatter(grad.astype(bf16), "fsdp", scatter_dimension=axis, tiled=True)


def column_weight_grad(grad, groups):
    rows, cols = grad.shape
    return line_scatter(grad.reshape(groups, rows // groups, cols), 1)


def shards(
    tokens,
    doc_starts,
    w_query,
    w_kv,
    w_out,
    w_fc,
    w_proj,
    ln1_gain,
    ln1_bias,
    b_query,
    b_value,
    b_out,
    ln2_gain,
    ln2_bias,
    b_fc,
    b_proj,
    cotangent,
):
    layers = lax.axis_size("fsdp")
    me = lax.axis_index("seq")
    streams, rows, width = tokens.shape
    own = streams * rows
    heads = HEADS // PLANE
    hidden = b_fc.shape[0]
    my_cols = heads * HD
    my_hidden = hidden // PLANE
    total = PLANE * own

    own_tokens = tokens.reshape(own, width)
    cot_low = cotangent.reshape(own, width)

    def row(vector):
        return vector.reshape(1, -1)

    wq_pieces, wf_pieces, low_kv, wo, low_hidden1, mean1, inverse1 = split_weights(
        own_tokens, row(ln1_gain), row(ln1_bias), w_query, w_fc, w_kv, w_out, layers, 1
    )
    wf = line_gather(wf_pieces, 1).reshape(width, my_hidden)
    wp = line_gather(w_proj)
    my_bq = row(lax.dynamic_slice_in_dim(b_query, me * my_cols, my_cols, 0))
    my_bf = row(lax.dynamic_slice_in_dim(b_fc, me * my_hidden, my_hidden, 0))
    bkv = row(jnp.concatenate([jnp.zeros((HD,), f32), b_value]))

    hidden1, w_kv_all, wq = gather_hidden1(low_hidden1, low_kv, wq_pieces, layers, 2)
    wq = wq.reshape(width, my_cols)
    cot_all, queries, keyval, mixed, lse = project_attend(
        doc_starts, hidden1, wq, w_kv_all, my_bq, bkv, cot_low, streams, heads, 3
    )
    mixed_rows = mixed.reshape(total, my_cols)
    residual, low_hidden2, mean2, inverse2 = scatter_attn(
        mixed_rows, wo, own_tokens, row(b_out), row(ln2_gain), row(ln2_bias), 4
    )
    hidden2, act_low, slope, grad_w_proj = gather_fc(low_hidden2, wf, my_bf, cot_all, 5)
    shard_proj = line_scatter(grad_w_proj)

    grad_residual, grad_attn, sums2, my_grad_b_fc, grad_w_fc = scatter_fc(
        cot_all, slope, wp, wf, hidden2, cot_low, residual, mean2, inverse2, row(ln2_gain), 6
    )
    fc_pieces = column_weight_grad(grad_w_fc, PLANE)
    grad_mixed, grad_w_out = gather_out(grad_attn, wo, mixed_rows, 7)
    gq, gkv, my_grad_b_query, sums_kv, grad_w_query, grad_w_kv, output = attend_back_scatter_proj(
        doc_starts,
        queries,
        keyval,
        after(grad_mixed, shard_proj).reshape(PLANE, streams, rows, my_cols),
        lse,
        act_low,
        wp,
        hidden1,
        residual,
        row(b_proj),
        layers,
        heads,
        8,
    )
    input_grad, sums1, shard_out, shard_query, shard_kv = scatter_query(
        gq.reshape(total, my_cols),
        gkv.reshape(total, 2 * HD),
        wq,
        w_kv_all,
        grad_w_out,
        grad_w_query,
        grad_w_kv,
        (own_tokens, mean1, inverse1, row(ln1_gain), grad_residual),
        layers,
        9,
    )

    zero = jnp.zeros_like
    grad_b_query = lax.dynamic_update_slice_in_dim(
        zero(b_query), my_grad_b_query.reshape(-1), me * my_cols, 0
    )
    grad_b_fc = lax.dynamic_update_slice_in_dim(
        zero(b_fc), my_grad_b_fc.reshape(-1), me * my_hidden, 0
    )
    vectors = (
        sums1[0],
        sums1[1],
        grad_b_query,
        sums_kv[0, HD:],
        sums2[2],
        sums2[0],
        sums2[1],
        grad_b_fc,
        sums2[3],
    )
    packed, shard_fc = last_exchange(pack_vectors(vectors), fc_pieces, layers, 10)
    sums = unpack_vectors(packed, vectors)
    return (
        output.reshape(streams, rows, width),
        input_grad.reshape(streams, rows, width),
        shard_query.astype(f32),
        shard_kv,
        shard_out,
        shard_fc.astype(f32),
        shard_proj.astype(f32),
        *sums,
    )


def gather_seq(block):
    return lax.all_gather(block, "seq", axis=0, tiled=True)


def scatter_seq(partial):
    return lax.psum_scatter(partial.astype(bf16), "seq", scatter_dimension=0, tiled=True).astype(f32)


def columns_to_rows(part, groups):
    rows = part.shape[0]
    spread = part.reshape(rows, groups, part.shape[1] // groups).transpose(1, 0, 2)
    return lax.all_to_all(spread, "seq", split_axis=0, concat_axis=0, tiled=True)


def column_weight(shard, groups):
    pieces = columns_to_rows(shard, groups)
    full = lax.all_gather(pieces, "fsdp", axis=1, tiled=True)
    return full.reshape(-1, full.shape[2])


def plain_column_grad(grad, groups):
    rows, cols = grad.shape
    kept = lax.psum_scatter(
        grad.astype(bf16).reshape(groups, rows // groups, cols), "fsdp", scatter_dimension=1, tiled=True
    )
    moved = lax.all_to_all(kept, "seq", split_axis=0, concat_axis=0, tiled=True)
    return moved.transpose(1, 0, 2).reshape(moved.shape[1], groups * cols).astype(f32)


def row_weight_grad(grad):
    return lax.psum_scatter(grad.astype(bf16), "fsdp", scatter_dimension=0, tiled=True).astype(f32)


def plain_attend(queries, keyval, starts, groups, streams, rows, heads):
    length = groups * rows
    scale = HD ** (-0.5)
    position = jnp.arange(length, dtype=jnp.int32)
    mixed_list, lse_list = [], []
    for stream in range(streams):
        q = queries[:, stream].reshape(length, heads, HD)
        k = keyval[:, stream, :, :HD].reshape(length, HD)
        v = keyval[:, stream, :, HD:].reshape(length, HD)
        segment = jnp.sum((starts[stream][None, :] <= position[:, None]).astype(jnp.int32), axis=1)
        allowed = (position[None, :] <= position[:, None]) & (segment[None, :] == segment[:, None])
        scores = jnp.einsum("thd,ud->htu", q, k, preferred_element_type=f32) * scale
        scores = jnp.where(allowed[None], scores, -1e30)
        top = jnp.max(scores, axis=-1, keepdims=True)
        lse = top + jnp.log(jnp.sum(jnp.exp(scores - top), axis=-1, keepdims=True))
        probs = jnp.exp(scores - lse).astype(bf16)
        mixed = jnp.einsum("htu,ud->thd", probs, v, preferred_element_type=f32)
        mixed_list.append(mixed.astype(bf16).reshape(groups, rows, heads * HD))
        lse_list.append(lse)
    return jnp.stack(mixed_list, axis=1), lse_list


def plain_attend_back(queries, keyval, grads, lse_list, starts, groups, streams, rows, heads):
    length = groups * rows
    scale = HD ** (-0.5)
    position = jnp.arange(length, dtype=jnp.int32)
    gq_list, gkv_list = [], []
    for stream in range(streams):
        q = queries[:, stream].reshape(length, heads, HD)
        g = grads[:, stream].reshape(length, heads, HD)
        k = keyval[:, stream, :, :HD].reshape(length, HD)
        v = keyval[:, stream, :, HD:].reshape(length, HD)
        segment = jnp.sum((starts[stream][None, :] <= position[:, None]).astype(jnp.int32), axis=1)
        allowed = (position[None, :] <= position[:, None]) & (segment[None, :] == segment[:, None])
        scores = jnp.einsum("thd,ud->htu", q, k, preferred_element_type=f32) * scale
        probs = jnp.exp(jnp.where(allowed[None], scores, -1e30) - lse_list[stream])
        grad_probs = jnp.einsum("thd,ud->htu", g, v, preferred_element_type=f32)
        delta = jnp.sum(probs * grad_probs, axis=-1, keepdims=True)
        gs = (probs * (grad_probs - delta)).astype(bf16)
        gq = jnp.einsum("htu,ud->thd", gs, k, preferred_element_type=f32) * scale
        gk = jnp.einsum("htu,thd->ud", gs, q, preferred_element_type=f32) * scale
        gv = jnp.einsum("htu,thd->ud", probs.astype(bf16), g, preferred_element_type=f32)
        gq_list.append(gq.astype(bf16).reshape(groups, rows, heads * HD))
        gkv_list.append(jnp.concatenate([gk, gv], axis=1).reshape(groups, rows, 2 * HD))
    return jnp.stack(gq_list, axis=1), jnp.stack(gkv_list, axis=1)


def plain_shards(
    tokens,
    doc_starts,
    w_query,
    w_kv,
    w_out,
    w_fc,
    w_proj,
    ln1_gain,
    ln1_bias,
    b_query,
    b_value,
    b_out,
    ln2_gain,
    ln2_bias,
    b_fc,
    b_proj,
    cotangent,
):
    groups = lax.axis_size("seq")
    me = lax.axis_index("seq")
    streams, rows, width = tokens.shape
    own = streams * rows
    heads = HEADS // groups
    hidden = b_fc.shape[0]
    my_cols = heads * HD
    my_hidden = hidden // groups

    wq = column_weight(w_query, groups)
    w_kv_all = gather_seq(lax.all_gather(w_kv, "fsdp", axis=0, tiled=True))
    wo = lax.all_gather(w_out, "fsdp", axis=0, tiled=True)
    wf = column_weight(w_fc, groups)
    wp = lax.all_gather(w_proj, "fsdp", axis=0, tiled=True)
    my_bq = lax.dynamic_slice_in_dim(b_query, me * my_cols, my_cols, 0)
    my_bf = lax.dynamic_slice_in_dim(b_fc, me * my_hidden, my_hidden, 0)

    inputs = tokens.reshape(own, width).astype(f32)
    cot_low = cotangent.reshape(own, width)
    cot_full = cot_low.astype(f32)
    shifted1, normed1, inverse1 = normalize(inputs, ln1_gain, ln1_bias)
    hidden1 = gather_seq(shifted1.astype(bf16))
    queries = (dot(hidden1, wq) + my_bq).astype(bf16).reshape(groups, streams, rows, my_cols)
    value_shift = jnp.concatenate([jnp.zeros((HD,), f32), b_value])
    keyval = (dot(hidden1, w_kv_all) + value_shift).astype(bf16).reshape(groups, streams, rows, 2 * HD)
    mixed, lse = plain_attend(queries, keyval, doc_starts, groups, streams, rows, heads)
    mixed_rows = mixed.reshape(groups * own, my_cols)
    residual = inputs + scatter_seq(dot(mixed_rows, wo)) + b_out
    shifted2, normed2, inverse2 = normalize(residual, ln2_gain, ln2_bias)
    hidden2 = gather_seq(shifted2.astype(bf16))
    cot_all = gather_seq(cot_low)
    pre_act = dot(hidden2, wf) + my_bf
    activated, slope = gelu_pair(pre_act)
    act_low = activated.astype(bf16)
    output = residual + scatter_seq(dot(act_low, wp)) + b_proj

    grad_b_proj = jnp.sum(cot_full, axis=0)
    shard_proj = row_weight_grad(dot_tn(act_low, cot_all))
    grad_pre = (dot_nt(cot_all, wp) * slope).astype(bf16)
    my_grad_b_fc = jnp.sum(grad_pre.astype(f32), axis=0)
    shard_fc = plain_column_grad(dot_tn(hidden2, grad_pre), groups)
    grad_hidden2 = scatter_seq(dot_nt(grad_pre, wf))
    back_second, grad_ln2_gain, grad_ln2_bias = normalize_back(
        grad_hidden2, normed2, inverse2, ln2_gain
    )
    grad_residual = cot_full + back_second
    grad_attn = grad_residual.astype(bf16)
    grad_b_out = jnp.sum(grad_attn.astype(f32), axis=0)
    grad_attn_all = gather_seq(grad_attn)
    shard_out = row_weight_grad(dot_tn(mixed_rows, grad_attn_all))
    grad_mixed = dot_nt(grad_attn_all, wo).astype(bf16).reshape(groups, streams, rows, my_cols)
    gq, gkv = plain_attend_back(
        queries, keyval, grad_mixed, lse, doc_starts, groups, streams, rows, heads
    )
    gq_rows = gq.reshape(groups * own, my_cols)
    gkv_rows = gkv.reshape(groups * own, 2 * HD)
    my_grad_b_query = jnp.sum(gq_rows.astype(f32), axis=0)
    grad_b_value = jnp.sum(gkv_rows[:, HD:], axis=0)
    gkv_low = gkv_rows.astype(bf16)
    shard_query = plain_column_grad(dot_tn(hidden1, gq_rows), groups)
    shard_kv = row_weight_grad(scatter_seq(dot_tn(hidden1, gkv_low)))
    grad_hidden1 = scatter_seq(dot_nt(gq_rows, wq) + dot_nt(gkv_low, w_kv_all))
    back_first, grad_ln1_gain, grad_ln1_bias = normalize_back(
        grad_hidden1, normed1, inverse1, ln1_gain
    )
    input_grad = grad_residual + back_first

    zero = jnp.zeros_like
    grad_b_query = lax.dynamic_update_slice_in_dim(zero(b_query), my_grad_b_query, me * my_cols, 0)
    grad_b_fc = lax.dynamic_update_slice_in_dim(zero(b_fc), my_grad_b_fc, me * my_hidden, 0)
    vectors = (
        grad_ln1_gain,
        grad_ln1_bias,
        grad_b_query,
        grad_b_value,
        grad_b_out,
        grad_ln2_gain,
        grad_ln2_bias,
        grad_b_fc,
        grad_b_proj,
    )
    sums = lax.psum(vectors, ("seq", "fsdp"))
    return (
        output.reshape(streams, rows, width),
        input_grad.reshape(streams, rows, width),
        shard_query,
        shard_kv,
        shard_out,
        shard_fc,
        shard_proj,
        *sums,
    )


def solution(mesh):
    acts = P("fsdp", "seq", None)
    weight = P(("seq", "fsdp"), None)
    return jax.shard_map(
        shards if mesh.shape["seq"] == PLANE else plain_shards,
        mesh=mesh,
        in_specs=(acts, P("fsdp", None)) + (weight,) * 5 + (P(),) * 9 + (acts,),
        out_specs=(acts, acts) + (weight,) * 5 + (P(),) * 9,
        check_vma=False,
    )
```

```python
import functools

import jax
import jax.numpy as jnp
from jax import lax
from jax.experimental import pallas as pl
from jax.experimental.pallas import tpu as pltpu
from jax.sharding import PartitionSpec as P

HEADS = 16
HD = 128

root_two_pi = 0.7978845608028654
cubic_coef = 0.044715
epsilon = 1e-05
f32 = jnp.float32
bf16 = jnp.bfloat16
MESH = pl.DeviceIdType.MESH
ANY = pl.BlockSpec(memory_space=pl.ANY)
WHOLE = pl.BlockSpec(memory_space=pltpu.VMEM)
VMEM_LIMIT = 62 * 1024 * 1024
PLANE = 8


def normalize(values, gain_row, shift_row):
    center = values - jnp.mean(values, axis=-1, keepdims=True)
    inverse = lax.rsqrt(jnp.mean(center * center, axis=-1, keepdims=True) + epsilon)
    normed = center * inverse
    return (normed * gain_row + shift_row, normed, inverse)


def normalize_back(grad_out, normed, inverse, gain_row):
    scaled = grad_out * gain_row
    grad_in = inverse * (
        scaled
        - jnp.mean(scaled, axis=-1, keepdims=True)
        - normed * jnp.mean(scaled * normed, axis=-1, keepdims=True)
    )
    return (grad_in, jnp.sum(grad_out * normed, axis=0), jnp.sum(grad_out, axis=0))


def norm_stats(values):
    mean = jnp.mean(values, axis=-1, keepdims=True)
    center = values - mean
    return mean, lax.rsqrt(jnp.mean(center * center, axis=-1, keepdims=True) + epsilon)


def norm_back(grad_out, normed, inverse, gain_row):
    scaled = grad_out * gain_row
    return inverse * (
        scaled
        - jnp.mean(scaled, axis=-1, keepdims=True)
        - normed * jnp.mean(scaled * normed, axis=-1, keepdims=True)
    )


def gelu_pair(inputs):
    tangent = jnp.tanh(root_two_pi * (inputs + cubic_coef * inputs * inputs * inputs))
    activated = 0.5 * inputs * (1.0 + tangent)
    gradient_slope = 0.5 * (1.0 + tangent) + 0.5 * inputs * (
        1.0 - tangent * tangent
    ) * root_two_pi * (1.0 + 3.0 * cubic_coef * inputs * inputs)
    return (activated, gradient_slope)


def dot(a, b):
    return jnp.dot(a, b, preferred_element_type=f32)


def dot_nt(a, b):
    return lax.dot_general(a, b, (((1,), (1,)), ((), ())), preferred_element_type=f32)


def dot_tn(a, b):
    return lax.dot_general(a, b, (((0,), (0,)), ((), ())), preferred_element_type=f32)


def push(src, dst, send, recv, to):
    return pltpu.make_async_remote_copy(
        src_ref=src, dst_ref=dst, send_sem=send, recv_sem=recv, device_id=to, device_id_type=MESH
    )


def sems(*shape):
    return pltpu.SemaphoreType.DMA(shape)


def rows_at(start, size):
    return pl.ds(pl.multiple_of(start, size), size)


class Place:
    def __init__(self):
        me = lax.axis_index("seq")
        self.me = me
        self.core = lax.rem(me, 2)
        x = lax.rem(lax.div(me, 2), 2)
        y = lax.div(me, 4)
        self.sib = me + 1 - 2 * self.core
        self.xn = me + 2 - 4 * x
        self.yn = me + 4 - 8 * y
        self.dg = me + 2 - 4 * x + 4 - 8 * y
        turn = 1 - 2 * self.core
        self.xs, self.ys, self.ds = self.xn + turn, self.yn + turn, self.dg + turn
        self.layer = lax.axis_index("fsdp")

    def plane_peer(self, step):
        return lax.rem(self.me + step, PLANE)

    def line_peer(self, step, layers):
        return lax.rem(self.layer + step, layers)

    def greet(self, whole_plane=False, layers=1):
        barrier = pltpu.get_barrier_semaphore()
        if whole_plane:
            others = [self.plane_peer(step) for step in range(1, PLANE)]
        else:
            others = [self.sib, self.xn, self.yn]
        for other in others:
            pl.semaphore_signal(barrier, inc=1, device_id={"seq": other}, device_id_type=MESH)
        for step in range(1, layers):
            other = self.line_peer(step, layers)
            pl.semaphore_signal(barrier, inc=1, device_id={"fsdp": other}, device_id_type=MESH)
        pl.semaphore_wait(barrier, len(others) + layers - 1)


class Gather:
    sends = 14
    scratch = [sems(14), sems(PLANE, 2)]

    def __init__(self, place, buf, rows, send, recv):
        self.p, self.buf, self.rows, self.half = place, buf, rows, rows // 2
        self.send_sem, self.recv_sem = send, recv
        self.copies = []

    def piece(self, dev, half):
        return self.buf.at[rows_at(dev * self.rows + half * self.half, self.half), :]

    def pair(self, dev):
        return rows_at(lax.div(dev, 2) * (2 * self.rows), 2 * self.rows)

    def send(self, dev, half, to, src=None):
        k = len(self.copies)
        piece = self.piece(dev, half)
        copy = push(
            piece if src is None else src,
            piece,
            self.send_sem.at[k],
            self.recv_sem.at[dev, half],
            {"seq": to},
        )
        copy.start()
        self.copies.append(copy)

    def arrived(self, dev, half):
        piece = self.piece(dev, half)
        push(
            piece, piece, self.send_sem.at[0], self.recv_sem.at[dev, half], {"seq": self.p.sib}
        ).wait_recv()

    def start(self, own):
        p = self.p
        parts = [own.at[pl.ds(h * self.half, self.half), :] for h in range(2)]
        self.send(p.me, 0, p.yn, parts[0])
        self.send(p.me, 1, p.xn, parts[1])
        self.send(p.me, 1, p.yn, parts[1])
        self.send(p.me, 0, p.xn, parts[0])
        for h in range(2):
            self.send(p.me, h, p.sib, parts[h])

    def relay_first(self):
        p = self.p
        self.arrived(p.yn, 0)
        self.send(p.yn, 0, p.xn)
        self.arrived(p.xn, 1)
        self.send(p.xn, 1, p.yn)
        self.send(p.yn, 0, p.sib)
        self.send(p.xn, 1, p.sib)

    def relay_rest(self):
        p = self.p
        self.arrived(p.xn, 0)
        self.send(p.xn, 0, p.sib)
        self.arrived(p.yn, 1)
        self.send(p.yn, 1, p.sib)

    def relay(self):
        self.relay_first()
        self.relay_rest()

    def have(self, dev):
        self.arrived(dev, 0)
        self.arrived(dev, 1)

    def relay_corner(self):
        p = self.p
        for h in range(2):
            self.arrived(p.dg, h)
            self.send(p.dg, h, p.sib)

    def finish(self):
        for copy in self.copies:
            copy.wait_send()


class Scatter:
    LINES = 32

    def __init__(
        self, place, rows, acc, part, sib_out, sib_in, boxes, sib_send, sib_recv, send, recv
    ):
        self.p, self.rows, self.half = place, rows, rows // 2
        self.wide = part.shape[2]
        self.acc, self.part, self.sib_out, self.sib_in = acc, part, sib_out, sib_in
        self.out_d, self.out_x, self.out_y, self.in_d, self.in_x, self.in_y = boxes
        self.sib_send, self.sib_recv, self.send, self.recv = sib_send, sib_recv, send, recv
        self.copies = []

    @staticmethod
    def scratch(rows, wide):
        return [
            pltpu.VMEM((2 * rows, wide // 2), f32),
            pltpu.VMEM((4, rows, wide), f32),
            pltpu.VMEM((4, rows, wide), bf16),
            pltpu.VMEM((4, rows, wide), bf16),
            *[pltpu.VMEM((rows, wide), bf16)] * 6,
            sems(4, 2),
            sems(4, 2),
            sems(8),
            sems(8),
        ]

    @classmethod
    def take(cls, place, rows, refs):
        return cls(place, rows, *refs[:4], refs[4:10], *refs[10:14])

    refs = 14

    def cols(self, c):
        return pl.ds(c * (self.wide // 2), self.wide // 2)

    def swap(self, role, dev, product, c):
        p = self.p
        self.acc[...] = product(role, rows_at(lax.div(dev, 2) * (2 * self.rows), 2 * self.rows), c)
        theirs = rows_at((1 - p.core) * self.rows, self.rows)
        ours = rows_at(p.core * self.rows, self.rows)
        self.sib_out[role, :, self.cols(c)] = self.acc[theirs, :].astype(bf16)
        copy = push(
            self.sib_out.at[role, :, self.cols(c)],
            self.sib_in.at[role, :, self.cols(c)],
            self.sib_send.at[role, c],
            self.sib_recv.at[role, c],
            {"seq": p.sib},
        )
        copy.start()
        self.copies.append(copy)
        self.part[role, :, self.cols(c)] = self.acc[ours, :]
        return copy

    def swap_all(self, role, dev, product):
        return [self.swap(role, dev, product, c) for c in range(2)]

    def add_into(self, dst, role, first, size, more=(), cols=slice(None)):
        lines = self.LINES

        @pl.loop(0, size // lines)
        def _(i):
            line = rows_at(first + i * lines, lines)
            value = self.part[role, line, cols] + self.sib_in[role, line, cols].astype(f32)
            for ref in more:
                value = value + ref[line, cols].astype(f32)
            if dst is None:
                self.emit(line, value)
            else:
                dst[line, cols] = value.astype(dst.dtype)

    def ship(self, src, dst, h, k, to, cols=slice(None)):
        lines = pl.ds(h * self.half, self.half)
        copy = push(
            src.at[lines, cols], dst.at[lines, cols], self.send.at[k], self.recv.at[k], {"seq": to}
        )
        copy.start()
        self.copies.append(copy)
        return copy

    def ship_corner(self, c):
        cols = self.cols(c)
        self.add_into(self.out_d, 0, 0, self.rows, (), cols)
        return (
            self.ship(self.out_d, self.in_d, 0, 2 * c, self.p.xn, cols),
            self.ship(self.out_d, self.in_d, 1, 2 * c + 1, self.p.yn, cols),
        )

    def run(self, product, emit, idle=None, early=None):
        p, rows, half = self.p, self.rows, self.half
        self.emit = emit
        d0 = self.swap(0, p.dg, product, 0)
        d1 = self.swap(0, p.dg, product, 1)
        d0.wait_recv()
        dx0, dy0 = self.ship_corner(0)
        to_x = [self.swap(1, p.xn, product, 0)]
        d1.wait_recv()
        dx1, dy1 = self.ship_corner(1)
        to_x.append(self.swap(1, p.xn, product, 1))
        to_y = self.swap_all(2, p.yn, product)
        for copy in to_x:
            copy.wait_recv()
        self.add_into(self.out_x, 1, 0, half)
        x0 = self.ship(self.out_x, self.in_x, 0, 4, p.xn)
        for copy in to_y:
            copy.wait_recv()
        self.add_into(self.out_y, 2, half, half)
        y1 = self.ship(self.out_y, self.in_y, 1, 5, p.yn)
        to_me = self.swap_all(3, p.me, product)
        if early is not None:
            early()
        dy0.wait_recv()
        dy1.wait_recv()
        self.add_into(self.out_x, 1, half, half, (self.in_d,))
        x1 = self.ship(self.out_x, self.in_x, 1, 6, p.xn)
        dx0.wait_recv()
        dx1.wait_recv()
        self.add_into(self.out_y, 2, 0, half, (self.in_d,))
        y0 = self.ship(self.out_y, self.in_y, 0, 7, p.yn)
        if idle is not None:
            idle()
        for copy in to_me:
            copy.wait_recv()
        x0.wait_recv()
        y0.wait_recv()
        self.add_into(None, 3, 0, half, (self.in_x, self.in_y))
        y1.wait_recv()
        x1.wait_recv()
        self.add_into(None, 3, half, half, (self.in_x, self.in_y))
        for copy in self.copies:
            copy.wait_send()


class LineGather:
    def __init__(self, place, src, block, layers, send, recv):
        self.me, self.src, self.block, self.layers = place.layer, src, block, layers
        self.send, self.recv = send, recv
        self.step = 0

    @staticmethod
    def scratch(layers):
        return [sems(2 * layers), sems(layers)]

    def copy(self, src, layer, k, to):
        return push(src, self.block(layer), self.send.at[k], self.recv.at[layer], {"fsdp": to})

    def wait_from(self, layer):
        other = lax.rem(self.me + 1, self.layers)
        self.copy(self.block(layer), layer, 0, other).wait_recv()

    def start(self):
        me, top = self.me, self.layers - 1

        @pl.when(me < top)
        def _():
            self.copy(self.src, me, 0, me + 1).start()

        @pl.when(me > 0)
        def _():
            self.copy(self.src, me, self.layers, me - 1).start()

    def poll(self):
        me, top, hop = self.me, self.layers - 1, self.step
        self.step += 1
        below, above = me - 1 - hop, me + 1 + hop

        @pl.when((below >= 0) & (me < top))
        def _():
            self.wait_from(below)
            self.copy(self.block(below), below, hop + 1, me + 1).start()

        @pl.when((above <= top) & (me > 0))
        def _():
            self.wait_from(above)
            self.copy(self.block(above), above, self.layers + hop + 1, me - 1).start()

    def finish(self):
        while self.step < self.layers - 2:
            self.poll()
        me, top = self.me, self.layers - 1

        @pl.when(me == top)
        def _():
            for layer in range(top):
                self.wait_from(layer)

        @pl.when(me == 0)
        def _():
            for layer in range(1, top + 1):
                self.wait_from(layer)

        for hop in range(top):

            @pl.when((hop <= me) & (me < top))
            def _(hop=hop):
                self.copy(self.block(me), me, hop, me + 1).wait_send()

            @pl.when((hop <= top - me) & (me > 0))
            def _(hop=hop):
                self.copy(self.block(me), me, self.layers + hop, me - 1).wait_send()


class LineSum:
    def __init__(self, place, block, layers, own, up, down, us, ur, ds, dr, local):
        self.me, self.block, self.layers = place.layer, block, layers
        self.own, self.up, self.down = own, up, down
        self.us, self.ur, self.ds, self.dr, self.local = us, ur, ds, dr, local
        self.step = 0
        self.loads = [load(block(f), own.at[f], local.at[f]) for f in range(layers)]

    @staticmethod
    def scratch(shape, layers):
        return [
            pltpu.VMEM((layers, *shape), bf16),
            pltpu.VMEM((layers - 1, *shape), bf16),
            pltpu.VMEM((layers - 1, *shape), bf16),
            *[sems(layers)] * 5,
        ]

    refs = 8

    def up_copy(self, src, f, to):
        return push(src, self.up.at[f - 1], self.us.at[f], self.ur.at[f], {"fsdp": to})

    def down_copy(self, src, f, to):
        return push(src, self.down.at[f], self.ds.at[f], self.dr.at[f], {"fsdp": to})

    def start(self):
        top = self.layers - 1

        @pl.when(self.me == 0)
        def _():
            for f in range(top, 0, -1):
                self.up_copy(self.block(f), f, 1).start()
            self.up[0] = jnp.zeros(self.up.shape[1:], bf16)

        @pl.when(self.me == top)
        def _():
            for f in range(top):
                self.down_copy(self.block(f), f, top - 1).start()
            self.down[top - 1] = jnp.zeros(self.down.shape[1:], bf16)

    def chunks(self):
        shape = self.own.shape[1:]
        size = 1 if len(shape) == 3 else 32
        return shape[0] // size, lambda i: rows_at(i * size, size) if size > 1 else i

    def add(self, box, slot, f):
        count, where = self.chunks()

        @pl.loop(0, count)
        def _(i):
            here = where(i)
            value = box[slot, here].astype(f32) + self.own[f, here].astype(f32)
            box[slot, here] = value.astype(bf16)

    def poll(self):
        top, k = self.layers - 1, self.step
        self.step += 1
        if k == 0:
            for copy in self.loads:
                copy.wait()
        for f in range(2, top + 1):
            at = f - top + 1 + k
            if not 1 <= at < f:
                continue

            @pl.when(self.me == at)
            def _(f=f, at=at):
                self.up_copy(self.up.at[f - 1], f, at + 1).wait_recv()
                self.add(self.up, f - 1, f)
                self.up_copy(self.up.at[f - 1], f, at + 1).start()

            @pl.when(self.me == top - at)
            def _(f=top - f, at=top - at):
                self.down_copy(self.down.at[f], f, at - 1).wait_recv()
                self.add(self.down, f, f)
                self.down_copy(self.down.at[f], f, at - 1).start()

    def finish(self, emit):
        while self.step < self.layers - 2:
            self.poll()
        me, top = self.me, self.layers - 1

        @pl.when(me > 0)
        def _():
            self.up_copy(self.up.at[me - 1], me, me - 1).wait_recv()

        @pl.when(me < top)
        def _():
            self.down_copy(self.down.at[me], me, me + 1).wait_recv()

        count, where = self.chunks()
        below, above = jnp.maximum(me - 1, 0), jnp.minimum(me, top - 1)

        @pl.loop(0, count)
        def _(i):
            here = where(i)
            value = self.up[below, here].astype(f32) + self.down[above, here].astype(f32)
            emit(here, value + self.own[me, here].astype(f32))

        for f in range(1, top + 1):

            @pl.when(me < f)
            def _(f=f):
                self.up_copy(self.up.at[f - 1], f, me + 1).wait_send()

        for f in range(top):

            @pl.when(me > f)
            def _(f=f):
                self.down_copy(self.down.at[f], f, me - 1).wait_send()


class PlaneSum:
    def __init__(self, place, src, box, send, recv):
        self.p, self.src, self.box = place, src, box
        self.copies = []
        for step in range(1, PLANE):
            to = place.plane_peer(step)
            copy = push(src.at[to], box.at[step], send.at[step], recv.at[step], {"seq": to})
            copy.start()
            self.copies.append(copy)

    def total(self):
        value = self.src[self.p.me].astype(f32)
        for step, copy in enumerate(self.copies):
            copy.wait_recv()
            value = value + self.box[step + 1].astype(f32)
        return value

    def finish(self):
        for copy in self.copies:
            copy.wait_send()


class Spread:
    def __init__(self, place, src, out, send, recv, local, room=None):
        cols = src.shape[2]
        spot = out.at[:, rows_at(place.me * cols, cols)]
        if room is None:
            self.copies = [load(src.at[place.me], spot, local)]
        else:
            self.copies = [Through(src.at[place.me], room, spot, local)]
        for step in range(1, PLANE):
            to = place.plane_peer(step)
            copy = push(src.at[to], spot, send.at[step], recv.at[step], {"seq": to})
            copy.start()
            self.copies.append(copy)

    def finish(self):
        for copy in self.copies:
            copy.wait()


def fold(ref, first, value):
    rows, wide = value.shape
    total = jnp.sum(value.reshape(rows // 8, 8, wide), axis=0)

    @pl.when(first)
    def _():
        ref[...] = total

    @pl.when(jnp.logical_not(first))
    def _():
        ref[...] += total


def params(number, vmem=True):
    return pltpu.CompilerParams(
        collective_id=number,
        has_side_effects=True,
        vmem_limit_bytes=VMEM_LIMIT if vmem else None,
    )


def cost(flops, mib=40):
    return pl.CostEstimate(flops=flops, bytes_accessed=mib * 1024 * 1024, transcendentals=0)


def load(src, dst, sem):
    copy = pltpu.make_async_copy(src, dst, sem)
    copy.start()
    return copy


class Through:
    def __init__(self, src, room, dst, sem):
        self.room, self.dst, self.sem = room, dst, sem
        self.copy = load(src, room, sem)

    def put(self):
        self.copy.wait()
        self.copy = load(self.room, self.dst, self.sem)

    def wait(self):
        self.copy.wait()


def rows_of(ref, rows):
    return lambda k: ref.at[rows_at(k * rows, rows), :]


def split_weights(tokens, gain, shift, w_query, w_fc, w_kv, w_out, layers, number):
    arrays, lined = (w_query, w_fc), (w_kv, w_out)
    own_rows, width = tokens.shape

    def kernel(tok_ref, gain_ref, shift_ref, wq_ref, wf_ref, kv_ref, wo_ref, *refs):
        wq_out, wf_out, kv_out, wo_out, hidden, mean_out, inverse_out = refs[:7]
        send, recv, kv_send, kv_recv, wo_send, wo_recv, local = refs[7:14]
        rooms = refs[14:]
        p = Place()
        ins, outs = (wq_ref, wf_ref), (wq_out, wf_out)
        lines = (
            LineGather(p, kv_ref, rows_of(kv_out, kv_ref.shape[0]), layers, kv_send, kv_recv),
            LineGather(p, wo_ref, rows_of(wo_out, wo_ref.shape[0]), layers, wo_send, wo_recv),
        )

        def block(i, dev):
            cols = ins[i].shape[1] // PLANE
            return ins[i].at[:, rows_at(dev * cols, cols)]

        own = []
        for i in range(2):
            own.append(Through(block(i, p.me), rooms[i], outs[i].at[p.me], local.at[i]))
            own.append(Through(lines[i].src, rooms[2 + i], lines[i].block(p.layer), local.at[2 + i]))
        p.greet(True, layers)
        for line in lines:
            line.start()
        copies = []
        for i in (1, 0):
            for step in range(1, PLANE):
                to = p.plane_peer(step)
                copies.append(
                    push(
                        block(i, to),
                        outs[i].at[p.me],
                        send.at[i, step],
                        recv.at[i, step],
                        {"seq": to},
                    )
                )
                copies[-1].start()

        for copy in own:
            copy.put()

        @pl.loop(0, own_rows // 32)
        def _(i):
            here = rows_at(i * 32, 32)
            values = tok_ref[here, :].astype(f32)
            mean, inverse = norm_stats(values)
            hidden[here, :] = (
                (values - mean) * inverse * gain_ref[...] + shift_ref[...]
            ).astype(bf16)
            mean_out[here, :] = mean
            inverse_out[here, :] = inverse

        for _ in range(layers - 2):
            for line in lines:
                line.poll()
        for copy in own + copies:
            copy.wait()
        for line in lines:
            line.finish()

    return pl.pallas_call(
        kernel,
        out_shape=[
            jax.ShapeDtypeStruct((PLANE, a.shape[0], a.shape[1] // PLANE), a.dtype)
            for a in arrays
        ]
        + [jax.ShapeDtypeStruct((layers * a.shape[0], a.shape[1]), a.dtype) for a in lined]
        + [jax.ShapeDtypeStruct((own_rows, width), bf16)]
        + [jax.ShapeDtypeStruct((own_rows, 1), f32)] * 2,
        in_specs=[WHOLE] * 3 + [ANY] * 4,
        out_specs=[ANY] * 4 + [WHOLE] * 3,
        scratch_shapes=[sems(2, PLANE), sems(2, PLANE)]
        + LineGather.scratch(layers) * 2
        + [sems(4)]
        + [pltpu.VMEM((a.shape[0], a.shape[1] // PLANE), bf16) for a in arrays]
        + [pltpu.VMEM(a.shape, bf16) for a in lined],
        compiler_params=params(number),
        name="split_weights",
    )(tokens, gain, shift, w_query, w_fc, w_kv, w_out)


def gather_hidden1(hidden1, low_kv, pieces, layers, number):
    count = len(pieces)
    shapes = [(stop - start, *a.shape[1:]) for a, start, stop in pieces]

    def kernel(h_ref, kv_ref, *refs):
        ins = [refs[i].at[pl.ds(pieces[i][1], shapes[i][0])] for i in range(count)]
        (h_all, kv_all), outs = refs[count : count + 2], refs[count + 2 :]
        outs, refs = outs[:count], outs[count:]
        hs, hr, ks, kr, local, h_room, kv_room = refs[:7]
        refs = refs[7:]
        rooms, refs = refs[:count], refs[count:]
        p = Place()
        h_rows, kv_rows = h_ref.shape[0], kv_ref.shape[0]
        own = [
            Through(h_ref, h_room, h_all.at[rows_at(p.me * h_rows, h_rows), :], local.at[0]),
            Through(kv_ref, kv_room, kv_all.at[rows_at(p.me * kv_rows, kv_rows), :], local.at[1]),
        ]
        lines = []
        for i in range(count):
            own.append(Through(ins[i], rooms[i], outs[i].at[:, p.layer], local.at[2 + i]))
            lines.append(
                LineGather(
                    p, ins[i], lambda k, i=i: outs[i].at[:, k], layers, *refs[2 * i : 2 * i + 2]
                )
            )
        p.greet(False, layers)
        kv = Gather(p, kv_all, kv_rows, ks, kr)
        h = Gather(p, h_all, h_rows, hs, hr)
        kv.start(kv_ref)
        h.start(h_ref)
        for line in lines:
            line.start()
        for copy in own:
            copy.put()
        kv.relay()
        kv.relay_corner()
        lines[0].poll()
        h.relay_first()
        for line in lines[1:]:
            line.poll()
        lines[0].poll()
        h.relay_rest()
        for line in lines[1:]:
            line.poll()
        h.relay_corner()
        for g in (kv, h):
            for dev in (p.sib, p.xs, p.ys, p.ds):
                g.have(dev)
            g.finish()
        for item in own:
            item.wait()
        for line in lines:
            line.finish()

    return pl.pallas_call(
        kernel,
        out_shape=[
            jax.ShapeDtypeStruct((PLANE * hidden1.shape[0], hidden1.shape[1]), bf16),
            jax.ShapeDtypeStruct((PLANE * low_kv.shape[0], low_kv.shape[1]), bf16),
        ]
        + [jax.ShapeDtypeStruct((a[0], layers, *a[1:]), bf16) for a in shapes],
        in_specs=[ANY] * (2 + count),
        out_specs=[ANY] * (2 + count),
        scratch_shapes=Gather.scratch * 2
        + [sems(2 + count)]
        + [pltpu.VMEM(a, bf16) for a in (hidden1.shape, low_kv.shape, *shapes)]
        + LineGather.scratch(layers) * count,
        compiler_params=params(number),
        name="gather_hidden1",
    )(hidden1, low_kv, *[a for a, _, _ in pieces])


def project_attend(
    docs, hidden1, wq, w_kv, bq, bkv, cot, piece, streams, heads, layers, number
):
    piece, first, last = piece
    piece_shape = (last - first, *piece.shape[1:])
    total, depth = hidden1.shape
    cols, kv_cols = wq.shape[1], w_kv.shape[1]
    rows = total // PLANE // streams
    length = PLANE * rows
    block = min(QROWS, length)
    chunk = total // 4

    def kernel(docs_ref, h_ref, wq_ref, wkv_ref, bq_ref, bkv_ref, cot_ref, piece_ref, *refs):
        cot_all, line_all, q_out, kv_out, mixed_out, lse_ref = refs[:6]
        h_buf, wq_buf, wkv_buf, q_buf, kv_buf, mixed_buf, room, line_room = refs[6:14]
        send, recv, zsend, zrecv, local = refs[14:]
        p = Place()
        piece_ref = piece_ref.at[pl.ds(first, last - first)]
        own_rows = cot_ref.shape[0]

        def fetch(k):
            return load(
                h_ref.at[pl.ds(k * chunk, chunk), :], h_buf.at[k % 2], local.at[k % 2]
            )

        fetches = [fetch(0)]
        weights = [load(wq_ref, wq_buf, local.at[2]), load(wkv_ref, wkv_buf, local.at[3])]
        own = Through(
            cot_ref, room, cot_all.at[rows_at(p.me * own_rows, own_rows), :], local.at[4]
        )
        own_line = Through(piece_ref, line_room, line_all.at[:, p.layer], local.at[8])
        line = LineGather(p, piece_ref, lambda k: line_all.at[:, k], layers, zsend, zrecv)
        p.greet(False, layers)
        g = Gather(p, cot_all, own_rows, send, recv)
        g.start(cot_ref)
        line.start()
        own.put()
        own_line.put()
        for copy in weights:
            copy.wait()
        per = chunk // (streams * rows)
        for k in range(4):
            fetches[k].wait()
            if k < 3:
                fetches.append(fetch(k + 1))
            where = pl.ds(k * per, per)
            q = dot(h_buf[k % 2], wq_buf[...]) + bq_ref[...]
            q_buf[where] = q.astype(bf16).reshape(per, streams, rows, cols)
            kv = dot(h_buf[k % 2], wkv_buf[...]) + bkv_ref[...]
            kv_buf[where] = kv.astype(bf16).reshape(per, streams, rows, kv_cols)
        stores = [load(q_buf, q_out, local.at[5]), load(kv_buf, kv_out, local.at[6])]
        g.relay_first()
        line.poll()
        for stream in range(streams):
            attend_stream(
                docs_ref,
                stream,
                q_buf.at[:, stream],
                kv_buf.at[:, stream],
                mixed_buf.at[:, stream],
                lse_ref.at[stream],
                block,
                heads,
            )
        stores.append(load(mixed_buf, mixed_out, local.at[7]))
        g.relay_rest()
        line.poll()
        g.relay_corner()
        for dev in (p.sib, p.xs, p.ys, p.ds):
            g.have(dev)
        g.finish()
        line.finish()
        own.wait()
        own_line.wait()
        for copy in stores:
            copy.wait()

    q_shape = (PLANE, streams, rows, cols)
    kv_shape = (PLANE, streams, rows, kv_cols)
    return pl.pallas_call(
        kernel,
        out_shape=[
            jax.ShapeDtypeStruct((PLANE * cot.shape[0], cot.shape[1]), bf16),
            jax.ShapeDtypeStruct((piece_shape[0], layers, *piece_shape[1:]), bf16),
            jax.ShapeDtypeStruct(q_shape, bf16),
            jax.ShapeDtypeStruct(kv_shape, bf16),
            jax.ShapeDtypeStruct(q_shape, bf16),
            jax.ShapeDtypeStruct((streams, heads, length), f32),
        ],
        in_specs=[pl.BlockSpec(memory_space=pltpu.SMEM)] + [ANY] * 3 + [WHOLE] * 2 + [ANY] * 2,
        out_specs=[ANY] * 5 + [WHOLE],
        scratch_shapes=[
            pltpu.VMEM((2, chunk, depth), bf16),
            pltpu.VMEM(wq.shape, bf16),
            pltpu.VMEM(w_kv.shape, bf16),
            pltpu.VMEM(q_shape, bf16),
            pltpu.VMEM(kv_shape, bf16),
            pltpu.VMEM(q_shape, bf16),
            pltpu.VMEM(cot.shape, bf16),
            pltpu.VMEM(piece_shape, bf16),
        ]
        + Gather.scratch
        + LineGather.scratch(layers)
        + [sems(9)],
        compiler_params=params(number),
        cost_estimate=cost(2 * total * depth * (cols + kv_cols)),
        name="project_attend",
    )(docs, hidden1, wq, w_kv, bq, bkv, cot, piece)


def load_parts(parts, dst, local):
    copies, at = [], 0
    for i, part in enumerate(parts):
        rows = part.shape[0]
        copies.append(load(part, dst.at[pl.ds(at, rows), :], local.at[i]))
        at += rows
    return copies


def load_blocks(parts, dst, local):
    copies, at = [], 0
    for layer in range(parts[0].shape[0]):
        for part in parts:
            rows = part.shape[1]
            copies.append(load(part.at[layer], dst.at[pl.ds(at, rows), :], local.at[len(copies)]))
            at += rows
    return copies


def gather_fc(hidden2, wf, bf, cot_all, part, layers, number):
    part, first, last = part
    part_shape = (last - first, part.shape[1])
    rows, depth = hidden2.shape
    wide = wf[0].shape[1]
    n_wf = len(wf)
    total = PLANE * rows
    out_wide = cot_all.shape[1]
    tile = 256

    def kernel(own_ref, b_ref, cot_ref, part_ref, *refs):
        w_refs, refs = refs[:n_wf], refs[n_wf:]
        all_ref, act_ref, slope_ref, dw_ref, line_all = refs[:5]
        buf, w_buf, act, slope, cot, acc, dw, room, send, recv, zsend, zrecv, local, wlocal = refs[
            5:
        ]
        p = Place()
        part_ref = part_ref.at[pl.ds(first, last - first), :]
        load_own = load(own_ref, buf.at[rows_at(p.me * rows, rows), :], local.at[0])
        loads_w = load_parts(w_refs, w_buf, wlocal)
        own_line = Through(part_ref, room, line_all.at[p.layer], local.at[1])
        line = LineGather(p, part_ref, lambda k: line_all.at[k], layers, zsend, zrecv)
        p.greet(False, layers)
        g = Gather(p, buf, rows, send, recv)
        g.start(own_ref)
        line.start()
        own_line.put()
        stores = []
        cots = {}

        def fetch(k, dev):
            cots[k] = load(cot_ref.at[g.pair(dev), :], cot.at[k % 2], local.at[2 + k % 2])

        def work(k, dev):
            block = g.pair(dev)
            stores.append(load(buf.at[block, :], all_ref.at[block, :], local.at[4 + 3 * k]))

            @pl.loop(0, wide // 512)
            def _(j):
                cols = rows_at(j * 512, 512)
                acc_fc = dot(buf[block, :], w_buf[:, cols]) + b_ref[:, cols]
                activated, gradient = gelu_pair(acc_fc)
                act[block, cols] = activated.astype(bf16)
                slope[block, cols] = gradient.astype(bf16)

            for i, (src, dst) in enumerate(((act, act_ref), (slope, slope_ref))):
                stores.append(
                    load(src.at[block, :], dst.at[block, :], local.at[4 + 3 * k + 1 + i])
                )

        def grads(k, dev):
            block = g.pair(dev)
            cots[k].wait()

            for j in range(wide // tile):
                cols = pl.ds(j * tile, tile)
                term = dot_tn(act[block, cols], cot[k % 2])
                if k == 0:
                    acc[cols, :] = term
                elif k < 3:
                    acc[cols, :] += term
                else:
                    dw[cols, :] = (acc[cols, :] + term).astype(bf16)
                    stores.append(load(dw.at[cols, :], dw_ref.at[cols, :], local.at[16 + j]))

        fetch(0, p.me)
        fetch(1, p.xn)
        load_own.wait()
        for copy in loads_w:
            copy.wait()
        g.have(p.sib)
        work(0, p.me)
        g.relay_first()
        grads(0, p.me)
        line.poll()
        fetch(2, p.yn)
        g.relay_rest()
        g.have(p.xs)
        work(1, p.xn)
        g.have(p.ys)
        work(2, p.yn)
        line.poll()
        grads(1, p.xn)
        fetch(3, p.dg)
        g.relay_corner()
        grads(2, p.yn)
        g.have(p.ds)
        work(3, p.dg)
        grads(3, p.dg)
        g.finish()
        line.finish()
        own_line.wait()
        for copy in stores:
            copy.wait()

    return pl.pallas_call(
        kernel,
        out_shape=[
            jax.ShapeDtypeStruct((total, depth), bf16),
            jax.ShapeDtypeStruct((total, wide), bf16),
            jax.ShapeDtypeStruct((total, wide), bf16),
            jax.ShapeDtypeStruct((wide, out_wide), bf16),
            jax.ShapeDtypeStruct((layers, *part_shape), bf16),
        ],
        in_specs=[ANY, WHOLE] + [ANY] * (2 + n_wf),
        out_specs=[ANY] * 5,
        scratch_shapes=[
            pltpu.VMEM((total, depth), bf16),
            pltpu.VMEM((depth, wide), bf16),
            pltpu.VMEM((total, wide), bf16),
            pltpu.VMEM((total, wide), bf16),
            pltpu.VMEM((2, 2 * rows, out_wide), bf16),
            pltpu.VMEM((wide, out_wide), f32),
            pltpu.VMEM((wide, out_wide), bf16),
            pltpu.VMEM(part_shape, bf16),
        ]
        + Gather.scratch
        + LineGather.scratch(layers)
        + [sems(16 + wide // tile), sems(n_wf)],
        compiler_params=params(number),
        cost_estimate=cost(4 * total * depth * wide),
        name="gather_fc",
    )(hidden2, bf, cot_all, part, *wf)


def gather_out(
    grad_attn, wo, mixed, hidden2, grad_pre, first_fc, grad_proj, proj_cut, fc_part, layers, number
):
    rows, depth = grad_attn.shape
    wide = wo.shape[0]
    total = PLANE * rows
    hidden = grad_pre.shape[1]
    tile = 512
    steps = (depth - first_fc) // tile
    proj_shape = (grad_proj.shape[1] - proj_cut, grad_proj.shape[2])
    fc_shape = (fc_part.shape[0], *fc_part.shape[2:])

    def kernel(own_ref, w_ref, mixed_ref, h_ref, gp_ref, proj_ref, fc_ref, *refs):
        gm_ref, dw_ref, dwfc_ref, proj_out, fc_out = refs[:5]
        buf, w_buf, mixed_buf, gm, acc, dw, gp, h_buf, dwfc = refs[5:14]
        send, recv = refs[14:16]
        line_refs = refs[16:32]
        (local,) = refs[32:]
        p = Place()
        load_own = load(own_ref, buf.at[rows_at(p.me * rows, rows), :], local.at[0])
        loads = [load(w_ref, w_buf, local.at[1]), load(mixed_ref, mixed_buf, local.at[2])]
        load_gp = load(gp_ref, gp, local.at[3])
        proj = LineSum(p, lambda f: proj_ref.at[f, pl.ds(proj_cut, proj_shape[0]), :], layers, *line_refs[:8])
        fc = LineSum(p, lambda f: fc_ref.at[:, f], layers, *line_refs[8:])

        def h_fetch(i):
            here = pl.ds(first_fc + i * tile, tile)
            return load(h_ref.at[:, here], h_buf.at[i % 2], local.at[4 + i % 2])

        tiles = [h_fetch(0)]
        stores = []
        p.greet(False, layers)
        g = Gather(p, buf, rows, send, recv)
        g.start(own_ref)
        proj.start()
        fc.start()

        def work(dev):
            block = g.pair(dev)
            gm[block, :] = dot_nt(buf[block, :], w_buf[...]).astype(bf16)

        def grads(k, dev):
            block = g.pair(dev)
            term = dot_tn(mixed_buf[block, :], buf[block, :])
            if k == 0:
                acc[...] = term
            elif k < 3:
                acc[...] += term
            else:
                dw[...] = (acc[...] + term).astype(bf16)

        def fc_grads(i):
            tiles[i].wait()
            if i + 1 < steps:
                tiles.append(h_fetch(i + 1))
            if i >= 2:
                stores[i - 2].wait()
            dwfc[i % 2] = dot_tn(h_buf[i % 2], gp[...]).astype(bf16)
            stores.append(
                load(dwfc.at[i % 2], dwfc_ref.at[pl.ds(i * tile, tile), :], local.at[6 + i % 2])
            )

        load_own.wait()
        for copy in loads:
            copy.wait()
        g.have(p.sib)
        work(p.me)
        grads(0, p.me)
        load_gp.wait()
        fc_grads(0)
        proj.poll()
        g.relay_first()
        for i in range(1, steps):
            fc_grads(i)
            if i == 1:
                fc.poll()
        g.relay_rest()
        proj.poll()
        g.have(p.xs)
        work(p.xn)
        g.have(p.ys)
        work(p.yn)
        grads(1, p.xn)
        fc.poll()
        g.relay_corner()
        grads(2, p.yn)
        g.have(p.ds)
        work(p.dg)
        store = load(gm, gm_ref, local.at[8])
        grads(3, p.dg)
        store_dw = load(dw, dw_ref, local.at[9])
        g.finish()

        def keep_proj(where, value):
            proj_out[where, :] = value

        def keep_fc(where, value):
            fc_out[where] = value.astype(bf16)

        proj.finish(keep_proj)
        fc.finish(keep_fc)
        store.wait()
        store_dw.wait()
        for copy in stores[-2:]:
            copy.wait()

    return pl.pallas_call(
        kernel,
        out_shape=[
            jax.ShapeDtypeStruct((total, wide), bf16),
            jax.ShapeDtypeStruct((wide, depth), bf16),
            jax.ShapeDtypeStruct((depth - first_fc, hidden), bf16),
            jax.ShapeDtypeStruct(proj_shape, f32),
            jax.ShapeDtypeStruct(fc_shape, bf16),
        ],
        in_specs=[ANY] * 7,
        out_specs=[ANY] * 3 + [WHOLE] * 2,
        scratch_shapes=[
            pltpu.VMEM((total, depth), bf16),
            pltpu.VMEM(wo.shape, bf16),
            pltpu.VMEM(mixed.shape, bf16),
            pltpu.VMEM((total, wide), bf16),
            pltpu.VMEM((wide, depth), f32),
            pltpu.VMEM((wide, depth), bf16),
            pltpu.VMEM(grad_pre.shape, bf16),
            pltpu.VMEM((2, total, tile), bf16),
            pltpu.VMEM((2, tile, hidden), bf16),
        ]
        + Gather.scratch
        + LineSum.scratch(proj_shape, layers)
        + LineSum.scratch(fc_shape, layers)
        + [sems(10)],
        compiler_params=params(number),
        cost_estimate=cost(4 * total * depth * wide),
        name="gather_out",
    )(grad_attn, wo, mixed, hidden2, grad_pre, grad_proj, fc_part)


def scatter_attn(mixed, wo, tokens, b_out, gain, shift, piece, part, layers, number):
    piece, piece_first, piece_last = piece
    piece_shape = (piece_last - piece_first, *piece.shape[1:])
    part, part_first, part_last = part
    part_shape = (part_last - part_first, part.shape[1])
    total, depth = mixed.shape
    rows = total // PLANE
    wide = wo.shape[1]

    def kernel(a_ref, w_ref, piece_ref, part_ref, tok_ref, bias_ref, gain_ref, shift_ref, *refs):
        residual, hidden, mean_out, inverse_out, piece_all, part_all = refs[:6]
        a_buf, w_buf, piece_room, part_room = refs[6:10]
        s, line_refs, local = refs[10:24], refs[24:28], refs[28]
        p = Place()
        piece_ref = piece_ref.at[pl.ds(piece_first, piece_shape[0])]
        part_ref = part_ref.at[pl.ds(part_first, part_shape[0]), :]
        loads = [load(a_ref, a_buf, local.at[0]), load(w_ref, w_buf, local.at[1])]
        own = [
            Through(piece_ref, piece_room, piece_all.at[:, p.layer], local.at[2]),
            Through(part_ref, part_room, part_all.at[p.layer], local.at[3]),
        ]
        lines = [
            LineGather(p, piece_ref, lambda k: piece_all.at[:, k], layers, *line_refs[:2]),
            LineGather(p, part_ref, lambda k: part_all.at[k], layers, *line_refs[2:]),
        ]
        p.greet(False, layers)
        for line in lines:
            line.start()
        for copy in loads:
            copy.wait()

        def emit(line, value):
            values = tok_ref[line, :].astype(f32) + value + bias_ref[...]
            mean, inverse = norm_stats(values)
            residual[line, :] = values
            hidden[line, :] = (
                (values - mean) * inverse * gain_ref[...] + shift_ref[...]
            ).astype(bf16)
            mean_out[line, :] = mean
            inverse_out[line, :] = inverse

        def early():
            for copy in own:
                copy.put()
            lines[0].poll()

        def idle():
            lines[1].poll()
            lines[0].poll()
            lines[1].poll()

        Scatter.take(p, rows, s).run(plain_product(a_buf, w_buf), emit, idle, early)
        for line in lines:
            line.finish()
        for copy in own:
            copy.wait()

    return pl.pallas_call(
        kernel,
        out_shape=[
            jax.ShapeDtypeStruct((rows, wide), f32),
            jax.ShapeDtypeStruct((rows, wide), bf16),
            jax.ShapeDtypeStruct((rows, 1), f32),
            jax.ShapeDtypeStruct((rows, 1), f32),
            jax.ShapeDtypeStruct((piece_shape[0], layers, *piece_shape[1:]), bf16),
            jax.ShapeDtypeStruct((layers, *part_shape), bf16),
        ],
        in_specs=[ANY] * 4 + [WHOLE] * 4,
        out_specs=[WHOLE] * 4 + [ANY] * 2,
        scratch_shapes=[
            pltpu.VMEM(a, bf16) for a in (mixed.shape, wo.shape, piece_shape, part_shape)
        ]
        + Scatter.scratch(rows, wide)
        + LineGather.scratch(layers) * 2
        + [sems(4)],
        compiler_params=params(number),
        cost_estimate=cost(2 * total * depth * wide),
        name="scatter_attn",
    )(mixed, wo, piece, part, tokens, b_out, gain, shift)


def plain_product(a_buf, w_buf):
    half = w_buf.shape[1] // 2

    def product(role, here, c):
        return dot(a_buf[here, :], w_buf[:, pl.ds(c * half, half)])

    return product


def scatter_fc(cot_all, slope, wp, wf, hidden2, back, grad_proj, proj_cut, layers, number):
    total, depth = cot_all.shape
    rows = total // PLANE
    wide = slope.shape[1]
    tile = 512
    n_wp, n_wf = len(wp), len(wf)
    proj_shape = (proj_cut, grad_proj.shape[2])

    def kernel(cot_ref, slope_ref, h_ref, proj_ref, *refs):
        wp_refs, wf_refs, refs = refs[:n_wp], refs[n_wp : n_wp + n_wf], refs[n_wp + n_wf :]
        cot_own, residual_ref, mean_ref, inverse_ref, gain_ref = refs[:5]
        grad_residual, grad_attn, sums_ref, bias_ref, gp_ref, dw_ref, proj_out = refs[5:12]
        cot, slopes, wp_buf, wf_buf, gp, h_buf, dw_buf, folds = refs[12:20]
        s, line_refs = refs[20:34], refs[34:42]
        local, wlocal = refs[42:]
        p = Place()
        proj = LineSum(p, lambda f: proj_ref.at[f, pl.ds(0, proj_cut), :], layers, *line_refs)
        order = (p.dg, p.xn, p.yn, p.me)

        def chip(dev):
            return rows_at(lax.div(dev, 2) * (2 * rows), 2 * rows)

        def fetch(k):
            here = chip(order[k])
            return (
                load(cot_ref.at[here, :], cot.at[k % 2], local.at[k % 2]),
                load(slope_ref.at[here, :], slopes.at[k % 2], local.at[2 + k % 2]),
            )

        fetches = [fetch(0)]
        loads_wp = load_blocks(wp_refs, wp_buf, wlocal)
        loads_wf = load_parts(wf_refs, wf_buf, local.at[pl.ds(4, n_wf)])
        load_h = load(h_ref.at[:, pl.ds(0, tile)], h_buf, local.at[4 + n_wf])
        bias_ref[...] = jnp.zeros_like(bias_ref)
        p.greet(False, layers)
        proj.start()
        for copy in loads_wp:
            copy.wait()
        half = depth // 2

        def back_through_gelu(k):
            for copy in fetches[k]:
                copy.wait()
            if k < 3:
                fetches.append(fetch(k + 1))
            here = chip(order[k])

            @pl.loop(0, wide // 512)
            def _(j):
                cols = rows_at(j * 512, 512)
                grad_act = dot_nt(cot[k % 2], wp_buf[cols, :])
                grad_pre = (grad_act * slopes[k % 2, :, cols].astype(f32)).astype(bf16)
                gp[here, cols] = grad_pre
                bias_ref[:, cols] += jnp.sum(grad_pre.astype(f32), axis=0, keepdims=True)

            if k == 0:
                for copy in loads_wf:
                    copy.wait()

        def product(role, here, c):
            if c == 0:
                back_through_gelu(role)
            return dot_nt(gp[here, :], wf_buf[pl.ds(c * half, half), :])

        def emit(line, value):
            first = line.start == 0
            grad_out = cot_own[line, :].astype(f32)
            back = inverse_ref[line, :]
            normed = (residual_ref[line, :] - mean_ref[line, :]) * back
            result = grad_out + norm_back(value, normed, back, gain_ref[...])
            low = result.astype(bf16)
            grad_residual[line, :] = result
            grad_attn[line, :] = low
            for i, term in enumerate((value * normed, value, low.astype(f32), grad_out)):
                fold(folds.at[i], first, term)

        stores = []

        def early():
            stores.append(load(gp, gp_ref, local.at[5 + n_wf]))
            proj.poll()

        def idle():
            load_h.wait()
            dw_buf[...] = dot_tn(h_buf[...], gp[...]).astype(bf16)
            stores.append(load(dw_buf, dw_ref, local.at[6 + n_wf]))
            proj.poll()

        def keep(where, value):
            proj_out[where, :] = value.astype(bf16)

        Scatter.take(p, rows, s).run(product, emit, idle, early)
        sums_ref[...] = jnp.sum(folds[...], axis=1)
        proj.finish(keep)
        for copy in stores:
            copy.wait()

    return pl.pallas_call(
        kernel,
        out_shape=[
            jax.ShapeDtypeStruct((rows, depth), f32),
            jax.ShapeDtypeStruct((rows, depth), bf16),
            jax.ShapeDtypeStruct((4, depth), f32),
            jax.ShapeDtypeStruct((1, wide), f32),
            jax.ShapeDtypeStruct((total, wide), bf16),
            jax.ShapeDtypeStruct((tile, wide), bf16),
            jax.ShapeDtypeStruct(proj_shape, bf16),
        ],
        in_specs=[ANY] * (4 + n_wp + n_wf) + [WHOLE] * 5,
        out_specs=[WHOLE] * 4 + [ANY] * 2 + [WHOLE],
        scratch_shapes=[
            pltpu.VMEM((2, 2 * rows, depth), bf16),
            pltpu.VMEM((2, 2 * rows, wide), bf16),
            pltpu.VMEM((wide, depth), bf16),
            pltpu.VMEM((depth, wide), bf16),
            pltpu.VMEM((total, wide), bf16),
            pltpu.VMEM((total, tile), bf16),
            pltpu.VMEM((tile, wide), bf16),
            pltpu.VMEM((4, 8, depth), f32),
        ]
        + Scatter.scratch(rows, depth)
        + LineSum.scratch(proj_shape, layers)
        + [sems(7 + n_wf), sems(n_wp * layers)],
        compiler_params=params(number),
        cost_estimate=cost(6 * total * depth * wide),
        name="scatter_fc",
    )(cot_all, slope, hidden2, grad_proj, *wp, *wf, *back)


def scatter_query(gq, gkv, wq, w_kv, grad_w_query, grad_w_kv, fc_part, back, layers, number):
    total, cols = gq.shape
    kv_cols = gkv.shape[1]
    rows = total // PLANE
    depth = wq.shape[0]
    wide = depth + kv_cols
    q_shape = (grad_w_query.shape[0], *grad_w_query.shape[2:])
    fc_part, first, last = fc_part
    fc_shape = (last - first, *fc_part.shape[2:])

    def kernel(gq_ref, gkv_ref, wq_ref, wkv_ref, dwq_ref, dwkv_ref, fc_ref, *refs):
        tok_ref, mean_ref, inverse_ref, gain_ref, residual_ref = refs[:5]
        out_ref, sums_ref, dwkv_out, fc_out, dwq_out = refs[5:10]
        g_buf, wq_buf, wkv_buf, dwkv_buf, q_sum, folds = refs[10:16]
        s, line_refs = refs[16:30], refs[30:46]
        qsend, qrecv, local = refs[46:]
        p = Place()
        q_side, kv_side = pl.ds(0, cols), pl.ds(cols, kv_cols)
        loads = [
            load(gq_ref, g_buf.at[:, q_side], local.at[0]),
            load(gkv_ref, g_buf.at[:, kv_side], local.at[1]),
            load(wq_ref, wq_buf, local.at[2]),
            load(wkv_ref, wkv_buf, local.at[3]),
            load(dwkv_ref, dwkv_buf, local.at[4]),
        ]
        line_q = LineSum(p, lambda f: dwq_ref.at[:, f], layers, *line_refs[:8])
        line_fc = LineSum(p, lambda f: fc_ref.at[pl.ds(first, last - first), f], layers, *line_refs[8:])
        p.greet(True, layers)
        line_q.start()
        line_fc.start()
        for copy in loads:
            copy.wait()
        half = wide // 2

        def product(role, here, c):
            where = pl.ds(c * half, min(half, depth - c * half))
            value = dot_nt(g_buf[here, q_side], wq_buf[where, :]) + dot_nt(
                g_buf[here, kv_side], wkv_buf[where, :]
            )
            if c == 0:
                return value
            return jnp.concatenate([value, dwkv_buf[here, :].astype(f32)], axis=1)

        later = []

        def early():
            line_q.poll()

        def idle():
            line_fc.poll()
            line_q.poll()

            def keep(where, value):
                q_sum[where] = value.astype(bf16)

            line_fc.poll()
            line_q.finish(keep)
            later.append(Spread(p, q_sum, dwq_out, qsend, qrecv, local.at[5]))

        def emit(line, value):
            begin = line.start == 0
            grad = value[:, :depth]
            normed = (tok_ref[line, :].astype(f32) - mean_ref[line, :]) * inverse_ref[line, :]
            out_ref[line, :] = residual_ref[line, :] + norm_back(
                grad, normed, inverse_ref[line, :], gain_ref[...]
            )
            fold(folds.at[0], begin, grad * normed)
            fold(folds.at[1], begin, grad)
            dwkv_out[line, :] = value[:, depth:].astype(bf16)

        def keep_fc(where, value):
            fc_out[where] = value.astype(bf16)

        Scatter.take(p, rows, s).run(product, emit, idle, early)
        sums_ref[...] = jnp.sum(folds[...], axis=1)
        line_fc.finish(keep_fc)
        for item in later:
            item.finish()

    return pl.pallas_call(
        kernel,
        out_shape=[
            jax.ShapeDtypeStruct((rows, depth), f32),
            jax.ShapeDtypeStruct((2, depth), f32),
            jax.ShapeDtypeStruct((rows, kv_cols), bf16),
            jax.ShapeDtypeStruct(fc_shape, bf16),
            jax.ShapeDtypeStruct((q_shape[1], PLANE * q_shape[2]), bf16),
        ],
        in_specs=[ANY] * 7 + [WHOLE] * 5,
        out_specs=[WHOLE] * 4 + [ANY],
        scratch_shapes=[
            pltpu.VMEM((total, cols + kv_cols), bf16),
            pltpu.VMEM(wq.shape, bf16),
            pltpu.VMEM(w_kv.shape, bf16),
            pltpu.VMEM(grad_w_kv.shape, bf16),
            pltpu.VMEM(q_shape, bf16),
            pltpu.VMEM((2, 8, depth), f32),
        ]
        + Scatter.scratch(rows, wide)
        + LineSum.scratch(q_shape, layers)
        + LineSum.scratch(fc_shape, layers)
        + [sems(PLANE)] * 2
        + [sems(6)],
        compiler_params=params(number),
        cost_estimate=cost(2 * total * depth * (cols + kv_cols)),
        name="scatter_query",
    )(gq, gkv, wq, w_kv, grad_w_query, grad_w_kv, fc_part, *back)


def last_exchange(vector, grad_w_kv, fc_parts, layers, number):
    lines = vector.shape[1]
    kv_rows, kv_cols = grad_w_kv.shape[0] // layers, grad_w_kv.shape[1]
    count = len(fc_parts)
    sizes = [a.shape[0] for a in fc_parts]
    fc_rows, fc_cols = fc_parts[0].shape[1:]

    def kernel(vec, kv_ref, *refs):
        fc_refs, (vec_out, kv_out, fc_out), refs = (
            refs[:count],
            refs[count : count + 3],
            refs[count + 3 :],
        )
        pieces, box, plane_sum, zbox, kv_box = refs[:5]
        vsend, vrecv, zsend, zrecv, ksend, krecv, gsend, grecv, send, recv, local = refs[5:]
        p = Place()
        loads, at = [], 0
        for i, ref in enumerate(fc_refs):
            loads.append(load(ref, pieces.at[pl.ds(at, sizes[i])], local.at[i]))
            at += sizes[i]
        p.greet(True, layers)
        plane = PlaneSum(p, vec, box, vsend, vrecv)
        across_kv = []
        for step in range(1, layers):
            to = p.line_peer(step, layers)
            block = kv_ref.at[rows_at(to * kv_rows, kv_rows), :]
            copy = push(block, kv_box.at[step], ksend.at[step], krecv.at[step], {"fsdp": to})
            copy.start()
            across_kv.append(copy)
        for copy in loads:
            copy.wait()
        spread = Spread(p, pieces, fc_out, send, recv, local.at[count])
        total = plane.total()
        plane_sum[...] = total
        zbox[0] = total
        across = []
        for step in range(1, layers):
            to = p.line_peer(step, layers)
            copy = push(plane_sum, zbox.at[step], zsend.at[step], zrecv.at[step], {"fsdp": to})
            copy.start()
            across.append(copy)
        value = kv_ref[rows_at(p.layer * kv_rows, kv_rows), :].astype(f32)
        for step, copy in enumerate(across_kv):
            copy.wait_recv()
            value = value + kv_box[step + 1].astype(f32)
        kv_out[...] = value
        for copy in across:
            copy.wait_recv()
        total = None
        for k in range(layers):
            term = zbox[lax.rem(p.layer - k + layers, layers)]
            total = term if total is None else total + term
        vec_out[p.me] = total
        last = []
        for step in range(1, PLANE):
            to = p.plane_peer(step)
            mine = vec_out.at[p.me]
            last.append(push(mine, mine, gsend.at[step], grecv.at[step], {"seq": to}))
            last[-1].start()
        for copy in last:
            copy.wait()
        spread.finish()
        plane.finish()
        for copy in across + across_kv:
            copy.wait_send()

    return pl.pallas_call(
        kernel,
        out_shape=[
            jax.ShapeDtypeStruct(vector.shape, f32),
            jax.ShapeDtypeStruct((kv_rows, kv_cols), f32),
            jax.ShapeDtypeStruct((fc_rows, PLANE * fc_cols), bf16),
        ],
        in_specs=[WHOLE, WHOLE] + [ANY] * count,
        out_specs=[WHOLE, WHOLE, ANY],
        scratch_shapes=[
            pltpu.VMEM((PLANE, fc_rows, fc_cols), bf16),
            pltpu.VMEM((PLANE, lines, 128), f32),
            pltpu.VMEM((lines, 128), f32),
            pltpu.VMEM((layers, lines, 128), f32),
            pltpu.VMEM((layers, kv_rows, kv_cols), bf16),
        ]
        + [sems(PLANE)] * 2
        + [sems(layers)] * 4
        + [sems(PLANE)] * 4
        + [sems(count + 1)],
        compiler_params=params(number),
        name="last_exchange",
    )(vector, grad_w_kv, *fc_parts)


def starts_of(docs, stream, positions):
    start = jnp.zeros_like(positions)
    for j in range(docs.shape[1]):
        here = docs[stream, j]
        start = jnp.maximum(start, jnp.where(here <= positions, here, 0))
    return start


def masked_scores(docs, stream, keys, q, first, limit):
    scores = dot_nt(keys, q) * (HD**-0.5)
    t = first + lax.broadcasted_iota(jnp.int32, (1, q.shape[0]), 1)
    u = lax.broadcasted_iota(jnp.int32, scores.shape, 0)
    return scores, (u >= starts_of(docs, stream, t)) & (u <= t)


QROWS = 256


def attend_stream(docs, stream, q_ref, kv_ref, mixed_ref, lse_ref, block, heads):
    groups, rows, cols = q_ref.shape
    length = groups * rows
    kv = kv_ref[...].reshape(length, 2 * HD)
    keys = kv[:, :HD]
    values_t = kv[:, HD:].T
    per = block // rows
    for b in range(length // block):
        limit = (b + 1) * block
        q_rows = q_ref[b * per : (b + 1) * per].reshape(block, cols)
        for h in range(heads):
            q = q_rows[:, h * HD : (h + 1) * HD]
            scores, allowed = masked_scores(docs, stream, keys[:limit], q, b * block, limit)
            scores = jnp.where(allowed, scores, -1e30)
            top = jnp.max(scores, axis=0, keepdims=True)
            weights = jnp.exp(scores - top)
            total = jnp.sum(weights, axis=0, keepdims=True)
            mixed = dot(values_t[:, :limit], weights.astype(bf16)) / total
            mixed_ref[b * per : (b + 1) * per, :, h * HD : (h + 1) * HD] = (
                mixed.T.astype(bf16).reshape(per, rows, HD)
            )
            lse_ref[h : h + 1, b * block : (b + 1) * block] = top + jnp.log(total)


def attend_stream_back(docs, stream, q_ref, kv_ref, g_ref, lse_ref, gq_ref, gkv_ref, gk, gv, heads):
    groups, rows, cols = q_ref.shape
    length = groups * rows
    block = min(QROWS, length)
    kv = kv_ref[...].reshape(length, 2 * HD)
    keys, values = kv[:, :HD], kv[:, HD:]
    keys_t = keys.T
    per = block // rows
    gk[...] = jnp.zeros_like(gk)
    gv[...] = jnp.zeros_like(gv)
    for b in range(length // block):
        limit = (b + 1) * block
        q_rows = q_ref[b * per : (b + 1) * per].reshape(block, cols)
        g_rows = g_ref[b * per : (b + 1) * per].reshape(block, cols)
        for h in range(heads):
            q = q_rows[:, h * HD : (h + 1) * HD]
            g = g_rows[:, h * HD : (h + 1) * HD]
            scores, allowed = masked_scores(docs, stream, keys[:limit], q, b * block, limit)
            shift = lse_ref[h : h + 1, b * block : (b + 1) * block]
            probs = jnp.where(allowed, jnp.exp(scores - shift), 0.0)
            grad_probs = dot_nt(values[:limit], g)
            weighted = probs * grad_probs
            delta = jnp.sum(weighted, axis=0, keepdims=True)
            grad_scores = (weighted - probs * delta).astype(bf16)
            gq = dot(keys_t[:, :limit], grad_scores) * (HD**-0.5)
            gq_ref[b * per : (b + 1) * per, :, h * HD : (h + 1) * HD] = (
                gq.T.astype(bf16).reshape(per, rows, HD)
            )
            gk[:limit, :] += dot(grad_scores, q)
            gv[:limit, :] += dot(probs.astype(bf16), g)
    gkv_ref[:, :, :HD] = (gk[...] * (HD**-0.5)).astype(bf16).reshape(groups, rows, HD)
    gkv_ref[:, :, HD:] = gv[...].astype(bf16).reshape(groups, rows, HD)


def attend_back_scatter_proj(
    docs, queries, keyval, grads, lse, act, wp, hidden1, out_part, fc_part, residual, b_proj,
    layers, heads, number
):
    groups, streams, rows, cols = queries.shape
    kv_cols = keyval.shape[3]
    length = groups * rows
    total, depth = act.shape
    own = total // PLANE
    wide = hidden1.shape[1]
    part = hidden1.shape[1] // PLANE
    n_wp = len(wp)
    out_shape = out_part.shape[1:]
    fc_part, first, last = fc_part
    fc_shape = (last - first, *fc_part.shape[2:])

    def kernel(docs_ref, q_ref, kv_ref, g_ref, lse_ref, act_ref, h_ref, dwo_ref, fc_ref, *refs):
        wp_refs, refs = refs[:n_wp], refs[n_wp:]
        residual_ref, bias_ref = refs[:2]
        gq_out, gkv_out, gq_sum, gkv_sum, dwq_out, dwkv_out = refs[2:8]
        out_ref, dwo_out, fc_out = refs[8:11]
        a_buf, w_buf, q_buf, kv_buf, g_buf, grad_buf, gk, gv, h_buf = refs[11:20]
        dwq_buf, dwkv_buf = refs[20:22]
        s, line_refs = refs[22:36], refs[36:52]
        local, wlocal = refs[52:]
        p = Place()
        loads = [load(act_ref, a_buf, local.at[0]), *load_blocks(wp_refs, w_buf, wlocal)]
        line_o = LineSum(p, lambda f: dwo_ref.at[f], layers, *line_refs[:8])
        line_fc = LineSum(p, lambda f: fc_ref.at[pl.ds(first, last - first), f], layers, *line_refs[8:])
        ins = [
            load(q_ref, q_buf, local.at[2]),
            load(kv_ref, kv_buf, local.at[3]),
            load(g_ref, g_buf, local.at[4]),
        ]

        def h_fetch(i):
            here = pl.ds(2 * i * part, 2 * part)
            return load(h_ref.at[:, here], h_buf.at[i % 2], local.at[5 + i % 2])

        tiles = [h_fetch(0)]
        p.greet(False, layers)
        line_o.start()
        line_fc.start()
        for copy in loads:
            copy.wait()
        stores = []

        def early():
            line_o.poll()

        def idle():
            line_fc.poll()
            for copy in ins:
                copy.wait()
            for stream in range(streams):
                if stream:
                    line_o.poll()
                attend_stream_back(
                    docs_ref,
                    stream,
                    q_buf.at[:, stream],
                    kv_buf.at[:, stream],
                    g_buf.at[:, stream],
                    lse_ref.at[stream],
                    grad_buf.at[:, stream, :, pl.ds(0, cols)],
                    grad_buf.at[:, stream, :, pl.ds(cols, kv_cols)],
                    gk,
                    gv,
                    heads,
                )
            stores.append(load(grad_buf.at[:, :, :, pl.ds(0, cols)], gq_out, local.at[7]))
            stores.append(load(grad_buf.at[:, :, :, pl.ds(cols, kv_cols)], gkv_out, local.at[8]))
            line_fc.poll()
            grad = grad_buf[...].reshape(total, cols + kv_cols)
            sums = jnp.sum(grad.astype(f32), axis=0, keepdims=True)
            gq_sum[...] = sums[:, :cols]
            gkv_sum[...] = sums[:, cols:]
            for i in range(PLANE // 2):
                tiles[i].wait()
                if i + 1 < PLANE // 2:
                    tiles.append(h_fetch(i + 1))
                term = dot_tn(h_buf[i % 2], grad).astype(bf16)
                for k in range(2):
                    lines = term[k * part : (k + 1) * part]
                    dwq_buf[2 * i + k] = lines[:, :cols].reshape(layers, part // layers, cols)
                    dwkv_buf[2 * i + k] = lines[:, cols:]
            stores.append(load(dwq_buf, dwq_out, local.at[9]))
            stores.append(load(dwkv_buf, dwkv_out, local.at[10]))

        def emit(line, value):
            out_ref[line, :] = residual_ref[line, :] + value + bias_ref[...]

        def keep_out(where, value):
            dwo_out[where, :] = value

        def keep_fc(where, value):
            fc_out[where] = value.astype(bf16)

        Scatter.take(p, own, s).run(plain_product(a_buf, w_buf), emit, idle, early)
        line_o.finish(keep_out)
        line_fc.finish(keep_fc)
        for copy in stores:
            copy.wait()

    return pl.pallas_call(
        kernel,
        out_shape=[
            jax.ShapeDtypeStruct(queries.shape, bf16),
            jax.ShapeDtypeStruct(keyval.shape, bf16),
            jax.ShapeDtypeStruct((1, cols), f32),
            jax.ShapeDtypeStruct((1, kv_cols), f32),
            jax.ShapeDtypeStruct((PLANE, layers, part // layers, cols), bf16),
            jax.ShapeDtypeStruct((PLANE, part, kv_cols), bf16),
            jax.ShapeDtypeStruct((own, wide), f32),
            jax.ShapeDtypeStruct(out_shape, f32),
            jax.ShapeDtypeStruct(fc_shape, bf16),
        ],
        in_specs=[pl.BlockSpec(memory_space=pltpu.SMEM)]
        + [ANY] * 3
        + [WHOLE]
        + [ANY] * (4 + n_wp)
        + [WHOLE] * 2,
        out_specs=[ANY, ANY, WHOLE, WHOLE, ANY, ANY] + [WHOLE] * 3,
        scratch_shapes=[
            pltpu.VMEM(act.shape, bf16),
            pltpu.VMEM((depth, wide), bf16),
            pltpu.VMEM(queries.shape, bf16),
            pltpu.VMEM(keyval.shape, bf16),
            pltpu.VMEM(grads.shape, bf16),
            pltpu.VMEM((groups, streams, rows, cols + kv_cols), bf16),
            pltpu.VMEM((length, HD), f32),
            pltpu.VMEM((length, HD), f32),
            pltpu.VMEM((2, total, 2 * part), bf16),
            pltpu.VMEM((PLANE, layers, part // layers, cols), bf16),
            pltpu.VMEM((PLANE, part, kv_cols), bf16),
        ]
        + Scatter.scratch(own, wide)
        + LineSum.scratch(out_shape, layers)
        + LineSum.scratch(fc_shape, layers)
        + [sems(11), sems(n_wp * layers)],
        compiler_params=params(number),
        cost_estimate=cost(2 * total * depth * wide),
        name="attend_back_scatter_proj",
    )(docs, queries, keyval, grads, lse, act, hidden1, out_part, fc_part, *wp, residual, b_proj)


def pack_vectors(vectors):
    sizes = [v.shape[0] for v in vectors]
    lines = -(-sum(sizes) // (PLANE * 8 * 128)) * 8
    pad = PLANE * lines * 128 - sum(sizes)
    return jnp.concatenate(vectors + (jnp.zeros((pad,), f32),)).reshape(PLANE, lines, 128)


def unpack_vectors(packed, vectors):
    flat = packed.reshape(-1)
    sums, at = [], 0
    for v in vectors:
        sums.append(flat[at : at + v.shape[0]])
        at += v.shape[0]
    return sums


def shards(
    tokens,
    doc_starts,
    w_query,
    w_kv,
    w_out,
    w_fc,
    w_proj,
    ln1_gain,
    ln1_bias,
    b_query,
    b_value,
    b_out,
    ln2_gain,
    ln2_bias,
    b_fc,
    b_proj,
    cotangent,
):
    layers = lax.axis_size("fsdp")
    me = lax.axis_index("seq")
    streams, rows, width = tokens.shape
    own = streams * rows
    heads = HEADS // PLANE
    hidden = b_fc.shape[0]
    my_cols = heads * HD
    my_hidden = hidden // PLANE
    total = PLANE * own

    own_tokens = tokens.reshape(own, width)
    cot_low = cotangent.reshape(own, width)

    def row(vector):
        return vector.reshape(1, -1)

    wq_pieces, wf_pieces, low_kv, wo, low_hidden1, mean1, inverse1 = split_weights(
        own_tokens, row(ln1_gain), row(ln1_bias), w_query, w_fc, w_kv, w_out, layers, 1
    )
    proj_rows = w_proj.shape[0]
    wp_half, proj_cut = proj_rows // 2, proj_rows * 5 // 8
    my_bq = row(lax.dynamic_slice_in_dim(b_query, me * my_cols, my_cols, 0))
    my_bf = row(lax.dynamic_slice_in_dim(b_fc, me * my_hidden, my_hidden, 0))
    bkv = row(jnp.concatenate([jnp.zeros((HD,), f32), b_value]))

    def rows_together(pieces):
        return pieces.reshape(-1, pieces.shape[-1])

    hidden1, w_kv_all, wq, wf_a = gather_hidden1(
        low_hidden1, low_kv, ((wq_pieces, 0, PLANE), (wf_pieces, 0, 3)), layers, 2
    )
    wq = rows_together(wq)
    cot_all, wf_b, queries, keyval, mixed, lse = project_attend(
        doc_starts, hidden1, wq, w_kv_all, my_bq, bkv, cot_low, (wf_pieces, 3, 7), streams, heads,
        layers, 3
    )
    mixed_rows = mixed.reshape(total, my_cols)
    residual, low_hidden2, mean2, inverse2, wf_c, wp_a = scatter_attn(
        mixed_rows,
        wo,
        own_tokens,
        row(b_out),
        row(ln2_gain),
        row(ln2_bias),
        (wf_pieces, 7, PLANE),
        (w_proj, 0, wp_half),
        layers,
        4,
    )
    wf = [rows_together(w) for w in (wf_a, wf_b, wf_c)]
    hidden2, act_low, slope, grad_w_proj, wp_b = gather_fc(
        low_hidden2, wf, my_bf, cot_all, (w_proj, wp_half, proj_rows), layers, 5
    )
    wp = (wp_a, wp_b)
    grad_w_proj = grad_w_proj.reshape(layers, proj_rows, width)
    grad_residual, grad_attn, sums2, my_grad_b_fc, grad_pre, grad_fc_a, shard_proj_a = scatter_fc(
        cot_all,
        slope,
        wp,
        wf,
        hidden2,
        (cot_low, residual, mean2, inverse2, row(ln2_gain)),
        grad_w_proj,
        proj_cut,
        layers,
        6,
    )

    def by_layer(grad):
        return grad.reshape(-1, layers, width // PLANE // layers, my_hidden)

    first_fc = grad_fc_a.shape[0]
    grad_mixed, grad_w_out, grad_fc_rest, shard_proj_b, fc_a = gather_out(
        grad_attn,
        wo,
        mixed_rows,
        hidden2,
        grad_pre,
        first_fc,
        grad_w_proj,
        proj_cut,
        by_layer(grad_fc_a),
        layers,
        7,
    )
    grad_fc_rest = by_layer(grad_fc_rest)
    fc_cut = grad_fc_rest.shape[0] // 2
    (
        gq,
        gkv,
        my_grad_b_query,
        sums_kv,
        grad_w_query,
        grad_w_kv,
        output,
        shard_out,
        fc_b,
    ) = attend_back_scatter_proj(
        doc_starts,
        queries,
        keyval,
        grad_mixed.reshape(PLANE, streams, rows, my_cols),
        lse,
        act_low,
        wp,
        hidden1,
        grad_w_out.reshape(layers, -1, width),
        (grad_fc_rest, 0, fc_cut),
        residual,
        row(b_proj),
        layers,
        heads,
        8,
    )
    input_grad, sums1, plane_kv, fc_c, shard_query = scatter_query(
        gq.reshape(total, my_cols),
        gkv.reshape(total, 2 * HD),
        wq,
        w_kv_all,
        grad_w_query,
        grad_w_kv.reshape(width, 2 * HD),
        (grad_fc_rest, fc_cut, grad_fc_rest.shape[0]),
        (own_tokens, mean1, inverse1, row(ln1_gain), grad_residual),
        layers,
        9,
    )
    shard_proj = jnp.concatenate([shard_proj_a.astype(f32), shard_proj_b])

    zero = jnp.zeros_like
    grad_b_query = lax.dynamic_update_slice_in_dim(
        zero(b_query), my_grad_b_query.reshape(-1), me * my_cols, 0
    )
    grad_b_fc = lax.dynamic_update_slice_in_dim(
        zero(b_fc), my_grad_b_fc.reshape(-1), me * my_hidden, 0
    )
    vectors = (
        sums1[0],
        sums1[1],
        grad_b_query,
        sums_kv[0, HD:],
        sums2[2],
        sums2[0],
        sums2[1],
        grad_b_fc,
        sums2[3],
    )
    packed, shard_kv, shard_fc = last_exchange(
        pack_vectors(vectors), plane_kv, (fc_a, fc_b, fc_c), layers, 10
    )
    sums = unpack_vectors(packed, vectors)
    return (
        output.reshape(streams, rows, width),
        input_grad.reshape(streams, rows, width),
        shard_query.astype(f32),
        shard_kv,
        shard_out,
        shard_fc.astype(f32),
        shard_proj,
        *sums,
    )


def gather_seq(block):
    return lax.all_gather(block, "seq", axis=0, tiled=True)


def scatter_seq(partial):
    return lax.psum_scatter(partial.astype(bf16), "seq", scatter_dimension=0, tiled=True).astype(f32)


def columns_to_rows(part, groups):
    rows = part.shape[0]
    spread = part.reshape(rows, groups, part.shape[1] // groups).transpose(1, 0, 2)
    return lax.all_to_all(spread, "seq", split_axis=0, concat_axis=0, tiled=True)


def column_weight(shard, groups):
    pieces = columns_to_rows(shard, groups)
    full = lax.all_gather(pieces, "fsdp", axis=1, tiled=True)
    return full.reshape(-1, full.shape[2])


def plain_column_grad(grad, groups):
    rows, cols = grad.shape
    kept = lax.psum_scatter(
        grad.astype(bf16).reshape(groups, rows // groups, cols), "fsdp", scatter_dimension=1, tiled=True
    )
    moved = lax.all_to_all(kept, "seq", split_axis=0, concat_axis=0, tiled=True)
    return moved.transpose(1, 0, 2).reshape(moved.shape[1], groups * cols).astype(f32)


def row_weight_grad(grad):
    return lax.psum_scatter(grad.astype(bf16), "fsdp", scatter_dimension=0, tiled=True).astype(f32)


def plain_attend(queries, keyval, starts, groups, streams, rows, heads):
    length = groups * rows
    scale = HD ** (-0.5)
    position = jnp.arange(length, dtype=jnp.int32)
    mixed_list, lse_list = [], []
    for stream in range(streams):
        q = queries[:, stream].reshape(length, heads, HD)
        k = keyval[:, stream, :, :HD].reshape(length, HD)
        v = keyval[:, stream, :, HD:].reshape(length, HD)
        segment = jnp.sum((starts[stream][None, :] <= position[:, None]).astype(jnp.int32), axis=1)
        allowed = (position[None, :] <= position[:, None]) & (segment[None, :] == segment[:, None])
        scores = jnp.einsum("thd,ud->htu", q, k, preferred_element_type=f32) * scale
        scores = jnp.where(allowed[None], scores, -1e30)
        top = jnp.max(scores, axis=-1, keepdims=True)
        lse = top + jnp.log(jnp.sum(jnp.exp(scores - top), axis=-1, keepdims=True))
        probs = jnp.exp(scores - lse).astype(bf16)
        mixed = jnp.einsum("htu,ud->thd", probs, v, preferred_element_type=f32)
        mixed_list.append(mixed.astype(bf16).reshape(groups, rows, heads * HD))
        lse_list.append(lse)
    return jnp.stack(mixed_list, axis=1), lse_list


def plain_attend_back(queries, keyval, grads, lse_list, starts, groups, streams, rows, heads):
    length = groups * rows
    scale = HD ** (-0.5)
    position = jnp.arange(length, dtype=jnp.int32)
    gq_list, gkv_list = [], []
    for stream in range(streams):
        q = queries[:, stream].reshape(length, heads, HD)
        g = grads[:, stream].reshape(length, heads, HD)
        k = keyval[:, stream, :, :HD].reshape(length, HD)
        v = keyval[:, stream, :, HD:].reshape(length, HD)
        segment = jnp.sum((starts[stream][None, :] <= position[:, None]).astype(jnp.int32), axis=1)
        allowed = (position[None, :] <= position[:, None]) & (segment[None, :] == segment[:, None])
        scores = jnp.einsum("thd,ud->htu", q, k, preferred_element_type=f32) * scale
        probs = jnp.exp(jnp.where(allowed[None], scores, -1e30) - lse_list[stream])
        grad_probs = jnp.einsum("thd,ud->htu", g, v, preferred_element_type=f32)
        delta = jnp.sum(probs * grad_probs, axis=-1, keepdims=True)
        gs = (probs * (grad_probs - delta)).astype(bf16)
        gq = jnp.einsum("htu,ud->thd", gs, k, preferred_element_type=f32) * scale
        gk = jnp.einsum("htu,thd->ud", gs, q, preferred_element_type=f32) * scale
        gv = jnp.einsum("htu,thd->ud", probs.astype(bf16), g, preferred_element_type=f32)
        gq_list.append(gq.astype(bf16).reshape(groups, rows, heads * HD))
        gkv_list.append(jnp.concatenate([gk, gv], axis=1).reshape(groups, rows, 2 * HD))
    return jnp.stack(gq_list, axis=1), jnp.stack(gkv_list, axis=1)


def plain_shards(
    tokens,
    doc_starts,
    w_query,
    w_kv,
    w_out,
    w_fc,
    w_proj,
    ln1_gain,
    ln1_bias,
    b_query,
    b_value,
    b_out,
    ln2_gain,
    ln2_bias,
    b_fc,
    b_proj,
    cotangent,
):
    groups = lax.axis_size("seq")
    me = lax.axis_index("seq")
    streams, rows, width = tokens.shape
    own = streams * rows
    heads = HEADS // groups
    hidden = b_fc.shape[0]
    my_cols = heads * HD
    my_hidden = hidden // groups

    wq = column_weight(w_query, groups)
    w_kv_all = gather_seq(lax.all_gather(w_kv, "fsdp", axis=0, tiled=True))
    wo = lax.all_gather(w_out, "fsdp", axis=0, tiled=True)
    wf = column_weight(w_fc, groups)
    wp = lax.all_gather(w_proj, "fsdp", axis=0, tiled=True)
    my_bq = lax.dynamic_slice_in_dim(b_query, me * my_cols, my_cols, 0)
    my_bf = lax.dynamic_slice_in_dim(b_fc, me * my_hidden, my_hidden, 0)

    inputs = tokens.reshape(own, width).astype(f32)
    cot_low = cotangent.reshape(own, width)
    cot_full = cot_low.astype(f32)
    shifted1, normed1, inverse1 = normalize(inputs, ln1_gain, ln1_bias)
    hidden1 = gather_seq(shifted1.astype(bf16))
    queries = (dot(hidden1, wq) + my_bq).astype(bf16).reshape(groups, streams, rows, my_cols)
    value_shift = jnp.concatenate([jnp.zeros((HD,), f32), b_value])
    keyval = (dot(hidden1, w_kv_all) + value_shift).astype(bf16).reshape(groups, streams, rows, 2 * HD)
    mixed, lse = plain_attend(queries, keyval, doc_starts, groups, streams, rows, heads)
    mixed_rows = mixed.reshape(groups * own, my_cols)
    residual = inputs + scatter_seq(dot(mixed_rows, wo)) + b_out
    shifted2, normed2, inverse2 = normalize(residual, ln2_gain, ln2_bias)
    hidden2 = gather_seq(shifted2.astype(bf16))
    cot_all = gather_seq(cot_low)
    pre_act = dot(hidden2, wf) + my_bf
    activated, slope = gelu_pair(pre_act)
    act_low = activated.astype(bf16)
    output = residual + scatter_seq(dot(act_low, wp)) + b_proj

    grad_b_proj = jnp.sum(cot_full, axis=0)
    shard_proj = row_weight_grad(dot_tn(act_low, cot_all))
    grad_pre = (dot_nt(cot_all, wp) * slope).astype(bf16)
    my_grad_b_fc = jnp.sum(grad_pre.astype(f32), axis=0)
    shard_fc = plain_column_grad(dot_tn(hidden2, grad_pre), groups)
    grad_hidden2 = scatter_seq(dot_nt(grad_pre, wf))
    back_second, grad_ln2_gain, grad_ln2_bias = normalize_back(
        grad_hidden2, normed2, inverse2, ln2_gain
    )
    grad_residual = cot_full + back_second
    grad_attn = grad_residual.astype(bf16)
    grad_b_out = jnp.sum(grad_attn.astype(f32), axis=0)
    grad_attn_all = gather_seq(grad_attn)
    shard_out = row_weight_grad(dot_tn(mixed_rows, grad_attn_all))
    grad_mixed = dot_nt(grad_attn_all, wo).astype(bf16).reshape(groups, streams, rows, my_cols)
    gq, gkv = plain_attend_back(
        queries, keyval, grad_mixed, lse, doc_starts, groups, streams, rows, heads
    )
    gq_rows = gq.reshape(groups * own, my_cols)
    gkv_rows = gkv.reshape(groups * own, 2 * HD)
    my_grad_b_query = jnp.sum(gq_rows.astype(f32), axis=0)
    grad_b_value = jnp.sum(gkv_rows[:, HD:], axis=0)
    gkv_low = gkv_rows.astype(bf16)
    shard_query = plain_column_grad(dot_tn(hidden1, gq_rows), groups)
    shard_kv = row_weight_grad(scatter_seq(dot_tn(hidden1, gkv_low)))
    grad_hidden1 = scatter_seq(dot_nt(gq_rows, wq) + dot_nt(gkv_low, w_kv_all))
    back_first, grad_ln1_gain, grad_ln1_bias = normalize_back(
        grad_hidden1, normed1, inverse1, ln1_gain
    )
    input_grad = grad_residual + back_first

    zero = jnp.zeros_like
    grad_b_query = lax.dynamic_update_slice_in_dim(zero(b_query), my_grad_b_query, me * my_cols, 0)
    grad_b_fc = lax.dynamic_update_slice_in_dim(zero(b_fc), my_grad_b_fc, me * my_hidden, 0)
    vectors = (
        grad_ln1_gain,
        grad_ln1_bias,
        grad_b_query,
        grad_b_value,
        grad_b_out,
        grad_ln2_gain,
        grad_ln2_bias,
        grad_b_fc,
        grad_b_proj,
    )
    sums = lax.psum(vectors, ("seq", "fsdp"))
    return (
        output.reshape(streams, rows, width),
        input_grad.reshape(streams, rows, width),
        shard_query,
        shard_kv,
        shard_out,
        shard_fc,
        shard_proj,
        *sums,
    )


def solution(mesh):
    acts = P("fsdp", "seq", None)
    weight = P(("seq", "fsdp"), None)
    return jax.shard_map(
        shards if mesh.shape["seq"] == PLANE else plain_shards,
        mesh=mesh,
        in_specs=(acts, P("fsdp", None)) + (weight,) * 5 + (P(),) * 9 + (acts,),
        out_specs=(acts, acts) + (weight,) * 5 + (P(),) * 9,
        check_vma=False,
    )
```

```python
import functools

import jax
import jax.numpy as jnp
from jax import lax
from jax.experimental import pallas as pl
from jax.experimental.pallas import tpu as pltpu
from jax.sharding import PartitionSpec as P

HEADS = 16
HD = 128

root_two_pi = 0.7978845608028654
cubic_coef = 0.044715
epsilon = 1e-05
f32 = jnp.float32
bf16 = jnp.bfloat16
MESH = pl.DeviceIdType.MESH
ANY = pl.BlockSpec(memory_space=pl.ANY)
WHOLE = pl.BlockSpec(memory_space=pltpu.VMEM)
VMEM_LIMIT = 62 * 1024 * 1024
PLANE = 8


def normalize(values, gain_row, shift_row):
    center = values - jnp.mean(values, axis=-1, keepdims=True)
    inverse = lax.rsqrt(jnp.mean(center * center, axis=-1, keepdims=True) + epsilon)
    normed = center * inverse
    return (normed * gain_row + shift_row, normed, inverse)


def normalize_back(grad_out, normed, inverse, gain_row):
    scaled = grad_out * gain_row
    grad_in = inverse * (
        scaled
        - jnp.mean(scaled, axis=-1, keepdims=True)
        - normed * jnp.mean(scaled * normed, axis=-1, keepdims=True)
    )
    return (grad_in, jnp.sum(grad_out * normed, axis=0), jnp.sum(grad_out, axis=0))


def norm_stats(values):
    mean = jnp.mean(values, axis=-1, keepdims=True)
    center = values - mean
    return mean, lax.rsqrt(jnp.mean(center * center, axis=-1, keepdims=True) + epsilon)


def norm_back(grad_out, normed, inverse, gain_row):
    scaled = grad_out * gain_row
    return inverse * (
        scaled
        - jnp.mean(scaled, axis=-1, keepdims=True)
        - normed * jnp.mean(scaled * normed, axis=-1, keepdims=True)
    )


def gelu_pair(inputs):
    tangent = jnp.tanh(root_two_pi * (inputs + cubic_coef * inputs * inputs * inputs))
    activated = 0.5 * inputs * (1.0 + tangent)
    gradient_slope = 0.5 * (1.0 + tangent) + 0.5 * inputs * (
        1.0 - tangent * tangent
    ) * root_two_pi * (1.0 + 3.0 * cubic_coef * inputs * inputs)
    return (activated, gradient_slope)


def dot(a, b):
    return jnp.dot(a, b, preferred_element_type=f32)


def dot_nt(a, b):
    return lax.dot_general(a, b, (((1,), (1,)), ((), ())), preferred_element_type=f32)


def dot_tn(a, b):
    return lax.dot_general(a, b, (((0,), (0,)), ((), ())), preferred_element_type=f32)


def push(src, dst, send, recv, to):
    return pltpu.make_async_remote_copy(
        src_ref=src, dst_ref=dst, send_sem=send, recv_sem=recv, device_id=to, device_id_type=MESH
    )


def sems(*shape):
    return pltpu.SemaphoreType.DMA(shape)


def rows_at(start, size):
    return pl.ds(pl.multiple_of(start, size), size)


class Place:
    def __init__(self):
        me = lax.axis_index("seq")
        self.me = me
        self.core = lax.rem(me, 2)
        x = lax.rem(lax.div(me, 2), 2)
        y = lax.div(me, 4)
        self.sib = me + 1 - 2 * self.core
        self.xn = me + 2 - 4 * x
        self.yn = me + 4 - 8 * y
        self.dg = me + 2 - 4 * x + 4 - 8 * y
        turn = 1 - 2 * self.core
        self.xs, self.ys, self.ds = self.xn + turn, self.yn + turn, self.dg + turn
        self.layer = lax.axis_index("fsdp")

    def plane_peer(self, step):
        return lax.rem(self.me + step, PLANE)

    def line_peer(self, step, layers):
        return lax.rem(self.layer + step, layers)

    def greet(self, whole_plane=False, layers=1):
        barrier = pltpu.get_barrier_semaphore()
        if whole_plane:
            others = [self.plane_peer(step) for step in range(1, PLANE)]
        else:
            others = [self.sib, self.xn, self.yn]
        for other in others:
            pl.semaphore_signal(barrier, inc=1, device_id={"seq": other}, device_id_type=MESH)
        for step in range(1, layers):
            other = self.line_peer(step, layers)
            pl.semaphore_signal(barrier, inc=1, device_id={"fsdp": other}, device_id_type=MESH)
        pl.semaphore_wait(barrier, len(others) + layers - 1)


class Gather:
    sends = 14
    scratch = [sems(14), sems(PLANE, 2)]

    def __init__(self, place, buf, rows, send, recv):
        self.p, self.buf, self.rows, self.half = place, buf, rows, rows // 2
        self.send_sem, self.recv_sem = send, recv
        self.copies = []

    def piece(self, dev, half):
        return self.buf.at[rows_at(dev * self.rows + half * self.half, self.half), :]

    def pair(self, dev):
        return rows_at(lax.div(dev, 2) * (2 * self.rows), 2 * self.rows)

    def send(self, dev, half, to, src=None):
        k = len(self.copies)
        piece = self.piece(dev, half)
        copy = push(
            piece if src is None else src,
            piece,
            self.send_sem.at[k],
            self.recv_sem.at[dev, half],
            {"seq": to},
        )
        copy.start()
        self.copies.append(copy)

    def arrived(self, dev, half):
        piece = self.piece(dev, half)
        push(
            piece, piece, self.send_sem.at[0], self.recv_sem.at[dev, half], {"seq": self.p.sib}
        ).wait_recv()

    def start(self, own):
        p = self.p
        parts = [own.at[pl.ds(h * self.half, self.half), :] for h in range(2)]
        self.send(p.me, 0, p.yn, parts[0])
        self.send(p.me, 1, p.xn, parts[1])
        self.send(p.me, 1, p.yn, parts[1])
        self.send(p.me, 0, p.xn, parts[0])
        for h in range(2):
            self.send(p.me, h, p.sib, parts[h])

    def relay_first(self):
        p = self.p
        self.arrived(p.yn, 0)
        self.send(p.yn, 0, p.xn)
        self.arrived(p.xn, 1)
        self.send(p.xn, 1, p.yn)
        self.send(p.yn, 0, p.sib)
        self.send(p.xn, 1, p.sib)

    def relay_rest(self):
        p = self.p
        self.arrived(p.xn, 0)
        self.send(p.xn, 0, p.sib)
        self.arrived(p.yn, 1)
        self.send(p.yn, 1, p.sib)

    def relay(self):
        self.relay_first()
        self.relay_rest()

    def have(self, dev):
        self.arrived(dev, 0)
        self.arrived(dev, 1)

    def relay_corner(self):
        p = self.p
        for h in range(2):
            self.arrived(p.dg, h)
            self.send(p.dg, h, p.sib)

    def finish(self):
        for copy in self.copies:
            copy.wait_send()


class Scatter:
    LINES = 32
    CHUNKS = 4

    def __init__(
        self, place, rows, acc, part, sib_out, sib_in, boxes, sib_send, sib_recv, send, recv
    ):
        self.p, self.rows, self.half = place, rows, rows // 2
        self.wide = part.shape[2]
        self.acc, self.part, self.sib_out, self.sib_in = acc, part, sib_out, sib_in
        self.out_d, self.out_x, self.out_y, self.in_d, self.in_x, self.in_y = boxes
        self.sib_send, self.sib_recv, self.send, self.recv = sib_send, sib_recv, send, recv
        self.copies = []

    @staticmethod
    def scratch(rows, wide):
        return [
            pltpu.VMEM((2 * rows, wide // 2), f32),
            pltpu.VMEM((4, rows, wide), f32),
            pltpu.VMEM((4, rows, wide), bf16),
            pltpu.VMEM((4, rows, wide), bf16),
            *[pltpu.VMEM((rows, wide), bf16)] * 6,
            sems(4, 2),
            sems(4, 2),
            sems(14),
            sems(14),
        ]

    @classmethod
    def take(cls, place, rows, refs):
        return cls(place, rows, *refs[:4], refs[4:10], *refs[10:14])

    refs = 14

    def cols(self, c):
        return pl.ds(c * (self.wide // 2), self.wide // 2)

    def swap(self, role, dev, product, c):
        p = self.p
        self.acc[...] = product(role, rows_at(lax.div(dev, 2) * (2 * self.rows), 2 * self.rows), c)
        theirs = rows_at((1 - p.core) * self.rows, self.rows)
        ours = rows_at(p.core * self.rows, self.rows)
        self.sib_out[role, :, self.cols(c)] = self.acc[theirs, :].astype(bf16)
        copy = push(
            self.sib_out.at[role, :, self.cols(c)],
            self.sib_in.at[role, :, self.cols(c)],
            self.sib_send.at[role, c],
            self.sib_recv.at[role, c],
            {"seq": p.sib},
        )
        copy.start()
        self.copies.append(copy)
        self.part[role, :, self.cols(c)] = self.acc[ours, :]
        return copy

    def swap_all(self, role, dev, product):
        return [self.swap(role, dev, product, c) for c in range(2)]

    def add_into(self, dst, role, first, size, more=(), cols=slice(None)):
        lines = self.LINES

        @pl.loop(0, size // lines)
        def _(i):
            line = rows_at(first + i * lines, lines)
            value = self.part[role, line, cols] + self.sib_in[role, line, cols].astype(f32)
            for ref in more:
                value = value + ref[line, cols].astype(f32)
            dst[line, cols] = value.astype(dst.dtype)

    def final(self, start, size):
        line = pl.ds(start, size)
        value = self.part[3, line, :] + self.sib_in[3, line, :].astype(f32)
        return line, value + self.in_x[line, :].astype(f32) + self.in_y[line, :].astype(f32)

    def ship(self, src, dst, h, k, to, cols=slice(None), chunk=None):
        lines = pl.ds(h * self.half, self.half)
        if chunk is not None:
            size = self.half // self.CHUNKS
            lines = pl.ds(h * self.half + chunk * size, size)
        copy = push(
            src.at[lines, cols], dst.at[lines, cols], self.send.at[k], self.recv.at[k], {"seq": to}
        )
        copy.start()
        self.copies.append(copy)
        return copy

    def ship_corner(self, c):
        cols = self.cols(c)
        self.add_into(self.out_d, 0, 0, self.rows, (), cols)
        return (
            self.ship(self.out_d, self.in_d, 0, 2 * c, self.p.xn, cols),
            self.ship(self.out_d, self.in_d, 1, 2 * c + 1, self.p.yn, cols),
        )

    def run(self, product, emit, idle=None, polls=(None, None, None)):
        polls = [poll or (lambda: None) for poll in polls]
        p, rows, half = self.p, self.rows, self.half
        d0 = self.swap(0, p.dg, product, 0)
        d1 = self.swap(0, p.dg, product, 1)
        d0.wait_recv()
        dx0, dy0 = self.ship_corner(0)
        to_x = [self.swap(1, p.xn, product, 0)]
        d1.wait_recv()
        dx1, dy1 = self.ship_corner(1)
        to_x.append(self.swap(1, p.xn, product, 1))
        polls[0]()
        to_y = self.swap_all(2, p.yn, product)
        for copy in to_x:
            copy.wait_recv()
        self.add_into(self.out_x, 1, 0, half)
        x0 = self.ship(self.out_x, self.in_x, 0, 4, p.xn)
        for copy in to_y:
            copy.wait_recv()
        self.add_into(self.out_y, 2, half, half)
        y1 = self.ship(self.out_y, self.in_y, 1, 5, p.yn)
        polls[1]()
        to_me = self.swap_all(3, p.me, product)
        polls[2]()
        size = half // self.CHUNKS
        x1, y0 = [], []
        for copy in (dx0, dx1, dy0, dy1):
            copy.wait_recv()
        for k in range(self.CHUNKS):
            self.add_into(self.out_y, 2, k * size, size, (self.in_d,))
            y0.append(self.ship(self.out_y, self.in_y, 0, 6 + k, p.yn, chunk=k))
            self.add_into(self.out_x, 1, half + k * size, size, (self.in_d,))
            x1.append(
                self.ship(self.out_x, self.in_x, 1, 6 + self.CHUNKS + k, p.xn, chunk=k)
            )
        if idle is not None:
            idle()
        for copy in (*to_me, x0, y1):
            copy.wait_recv()
        for k in range(self.CHUNKS):
            y0[k].wait_recv()
            emit(*self.final(k * size, size))
            x1[k].wait_recv()
            emit(*self.final(half + k * size, size))
        for copy in self.copies:
            copy.wait_send()


class LineGather:
    def __init__(self, place, src, block, layers, send, recv):
        self.me, self.src, self.block, self.layers = place.layer, src, block, layers
        self.send, self.recv = send, recv
        self.step = 0

    @staticmethod
    def scratch(layers):
        return [sems(2 * layers), sems(layers)]

    def copy(self, src, layer, k, to):
        return push(src, self.block(layer), self.send.at[k], self.recv.at[layer], {"fsdp": to})

    def wait_from(self, layer):
        other = lax.rem(self.me + 1, self.layers)
        self.copy(self.block(layer), layer, 0, other).wait_recv()

    def start(self):
        me, top = self.me, self.layers - 1

        @pl.when(me < top)
        def _():
            self.copy(self.src, me, 0, me + 1).start()

        @pl.when(me > 0)
        def _():
            self.copy(self.src, me, self.layers, me - 1).start()

    def poll(self):
        me, top, hop = self.me, self.layers - 1, self.step
        self.step += 1
        below, above = me - 1 - hop, me + 1 + hop

        @pl.when((below >= 0) & (me < top))
        def _():
            self.wait_from(below)
            self.copy(self.block(below), below, hop + 1, me + 1).start()

        @pl.when((above <= top) & (me > 0))
        def _():
            self.wait_from(above)
            self.copy(self.block(above), above, self.layers + hop + 1, me - 1).start()

    def finish(self):
        while self.step < self.layers - 2:
            self.poll()
        me, top = self.me, self.layers - 1

        @pl.when(me == top)
        def _():
            for layer in range(top):
                self.wait_from(layer)

        @pl.when(me == 0)
        def _():
            for layer in range(1, top + 1):
                self.wait_from(layer)

        for hop in range(top):

            @pl.when((hop <= me) & (me < top))
            def _(hop=hop):
                self.copy(self.block(me), me, hop, me + 1).wait_send()

            @pl.when((hop <= top - me) & (me > 0))
            def _(hop=hop):
                self.copy(self.block(me), me, self.layers + hop, me - 1).wait_send()


class LineSum:
    def __init__(self, place, block, layers, own, up, down, us, ur, ds, dr, local):
        self.me, self.block, self.layers = place.layer, block, layers
        self.own, self.up, self.down = own, up, down
        self.us, self.ur, self.ds, self.dr, self.local = us, ur, ds, dr, local
        self.step = 0
        self.loads = [load(block(f), own.at[f], local.at[f]) for f in range(layers)]

    @staticmethod
    def scratch(shape, layers):
        return [
            pltpu.VMEM((layers, *shape), bf16),
            pltpu.VMEM((layers - 1, *shape), bf16),
            pltpu.VMEM((layers - 1, *shape), bf16),
            *[sems(layers)] * 5,
        ]

    refs = 8

    def up_copy(self, src, f, to):
        return push(src, self.up.at[f - 1], self.us.at[f], self.ur.at[f], {"fsdp": to})

    def down_copy(self, src, f, to):
        return push(src, self.down.at[f], self.ds.at[f], self.dr.at[f], {"fsdp": to})

    @staticmethod
    def start(*lines):
        me, top = lines[0].me, lines[0].layers - 1

        @pl.when(me == 0)
        def _():
            for f in range(top, 0, -1):
                for line in lines:
                    line.up_copy(line.block(f), f, 1).start()
            for line in lines:
                line.up[0] = jnp.zeros(line.up.shape[1:], bf16)

        @pl.when(me == top)
        def _():
            for f in range(top):
                for line in lines:
                    line.down_copy(line.block(f), f, top - 1).start()
            for line in lines:
                line.down[top - 1] = jnp.zeros(line.down.shape[1:], bf16)

    def chunks(self):
        shape = self.own.shape[1:]
        size = 1 if len(shape) == 3 else 32
        return shape[0] // size, lambda i: rows_at(i * size, size) if size > 1 else i

    def add(self, box, slot, f):
        count, where = self.chunks()

        @pl.loop(0, count)
        def _(i):
            here = where(i)
            value = box[slot, here].astype(f32) + self.own[f, here].astype(f32)
            box[slot, here] = value.astype(bf16)

    def poll(self):
        top, k = self.layers - 1, self.step
        self.step += 1
        if k == 0:
            for copy in self.loads:
                copy.wait()
        for f in range(2, top + 1):
            at = f - top + 1 + k
            if not 1 <= at < f:
                continue

            @pl.when(self.me == at)
            def _(f=f, at=at):
                self.up_copy(self.up.at[f - 1], f, at + 1).wait_recv()
                self.add(self.up, f - 1, f)
                self.up_copy(self.up.at[f - 1], f, at + 1).start()

            @pl.when(self.me == top - at)
            def _(f=top - f, at=top - at):
                self.down_copy(self.down.at[f], f, at - 1).wait_recv()
                self.add(self.down, f, f)
                self.down_copy(self.down.at[f], f, at - 1).start()

    def finish(self, emit):
        while self.step < self.layers - 2:
            self.poll()
        me, top = self.me, self.layers - 1

        @pl.when(me > 0)
        def _():
            self.up_copy(self.up.at[me - 1], me, me - 1).wait_recv()

        @pl.when(me < top)
        def _():
            self.down_copy(self.down.at[me], me, me + 1).wait_recv()

        count, where = self.chunks()
        below, above = jnp.maximum(me - 1, 0), jnp.minimum(me, top - 1)

        @pl.loop(0, count)
        def _(i):
            here = where(i)
            value = self.up[below, here].astype(f32) + self.down[above, here].astype(f32)
            emit(here, value + self.own[me, here].astype(f32))

        for f in range(1, top + 1):

            @pl.when(me < f)
            def _(f=f):
                self.up_copy(self.up.at[f - 1], f, me + 1).wait_send()

        for f in range(top):

            @pl.when(me > f)
            def _(f=f):
                self.down_copy(self.down.at[f], f, me - 1).wait_send()


class PlaneSum:
    def __init__(self, place, src, box, send, recv):
        self.p, self.src, self.box = place, src, box
        self.copies = []
        for step in range(1, PLANE):
            to = place.plane_peer(step)
            copy = push(src.at[to], box.at[step], send.at[step], recv.at[step], {"seq": to})
            copy.start()
            self.copies.append(copy)

    def total(self):
        value = self.src[self.p.me].astype(f32)
        for step, copy in enumerate(self.copies):
            copy.wait_recv()
            value = value + self.box[step + 1].astype(f32)
        return value

    def finish(self):
        for copy in self.copies:
            copy.wait_send()


class Spread:
    def __init__(self, place, src, out, send, recv, local, room=None):
        cols = src.shape[2]
        spot = out.at[:, rows_at(place.me * cols, cols)]
        if room is None:
            self.copies = [load(src.at[place.me], spot, local)]
        else:
            self.copies = [Through(src.at[place.me], room, spot, local)]
        for step in range(1, PLANE):
            to = place.plane_peer(step)
            copy = push(src.at[to], spot, send.at[step], recv.at[step], {"seq": to})
            copy.start()
            self.copies.append(copy)

    def finish(self):
        for copy in self.copies:
            copy.wait()


def fold(ref, first, value):
    rows, wide = value.shape
    total = jnp.sum(value.reshape(rows // 8, 8, wide), axis=0)
    ref[...] = total if first else ref[...] + total


class Rows:
    @staticmethod
    def scratch(rows, wide, dtype):
        return [pltpu.VMEM((rows, wide), dtype), sems(2 * Scatter.CHUNKS)]

    def __init__(self, out, stage, sem):
        self.out, self.stage, self.sem = out, stage, sem
        self.copies = []

    def put(self, line, value):
        self.stage[line, :] = value.astype(self.stage.dtype)
        self.copies.append(
            load(self.stage.at[line, :], self.out.at[line, :], self.sem.at[len(self.copies)])
        )

    def finish(self):
        for copy in self.copies:
            copy.wait()


def params(number, vmem=True):
    return pltpu.CompilerParams(
        collective_id=number,
        has_side_effects=True,
        vmem_limit_bytes=VMEM_LIMIT if vmem else None,
    )


def cost(flops, mib=40):
    return pl.CostEstimate(flops=flops, bytes_accessed=mib * 1024 * 1024, transcendentals=0)


def load(src, dst, sem):
    copy = pltpu.make_async_copy(src, dst, sem)
    copy.start()
    return copy


class Through:
    def __init__(self, src, room, dst, sem):
        self.room, self.dst, self.sem = room, dst, sem
        self.copy = load(src, room, sem)

    def put(self):
        self.copy.wait()
        self.copy = load(self.room, self.dst, self.sem)

    def wait(self):
        self.copy.wait()


def rows_of(ref, rows):
    return lambda k: ref.at[rows_at(k * rows, rows), :]


def split_weights(tokens, gain, shift, w_query, w_fc, w_kv, w_out, layers, number):
    arrays, lined = (w_query, w_fc), (w_kv, w_out)
    own_rows, width = tokens.shape

    def kernel(tok_ref, gain_ref, shift_ref, wq_ref, wf_ref, kv_ref, wo_ref, *refs):
        wq_out, wf_out, kv_out, wo_out, hidden, mean_out, inverse_out = refs[:7]
        send, recv, kv_send, kv_recv, wo_send, wo_recv, local = refs[7:14]
        rooms = refs[14:]
        p = Place()
        ins, outs = (wq_ref, wf_ref), (wq_out, wf_out)
        lines = (
            LineGather(p, kv_ref, rows_of(kv_out, kv_ref.shape[0]), layers, kv_send, kv_recv),
            LineGather(p, wo_ref, rows_of(wo_out, wo_ref.shape[0]), layers, wo_send, wo_recv),
        )

        def block(i, dev):
            cols = ins[i].shape[1] // PLANE
            return ins[i].at[:, rows_at(dev * cols, cols)]

        own = []
        for i in range(2):
            own.append(Through(block(i, p.me), rooms[i], outs[i].at[p.me], local.at[i]))
            own.append(Through(lines[i].src, rooms[2 + i], lines[i].block(p.layer), local.at[2 + i]))
        p.greet(True, layers)
        for line in lines:
            line.start()
        copies = []
        for i in (1, 0):
            for step in range(1, PLANE):
                to = p.plane_peer(step)
                copies.append(
                    push(
                        block(i, to),
                        outs[i].at[p.me],
                        send.at[i, step],
                        recv.at[i, step],
                        {"seq": to},
                    )
                )
                copies[-1].start()

        for copy in own:
            copy.put()

        @pl.loop(0, own_rows // 32)
        def _(i):
            here = rows_at(i * 32, 32)
            values = tok_ref[here, :].astype(f32)
            mean, inverse = norm_stats(values)
            hidden[here, :] = (
                (values - mean) * inverse * gain_ref[...] + shift_ref[...]
            ).astype(bf16)
            mean_out[here, :] = mean
            inverse_out[here, :] = inverse

        for _ in range(layers - 2):
            for line in lines:
                line.poll()
        for copy in own + copies:
            copy.wait()
        for line in lines:
            line.finish()

    return pl.pallas_call(
        kernel,
        out_shape=[
            jax.ShapeDtypeStruct((PLANE, a.shape[0], a.shape[1] // PLANE), a.dtype)
            for a in arrays
        ]
        + [jax.ShapeDtypeStruct((layers * a.shape[0], a.shape[1]), a.dtype) for a in lined]
        + [jax.ShapeDtypeStruct((own_rows, width), bf16)]
        + [jax.ShapeDtypeStruct((own_rows, 1), f32)] * 2,
        in_specs=[WHOLE] * 3 + [ANY] * 4,
        out_specs=[ANY] * 4 + [WHOLE] * 3,
        scratch_shapes=[sems(2, PLANE), sems(2, PLANE)]
        + LineGather.scratch(layers) * 2
        + [sems(4)]
        + [pltpu.VMEM((a.shape[0], a.shape[1] // PLANE), bf16) for a in arrays]
        + [pltpu.VMEM(a.shape, bf16) for a in lined],
        compiler_params=params(number),
        name="split_weights",
    )(tokens, gain, shift, w_query, w_fc, w_kv, w_out)


def gather_hidden1(hidden1, low_kv, pieces, layers, number):
    count = len(pieces)
    shapes = [(stop - start, *a.shape[1:]) for a, start, stop in pieces]

    def kernel(h_ref, kv_ref, *refs):
        ins = [refs[i].at[pl.ds(pieces[i][1], shapes[i][0])] for i in range(count)]
        (h_all, kv_all), outs = refs[count : count + 2], refs[count + 2 :]
        outs, refs = outs[:count], outs[count:]
        hs, hr, ks, kr, local, h_room, kv_room = refs[:7]
        refs = refs[7:]
        rooms, refs = refs[:count], refs[count:]
        p = Place()
        h_rows, kv_rows = h_ref.shape[0], kv_ref.shape[0]
        own = [
            Through(h_ref, h_room, h_all.at[rows_at(p.me * h_rows, h_rows), :], local.at[0]),
            Through(kv_ref, kv_room, kv_all.at[rows_at(p.me * kv_rows, kv_rows), :], local.at[1]),
        ]
        lines = []
        for i in range(count):
            own.append(Through(ins[i], rooms[i], outs[i].at[:, p.layer], local.at[2 + i]))
            lines.append(
                LineGather(
                    p, ins[i], lambda k, i=i: outs[i].at[:, k], layers, *refs[2 * i : 2 * i + 2]
                )
            )
        p.greet(False, layers)
        kv = Gather(p, kv_all, kv_rows, ks, kr)
        h = Gather(p, h_all, h_rows, hs, hr)
        h.start(h_ref)
        kv.start(kv_ref)
        for line in lines:
            line.start()
        for copy in own:
            copy.put()
        lines[0].poll()
        h.relay_first()
        for line in lines[1:]:
            line.poll()
        h.relay_rest()
        lines[0].poll()
        kv.relay()
        for line in lines[1:]:
            line.poll()
        h.relay_corner()
        kv.relay_corner()
        for g in (kv, h):
            for dev in (p.sib, p.xs, p.ys, p.ds):
                g.have(dev)
            g.finish()
        for item in own:
            item.wait()
        for line in lines:
            line.finish()

    return pl.pallas_call(
        kernel,
        out_shape=[
            jax.ShapeDtypeStruct((PLANE * hidden1.shape[0], hidden1.shape[1]), bf16),
            jax.ShapeDtypeStruct((PLANE * low_kv.shape[0], low_kv.shape[1]), bf16),
        ]
        + [jax.ShapeDtypeStruct((a[0], layers, *a[1:]), bf16) for a in shapes],
        in_specs=[ANY] * (2 + count),
        out_specs=[ANY] * (2 + count),
        scratch_shapes=Gather.scratch * 2
        + [sems(2 + count)]
        + [pltpu.VMEM(a, bf16) for a in (hidden1.shape, low_kv.shape, *shapes)]
        + LineGather.scratch(layers) * count,
        compiler_params=params(number),
        name="gather_hidden1",
    )(hidden1, low_kv, *[a for a, _, _ in pieces])


def project_attend(
    docs, hidden1, wq, w_kv, bq, bv, cot, piece, streams, heads, layers, number
):
    piece, first, last = piece
    piece_shape = (last - first, *piece.shape[1:])
    total, depth = hidden1.shape
    cols, kv_cols = wq.shape[1], w_kv.shape[1]
    rows = total // PLANE // streams
    length = PLANE * rows
    block = min(QROWS, length)
    chunk = total // 4

    def kernel(docs_ref, h_ref, wq_ref, wkv_ref, bq_ref, bv_ref, cot_ref, piece_ref, *refs):
        cot_all, line_all, q_out, kv_out, mixed_out, lse_ref = refs[:6]
        h_buf, wq_buf, wkv_buf, q_buf, kv_buf, mixed_buf, room, line_room = refs[6:14]
        send, recv, zsend, zrecv, local = refs[14:]
        p = Place()
        piece_ref = piece_ref.at[pl.ds(first, last - first)]
        own_rows = cot_ref.shape[0]

        def fetch(k):
            return load(
                h_ref.at[pl.ds(k * chunk, chunk), :], h_buf.at[k % 2], local.at[k % 2]
            )

        fetches = [fetch(0)]
        weights = [load(wq_ref, wq_buf, local.at[2]), load(wkv_ref, wkv_buf, local.at[3])]
        own = Through(
            cot_ref, room, cot_all.at[rows_at(p.me * own_rows, own_rows), :], local.at[4]
        )
        own_line = Through(piece_ref, line_room, line_all.at[:, p.layer], local.at[8])
        line = LineGather(p, piece_ref, lambda k: line_all.at[:, k], layers, zsend, zrecv)
        p.greet(False, layers)
        g = Gather(p, cot_all, own_rows, send, recv)
        g.start(cot_ref)
        line.start()
        own.put()
        own_line.put()
        for copy in weights:
            copy.wait()
        per = chunk // (streams * rows)
        for k in range(4):
            fetches[k].wait()
            if k < 3:
                fetches.append(fetch(k + 1))
            where = pl.ds(k * per, per)
            q = dot(h_buf[k % 2], wq_buf[...]) + bq_ref[:, rows_at(p.me * cols, cols)]
            q_buf[where] = q.astype(bf16).reshape(per, streams, rows, cols)
            kv = dot(h_buf[k % 2], wkv_buf[...])
            kv = jnp.concatenate([kv[:, :HD], kv[:, HD:] + bv_ref[...]], axis=1)
            kv_buf[where] = kv.astype(bf16).reshape(per, streams, rows, kv_cols)
        stores = [load(q_buf, q_out, local.at[5]), load(kv_buf, kv_out, local.at[6])]
        g.relay_first()
        line.poll()
        for stream in range(streams):
            attend_stream(
                docs_ref,
                stream,
                q_buf.at[:, stream],
                kv_buf.at[:, stream],
                mixed_buf.at[:, stream],
                lse_ref.at[stream],
                block,
                heads,
            )
        stores.append(load(mixed_buf, mixed_out, local.at[7]))
        g.relay_rest()
        line.poll()
        g.relay_corner()
        for dev in (p.sib, p.xs, p.ys, p.ds):
            g.have(dev)
        g.finish()
        line.finish()
        own.wait()
        own_line.wait()
        for copy in stores:
            copy.wait()

    q_shape = (PLANE, streams, rows, cols)
    kv_shape = (PLANE, streams, rows, kv_cols)
    return pl.pallas_call(
        kernel,
        out_shape=[
            jax.ShapeDtypeStruct((PLANE * cot.shape[0], cot.shape[1]), bf16),
            jax.ShapeDtypeStruct((piece_shape[0], layers, *piece_shape[1:]), bf16),
            jax.ShapeDtypeStruct(q_shape, bf16),
            jax.ShapeDtypeStruct(kv_shape, bf16),
            jax.ShapeDtypeStruct(q_shape, bf16),
            jax.ShapeDtypeStruct((streams, heads, length), f32),
        ],
        in_specs=[pl.BlockSpec(memory_space=pltpu.SMEM)] + [ANY] * 3 + [WHOLE] * 2 + [ANY] * 2,
        out_specs=[ANY] * 5 + [WHOLE],
        scratch_shapes=[
            pltpu.VMEM((2, chunk, depth), bf16),
            pltpu.VMEM(wq.shape, bf16),
            pltpu.VMEM(w_kv.shape, bf16),
            pltpu.VMEM(q_shape, bf16),
            pltpu.VMEM(kv_shape, bf16),
            pltpu.VMEM(q_shape, bf16),
            pltpu.VMEM(cot.shape, bf16),
            pltpu.VMEM(piece_shape, bf16),
        ]
        + Gather.scratch
        + LineGather.scratch(layers)
        + [sems(9)],
        compiler_params=params(number),
        cost_estimate=cost(2 * total * depth * (cols + kv_cols)),
        name="project_attend",
    )(docs, hidden1, wq, w_kv, bq, bv, cot, piece)


def load_parts(parts, dst, local):
    copies, at = [], 0
    for i, part in enumerate(parts):
        rows = part.shape[0]
        copies.append(load(part, dst.at[pl.ds(at, rows), :], local.at[i]))
        at += rows
    return copies


def load_blocks(parts, dst, local):
    copies, at = [], 0
    for layer in range(parts[0].shape[0]):
        for part in parts:
            rows = part.shape[1]
            copies.append(load(part.at[layer], dst.at[pl.ds(at, rows), :], local.at[len(copies)]))
            at += rows
    return copies


def gather_fc(hidden2, wf, bf, cot_all, part, layers, number):
    part, first, last = part
    part_shape = (last - first, part.shape[1])
    rows, depth = hidden2.shape
    wide = wf[0].shape[1]
    n_wf = len(wf)
    total = PLANE * rows
    out_wide = cot_all.shape[1]
    tile = 256

    def kernel(own_ref, b_ref, cot_ref, part_ref, *refs):
        w_refs, refs = refs[:n_wf], refs[n_wf:]
        all_ref, act_ref, slope_ref, dw_ref, line_all = refs[:5]
        buf, w_buf, act, slope, cot, acc, dw, room, send, recv, zsend, zrecv, local, wlocal = refs[
            5:
        ]
        p = Place()
        part_ref = part_ref.at[pl.ds(first, last - first), :]
        load_own = load(own_ref, buf.at[rows_at(p.me * rows, rows), :], local.at[0])
        loads_w = load_parts(w_refs, w_buf, wlocal)
        own_line = Through(part_ref, room, line_all.at[p.layer], local.at[1])
        line = LineGather(p, part_ref, lambda k: line_all.at[k], layers, zsend, zrecv)
        p.greet(False, layers)
        g = Gather(p, buf, rows, send, recv)
        g.start(own_ref)
        line.start()
        own_line.put()
        stores = []
        cots = {}

        def fetch(k, dev):
            cots[k] = load(cot_ref.at[g.pair(dev), :], cot.at[k % 2], local.at[2 + k % 2])

        def work(k, dev):
            block = g.pair(dev)
            stores.append(load(buf.at[block, :], all_ref.at[block, :], local.at[4 + 3 * k]))

            @pl.loop(0, wide // 512)
            def _(j):
                cols = rows_at(j * 512, 512)
                bias = b_ref[:, rows_at(p.me * wide + j * 512, 512)]
                acc_fc = dot(buf[block, :], w_buf[:, cols]) + bias
                activated, gradient = gelu_pair(acc_fc)
                act[block, cols] = activated.astype(bf16)
                slope[block, cols] = gradient.astype(bf16)

            for i, (src, dst) in enumerate(((act, act_ref), (slope, slope_ref))):
                stores.append(
                    load(src.at[block, :], dst.at[block, :], local.at[4 + 3 * k + 1 + i])
                )

        def grads(k, dev):
            block = g.pair(dev)
            cots[k].wait()

            for j in range(wide // tile):
                cols = pl.ds(j * tile, tile)
                term = dot_tn(act[block, cols], cot[k % 2])
                if k == 0:
                    acc[cols, :] = term
                elif k < 3:
                    acc[cols, :] += term
                else:
                    dw[cols, :] = (acc[cols, :] + term).astype(bf16)
                    stores.append(load(dw.at[cols, :], dw_ref.at[cols, :], local.at[16 + j]))

        fetch(0, p.me)
        fetch(1, p.xn)
        load_own.wait()
        for copy in loads_w:
            copy.wait()
        g.have(p.sib)
        work(0, p.me)
        g.relay_first()
        grads(0, p.me)
        line.poll()
        fetch(2, p.yn)
        g.relay_rest()
        g.have(p.xs)
        work(1, p.xn)
        g.have(p.ys)
        work(2, p.yn)
        line.poll()
        grads(1, p.xn)
        fetch(3, p.dg)
        g.relay_corner()
        grads(2, p.yn)
        g.have(p.ds)
        work(3, p.dg)
        grads(3, p.dg)
        g.finish()
        line.finish()
        own_line.wait()
        for copy in stores:
            copy.wait()

    return pl.pallas_call(
        kernel,
        out_shape=[
            jax.ShapeDtypeStruct((total, depth), bf16),
            jax.ShapeDtypeStruct((total, wide), bf16),
            jax.ShapeDtypeStruct((total, wide), bf16),
            jax.ShapeDtypeStruct((wide, out_wide), bf16),
            jax.ShapeDtypeStruct((layers, *part_shape), bf16),
        ],
        in_specs=[ANY, WHOLE] + [ANY] * (2 + n_wf),
        out_specs=[ANY] * 5,
        scratch_shapes=[
            pltpu.VMEM((total, depth), bf16),
            pltpu.VMEM((depth, wide), bf16),
            pltpu.VMEM((total, wide), bf16),
            pltpu.VMEM((total, wide), bf16),
            pltpu.VMEM((2, 2 * rows, out_wide), bf16),
            pltpu.VMEM((wide, out_wide), f32),
            pltpu.VMEM((wide, out_wide), bf16),
            pltpu.VMEM(part_shape, bf16),
        ]
        + Gather.scratch
        + LineGather.scratch(layers)
        + [sems(16 + wide // tile), sems(n_wf)],
        compiler_params=params(number),
        cost_estimate=cost(4 * total * depth * wide),
        name="gather_fc",
    )(hidden2, bf, cot_all, part, *wf)


def gather_out(
    grad_attn, wo, mixed, hidden2, grad_pre, first_fc, grad_proj, proj_done, fc_part, layers, number
):
    rows, depth = grad_attn.shape
    wide = wo.shape[0]
    total = PLANE * rows
    hidden = grad_pre.shape[1]
    tile = 512
    steps = (depth - first_fc) // tile
    proj_cut = proj_done.shape[0]
    proj_shape = (grad_proj.shape[1] - proj_cut, grad_proj.shape[2])
    fc_shape = (fc_part.shape[0], *fc_part.shape[2:])

    def kernel(own_ref, w_ref, mixed_ref, h_ref, gp_ref, proj_ref, fc_ref, done_ref, *refs):
        gm_ref, dw_ref, dwfc_ref, proj_out, fc_out = refs[:5]
        buf, w_buf, mixed_buf, gm, acc, dw, gp, h_buf, dwfc = refs[5:14]
        send, recv = refs[14:16]
        line_refs = refs[16:32]
        (local,) = refs[32:]
        p = Place()
        load_own = load(own_ref, buf.at[rows_at(p.me * rows, rows), :], local.at[0])
        loads = [load(w_ref, w_buf, local.at[1]), load(mixed_ref, mixed_buf, local.at[2])]
        load_gp = load(gp_ref, gp, local.at[3])
        proj = LineSum(p, lambda f: proj_ref.at[f, pl.ds(proj_cut, proj_shape[0]), :], layers, *line_refs[:8])
        fc = LineSum(p, lambda f: fc_ref.at[:, f], layers, *line_refs[8:])

        def h_fetch(i):
            here = pl.ds(first_fc + i * tile, tile)
            return load(h_ref.at[:, here], h_buf.at[i % 2], local.at[4 + i % 2])

        tiles = [h_fetch(0)]
        stores = []
        p.greet(False, layers)
        g = Gather(p, buf, rows, send, recv)
        g.start(own_ref)
        LineSum.start(proj, fc)

        def work(dev):
            block = g.pair(dev)
            gm[block, :] = dot_nt(buf[block, :], w_buf[...]).astype(bf16)

        def grads(k, dev):
            block = g.pair(dev)
            term = dot_tn(mixed_buf[block, :], buf[block, :])
            if k == 0:
                acc[...] = term
            elif k < 3:
                acc[...] += term
            else:
                dw[...] = (acc[...] + term).astype(bf16)

        def fc_grads(i):
            tiles[i].wait()
            if i + 1 < steps:
                tiles.append(h_fetch(i + 1))
            if i >= 2:
                stores[i - 2].wait()
            dwfc[i % 2] = dot_tn(h_buf[i % 2], gp[...]).astype(bf16)
            stores.append(
                load(dwfc.at[i % 2], dwfc_ref.at[pl.ds(i * tile, tile), :], local.at[6 + i % 2])
            )

        load_own.wait()
        for copy in loads:
            copy.wait()
        g.have(p.sib)
        work(p.me)
        grads(0, p.me)
        for i in range(0, proj_cut, 32):
            proj_out[pl.ds(i, 32), :] = done_ref[pl.ds(i, 32), :].astype(f32)
        load_gp.wait()
        fc_grads(0)
        proj.poll()
        g.relay_first()
        fc_grads(1)
        fc.poll()
        for i in range(2, steps):
            fc_grads(i)
        proj.poll()
        g.relay_rest()
        fc.poll()
        g.have(p.xs)
        work(p.xn)
        g.have(p.ys)
        work(p.yn)
        grads(1, p.xn)
        g.relay_corner()
        grads(2, p.yn)
        g.have(p.ds)
        work(p.dg)
        store = load(gm, gm_ref, local.at[8])
        grads(3, p.dg)
        store_dw = load(dw, dw_ref, local.at[9])
        g.finish()

        def keep_proj(where, value):
            proj_out[pl.ds(proj_cut + where.start, where.size), :] = value

        def keep_fc(where, value):
            fc_out[where] = value.astype(bf16)

        proj.finish(keep_proj)
        fc.finish(keep_fc)
        store.wait()
        store_dw.wait()
        for copy in stores[-2:]:
            copy.wait()

    return pl.pallas_call(
        kernel,
        out_shape=[
            jax.ShapeDtypeStruct((total, wide), bf16),
            jax.ShapeDtypeStruct((wide, depth), bf16),
            jax.ShapeDtypeStruct((depth - first_fc, hidden), bf16),
            jax.ShapeDtypeStruct(grad_proj.shape[1:], f32),
            jax.ShapeDtypeStruct(fc_shape, bf16),
        ],
        in_specs=[ANY] * 7 + [WHOLE],
        out_specs=[ANY] * 3 + [WHOLE] * 2,
        scratch_shapes=[
            pltpu.VMEM((total, depth), bf16),
            pltpu.VMEM(wo.shape, bf16),
            pltpu.VMEM(mixed.shape, bf16),
            pltpu.VMEM((total, wide), bf16),
            pltpu.VMEM((wide, depth), f32),
            pltpu.VMEM((wide, depth), bf16),
            pltpu.VMEM(grad_pre.shape, bf16),
            pltpu.VMEM((2, total, tile), bf16),
            pltpu.VMEM((2, tile, hidden), bf16),
        ]
        + Gather.scratch
        + LineSum.scratch(proj_shape, layers)
        + LineSum.scratch(fc_shape, layers)
        + [sems(10)],
        compiler_params=params(number),
        cost_estimate=cost(4 * total * depth * wide),
        name="gather_out",
    )(grad_attn, wo, mixed, hidden2, grad_pre, grad_proj, fc_part, proj_done)


def scatter_attn(mixed, wo, tokens, b_out, gain, shift, piece, part, layers, number):
    piece, piece_first, piece_last = piece
    piece_shape = (piece_last - piece_first, *piece.shape[1:])
    part, part_first, part_last = part
    part_shape = (part_last - part_first, part.shape[1])
    total, depth = mixed.shape
    rows = total // PLANE
    wide = wo.shape[1]

    def kernel(a_ref, w_ref, piece_ref, part_ref, tok_ref, bias_ref, gain_ref, shift_ref, *refs):
        residual, hidden, mean_out, inverse_out, piece_all, part_all = refs[:6]
        a_buf, w_buf, piece_room, part_room = refs[6:10]
        s, line_refs, local = refs[10:24], refs[24:28], refs[28]
        residual, hidden = Rows(residual, *refs[29:31]), Rows(hidden, *refs[31:33])
        p = Place()
        piece_ref = piece_ref.at[pl.ds(piece_first, piece_shape[0])]
        part_ref = part_ref.at[pl.ds(part_first, part_shape[0]), :]
        loads = [load(a_ref, a_buf, local.at[0]), load(w_ref, w_buf, local.at[1])]
        own = [
            Through(piece_ref, piece_room, piece_all.at[:, p.layer], local.at[2]),
            Through(part_ref, part_room, part_all.at[p.layer], local.at[3]),
        ]
        lines = [
            LineGather(p, piece_ref, lambda k: piece_all.at[:, k], layers, *line_refs[:2]),
            LineGather(p, part_ref, lambda k: part_all.at[k], layers, *line_refs[2:]),
        ]
        p.greet(False, layers)
        for line in lines:
            line.start()
        for copy in loads:
            copy.wait()

        def emit(line, value):
            values = tok_ref[line, :].astype(f32) + value + bias_ref[...]
            mean, inverse = norm_stats(values)
            residual.put(line, values)
            hidden.put(line, (values - mean) * inverse * gain_ref[...] + shift_ref[...])
            mean_out[line, :] = mean
            inverse_out[line, :] = inverse

        def settle():
            for copy in own:
                copy.put()
            lines[0].poll()

        def idle():
            lines[1].poll()
            lines[0].poll()
            lines[1].poll()

        Scatter.take(p, rows, s).run(
            plain_product(a_buf, w_buf), emit, idle, (settle, None, None)
        )
        for line in lines:
            line.finish()
        for item in (*own, residual, hidden):
            item.finish() if isinstance(item, Rows) else item.wait()

    return pl.pallas_call(
        kernel,
        out_shape=[
            jax.ShapeDtypeStruct((rows, wide), f32),
            jax.ShapeDtypeStruct((rows, wide), bf16),
            jax.ShapeDtypeStruct((rows, 1), f32),
            jax.ShapeDtypeStruct((rows, 1), f32),
            jax.ShapeDtypeStruct((piece_shape[0], layers, *piece_shape[1:]), bf16),
            jax.ShapeDtypeStruct((layers, *part_shape), bf16),
        ],
        in_specs=[ANY] * 4 + [WHOLE] * 4,
        out_specs=[ANY] * 2 + [WHOLE] * 2 + [ANY] * 2,
        scratch_shapes=[
            pltpu.VMEM(a, bf16) for a in (mixed.shape, wo.shape, piece_shape, part_shape)
        ]
        + Scatter.scratch(rows, wide)
        + LineGather.scratch(layers) * 2
        + [sems(4)]
        + Rows.scratch(rows, wide, f32)
        + Rows.scratch(rows, wide, bf16),
        compiler_params=params(number),
        cost_estimate=cost(2 * total * depth * wide),
        name="scatter_attn",
    )(mixed, wo, piece, part, tokens, b_out, gain, shift)


def plain_product(a_buf, w_buf):
    half = w_buf.shape[1] // 2

    def product(role, here, c):
        return dot(a_buf[here, :], w_buf[:, pl.ds(c * half, half)])

    return product


def scatter_fc(cot_all, slope, wp, wf, hidden2, back, grad_proj, proj_cut, layers, number):
    total, depth = cot_all.shape
    rows = total // PLANE
    wide = slope.shape[1]
    tile = 512
    n_wp, n_wf = len(wp), len(wf)
    proj_shape = (proj_cut, grad_proj.shape[2])
    cuts = (0, proj_cut // 64 * 32, proj_cut)

    def kernel(cot_ref, slope_ref, h_ref, proj_ref, *refs):
        wp_refs, wf_refs, refs = refs[:n_wp], refs[n_wp : n_wp + n_wf], refs[n_wp + n_wf :]
        cot_own, residual_ref, mean_ref, inverse_ref, gain_ref = refs[:5]
        grad_residual, grad_attn, sums_ref, bias_ref, gp_ref, dw_ref, proj_out = refs[5:12]
        cot, slopes, wp_buf, wf_buf, gp, h_buf, dw_buf, folds = refs[12:20]
        s, line_refs = refs[20:34], refs[34:50]
        local, wlocal = refs[50:52]
        grad_residual, grad_attn = Rows(grad_residual, *refs[52:54]), Rows(grad_attn, *refs[54:56])
        p = Place()
        proj = [
            LineSum(
                p,
                lambda f, i=i: proj_ref.at[f, pl.ds(cuts[i], cuts[i + 1] - cuts[i]), :],
                layers,
                *line_refs[8 * i : 8 * i + 8],
            )
            for i in range(2)
        ]
        order = (p.dg, p.xn, p.yn, p.me)

        def chip(dev):
            return rows_at(lax.div(dev, 2) * (2 * rows), 2 * rows)

        def fetch(k):
            here = chip(order[k])
            return (
                load(cot_ref.at[here, :], cot.at[k % 2], local.at[k % 2]),
                load(slope_ref.at[here, :], slopes.at[k % 2], local.at[2 + k % 2]),
            )

        fetches = [fetch(0)]
        loads_wp = load_blocks(wp_refs, wp_buf, wlocal)
        loads_wf = load_parts(wf_refs, wf_buf, local.at[pl.ds(4, n_wf)])
        load_h = load(h_ref.at[:, pl.ds(0, tile)], h_buf, local.at[4 + n_wf])
        bias_ref[...] = jnp.zeros_like(bias_ref)
        p.greet(False, layers)
        LineSum.start(*proj)
        for copy in loads_wp:
            copy.wait()
        half = depth // 2

        def back_through_gelu(k):
            for copy in fetches[k]:
                copy.wait()
            if k < 3:
                fetches.append(fetch(k + 1))
            here = chip(order[k])

            @pl.loop(0, wide // 512)
            def _(j):
                cols = rows_at(j * 512, 512)
                grad_act = dot_nt(cot[k % 2], wp_buf[cols, :])
                grad_pre = (grad_act * slopes[k % 2, :, cols].astype(f32)).astype(bf16)
                gp[here, cols] = grad_pre
                bias_ref[:, cols] += jnp.sum(grad_pre.astype(f32), axis=0, keepdims=True)

            if k == 0:
                for copy in loads_wf:
                    copy.wait()

        def product(role, here, c):
            if c == 0:
                back_through_gelu(role)
            return dot_nt(gp[here, :], wf_buf[pl.ds(c * half, half), :])

        def emit(line, value):
            first = line.start == 0
            grad_out = cot_own[line, :].astype(f32)
            back = inverse_ref[line, :]
            normed = (residual_ref[line, :] - mean_ref[line, :]) * back
            result = grad_out + norm_back(value, normed, back, gain_ref[...])
            low = result.astype(bf16)
            grad_residual.put(line, result)
            grad_attn.put(line, low)
            for i, term in enumerate((value * normed, value, low.astype(f32), grad_out)):
                fold(folds.at[i], first, term)

        stores = []

        def last_poll():
            stores.append(load(gp, gp_ref, local.at[5 + n_wf]))
            proj[0].poll()

        def idle():
            load_h.wait()
            dw_buf[...] = dot_tn(h_buf[...], gp[...]).astype(bf16)
            stores.append(load(dw_buf, dw_ref, local.at[6 + n_wf]))
            proj[1].poll()

        Scatter.take(p, rows, s).run(
            product, emit, idle, (proj[0].poll, proj[1].poll, last_poll)
        )
        sums_ref[...] = jnp.sum(folds[...], axis=1)
        for i in range(2):

            def keep(where, value, i=i):
                proj_out[pl.ds(cuts[i] + where.start, where.size), :] = value.astype(bf16)

            proj[i].finish(keep)
        for copy in stores:
            copy.wait()
        grad_residual.finish()
        grad_attn.finish()

    return pl.pallas_call(
        kernel,
        out_shape=[
            jax.ShapeDtypeStruct((rows, depth), f32),
            jax.ShapeDtypeStruct((rows, depth), bf16),
            jax.ShapeDtypeStruct((4, depth), f32),
            jax.ShapeDtypeStruct((1, wide), f32),
            jax.ShapeDtypeStruct((total, wide), bf16),
            jax.ShapeDtypeStruct((tile, wide), bf16),
            jax.ShapeDtypeStruct(proj_shape, bf16),
        ],
        in_specs=[ANY] * (4 + n_wp + n_wf) + [WHOLE] * 5,
        out_specs=[ANY] * 2 + [WHOLE] * 2 + [ANY] * 2 + [WHOLE],
        scratch_shapes=[
            pltpu.VMEM((2, 2 * rows, depth), bf16),
            pltpu.VMEM((2, 2 * rows, wide), bf16),
            pltpu.VMEM((wide, depth), bf16),
            pltpu.VMEM((depth, wide), bf16),
            pltpu.VMEM((total, wide), bf16),
            pltpu.VMEM((total, tile), bf16),
            pltpu.VMEM((tile, wide), bf16),
            pltpu.VMEM((4, 8, depth), f32),
        ]
        + Scatter.scratch(rows, depth)
        + LineSum.scratch((cuts[1], depth), layers)
        + LineSum.scratch((proj_cut - cuts[1], depth), layers)
        + [sems(7 + n_wf), sems(n_wp * layers)]
        + Rows.scratch(rows, depth, f32)
        + Rows.scratch(rows, depth, bf16),
        compiler_params=params(number),
        cost_estimate=cost(6 * total * depth * wide),
        name="scatter_fc",
    )(cot_all, slope, hidden2, grad_proj, *wp, *wf, *back)


LANES = 128


def scatter_query(
    gq, gkv, wq, w_kv, grad_w_query, grad_w_kv, fc_part, back, sums, layers, number
):
    total, cols = gq.shape
    kv_cols = gkv.shape[1]
    rows = total // PLANE
    depth = wq.shape[0]
    wide = depth + kv_cols
    q_shape = (grad_w_query.shape[0], *grad_w_query.shape[2:])
    fc_part, first, last = fc_part
    fc_shape = (last - first, *fc_part.shape[2:])
    my_hidden = sums[1].shape[1]
    places, lines_total = {}, 0
    for name, size in (
        ("ln1_gain", depth),
        ("ln1_bias", depth),
        ("b_query", PLANE * cols),
        ("b_value", kv_cols // 2),
        ("b_out", depth),
        ("ln2_gain", depth),
        ("ln2_bias", depth),
        ("b_fc", PLANE * my_hidden),
        ("b_proj", depth),
    ):
        places[name] = lines_total
        lines_total += size // LANES
    padded = -(-lines_total // (8 * PLANE)) * 8 * PLANE

    def kernel(gq_ref, gkv_ref, wq_ref, wkv_ref, dwq_ref, dwkv_ref, fc_ref, *refs):
        tok_ref, mean_ref, inverse_ref, gain_ref, residual_ref = refs[:5]
        sums2_ref, sums_fc_ref, sums_q_ref, sums_kv_ref = refs[5:9]
        out_ref, vec_ref, dwkv_out, fc_out, dwq_out = refs[9:14]
        g_buf, wq_buf, wkv_buf, dwkv_buf, q_sum, folds = refs[14:20]
        s, line_refs = refs[20:34], refs[34:50]
        qsend, qrecv, local = refs[50:53]
        result = Rows(out_ref, *refs[53:])
        p = Place()

        def pack(at, row):
            for k in range(row.shape[1] // LANES):
                vec_ref[pl.ds(at + k, 1), :] = row[:, k * LANES : (k + 1) * LANES]
        q_side, kv_side = pl.ds(0, cols), pl.ds(cols, kv_cols)
        loads = [
            load(gq_ref, g_buf.at[:, q_side], local.at[0]),
            load(gkv_ref, g_buf.at[:, kv_side], local.at[1]),
            load(wq_ref, wq_buf, local.at[2]),
            load(wkv_ref, wkv_buf, local.at[3]),
            load(dwkv_ref, dwkv_buf, local.at[4]),
        ]
        line_q = LineSum(p, lambda f: dwq_ref.at[:, f], layers, *line_refs[:8])
        line_fc = LineSum(p, lambda f: fc_ref.at[pl.ds(first, last - first), f], layers, *line_refs[8:])
        p.greet(True, layers)
        LineSum.start(line_q, line_fc)
        for copy in loads:
            copy.wait()
        half = wide // 2

        def product(role, here, c):
            where = pl.ds(c * half, min(half, depth - c * half))
            value = dot_nt(g_buf[here, q_side], wq_buf[where, :]) + dot_nt(
                g_buf[here, kv_side], wkv_buf[where, :]
            )
            if c == 0:
                return value
            return jnp.concatenate([value, dwkv_buf[here, :].astype(f32)], axis=1)

        later = []

        def idle():
            def keep(where, value):
                q_sum[where] = value.astype(bf16)

            vec_ref[...] = jnp.zeros_like(vec_ref)
            for i, name in enumerate(("ln2_gain", "ln2_bias", "b_out", "b_proj")):
                pack(places[name], sums2_ref[i : i + 1, :])
            pack(places["b_fc"] + p.me * (my_hidden // LANES), sums_fc_ref[...])
            pack(places["b_query"] + p.me * (cols // LANES), sums_q_ref[...])
            pack(places["b_value"], sums_kv_ref[:, kv_cols // 2 :])
            line_fc.poll()
            line_q.finish(keep)
            later.append(Spread(p, q_sum, dwq_out, qsend, qrecv, local.at[5]))

        def emit(line, value):
            begin = line.start == 0
            grad = value[:, :depth]
            normed = (tok_ref[line, :].astype(f32) - mean_ref[line, :]) * inverse_ref[line, :]
            result.put(
                line,
                residual_ref[line, :]
                + norm_back(grad, normed, inverse_ref[line, :], gain_ref[...]),
            )
            fold(folds.at[0], begin, grad * normed)
            fold(folds.at[1], begin, grad)
            dwkv_out[line, :] = value[:, depth:].astype(bf16)

        def keep_fc(where, value):
            fc_out[where] = value.astype(bf16)

        polls = (line_q.poll, line_fc.poll, line_q.poll)
        Scatter.take(p, rows, s).run(product, emit, idle, polls)
        for i, name in enumerate(("ln1_gain", "ln1_bias")):
            pack(places[name], jnp.sum(folds[i], axis=0, keepdims=True))
        line_fc.finish(keep_fc)
        for item in (*later, result):
            item.finish()

    return pl.pallas_call(
        kernel,
        out_shape=[
            jax.ShapeDtypeStruct((rows, depth), f32),
            jax.ShapeDtypeStruct((padded, LANES), f32),
            jax.ShapeDtypeStruct((rows, kv_cols), bf16),
            jax.ShapeDtypeStruct(fc_shape, bf16),
            jax.ShapeDtypeStruct((q_shape[1], PLANE * q_shape[2]), bf16),
        ],
        in_specs=[ANY] * 7 + [WHOLE] * 9,
        out_specs=[ANY] + [WHOLE] * 3 + [ANY],
        scratch_shapes=[
            pltpu.VMEM((total, cols + kv_cols), bf16),
            pltpu.VMEM(wq.shape, bf16),
            pltpu.VMEM(w_kv.shape, bf16),
            pltpu.VMEM(grad_w_kv.shape, bf16),
            pltpu.VMEM(q_shape, bf16),
            pltpu.VMEM((2, 8, depth), f32),
        ]
        + Scatter.scratch(rows, wide)
        + LineSum.scratch(q_shape, layers)
        + LineSum.scratch(fc_shape, layers)
        + [sems(PLANE)] * 2
        + [sems(6)]
        + Rows.scratch(rows, depth, f32),
        compiler_params=params(number),
        cost_estimate=cost(2 * total * depth * (cols + kv_cols)),
        name="scatter_query",
    )(gq, gkv, wq, w_kv, grad_w_query, grad_w_kv, fc_part, *back, *sums)


def last_exchange(vector, grad_w_kv, fc_parts, layers, number):
    lines = vector.shape[1]
    kv_rows, kv_cols = grad_w_kv.shape[0] // layers, grad_w_kv.shape[1]
    count = len(fc_parts)
    sizes = [a.shape[0] for a in fc_parts]
    fc_rows, fc_cols = fc_parts[0].shape[1:]

    def kernel(vec, kv_ref, *refs):
        fc_refs, (vec_out, kv_out, fc_out), refs = (
            refs[:count],
            refs[count : count + 3],
            refs[count + 3 :],
        )
        pieces, box, plane_sum, zbox, kv_box = refs[:5]
        vsend, vrecv, zsend, zrecv, ksend, krecv, gsend, grecv, send, recv, local = refs[5:]
        p = Place()
        loads, at = [], 0
        for i, ref in enumerate(fc_refs):
            loads.append(load(ref, pieces.at[pl.ds(at, sizes[i])], local.at[i]))
            at += sizes[i]
        p.greet(True, layers)
        plane = PlaneSum(p, vec, box, vsend, vrecv)
        across_kv = []
        for step in range(1, layers):
            to = p.line_peer(step, layers)
            block = kv_ref.at[rows_at(to * kv_rows, kv_rows), :]
            copy = push(block, kv_box.at[step], ksend.at[step], krecv.at[step], {"fsdp": to})
            copy.start()
            across_kv.append(copy)
        for copy in loads:
            copy.wait()
        spread = Spread(p, pieces, fc_out, send, recv, local.at[count])
        total = plane.total()
        plane_sum[...] = total
        zbox[0] = total
        across = []
        for step in range(1, layers):
            to = p.line_peer(step, layers)
            copy = push(plane_sum, zbox.at[step], zsend.at[step], zrecv.at[step], {"fsdp": to})
            copy.start()
            across.append(copy)
        value = kv_ref[rows_at(p.layer * kv_rows, kv_rows), :].astype(f32)
        for step, copy in enumerate(across_kv):
            copy.wait_recv()
            value = value + kv_box[step + 1].astype(f32)
        kv_out[...] = value
        for copy in across:
            copy.wait_recv()
        total = None
        for k in range(layers):
            term = zbox[lax.rem(p.layer - k + layers, layers)]
            total = term if total is None else total + term
        vec_out[p.me] = total
        last = []
        for step in range(1, PLANE):
            to = p.plane_peer(step)
            mine = vec_out.at[p.me]
            last.append(push(mine, mine, gsend.at[step], grecv.at[step], {"seq": to}))
            last[-1].start()
        for copy in last:
            copy.wait()
        spread.finish()
        plane.finish()
        for copy in across + across_kv:
            copy.wait_send()

    return pl.pallas_call(
        kernel,
        out_shape=[
            jax.ShapeDtypeStruct(vector.shape, f32),
            jax.ShapeDtypeStruct((kv_rows, kv_cols), f32),
            jax.ShapeDtypeStruct((fc_rows, PLANE * fc_cols), bf16),
        ],
        in_specs=[WHOLE, WHOLE] + [ANY] * count,
        out_specs=[WHOLE, WHOLE, ANY],
        scratch_shapes=[
            pltpu.VMEM((PLANE, fc_rows, fc_cols), bf16),
            pltpu.VMEM((PLANE, lines, 128), f32),
            pltpu.VMEM((lines, 128), f32),
            pltpu.VMEM((layers, lines, 128), f32),
            pltpu.VMEM((layers, kv_rows, kv_cols), bf16),
        ]
        + [sems(PLANE)] * 2
        + [sems(layers)] * 4
        + [sems(PLANE)] * 4
        + [sems(count + 1)],
        compiler_params=params(number),
        name="last_exchange",
    )(vector, grad_w_kv, *fc_parts)


def starts_of(docs, stream, positions):
    start = jnp.zeros_like(positions)
    for j in range(docs.shape[1]):
        here = docs[stream, j]
        start = jnp.maximum(start, jnp.where(here <= positions, here, 0))
    return start


def masked_scores(docs, stream, keys, q, first, limit):
    scores = dot_nt(keys, q) * (HD**-0.5)
    t = first + lax.broadcasted_iota(jnp.int32, (1, q.shape[0]), 1)
    u = lax.broadcasted_iota(jnp.int32, scores.shape, 0)
    return scores, (u >= starts_of(docs, stream, t)) & (u <= t)


QROWS = 256


def attend_stream(docs, stream, q_ref, kv_ref, mixed_ref, lse_ref, block, heads):
    groups, rows, cols = q_ref.shape
    length = groups * rows
    kv = kv_ref[...].reshape(length, 2 * HD)
    keys = kv[:, :HD]
    values_t = kv[:, HD:].T
    per = block // rows
    for b in range(length // block):
        limit = (b + 1) * block
        q_rows = q_ref[b * per : (b + 1) * per].reshape(block, cols)
        for h in range(heads):
            q = q_rows[:, h * HD : (h + 1) * HD]
            scores, allowed = masked_scores(docs, stream, keys[:limit], q, b * block, limit)
            scores = jnp.where(allowed, scores, -1e30)
            top = jnp.max(scores, axis=0, keepdims=True)
            weights = jnp.exp(scores - top)
            total = jnp.sum(weights, axis=0, keepdims=True)
            mixed = dot(values_t[:, :limit], weights.astype(bf16)) / total
            mixed_ref[b * per : (b + 1) * per, :, h * HD : (h + 1) * HD] = (
                mixed.T.astype(bf16).reshape(per, rows, HD)
            )
            lse_ref[h : h + 1, b * block : (b + 1) * block] = top + jnp.log(total)


def attend_stream_back(docs, stream, q_ref, kv_ref, g_ref, lse_ref, gq_ref, gkv_ref, gk, gv, heads):
    groups, rows, cols = q_ref.shape
    length = groups * rows
    block = min(QROWS, length)
    kv = kv_ref[...].reshape(length, 2 * HD)
    keys, values = kv[:, :HD], kv[:, HD:]
    keys_t = keys.T
    per = block // rows
    gk[...] = jnp.zeros_like(gk)
    gv[...] = jnp.zeros_like(gv)
    for b in range(length // block):
        limit = (b + 1) * block
        q_rows = q_ref[b * per : (b + 1) * per].reshape(block, cols)
        g_rows = g_ref[b * per : (b + 1) * per].reshape(block, cols)
        for h in range(heads):
            q = q_rows[:, h * HD : (h + 1) * HD]
            g = g_rows[:, h * HD : (h + 1) * HD]
            scores, allowed = masked_scores(docs, stream, keys[:limit], q, b * block, limit)
            shift = lse_ref[h : h + 1, b * block : (b + 1) * block]
            probs = jnp.where(allowed, jnp.exp(scores - shift), 0.0)
            grad_probs = dot_nt(values[:limit], g)
            weighted = probs * grad_probs
            delta = jnp.sum(weighted, axis=0, keepdims=True)
            grad_scores = (weighted - probs * delta).astype(bf16)
            gq = dot(keys_t[:, :limit], grad_scores) * (HD**-0.5)
            gq_ref[b * per : (b + 1) * per, :, h * HD : (h + 1) * HD] = (
                gq.T.astype(bf16).reshape(per, rows, HD)
            )
            gk[:limit, :] += dot(grad_scores, q)
            gv[:limit, :] += dot(probs.astype(bf16), g)
    gkv_ref[:, :, :HD] = (gk[...] * (HD**-0.5)).astype(bf16).reshape(groups, rows, HD)
    gkv_ref[:, :, HD:] = gv[...].astype(bf16).reshape(groups, rows, HD)


def attend_back_scatter_proj(
    docs, queries, keyval, grads, lse, act, wp, hidden1, out_part, fc_part, residual, b_proj,
    layers, heads, number
):
    groups, streams, rows, cols = queries.shape
    kv_cols = keyval.shape[3]
    length = groups * rows
    total, depth = act.shape
    own = total // PLANE
    wide = hidden1.shape[1]
    part = hidden1.shape[1] // PLANE
    n_wp = len(wp)
    out_shape = out_part.shape[1:]
    fc_part, first, last = fc_part
    fc_shape = (last - first, *fc_part.shape[2:])

    def kernel(docs_ref, q_ref, kv_ref, g_ref, lse_ref, act_ref, h_ref, dwo_ref, fc_ref, *refs):
        wp_refs, refs = refs[:n_wp], refs[n_wp:]
        residual_ref, bias_ref = refs[:2]
        gq_out, gkv_out, gq_sum, gkv_sum, dwq_out, dwkv_out = refs[2:8]
        out_ref, dwo_out, fc_out = refs[8:11]
        a_buf, w_buf, q_buf, kv_buf, g_buf, grad_buf, gk, gv, h_buf = refs[11:20]
        dwq_buf, dwkv_buf = refs[20:22]
        s, line_refs = refs[22:36], refs[36:52]
        local, wlocal = refs[52:54]
        result = Rows(out_ref, *refs[54:])
        p = Place()
        loads = [load(act_ref, a_buf, local.at[0]), *load_blocks(wp_refs, w_buf, wlocal)]
        line_o = LineSum(p, lambda f: dwo_ref.at[f], layers, *line_refs[:8])
        line_fc = LineSum(p, lambda f: fc_ref.at[pl.ds(first, last - first), f], layers, *line_refs[8:])
        ins = [
            load(q_ref, q_buf, local.at[2]),
            load(kv_ref, kv_buf, local.at[3]),
            load(g_ref, g_buf, local.at[4]),
        ]

        def h_fetch(i):
            here = pl.ds(2 * i * part, 2 * part)
            return load(h_ref.at[:, here], h_buf.at[i % 2], local.at[5 + i % 2])

        tiles = [h_fetch(0)]
        p.greet(False, layers)
        LineSum.start(line_o, line_fc)
        for copy in loads:
            copy.wait()
        stores = []

        def idle():
            for copy in ins:
                copy.wait()
            for stream in range(streams):
                attend_stream_back(
                    docs_ref,
                    stream,
                    q_buf.at[:, stream],
                    kv_buf.at[:, stream],
                    g_buf.at[:, stream],
                    lse_ref.at[stream],
                    grad_buf.at[:, stream, :, pl.ds(0, cols)],
                    grad_buf.at[:, stream, :, pl.ds(cols, kv_cols)],
                    gk,
                    gv,
                    heads,
                )
                if stream == 0:
                    line_fc.poll()
            stores.append(load(grad_buf.at[:, :, :, pl.ds(0, cols)], gq_out, local.at[7]))
            stores.append(load(grad_buf.at[:, :, :, pl.ds(cols, kv_cols)], gkv_out, local.at[8]))
            grad = grad_buf[...].reshape(total, cols + kv_cols)
            sums = jnp.sum(grad.astype(f32), axis=0, keepdims=True)
            gq_sum[...] = sums[:, :cols]
            gkv_sum[...] = sums[:, cols:]
            for i in range(PLANE // 2):
                tiles[i].wait()
                if i + 1 < PLANE // 2:
                    tiles.append(h_fetch(i + 1))
                term = dot_tn(h_buf[i % 2], grad).astype(bf16)
                for k in range(2):
                    lines = term[k * part : (k + 1) * part]
                    dwq_buf[2 * i + k] = lines[:, :cols].reshape(layers, part // layers, cols)
                    dwkv_buf[2 * i + k] = lines[:, cols:]
            stores.append(load(dwq_buf, dwq_out, local.at[9]))
            stores.append(load(dwkv_buf, dwkv_out, local.at[10]))

        def emit(line, value):
            result.put(line, residual_ref[line, :] + value + bias_ref[...])

        def keep_out(where, value):
            dwo_out[where, :] = value

        def keep_fc(where, value):
            fc_out[where] = value.astype(bf16)

        polls = (line_o.poll, line_fc.poll, line_o.poll)
        Scatter.take(p, own, s).run(plain_product(a_buf, w_buf), emit, idle, polls)
        line_o.finish(keep_out)
        line_fc.finish(keep_fc)
        for copy in stores:
            copy.wait()
        result.finish()

    return pl.pallas_call(
        kernel,
        out_shape=[
            jax.ShapeDtypeStruct(queries.shape, bf16),
            jax.ShapeDtypeStruct(keyval.shape, bf16),
            jax.ShapeDtypeStruct((1, cols), f32),
            jax.ShapeDtypeStruct((1, kv_cols), f32),
            jax.ShapeDtypeStruct((PLANE, layers, part // layers, cols), bf16),
            jax.ShapeDtypeStruct((PLANE, part, kv_cols), bf16),
            jax.ShapeDtypeStruct((own, wide), f32),
            jax.ShapeDtypeStruct(out_shape, f32),
            jax.ShapeDtypeStruct(fc_shape, bf16),
        ],
        in_specs=[pl.BlockSpec(memory_space=pltpu.SMEM)]
        + [ANY] * 3
        + [WHOLE]
        + [ANY] * (4 + n_wp)
        + [WHOLE] * 2,
        out_specs=[ANY, ANY, WHOLE, WHOLE, ANY, ANY, ANY] + [WHOLE] * 2,
        scratch_shapes=[
            pltpu.VMEM(act.shape, bf16),
            pltpu.VMEM((depth, wide), bf16),
            pltpu.VMEM(queries.shape, bf16),
            pltpu.VMEM(keyval.shape, bf16),
            pltpu.VMEM(grads.shape, bf16),
            pltpu.VMEM((groups, streams, rows, cols + kv_cols), bf16),
            pltpu.VMEM((length, HD), f32),
            pltpu.VMEM((length, HD), f32),
            pltpu.VMEM((2, total, 2 * part), bf16),
            pltpu.VMEM((PLANE, layers, part // layers, cols), bf16),
            pltpu.VMEM((PLANE, part, kv_cols), bf16),
        ]
        + Scatter.scratch(own, wide)
        + LineSum.scratch(out_shape, layers)
        + LineSum.scratch(fc_shape, layers)
        + [sems(11), sems(n_wp * layers)]
        + Rows.scratch(own, wide, f32),
        compiler_params=params(number),
        cost_estimate=cost(2 * total * depth * wide),
        name="attend_back_scatter_proj",
    )(docs, queries, keyval, grads, lse, act, hidden1, out_part, fc_part, *wp, residual, b_proj)


def finish(copied, cast, packed, vectors):
    n_copy, n_cast, n_vec = len(copied), len(cast), len(vectors)
    count = n_copy + n_cast

    def kernel(*refs):
        ins, packed_ref, refs = refs[:count], refs[count], refs[count + 1 :]
        outs, refs = refs[: count + n_vec], refs[count + n_vec :]
        rooms, wide, parts = refs[:count], refs[count : count + n_cast], refs[count + n_cast : -2]
        load_sem, store_sem = refs[-2:]
        loads = [load(src, room, load_sem.at[i]) for i, (src, room) in enumerate(zip(ins, rooms))]
        stores = []

        def store(src, dst):
            stores.append(load(src, dst, store_sem.at[len(stores)]))

        at = 0
        for part, out in zip(parts, outs[count:]):
            for k in range(part.shape[1] // LANES):
                part[:, k * LANES : (k + 1) * LANES] = packed_ref[at : at + 1, :]
                at += 1
            store(part, out)
        for i in range(n_copy):
            loads[i].wait()
            store(rooms[i], outs[i])
        for i in range(n_cast):
            loads[n_copy + i].wait()
            wide[i][...] = rooms[n_copy + i][...].astype(f32)
            store(wide[i], outs[n_copy + i])
        for copy in stores:
            copy.wait()

    shapes = [(a.shape, a.dtype) for a in copied] + [(a.shape, f32) for a in cast]
    shapes += [((1, size), f32) for size in vectors]
    return pl.pallas_call(
        kernel,
        out_shape=[jax.ShapeDtypeStruct(*shape) for shape in shapes],
        in_specs=[ANY] * count + [WHOLE],
        out_specs=[ANY] * (count + n_vec),
        scratch_shapes=[pltpu.VMEM(a.shape, a.dtype) for a in (*copied, *cast)]
        + [pltpu.VMEM(a.shape, f32) for a in cast]
        + [pltpu.VMEM((1, size), f32) for size in vectors]
        + [sems(count), sems(count + n_vec)],
        compiler_params=pltpu.CompilerParams(vmem_limit_bytes=VMEM_LIMIT),
        name="finish",
    )(*copied, *cast, packed)


def shards(
    tokens,
    doc_starts,
    w_query,
    w_kv,
    w_out,
    w_fc,
    w_proj,
    ln1_gain,
    ln1_bias,
    b_query,
    b_value,
    b_out,
    ln2_gain,
    ln2_bias,
    b_fc,
    b_proj,
    cotangent,
):
    layers = lax.axis_size("fsdp")
    streams, rows, width = tokens.shape
    own = streams * rows
    heads = HEADS // PLANE
    hidden = b_fc.shape[0]
    my_cols = heads * HD
    my_hidden = hidden // PLANE
    total = PLANE * own

    own_tokens = tokens.reshape(own, width)
    cot_low = cotangent.reshape(own, width)

    def row(vector):
        return vector.reshape(1, -1)

    wq_pieces, wf_pieces, low_kv, wo, low_hidden1, mean1, inverse1 = split_weights(
        own_tokens, row(ln1_gain), row(ln1_bias), w_query, w_fc, w_kv, w_out, layers, 1
    )
    proj_rows = w_proj.shape[0]
    wp_half, proj_cut = proj_rows * 3 // 8, proj_rows * 5 // 8

    def rows_together(pieces):
        return pieces.reshape(-1, pieces.shape[-1])

    hidden1, w_kv_all, wq, wf_a = gather_hidden1(
        low_hidden1, low_kv, ((wq_pieces, 0, PLANE), (wf_pieces, 0, 3)), layers, 2
    )
    wq = rows_together(wq)
    cot_all, wf_b, queries, keyval, mixed, lse = project_attend(
        doc_starts, hidden1, wq, w_kv_all, row(b_query), row(b_value), cot_low, (wf_pieces, 3, 7), streams, heads,
        layers, 3
    )
    mixed_rows = mixed.reshape(total, my_cols)
    residual, low_hidden2, mean2, inverse2, wf_c, wp_a = scatter_attn(
        mixed_rows,
        wo,
        own_tokens,
        row(b_out),
        row(ln2_gain),
        row(ln2_bias),
        (wf_pieces, 7, PLANE),
        (w_proj, 0, wp_half),
        layers,
        4,
    )
    wf = [rows_together(w) for w in (wf_a, wf_b, wf_c)]
    hidden2, act_low, slope, grad_w_proj, wp_b = gather_fc(
        low_hidden2, wf, row(b_fc), cot_all, (w_proj, wp_half, proj_rows), layers, 5
    )
    wp = (wp_a, wp_b)
    grad_w_proj = grad_w_proj.reshape(layers, proj_rows, width)
    grad_residual, grad_attn, sums2, my_grad_b_fc, grad_pre, grad_fc_a, shard_proj_a = scatter_fc(
        cot_all,
        slope,
        wp,
        wf,
        hidden2,
        (cot_low, residual, mean2, inverse2, row(ln2_gain)),
        grad_w_proj,
        proj_cut,
        layers,
        6,
    )

    def by_layer(grad):
        return grad.reshape(-1, layers, width // PLANE // layers, my_hidden)

    first_fc = grad_fc_a.shape[0]
    grad_mixed, grad_w_out, grad_fc_rest, shard_proj, fc_a = gather_out(
        grad_attn,
        wo,
        mixed_rows,
        hidden2,
        grad_pre,
        first_fc,
        grad_w_proj,
        shard_proj_a,
        by_layer(grad_fc_a),
        layers,
        7,
    )
    grad_fc_rest = by_layer(grad_fc_rest)
    fc_cut = grad_fc_rest.shape[0] // 2
    (
        gq,
        gkv,
        my_grad_b_query,
        sums_kv,
        grad_w_query,
        grad_w_kv,
        output,
        shard_out,
        fc_b,
    ) = attend_back_scatter_proj(
        doc_starts,
        queries,
        keyval,
        grad_mixed.reshape(PLANE, streams, rows, my_cols),
        lse,
        act_low,
        wp,
        hidden1,
        grad_w_out.reshape(layers, -1, width),
        (grad_fc_rest, 0, fc_cut),
        residual,
        row(b_proj),
        layers,
        heads,
        8,
    )
    input_grad, packed, plane_kv, fc_c, shard_query = scatter_query(
        gq.reshape(total, my_cols),
        gkv.reshape(total, 2 * HD),
        wq,
        w_kv_all,
        grad_w_query,
        grad_w_kv.reshape(width, 2 * HD),
        (grad_fc_rest, fc_cut, grad_fc_rest.shape[0]),
        (own_tokens, mean1, inverse1, row(ln1_gain), grad_residual),
        (sums2, my_grad_b_fc, my_grad_b_query, sums_kv),
        layers,
        9,
    )
    packed, shard_kv, shard_fc = last_exchange(
        packed.reshape(PLANE, -1, LANES), plane_kv, (fc_a, fc_b, fc_c), layers, 10
    )
    vectors = (ln1_gain, ln1_bias, b_query, b_value, b_out, ln2_gain, ln2_bias, b_fc, b_proj)
    output, input_grad, shard_kv, shard_out, shard_proj, shard_query, shard_fc, *sums = finish(
        (output, input_grad, shard_kv, shard_out, shard_proj),
        (shard_query, shard_fc),
        packed.reshape(-1, LANES),
        [v.shape[0] for v in vectors],
    )
    return (
        output.reshape(streams, rows, width),
        input_grad.reshape(streams, rows, width),
        shard_query,
        shard_kv,
        shard_out,
        shard_fc,
        shard_proj,
        *[v.reshape(-1) for v in sums],
    )


def gather_seq(block):
    return lax.all_gather(block, "seq", axis=0, tiled=True)


def scatter_seq(partial):
    return lax.psum_scatter(partial.astype(bf16), "seq", scatter_dimension=0, tiled=True).astype(f32)


def columns_to_rows(part, groups):
    rows = part.shape[0]
    spread = part.reshape(rows, groups, part.shape[1] // groups).transpose(1, 0, 2)
    return lax.all_to_all(spread, "seq", split_axis=0, concat_axis=0, tiled=True)


def column_weight(shard, groups):
    pieces = columns_to_rows(shard, groups)
    full = lax.all_gather(pieces, "fsdp", axis=1, tiled=True)
    return full.reshape(-1, full.shape[2])


def plain_column_grad(grad, groups):
    rows, cols = grad.shape
    kept = lax.psum_scatter(
        grad.astype(bf16).reshape(groups, rows // groups, cols), "fsdp", scatter_dimension=1, tiled=True
    )
    moved = lax.all_to_all(kept, "seq", split_axis=0, concat_axis=0, tiled=True)
    return moved.transpose(1, 0, 2).reshape(moved.shape[1], groups * cols).astype(f32)


def row_weight_grad(grad):
    return lax.psum_scatter(grad.astype(bf16), "fsdp", scatter_dimension=0, tiled=True).astype(f32)


def plain_attend(queries, keyval, starts, groups, streams, rows, heads):
    length = groups * rows
    scale = HD ** (-0.5)
    position = jnp.arange(length, dtype=jnp.int32)
    mixed_list, lse_list = [], []
    for stream in range(streams):
        q = queries[:, stream].reshape(length, heads, HD)
        k = keyval[:, stream, :, :HD].reshape(length, HD)
        v = keyval[:, stream, :, HD:].reshape(length, HD)
        segment = jnp.sum((starts[stream][None, :] <= position[:, None]).astype(jnp.int32), axis=1)
        allowed = (position[None, :] <= position[:, None]) & (segment[None, :] == segment[:, None])
        scores = jnp.einsum("thd,ud->htu", q, k, preferred_element_type=f32) * scale
        scores = jnp.where(allowed[None], scores, -1e30)
        top = jnp.max(scores, axis=-1, keepdims=True)
        lse = top + jnp.log(jnp.sum(jnp.exp(scores - top), axis=-1, keepdims=True))
        probs = jnp.exp(scores - lse).astype(bf16)
        mixed = jnp.einsum("htu,ud->thd", probs, v, preferred_element_type=f32)
        mixed_list.append(mixed.astype(bf16).reshape(groups, rows, heads * HD))
        lse_list.append(lse)
    return jnp.stack(mixed_list, axis=1), lse_list


def plain_attend_back(queries, keyval, grads, lse_list, starts, groups, streams, rows, heads):
    length = groups * rows
    scale = HD ** (-0.5)
    position = jnp.arange(length, dtype=jnp.int32)
    gq_list, gkv_list = [], []
    for stream in range(streams):
        q = queries[:, stream].reshape(length, heads, HD)
        g = grads[:, stream].reshape(length, heads, HD)
        k = keyval[:, stream, :, :HD].reshape(length, HD)
        v = keyval[:, stream, :, HD:].reshape(length, HD)
        segment = jnp.sum((starts[stream][None, :] <= position[:, None]).astype(jnp.int32), axis=1)
        allowed = (position[None, :] <= position[:, None]) & (segment[None, :] == segment[:, None])
        scores = jnp.einsum("thd,ud->htu", q, k, preferred_element_type=f32) * scale
        probs = jnp.exp(jnp.where(allowed[None], scores, -1e30) - lse_list[stream])
        grad_probs = jnp.einsum("thd,ud->htu", g, v, preferred_element_type=f32)
        delta = jnp.sum(probs * grad_probs, axis=-1, keepdims=True)
        gs = (probs * (grad_probs - delta)).astype(bf16)
        gq = jnp.einsum("htu,ud->thd", gs, k, preferred_element_type=f32) * scale
        gk = jnp.einsum("htu,thd->ud", gs, q, preferred_element_type=f32) * scale
        gv = jnp.einsum("htu,thd->ud", probs.astype(bf16), g, preferred_element_type=f32)
        gq_list.append(gq.astype(bf16).reshape(groups, rows, heads * HD))
        gkv_list.append(jnp.concatenate([gk, gv], axis=1).reshape(groups, rows, 2 * HD))
    return jnp.stack(gq_list, axis=1), jnp.stack(gkv_list, axis=1)


def plain_shards(
    tokens,
    doc_starts,
    w_query,
    w_kv,
    w_out,
    w_fc,
    w_proj,
    ln1_gain,
    ln1_bias,
    b_query,
    b_value,
    b_out,
    ln2_gain,
    ln2_bias,
    b_fc,
    b_proj,
    cotangent,
):
    groups = lax.axis_size("seq")
    me = lax.axis_index("seq")
    streams, rows, width = tokens.shape
    own = streams * rows
    heads = HEADS // groups
    hidden = b_fc.shape[0]
    my_cols = heads * HD
    my_hidden = hidden // groups

    wq = column_weight(w_query, groups)
    w_kv_all = gather_seq(lax.all_gather(w_kv, "fsdp", axis=0, tiled=True))
    wo = lax.all_gather(w_out, "fsdp", axis=0, tiled=True)
    wf = column_weight(w_fc, groups)
    wp = lax.all_gather(w_proj, "fsdp", axis=0, tiled=True)
    my_bq = lax.dynamic_slice_in_dim(b_query, me * my_cols, my_cols, 0)
    my_bf = lax.dynamic_slice_in_dim(b_fc, me * my_hidden, my_hidden, 0)

    inputs = tokens.reshape(own, width).astype(f32)
    cot_low = cotangent.reshape(own, width)
    cot_full = cot_low.astype(f32)
    shifted1, normed1, inverse1 = normalize(inputs, ln1_gain, ln1_bias)
    hidden1 = gather_seq(shifted1.astype(bf16))
    queries = (dot(hidden1, wq) + my_bq).astype(bf16).reshape(groups, streams, rows, my_cols)
    value_shift = jnp.concatenate([jnp.zeros((HD,), f32), b_value])
    keyval = (dot(hidden1, w_kv_all) + value_shift).astype(bf16).reshape(groups, streams, rows, 2 * HD)
    mixed, lse = plain_attend(queries, keyval, doc_starts, groups, streams, rows, heads)
    mixed_rows = mixed.reshape(groups * own, my_cols)
    residual = inputs + scatter_seq(dot(mixed_rows, wo)) + b_out
    shifted2, normed2, inverse2 = normalize(residual, ln2_gain, ln2_bias)
    hidden2 = gather_seq(shifted2.astype(bf16))
    cot_all = gather_seq(cot_low)
    pre_act = dot(hidden2, wf) + my_bf
    activated, slope = gelu_pair(pre_act)
    act_low = activated.astype(bf16)
    output = residual + scatter_seq(dot(act_low, wp)) + b_proj

    grad_b_proj = jnp.sum(cot_full, axis=0)
    shard_proj = row_weight_grad(dot_tn(act_low, cot_all))
    grad_pre = (dot_nt(cot_all, wp) * slope).astype(bf16)
    my_grad_b_fc = jnp.sum(grad_pre.astype(f32), axis=0)
    shard_fc = plain_column_grad(dot_tn(hidden2, grad_pre), groups)
    grad_hidden2 = scatter_seq(dot_nt(grad_pre, wf))
    back_second, grad_ln2_gain, grad_ln2_bias = normalize_back(
        grad_hidden2, normed2, inverse2, ln2_gain
    )
    grad_residual = cot_full + back_second
    grad_attn = grad_residual.astype(bf16)
    grad_b_out = jnp.sum(grad_attn.astype(f32), axis=0)
    grad_attn_all = gather_seq(grad_attn)
    shard_out = row_weight_grad(dot_tn(mixed_rows, grad_attn_all))
    grad_mixed = dot_nt(grad_attn_all, wo).astype(bf16).reshape(groups, streams, rows, my_cols)
    gq, gkv = plain_attend_back(
        queries, keyval, grad_mixed, lse, doc_starts, groups, streams, rows, heads
    )
    gq_rows = gq.reshape(groups * own, my_cols)
    gkv_rows = gkv.reshape(groups * own, 2 * HD)
    my_grad_b_query = jnp.sum(gq_rows.astype(f32), axis=0)
    grad_b_value = jnp.sum(gkv_rows[:, HD:], axis=0)
    gkv_low = gkv_rows.astype(bf16)
    shard_query = plain_column_grad(dot_tn(hidden1, gq_rows), groups)
    shard_kv = row_weight_grad(scatter_seq(dot_tn(hidden1, gkv_low)))
    grad_hidden1 = scatter_seq(dot_nt(gq_rows, wq) + dot_nt(gkv_low, w_kv_all))
    back_first, grad_ln1_gain, grad_ln1_bias = normalize_back(
        grad_hidden1, normed1, inverse1, ln1_gain
    )
    input_grad = grad_residual + back_first

    zero = jnp.zeros_like
    grad_b_query = lax.dynamic_update_slice_in_dim(zero(b_query), my_grad_b_query, me * my_cols, 0)
    grad_b_fc = lax.dynamic_update_slice_in_dim(zero(b_fc), my_grad_b_fc, me * my_hidden, 0)
    vectors = (
        grad_ln1_gain,
        grad_ln1_bias,
        grad_b_query,
        grad_b_value,
        grad_b_out,
        grad_ln2_gain,
        grad_ln2_bias,
        grad_b_fc,
        grad_b_proj,
    )
    sums = lax.psum(vectors, ("seq", "fsdp"))
    return (
        output.reshape(streams, rows, width),
        input_grad.reshape(streams, rows, width),
        shard_query,
        shard_kv,
        shard_out,
        shard_fc,
        shard_proj,
        *sums,
    )


def solution(mesh):
    acts = P("fsdp", "seq", None)
    weight = P(("seq", "fsdp"), None)
    return jax.shard_map(
        shards if mesh.shape["seq"] == PLANE else plain_shards,
        mesh=mesh,
        in_specs=(acts, P("fsdp", None)) + (weight,) * 5 + (P(),) * 9 + (acts,),
        out_specs=(acts, acts) + (weight,) * 5 + (P(),) * 9,
        check_vma=False,
    )
```

```python
import functools

import jax
import jax.numpy as jnp
from jax import lax
from jax.experimental import pallas as pl
from jax.experimental.pallas import tpu as pltpu
from jax.sharding import PartitionSpec as P

HEADS = 16
HD = 128

root_two_pi = 0.7978845608028654
cubic_coef = 0.044715
epsilon = 1e-05
f32 = jnp.float32
bf16 = jnp.bfloat16
MESH = pl.DeviceIdType.MESH
ANY = pl.BlockSpec(memory_space=pl.ANY)
WHOLE = pl.BlockSpec(memory_space=pltpu.VMEM)
VMEM_LIMIT = 62 * 1024 * 1024
PLANE = 8


def normalize(values, gain_row, shift_row):
    center = values - jnp.mean(values, axis=-1, keepdims=True)
    inverse = lax.rsqrt(jnp.mean(center * center, axis=-1, keepdims=True) + epsilon)
    normed = center * inverse
    return (normed * gain_row + shift_row, normed, inverse)


def normalize_back(grad_out, normed, inverse, gain_row):
    scaled = grad_out * gain_row
    grad_in = inverse * (
        scaled
        - jnp.mean(scaled, axis=-1, keepdims=True)
        - normed * jnp.mean(scaled * normed, axis=-1, keepdims=True)
    )
    return (grad_in, jnp.sum(grad_out * normed, axis=0), jnp.sum(grad_out, axis=0))


def norm_stats(values):
    mean = jnp.mean(values, axis=-1, keepdims=True)
    center = values - mean
    return mean, lax.rsqrt(jnp.mean(center * center, axis=-1, keepdims=True) + epsilon)


def norm_back(grad_out, normed, inverse, gain_row):
    scaled = grad_out * gain_row
    return inverse * (
        scaled
        - jnp.mean(scaled, axis=-1, keepdims=True)
        - normed * jnp.mean(scaled * normed, axis=-1, keepdims=True)
    )


def gelu_pair(inputs):
    tangent = jnp.tanh(root_two_pi * (inputs + cubic_coef * inputs * inputs * inputs))
    activated = 0.5 * inputs * (1.0 + tangent)
    gradient_slope = 0.5 * (1.0 + tangent) + 0.5 * inputs * (
        1.0 - tangent * tangent
    ) * root_two_pi * (1.0 + 3.0 * cubic_coef * inputs * inputs)
    return (activated, gradient_slope)


def dot(a, b):
    return jnp.dot(a, b, preferred_element_type=f32)


def dot_nt(a, b):
    return lax.dot_general(a, b, (((1,), (1,)), ((), ())), preferred_element_type=f32)


def dot_tn(a, b):
    return lax.dot_general(a, b, (((0,), (0,)), ((), ())), preferred_element_type=f32)


def push(src, dst, send, recv, to):
    return pltpu.make_async_remote_copy(
        src_ref=src, dst_ref=dst, send_sem=send, recv_sem=recv, device_id=to, device_id_type=MESH
    )


def sems(*shape):
    return pltpu.SemaphoreType.DMA(shape)


def rows_at(start, size):
    return pl.ds(pl.multiple_of(start, size), size)


class Place:
    def __init__(self):
        me = lax.axis_index("seq")
        self.me = me
        self.core = lax.rem(me, 2)
        x = lax.rem(lax.div(me, 2), 2)
        y = lax.div(me, 4)
        self.sib = me + 1 - 2 * self.core
        self.xn = me + 2 - 4 * x
        self.yn = me + 4 - 8 * y
        self.dg = me + 2 - 4 * x + 4 - 8 * y
        turn = 1 - 2 * self.core
        self.xs, self.ys, self.ds = self.xn + turn, self.yn + turn, self.dg + turn
        self.layer = lax.axis_index("fsdp")

    def plane_peer(self, step):
        return lax.rem(self.me + step, PLANE)

    def line_peer(self, step, layers):
        return lax.rem(self.layer + step, layers)

    def greet(self, whole_plane=False, layers=1):
        barrier = pltpu.get_barrier_semaphore()
        if whole_plane:
            others = [self.plane_peer(step) for step in range(1, PLANE)]
        else:
            others = [self.sib, self.xn, self.yn]
        for other in others:
            pl.semaphore_signal(barrier, inc=1, device_id={"seq": other}, device_id_type=MESH)
        for step in range(1, layers):
            other = self.line_peer(step, layers)
            pl.semaphore_signal(barrier, inc=1, device_id={"fsdp": other}, device_id_type=MESH)
        pl.semaphore_wait(barrier, len(others) + layers - 1)


class Gather:
    sends = 14
    scratch = [sems(14), sems(PLANE, 2)]

    def __init__(self, place, buf, rows, send, recv):
        self.p, self.buf, self.rows, self.half = place, buf, rows, rows // 2
        self.send_sem, self.recv_sem = send, recv
        self.copies = []

    def piece(self, dev, half):
        return self.buf.at[rows_at(dev * self.rows + half * self.half, self.half), :]

    def pair(self, dev):
        return rows_at(lax.div(dev, 2) * (2 * self.rows), 2 * self.rows)

    def send(self, dev, half, to, src=None):
        k = len(self.copies)
        piece = self.piece(dev, half)
        copy = push(
            piece if src is None else src,
            piece,
            self.send_sem.at[k],
            self.recv_sem.at[dev, half],
            {"seq": to},
        )
        copy.start()
        self.copies.append(copy)

    def arrived(self, dev, half):
        piece = self.piece(dev, half)
        push(
            piece, piece, self.send_sem.at[0], self.recv_sem.at[dev, half], {"seq": self.p.sib}
        ).wait_recv()

    def start(self, own):
        p = self.p
        parts = [own.at[pl.ds(h * self.half, self.half), :] for h in range(2)]
        self.send(p.me, 0, p.yn, parts[0])
        self.send(p.me, 1, p.xn, parts[1])
        self.send(p.me, 1, p.yn, parts[1])
        self.send(p.me, 0, p.xn, parts[0])
        for h in range(2):
            self.send(p.me, h, p.sib, parts[h])

    def relay_first(self):
        p = self.p
        self.arrived(p.yn, 0)
        self.send(p.yn, 0, p.xn)
        self.arrived(p.xn, 1)
        self.send(p.xn, 1, p.yn)
        self.send(p.yn, 0, p.sib)
        self.send(p.xn, 1, p.sib)

    def relay_rest(self):
        p = self.p
        self.arrived(p.xn, 0)
        self.send(p.xn, 0, p.sib)
        self.arrived(p.yn, 1)
        self.send(p.yn, 1, p.sib)

    def relay(self):
        self.relay_first()
        self.relay_rest()

    def have(self, dev):
        self.arrived(dev, 0)
        self.arrived(dev, 1)

    def relay_corner(self):
        p = self.p
        for h in range(2):
            self.arrived(p.dg, h)
            self.send(p.dg, h, p.sib)

    def finish(self):
        for copy in self.copies:
            copy.wait_send()


class Scatter:
    LINES = 32
    CHUNKS = 4

    def __init__(
        self, place, rows, acc, part, sib_out, sib_in, boxes, sib_send, sib_recv, send, recv
    ):
        self.p, self.rows, self.half = place, rows, rows // 2
        self.wide = part.shape[2]
        self.acc, self.part, self.sib_out, self.sib_in = acc, part, sib_out, sib_in
        self.out_d, self.out_x, self.out_y, self.in_d, self.in_x, self.in_y = boxes
        self.sib_send, self.sib_recv, self.send, self.recv = sib_send, sib_recv, send, recv
        self.copies = []

    @staticmethod
    def scratch(rows, wide):
        return [
            pltpu.VMEM((2 * rows, wide // 2), f32),
            pltpu.VMEM((4, rows, wide), f32),
            pltpu.VMEM((4, rows, wide), bf16),
            pltpu.VMEM((4, rows, wide), bf16),
            *[pltpu.VMEM((rows, wide), bf16)] * 6,
            sems(4, 2),
            sems(4, 2),
            sems(14),
            sems(14),
        ]

    @classmethod
    def take(cls, place, rows, refs):
        return cls(place, rows, *refs[:4], refs[4:10], *refs[10:14])

    refs = 14

    def cols(self, c):
        return pl.ds(c * (self.wide // 2), self.wide // 2)

    def swap(self, role, dev, product, c):
        p = self.p
        self.acc[...] = product(role, rows_at(lax.div(dev, 2) * (2 * self.rows), 2 * self.rows), c)
        theirs = rows_at((1 - p.core) * self.rows, self.rows)
        ours = rows_at(p.core * self.rows, self.rows)
        self.sib_out[role, :, self.cols(c)] = self.acc[theirs, :].astype(bf16)
        copy = push(
            self.sib_out.at[role, :, self.cols(c)],
            self.sib_in.at[role, :, self.cols(c)],
            self.sib_send.at[role, c],
            self.sib_recv.at[role, c],
            {"seq": p.sib},
        )
        copy.start()
        self.copies.append(copy)
        self.part[role, :, self.cols(c)] = self.acc[ours, :]
        return copy

    def swap_all(self, role, dev, product):
        return [self.swap(role, dev, product, c) for c in range(2)]

    def add_into(self, dst, role, first, size, more=(), cols=slice(None)):
        lines = self.LINES

        @pl.loop(0, size // lines)
        def _(i):
            line = rows_at(first + i * lines, lines)
            value = self.part[role, line, cols] + self.sib_in[role, line, cols].astype(f32)
            for ref in more:
                value = value + ref[line, cols].astype(f32)
            dst[line, cols] = value.astype(dst.dtype)

    def final(self, start, size):
        line = pl.ds(start, size)
        value = self.part[3, line, :] + self.sib_in[3, line, :].astype(f32)
        return line, value + self.in_x[line, :].astype(f32) + self.in_y[line, :].astype(f32)

    def ship(self, src, dst, h, k, to, cols=slice(None), chunk=None):
        lines = pl.ds(h * self.half, self.half)
        if chunk is not None:
            size = self.half // self.CHUNKS
            lines = pl.ds(h * self.half + chunk * size, size)
        copy = push(
            src.at[lines, cols], dst.at[lines, cols], self.send.at[k], self.recv.at[k], {"seq": to}
        )
        copy.start()
        self.copies.append(copy)
        return copy

    def ship_corner(self, c):
        cols = self.cols(c)
        self.add_into(self.out_d, 0, 0, self.rows, (), cols)
        return (
            self.ship(self.out_d, self.in_d, 0, 2 * c, self.p.xn, cols),
            self.ship(self.out_d, self.in_d, 1, 2 * c + 1, self.p.yn, cols),
        )

    def run(self, product, emit, idle=None, polls=(None, None, None)):
        polls = [poll or (lambda: None) for poll in polls]
        p, rows, half = self.p, self.rows, self.half
        d0 = self.swap(0, p.dg, product, 0)
        d1 = self.swap(0, p.dg, product, 1)
        d0.wait_recv()
        dx0, dy0 = self.ship_corner(0)
        to_x = [self.swap(1, p.xn, product, 0)]
        d1.wait_recv()
        dx1, dy1 = self.ship_corner(1)
        to_x.append(self.swap(1, p.xn, product, 1))
        polls[0]()
        to_y = self.swap_all(2, p.yn, product)
        for copy in to_x:
            copy.wait_recv()
        self.add_into(self.out_x, 1, 0, half)
        x0 = self.ship(self.out_x, self.in_x, 0, 4, p.xn)
        for copy in to_y:
            copy.wait_recv()
        self.add_into(self.out_y, 2, half, half)
        y1 = self.ship(self.out_y, self.in_y, 1, 5, p.yn)
        polls[1]()
        to_me = self.swap_all(3, p.me, product)
        polls[2]()
        size = half // self.CHUNKS
        x1, y0 = [], []
        for copy in (dx0, dx1, dy0, dy1):
            copy.wait_recv()
        for k in range(self.CHUNKS):
            self.add_into(self.out_y, 2, k * size, size, (self.in_d,))
            y0.append(self.ship(self.out_y, self.in_y, 0, 6 + k, p.yn, chunk=k))
            self.add_into(self.out_x, 1, half + k * size, size, (self.in_d,))
            x1.append(
                self.ship(self.out_x, self.in_x, 1, 6 + self.CHUNKS + k, p.xn, chunk=k)
            )
        if idle is not None:
            idle()
        for copy in (*to_me, x0, y1):
            copy.wait_recv()
        for k in range(self.CHUNKS):
            y0[k].wait_recv()
            emit(*self.final(k * size, size))
            x1[k].wait_recv()
            emit(*self.final(half + k * size, size))
        for copy in self.copies:
            copy.wait_send()


class LineGather:
    def __init__(self, place, src, block, layers, send, recv):
        self.me, self.src, self.block, self.layers = place.layer, src, block, layers
        self.send, self.recv = send, recv
        self.step = 0

    @staticmethod
    def scratch(layers):
        return [sems(2 * layers), sems(layers)]

    def copy(self, src, layer, k, to):
        return push(src, self.block(layer), self.send.at[k], self.recv.at[layer], {"fsdp": to})

    def wait_from(self, layer):
        other = lax.rem(self.me + 1, self.layers)
        self.copy(self.block(layer), layer, 0, other).wait_recv()

    def start(self):
        me, top = self.me, self.layers - 1

        @pl.when(me < top)
        def _():
            self.copy(self.src, me, 0, me + 1).start()

        @pl.when(me > 0)
        def _():
            self.copy(self.src, me, self.layers, me - 1).start()

    def poll(self):
        me, top, hop = self.me, self.layers - 1, self.step
        self.step += 1
        below, above = me - 1 - hop, me + 1 + hop

        @pl.when((below >= 0) & (me < top))
        def _():
            self.wait_from(below)
            self.copy(self.block(below), below, hop + 1, me + 1).start()

        @pl.when((above <= top) & (me > 0))
        def _():
            self.wait_from(above)
            self.copy(self.block(above), above, self.layers + hop + 1, me - 1).start()

    def finish(self):
        while self.step < self.layers - 2:
            self.poll()
        me, top = self.me, self.layers - 1

        @pl.when(me == top)
        def _():
            for layer in range(top):
                self.wait_from(layer)

        @pl.when(me == 0)
        def _():
            for layer in range(1, top + 1):
                self.wait_from(layer)

        for hop in range(top):

            @pl.when((hop <= me) & (me < top))
            def _(hop=hop):
                self.copy(self.block(me), me, hop, me + 1).wait_send()

            @pl.when((hop <= top - me) & (me > 0))
            def _(hop=hop):
                self.copy(self.block(me), me, self.layers + hop, me - 1).wait_send()


class LineSum:
    def __init__(self, place, block, layers, own, up, down, us, ur, ds, dr, local):
        self.me, self.block, self.layers = place.layer, block, layers
        self.own, self.up, self.down = own, up, down
        self.us, self.ur, self.ds, self.dr, self.local = us, ur, ds, dr, local
        self.step = 0
        self.loads = [load(block(f), own.at[f], local.at[f]) for f in range(layers)]

    @staticmethod
    def scratch(shape, layers):
        return [
            pltpu.VMEM((layers, *shape), bf16),
            pltpu.VMEM((layers - 1, *shape), bf16),
            pltpu.VMEM((layers - 1, *shape), bf16),
            *[sems(layers)] * 5,
        ]

    refs = 8

    def up_copy(self, src, f, to):
        return push(src, self.up.at[f - 1], self.us.at[f], self.ur.at[f], {"fsdp": to})

    def down_copy(self, src, f, to):
        return push(src, self.down.at[f], self.ds.at[f], self.dr.at[f], {"fsdp": to})

    @staticmethod
    def start(*lines):
        me, top = lines[0].me, lines[0].layers - 1

        @pl.when(me == 0)
        def _():
            for f in range(top, 0, -1):
                for line in lines:
                    line.up_copy(line.block(f), f, 1).start()
            for line in lines:
                line.up[0] = jnp.zeros(line.up.shape[1:], bf16)

        @pl.when(me == top)
        def _():
            for f in range(top):
                for line in lines:
                    line.down_copy(line.block(f), f, top - 1).start()
            for line in lines:
                line.down[top - 1] = jnp.zeros(line.down.shape[1:], bf16)

    def chunks(self):
        shape = self.own.shape[1:]
        size = 1 if len(shape) == 3 else 32
        return shape[0] // size, lambda i: rows_at(i * size, size) if size > 1 else i

    def add(self, box, slot, f):
        count, where = self.chunks()

        @pl.loop(0, count)
        def _(i):
            here = where(i)
            value = box[slot, here].astype(f32) + self.own[f, here].astype(f32)
            box[slot, here] = value.astype(bf16)

    def poll(self):
        top, k = self.layers - 1, self.step
        self.step += 1
        if k == 0:
            for copy in self.loads:
                copy.wait()
        for f in range(2, top + 1):
            at = f - top + 1 + k
            if not 1 <= at < f:
                continue

            @pl.when(self.me == at)
            def _(f=f, at=at):
                self.up_copy(self.up.at[f - 1], f, at + 1).wait_recv()
                self.add(self.up, f - 1, f)
                self.up_copy(self.up.at[f - 1], f, at + 1).start()

            @pl.when(self.me == top - at)
            def _(f=top - f, at=top - at):
                self.down_copy(self.down.at[f], f, at - 1).wait_recv()
                self.add(self.down, f, f)
                self.down_copy(self.down.at[f], f, at - 1).start()

    def finish(self, emit):
        while self.step < self.layers - 2:
            self.poll()
        me, top = self.me, self.layers - 1

        @pl.when(me > 0)
        def _():
            self.up_copy(self.up.at[me - 1], me, me - 1).wait_recv()

        @pl.when(me < top)
        def _():
            self.down_copy(self.down.at[me], me, me + 1).wait_recv()

        count, where = self.chunks()
        below, above = jnp.maximum(me - 1, 0), jnp.minimum(me, top - 1)

        @pl.loop(0, count)
        def _(i):
            here = where(i)
            value = self.up[below, here].astype(f32) + self.down[above, here].astype(f32)
            emit(here, value + self.own[me, here].astype(f32))

        for f in range(1, top + 1):

            @pl.when(me < f)
            def _(f=f):
                self.up_copy(self.up.at[f - 1], f, me + 1).wait_send()

        for f in range(top):

            @pl.when(me > f)
            def _(f=f):
                self.down_copy(self.down.at[f], f, me - 1).wait_send()


class PlaneSum:
    def __init__(self, place, src, box, send, recv):
        self.p, self.src, self.box = place, src, box
        self.copies = []
        for step in range(1, PLANE):
            to = place.plane_peer(step)
            copy = push(src.at[to], box.at[step], send.at[step], recv.at[step], {"seq": to})
            copy.start()
            self.copies.append(copy)

    def total(self):
        value = self.src[self.p.me].astype(f32)
        for step, copy in enumerate(self.copies):
            copy.wait_recv()
            value = value + self.box[step + 1].astype(f32)
        return value

    def finish(self):
        for copy in self.copies:
            copy.wait_send()


class Spread:
    def __init__(self, place, src, out, send, recv, local, room=None):
        cols = src.shape[2]
        spot = out.at[:, rows_at(place.me * cols, cols)]
        if room is None:
            self.copies = [load(src.at[place.me], spot, local)]
        else:
            self.copies = [Through(src.at[place.me], room, spot, local)]
        for step in range(1, PLANE):
            to = place.plane_peer(step)
            copy = push(src.at[to], spot, send.at[step], recv.at[step], {"seq": to})
            copy.start()
            self.copies.append(copy)

    def finish(self):
        for copy in self.copies:
            copy.wait()


def fold(ref, first, value):
    rows, wide = value.shape
    total = jnp.sum(value.reshape(rows // 8, 8, wide), axis=0)
    ref[...] = total if first else ref[...] + total


class Rows:
    @staticmethod
    def scratch(rows, wide, dtype):
        return [pltpu.VMEM((rows, wide), dtype), sems(2 * Scatter.CHUNKS)]

    def __init__(self, out, stage, sem):
        self.out, self.stage, self.sem = out, stage, sem
        self.copies = []

    def put(self, line, value):
        self.stage[line, :] = value.astype(self.stage.dtype)
        self.copies.append(
            load(self.stage.at[line, :], self.out.at[line, :], self.sem.at[len(self.copies)])
        )

    def finish(self):
        for copy in self.copies:
            copy.wait()


def params(number, vmem=True):
    return pltpu.CompilerParams(
        collective_id=number,
        has_side_effects=True,
        vmem_limit_bytes=VMEM_LIMIT if vmem else None,
    )


def cost(flops, mib=40):
    return pl.CostEstimate(flops=flops, bytes_accessed=mib * 1024 * 1024, transcendentals=0)


def load(src, dst, sem):
    copy = pltpu.make_async_copy(src, dst, sem)
    copy.start()
    return copy


class Through:
    def __init__(self, src, room, dst, sem):
        self.room, self.dst, self.sem = room, dst, sem
        self.copy = load(src, room, sem)

    def put(self):
        self.copy.wait()
        self.copy = load(self.room, self.dst, self.sem)

    def wait(self):
        self.copy.wait()


def rows_of(ref, rows):
    return lambda k: ref.at[rows_at(k * rows, rows), :]


def front(
    docs, tokens, gain, shift, w_query, w_fc, w_kv, w_out, cot, bq, bv, cut, streams, heads, layers, number
):
    own_rows, depth = tokens.shape
    total = PLANE * own_rows
    cols = w_query.shape[1] // PLANE
    kv_cols = w_kv.shape[1]
    rows = own_rows // streams
    length = PLANE * rows
    block = min(QROWS, length)
    piece_rows = w_query.shape[0]
    hidden = w_fc.shape[1] // PLANE
    wo_rows = w_out.shape[0]
    cuts = (0, cut // 2, cut)

    def kernel(docs_ref, tok_ref, gain_ref, shift_ref, bq_ref, bv_ref, *refs):
        wq_ref, wf_ref, wkv_ref, wo_ref, cot_ref = refs[:5]
        h_all, kv_all, cot_all, q_out, k_out, mixed_out = refs[5:11]
        wq_all, wo_all, wf_out, wfa_all, wfb_all, lse_ref, mean_out, inverse_out = refs[11:19]
        h_buf, low_kv, kv_full, wq_own, wq_buf, wf_own, wo_room, cot_room = refs[19:27]
        q_buf, kv_buf, mixed_buf = refs[27:30]
        hs, hr, ks, kr, cs, cr = refs[30:36]
        line_refs, (qsend, qrecv, fsend, frecv, local) = refs[36:46], refs[46:]
        p = Place()

        def column_block(ref, dev):
            wide = ref.shape[1] // PLANE
            return ref.at[:, rows_at(dev * wide, wide)]

        my_pieces = [
            load(column_block(wq_ref, p.me), wq_own.at[p.me], local.at[0]),
            load(column_block(wf_ref, p.me), wf_own.at[p.me], local.at[1]),
        ]
        my_kv = load(wkv_ref, low_kv.at[rows_at(p.layer * piece_rows, piece_rows), :], local.at[2])
        own = [
            Through(wo_ref, wo_room, rows_of(wo_all, wo_rows)(p.layer), local.at[3]),
            Through(cot_ref, cot_room, rows_of(cot_all, own_rows)(p.me), local.at[4]),
        ]
        line_kv = LineGather(p, wkv_ref, rows_of(low_kv, piece_rows), layers, *line_refs[:2])
        line_wo = LineGather(p, wo_ref, rows_of(wo_all, wo_rows), layers, *line_refs[2:4])
        line_wq = LineGather(p, wq_own, lambda k: wq_buf.at[:, k], layers, *line_refs[4:6])
        wf_alls = (wfa_all, wfb_all)
        lines_wf = [
            LineGather(
                p,
                wf_own.at[pl.ds(cuts[i], cuts[i + 1] - cuts[i])],
                lambda k, i=i: wf_alls[i].at[:, k],
                layers,
                *line_refs[6 + 2 * i : 8 + 2 * i],
            )
            for i in range(2)
        ]
        p.greet(True, layers)
        line_kv.start()
        line_wo.start()

        def split(ref, out, send, recv):
            copies = []
            for step in range(1, PLANE):
                to = p.plane_peer(step)
                copies.append(
                    push(
                        column_block(ref, to),
                        out.at[p.me],
                        send.at[step],
                        recv.at[step],
                        {"seq": to},
                    )
                )
                copies[-1].start()
            return copies

        split_q = split(wq_ref, wq_own, qsend, qrecv)
        split_f = split(wf_ref, wf_own, fsend, frecv)

        @pl.loop(0, own_rows // 32)
        def _(i):
            here = rows_at(i * 32, 32)
            values = tok_ref[here, :].astype(f32)
            mean, inverse = norm_stats(values)
            h_buf[rows_at(p.me * own_rows + i * 32, 32), :] = (
                (values - mean) * inverse * gain_ref[...] + shift_ref[...]
            ).astype(bf16)
            mean_out[here, :] = mean
            inverse_out[here, :] = inverse

        g = Gather(p, h_buf, own_rows, hs, hr)
        g.start(h_buf.at[rows_at(p.me * own_rows, own_rows), :])
        for copy in own:
            copy.put()
        line_kv.poll()
        for copy in (*my_pieces, my_kv):
            copy.wait()
        for copy in split_q:
            copy.wait_recv()
        line_wq.start()
        stores = [load(wq_own, wq_buf.at[:, p.layer], local.at[5])]
        line_kv.poll()
        line_wo.poll()
        line_kv.finish()
        kv_rows = layers * piece_rows
        stores.append(load(low_kv, kv_full.at[rows_at(p.me * kv_rows, kv_rows), :], local.at[6]))
        gkv = Gather(p, kv_full, kv_rows, ks, kr)
        gkv.start(low_kv)
        line_wq.poll()
        for copy in split_f:
            copy.wait_recv()
        stores.append(load(wf_own, wf_out, local.at[7]))
        for i in range(2):
            here = pl.ds(cuts[i], cuts[i + 1] - cuts[i])
            stores.append(load(wf_own.at[here], wf_alls[i].at[:, p.layer], local.at[8 + i]))
        line_wo.poll()
        line_wq.poll()
        for line in lines_wf:
            line.start()
        g.relay_first()
        g.relay_rest()
        gkv.relay()
        gc = Gather(p, cot_all, own_rows, cs, cr)
        gc.start(cot_ref)
        lines_wf[0].poll()
        line_wq.finish()
        line_wo.finish()
        for copy in stores[:2]:
            copy.wait()
        stores.append(load(wq_buf, wq_all, local.at[10]))

        def project(dev, k):
            here = g.pair(dev)
            stores.append(load(h_buf.at[here, :], h_all.at[here, :], local.at[11 + k]))
            q = dot(h_buf[here, :], wq_buf[...].reshape(depth, cols))
            q = q + bq_ref[:, rows_at(p.me * cols, cols)]
            chip = rows_at(lax.div(dev, 2) * 2, 2)
            q_buf[chip] = q.astype(bf16).reshape(2, streams, rows, cols)

        g.have(p.sib)
        project(p.me, 0)
        g.have(p.xs)
        project(p.xn, 1)
        g.have(p.ys)
        project(p.yn, 2)
        lines_wf[1].poll()
        g.relay_corner()
        g.have(p.ds)
        project(p.dg, 3)
        stores.append(load(q_buf, q_out, local.at[15]))
        gkv.relay_corner()
        for dev in (p.sib, p.xs, p.ys, p.ds):
            gkv.have(dev)
        stores.append(load(kv_full, kv_all, local.at[16]))
        for k in range(4):
            kv = dot(h_buf[pl.ds(k * total // 4, total // 4), :], kv_full[...])
            kv = jnp.concatenate([kv[:, :HD], kv[:, HD:] + bv_ref[...]], axis=1)
            kv_buf[pl.ds(2 * k, 2)] = kv.astype(bf16).reshape(2, streams, rows, kv_cols)
        stores.append(load(kv_buf, k_out, local.at[17]))
        lines_wf[0].poll()
        for stream in range(streams):
            attend_stream(
                docs_ref,
                stream,
                q_buf.at[:, stream],
                kv_buf.at[:, stream],
                mixed_buf.at[:, stream],
                lse_ref.at[stream],
                block,
                heads,
            )
            if stream == 0:
                gc.relay_first()
                lines_wf[1].poll()
        stores.append(load(mixed_buf, mixed_out, local.at[18]))
        gc.relay_rest()
        gc.relay_corner()
        for dev in (p.sib, p.xs, p.ys, p.ds):
            gc.have(dev)
        for item in (g, gkv, gc, *lines_wf):
            item.finish()
        for copy in (*split_q, *split_f):
            copy.wait_send()
        for copy in (*own, *stores[2:]):
            copy.wait()

    q_shape = (PLANE, streams, rows, cols)
    kv_shape = (PLANE, streams, rows, kv_cols)
    wq_shape = (PLANE, layers, piece_rows, cols)
    wf_shape = (PLANE, piece_rows, hidden)
    half = [(cuts[i + 1] - cuts[i], layers, piece_rows, hidden) for i in range(2)]
    return pl.pallas_call(
        kernel,
        out_shape=[
            jax.ShapeDtypeStruct((total, depth), bf16),
            jax.ShapeDtypeStruct((depth, kv_cols), bf16),
            jax.ShapeDtypeStruct((total, cot.shape[1]), bf16),
            jax.ShapeDtypeStruct(q_shape, bf16),
            jax.ShapeDtypeStruct(kv_shape, bf16),
            jax.ShapeDtypeStruct(q_shape, bf16),
            jax.ShapeDtypeStruct(wq_shape, bf16),
            jax.ShapeDtypeStruct((layers * wo_rows, w_out.shape[1]), bf16),
            jax.ShapeDtypeStruct(wf_shape, bf16),
            jax.ShapeDtypeStruct(half[0], bf16),
            jax.ShapeDtypeStruct(half[1], bf16),
            jax.ShapeDtypeStruct((streams, heads, length), f32),
            jax.ShapeDtypeStruct((own_rows, 1), f32),
            jax.ShapeDtypeStruct((own_rows, 1), f32),
        ],
        in_specs=[pl.BlockSpec(memory_space=pltpu.SMEM)] + [WHOLE] * 5 + [ANY] * 5,
        out_specs=[ANY] * 11 + [WHOLE] * 3,
        scratch_shapes=[
            pltpu.VMEM((total, depth), bf16),
            pltpu.VMEM((layers * piece_rows, kv_cols), bf16),
            pltpu.VMEM((depth, kv_cols), bf16),
            pltpu.VMEM((PLANE, piece_rows, cols), bf16),
            pltpu.VMEM(wq_shape, bf16),
            pltpu.VMEM(wf_shape, bf16),
            pltpu.VMEM(w_out.shape, bf16),
            pltpu.VMEM(cot.shape, bf16),
            pltpu.VMEM(q_shape, bf16),
            pltpu.VMEM(kv_shape, bf16),
            pltpu.VMEM(q_shape, bf16),
        ]
        + Gather.scratch * 3
        + LineGather.scratch(layers) * 5
        + [sems(PLANE)] * 4
        + [sems(19)],
        compiler_params=params(number),
        cost_estimate=cost(2 * total * depth * (cols + kv_cols)),
        name="front",
    )(docs, tokens, gain, shift, bq, bv, w_query, w_fc, w_kv, w_out, cot)


def load_parts(parts, dst, local):
    copies, at = [], 0
    for i, part in enumerate(parts):
        rows = part.shape[0]
        copies.append(load(part, dst.at[pl.ds(at, rows), :], local.at[i]))
        at += rows
    return copies


def load_blocks(parts, dst, local):
    copies, at = [], 0
    for layer in range(parts[0].shape[0]):
        for part in parts:
            rows = part.shape[1]
            copies.append(load(part.at[layer], dst.at[pl.ds(at, rows), :], local.at[len(copies)]))
            at += rows
    return copies


def gather_fc(hidden2, wf, bf, cot_all, part, layers, number):
    part, first, last = part
    part_shape = (last - first, part.shape[1])
    rows, depth = hidden2.shape
    wide = wf[0].shape[1]
    n_wf = len(wf)
    total = PLANE * rows
    out_wide = cot_all.shape[1]
    tile = 256

    def kernel(own_ref, b_ref, cot_ref, part_ref, *refs):
        w_refs, refs = refs[:n_wf], refs[n_wf:]
        all_ref, act_ref, slope_ref, dw_ref, line_all = refs[:5]
        buf, w_buf, act, slope, cot, acc, dw, room, send, recv, zsend, zrecv, local, wlocal = refs[
            5:
        ]
        p = Place()
        part_ref = part_ref.at[pl.ds(first, last - first), :]
        load_own = load(own_ref, buf.at[rows_at(p.me * rows, rows), :], local.at[0])
        loads_w = load_parts(w_refs, w_buf, wlocal)
        own_line = Through(part_ref, room, line_all.at[p.layer], local.at[1])
        line = LineGather(p, part_ref, lambda k: line_all.at[k], layers, zsend, zrecv)
        p.greet(False, layers)
        g = Gather(p, buf, rows, send, recv)
        g.start(own_ref)
        line.start()
        own_line.put()
        stores = []
        cots = {}

        def fetch(k, dev):
            cots[k] = load(cot_ref.at[g.pair(dev), :], cot.at[k % 2], local.at[2 + k % 2])

        def work(k, dev):
            block = g.pair(dev)
            stores.append(load(buf.at[block, :], all_ref.at[block, :], local.at[4 + 3 * k]))

            @pl.loop(0, wide // 512)
            def _(j):
                cols = rows_at(j * 512, 512)
                bias = b_ref[:, rows_at(p.me * wide + j * 512, 512)]
                acc_fc = dot(buf[block, :], w_buf[:, cols]) + bias
                activated, gradient = gelu_pair(acc_fc)
                act[block, cols] = activated.astype(bf16)
                slope[block, cols] = gradient.astype(bf16)

            for i, (src, dst) in enumerate(((act, act_ref), (slope, slope_ref))):
                stores.append(
                    load(src.at[block, :], dst.at[block, :], local.at[4 + 3 * k + 1 + i])
                )

        def grads(k, dev):
            block = g.pair(dev)
            cots[k].wait()

            for j in range(wide // tile):
                cols = pl.ds(j * tile, tile)
                term = dot_tn(act[block, cols], cot[k % 2])
                if k == 0:
                    acc[cols, :] = term
                elif k < 3:
                    acc[cols, :] += term
                else:
                    dw[cols, :] = (acc[cols, :] + term).astype(bf16)
                    stores.append(load(dw.at[cols, :], dw_ref.at[cols, :], local.at[16 + j]))

        fetch(0, p.me)
        fetch(1, p.xn)
        load_own.wait()
        for copy in loads_w:
            copy.wait()
        g.have(p.sib)
        work(0, p.me)
        g.relay_first()
        grads(0, p.me)
        line.poll()
        fetch(2, p.yn)
        g.relay_rest()
        g.have(p.xs)
        work(1, p.xn)
        g.have(p.ys)
        work(2, p.yn)
        line.poll()
        grads(1, p.xn)
        fetch(3, p.dg)
        g.relay_corner()
        grads(2, p.yn)
        g.have(p.ds)
        work(3, p.dg)
        grads(3, p.dg)
        g.finish()
        line.finish()
        own_line.wait()
        for copy in stores:
            copy.wait()

    return pl.pallas_call(
        kernel,
        out_shape=[
            jax.ShapeDtypeStruct((total, depth), bf16),
            jax.ShapeDtypeStruct((total, wide), bf16),
            jax.ShapeDtypeStruct((total, wide), bf16),
            jax.ShapeDtypeStruct((wide, out_wide), bf16),
            jax.ShapeDtypeStruct((layers, *part_shape), bf16),
        ],
        in_specs=[ANY, WHOLE] + [ANY] * (2 + n_wf),
        out_specs=[ANY] * 5,
        scratch_shapes=[
            pltpu.VMEM((total, depth), bf16),
            pltpu.VMEM((depth, wide), bf16),
            pltpu.VMEM((total, wide), bf16),
            pltpu.VMEM((total, wide), bf16),
            pltpu.VMEM((2, 2 * rows, out_wide), bf16),
            pltpu.VMEM((wide, out_wide), f32),
            pltpu.VMEM((wide, out_wide), bf16),
            pltpu.VMEM(part_shape, bf16),
        ]
        + Gather.scratch
        + LineGather.scratch(layers)
        + [sems(16 + wide // tile), sems(n_wf)],
        compiler_params=params(number),
        cost_estimate=cost(4 * total * depth * wide),
        name="gather_fc",
    )(hidden2, bf, cot_all, part, *wf)


def gather_out(
    grad_attn, wo, mixed, hidden2, grad_pre, first_fc, grad_proj, proj_done, fc_part, layers, number
):
    rows, depth = grad_attn.shape
    wide = wo.shape[0]
    total = PLANE * rows
    hidden = grad_pre.shape[1]
    tile = 512
    steps = (depth - first_fc) // tile
    proj_cut = proj_done.shape[0]
    proj_shape = (grad_proj.shape[1] - proj_cut, grad_proj.shape[2])
    fc_shape = (fc_part.shape[0], *fc_part.shape[2:])

    def kernel(own_ref, w_ref, mixed_ref, h_ref, gp_ref, proj_ref, fc_ref, done_ref, *refs):
        gm_ref, dw_ref, dwfc_ref, proj_out, fc_out = refs[:5]
        buf, w_buf, mixed_buf, gm, acc, dw, gp, h_buf, dwfc = refs[5:14]
        send, recv = refs[14:16]
        line_refs = refs[16:32]
        (local,) = refs[32:]
        p = Place()
        load_own = load(own_ref, buf.at[rows_at(p.me * rows, rows), :], local.at[0])
        loads = [load(w_ref, w_buf, local.at[1]), load(mixed_ref, mixed_buf, local.at[2])]
        load_gp = load(gp_ref, gp, local.at[3])
        proj = LineSum(p, lambda f: proj_ref.at[f, pl.ds(proj_cut, proj_shape[0]), :], layers, *line_refs[:8])
        fc = LineSum(p, lambda f: fc_ref.at[:, f], layers, *line_refs[8:])

        def h_fetch(i):
            here = pl.ds(first_fc + i * tile, tile)
            return load(h_ref.at[:, here], h_buf.at[i % 2], local.at[4 + i % 2])

        tiles = [h_fetch(0)]
        stores = []
        p.greet(False, layers)
        g = Gather(p, buf, rows, send, recv)
        g.start(own_ref)
        LineSum.start(proj, fc)

        def work(dev):
            block = g.pair(dev)
            gm[block, :] = dot_nt(buf[block, :], w_buf[...]).astype(bf16)

        def grads(k, dev):
            block = g.pair(dev)
            term = dot_tn(mixed_buf[block, :], buf[block, :])
            if k == 0:
                acc[...] = term
            elif k < 3:
                acc[...] += term
            else:
                dw[...] = (acc[...] + term).astype(bf16)

        def fc_grads(i):
            tiles[i].wait()
            if i + 1 < steps:
                tiles.append(h_fetch(i + 1))
            if i >= 2:
                stores[i - 2].wait()
            dwfc[i % 2] = dot_tn(h_buf[i % 2], gp[...]).astype(bf16)
            stores.append(
                load(dwfc.at[i % 2], dwfc_ref.at[pl.ds(i * tile, tile), :], local.at[6 + i % 2])
            )

        load_own.wait()
        for copy in loads:
            copy.wait()
        g.have(p.sib)
        work(p.me)
        grads(0, p.me)
        for i in range(0, proj_cut, 32):
            proj_out[pl.ds(i, 32), :] = done_ref[pl.ds(i, 32), :].astype(f32)
        load_gp.wait()
        fc_grads(0)
        proj.poll()
        g.relay_first()
        fc_grads(1)
        fc.poll()
        for i in range(2, steps):
            fc_grads(i)
        proj.poll()
        g.relay_rest()
        fc.poll()
        g.have(p.xs)
        work(p.xn)
        g.have(p.ys)
        work(p.yn)
        grads(1, p.xn)
        g.relay_corner()
        grads(2, p.yn)
        g.have(p.ds)
        work(p.dg)
        store = load(gm, gm_ref, local.at[8])
        grads(3, p.dg)
        store_dw = load(dw, dw_ref, local.at[9])
        g.finish()

        def keep_proj(where, value):
            proj_out[pl.ds(proj_cut + where.start, where.size), :] = value

        def keep_fc(where, value):
            fc_out[where] = value.astype(bf16)

        proj.finish(keep_proj)
        fc.finish(keep_fc)
        store.wait()
        store_dw.wait()
        for copy in stores[-2:]:
            copy.wait()

    return pl.pallas_call(
        kernel,
        out_shape=[
            jax.ShapeDtypeStruct((total, wide), bf16),
            jax.ShapeDtypeStruct((wide, depth), bf16),
            jax.ShapeDtypeStruct((depth - first_fc, hidden), bf16),
            jax.ShapeDtypeStruct(grad_proj.shape[1:], f32),
            jax.ShapeDtypeStruct(fc_shape, bf16),
        ],
        in_specs=[ANY] * 7 + [WHOLE],
        out_specs=[ANY] * 3 + [WHOLE] * 2,
        scratch_shapes=[
            pltpu.VMEM((total, depth), bf16),
            pltpu.VMEM(wo.shape, bf16),
            pltpu.VMEM(mixed.shape, bf16),
            pltpu.VMEM((total, wide), bf16),
            pltpu.VMEM((wide, depth), f32),
            pltpu.VMEM((wide, depth), bf16),
            pltpu.VMEM(grad_pre.shape, bf16),
            pltpu.VMEM((2, total, tile), bf16),
            pltpu.VMEM((2, tile, hidden), bf16),
        ]
        + Gather.scratch
        + LineSum.scratch(proj_shape, layers)
        + LineSum.scratch(fc_shape, layers)
        + [sems(10)],
        compiler_params=params(number),
        cost_estimate=cost(4 * total * depth * wide),
        name="gather_out",
    )(grad_attn, wo, mixed, hidden2, grad_pre, grad_proj, fc_part, proj_done)


def scatter_attn(mixed, wo, tokens, b_out, gain, shift, piece, part, layers, number):
    piece, piece_first, piece_last = piece
    piece_shape = (piece_last - piece_first, *piece.shape[1:])
    part, part_first, part_last = part
    part_shape = (part_last - part_first, part.shape[1])
    total, depth = mixed.shape
    rows = total // PLANE
    wide = wo.shape[1]

    def kernel(a_ref, w_ref, piece_ref, part_ref, tok_ref, bias_ref, gain_ref, shift_ref, *refs):
        residual, hidden, mean_out, inverse_out, piece_all, part_all = refs[:6]
        a_buf, w_buf, piece_room, part_room = refs[6:10]
        s, line_refs, local = refs[10:24], refs[24:28], refs[28]
        residual, hidden = Rows(residual, *refs[29:31]), Rows(hidden, *refs[31:33])
        p = Place()
        piece_ref = piece_ref.at[pl.ds(piece_first, piece_shape[0])]
        part_ref = part_ref.at[pl.ds(part_first, part_shape[0]), :]
        loads = [load(a_ref, a_buf, local.at[0]), load(w_ref, w_buf, local.at[1])]
        own = [
            Through(piece_ref, piece_room, piece_all.at[:, p.layer], local.at[2]),
            Through(part_ref, part_room, part_all.at[p.layer], local.at[3]),
        ]
        lines = [
            LineGather(p, piece_ref, lambda k: piece_all.at[:, k], layers, *line_refs[:2]),
            LineGather(p, part_ref, lambda k: part_all.at[k], layers, *line_refs[2:]),
        ]
        p.greet(False, layers)
        for line in lines:
            line.start()
        for copy in loads:
            copy.wait()

        def emit(line, value):
            values = tok_ref[line, :].astype(f32) + value + bias_ref[...]
            mean, inverse = norm_stats(values)
            residual.put(line, values)
            hidden.put(line, (values - mean) * inverse * gain_ref[...] + shift_ref[...])
            mean_out[line, :] = mean
            inverse_out[line, :] = inverse

        def settle():
            for copy in own:
                copy.put()
            lines[0].poll()

        def idle():
            lines[1].poll()
            lines[0].poll()
            lines[1].poll()

        Scatter.take(p, rows, s).run(
            plain_product(a_buf, w_buf), emit, idle, (settle, None, None)
        )
        for line in lines:
            line.finish()
        for item in (*own, residual, hidden):
            item.finish() if isinstance(item, Rows) else item.wait()

    return pl.pallas_call(
        kernel,
        out_shape=[
            jax.ShapeDtypeStruct((rows, wide), f32),
            jax.ShapeDtypeStruct((rows, wide), bf16),
            jax.ShapeDtypeStruct((rows, 1), f32),
            jax.ShapeDtypeStruct((rows, 1), f32),
            jax.ShapeDtypeStruct((piece_shape[0], layers, *piece_shape[1:]), bf16),
            jax.ShapeDtypeStruct((layers, *part_shape), bf16),
        ],
        in_specs=[ANY] * 4 + [WHOLE] * 4,
        out_specs=[ANY] * 2 + [WHOLE] * 2 + [ANY] * 2,
        scratch_shapes=[
            pltpu.VMEM(a, bf16) for a in (mixed.shape, wo.shape, piece_shape, part_shape)
        ]
        + Scatter.scratch(rows, wide)
        + LineGather.scratch(layers) * 2
        + [sems(4)]
        + Rows.scratch(rows, wide, f32)
        + Rows.scratch(rows, wide, bf16),
        compiler_params=params(number),
        cost_estimate=cost(2 * total * depth * wide),
        name="scatter_attn",
    )(mixed, wo, piece, part, tokens, b_out, gain, shift)


def plain_product(a_buf, w_buf):
    half = w_buf.shape[1] // 2

    def product(role, here, c):
        return dot(a_buf[here, :], w_buf[:, pl.ds(c * half, half)])

    return product


def scatter_fc(cot_all, slope, wp, wf, hidden2, back, grad_proj, proj_cut, layers, number):
    total, depth = cot_all.shape
    rows = total // PLANE
    wide = slope.shape[1]
    tile = 512
    n_wp, n_wf = len(wp), len(wf)
    proj_shape = (proj_cut, grad_proj.shape[2])
    cuts = (0, proj_cut // 64 * 32, proj_cut)

    def kernel(cot_ref, slope_ref, h_ref, proj_ref, *refs):
        wp_refs, wf_refs, refs = refs[:n_wp], refs[n_wp : n_wp + n_wf], refs[n_wp + n_wf :]
        cot_own, residual_ref, mean_ref, inverse_ref, gain_ref = refs[:5]
        grad_residual, grad_attn, sums_ref, bias_ref, gp_ref, dw_ref, proj_out = refs[5:12]
        cot, slopes, wp_buf, wf_buf, gp, h_buf, dw_buf, folds = refs[12:20]
        s, line_refs = refs[20:34], refs[34:50]
        local, wlocal = refs[50:52]
        grad_residual, grad_attn = Rows(grad_residual, *refs[52:54]), Rows(grad_attn, *refs[54:56])
        p = Place()
        proj = [
            LineSum(
                p,
                lambda f, i=i: proj_ref.at[f, pl.ds(cuts[i], cuts[i + 1] - cuts[i]), :],
                layers,
                *line_refs[8 * i : 8 * i + 8],
            )
            for i in range(2)
        ]
        order = (p.dg, p.xn, p.yn, p.me)

        def chip(dev):
            return rows_at(lax.div(dev, 2) * (2 * rows), 2 * rows)

        def fetch(k):
            here = chip(order[k])
            return (
                load(cot_ref.at[here, :], cot.at[k % 2], local.at[k % 2]),
                load(slope_ref.at[here, :], slopes.at[k % 2], local.at[2 + k % 2]),
            )

        fetches = [fetch(0)]
        loads_wp = load_blocks(wp_refs, wp_buf, wlocal)
        loads_wf = load_parts(wf_refs, wf_buf, local.at[pl.ds(4, n_wf)])
        load_h = load(h_ref.at[:, pl.ds(0, tile)], h_buf, local.at[4 + n_wf])
        bias_ref[...] = jnp.zeros_like(bias_ref)
        p.greet(False, layers)
        LineSum.start(*proj)
        for copy in loads_wp:
            copy.wait()
        half = depth // 2

        def back_through_gelu(k):
            for copy in fetches[k]:
                copy.wait()
            if k < 3:
                fetches.append(fetch(k + 1))
            here = chip(order[k])

            @pl.loop(0, wide // 512)
            def _(j):
                cols = rows_at(j * 512, 512)
                grad_act = dot_nt(cot[k % 2], wp_buf[cols, :])
                grad_pre = (grad_act * slopes[k % 2, :, cols].astype(f32)).astype(bf16)
                gp[here, cols] = grad_pre
                bias_ref[:, cols] += jnp.sum(grad_pre.astype(f32), axis=0, keepdims=True)

            if k == 0:
                for copy in loads_wf:
                    copy.wait()

        def product(role, here, c):
            if c == 0:
                back_through_gelu(role)
            return dot_nt(gp[here, :], wf_buf[pl.ds(c * half, half), :])

        def emit(line, value):
            first = line.start == 0
            grad_out = cot_own[line, :].astype(f32)
            back = inverse_ref[line, :]
            normed = (residual_ref[line, :] - mean_ref[line, :]) * back
            result = grad_out + norm_back(value, normed, back, gain_ref[...])
            low = result.astype(bf16)
            grad_residual.put(line, result)
            grad_attn.put(line, low)
            for i, term in enumerate((value * normed, value, low.astype(f32), grad_out)):
                fold(folds.at[i], first, term)

        stores = []

        def last_poll():
            stores.append(load(gp, gp_ref, local.at[5 + n_wf]))
            proj[0].poll()

        def idle():
            load_h.wait()
            dw_buf[...] = dot_tn(h_buf[...], gp[...]).astype(bf16)
            stores.append(load(dw_buf, dw_ref, local.at[6 + n_wf]))
            proj[1].poll()

        Scatter.take(p, rows, s).run(
            product, emit, idle, (proj[0].poll, proj[1].poll, last_poll)
        )
        sums_ref[...] = jnp.sum(folds[...], axis=1)
        for i in range(2):

            def keep(where, value, i=i):
                proj_out[pl.ds(cuts[i] + where.start, where.size), :] = value.astype(bf16)

            proj[i].finish(keep)
        for copy in stores:
            copy.wait()
        grad_residual.finish()
        grad_attn.finish()

    return pl.pallas_call(
        kernel,
        out_shape=[
            jax.ShapeDtypeStruct((rows, depth), f32),
            jax.ShapeDtypeStruct((rows, depth), bf16),
            jax.ShapeDtypeStruct((4, depth), f32),
            jax.ShapeDtypeStruct((1, wide), f32),
            jax.ShapeDtypeStruct((total, wide), bf16),
            jax.ShapeDtypeStruct((tile, wide), bf16),
            jax.ShapeDtypeStruct(proj_shape, bf16),
        ],
        in_specs=[ANY] * (4 + n_wp + n_wf) + [WHOLE] * 5,
        out_specs=[ANY] * 2 + [WHOLE] * 2 + [ANY] * 2 + [WHOLE],
        scratch_shapes=[
            pltpu.VMEM((2, 2 * rows, depth), bf16),
            pltpu.VMEM((2, 2 * rows, wide), bf16),
            pltpu.VMEM((wide, depth), bf16),
            pltpu.VMEM((depth, wide), bf16),
            pltpu.VMEM((total, wide), bf16),
            pltpu.VMEM((total, tile), bf16),
            pltpu.VMEM((tile, wide), bf16),
            pltpu.VMEM((4, 8, depth), f32),
        ]
        + Scatter.scratch(rows, depth)
        + LineSum.scratch((cuts[1], depth), layers)
        + LineSum.scratch((proj_cut - cuts[1], depth), layers)
        + [sems(7 + n_wf), sems(n_wp * layers)]
        + Rows.scratch(rows, depth, f32)
        + Rows.scratch(rows, depth, bf16),
        compiler_params=params(number),
        cost_estimate=cost(6 * total * depth * wide),
        name="scatter_fc",
    )(cot_all, slope, hidden2, grad_proj, *wp, *wf, *back)


LANES = 128


def scatter_query(
    gq, gkv, wq, w_kv, grad_w_query, grad_w_kv, fc_done, fc_part, back, sums, layers, number
):
    total, cols = gq.shape
    kv_cols = gkv.shape[1]
    rows = total // PLANE
    depth = wq.shape[0]
    wide = depth + kv_cols
    q_shape = (grad_w_query.shape[0], *grad_w_query.shape[2:])
    fc_part, first, last = fc_part
    fc_shape = (last - first, *fc_part.shape[2:])
    my_hidden = sums[1].shape[1]
    places, lines_total = {}, 0
    for name, size in (
        ("ln1_gain", depth),
        ("ln1_bias", depth),
        ("b_query", PLANE * cols),
        ("b_value", kv_cols // 2),
        ("b_out", depth),
        ("ln2_gain", depth),
        ("ln2_bias", depth),
        ("b_fc", PLANE * my_hidden),
        ("b_proj", depth),
    ):
        places[name] = lines_total
        lines_total += size // LANES
    padded = -(-lines_total // (8 * PLANE)) * 8
    n_done = len(fc_done)
    done_cut = sum(a.shape[0] for a in fc_done)
    fc_rows, fc_cols = fc_shape[1:]
    kv_rows = rows // layers

    def kernel(gq_ref, gkv_ref, wq_ref, wkv_ref, dwq_ref, dwkv_ref, fc_ref, *refs):
        tok_ref, mean_ref, inverse_ref, gain_ref, residual_ref = refs[:5]
        sums2_ref, sums_fc_ref, sums_q_ref, sums_kv_ref = refs[5:9]
        done_refs, refs = refs[9 : 9 + n_done], refs[9 + n_done :]
        out_ref, vec_out, dwkv_out, fc_out, dwq_out = refs[:5]
        g_buf, wq_buf, wkv_buf, dwkv_buf, q_sum, folds = refs[5:11]
        vec, box, zbox, plane_sum, pieces, dwkv, kv_box = refs[11:18]
        s, line_refs = refs[18:32], refs[32:48]
        qsend, qrecv, local = refs[48:51]
        result = Rows(out_ref, *refs[51:53])
        vsend, vrecv, zsend, zrecv, gsend, grecv, fsend, frecv, ksend, krecv, flocal = refs[53:]
        p = Place()
        at, done_loads = 0, []
        for i, ref in enumerate(done_refs):
            done_loads.append(load(ref, pieces.at[pl.ds(at, ref.shape[0])], flocal.at[i]))
            at += ref.shape[0]

        def pack(at, row):
            for k in range(row.shape[1] // LANES):
                line = at + k
                vec[lax.div(line, padded), pl.ds(lax.rem(line, padded), 1), :] = row[
                    :, k * LANES : (k + 1) * LANES
                ]

        fc_spot = fc_out.at[:, rows_at(p.me * fc_cols, fc_cols)]

        def fc_copy(step):
            to = p.plane_peer(step)
            return push(pieces.at[to], fc_spot, fsend.at[step], frecv.at[step], {"seq": to})

        def spread_fc():
            for step in range(1, PLANE):
                fc_copy(step).start()

        q_side, kv_side = pl.ds(0, cols), pl.ds(cols, kv_cols)
        loads = [
            load(gq_ref, g_buf.at[:, q_side], local.at[0]),
            load(gkv_ref, g_buf.at[:, kv_side], local.at[1]),
            load(wq_ref, wq_buf, local.at[2]),
            load(wkv_ref, wkv_buf, local.at[3]),
            load(dwkv_ref, dwkv_buf, local.at[4]),
        ]
        line_q = LineSum(p, lambda f: dwq_ref.at[:, f], layers, *line_refs[:8])
        line_fc = LineSum(p, lambda f: fc_ref.at[pl.ds(first, last - first), f], layers, *line_refs[8:])
        p.greet(True, layers)
        LineSum.start(line_q, line_fc)
        for copy in loads:
            copy.wait()
        half = wide // 2

        def product(role, here, c):
            where = pl.ds(c * half, min(half, depth - c * half))
            value = dot_nt(g_buf[here, q_side], wq_buf[where, :]) + dot_nt(
                g_buf[here, kv_side], wkv_buf[where, :]
            )
            if c == 0:
                return value
            return jnp.concatenate([value, dwkv_buf[here, :].astype(f32)], axis=1)

        later = []

        def idle():
            def keep(where, value):
                q_sum[where] = value.astype(bf16)

            for copy in done_loads:
                copy.wait()
            vec[...] = jnp.zeros_like(vec)
            for i, name in enumerate(("ln2_gain", "ln2_bias", "b_out", "b_proj")):
                pack(places[name], sums2_ref[i : i + 1, :])
            pack(places["b_fc"] + p.me * (my_hidden // LANES), sums_fc_ref[...])
            pack(places["b_query"] + p.me * (cols // LANES), sums_q_ref[...])
            pack(places["b_value"], sums_kv_ref[:, kv_cols // 2 :])
            line_fc.poll()
            line_q.finish(keep)
            later.append(Spread(p, q_sum, dwq_out, qsend, qrecv, local.at[5]))

        def emit(line, value):
            begin = line.start == 0
            grad = value[:, :depth]
            normed = (tok_ref[line, :].astype(f32) - mean_ref[line, :]) * inverse_ref[line, :]
            result.put(
                line,
                residual_ref[line, :]
                + norm_back(grad, normed, inverse_ref[line, :], gain_ref[...]),
            )
            fold(folds.at[0], begin, grad * normed)
            fold(folds.at[1], begin, grad)
            dwkv[line, :] = value[:, depth:].astype(bf16)

        def keep_fc(where, value):
            pieces[done_cut + where] = value.astype(bf16)

        polls = (line_q.poll, line_fc.poll, line_q.poll)
        Scatter.take(p, rows, s).run(product, emit, idle, polls)
        for i, name in enumerate(("ln1_gain", "ln1_bias")):
            pack(places[name], jnp.sum(folds[i], axis=0, keepdims=True))
        plane = PlaneSum(p, vec, box, vsend, vrecv)
        across = []

        def kv_block(layer):
            return dwkv.at[rows_at(layer * kv_rows, kv_rows), :]

        for step in range(1, layers):
            to = p.line_peer(step, layers)
            across.append(
                push(kv_block(to), kv_box.at[step], ksend.at[step], krecv.at[step], {"fsdp": to})
            )
            across[-1].start()
        line_fc.finish(keep_fc)
        spread_fc()
        my_fc = load(pieces.at[p.me], fc_spot, flocal.at[n_done])
        total_vec = plane.total()
        plane_sum[...] = total_vec
        zbox[0] = total_vec
        for step in range(1, layers):
            to = p.line_peer(step, layers)
            across.append(
                push(plane_sum, zbox.at[step], zsend.at[step], zrecv.at[step], {"fsdp": to})
            )
            across[-1].start()
        for copy in across:
            copy.wait_recv()
        total_vec = None
        for k in range(layers):
            term = zbox[lax.rem(p.layer - k + layers, layers)]
            total_vec = term if total_vec is None else total_vec + term
        vec_out[p.me] = total_vec
        for step in range(1, PLANE):
            to = p.plane_peer(step)
            mine = vec_out.at[p.me]
            later.append(push(mine, mine, gsend.at[step], grecv.at[step], {"seq": to}))
            later[-1].start()
        value = dwkv[rows_at(p.layer * kv_rows, kv_rows), :].astype(f32)
        for step in range(1, layers):
            value = value + kv_box[step].astype(f32)
        dwkv_out[...] = value
        for item in (*later, result):
            item.finish() if hasattr(item, "finish") else item.wait()
        for step in range(1, PLANE):
            fc_copy(step).wait()
        my_fc.wait()
        plane.finish()
        for copy in across:
            copy.wait_send()

    return pl.pallas_call(
        kernel,
        out_shape=[
            jax.ShapeDtypeStruct((rows, depth), f32),
            jax.ShapeDtypeStruct((PLANE, padded, LANES), f32),
            jax.ShapeDtypeStruct((kv_rows, kv_cols), f32),
            jax.ShapeDtypeStruct((fc_rows, PLANE * fc_cols), bf16),
            jax.ShapeDtypeStruct((q_shape[1], PLANE * q_shape[2]), bf16),
        ],
        in_specs=[ANY] * 7 + [WHOLE] * 9 + [ANY] * n_done,
        out_specs=[ANY, WHOLE, WHOLE, ANY, ANY],
        scratch_shapes=[
            pltpu.VMEM((total, cols + kv_cols), bf16),
            pltpu.VMEM(wq.shape, bf16),
            pltpu.VMEM(w_kv.shape, bf16),
            pltpu.VMEM(grad_w_kv.shape, bf16),
            pltpu.VMEM(q_shape, bf16),
            pltpu.VMEM((2, 8, depth), f32),
            pltpu.VMEM((PLANE, padded, LANES), f32),
            pltpu.VMEM((PLANE, padded, LANES), f32),
            pltpu.VMEM((layers, padded, LANES), f32),
            pltpu.VMEM((padded, LANES), f32),
            pltpu.VMEM((PLANE, fc_rows, fc_cols), bf16),
            pltpu.VMEM((rows, kv_cols), bf16),
            pltpu.VMEM((layers, kv_rows, kv_cols), bf16),
        ]
        + Scatter.scratch(rows, wide)
        + LineSum.scratch(q_shape, layers)
        + LineSum.scratch(fc_shape, layers)
        + [sems(PLANE)] * 2
        + [sems(6)]
        + Rows.scratch(rows, depth, f32)
        + [sems(PLANE)] * 2
        + [sems(layers)] * 2
        + [sems(PLANE)] * 4
        + [sems(layers)] * 2
        + [sems(n_done + 1)],
        compiler_params=params(number),
        cost_estimate=cost(2 * total * depth * (cols + kv_cols)),
        name="scatter_query",
    )(gq, gkv, wq, w_kv, grad_w_query, grad_w_kv, fc_part, *back, *sums, *fc_done)


def starts_of(docs, stream, positions):
    start = jnp.zeros_like(positions)
    for j in range(docs.shape[1]):
        here = docs[stream, j]
        start = jnp.maximum(start, jnp.where(here <= positions, here, 0))
    return start


def masked_scores(docs, stream, keys, q, first, limit):
    scores = dot_nt(keys, q) * (HD**-0.5)
    t = first + lax.broadcasted_iota(jnp.int32, (1, q.shape[0]), 1)
    u = lax.broadcasted_iota(jnp.int32, scores.shape, 0)
    return scores, (u >= starts_of(docs, stream, t)) & (u <= t)


QROWS = 256


def attend_stream(docs, stream, q_ref, kv_ref, mixed_ref, lse_ref, block, heads):
    groups, rows, cols = q_ref.shape
    length = groups * rows
    kv = kv_ref[...].reshape(length, 2 * HD)
    keys = kv[:, :HD]
    values_t = kv[:, HD:].T
    per = block // rows
    for b in range(length // block):
        limit = (b + 1) * block
        q_rows = q_ref[b * per : (b + 1) * per].reshape(block, cols)
        for h in range(heads):
            q = q_rows[:, h * HD : (h + 1) * HD]
            scores, allowed = masked_scores(docs, stream, keys[:limit], q, b * block, limit)
            scores = jnp.where(allowed, scores, -1e30)
            top = jnp.max(scores, axis=0, keepdims=True)
            weights = jnp.exp(scores - top)
            total = jnp.sum(weights, axis=0, keepdims=True)
            mixed = dot(values_t[:, :limit], weights.astype(bf16)) / total
            mixed_ref[b * per : (b + 1) * per, :, h * HD : (h + 1) * HD] = (
                mixed.T.astype(bf16).reshape(per, rows, HD)
            )
            lse_ref[h : h + 1, b * block : (b + 1) * block] = top + jnp.log(total)


def attend_stream_back(docs, stream, q_ref, kv_ref, g_ref, lse_ref, gq_ref, gkv_ref, gk, gv, heads):
    groups, rows, cols = q_ref.shape
    length = groups * rows
    block = min(QROWS, length)
    kv = kv_ref[...].reshape(length, 2 * HD)
    keys, values = kv[:, :HD], kv[:, HD:]
    keys_t = keys.T
    per = block // rows
    gk[...] = jnp.zeros_like(gk)
    gv[...] = jnp.zeros_like(gv)
    for b in range(length // block):
        limit = (b + 1) * block
        q_rows = q_ref[b * per : (b + 1) * per].reshape(block, cols)
        g_rows = g_ref[b * per : (b + 1) * per].reshape(block, cols)
        for h in range(heads):
            q = q_rows[:, h * HD : (h + 1) * HD]
            g = g_rows[:, h * HD : (h + 1) * HD]
            scores, allowed = masked_scores(docs, stream, keys[:limit], q, b * block, limit)
            shift = lse_ref[h : h + 1, b * block : (b + 1) * block]
            probs = jnp.where(allowed, jnp.exp(scores - shift), 0.0)
            grad_probs = dot_nt(values[:limit], g)
            weighted = probs * grad_probs
            delta = jnp.sum(weighted, axis=0, keepdims=True)
            grad_scores = (weighted - probs * delta).astype(bf16)
            gq = dot(keys_t[:, :limit], grad_scores) * (HD**-0.5)
            gq_ref[b * per : (b + 1) * per, :, h * HD : (h + 1) * HD] = (
                gq.T.astype(bf16).reshape(per, rows, HD)
            )
            gk[:limit, :] += dot(grad_scores, q)
            gv[:limit, :] += dot(probs.astype(bf16), g)
    gkv_ref[:, :, :HD] = (gk[...] * (HD**-0.5)).astype(bf16).reshape(groups, rows, HD)
    gkv_ref[:, :, HD:] = gv[...].astype(bf16).reshape(groups, rows, HD)


def attend_back_scatter_proj(
    docs, queries, keyval, grads, lse, act, wp, hidden1, out_part, fc_part, residual, b_proj,
    layers, heads, number
):
    groups, streams, rows, cols = queries.shape
    kv_cols = keyval.shape[3]
    length = groups * rows
    total, depth = act.shape
    own = total // PLANE
    wide = hidden1.shape[1]
    part = hidden1.shape[1] // PLANE
    n_wp = len(wp)
    out_shape = out_part.shape[1:]
    fc_part, first, last = fc_part
    fc_shape = (last - first, *fc_part.shape[2:])

    def kernel(docs_ref, q_ref, kv_ref, g_ref, lse_ref, act_ref, h_ref, dwo_ref, fc_ref, *refs):
        wp_refs, refs = refs[:n_wp], refs[n_wp:]
        residual_ref, bias_ref = refs[:2]
        gq_out, gkv_out, gq_sum, gkv_sum, dwq_out, dwkv_out = refs[2:8]
        out_ref, dwo_out, fc_out = refs[8:11]
        a_buf, w_buf, q_buf, kv_buf, g_buf, grad_buf, gk, gv, h_buf = refs[11:20]
        dwq_buf, dwkv_buf = refs[20:22]
        s, line_refs = refs[22:36], refs[36:52]
        local, wlocal = refs[52:54]
        result = Rows(out_ref, *refs[54:])
        p = Place()
        loads = [load(act_ref, a_buf, local.at[0]), *load_blocks(wp_refs, w_buf, wlocal)]
        line_o = LineSum(p, lambda f: dwo_ref.at[f], layers, *line_refs[:8])
        line_fc = LineSum(p, lambda f: fc_ref.at[pl.ds(first, last - first), f], layers, *line_refs[8:])
        ins = [
            load(q_ref, q_buf, local.at[2]),
            load(kv_ref, kv_buf, local.at[3]),
            load(g_ref, g_buf, local.at[4]),
        ]

        def h_fetch(i):
            here = pl.ds(2 * i * part, 2 * part)
            return load(h_ref.at[:, here], h_buf.at[i % 2], local.at[5 + i % 2])

        tiles = [h_fetch(0)]
        p.greet(False, layers)
        LineSum.start(line_o, line_fc)
        for copy in loads:
            copy.wait()
        stores = []

        def idle():
            for copy in ins:
                copy.wait()
            for stream in range(streams):
                attend_stream_back(
                    docs_ref,
                    stream,
                    q_buf.at[:, stream],
                    kv_buf.at[:, stream],
                    g_buf.at[:, stream],
                    lse_ref.at[stream],
                    grad_buf.at[:, stream, :, pl.ds(0, cols)],
                    grad_buf.at[:, stream, :, pl.ds(cols, kv_cols)],
                    gk,
                    gv,
                    heads,
                )
                if stream == 0:
                    line_fc.poll()
            stores.append(load(grad_buf.at[:, :, :, pl.ds(0, cols)], gq_out, local.at[7]))
            stores.append(load(grad_buf.at[:, :, :, pl.ds(cols, kv_cols)], gkv_out, local.at[8]))
            grad = grad_buf[...].reshape(total, cols + kv_cols)
            sums = jnp.sum(grad.astype(f32), axis=0, keepdims=True)
            gq_sum[...] = sums[:, :cols]
            gkv_sum[...] = sums[:, cols:]
            for i in range(PLANE // 2):
                tiles[i].wait()
                if i + 1 < PLANE // 2:
                    tiles.append(h_fetch(i + 1))
                term = dot_tn(h_buf[i % 2], grad).astype(bf16)
                for k in range(2):
                    lines = term[k * part : (k + 1) * part]
                    dwq_buf[2 * i + k] = lines[:, :cols].reshape(layers, part // layers, cols)
                    dwkv_buf[2 * i + k] = lines[:, cols:]
            stores.append(load(dwq_buf, dwq_out, local.at[9]))
            stores.append(load(dwkv_buf, dwkv_out, local.at[10]))

        def emit(line, value):
            result.put(line, residual_ref[line, :] + value + bias_ref[...])

        def keep_out(where, value):
            dwo_out[where, :] = value

        def keep_fc(where, value):
            fc_out[where] = value.astype(bf16)

        polls = (line_o.poll, line_fc.poll, line_o.poll)
        Scatter.take(p, own, s).run(plain_product(a_buf, w_buf), emit, idle, polls)
        line_o.finish(keep_out)
        line_fc.finish(keep_fc)
        for copy in stores:
            copy.wait()
        result.finish()

    return pl.pallas_call(
        kernel,
        out_shape=[
            jax.ShapeDtypeStruct(queries.shape, bf16),
            jax.ShapeDtypeStruct(keyval.shape, bf16),
            jax.ShapeDtypeStruct((1, cols), f32),
            jax.ShapeDtypeStruct((1, kv_cols), f32),
            jax.ShapeDtypeStruct((PLANE, layers, part // layers, cols), bf16),
            jax.ShapeDtypeStruct((PLANE, part, kv_cols), bf16),
            jax.ShapeDtypeStruct((own, wide), f32),
            jax.ShapeDtypeStruct(out_shape, f32),
            jax.ShapeDtypeStruct(fc_shape, bf16),
        ],
        in_specs=[pl.BlockSpec(memory_space=pltpu.SMEM)]
        + [ANY] * 3
        + [WHOLE]
        + [ANY] * (4 + n_wp)
        + [WHOLE] * 2,
        out_specs=[ANY, ANY, WHOLE, WHOLE, ANY, ANY, ANY] + [WHOLE] * 2,
        scratch_shapes=[
            pltpu.VMEM(act.shape, bf16),
            pltpu.VMEM((depth, wide), bf16),
            pltpu.VMEM(queries.shape, bf16),
            pltpu.VMEM(keyval.shape, bf16),
            pltpu.VMEM(grads.shape, bf16),
            pltpu.VMEM((groups, streams, rows, cols + kv_cols), bf16),
            pltpu.VMEM((length, HD), f32),
            pltpu.VMEM((length, HD), f32),
            pltpu.VMEM((2, total, 2 * part), bf16),
            pltpu.VMEM((PLANE, layers, part // layers, cols), bf16),
            pltpu.VMEM((PLANE, part, kv_cols), bf16),
        ]
        + Scatter.scratch(own, wide)
        + LineSum.scratch(out_shape, layers)
        + LineSum.scratch(fc_shape, layers)
        + [sems(11), sems(n_wp * layers)]
        + Rows.scratch(own, wide, f32),
        compiler_params=params(number),
        cost_estimate=cost(2 * total * depth * wide),
        name="attend_back_scatter_proj",
    )(docs, queries, keyval, grads, lse, act, hidden1, out_part, fc_part, *wp, residual, b_proj)


def finish(copied, cast, packed, vectors):
    n_copy, n_cast, n_vec = len(copied), len(cast), len(vectors)
    count = n_copy + n_cast

    def kernel(*refs):
        ins, packed_ref, refs = refs[:count], refs[count], refs[count + 1 :]
        outs, refs = refs[: count + n_vec], refs[count + n_vec :]
        rooms, wide, parts = refs[:count], refs[count : count + n_cast], refs[count + n_cast : -2]
        load_sem, store_sem = refs[-2:]
        loads = [load(src, room, load_sem.at[i]) for i, (src, room) in enumerate(zip(ins, rooms))]
        stores = []

        def store(src, dst):
            stores.append(load(src, dst, store_sem.at[len(stores)]))

        at = 0
        for part, out in zip(parts, outs[count:]):
            for k in range(part.shape[1] // LANES):
                part[:, k * LANES : (k + 1) * LANES] = packed_ref[at : at + 1, :]
                at += 1
            store(part, out)
        for i in range(n_copy):
            loads[i].wait()
            store(rooms[i], outs[i])
        for i in range(n_cast):
            loads[n_copy + i].wait()
            wide[i][...] = rooms[n_copy + i][...].astype(f32)
            store(wide[i], outs[n_copy + i])
        for copy in stores:
            copy.wait()

    shapes = [(a.shape, a.dtype) for a in copied] + [(a.shape, f32) for a in cast]
    shapes += [((1, size), f32) for size in vectors]
    return pl.pallas_call(
        kernel,
        out_shape=[jax.ShapeDtypeStruct(*shape) for shape in shapes],
        in_specs=[ANY] * count + [WHOLE],
        out_specs=[ANY] * (count + n_vec),
        scratch_shapes=[pltpu.VMEM(a.shape, a.dtype) for a in (*copied, *cast)]
        + [pltpu.VMEM(a.shape, f32) for a in cast]
        + [pltpu.VMEM((1, size), f32) for size in vectors]
        + [sems(count), sems(count + n_vec)],
        compiler_params=pltpu.CompilerParams(vmem_limit_bytes=VMEM_LIMIT),
        name="finish",
    )(*copied, *cast, packed)


def shards(
    tokens,
    doc_starts,
    w_query,
    w_kv,
    w_out,
    w_fc,
    w_proj,
    ln1_gain,
    ln1_bias,
    b_query,
    b_value,
    b_out,
    ln2_gain,
    ln2_bias,
    b_fc,
    b_proj,
    cotangent,
):
    layers = lax.axis_size("fsdp")
    streams, rows, width = tokens.shape
    own = streams * rows
    heads = HEADS // PLANE
    hidden = b_fc.shape[0]
    my_cols = heads * HD
    my_hidden = hidden // PLANE
    total = PLANE * own

    own_tokens = tokens.reshape(own, width)
    cot_low = cotangent.reshape(own, width)

    def row(vector):
        return vector.reshape(1, -1)

    fc_cut = PLANE * 6 // 8
    proj_rows = w_proj.shape[0]
    wp_cut, proj_cut = proj_rows * 5 // 16, proj_rows * 5 // 8

    def rows_together(pieces):
        return pieces.reshape(-1, pieces.shape[-1])

    (
        hidden1,
        w_kv_all,
        cot_all,
        queries,
        keyval,
        mixed,
        wq,
        wo,
        wf_pieces,
        wf_a,
        wf_b,
        lse,
        mean1,
        inverse1,
    ) = front(
        doc_starts,
        own_tokens,
        row(ln1_gain),
        row(ln1_bias),
        w_query,
        w_fc,
        w_kv,
        w_out,
        cot_low,
        row(b_query),
        row(b_value),
        fc_cut,
        streams,
        heads,
        layers,
        1,
    )
    wq = rows_together(wq)
    mixed_rows = mixed.reshape(total, my_cols)
    residual, low_hidden2, mean2, inverse2, wf_c, wp_a = scatter_attn(
        mixed_rows,
        wo,
        own_tokens,
        row(b_out),
        row(ln2_gain),
        row(ln2_bias),
        (wf_pieces, fc_cut, PLANE),
        (w_proj, 0, wp_cut),
        layers,
        4,
    )
    wf = [rows_together(w) for w in (wf_a, wf_b, wf_c)]
    hidden2, act_low, slope, grad_w_proj, wp_b = gather_fc(
        low_hidden2, wf, row(b_fc), cot_all, (w_proj, wp_cut, proj_rows), layers, 5
    )
    wp = (wp_a, wp_b)
    grad_w_proj = grad_w_proj.reshape(layers, proj_rows, width)
    grad_residual, grad_attn, sums2, my_grad_b_fc, grad_pre, grad_fc_a, shard_proj_a = scatter_fc(
        cot_all,
        slope,
        wp,
        wf,
        hidden2,
        (cot_low, residual, mean2, inverse2, row(ln2_gain)),
        grad_w_proj,
        proj_cut,
        layers,
        6,
    )

    def by_layer(grad):
        return grad.reshape(-1, layers, width // PLANE // layers, my_hidden)

    first_fc = grad_fc_a.shape[0]
    grad_mixed, grad_w_out, grad_fc_rest, shard_proj, fc_a = gather_out(
        grad_attn,
        wo,
        mixed_rows,
        hidden2,
        grad_pre,
        first_fc,
        grad_w_proj,
        shard_proj_a,
        by_layer(grad_fc_a),
        layers,
        7,
    )
    grad_fc_rest = by_layer(grad_fc_rest)
    rest_cut = grad_fc_rest.shape[0] // 2
    (
        gq,
        gkv,
        my_grad_b_query,
        sums_kv,
        grad_w_query,
        grad_w_kv,
        output,
        shard_out,
        fc_b,
    ) = attend_back_scatter_proj(
        doc_starts,
        queries,
        keyval,
        grad_mixed.reshape(PLANE, streams, rows, my_cols),
        lse,
        act_low,
        wp,
        hidden1,
        grad_w_out.reshape(layers, -1, width),
        (grad_fc_rest, 0, rest_cut),
        residual,
        row(b_proj),
        layers,
        heads,
        8,
    )
    input_grad, packed, shard_kv, shard_fc, shard_query = scatter_query(
        gq.reshape(total, my_cols),
        gkv.reshape(total, 2 * HD),
        wq,
        w_kv_all,
        grad_w_query,
        grad_w_kv.reshape(width, 2 * HD),
        (fc_a, fc_b),
        (grad_fc_rest, rest_cut, grad_fc_rest.shape[0]),
        (own_tokens, mean1, inverse1, row(ln1_gain), grad_residual),
        (sums2, my_grad_b_fc, my_grad_b_query, sums_kv),
        layers,
        9,
    )
    vectors = (ln1_gain, ln1_bias, b_query, b_value, b_out, ln2_gain, ln2_bias, b_fc, b_proj)
    output, input_grad, shard_kv, shard_out, shard_proj, shard_query, shard_fc, *sums = finish(
        (output, input_grad, shard_kv, shard_out, shard_proj),
        (shard_query, shard_fc),
        packed.reshape(-1, LANES),
        [v.shape[0] for v in vectors],
    )
    return (
        output.reshape(streams, rows, width),
        input_grad.reshape(streams, rows, width),
        shard_query,
        shard_kv,
        shard_out,
        shard_fc,
        shard_proj,
        *[v.reshape(-1) for v in sums],
    )


def gather_seq(block):
    return lax.all_gather(block, "seq", axis=0, tiled=True)


def scatter_seq(partial):
    return lax.psum_scatter(partial.astype(bf16), "seq", scatter_dimension=0, tiled=True).astype(f32)


def columns_to_rows(part, groups):
    rows = part.shape[0]
    spread = part.reshape(rows, groups, part.shape[1] // groups).transpose(1, 0, 2)
    return lax.all_to_all(spread, "seq", split_axis=0, concat_axis=0, tiled=True)


def column_weight(shard, groups):
    pieces = columns_to_rows(shard, groups)
    full = lax.all_gather(pieces, "fsdp", axis=1, tiled=True)
    return full.reshape(-1, full.shape[2])


def plain_column_grad(grad, groups):
    rows, cols = grad.shape
    kept = lax.psum_scatter(
        grad.astype(bf16).reshape(groups, rows // groups, cols), "fsdp", scatter_dimension=1, tiled=True
    )
    moved = lax.all_to_all(kept, "seq", split_axis=0, concat_axis=0, tiled=True)
    return moved.transpose(1, 0, 2).reshape(moved.shape[1], groups * cols).astype(f32)


def row_weight_grad(grad):
    return lax.psum_scatter(grad.astype(bf16), "fsdp", scatter_dimension=0, tiled=True).astype(f32)


def plain_attend(queries, keyval, starts, groups, streams, rows, heads):
    length = groups * rows
    scale = HD ** (-0.5)
    position = jnp.arange(length, dtype=jnp.int32)
    mixed_list, lse_list = [], []
    for stream in range(streams):
        q = queries[:, stream].reshape(length, heads, HD)
        k = keyval[:, stream, :, :HD].reshape(length, HD)
        v = keyval[:, stream, :, HD:].reshape(length, HD)
        segment = jnp.sum((starts[stream][None, :] <= position[:, None]).astype(jnp.int32), axis=1)
        allowed = (position[None, :] <= position[:, None]) & (segment[None, :] == segment[:, None])
        scores = jnp.einsum("thd,ud->htu", q, k, preferred_element_type=f32) * scale
        scores = jnp.where(allowed[None], scores, -1e30)
        top = jnp.max(scores, axis=-1, keepdims=True)
        lse = top + jnp.log(jnp.sum(jnp.exp(scores - top), axis=-1, keepdims=True))
        probs = jnp.exp(scores - lse).astype(bf16)
        mixed = jnp.einsum("htu,ud->thd", probs, v, preferred_element_type=f32)
        mixed_list.append(mixed.astype(bf16).reshape(groups, rows, heads * HD))
        lse_list.append(lse)
    return jnp.stack(mixed_list, axis=1), lse_list


def plain_attend_back(queries, keyval, grads, lse_list, starts, groups, streams, rows, heads):
    length = groups * rows
    scale = HD ** (-0.5)
    position = jnp.arange(length, dtype=jnp.int32)
    gq_list, gkv_list = [], []
    for stream in range(streams):
        q = queries[:, stream].reshape(length, heads, HD)
        g = grads[:, stream].reshape(length, heads, HD)
        k = keyval[:, stream, :, :HD].reshape(length, HD)
        v = keyval[:, stream, :, HD:].reshape(length, HD)
        segment = jnp.sum((starts[stream][None, :] <= position[:, None]).astype(jnp.int32), axis=1)
        allowed = (position[None, :] <= position[:, None]) & (segment[None, :] == segment[:, None])
        scores = jnp.einsum("thd,ud->htu", q, k, preferred_element_type=f32) * scale
        probs = jnp.exp(jnp.where(allowed[None], scores, -1e30) - lse_list[stream])
        grad_probs = jnp.einsum("thd,ud->htu", g, v, preferred_element_type=f32)
        delta = jnp.sum(probs * grad_probs, axis=-1, keepdims=True)
        gs = (probs * (grad_probs - delta)).astype(bf16)
        gq = jnp.einsum("htu,ud->thd", gs, k, preferred_element_type=f32) * scale
        gk = jnp.einsum("htu,thd->ud", gs, q, preferred_element_type=f32) * scale
        gv = jnp.einsum("htu,thd->ud", probs.astype(bf16), g, preferred_element_type=f32)
        gq_list.append(gq.astype(bf16).reshape(groups, rows, heads * HD))
        gkv_list.append(jnp.concatenate([gk, gv], axis=1).reshape(groups, rows, 2 * HD))
    return jnp.stack(gq_list, axis=1), jnp.stack(gkv_list, axis=1)


def plain_shards(
    tokens,
    doc_starts,
    w_query,
    w_kv,
    w_out,
    w_fc,
    w_proj,
    ln1_gain,
    ln1_bias,
    b_query,
    b_value,
    b_out,
    ln2_gain,
    ln2_bias,
    b_fc,
    b_proj,
    cotangent,
):
    groups = lax.axis_size("seq")
    me = lax.axis_index("seq")
    streams, rows, width = tokens.shape
    own = streams * rows
    heads = HEADS // groups
    hidden = b_fc.shape[0]
    my_cols = heads * HD
    my_hidden = hidden // groups

    wq = column_weight(w_query, groups)
    w_kv_all = gather_seq(lax.all_gather(w_kv, "fsdp", axis=0, tiled=True))
    wo = lax.all_gather(w_out, "fsdp", axis=0, tiled=True)
    wf = column_weight(w_fc, groups)
    wp = lax.all_gather(w_proj, "fsdp", axis=0, tiled=True)
    my_bq = lax.dynamic_slice_in_dim(b_query, me * my_cols, my_cols, 0)
    my_bf = lax.dynamic_slice_in_dim(b_fc, me * my_hidden, my_hidden, 0)

    inputs = tokens.reshape(own, width).astype(f32)
    cot_low = cotangent.reshape(own, width)
    cot_full = cot_low.astype(f32)
    shifted1, normed1, inverse1 = normalize(inputs, ln1_gain, ln1_bias)
    hidden1 = gather_seq(shifted1.astype(bf16))
    queries = (dot(hidden1, wq) + my_bq).astype(bf16).reshape(groups, streams, rows, my_cols)
    value_shift = jnp.concatenate([jnp.zeros((HD,), f32), b_value])
    keyval = (dot(hidden1, w_kv_all) + value_shift).astype(bf16).reshape(groups, streams, rows, 2 * HD)
    mixed, lse = plain_attend(queries, keyval, doc_starts, groups, streams, rows, heads)
    mixed_rows = mixed.reshape(groups * own, my_cols)
    residual = inputs + scatter_seq(dot(mixed_rows, wo)) + b_out
    shifted2, normed2, inverse2 = normalize(residual, ln2_gain, ln2_bias)
    hidden2 = gather_seq(shifted2.astype(bf16))
    cot_all = gather_seq(cot_low)
    pre_act = dot(hidden2, wf) + my_bf
    activated, slope = gelu_pair(pre_act)
    act_low = activated.astype(bf16)
    output = residual + scatter_seq(dot(act_low, wp)) + b_proj

    grad_b_proj = jnp.sum(cot_full, axis=0)
    shard_proj = row_weight_grad(dot_tn(act_low, cot_all))
    grad_pre = (dot_nt(cot_all, wp) * slope).astype(bf16)
    my_grad_b_fc = jnp.sum(grad_pre.astype(f32), axis=0)
    shard_fc = plain_column_grad(dot_tn(hidden2, grad_pre), groups)
    grad_hidden2 = scatter_seq(dot_nt(grad_pre, wf))
    back_second, grad_ln2_gain, grad_ln2_bias = normalize_back(
        grad_hidden2, normed2, inverse2, ln2_gain
    )
    grad_residual = cot_full + back_second
    grad_attn = grad_residual.astype(bf16)
    grad_b_out = jnp.sum(grad_attn.astype(f32), axis=0)
    grad_attn_all = gather_seq(grad_attn)
    shard_out = row_weight_grad(dot_tn(mixed_rows, grad_attn_all))
    grad_mixed = dot_nt(grad_attn_all, wo).astype(bf16).reshape(groups, streams, rows, my_cols)
    gq, gkv = plain_attend_back(
        queries, keyval, grad_mixed, lse, doc_starts, groups, streams, rows, heads
    )
    gq_rows = gq.reshape(groups * own, my_cols)
    gkv_rows = gkv.reshape(groups * own, 2 * HD)
    my_grad_b_query = jnp.sum(gq_rows.astype(f32), axis=0)
    grad_b_value = jnp.sum(gkv_rows[:, HD:], axis=0)
    gkv_low = gkv_rows.astype(bf16)
    shard_query = plain_column_grad(dot_tn(hidden1, gq_rows), groups)
    shard_kv = row_weight_grad(scatter_seq(dot_tn(hidden1, gkv_low)))
    grad_hidden1 = scatter_seq(dot_nt(gq_rows, wq) + dot_nt(gkv_low, w_kv_all))
    back_first, grad_ln1_gain, grad_ln1_bias = normalize_back(
        grad_hidden1, normed1, inverse1, ln1_gain
    )
    input_grad = grad_residual + back_first

    zero = jnp.zeros_like
    grad_b_query = lax.dynamic_update_slice_in_dim(zero(b_query), my_grad_b_query, me * my_cols, 0)
    grad_b_fc = lax.dynamic_update_slice_in_dim(zero(b_fc), my_grad_b_fc, me * my_hidden, 0)
    vectors = (
        grad_ln1_gain,
        grad_ln1_bias,
        grad_b_query,
        grad_b_value,
        grad_b_out,
        grad_ln2_gain,
        grad_ln2_bias,
        grad_b_fc,
        grad_b_proj,
    )
    sums = lax.psum(vectors, ("seq", "fsdp"))
    return (
        output.reshape(streams, rows, width),
        input_grad.reshape(streams, rows, width),
        shard_query,
        shard_kv,
        shard_out,
        shard_fc,
        shard_proj,
        *sums,
    )


def solution(mesh):
    acts = P("fsdp", "seq", None)
    weight = P(("seq", "fsdp"), None)
    return jax.shard_map(
        shards if mesh.shape["seq"] == PLANE else plain_shards,
        mesh=mesh,
        in_specs=(acts, P("fsdp", None)) + (weight,) * 5 + (P(),) * 9 + (acts,),
        out_specs=(acts, acts) + (weight,) * 5 + (P(),) * 9,
        check_vma=False,
    )
```

```python
import functools

import jax
import jax.numpy as jnp
from jax import lax
from jax.experimental import pallas as pl
from jax.experimental.pallas import tpu as pltpu
from jax.sharding import PartitionSpec as P

HEADS = 16
HD = 128

root_two_pi = 0.7978845608028654
cubic_coef = 0.044715
epsilon = 1e-05
f32 = jnp.float32
bf16 = jnp.bfloat16
MESH = pl.DeviceIdType.MESH
ANY = pl.BlockSpec(memory_space=pl.ANY)
WHOLE = pl.BlockSpec(memory_space=pltpu.VMEM)
VMEM_LIMIT = 62 * 1024 * 1024
PLANE = 8


def normalize(values, gain_row, shift_row):
    center = values - jnp.mean(values, axis=-1, keepdims=True)
    inverse = lax.rsqrt(jnp.mean(center * center, axis=-1, keepdims=True) + epsilon)
    normed = center * inverse
    return (normed * gain_row + shift_row, normed, inverse)


def normalize_back(grad_out, normed, inverse, gain_row):
    scaled = grad_out * gain_row
    grad_in = inverse * (
        scaled
        - jnp.mean(scaled, axis=-1, keepdims=True)
        - normed * jnp.mean(scaled * normed, axis=-1, keepdims=True)
    )
    return (grad_in, jnp.sum(grad_out * normed, axis=0), jnp.sum(grad_out, axis=0))


def norm_stats(values):
    mean = jnp.mean(values, axis=-1, keepdims=True)
    center = values - mean
    return mean, lax.rsqrt(jnp.mean(center * center, axis=-1, keepdims=True) + epsilon)


def norm_back(grad_out, normed, inverse, gain_row):
    scaled = grad_out * gain_row
    return inverse * (
        scaled
        - jnp.mean(scaled, axis=-1, keepdims=True)
        - normed * jnp.mean(scaled * normed, axis=-1, keepdims=True)
    )


def gelu_pair(inputs):
    tangent = jnp.tanh(root_two_pi * (inputs + cubic_coef * inputs * inputs * inputs))
    activated = 0.5 * inputs * (1.0 + tangent)
    gradient_slope = 0.5 * (1.0 + tangent) + 0.5 * inputs * (
        1.0 - tangent * tangent
    ) * root_two_pi * (1.0 + 3.0 * cubic_coef * inputs * inputs)
    return (activated, gradient_slope)


def dot(a, b):
    return jnp.dot(a, b, preferred_element_type=f32)


def dot_nt(a, b):
    return lax.dot_general(a, b, (((1,), (1,)), ((), ())), preferred_element_type=f32)


def dot_tn(a, b):
    return lax.dot_general(a, b, (((0,), (0,)), ((), ())), preferred_element_type=f32)


def push(src, dst, send, recv, to):
    return pltpu.make_async_remote_copy(
        src_ref=src, dst_ref=dst, send_sem=send, recv_sem=recv, device_id=to, device_id_type=MESH
    )


def sems(*shape):
    return pltpu.SemaphoreType.DMA(shape)


def rows_at(start, size):
    return pl.ds(pl.multiple_of(start, size), size)


class Place:
    def __init__(self):
        me = lax.axis_index("seq")
        self.me = me
        self.core = lax.rem(me, 2)
        x = lax.rem(lax.div(me, 2), 2)
        y = lax.div(me, 4)
        self.sib = me + 1 - 2 * self.core
        self.xn = me + 2 - 4 * x
        self.yn = me + 4 - 8 * y
        self.dg = me + 2 - 4 * x + 4 - 8 * y
        turn = 1 - 2 * self.core
        self.xs, self.ys, self.ds = self.xn + turn, self.yn + turn, self.dg + turn
        self.layer = lax.axis_index("fsdp")

    def plane_peer(self, step):
        return lax.rem(self.me + step, PLANE)

    def line_peer(self, step, layers):
        return lax.rem(self.layer + step, layers)

    def greet(self, whole_plane=False, layers=1):
        barrier = pltpu.get_barrier_semaphore()
        if whole_plane:
            others = [self.plane_peer(step) for step in range(1, PLANE)]
        else:
            others = [self.sib, self.xn, self.yn]
        for other in others:
            pl.semaphore_signal(barrier, inc=1, device_id={"seq": other}, device_id_type=MESH)
        for step in range(1, layers):
            other = self.line_peer(step, layers)
            pl.semaphore_signal(barrier, inc=1, device_id={"fsdp": other}, device_id_type=MESH)
        pl.semaphore_wait(barrier, len(others) + layers - 1)


class Gather:
    @staticmethod
    def scratch(subs=1):
        return [sems(14 * subs), sems(PLANE, 2 * subs)]

    def __init__(self, place, buf, rows, send, recv, subs=1):
        self.p, self.buf, self.rows, self.subs = place, buf, rows, subs
        self.size = rows // (2 * subs)
        self.send_sem, self.recv_sem = send, recv
        self.copies = []
        self.low, self.high = range(subs), range(subs, 2 * subs)

    def piece(self, dev, k):
        return self.buf.at[rows_at(dev * self.rows + k * self.size, self.size), :]

    def pair(self, dev):
        return rows_at(lax.div(dev, 2) * (2 * self.rows), 2 * self.rows)

    def send(self, dev, k, to, src=None):
        piece = self.piece(dev, k)
        copy = push(
            piece if src is None else src,
            piece,
            self.send_sem.at[len(self.copies)],
            self.recv_sem.at[dev, k],
            {"seq": to},
        )
        copy.start()
        self.copies.append(copy)

    def arrived(self, dev, k):
        piece = self.piece(dev, k)
        push(
            piece, piece, self.send_sem.at[0], self.recv_sem.at[dev, k], {"seq": self.p.sib}
        ).wait_recv()

    def start(self, own):
        parts = [own.at[pl.ds(k * self.size, self.size), :] for k in range(2 * self.subs)]
        for k in self.low:
            self.start_piece(k, parts)
        self.start_rest(parts)

    def start_piece(self, k, parts):
        p, other = self.p, k + self.subs
        self.send(p.me, k, p.yn, parts[k])
        self.send(p.me, other, p.xn, parts[other])

    def start_rest(self, parts):
        p = self.p
        for k, other in zip(self.low, self.high):
            self.send(p.me, other, p.yn, parts[other])
            self.send(p.me, k, p.xn, parts[k])
        for k in range(2 * self.subs):
            self.send(p.me, k, p.sib, parts[k])

    def relay_first(self):
        p = self.p
        for k, other in zip(self.low, self.high):
            self.arrived(p.yn, k)
            self.send(p.yn, k, p.xn)
            self.arrived(p.xn, other)
            self.send(p.xn, other, p.yn)
            self.send(p.yn, k, p.sib)
            self.send(p.xn, other, p.sib)

    def relay_rest(self):
        p = self.p
        for k, other in zip(self.low, self.high):
            self.arrived(p.xn, k)
            self.send(p.xn, k, p.sib)
            self.arrived(p.yn, other)
            self.send(p.yn, other, p.sib)

    def relay(self):
        self.relay_first()
        self.relay_rest()

    def have(self, dev):
        for k in range(2 * self.subs):
            self.arrived(dev, k)

    def relay_corner(self):
        p = self.p
        for k in range(2 * self.subs):
            self.arrived(p.dg, k)
            self.send(p.dg, k, p.sib)

    def finish(self):
        for copy in self.copies:
            copy.wait_send()


class Scatter:
    LINES = 32
    CHUNKS = 4

    def __init__(
        self, place, rows, acc, part, sib_out, sib_in, boxes, sib_send, sib_recv, send, recv
    ):
        self.p, self.rows, self.half = place, rows, rows // 2
        self.wide = part.shape[2]
        self.acc, self.part, self.sib_out, self.sib_in = acc, part, sib_out, sib_in
        self.out_d, self.out_x, self.out_y, self.in_d, self.in_x, self.in_y = boxes
        self.sib_send, self.sib_recv, self.send, self.recv = sib_send, sib_recv, send, recv
        self.copies = []

    @staticmethod
    def scratch(rows, wide):
        return [
            pltpu.VMEM((2 * rows, wide // 2), f32),
            pltpu.VMEM((4, rows, wide), f32),
            pltpu.VMEM((4, rows, wide), bf16),
            pltpu.VMEM((4, rows, wide), bf16),
            *[pltpu.VMEM((rows, wide), bf16)] * 6,
            sems(4, 2),
            sems(4, 2),
            sems(14),
            sems(14),
        ]

    @classmethod
    def take(cls, place, rows, refs):
        return cls(place, rows, *refs[:4], refs[4:10], *refs[10:14])

    refs = 14

    def cols(self, c):
        return pl.ds(c * (self.wide // 2), self.wide // 2)

    def swap(self, role, dev, product, c):
        p = self.p
        self.acc[...] = product(role, rows_at(lax.div(dev, 2) * (2 * self.rows), 2 * self.rows), c)
        theirs = rows_at((1 - p.core) * self.rows, self.rows)
        ours = rows_at(p.core * self.rows, self.rows)
        self.sib_out[role, :, self.cols(c)] = self.acc[theirs, :].astype(bf16)
        copy = push(
            self.sib_out.at[role, :, self.cols(c)],
            self.sib_in.at[role, :, self.cols(c)],
            self.sib_send.at[role, c],
            self.sib_recv.at[role, c],
            {"seq": p.sib},
        )
        copy.start()
        self.copies.append(copy)
        self.part[role, :, self.cols(c)] = self.acc[ours, :]
        return copy

    def swap_all(self, role, dev, product):
        return [self.swap(role, dev, product, c) for c in range(2)]

    def add_into(self, dst, role, first, size, more=(), cols=slice(None)):
        lines = self.LINES

        @pl.loop(0, size // lines)
        def _(i):
            line = rows_at(first + i * lines, lines)
            value = self.part[role, line, cols] + self.sib_in[role, line, cols].astype(f32)
            for ref in more:
                value = value + ref[line, cols].astype(f32)
            dst[line, cols] = value.astype(dst.dtype)

    def final(self, start, size):
        line = pl.ds(start, size)
        value = self.part[3, line, :] + self.sib_in[3, line, :].astype(f32)
        return line, value + self.in_x[line, :].astype(f32) + self.in_y[line, :].astype(f32)

    def ship(self, src, dst, h, k, to, cols=slice(None), chunk=None):
        lines = pl.ds(h * self.half, self.half)
        if chunk is not None:
            size = self.half // self.CHUNKS
            lines = pl.ds(h * self.half + chunk * size, size)
        copy = push(
            src.at[lines, cols], dst.at[lines, cols], self.send.at[k], self.recv.at[k], {"seq": to}
        )
        copy.start()
        self.copies.append(copy)
        return copy

    def ship_corner(self, c):
        cols = self.cols(c)
        self.add_into(self.out_d, 0, 0, self.rows, (), cols)
        return (
            self.ship(self.out_d, self.in_d, 0, 2 * c, self.p.xn, cols),
            self.ship(self.out_d, self.in_d, 1, 2 * c + 1, self.p.yn, cols),
        )

    def run(self, product, emit, idle=None, polls=(None, None, None)):
        polls = [poll or (lambda: None) for poll in polls]
        p, rows, half = self.p, self.rows, self.half
        d0 = self.swap(0, p.dg, product, 0)
        d1 = self.swap(0, p.dg, product, 1)
        d0.wait_recv()
        dx0, dy0 = self.ship_corner(0)
        to_x = [self.swap(1, p.xn, product, 0)]
        d1.wait_recv()
        dx1, dy1 = self.ship_corner(1)
        to_x.append(self.swap(1, p.xn, product, 1))
        polls[0]()
        to_y = self.swap_all(2, p.yn, product)
        for copy in to_x:
            copy.wait_recv()
        self.add_into(self.out_x, 1, 0, half)
        x0 = self.ship(self.out_x, self.in_x, 0, 4, p.xn)
        for copy in to_y:
            copy.wait_recv()
        self.add_into(self.out_y, 2, half, half)
        y1 = self.ship(self.out_y, self.in_y, 1, 5, p.yn)
        polls[1]()
        to_me = self.swap_all(3, p.me, product)
        polls[2]()
        size = half // self.CHUNKS
        x1, y0 = [], []
        for copy in (dx0, dx1, dy0, dy1):
            copy.wait_recv()
        for k in range(self.CHUNKS):
            self.add_into(self.out_y, 2, k * size, size, (self.in_d,))
            y0.append(self.ship(self.out_y, self.in_y, 0, 6 + k, p.yn, chunk=k))
            self.add_into(self.out_x, 1, half + k * size, size, (self.in_d,))
            x1.append(
                self.ship(self.out_x, self.in_x, 1, 6 + self.CHUNKS + k, p.xn, chunk=k)
            )
        if idle is not None:
            idle()
        for copy in (*to_me, x0, y1):
            copy.wait_recv()
        for k in range(self.CHUNKS):
            y0[k].wait_recv()
            emit(*self.final(k * size, size))
            x1[k].wait_recv()
            emit(*self.final(half + k * size, size))
        for copy in self.copies:
            copy.wait_send()


class LineGather:
    def __init__(self, place, src, block, layers, send, recv):
        self.me, self.src, self.block, self.layers = place.layer, src, block, layers
        self.send, self.recv = send, recv
        self.step = 0

    @staticmethod
    def scratch(layers):
        return [sems(2 * layers), sems(layers)]

    def copy(self, src, layer, k, to):
        return push(src, self.block(layer), self.send.at[k], self.recv.at[layer], {"fsdp": to})

    def wait_from(self, layer):
        other = lax.rem(self.me + 1, self.layers)
        self.copy(self.block(layer), layer, 0, other).wait_recv()

    def start(self):
        me, top = self.me, self.layers - 1

        @pl.when(me < top)
        def _():
            self.copy(self.src, me, 0, me + 1).start()

        @pl.when(me > 0)
        def _():
            self.copy(self.src, me, self.layers, me - 1).start()

    def poll(self):
        me, top, hop = self.me, self.layers - 1, self.step
        self.step += 1
        below, above = me - 1 - hop, me + 1 + hop

        @pl.when((below >= 0) & (me < top))
        def _():
            self.wait_from(below)
            self.copy(self.block(below), below, hop + 1, me + 1).start()

        @pl.when((above <= top) & (me > 0))
        def _():
            self.wait_from(above)
            self.copy(self.block(above), above, self.layers + hop + 1, me - 1).start()

    def finish(self):
        while self.step < self.layers - 2:
            self.poll()
        me, top = self.me, self.layers - 1

        @pl.when(me == top)
        def _():
            for layer in range(top):
                self.wait_from(layer)

        @pl.when(me == 0)
        def _():
            for layer in range(1, top + 1):
                self.wait_from(layer)

        for hop in range(top):

            @pl.when((hop <= me) & (me < top))
            def _(hop=hop):
                self.copy(self.block(me), me, hop, me + 1).wait_send()

            @pl.when((hop <= top - me) & (me > 0))
            def _(hop=hop):
                self.copy(self.block(me), me, self.layers + hop, me - 1).wait_send()


class LineSum:
    def __init__(self, place, block, layers, own, up, down, us, ur, ds, dr, local):
        self.me, self.block, self.layers = place.layer, block, layers
        self.own, self.up, self.down = own, up, down
        self.us, self.ur, self.ds, self.dr, self.local = us, ur, ds, dr, local
        self.step = 0
        self.loads = [load(block(f), own.at[f], local.at[f]) for f in range(layers)]

    @staticmethod
    def scratch(shape, layers):
        return [
            pltpu.VMEM((layers, *shape), bf16),
            pltpu.VMEM((layers - 1, *shape), bf16),
            pltpu.VMEM((layers - 1, *shape), bf16),
            *[sems(layers)] * 5,
        ]

    refs = 8

    def up_copy(self, src, f, to):
        return push(src, self.up.at[f - 1], self.us.at[f], self.ur.at[f], {"fsdp": to})

    def down_copy(self, src, f, to):
        return push(src, self.down.at[f], self.ds.at[f], self.dr.at[f], {"fsdp": to})

    @staticmethod
    def start(*lines):
        me, top = lines[0].me, lines[0].layers - 1

        @pl.when(me == 0)
        def _():
            for f in range(top, 0, -1):
                for line in lines:
                    line.up_copy(line.block(f), f, 1).start()
            for line in lines:
                line.up[0] = jnp.zeros(line.up.shape[1:], bf16)

        @pl.when(me == top)
        def _():
            for f in range(top):
                for line in lines:
                    line.down_copy(line.block(f), f, top - 1).start()
            for line in lines:
                line.down[top - 1] = jnp.zeros(line.down.shape[1:], bf16)

    def chunks(self):
        shape = self.own.shape[1:]
        size = 1 if len(shape) == 3 else 32
        return shape[0] // size, lambda i: rows_at(i * size, size) if size > 1 else i

    def add(self, box, slot, f):
        count, where = self.chunks()

        @pl.loop(0, count)
        def _(i):
            here = where(i)
            value = box[slot, here].astype(f32) + self.own[f, here].astype(f32)
            box[slot, here] = value.astype(bf16)

    def poll(self):
        top, k = self.layers - 1, self.step
        self.step += 1
        if k == 0:
            for copy in self.loads:
                copy.wait()
        for f in range(2, top + 1):
            at = f - top + 1 + k
            if not 1 <= at < f:
                continue

            @pl.when(self.me == at)
            def _(f=f, at=at):
                self.up_copy(self.up.at[f - 1], f, at + 1).wait_recv()
                self.add(self.up, f - 1, f)
                self.up_copy(self.up.at[f - 1], f, at + 1).start()

            @pl.when(self.me == top - at)
            def _(f=top - f, at=top - at):
                self.down_copy(self.down.at[f], f, at - 1).wait_recv()
                self.add(self.down, f, f)
                self.down_copy(self.down.at[f], f, at - 1).start()

    def finish(self, emit):
        while self.step < self.layers - 2:
            self.poll()
        me, top = self.me, self.layers - 1

        @pl.when(me > 0)
        def _():
            self.up_copy(self.up.at[me - 1], me, me - 1).wait_recv()

        @pl.when(me < top)
        def _():
            self.down_copy(self.down.at[me], me, me + 1).wait_recv()

        count, where = self.chunks()
        below, above = jnp.maximum(me - 1, 0), jnp.minimum(me, top - 1)

        @pl.loop(0, count)
        def _(i):
            here = where(i)
            value = self.up[below, here].astype(f32) + self.down[above, here].astype(f32)
            emit(here, value + self.own[me, here].astype(f32))

        for f in range(1, top + 1):

            @pl.when(me < f)
            def _(f=f):
                self.up_copy(self.up.at[f - 1], f, me + 1).wait_send()

        for f in range(top):

            @pl.when(me > f)
            def _(f=f):
                self.down_copy(self.down.at[f], f, me - 1).wait_send()


class PlaneSum:
    def __init__(self, place, src, box, send, recv):
        self.p, self.src, self.box = place, src, box
        self.copies = []
        for step in range(1, PLANE):
            to = place.plane_peer(step)
            copy = push(src.at[to], box.at[step], send.at[step], recv.at[step], {"seq": to})
            copy.start()
            self.copies.append(copy)

    def total(self):
        value = self.src[self.p.me].astype(f32)
        for step, copy in enumerate(self.copies):
            copy.wait_recv()
            value = value + self.box[step + 1].astype(f32)
        return value

    def finish(self):
        for copy in self.copies:
            copy.wait_send()


class Spread:
    def __init__(self, place, src, out, send, recv, local, room=None):
        cols = src.shape[2]
        spot = out.at[:, rows_at(place.me * cols, cols)]
        if room is None:
            self.copies = [load(src.at[place.me], spot, local)]
        else:
            self.copies = [Through(src.at[place.me], room, spot, local)]
        for step in range(1, PLANE):
            to = place.plane_peer(step)
            copy = push(src.at[to], spot, send.at[step], recv.at[step], {"seq": to})
            copy.start()
            self.copies.append(copy)

    def finish(self):
        for copy in self.copies:
            copy.wait()


def fold(ref, first, value):
    rows, wide = value.shape
    total = jnp.sum(value.reshape(rows // 8, 8, wide), axis=0)
    ref[...] = total if first else ref[...] + total


class Rows:
    @staticmethod
    def scratch(rows, wide, dtype):
        return [pltpu.VMEM((rows, wide), dtype), sems(2 * Scatter.CHUNKS)]

    def __init__(self, out, stage, sem):
        self.out, self.stage, self.sem = out, stage, sem
        self.copies = []

    def put(self, line, value):
        self.stage[line, :] = value.astype(self.stage.dtype)
        self.copies.append(
            load(self.stage.at[line, :], self.out.at[line, :], self.sem.at[len(self.copies)])
        )

    def finish(self):
        for copy in self.copies:
            copy.wait()


def params(number, vmem=True):
    return pltpu.CompilerParams(
        collective_id=number,
        has_side_effects=True,
        vmem_limit_bytes=VMEM_LIMIT if vmem else None,
    )


def cost(flops, mib=40):
    return pl.CostEstimate(flops=flops, bytes_accessed=mib * 1024 * 1024, transcendentals=0)


def load(src, dst, sem):
    copy = pltpu.make_async_copy(src, dst, sem)
    copy.start()
    return copy


class Through:
    def __init__(self, src, room, dst, sem):
        self.room, self.dst, self.sem = room, dst, sem
        self.copy = load(src, room, sem)

    def put(self):
        self.copy.wait()
        self.copy = load(self.room, self.dst, self.sem)

    def wait(self):
        self.copy.wait()


def rows_of(ref, rows):
    return lambda k: ref.at[rows_at(k * rows, rows), :]


def front(
    docs, tokens, gain, shift, w_query, w_fc, w_kv, w_out, cot, bq, bv, cut, streams, heads, layers, number
):
    own_rows, depth = tokens.shape
    total = PLANE * own_rows
    cols = w_query.shape[1] // PLANE
    kv_cols = w_kv.shape[1]
    rows = own_rows // streams
    length = PLANE * rows
    block = min(QROWS, length)
    piece_rows = w_query.shape[0]
    hidden = w_fc.shape[1] // PLANE
    wo_rows = w_out.shape[0]
    cuts = (0, cut // 2, cut)

    def kernel(docs_ref, tok_ref, gain_ref, shift_ref, bq_ref, bv_ref, *refs):
        wq_ref, wf_ref, wkv_ref, wo_ref, cot_ref = refs[:5]
        h_all, kv_all, cot_all, q_out, k_out, mixed_out = refs[5:11]
        wq_all, wo_all, wf_out, wfa_all, wfb_all, lse_ref, mean_out, inverse_out = refs[11:19]
        h_buf, low_kv, kv_full, wq_own, wq_buf, wf_own, wo_room, cot_room = refs[19:27]
        q_buf, kv_buf, mixed_buf = refs[27:30]
        hs, hr, ks, kr, cs, cr = refs[30:36]
        line_refs, (qsend, qrecv, fsend, frecv, local) = refs[36:46], refs[46:]
        p = Place()

        def column_block(ref, dev):
            wide = ref.shape[1] // PLANE
            return ref.at[:, rows_at(dev * wide, wide)]

        my_pieces = [
            load(column_block(wq_ref, p.me), wq_own.at[p.me], local.at[0]),
            load(column_block(wf_ref, p.me), wf_own.at[p.me], local.at[1]),
        ]
        my_kv = load(wkv_ref, low_kv.at[rows_at(p.layer * piece_rows, piece_rows), :], local.at[2])
        own = [
            Through(wo_ref, wo_room, rows_of(wo_all, wo_rows)(p.layer), local.at[3]),
            Through(cot_ref, cot_room, rows_of(cot_all, own_rows)(p.me), local.at[4]),
        ]
        line_kv = LineGather(p, wkv_ref, rows_of(low_kv, piece_rows), layers, *line_refs[:2])
        line_wo = LineGather(p, wo_ref, rows_of(wo_all, wo_rows), layers, *line_refs[2:4])
        line_wq = LineGather(p, wq_own, lambda k: wq_buf.at[:, k], layers, *line_refs[4:6])
        wf_alls = (wfa_all, wfb_all)
        lines_wf = [
            LineGather(
                p,
                wf_own.at[pl.ds(cuts[i], cuts[i + 1] - cuts[i])],
                lambda k, i=i: wf_alls[i].at[:, k],
                layers,
                *line_refs[6 + 2 * i : 8 + 2 * i],
            )
            for i in range(2)
        ]
        p.greet(True, layers)
        line_kv.start()
        line_wo.start()

        def split(ref, out, send, recv):
            copies = []
            for step in range(1, PLANE):
                to = p.plane_peer(step)
                copies.append(
                    push(
                        column_block(ref, to),
                        out.at[p.me],
                        send.at[step],
                        recv.at[step],
                        {"seq": to},
                    )
                )
                copies[-1].start()
            return copies

        split_q = split(wq_ref, wq_own, qsend, qrecv)
        split_f = split(wf_ref, wf_own, fsend, frecv)

        @pl.loop(0, own_rows // 32)
        def _(i):
            here = rows_at(i * 32, 32)
            values = tok_ref[here, :].astype(f32)
            mean, inverse = norm_stats(values)
            h_buf[rows_at(p.me * own_rows + i * 32, 32), :] = (
                (values - mean) * inverse * gain_ref[...] + shift_ref[...]
            ).astype(bf16)
            mean_out[here, :] = mean
            inverse_out[here, :] = inverse

        g = Gather(p, h_buf, own_rows, hs, hr)
        g.start(h_buf.at[rows_at(p.me * own_rows, own_rows), :])
        for copy in own:
            copy.put()
        line_kv.poll()
        for copy in (*my_pieces, my_kv):
            copy.wait()
        for copy in split_q:
            copy.wait_recv()
        line_wq.start()
        stores = [load(wq_own, wq_buf.at[:, p.layer], local.at[5])]
        line_kv.poll()
        line_wo.poll()
        line_kv.finish()
        kv_rows = layers * piece_rows
        stores.append(load(low_kv, kv_full.at[rows_at(p.me * kv_rows, kv_rows), :], local.at[6]))
        gkv = Gather(p, kv_full, kv_rows, ks, kr)
        gkv.start(low_kv)
        line_wq.poll()
        for copy in split_f:
            copy.wait_recv()
        stores.append(load(wf_own, wf_out, local.at[7]))
        for i in range(2):
            here = pl.ds(cuts[i], cuts[i + 1] - cuts[i])
            stores.append(load(wf_own.at[here], wf_alls[i].at[:, p.layer], local.at[8 + i]))
        line_wo.poll()
        line_wq.poll()
        for line in lines_wf:
            line.start()
        g.relay_first()
        g.relay_rest()
        gkv.relay()
        gc = Gather(p, cot_all, own_rows, cs, cr)
        gc.start(cot_ref)
        lines_wf[0].poll()
        line_wq.finish()
        line_wo.finish()
        for copy in stores[:2]:
            copy.wait()
        stores.append(load(wq_buf, wq_all, local.at[10]))

        def project(dev, k):
            here = g.pair(dev)
            stores.append(load(h_buf.at[here, :], h_all.at[here, :], local.at[11 + k]))
            q = dot(h_buf[here, :], wq_buf[...].reshape(depth, cols))
            q = q + bq_ref[:, rows_at(p.me * cols, cols)]
            chip = rows_at(lax.div(dev, 2) * 2, 2)
            q_buf[chip] = q.astype(bf16).reshape(2, streams, rows, cols)

        g.have(p.sib)
        project(p.me, 0)
        g.have(p.xs)
        project(p.xn, 1)
        g.have(p.ys)
        project(p.yn, 2)
        lines_wf[1].poll()
        g.relay_corner()
        g.have(p.ds)
        project(p.dg, 3)
        stores.append(load(q_buf, q_out, local.at[15]))
        gkv.relay_corner()
        for dev in (p.sib, p.xs, p.ys, p.ds):
            gkv.have(dev)
        stores.append(load(kv_full, kv_all, local.at[16]))
        for k in range(4):
            kv = dot(h_buf[pl.ds(k * total // 4, total // 4), :], kv_full[...])
            kv = jnp.concatenate([kv[:, :HD], kv[:, HD:] + bv_ref[...]], axis=1)
            kv_buf[pl.ds(2 * k, 2)] = kv.astype(bf16).reshape(2, streams, rows, kv_cols)
        stores.append(load(kv_buf, k_out, local.at[17]))
        lines_wf[0].poll()
        for stream in range(streams):
            attend_stream(
                docs_ref,
                stream,
                q_buf.at[:, stream],
                kv_buf.at[:, stream],
                mixed_buf.at[:, stream],
                lse_ref.at[stream],
                block,
                heads,
            )
            if stream == 0:
                gc.relay_first()
                lines_wf[1].poll()
        stores.append(load(mixed_buf, mixed_out, local.at[18]))
        gc.relay_rest()
        gc.relay_corner()
        for dev in (p.sib, p.xs, p.ys, p.ds):
            gc.have(dev)
        for item in (g, gkv, gc, *lines_wf):
            item.finish()
        for copy in (*split_q, *split_f):
            copy.wait_send()
        for copy in (*own, *stores[2:]):
            copy.wait()

    q_shape = (PLANE, streams, rows, cols)
    kv_shape = (PLANE, streams, rows, kv_cols)
    wq_shape = (PLANE, layers, piece_rows, cols)
    wf_shape = (PLANE, piece_rows, hidden)
    half = [(cuts[i + 1] - cuts[i], layers, piece_rows, hidden) for i in range(2)]
    return pl.pallas_call(
        kernel,
        out_shape=[
            jax.ShapeDtypeStruct((total, depth), bf16),
            jax.ShapeDtypeStruct((depth, kv_cols), bf16),
            jax.ShapeDtypeStruct((total, cot.shape[1]), bf16),
            jax.ShapeDtypeStruct(q_shape, bf16),
            jax.ShapeDtypeStruct(kv_shape, bf16),
            jax.ShapeDtypeStruct(q_shape, bf16),
            jax.ShapeDtypeStruct(wq_shape, bf16),
            jax.ShapeDtypeStruct((layers * wo_rows, w_out.shape[1]), bf16),
            jax.ShapeDtypeStruct(wf_shape, bf16),
            jax.ShapeDtypeStruct(half[0], bf16),
            jax.ShapeDtypeStruct(half[1], bf16),
            jax.ShapeDtypeStruct((streams, heads, length), f32),
            jax.ShapeDtypeStruct((own_rows, 1), f32),
            jax.ShapeDtypeStruct((own_rows, 1), f32),
        ],
        in_specs=[pl.BlockSpec(memory_space=pltpu.SMEM)] + [WHOLE] * 5 + [ANY] * 5,
        out_specs=[ANY] * 11 + [WHOLE] * 3,
        scratch_shapes=[
            pltpu.VMEM((total, depth), bf16),
            pltpu.VMEM((layers * piece_rows, kv_cols), bf16),
            pltpu.VMEM((depth, kv_cols), bf16),
            pltpu.VMEM((PLANE, piece_rows, cols), bf16),
            pltpu.VMEM(wq_shape, bf16),
            pltpu.VMEM(wf_shape, bf16),
            pltpu.VMEM(w_out.shape, bf16),
            pltpu.VMEM(cot.shape, bf16),
            pltpu.VMEM(q_shape, bf16),
            pltpu.VMEM(kv_shape, bf16),
            pltpu.VMEM(q_shape, bf16),
        ]
        + Gather.scratch() * 3
        + LineGather.scratch(layers) * 5
        + [sems(PLANE)] * 4
        + [sems(19)],
        compiler_params=params(number),
        cost_estimate=cost(2 * total * depth * (cols + kv_cols)),
        name="front",
    )(docs, tokens, gain, shift, bq, bv, w_query, w_fc, w_kv, w_out, cot)


def load_parts(parts, dst, local):
    copies, at = [], 0
    for i, part in enumerate(parts):
        rows = part.shape[0]
        copies.append(load(part, dst.at[pl.ds(at, rows), :], local.at[i]))
        at += rows
    return copies


def load_blocks(parts, dst, local):
    copies, at = [], 0
    for layer in range(parts[0].shape[0]):
        for part in parts:
            rows = part.shape[1]
            copies.append(load(part.at[layer], dst.at[pl.ds(at, rows), :], local.at[len(copies)]))
            at += rows
    return copies


def middle(
    mixed, wo, tokens, b_out, gain, shift, wf, piece, bf, cot_all, w_proj, layers, number
):
    total, depth = mixed.shape
    rows = total // PLANE
    wide = wo.shape[1]
    n_wf = len(wf)
    piece, first, last = piece
    piece_rows, hidden = piece.shape[1:]
    w_shape = (piece.shape[0], layers, piece_rows, hidden)
    out_wide = cot_all.shape[1]
    half, proj_half = rows // 2, w_proj.shape[0] // 2
    tiles, tile = 4, hidden // 4

    def kernel(mixed_ref, wo_ref, piece_ref, proj_ref, cot_ref, *refs):
        wf_refs, refs = refs[:n_wf], refs[n_wf:]
        tok_ref, bias_ref, gain_ref, shift_ref, bf_ref = refs[:5]
        residual, all_ref, act_ref, slope_ref, dw_ref, piece_all, proj_all = refs[5:12]
        mean_out, inverse_out = refs[12:14]
        a_buf, wo_buf, proj_room, buf, w_buf, act, slope, cot, dw = refs[14:23]
        s, line_refs, residual_refs = refs[23:37], refs[37:43], refs[43:45]
        send, recv, local, store_sem = refs[45:]
        residual = Rows(residual, *residual_refs)
        acc = s[1]
        p = Place()
        piece_ref = piece_ref.at[pl.ds(first, last - first)]
        w_rest = w_buf.at[pl.ds(first, last - first)]
        loads = [load(mixed_ref, a_buf, local.at[0]), load(wo_ref, wo_buf, local.at[1])]
        own = Through(proj_ref, proj_room, proj_all.at[p.layer], local.at[2])
        loads_w, at = [load(piece_ref, w_rest.at[:, p.layer], local.at[3])], 0
        for i, ref in enumerate(wf_refs):
            loads_w.append(load(ref, w_buf.at[pl.ds(at, ref.shape[0])], local.at[4 + i]))
            at += ref.shape[0]
        line_fc = LineGather(p, piece_ref, lambda k: w_rest.at[:, k], layers, *line_refs[:2])
        lines_proj = [
            LineGather(
                p,
                proj_ref.at[pl.ds(i * proj_half, proj_half), :],
                lambda k, i=i: proj_all.at[k, pl.ds(i * proj_half, proj_half), :],
                layers,
                *line_refs[2 + 2 * i : 4 + 2 * i],
            )
            for i in range(2)
        ]
        p.greet(False, layers)
        line_fc.start()
        g = Gather(p, buf, rows, send, recv, 2)
        cots, stores = {}, []

        def fetch(k, dev):
            cots[k] = load(cot_ref.at[g.pair(dev), :], cot.at[k % 2], local.at[4 + n_wf + k % 2])

        def keep(src, dst):
            stores.append(load(src, dst, store_sem.at[len(stores)]))

        fetch(0, p.me)
        fetch(1, p.xn)
        for copy in loads:
            copy.wait()
        my_rows = [g.piece(p.me, k) for k in range(4)]

        def emit(line, value):
            values = tok_ref[line, :].astype(f32) + value + bias_ref[...]
            mean, inverse = norm_stats(values)
            residual.put(line, values)
            buf[rows_at(p.me * rows + line.start, line.size), :] = (
                (values - mean) * inverse * gain_ref[...] + shift_ref[...]
            ).astype(bf16)
            mean_out[line, :] = mean
            inverse_out[line, :] = inverse
            done = line.start + line.size - half
            if done > 0 and done % g.size == 0:
                g.start_piece(done // g.size - 1, my_rows)

        def poll_fc():
            line_fc.poll()
            if line_fc.step == 1:
                own.put()
            lines_proj[line_fc.step - 1].start()

        Scatter.take(p, rows, s).run(
            plain_product(a_buf, wo_buf), emit, lines_proj[0].poll, (poll_fc, None, poll_fc)
        )
        g.start_rest(my_rows)

        def work(dev):
            block = g.pair(dev)
            keep(buf.at[block, :], all_ref.at[block, :])

            @pl.loop(0, hidden // 512)
            def _(j):
                cols = rows_at(j * 512, 512)
                value = dot(buf[block, :], w_buf[:, :, :, cols].reshape(wide, 512))
                value = value + bf_ref[:, rows_at(p.me * hidden + j * 512, 512)]
                activated, gradient = gelu_pair(value)
                act[block, cols] = activated.astype(bf16)
                slope[block, cols] = gradient.astype(bf16)

            keep(act.at[block, :], act_ref.at[block, :])
            keep(slope.at[block, :], slope_ref.at[block, :])

        def grads(k, dev):
            block = g.pair(dev)
            cots[k].wait()
            for j in range(tiles):
                cols = pl.ds(j * tile, tile)
                term = dot_tn(act[block, cols], cot[k % 2])
                if k == 0:
                    acc[j] = term
                elif k < 3:
                    acc[j] += term
                else:
                    dw[j] = (acc[j] + term).astype(bf16)
                    keep(dw.at[j], dw_ref.at[cols, :])

        lines_proj[1].poll()
        line_fc.finish()
        for copy in loads_w:
            copy.wait()
        keep(w_rest, piece_all)
        g.have(p.sib)
        work(p.me)
        grads(0, p.me)
        fetch(2, p.yn)
        g.relay_first()
        lines_proj[0].poll()
        g.relay_rest()
        g.have(p.xs)
        work(p.xn)
        g.have(p.ys)
        work(p.yn)
        lines_proj[1].poll()
        grads(1, p.xn)
        fetch(3, p.dg)
        g.relay_corner()
        grads(2, p.yn)
        g.have(p.ds)
        work(p.dg)
        grads(3, p.dg)
        g.finish()
        for line in lines_proj:
            line.finish()
        own.wait()
        residual.finish()
        for copy in stores:
            copy.wait()

    return pl.pallas_call(
        kernel,
        out_shape=[
            jax.ShapeDtypeStruct((rows, wide), f32),
            jax.ShapeDtypeStruct((total, wide), bf16),
            jax.ShapeDtypeStruct((total, hidden), bf16),
            jax.ShapeDtypeStruct((total, hidden), bf16),
            jax.ShapeDtypeStruct((hidden, out_wide), bf16),
            jax.ShapeDtypeStruct((last - first, *w_shape[1:]), bf16),
            jax.ShapeDtypeStruct((layers, *w_proj.shape), bf16),
            jax.ShapeDtypeStruct((rows, 1), f32),
            jax.ShapeDtypeStruct((rows, 1), f32),
        ],
        in_specs=[ANY] * (5 + n_wf) + [WHOLE] * 5,
        out_specs=[ANY] * 7 + [WHOLE] * 2,
        scratch_shapes=[
            pltpu.VMEM(mixed.shape, bf16),
            pltpu.VMEM(wo.shape, bf16),
            pltpu.VMEM(w_proj.shape, bf16),
            pltpu.VMEM((total, wide), bf16),
            pltpu.VMEM(w_shape, bf16),
            pltpu.VMEM((total, hidden), bf16),
            pltpu.VMEM((total, hidden), bf16),
            pltpu.VMEM((2, 2 * rows, out_wide), bf16),
            pltpu.VMEM((tiles, tile, out_wide), bf16),
        ]
        + Scatter.scratch(rows, wide)
        + LineGather.scratch(layers) * 3
        + Rows.scratch(rows, wide, f32)
        + Gather.scratch(2)
        + [sems(6 + n_wf), sems(13 + tiles)],
        compiler_params=params(number),
        cost_estimate=cost(4 * total * wide * hidden),
        name="middle",
    )(mixed, wo, piece, w_proj, cot_all, *wf, tokens, b_out, gain, shift, bf)


def gather_out(
    grad_attn, wo, mixed, hidden2, grad_pre, first_fc, grad_proj, proj_done, fc_part, layers, number
):
    rows, depth = grad_attn.shape
    wide = wo.shape[0]
    total = PLANE * rows
    hidden = grad_pre.shape[1]
    tile = 512
    steps = (depth - first_fc) // tile
    proj_cut = proj_done.shape[0]
    proj_shape = (grad_proj.shape[1] - proj_cut, grad_proj.shape[2])
    fc_shape = (fc_part.shape[0], *fc_part.shape[2:])

    def kernel(own_ref, w_ref, mixed_ref, h_ref, gp_ref, proj_ref, fc_ref, done_ref, *refs):
        gm_ref, dw_ref, dwfc_ref, proj_out, fc_out = refs[:5]
        buf, w_buf, mixed_buf, gm, acc, dw, gp, h_buf, dwfc = refs[5:14]
        send, recv = refs[14:16]
        line_refs = refs[16:32]
        (local,) = refs[32:]
        p = Place()
        load_own = load(own_ref, buf.at[rows_at(p.me * rows, rows), :], local.at[0])
        loads = [load(w_ref, w_buf, local.at[1]), load(mixed_ref, mixed_buf, local.at[2])]
        load_gp = load(gp_ref, gp, local.at[3])
        proj = LineSum(p, lambda f: proj_ref.at[f, pl.ds(proj_cut, proj_shape[0]), :], layers, *line_refs[:8])
        fc = LineSum(p, lambda f: fc_ref.at[:, f], layers, *line_refs[8:])

        def h_fetch(i):
            here = pl.ds(first_fc + i * tile, tile)
            return load(h_ref.at[:, here], h_buf.at[i % 2], local.at[4 + i % 2])

        tiles = [h_fetch(0)]
        stores = []
        p.greet(False, layers)
        g = Gather(p, buf, rows, send, recv)
        g.start(own_ref)
        LineSum.start(proj, fc)

        def work(dev):
            block = g.pair(dev)
            gm[block, :] = dot_nt(buf[block, :], w_buf[...]).astype(bf16)

        def grads(k, dev):
            block = g.pair(dev)
            term = dot_tn(mixed_buf[block, :], buf[block, :])
            if k == 0:
                acc[...] = term
            elif k < 3:
                acc[...] += term
            else:
                dw[...] = (acc[...] + term).astype(bf16)

        def fc_grads(i):
            tiles[i].wait()
            if i + 1 < steps:
                tiles.append(h_fetch(i + 1))
            if i >= 2:
                stores[i - 2].wait()
            dwfc[i % 2] = dot_tn(h_buf[i % 2], gp[...]).astype(bf16)
            stores.append(
                load(dwfc.at[i % 2], dwfc_ref.at[pl.ds(i * tile, tile), :], local.at[6 + i % 2])
            )

        load_own.wait()
        for copy in loads:
            copy.wait()
        g.have(p.sib)
        work(p.me)
        grads(0, p.me)
        for i in range(0, proj_cut, 32):
            proj_out[pl.ds(i, 32), :] = done_ref[pl.ds(i, 32), :].astype(f32)
        load_gp.wait()
        fc_grads(0)
        proj.poll()
        g.relay_first()
        fc_grads(1)
        fc.poll()
        for i in range(2, steps):
            fc_grads(i)
        proj.poll()
        g.relay_rest()
        fc.poll()
        g.have(p.xs)
        work(p.xn)
        g.have(p.ys)
        work(p.yn)
        grads(1, p.xn)
        g.relay_corner()
        grads(2, p.yn)
        g.have(p.ds)
        work(p.dg)
        store = load(gm, gm_ref, local.at[8])
        grads(3, p.dg)
        store_dw = load(dw, dw_ref, local.at[9])
        g.finish()

        def keep_proj(where, value):
            proj_out[pl.ds(proj_cut + where.start, where.size), :] = value

        def keep_fc(where, value):
            fc_out[where] = value.astype(bf16)

        proj.finish(keep_proj)
        fc.finish(keep_fc)
        store.wait()
        store_dw.wait()
        for copy in stores[-2:]:
            copy.wait()

    return pl.pallas_call(
        kernel,
        out_shape=[
            jax.ShapeDtypeStruct((total, wide), bf16),
            jax.ShapeDtypeStruct((wide, depth), bf16),
            jax.ShapeDtypeStruct((depth - first_fc, hidden), bf16),
            jax.ShapeDtypeStruct(grad_proj.shape[1:], f32),
            jax.ShapeDtypeStruct(fc_shape, bf16),
        ],
        in_specs=[ANY] * 7 + [WHOLE],
        out_specs=[ANY] * 3 + [WHOLE] * 2,
        scratch_shapes=[
            pltpu.VMEM((total, depth), bf16),
            pltpu.VMEM(wo.shape, bf16),
            pltpu.VMEM(mixed.shape, bf16),
            pltpu.VMEM((total, wide), bf16),
            pltpu.VMEM((wide, depth), f32),
            pltpu.VMEM((wide, depth), bf16),
            pltpu.VMEM(grad_pre.shape, bf16),
            pltpu.VMEM((2, total, tile), bf16),
            pltpu.VMEM((2, tile, hidden), bf16),
        ]
        + Gather.scratch()
        + LineSum.scratch(proj_shape, layers)
        + LineSum.scratch(fc_shape, layers)
        + [sems(10)],
        compiler_params=params(number),
        cost_estimate=cost(4 * total * depth * wide),
        name="gather_out",
    )(grad_attn, wo, mixed, hidden2, grad_pre, grad_proj, fc_part, proj_done)


def plain_product(a_buf, w_buf):
    half = w_buf.shape[1] // 2

    def product(role, here, c):
        return dot(a_buf[here, :], w_buf[:, pl.ds(c * half, half)])

    return product


def scatter_fc(cot_all, slope, wp, wf, hidden2, back, grad_proj, proj_cut, layers, number):
    total, depth = cot_all.shape
    rows = total // PLANE
    wide = slope.shape[1]
    tile = 512
    n_wp, n_wf = len(wp), len(wf)
    proj_shape = (proj_cut, grad_proj.shape[2])
    cuts = (0, proj_cut // 64 * 32, proj_cut)

    def kernel(cot_ref, slope_ref, h_ref, proj_ref, *refs):
        wp_refs, wf_refs, refs = refs[:n_wp], refs[n_wp : n_wp + n_wf], refs[n_wp + n_wf :]
        cot_own, residual_ref, mean_ref, inverse_ref, gain_ref = refs[:5]
        grad_residual, grad_attn, sums_ref, bias_ref, gp_ref, dw_ref, proj_out = refs[5:12]
        cot, slopes, wp_buf, wf_buf, gp, h_buf, dw_buf, folds = refs[12:20]
        s, line_refs = refs[20:34], refs[34:50]
        local, wlocal = refs[50:52]
        grad_residual, grad_attn = Rows(grad_residual, *refs[52:54]), Rows(grad_attn, *refs[54:56])
        p = Place()
        proj = [
            LineSum(
                p,
                lambda f, i=i: proj_ref.at[f, pl.ds(cuts[i], cuts[i + 1] - cuts[i]), :],
                layers,
                *line_refs[8 * i : 8 * i + 8],
            )
            for i in range(2)
        ]
        order = (p.dg, p.xn, p.yn, p.me)

        def chip(dev):
            return rows_at(lax.div(dev, 2) * (2 * rows), 2 * rows)

        def fetch(k):
            here = chip(order[k])
            return (
                load(cot_ref.at[here, :], cot.at[k % 2], local.at[k % 2]),
                load(slope_ref.at[here, :], slopes.at[k % 2], local.at[2 + k % 2]),
            )

        fetches = [fetch(0)]
        loads_wp = load_blocks(wp_refs, wp_buf, wlocal)
        loads_wf = load_parts(wf_refs, wf_buf, local.at[pl.ds(4, n_wf)])
        load_h = load(h_ref.at[:, pl.ds(0, tile)], h_buf, local.at[4 + n_wf])
        bias_ref[...] = jnp.zeros_like(bias_ref)
        p.greet(False, layers)
        LineSum.start(*proj)
        for copy in loads_wp:
            copy.wait()
        half = depth // 2

        def back_through_gelu(k):
            for copy in fetches[k]:
                copy.wait()
            if k < 3:
                fetches.append(fetch(k + 1))
            here = chip(order[k])

            @pl.loop(0, wide // 512)
            def _(j):
                cols = rows_at(j * 512, 512)
                grad_act = dot_nt(cot[k % 2], wp_buf[cols, :])
                grad_pre = (grad_act * slopes[k % 2, :, cols].astype(f32)).astype(bf16)
                gp[here, cols] = grad_pre
                bias_ref[:, cols] += jnp.sum(grad_pre.astype(f32), axis=0, keepdims=True)

            if k == 0:
                for copy in loads_wf:
                    copy.wait()

        def product(role, here, c):
            if c == 0:
                back_through_gelu(role)
            return dot_nt(gp[here, :], wf_buf[pl.ds(c * half, half), :])

        def emit(line, value):
            first = line.start == 0
            grad_out = cot_own[line, :].astype(f32)
            back = inverse_ref[line, :]
            normed = (residual_ref[line, :] - mean_ref[line, :]) * back
            result = grad_out + norm_back(value, normed, back, gain_ref[...])
            low = result.astype(bf16)
            grad_residual.put(line, result)
            grad_attn.put(line, low)
            for i, term in enumerate((value * normed, value, low.astype(f32), grad_out)):
                fold(folds.at[i], first, term)

        stores = []

        def last_poll():
            stores.append(load(gp, gp_ref, local.at[5 + n_wf]))
            proj[0].poll()

        def idle():
            load_h.wait()
            dw_buf[...] = dot_tn(h_buf[...], gp[...]).astype(bf16)
            stores.append(load(dw_buf, dw_ref, local.at[6 + n_wf]))
            proj[1].poll()

        Scatter.take(p, rows, s).run(
            product, emit, idle, (proj[0].poll, proj[1].poll, last_poll)
        )
        sums_ref[...] = jnp.sum(folds[...], axis=1)
        for i in range(2):

            def keep(where, value, i=i):
                proj_out[pl.ds(cuts[i] + where.start, where.size), :] = value.astype(bf16)

            proj[i].finish(keep)
        for copy in stores:
            copy.wait()
        grad_residual.finish()
        grad_attn.finish()

    return pl.pallas_call(
        kernel,
        out_shape=[
            jax.ShapeDtypeStruct((rows, depth), f32),
            jax.ShapeDtypeStruct((rows, depth), bf16),
            jax.ShapeDtypeStruct((4, depth), f32),
            jax.ShapeDtypeStruct((1, wide), f32),
            jax.ShapeDtypeStruct((total, wide), bf16),
            jax.ShapeDtypeStruct((tile, wide), bf16),
            jax.ShapeDtypeStruct(proj_shape, bf16),
        ],
        in_specs=[ANY] * (4 + n_wp + n_wf) + [WHOLE] * 5,
        out_specs=[ANY] * 2 + [WHOLE] * 2 + [ANY] * 2 + [WHOLE],
        scratch_shapes=[
            pltpu.VMEM((2, 2 * rows, depth), bf16),
            pltpu.VMEM((2, 2 * rows, wide), bf16),
            pltpu.VMEM((wide, depth), bf16),
            pltpu.VMEM((depth, wide), bf16),
            pltpu.VMEM((total, wide), bf16),
            pltpu.VMEM((total, tile), bf16),
            pltpu.VMEM((tile, wide), bf16),
            pltpu.VMEM((4, 8, depth), f32),
        ]
        + Scatter.scratch(rows, depth)
        + LineSum.scratch((cuts[1], depth), layers)
        + LineSum.scratch((proj_cut - cuts[1], depth), layers)
        + [sems(7 + n_wf), sems(n_wp * layers)]
        + Rows.scratch(rows, depth, f32)
        + Rows.scratch(rows, depth, bf16),
        compiler_params=params(number),
        cost_estimate=cost(6 * total * depth * wide),
        name="scatter_fc",
    )(cot_all, slope, hidden2, grad_proj, *wp, *wf, *back)


LANES = 128


def scatter_query(
    gq, gkv, wq, w_kv, grad_w_query, grad_w_kv, fc_done, fc_part, back, sums, layers, number
):
    total, cols = gq.shape
    kv_cols = gkv.shape[1]
    rows = total // PLANE
    depth = wq.shape[0]
    wide = depth + kv_cols
    q_shape = (grad_w_query.shape[0], *grad_w_query.shape[2:])
    fc_part, first, last = fc_part
    fc_shape = (last - first, *fc_part.shape[2:])
    my_hidden = sums[1].shape[1]
    places, lines_total = {}, 0
    for name, size in (
        ("ln1_gain", depth),
        ("ln1_bias", depth),
        ("b_query", PLANE * cols),
        ("b_value", kv_cols // 2),
        ("b_out", depth),
        ("ln2_gain", depth),
        ("ln2_bias", depth),
        ("b_fc", PLANE * my_hidden),
        ("b_proj", depth),
    ):
        places[name] = lines_total
        lines_total += size // LANES
    padded = -(-lines_total // (8 * PLANE)) * 8
    n_done = len(fc_done)
    done_cut = sum(a.shape[0] for a in fc_done)
    fc_rows, fc_cols = fc_shape[1:]
    kv_rows = rows // layers

    def kernel(gq_ref, gkv_ref, wq_ref, wkv_ref, dwq_ref, dwkv_ref, fc_ref, *refs):
        tok_ref, mean_ref, inverse_ref, gain_ref, residual_ref = refs[:5]
        sums2_ref, sums_fc_ref, sums_q_ref, sums_kv_ref = refs[5:9]
        done_refs, refs = refs[9 : 9 + n_done], refs[9 + n_done :]
        out_ref, vec_out, dwkv_out, fc_out, dwq_out = refs[:5]
        g_buf, wq_buf, wkv_buf, dwkv_buf, q_sum, folds = refs[5:11]
        vec, box, zbox, plane_sum, pieces, dwkv, kv_box = refs[11:18]
        s, line_refs = refs[18:32], refs[32:48]
        qsend, qrecv, local = refs[48:51]
        result = Rows(out_ref, *refs[51:53])
        vsend, vrecv, zsend, zrecv, gsend, grecv, fsend, frecv, ksend, krecv, flocal = refs[53:]
        p = Place()
        at, done_loads = 0, []
        for i, ref in enumerate(done_refs):
            done_loads.append(load(ref, pieces.at[pl.ds(at, ref.shape[0])], flocal.at[i]))
            at += ref.shape[0]

        def pack(at, row):
            for k in range(row.shape[1] // LANES):
                line = at + k
                vec[lax.div(line, padded), pl.ds(lax.rem(line, padded), 1), :] = row[
                    :, k * LANES : (k + 1) * LANES
                ]

        fc_spot = fc_out.at[:, rows_at(p.me * fc_cols, fc_cols)]

        def fc_copy(step):
            to = p.plane_peer(step)
            return push(pieces.at[to], fc_spot, fsend.at[step], frecv.at[step], {"seq": to})

        def spread_fc():
            for step in range(1, PLANE):
                fc_copy(step).start()

        q_side, kv_side = pl.ds(0, cols), pl.ds(cols, kv_cols)
        loads = [
            load(gq_ref, g_buf.at[:, q_side], local.at[0]),
            load(gkv_ref, g_buf.at[:, kv_side], local.at[1]),
            load(wq_ref, wq_buf, local.at[2]),
            load(wkv_ref, wkv_buf, local.at[3]),
            load(dwkv_ref, dwkv_buf, local.at[4]),
        ]
        line_q = LineSum(p, lambda f: dwq_ref.at[:, f], layers, *line_refs[:8])
        line_fc = LineSum(p, lambda f: fc_ref.at[pl.ds(first, last - first), f], layers, *line_refs[8:])
        p.greet(True, layers)
        LineSum.start(line_q, line_fc)
        for copy in loads:
            copy.wait()
        half = wide // 2

        def product(role, here, c):
            where = pl.ds(c * half, min(half, depth - c * half))
            value = dot_nt(g_buf[here, q_side], wq_buf[where, :]) + dot_nt(
                g_buf[here, kv_side], wkv_buf[where, :]
            )
            if c == 0:
                return value
            return jnp.concatenate([value, dwkv_buf[here, :].astype(f32)], axis=1)

        later = []

        def idle():
            def keep(where, value):
                q_sum[where] = value.astype(bf16)

            for copy in done_loads:
                copy.wait()
            vec[...] = jnp.zeros_like(vec)
            for i, name in enumerate(("ln2_gain", "ln2_bias", "b_out", "b_proj")):
                pack(places[name], sums2_ref[i : i + 1, :])
            pack(places["b_fc"] + p.me * (my_hidden // LANES), sums_fc_ref[...])
            pack(places["b_query"] + p.me * (cols // LANES), sums_q_ref[...])
            pack(places["b_value"], sums_kv_ref[:, kv_cols // 2 :])
            line_fc.poll()
            line_q.finish(keep)
            later.append(Spread(p, q_sum, dwq_out, qsend, qrecv, local.at[5]))

        def emit(line, value):
            begin = line.start == 0
            grad = value[:, :depth]
            normed = (tok_ref[line, :].astype(f32) - mean_ref[line, :]) * inverse_ref[line, :]
            result.put(
                line,
                residual_ref[line, :]
                + norm_back(grad, normed, inverse_ref[line, :], gain_ref[...]),
            )
            fold(folds.at[0], begin, grad * normed)
            fold(folds.at[1], begin, grad)
            dwkv[line, :] = value[:, depth:].astype(bf16)

        def keep_fc(where, value):
            pieces[done_cut + where] = value.astype(bf16)

        polls = (line_q.poll, line_fc.poll, line_q.poll)
        Scatter.take(p, rows, s).run(product, emit, idle, polls)
        for i, name in enumerate(("ln1_gain", "ln1_bias")):
            pack(places[name], jnp.sum(folds[i], axis=0, keepdims=True))
        plane = PlaneSum(p, vec, box, vsend, vrecv)
        across = []

        def kv_block(layer):
            return dwkv.at[rows_at(layer * kv_rows, kv_rows), :]

        for step in range(1, layers):
            to = p.line_peer(step, layers)
            across.append(
                push(kv_block(to), kv_box.at[step], ksend.at[step], krecv.at[step], {"fsdp": to})
            )
            across[-1].start()
        line_fc.finish(keep_fc)
        spread_fc()
        my_fc = load(pieces.at[p.me], fc_spot, flocal.at[n_done])
        total_vec = plane.total()
        plane_sum[...] = total_vec
        zbox[0] = total_vec
        for step in range(1, layers):
            to = p.line_peer(step, layers)
            across.append(
                push(plane_sum, zbox.at[step], zsend.at[step], zrecv.at[step], {"fsdp": to})
            )
            across[-1].start()
        for copy in across:
            copy.wait_recv()
        total_vec = None
        for k in range(layers):
            term = zbox[lax.rem(p.layer - k + layers, layers)]
            total_vec = term if total_vec is None else total_vec + term
        vec_out[p.me] = total_vec
        for step in range(1, PLANE):
            to = p.plane_peer(step)
            mine = vec_out.at[p.me]
            later.append(push(mine, mine, gsend.at[step], grecv.at[step], {"seq": to}))
            later[-1].start()
        value = dwkv[rows_at(p.layer * kv_rows, kv_rows), :].astype(f32)
        for step in range(1, layers):
            value = value + kv_box[step].astype(f32)
        dwkv_out[...] = value
        for item in (*later, result):
            item.finish() if hasattr(item, "finish") else item.wait()
        for step in range(1, PLANE):
            fc_copy(step).wait()
        my_fc.wait()
        plane.finish()
        for copy in across:
            copy.wait_send()

    return pl.pallas_call(
        kernel,
        out_shape=[
            jax.ShapeDtypeStruct((rows, depth), f32),
            jax.ShapeDtypeStruct((PLANE, padded, LANES), f32),
            jax.ShapeDtypeStruct((kv_rows, kv_cols), f32),
            jax.ShapeDtypeStruct((fc_rows, PLANE * fc_cols), bf16),
            jax.ShapeDtypeStruct((q_shape[1], PLANE * q_shape[2]), bf16),
        ],
        in_specs=[ANY] * 7 + [WHOLE] * 9 + [ANY] * n_done,
        out_specs=[ANY, WHOLE, WHOLE, ANY, ANY],
        scratch_shapes=[
            pltpu.VMEM((total, cols + kv_cols), bf16),
            pltpu.VMEM(wq.shape, bf16),
            pltpu.VMEM(w_kv.shape, bf16),
            pltpu.VMEM(grad_w_kv.shape, bf16),
            pltpu.VMEM(q_shape, bf16),
            pltpu.VMEM((2, 8, depth), f32),
            pltpu.VMEM((PLANE, padded, LANES), f32),
            pltpu.VMEM((PLANE, padded, LANES), f32),
            pltpu.VMEM((layers, padded, LANES), f32),
            pltpu.VMEM((padded, LANES), f32),
            pltpu.VMEM((PLANE, fc_rows, fc_cols), bf16),
            pltpu.VMEM((rows, kv_cols), bf16),
            pltpu.VMEM((layers, kv_rows, kv_cols), bf16),
        ]
        + Scatter.scratch(rows, wide)
        + LineSum.scratch(q_shape, layers)
        + LineSum.scratch(fc_shape, layers)
        + [sems(PLANE)] * 2
        + [sems(6)]
        + Rows.scratch(rows, depth, f32)
        + [sems(PLANE)] * 2
        + [sems(layers)] * 2
        + [sems(PLANE)] * 4
        + [sems(layers)] * 2
        + [sems(n_done + 1)],
        compiler_params=params(number),
        cost_estimate=cost(2 * total * depth * (cols + kv_cols)),
        name="scatter_query",
    )(gq, gkv, wq, w_kv, grad_w_query, grad_w_kv, fc_part, *back, *sums, *fc_done)


def starts_of(docs, stream, positions):
    start = jnp.zeros_like(positions)
    for j in range(docs.shape[1]):
        here = docs[stream, j]
        start = jnp.maximum(start, jnp.where(here <= positions, here, 0))
    return start


def masked_scores(docs, stream, keys, q, first, limit):
    scores = dot_nt(keys, q) * (HD**-0.5)
    t = first + lax.broadcasted_iota(jnp.int32, (1, q.shape[0]), 1)
    u = lax.broadcasted_iota(jnp.int32, scores.shape, 0)
    return scores, (u >= starts_of(docs, stream, t)) & (u <= t)


QROWS = 256


def attend_stream(docs, stream, q_ref, kv_ref, mixed_ref, lse_ref, block, heads):
    groups, rows, cols = q_ref.shape
    length = groups * rows
    kv = kv_ref[...].reshape(length, 2 * HD)
    keys = kv[:, :HD]
    values_t = kv[:, HD:].T
    per = block // rows
    for b in range(length // block):
        limit = (b + 1) * block
        q_rows = q_ref[b * per : (b + 1) * per].reshape(block, cols)
        for h in range(heads):
            q = q_rows[:, h * HD : (h + 1) * HD]
            scores, allowed = masked_scores(docs, stream, keys[:limit], q, b * block, limit)
            scores = jnp.where(allowed, scores, -1e30)
            top = jnp.max(scores, axis=0, keepdims=True)
            weights = jnp.exp(scores - top)
            total = jnp.sum(weights, axis=0, keepdims=True)
            mixed = dot(values_t[:, :limit], weights.astype(bf16)) / total
            mixed_ref[b * per : (b + 1) * per, :, h * HD : (h + 1) * HD] = (
                mixed.T.astype(bf16).reshape(per, rows, HD)
            )
            lse_ref[h : h + 1, b * block : (b + 1) * block] = top + jnp.log(total)


def attend_stream_back(docs, stream, q_ref, kv_ref, g_ref, lse_ref, gq_ref, gkv_ref, gk, gv, heads):
    groups, rows, cols = q_ref.shape
    length = groups * rows
    block = min(QROWS, length)
    kv = kv_ref[...].reshape(length, 2 * HD)
    keys, values = kv[:, :HD], kv[:, HD:]
    keys_t = keys.T
    per = block // rows
    gk[...] = jnp.zeros_like(gk)
    gv[...] = jnp.zeros_like(gv)
    for b in range(length // block):
        limit = (b + 1) * block
        q_rows = q_ref[b * per : (b + 1) * per].reshape(block, cols)
        g_rows = g_ref[b * per : (b + 1) * per].reshape(block, cols)
        for h in range(heads):
            q = q_rows[:, h * HD : (h + 1) * HD]
            g = g_rows[:, h * HD : (h + 1) * HD]
            scores, allowed = masked_scores(docs, stream, keys[:limit], q, b * block, limit)
            shift = lse_ref[h : h + 1, b * block : (b + 1) * block]
            probs = jnp.where(allowed, jnp.exp(scores - shift), 0.0)
            grad_probs = dot_nt(values[:limit], g)
            weighted = probs * grad_probs
            delta = jnp.sum(weighted, axis=0, keepdims=True)
            grad_scores = (weighted - probs * delta).astype(bf16)
            gq = dot(keys_t[:, :limit], grad_scores) * (HD**-0.5)
            gq_ref[b * per : (b + 1) * per, :, h * HD : (h + 1) * HD] = (
                gq.T.astype(bf16).reshape(per, rows, HD)
            )
            gk[:limit, :] += dot(grad_scores, q)
            gv[:limit, :] += dot(probs.astype(bf16), g)
    gkv_ref[:, :, :HD] = (gk[...] * (HD**-0.5)).astype(bf16).reshape(groups, rows, HD)
    gkv_ref[:, :, HD:] = gv[...].astype(bf16).reshape(groups, rows, HD)


def attend_back_scatter_proj(
    docs, queries, keyval, grads, lse, act, wp, hidden1, out_part, fc_part, residual, b_proj,
    layers, heads, number
):
    groups, streams, rows, cols = queries.shape
    kv_cols = keyval.shape[3]
    length = groups * rows
    total, depth = act.shape
    own = total // PLANE
    wide = hidden1.shape[1]
    part = hidden1.shape[1] // PLANE
    n_wp = len(wp)
    out_shape = out_part.shape[1:]
    fc_part, first, last = fc_part
    fc_shape = (last - first, *fc_part.shape[2:])

    def kernel(docs_ref, q_ref, kv_ref, g_ref, lse_ref, act_ref, h_ref, dwo_ref, fc_ref, *refs):
        wp_refs, refs = refs[:n_wp], refs[n_wp:]
        residual_ref, bias_ref = refs[:2]
        gq_out, gkv_out, gq_sum, gkv_sum, dwq_out, dwkv_out = refs[2:8]
        out_ref, dwo_out, fc_out = refs[8:11]
        a_buf, w_buf, q_buf, kv_buf, g_buf, grad_buf, gk, gv, h_buf = refs[11:20]
        dwq_buf, dwkv_buf = refs[20:22]
        s, line_refs = refs[22:36], refs[36:52]
        local, wlocal = refs[52:54]
        result = Rows(out_ref, *refs[54:])
        p = Place()
        loads = [load(act_ref, a_buf, local.at[0]), *load_blocks(wp_refs, w_buf, wlocal)]
        line_o = LineSum(p, lambda f: dwo_ref.at[f], layers, *line_refs[:8])
        line_fc = LineSum(p, lambda f: fc_ref.at[pl.ds(first, last - first), f], layers, *line_refs[8:])
        ins = [
            load(q_ref, q_buf, local.at[2]),
            load(kv_ref, kv_buf, local.at[3]),
            load(g_ref, g_buf, local.at[4]),
        ]

        def h_fetch(i):
            here = pl.ds(2 * i * part, 2 * part)
            return load(h_ref.at[:, here], h_buf.at[i % 2], local.at[5 + i % 2])

        tiles = [h_fetch(0)]
        p.greet(False, layers)
        LineSum.start(line_o, line_fc)
        for copy in loads:
            copy.wait()
        stores = []

        def idle():
            for copy in ins:
                copy.wait()
            for stream in range(streams):
                attend_stream_back(
                    docs_ref,
                    stream,
                    q_buf.at[:, stream],
                    kv_buf.at[:, stream],
                    g_buf.at[:, stream],
                    lse_ref.at[stream],
                    grad_buf.at[:, stream, :, pl.ds(0, cols)],
                    grad_buf.at[:, stream, :, pl.ds(cols, kv_cols)],
                    gk,
                    gv,
                    heads,
                )
                if stream == 0:
                    line_fc.poll()
            stores.append(load(grad_buf.at[:, :, :, pl.ds(0, cols)], gq_out, local.at[7]))
            stores.append(load(grad_buf.at[:, :, :, pl.ds(cols, kv_cols)], gkv_out, local.at[8]))
            grad = grad_buf[...].reshape(total, cols + kv_cols)
            sums = jnp.sum(grad.astype(f32), axis=0, keepdims=True)
            gq_sum[...] = sums[:, :cols]
            gkv_sum[...] = sums[:, cols:]
            for i in range(PLANE // 2):
                tiles[i].wait()
                if i + 1 < PLANE // 2:
                    tiles.append(h_fetch(i + 1))
                term = dot_tn(h_buf[i % 2], grad).astype(bf16)
                for k in range(2):
                    lines = term[k * part : (k + 1) * part]
                    dwq_buf[2 * i + k] = lines[:, :cols].reshape(layers, part // layers, cols)
                    dwkv_buf[2 * i + k] = lines[:, cols:]
            stores.append(load(dwq_buf, dwq_out, local.at[9]))
            stores.append(load(dwkv_buf, dwkv_out, local.at[10]))

        def emit(line, value):
            result.put(line, residual_ref[line, :] + value + bias_ref[...])

        def keep_out(where, value):
            dwo_out[where, :] = value

        def keep_fc(where, value):
            fc_out[where] = value.astype(bf16)

        polls = (line_o.poll, line_fc.poll, line_o.poll)
        Scatter.take(p, own, s).run(plain_product(a_buf, w_buf), emit, idle, polls)
        line_o.finish(keep_out)
        line_fc.finish(keep_fc)
        for copy in stores:
            copy.wait()
        result.finish()

    return pl.pallas_call(
        kernel,
        out_shape=[
            jax.ShapeDtypeStruct(queries.shape, bf16),
            jax.ShapeDtypeStruct(keyval.shape, bf16),
            jax.ShapeDtypeStruct((1, cols), f32),
            jax.ShapeDtypeStruct((1, kv_cols), f32),
            jax.ShapeDtypeStruct((PLANE, layers, part // layers, cols), bf16),
            jax.ShapeDtypeStruct((PLANE, part, kv_cols), bf16),
            jax.ShapeDtypeStruct((own, wide), f32),
            jax.ShapeDtypeStruct(out_shape, f32),
            jax.ShapeDtypeStruct(fc_shape, bf16),
        ],
        in_specs=[pl.BlockSpec(memory_space=pltpu.SMEM)]
        + [ANY] * 3
        + [WHOLE]
        + [ANY] * (4 + n_wp)
        + [WHOLE] * 2,
        out_specs=[ANY, ANY, WHOLE, WHOLE, ANY, ANY, ANY] + [WHOLE] * 2,
        scratch_shapes=[
            pltpu.VMEM(act.shape, bf16),
            pltpu.VMEM((depth, wide), bf16),
            pltpu.VMEM(queries.shape, bf16),
            pltpu.VMEM(keyval.shape, bf16),
            pltpu.VMEM(grads.shape, bf16),
            pltpu.VMEM((groups, streams, rows, cols + kv_cols), bf16),
            pltpu.VMEM((length, HD), f32),
            pltpu.VMEM((length, HD), f32),
            pltpu.VMEM((2, total, 2 * part), bf16),
            pltpu.VMEM((PLANE, layers, part // layers, cols), bf16),
            pltpu.VMEM((PLANE, part, kv_cols), bf16),
        ]
        + Scatter.scratch(own, wide)
        + LineSum.scratch(out_shape, layers)
        + LineSum.scratch(fc_shape, layers)
        + [sems(11), sems(n_wp * layers)]
        + Rows.scratch(own, wide, f32),
        compiler_params=params(number),
        cost_estimate=cost(2 * total * depth * wide),
        name="attend_back_scatter_proj",
    )(docs, queries, keyval, grads, lse, act, hidden1, out_part, fc_part, *wp, residual, b_proj)


def finish(copied, cast, packed, vectors):
    n_copy, n_cast, n_vec = len(copied), len(cast), len(vectors)
    count = n_copy + n_cast

    def kernel(*refs):
        ins, packed_ref, refs = refs[:count], refs[count], refs[count + 1 :]
        outs, refs = refs[: count + n_vec], refs[count + n_vec :]
        rooms, wide, parts = refs[:count], refs[count : count + n_cast], refs[count + n_cast : -2]
        load_sem, store_sem = refs[-2:]
        loads = [load(src, room, load_sem.at[i]) for i, (src, room) in enumerate(zip(ins, rooms))]
        stores = []

        def store(src, dst):
            stores.append(load(src, dst, store_sem.at[len(stores)]))

        at = 0
        for part, out in zip(parts, outs[count:]):
            for k in range(part.shape[1] // LANES):
                part[:, k * LANES : (k + 1) * LANES] = packed_ref[at : at + 1, :]
                at += 1
            store(part, out)
        for i in range(n_copy):
            loads[i].wait()
            store(rooms[i], outs[i])
        for i in range(n_cast):
            loads[n_copy + i].wait()
            wide[i][...] = rooms[n_copy + i][...].astype(f32)
            store(wide[i], outs[n_copy + i])
        for copy in stores:
            copy.wait()

    shapes = [(a.shape, a.dtype) for a in copied] + [(a.shape, f32) for a in cast]
    shapes += [((1, size), f32) for size in vectors]
    return pl.pallas_call(
        kernel,
        out_shape=[jax.ShapeDtypeStruct(*shape) for shape in shapes],
        in_specs=[ANY] * count + [WHOLE],
        out_specs=[ANY] * (count + n_vec),
        scratch_shapes=[pltpu.VMEM(a.shape, a.dtype) for a in (*copied, *cast)]
        + [pltpu.VMEM(a.shape, f32) for a in cast]
        + [pltpu.VMEM((1, size), f32) for size in vectors]
        + [sems(count), sems(count + n_vec)],
        compiler_params=pltpu.CompilerParams(vmem_limit_bytes=VMEM_LIMIT),
        name="finish",
    )(*copied, *cast, packed)


def shards(
    tokens,
    doc_starts,
    w_query,
    w_kv,
    w_out,
    w_fc,
    w_proj,
    ln1_gain,
    ln1_bias,
    b_query,
    b_value,
    b_out,
    ln2_gain,
    ln2_bias,
    b_fc,
    b_proj,
    cotangent,
):
    layers = lax.axis_size("fsdp")
    streams, rows, width = tokens.shape
    own = streams * rows
    heads = HEADS // PLANE
    hidden = b_fc.shape[0]
    my_cols = heads * HD
    my_hidden = hidden // PLANE
    total = PLANE * own

    own_tokens = tokens.reshape(own, width)
    cot_low = cotangent.reshape(own, width)

    def row(vector):
        return vector.reshape(1, -1)

    fc_cut = PLANE * 6 // 8
    proj_rows = w_proj.shape[0]
    proj_cut = proj_rows * 5 // 8

    def rows_together(pieces):
        return pieces.reshape(-1, pieces.shape[-1])

    (
        hidden1,
        w_kv_all,
        cot_all,
        queries,
        keyval,
        mixed,
        wq,
        wo,
        wf_pieces,
        wf_a,
        wf_b,
        lse,
        mean1,
        inverse1,
    ) = front(
        doc_starts,
        own_tokens,
        row(ln1_gain),
        row(ln1_bias),
        w_query,
        w_fc,
        w_kv,
        w_out,
        cot_low,
        row(b_query),
        row(b_value),
        fc_cut,
        streams,
        heads,
        layers,
        1,
    )
    wq = rows_together(wq)
    mixed_rows = mixed.reshape(total, my_cols)
    residual, hidden2, act_low, slope, grad_w_proj, wf_c, wp, mean2, inverse2 = middle(
        mixed_rows,
        wo,
        own_tokens,
        row(b_out),
        row(ln2_gain),
        row(ln2_bias),
        (wf_a, wf_b),
        (wf_pieces, fc_cut, PLANE),
        row(b_fc),
        cot_all,
        w_proj,
        layers,
        2,
    )
    wf = [rows_together(w) for w in (wf_a, wf_b, wf_c)]
    wp = (wp,)
    grad_w_proj = grad_w_proj.reshape(layers, proj_rows, width)
    grad_residual, grad_attn, sums2, my_grad_b_fc, grad_pre, grad_fc_a, shard_proj_a = scatter_fc(
        cot_all,
        slope,
        wp,
        wf,
        hidden2,
        (cot_low, residual, mean2, inverse2, row(ln2_gain)),
        grad_w_proj,
        proj_cut,
        layers,
        6,
    )

    def by_layer(grad):
        return grad.reshape(-1, layers, width // PLANE // layers, my_hidden)

    first_fc = grad_fc_a.shape[0]
    grad_mixed, grad_w_out, grad_fc_rest, shard_proj, fc_a = gather_out(
        grad_attn,
        wo,
        mixed_rows,
        hidden2,
        grad_pre,
        first_fc,
        grad_w_proj,
        shard_proj_a,
        by_layer(grad_fc_a),
        layers,
        7,
    )
    grad_fc_rest = by_layer(grad_fc_rest)
    rest_cut = grad_fc_rest.shape[0] // 2
    (
        gq,
        gkv,
        my_grad_b_query,
        sums_kv,
        grad_w_query,
        grad_w_kv,
        output,
        shard_out,
        fc_b,
    ) = attend_back_scatter_proj(
        doc_starts,
        queries,
        keyval,
        grad_mixed.reshape(PLANE, streams, rows, my_cols),
        lse,
        act_low,
        wp,
        hidden1,
        grad_w_out.reshape(layers, -1, width),
        (grad_fc_rest, 0, rest_cut),
        residual,
        row(b_proj),
        layers,
        heads,
        8,
    )
    input_grad, packed, shard_kv, shard_fc, shard_query = scatter_query(
        gq.reshape(total, my_cols),
        gkv.reshape(total, 2 * HD),
        wq,
        w_kv_all,
        grad_w_query,
        grad_w_kv.reshape(width, 2 * HD),
        (fc_a, fc_b),
        (grad_fc_rest, rest_cut, grad_fc_rest.shape[0]),
        (own_tokens, mean1, inverse1, row(ln1_gain), grad_residual),
        (sums2, my_grad_b_fc, my_grad_b_query, sums_kv),
        layers,
        9,
    )
    vectors = (ln1_gain, ln1_bias, b_query, b_value, b_out, ln2_gain, ln2_bias, b_fc, b_proj)
    output, input_grad, shard_kv, shard_out, shard_proj, shard_query, shard_fc, *sums = finish(
        (output, input_grad, shard_kv, shard_out, shard_proj),
        (shard_query, shard_fc),
        packed.reshape(-1, LANES),
        [v.shape[0] for v in vectors],
    )
    return (
        output.reshape(streams, rows, width),
        input_grad.reshape(streams, rows, width),
        shard_query,
        shard_kv,
        shard_out,
        shard_fc,
        shard_proj,
        *[v.reshape(-1) for v in sums],
    )


def gather_seq(block):
    return lax.all_gather(block, "seq", axis=0, tiled=True)


def scatter_seq(partial):
    return lax.psum_scatter(partial.astype(bf16), "seq", scatter_dimension=0, tiled=True).astype(f32)


def columns_to_rows(part, groups):
    rows = part.shape[0]
    spread = part.reshape(rows, groups, part.shape[1] // groups).transpose(1, 0, 2)
    return lax.all_to_all(spread, "seq", split_axis=0, concat_axis=0, tiled=True)


def column_weight(shard, groups):
    pieces = columns_to_rows(shard, groups)
    full = lax.all_gather(pieces, "fsdp", axis=1, tiled=True)
    return full.reshape(-1, full.shape[2])


def plain_column_grad(grad, groups):
    rows, cols = grad.shape
    kept = lax.psum_scatter(
        grad.astype(bf16).reshape(groups, rows // groups, cols), "fsdp", scatter_dimension=1, tiled=True
    )
    moved = lax.all_to_all(kept, "seq", split_axis=0, concat_axis=0, tiled=True)
    return moved.transpose(1, 0, 2).reshape(moved.shape[1], groups * cols).astype(f32)


def row_weight_grad(grad):
    return lax.psum_scatter(grad.astype(bf16), "fsdp", scatter_dimension=0, tiled=True).astype(f32)


def plain_attend(queries, keyval, starts, groups, streams, rows, heads):
    length = groups * rows
    scale = HD ** (-0.5)
    position = jnp.arange(length, dtype=jnp.int32)
    mixed_list, lse_list = [], []
    for stream in range(streams):
        q = queries[:, stream].reshape(length, heads, HD)
        k = keyval[:, stream, :, :HD].reshape(length, HD)
        v = keyval[:, stream, :, HD:].reshape(length, HD)
        segment = jnp.sum((starts[stream][None, :] <= position[:, None]).astype(jnp.int32), axis=1)
        allowed = (position[None, :] <= position[:, None]) & (segment[None, :] == segment[:, None])
        scores = jnp.einsum("thd,ud->htu", q, k, preferred_element_type=f32) * scale
        scores = jnp.where(allowed[None], scores, -1e30)
        top = jnp.max(scores, axis=-1, keepdims=True)
        lse = top + jnp.log(jnp.sum(jnp.exp(scores - top), axis=-1, keepdims=True))
        probs = jnp.exp(scores - lse).astype(bf16)
        mixed = jnp.einsum("htu,ud->thd", probs, v, preferred_element_type=f32)
        mixed_list.append(mixed.astype(bf16).reshape(groups, rows, heads * HD))
        lse_list.append(lse)
    return jnp.stack(mixed_list, axis=1), lse_list


def plain_attend_back(queries, keyval, grads, lse_list, starts, groups, streams, rows, heads):
    length = groups * rows
    scale = HD ** (-0.5)
    position = jnp.arange(length, dtype=jnp.int32)
    gq_list, gkv_list = [], []
    for stream in range(streams):
        q = queries[:, stream].reshape(length, heads, HD)
        g = grads[:, stream].reshape(length, heads, HD)
        k = keyval[:, stream, :, :HD].reshape(length, HD)
        v = keyval[:, stream, :, HD:].reshape(length, HD)
        segment = jnp.sum((starts[stream][None, :] <= position[:, None]).astype(jnp.int32), axis=1)
        allowed = (position[None, :] <= position[:, None]) & (segment[None, :] == segment[:, None])
        scores = jnp.einsum("thd,ud->htu", q, k, preferred_element_type=f32) * scale
        probs = jnp.exp(jnp.where(allowed[None], scores, -1e30) - lse_list[stream])
        grad_probs = jnp.einsum("thd,ud->htu", g, v, preferred_element_type=f32)
        delta = jnp.sum(probs * grad_probs, axis=-1, keepdims=True)
        gs = (probs * (grad_probs - delta)).astype(bf16)
        gq = jnp.einsum("htu,ud->thd", gs, k, preferred_element_type=f32) * scale
        gk = jnp.einsum("htu,thd->ud", gs, q, preferred_element_type=f32) * scale
        gv = jnp.einsum("htu,thd->ud", probs.astype(bf16), g, preferred_element_type=f32)
        gq_list.append(gq.astype(bf16).reshape(groups, rows, heads * HD))
        gkv_list.append(jnp.concatenate([gk, gv], axis=1).reshape(groups, rows, 2 * HD))
    return jnp.stack(gq_list, axis=1), jnp.stack(gkv_list, axis=1)


def plain_shards(
    tokens,
    doc_starts,
    w_query,
    w_kv,
    w_out,
    w_fc,
    w_proj,
    ln1_gain,
    ln1_bias,
    b_query,
    b_value,
    b_out,
    ln2_gain,
    ln2_bias,
    b_fc,
    b_proj,
    cotangent,
):
    groups = lax.axis_size("seq")
    me = lax.axis_index("seq")
    streams, rows, width = tokens.shape
    own = streams * rows
    heads = HEADS // groups
    hidden = b_fc.shape[0]
    my_cols = heads * HD
    my_hidden = hidden // groups

    wq = column_weight(w_query, groups)
    w_kv_all = gather_seq(lax.all_gather(w_kv, "fsdp", axis=0, tiled=True))
    wo = lax.all_gather(w_out, "fsdp", axis=0, tiled=True)
    wf = column_weight(w_fc, groups)
    wp = lax.all_gather(w_proj, "fsdp", axis=0, tiled=True)
    my_bq = lax.dynamic_slice_in_dim(b_query, me * my_cols, my_cols, 0)
    my_bf = lax.dynamic_slice_in_dim(b_fc, me * my_hidden, my_hidden, 0)

    inputs = tokens.reshape(own, width).astype(f32)
    cot_low = cotangent.reshape(own, width)
    cot_full = cot_low.astype(f32)
    shifted1, normed1, inverse1 = normalize(inputs, ln1_gain, ln1_bias)
    hidden1 = gather_seq(shifted1.astype(bf16))
    queries = (dot(hidden1, wq) + my_bq).astype(bf16).reshape(groups, streams, rows, my_cols)
    value_shift = jnp.concatenate([jnp.zeros((HD,), f32), b_value])
    keyval = (dot(hidden1, w_kv_all) + value_shift).astype(bf16).reshape(groups, streams, rows, 2 * HD)
    mixed, lse = plain_attend(queries, keyval, doc_starts, groups, streams, rows, heads)
    mixed_rows = mixed.reshape(groups * own, my_cols)
    residual = inputs + scatter_seq(dot(mixed_rows, wo)) + b_out
    shifted2, normed2, inverse2 = normalize(residual, ln2_gain, ln2_bias)
    hidden2 = gather_seq(shifted2.astype(bf16))
    cot_all = gather_seq(cot_low)
    pre_act = dot(hidden2, wf) + my_bf
    activated, slope = gelu_pair(pre_act)
    act_low = activated.astype(bf16)
    output = residual + scatter_seq(dot(act_low, wp)) + b_proj

    grad_b_proj = jnp.sum(cot_full, axis=0)
    shard_proj = row_weight_grad(dot_tn(act_low, cot_all))
    grad_pre = (dot_nt(cot_all, wp) * slope).astype(bf16)
    my_grad_b_fc = jnp.sum(grad_pre.astype(f32), axis=0)
    shard_fc = plain_column_grad(dot_tn(hidden2, grad_pre), groups)
    grad_hidden2 = scatter_seq(dot_nt(grad_pre, wf))
    back_second, grad_ln2_gain, grad_ln2_bias = normalize_back(
        grad_hidden2, normed2, inverse2, ln2_gain
    )
    grad_residual = cot_full + back_second
    grad_attn = grad_residual.astype(bf16)
    grad_b_out = jnp.sum(grad_attn.astype(f32), axis=0)
    grad_attn_all = gather_seq(grad_attn)
    shard_out = row_weight_grad(dot_tn(mixed_rows, grad_attn_all))
    grad_mixed = dot_nt(grad_attn_all, wo).astype(bf16).reshape(groups, streams, rows, my_cols)
    gq, gkv = plain_attend_back(
        queries, keyval, grad_mixed, lse, doc_starts, groups, streams, rows, heads
    )
    gq_rows = gq.reshape(groups * own, my_cols)
    gkv_rows = gkv.reshape(groups * own, 2 * HD)
    my_grad_b_query = jnp.sum(gq_rows.astype(f32), axis=0)
    grad_b_value = jnp.sum(gkv_rows[:, HD:], axis=0)
    gkv_low = gkv_rows.astype(bf16)
    shard_query = plain_column_grad(dot_tn(hidden1, gq_rows), groups)
    shard_kv = row_weight_grad(scatter_seq(dot_tn(hidden1, gkv_low)))
    grad_hidden1 = scatter_seq(dot_nt(gq_rows, wq) + dot_nt(gkv_low, w_kv_all))
    back_first, grad_ln1_gain, grad_ln1_bias = normalize_back(
        grad_hidden1, normed1, inverse1, ln1_gain
    )
    input_grad = grad_residual + back_first

    zero = jnp.zeros_like
    grad_b_query = lax.dynamic_update_slice_in_dim(zero(b_query), my_grad_b_query, me * my_cols, 0)
    grad_b_fc = lax.dynamic_update_slice_in_dim(zero(b_fc), my_grad_b_fc, me * my_hidden, 0)
    vectors = (
        grad_ln1_gain,
        grad_ln1_bias,
        grad_b_query,
        grad_b_value,
        grad_b_out,
        grad_ln2_gain,
        grad_ln2_bias,
        grad_b_fc,
        grad_b_proj,
    )
    sums = lax.psum(vectors, ("seq", "fsdp"))
    return (
        output.reshape(streams, rows, width),
        input_grad.reshape(streams, rows, width),
        shard_query,
        shard_kv,
        shard_out,
        shard_fc,
        shard_proj,
        *sums,
    )


def solution(mesh):
    acts = P("fsdp", "seq", None)
    weight = P(("seq", "fsdp"), None)
    return jax.shard_map(
        shards if mesh.shape["seq"] == PLANE else plain_shards,
        mesh=mesh,
        in_specs=(acts, P("fsdp", None)) + (weight,) * 5 + (P(),) * 9 + (acts,),
        out_specs=(acts, acts) + (weight,) * 5 + (P(),) * 9,
        check_vma=False,
    )
```

```python
import functools

import jax
import jax.numpy as jnp
from jax import lax
from jax.experimental import pallas as pl
from jax.experimental.pallas import tpu as pltpu
from jax.sharding import PartitionSpec as P

HEADS = 16
HD = 128

root_two_pi = 0.7978845608028654
cubic_coef = 0.044715
epsilon = 1e-05
f32 = jnp.float32
bf16 = jnp.bfloat16
MESH = pl.DeviceIdType.MESH
ANY = pl.BlockSpec(memory_space=pl.ANY)
WHOLE = pl.BlockSpec(memory_space=pltpu.VMEM)
VMEM_LIMIT = 62 * 1024 * 1024
PLANE = 8


def normalize(values, gain_row, shift_row):
    center = values - jnp.mean(values, axis=-1, keepdims=True)
    inverse = lax.rsqrt(jnp.mean(center * center, axis=-1, keepdims=True) + epsilon)
    normed = center * inverse
    return (normed * gain_row + shift_row, normed, inverse)


def normalize_back(grad_out, normed, inverse, gain_row):
    scaled = grad_out * gain_row
    grad_in = inverse * (
        scaled
        - jnp.mean(scaled, axis=-1, keepdims=True)
        - normed * jnp.mean(scaled * normed, axis=-1, keepdims=True)
    )
    return (grad_in, jnp.sum(grad_out * normed, axis=0), jnp.sum(grad_out, axis=0))


def norm_stats(values):
    mean = jnp.mean(values, axis=-1, keepdims=True)
    center = values - mean
    return mean, lax.rsqrt(jnp.mean(center * center, axis=-1, keepdims=True) + epsilon)


def norm_back(grad_out, normed, inverse, gain_row):
    scaled = grad_out * gain_row
    return inverse * (
        scaled
        - jnp.mean(scaled, axis=-1, keepdims=True)
        - normed * jnp.mean(scaled * normed, axis=-1, keepdims=True)
    )


def gelu_pair(inputs):
    tangent = jnp.tanh(root_two_pi * (inputs + cubic_coef * inputs * inputs * inputs))
    activated = 0.5 * inputs * (1.0 + tangent)
    gradient_slope = 0.5 * (1.0 + tangent) + 0.5 * inputs * (
        1.0 - tangent * tangent
    ) * root_two_pi * (1.0 + 3.0 * cubic_coef * inputs * inputs)
    return (activated, gradient_slope)


def dot(a, b):
    return jnp.dot(a, b, preferred_element_type=f32)


def dot_nt(a, b):
    return lax.dot_general(a, b, (((1,), (1,)), ((), ())), preferred_element_type=f32)


def dot_tn(a, b):
    return lax.dot_general(a, b, (((0,), (0,)), ((), ())), preferred_element_type=f32)


def push(src, dst, send, recv, to):
    return pltpu.make_async_remote_copy(
        src_ref=src, dst_ref=dst, send_sem=send, recv_sem=recv, device_id=to, device_id_type=MESH
    )


def sems(*shape):
    return pltpu.SemaphoreType.DMA(shape)


def rows_at(start, size):
    return pl.ds(pl.multiple_of(start, size), size)


class Place:
    def __init__(self):
        me = lax.axis_index("seq")
        self.me = me
        self.core = lax.rem(me, 2)
        x = lax.rem(lax.div(me, 2), 2)
        y = lax.div(me, 4)
        self.sib = me + 1 - 2 * self.core
        self.xn = me + 2 - 4 * x
        self.yn = me + 4 - 8 * y
        self.dg = me + 2 - 4 * x + 4 - 8 * y
        turn = 1 - 2 * self.core
        self.xs, self.ys, self.ds = self.xn + turn, self.yn + turn, self.dg + turn
        self.layer = lax.axis_index("fsdp")

    def plane_peer(self, step):
        return lax.rem(self.me + step, PLANE)

    def line_peer(self, step, layers):
        return lax.rem(self.layer + step, layers)

    def greet(self, whole_plane=False, layers=1):
        barrier = pltpu.get_barrier_semaphore()
        if whole_plane:
            others = [self.plane_peer(step) for step in range(1, PLANE)]
        else:
            others = [self.sib, self.xn, self.yn]
        for other in others:
            pl.semaphore_signal(barrier, inc=1, device_id={"seq": other}, device_id_type=MESH)
        for step in range(1, layers):
            other = self.line_peer(step, layers)
            pl.semaphore_signal(barrier, inc=1, device_id={"fsdp": other}, device_id_type=MESH)
        pl.semaphore_wait(barrier, len(others) + layers - 1)


class Gather:
    @staticmethod
    def scratch(subs=1):
        return [sems(14 * subs), sems(PLANE, 2 * subs)]

    def __init__(self, place, buf, rows, send, recv, subs=1):
        self.p, self.buf, self.rows, self.subs = place, buf, rows, subs
        self.size = rows // (2 * subs)
        self.send_sem, self.recv_sem = send, recv
        self.copies = []
        self.low, self.high = range(subs), range(subs, 2 * subs)

    def piece(self, dev, k):
        return self.buf.at[rows_at(dev * self.rows + k * self.size, self.size), :]

    def pair(self, dev):
        return rows_at(lax.div(dev, 2) * (2 * self.rows), 2 * self.rows)

    def send(self, dev, k, to, src=None):
        piece = self.piece(dev, k)
        copy = push(
            piece if src is None else src,
            piece,
            self.send_sem.at[len(self.copies)],
            self.recv_sem.at[dev, k],
            {"seq": to},
        )
        copy.start()
        self.copies.append(copy)

    def arrived(self, dev, k):
        piece = self.piece(dev, k)
        push(
            piece, piece, self.send_sem.at[0], self.recv_sem.at[dev, k], {"seq": self.p.sib}
        ).wait_recv()

    def start(self, own):
        parts = [own.at[pl.ds(k * self.size, self.size), :] for k in range(2 * self.subs)]
        for k in self.low:
            self.start_piece(k, parts)
        self.start_rest(parts)

    def start_piece(self, k, parts):
        p, other = self.p, k + self.subs
        self.send(p.me, k, p.yn, parts[k])
        self.send(p.me, other, p.xn, parts[other])

    def start_rest(self, parts):
        p = self.p
        for k, other in zip(self.low, self.high):
            self.send(p.me, other, p.yn, parts[other])
            self.send(p.me, k, p.xn, parts[k])
        for k in range(2 * self.subs):
            self.send(p.me, k, p.sib, parts[k])

    def relay_first(self):
        p = self.p
        for k, other in zip(self.low, self.high):
            self.arrived(p.yn, k)
            self.send(p.yn, k, p.xn)
            self.arrived(p.xn, other)
            self.send(p.xn, other, p.yn)
            self.send(p.yn, k, p.sib)
            self.send(p.xn, other, p.sib)

    def relay_rest(self):
        p = self.p
        for k, other in zip(self.low, self.high):
            self.arrived(p.xn, k)
            self.send(p.xn, k, p.sib)
            self.arrived(p.yn, other)
            self.send(p.yn, other, p.sib)

    def relay(self):
        self.relay_first()
        self.relay_rest()

    def have(self, dev):
        for k in range(2 * self.subs):
            self.arrived(dev, k)

    def relay_corner(self):
        p = self.p
        for k in range(2 * self.subs):
            self.arrived(p.dg, k)
            self.send(p.dg, k, p.sib)

    def finish(self):
        for copy in self.copies:
            copy.wait_send()


class Scatter:
    LINES = 32
    CHUNKS = 4

    def __init__(
        self, place, rows, acc, part, sib_out, sib_in, boxes, sib_send, sib_recv, send, recv
    ):
        self.p, self.rows, self.half = place, rows, rows // 2
        self.wide = part.shape[2]
        self.acc, self.part, self.sib_out, self.sib_in = acc, part, sib_out, sib_in
        self.out_d, self.out_x, self.out_y, self.in_d, self.in_x, self.in_y = boxes
        self.sib_send, self.sib_recv, self.send, self.recv = sib_send, sib_recv, send, recv
        self.copies = []

    @staticmethod
    def scratch(rows, wide):
        return [
            pltpu.VMEM((2 * rows, wide // 2), f32),
            pltpu.VMEM((4, rows, wide), f32),
            pltpu.VMEM((4, rows, wide), bf16),
            pltpu.VMEM((4, rows, wide), bf16),
            *[pltpu.VMEM((rows, wide), bf16)] * 6,
            sems(4, 2),
            sems(4, 2),
            sems(14),
            sems(14),
        ]

    @classmethod
    def take(cls, place, rows, refs):
        return cls(place, rows, *refs[:4], refs[4:10], *refs[10:14])

    refs = 14

    def cols(self, c):
        return pl.ds(c * (self.wide // 2), self.wide // 2)

    def swap(self, role, dev, product, c):
        p = self.p
        self.acc[...] = product(role, rows_at(lax.div(dev, 2) * (2 * self.rows), 2 * self.rows), c)
        theirs = rows_at((1 - p.core) * self.rows, self.rows)
        ours = rows_at(p.core * self.rows, self.rows)
        self.sib_out[role, :, self.cols(c)] = self.acc[theirs, :].astype(bf16)
        copy = push(
            self.sib_out.at[role, :, self.cols(c)],
            self.sib_in.at[role, :, self.cols(c)],
            self.sib_send.at[role, c],
            self.sib_recv.at[role, c],
            {"seq": p.sib},
        )
        copy.start()
        self.copies.append(copy)
        self.part[role, :, self.cols(c)] = self.acc[ours, :]
        return copy

    def swap_all(self, role, dev, product):
        return [self.swap(role, dev, product, c) for c in range(2)]

    def add_into(self, dst, role, first, size, more=(), cols=slice(None)):
        lines = self.LINES

        @pl.loop(0, size // lines)
        def _(i):
            line = rows_at(first + i * lines, lines)
            value = self.part[role, line, cols] + self.sib_in[role, line, cols].astype(f32)
            for ref in more:
                value = value + ref[line, cols].astype(f32)
            dst[line, cols] = value.astype(dst.dtype)

    def final(self, start, size):
        line = pl.ds(start, size)
        value = self.part[3, line, :] + self.sib_in[3, line, :].astype(f32)
        return line, value + self.in_x[line, :].astype(f32) + self.in_y[line, :].astype(f32)

    def ship(self, src, dst, h, k, to, cols=slice(None), chunk=None):
        lines = pl.ds(h * self.half, self.half)
        if chunk is not None:
            size = self.half // self.CHUNKS
            lines = pl.ds(h * self.half + chunk * size, size)
        copy = push(
            src.at[lines, cols], dst.at[lines, cols], self.send.at[k], self.recv.at[k], {"seq": to}
        )
        copy.start()
        self.copies.append(copy)
        return copy

    def ship_corner(self, c):
        cols = self.cols(c)
        self.add_into(self.out_d, 0, 0, self.rows, (), cols)
        return (
            self.ship(self.out_d, self.in_d, 0, 2 * c, self.p.xn, cols),
            self.ship(self.out_d, self.in_d, 1, 2 * c + 1, self.p.yn, cols),
        )

    def run(self, product, emit, idle=None, polls=(None, None, None)):
        polls = [poll or (lambda: None) for poll in polls]
        p, rows, half = self.p, self.rows, self.half
        d0 = self.swap(0, p.dg, product, 0)
        d1 = self.swap(0, p.dg, product, 1)
        d0.wait_recv()
        dx0, dy0 = self.ship_corner(0)
        to_x = [self.swap(1, p.xn, product, 0)]
        d1.wait_recv()
        dx1, dy1 = self.ship_corner(1)
        to_x.append(self.swap(1, p.xn, product, 1))
        polls[0]()
        to_y = self.swap_all(2, p.yn, product)
        for copy in to_x:
            copy.wait_recv()
        self.add_into(self.out_x, 1, 0, half)
        x0 = self.ship(self.out_x, self.in_x, 0, 4, p.xn)
        for copy in to_y:
            copy.wait_recv()
        self.add_into(self.out_y, 2, half, half)
        y1 = self.ship(self.out_y, self.in_y, 1, 5, p.yn)
        polls[1]()
        to_me = self.swap_all(3, p.me, product)
        polls[2]()
        size = half // self.CHUNKS
        x1, y0 = [], []
        for copy in (dx0, dx1, dy0, dy1):
            copy.wait_recv()
        for k in range(self.CHUNKS):
            self.add_into(self.out_y, 2, k * size, size, (self.in_d,))
            y0.append(self.ship(self.out_y, self.in_y, 0, 6 + k, p.yn, chunk=k))
            self.add_into(self.out_x, 1, half + k * size, size, (self.in_d,))
            x1.append(
                self.ship(self.out_x, self.in_x, 1, 6 + self.CHUNKS + k, p.xn, chunk=k)
            )
        if idle is not None:
            idle()
        for copy in (*to_me, x0, y1):
            copy.wait_recv()
        for k in range(self.CHUNKS):
            y0[k].wait_recv()
            emit(*self.final(k * size, size))
            x1[k].wait_recv()
            emit(*self.final(half + k * size, size))
        for copy in self.copies:
            copy.wait_send()


class LineGather:
    def __init__(self, place, src, block, layers, send, recv):
        self.me, self.src, self.block, self.layers = place.layer, src, block, layers
        self.send, self.recv = send, recv
        self.step = 0

    @staticmethod
    def scratch(layers):
        return [sems(2 * layers), sems(layers)]

    def copy(self, src, layer, k, to):
        return push(src, self.block(layer), self.send.at[k], self.recv.at[layer], {"fsdp": to})

    def wait_from(self, layer):
        other = lax.rem(self.me + 1, self.layers)
        self.copy(self.block(layer), layer, 0, other).wait_recv()

    def start(self):
        me, top = self.me, self.layers - 1

        @pl.when(me < top)
        def _():
            self.copy(self.src, me, 0, me + 1).start()

        @pl.when(me > 0)
        def _():
            self.copy(self.src, me, self.layers, me - 1).start()

    def poll(self):
        me, top, hop = self.me, self.layers - 1, self.step
        self.step += 1
        below, above = me - 1 - hop, me + 1 + hop

        @pl.when((below >= 0) & (me < top))
        def _():
            self.wait_from(below)
            self.copy(self.block(below), below, hop + 1, me + 1).start()

        @pl.when((above <= top) & (me > 0))
        def _():
            self.wait_from(above)
            self.copy(self.block(above), above, self.layers + hop + 1, me - 1).start()

    def finish(self):
        while self.step < self.layers - 2:
            self.poll()
        me, top = self.me, self.layers - 1

        @pl.when(me == top)
        def _():
            for layer in range(top):
                self.wait_from(layer)

        @pl.when(me == 0)
        def _():
            for layer in range(1, top + 1):
                self.wait_from(layer)

        for hop in range(top):

            @pl.when((hop <= me) & (me < top))
            def _(hop=hop):
                self.copy(self.block(me), me, hop, me + 1).wait_send()

            @pl.when((hop <= top - me) & (me > 0))
            def _(hop=hop):
                self.copy(self.block(me), me, self.layers + hop, me - 1).wait_send()


class LineSum:
    def __init__(self, place, block, layers, own, up, down, us, ur, ds, dr, local):
        self.me, self.block, self.layers = place.layer, block, layers
        self.own, self.up, self.down = own, up, down
        self.us, self.ur, self.ds, self.dr, self.local = us, ur, ds, dr, local
        self.step = 0
        self.loads = [load(block(f), own.at[f], local.at[f]) for f in range(layers)]

    @staticmethod
    def scratch(shape, layers):
        return [
            pltpu.VMEM((layers, *shape), bf16),
            pltpu.VMEM((layers - 1, *shape), bf16),
            pltpu.VMEM((layers - 1, *shape), bf16),
            *[sems(layers)] * 5,
        ]

    refs = 8

    def up_copy(self, src, f, to):
        return push(src, self.up.at[f - 1], self.us.at[f], self.ur.at[f], {"fsdp": to})

    def down_copy(self, src, f, to):
        return push(src, self.down.at[f], self.ds.at[f], self.dr.at[f], {"fsdp": to})

    @staticmethod
    def start(*lines):
        me, top = lines[0].me, lines[0].layers - 1

        @pl.when(me == 0)
        def _():
            for f in range(top, 0, -1):
                for line in lines:
                    line.up_copy(line.block(f), f, 1).start()
            for line in lines:
                line.up[0] = jnp.zeros(line.up.shape[1:], bf16)

        @pl.when(me == top)
        def _():
            for f in range(top):
                for line in lines:
                    line.down_copy(line.block(f), f, top - 1).start()
            for line in lines:
                line.down[top - 1] = jnp.zeros(line.down.shape[1:], bf16)

    def chunks(self):
        shape = self.own.shape[1:]
        size = 1 if len(shape) == 3 else 32
        return shape[0] // size, lambda i: rows_at(i * size, size) if size > 1 else i

    def add(self, box, slot, f):
        count, where = self.chunks()

        @pl.loop(0, count)
        def _(i):
            here = where(i)
            value = box[slot, here].astype(f32) + self.own[f, here].astype(f32)
            box[slot, here] = value.astype(bf16)

    def poll(self):
        top, k = self.layers - 1, self.step
        self.step += 1
        if k == 0:
            for copy in self.loads:
                copy.wait()
        for f in range(2, top + 1):
            at = f - top + 1 + k
            if not 1 <= at < f:
                continue

            @pl.when(self.me == at)
            def _(f=f, at=at):
                self.up_copy(self.up.at[f - 1], f, at + 1).wait_recv()
                self.add(self.up, f - 1, f)
                self.up_copy(self.up.at[f - 1], f, at + 1).start()

            @pl.when(self.me == top - at)
            def _(f=top - f, at=top - at):
                self.down_copy(self.down.at[f], f, at - 1).wait_recv()
                self.add(self.down, f, f)
                self.down_copy(self.down.at[f], f, at - 1).start()

    def finish(self, emit):
        while self.step < self.layers - 2:
            self.poll()
        me, top = self.me, self.layers - 1

        @pl.when(me > 0)
        def _():
            self.up_copy(self.up.at[me - 1], me, me - 1).wait_recv()

        @pl.when(me < top)
        def _():
            self.down_copy(self.down.at[me], me, me + 1).wait_recv()

        count, where = self.chunks()
        below, above = jnp.maximum(me - 1, 0), jnp.minimum(me, top - 1)

        @pl.loop(0, count)
        def _(i):
            here = where(i)
            value = self.up[below, here].astype(f32) + self.down[above, here].astype(f32)
            emit(here, value + self.own[me, here].astype(f32))

        for f in range(1, top + 1):

            @pl.when(me < f)
            def _(f=f):
                self.up_copy(self.up.at[f - 1], f, me + 1).wait_send()

        for f in range(top):

            @pl.when(me > f)
            def _(f=f):
                self.down_copy(self.down.at[f], f, me - 1).wait_send()


class PlaneSum:
    def __init__(self, place, src, box, send, recv):
        self.p, self.src, self.box = place, src, box
        self.copies = []
        for step in range(1, PLANE):
            to = place.plane_peer(step)
            copy = push(src.at[to], box.at[step], send.at[step], recv.at[step], {"seq": to})
            copy.start()
            self.copies.append(copy)

    def total(self):
        value = self.src[self.p.me].astype(f32)
        for step, copy in enumerate(self.copies):
            copy.wait_recv()
            value = value + self.box[step + 1].astype(f32)
        return value

    def finish(self):
        for copy in self.copies:
            copy.wait_send()


class Spread:
    def __init__(self, place, src, out, send, recv, local, room=None):
        cols = src.shape[2]
        spot = out.at[:, rows_at(place.me * cols, cols)]
        if room is None:
            self.copies = [load(src.at[place.me], spot, local)]
        else:
            self.copies = [Through(src.at[place.me], room, spot, local)]
        for step in range(1, PLANE):
            to = place.plane_peer(step)
            copy = push(src.at[to], spot, send.at[step], recv.at[step], {"seq": to})
            copy.start()
            self.copies.append(copy)

    def finish(self):
        for copy in self.copies:
            copy.wait()


def fold(ref, first, value):
    rows, wide = value.shape
    total = jnp.sum(value.reshape(rows // 8, 8, wide), axis=0)
    ref[...] = total if first else ref[...] + total


class Rows:
    @staticmethod
    def scratch(rows, wide, dtype):
        return [pltpu.VMEM((rows, wide), dtype), sems(2 * Scatter.CHUNKS)]

    def __init__(self, out, stage, sem):
        self.out, self.stage, self.sem = out, stage, sem
        self.copies = []

    def put(self, line, value):
        self.stage[line, :] = value.astype(self.stage.dtype)
        self.copies.append(
            load(self.stage.at[line, :], self.out.at[line, :], self.sem.at[len(self.copies)])
        )

    def finish(self):
        for copy in self.copies:
            copy.wait()


def params(number, vmem=True):
    return pltpu.CompilerParams(
        collective_id=number,
        has_side_effects=True,
        vmem_limit_bytes=VMEM_LIMIT if vmem else None,
    )


def cost(flops, mib=40):
    return pl.CostEstimate(flops=flops, bytes_accessed=mib * 1024 * 1024, transcendentals=0)


def load(src, dst, sem):
    copy = pltpu.make_async_copy(src, dst, sem)
    copy.start()
    return copy


class Late:
    @staticmethod
    def scratch(*operands):
        return [pltpu.VMEM(a.shape, a.dtype) for a in operands] + [sems(len(operands))]

    def __init__(self, refs, room):
        self.refs = room[:-1]
        self.copies = [load(ref, buf, room[-1].at[i]) for i, (ref, buf) in enumerate(zip(refs, room))]

    def wait(self):
        for copy in self.copies:
            copy.wait()


class Through:
    def __init__(self, src, room, dst, sem):
        self.room, self.dst, self.sem = room, dst, sem
        self.copy = load(src, room, sem)

    def put(self):
        self.copy.wait()
        self.copy = load(self.room, self.dst, self.sem)

    def wait(self):
        self.copy.wait()


def rows_of(ref, rows):
    return lambda k: ref.at[rows_at(k * rows, rows), :]


def front(
    docs, tokens, gain, shift, w_query, w_fc, w_kv, w_out, cot, bq, bv, cut, streams, heads, layers, number
):
    own_rows, depth = tokens.shape
    total = PLANE * own_rows
    cols = w_query.shape[1] // PLANE
    kv_cols = w_kv.shape[1]
    rows = own_rows // streams
    length = PLANE * rows
    block = min(QROWS, length)
    piece_rows = w_query.shape[0]
    hidden = w_fc.shape[1] // PLANE
    wo_rows = w_out.shape[0]
    cuts = (0, cut // 2, cut)

    def kernel(docs_ref, *refs):
        late, refs = Late(refs[:5], refs[-6:]), refs[5:-6]
        tok_ref, gain_ref, shift_ref, bq_ref, bv_ref = late.refs
        wq_ref, wf_ref, wkv_ref, wo_ref, cot_ref = refs[:5]
        h_all, kv_all, cot_all, q_out, k_out, mixed_out = refs[5:11]
        wq_all, wo_all, wf_out, wfa_all, wfb_all, lse_ref, mean_out, inverse_out = refs[11:19]
        h_buf, low_kv, kv_full, wq_own, wq_buf, wf_own, wo_room, cot_room = refs[19:27]
        q_buf, kv_buf, mixed_buf = refs[27:30]
        hs, hr, ks, kr, cs, cr = refs[30:36]
        line_refs, (qsend, qrecv, fsend, frecv, local) = refs[36:46], refs[46:]
        p = Place()

        def column_block(ref, dev):
            wide = ref.shape[1] // PLANE
            return ref.at[:, rows_at(dev * wide, wide)]

        my_pieces = [
            load(column_block(wq_ref, p.me), wq_own.at[p.me], local.at[0]),
            load(column_block(wf_ref, p.me), wf_own.at[p.me], local.at[1]),
        ]
        my_kv = load(wkv_ref, low_kv.at[rows_at(p.layer * piece_rows, piece_rows), :], local.at[2])
        own = [
            Through(wo_ref, wo_room, rows_of(wo_all, wo_rows)(p.layer), local.at[3]),
            Through(cot_ref, cot_room, rows_of(cot_all, own_rows)(p.me), local.at[4]),
        ]
        line_kv = LineGather(p, wkv_ref, rows_of(low_kv, piece_rows), layers, *line_refs[:2])
        line_wo = LineGather(p, wo_ref, rows_of(wo_all, wo_rows), layers, *line_refs[2:4])
        line_wq = LineGather(p, wq_own, lambda k: wq_buf.at[:, k], layers, *line_refs[4:6])
        wf_alls = (wfa_all, wfb_all)
        lines_wf = [
            LineGather(
                p,
                wf_own.at[pl.ds(cuts[i], cuts[i + 1] - cuts[i])],
                lambda k, i=i: wf_alls[i].at[:, k],
                layers,
                *line_refs[6 + 2 * i : 8 + 2 * i],
            )
            for i in range(2)
        ]
        p.greet(True, layers)
        line_kv.start()
        line_wo.start()

        def split(ref, out, send, recv):
            copies = []
            for step in range(1, PLANE):
                to = p.plane_peer(step)
                copies.append(
                    push(
                        column_block(ref, to),
                        out.at[p.me],
                        send.at[step],
                        recv.at[step],
                        {"seq": to},
                    )
                )
                copies[-1].start()
            return copies

        split_q = split(wq_ref, wq_own, qsend, qrecv)
        split_f = split(wf_ref, wf_own, fsend, frecv)
        late.wait()

        @pl.loop(0, own_rows // 32)
        def _(i):
            here = rows_at(i * 32, 32)
            values = tok_ref[here, :].astype(f32)
            mean, inverse = norm_stats(values)
            h_buf[rows_at(p.me * own_rows + i * 32, 32), :] = (
                (values - mean) * inverse * gain_ref[...] + shift_ref[...]
            ).astype(bf16)
            mean_out[here, :] = mean
            inverse_out[here, :] = inverse

        g = Gather(p, h_buf, own_rows, hs, hr)
        g.start(h_buf.at[rows_at(p.me * own_rows, own_rows), :])
        for copy in own:
            copy.put()
        line_kv.poll()
        for copy in (*my_pieces, my_kv):
            copy.wait()
        for copy in split_q:
            copy.wait_recv()
        line_wq.start()
        stores = [load(wq_own, wq_buf.at[:, p.layer], local.at[5])]
        line_kv.poll()
        line_wo.poll()
        line_kv.finish()
        kv_rows = layers * piece_rows
        stores.append(load(low_kv, kv_full.at[rows_at(p.me * kv_rows, kv_rows), :], local.at[6]))
        gkv = Gather(p, kv_full, kv_rows, ks, kr)
        gkv.start(low_kv)
        line_wq.poll()
        for copy in split_f:
            copy.wait_recv()
        stores.append(load(wf_own, wf_out, local.at[7]))
        for i in range(2):
            here = pl.ds(cuts[i], cuts[i + 1] - cuts[i])
            stores.append(load(wf_own.at[here], wf_alls[i].at[:, p.layer], local.at[8 + i]))
        line_wo.poll()
        line_wq.poll()
        for line in lines_wf:
            line.start()
        g.relay_first()
        g.relay_rest()
        gkv.relay()
        gc = Gather(p, cot_all, own_rows, cs, cr)
        gc.start(cot_ref)
        lines_wf[0].poll()
        line_wq.finish()
        line_wo.finish()
        for copy in stores[:2]:
            copy.wait()
        stores.append(load(wq_buf, wq_all, local.at[10]))

        def project(dev, k):
            here = g.pair(dev)
            stores.append(load(h_buf.at[here, :], h_all.at[here, :], local.at[11 + k]))
            q = dot(h_buf[here, :], wq_buf[...].reshape(depth, cols))
            q = q + bq_ref[:, rows_at(p.me * cols, cols)]
            chip = rows_at(lax.div(dev, 2) * 2, 2)
            q_buf[chip] = q.astype(bf16).reshape(2, streams, rows, cols)

        g.have(p.sib)
        project(p.me, 0)
        g.have(p.xs)
        project(p.xn, 1)
        g.have(p.ys)
        project(p.yn, 2)
        lines_wf[1].poll()
        g.relay_corner()
        g.have(p.ds)
        project(p.dg, 3)
        stores.append(load(q_buf, q_out, local.at[15]))
        gkv.relay_corner()
        for dev in (p.sib, p.xs, p.ys, p.ds):
            gkv.have(dev)
        stores.append(load(kv_full, kv_all, local.at[16]))
        for k in range(4):
            kv = dot(h_buf[pl.ds(k * total // 4, total // 4), :], kv_full[...])
            kv = jnp.concatenate([kv[:, :HD], kv[:, HD:] + bv_ref[...]], axis=1)
            kv_buf[pl.ds(2 * k, 2)] = kv.astype(bf16).reshape(2, streams, rows, kv_cols)
        stores.append(load(kv_buf, k_out, local.at[17]))
        lines_wf[0].poll()
        for stream in range(streams):
            attend_stream(
                docs_ref,
                stream,
                q_buf.at[:, stream],
                kv_buf.at[:, stream],
                mixed_buf.at[:, stream],
                lse_ref.at[stream],
                block,
                heads,
            )
            if stream == 0:
                gc.relay_first()
                lines_wf[1].poll()
        stores.append(load(mixed_buf, mixed_out, local.at[18]))
        gc.relay_rest()
        gc.relay_corner()
        for dev in (p.sib, p.xs, p.ys, p.ds):
            gc.have(dev)
        for item in (g, gkv, gc, *lines_wf):
            item.finish()
        for copy in (*split_q, *split_f):
            copy.wait_send()
        for copy in (*own, *stores[2:]):
            copy.wait()

    q_shape = (PLANE, streams, rows, cols)
    kv_shape = (PLANE, streams, rows, kv_cols)
    wq_shape = (PLANE, layers, piece_rows, cols)
    wf_shape = (PLANE, piece_rows, hidden)
    half = [(cuts[i + 1] - cuts[i], layers, piece_rows, hidden) for i in range(2)]
    return pl.pallas_call(
        kernel,
        out_shape=[
            jax.ShapeDtypeStruct((total, depth), bf16),
            jax.ShapeDtypeStruct((depth, kv_cols), bf16),
            jax.ShapeDtypeStruct((total, cot.shape[1]), bf16),
            jax.ShapeDtypeStruct(q_shape, bf16),
            jax.ShapeDtypeStruct(kv_shape, bf16),
            jax.ShapeDtypeStruct(q_shape, bf16),
            jax.ShapeDtypeStruct(wq_shape, bf16),
            jax.ShapeDtypeStruct((layers * wo_rows, w_out.shape[1]), bf16),
            jax.ShapeDtypeStruct(wf_shape, bf16),
            jax.ShapeDtypeStruct(half[0], bf16),
            jax.ShapeDtypeStruct(half[1], bf16),
            jax.ShapeDtypeStruct((streams, heads, length), f32),
            jax.ShapeDtypeStruct((own_rows, 1), f32),
            jax.ShapeDtypeStruct((own_rows, 1), f32),
        ],
        in_specs=[pl.BlockSpec(memory_space=pltpu.SMEM)] + [ANY] * 10,
        out_specs=[ANY] * 11 + [WHOLE] * 3,
        scratch_shapes=[
            pltpu.VMEM((total, depth), bf16),
            pltpu.VMEM((layers * piece_rows, kv_cols), bf16),
            pltpu.VMEM((depth, kv_cols), bf16),
            pltpu.VMEM((PLANE, piece_rows, cols), bf16),
            pltpu.VMEM(wq_shape, bf16),
            pltpu.VMEM(wf_shape, bf16),
            pltpu.VMEM(w_out.shape, bf16),
            pltpu.VMEM(cot.shape, bf16),
            pltpu.VMEM(q_shape, bf16),
            pltpu.VMEM(kv_shape, bf16),
            pltpu.VMEM(q_shape, bf16),
        ]
        + Gather.scratch() * 3
        + LineGather.scratch(layers) * 5
        + [sems(PLANE)] * 4
        + [sems(19)]
        + Late.scratch(tokens, gain, shift, bq, bv),
        compiler_params=params(number),
        cost_estimate=cost(2 * total * depth * (cols + kv_cols)),
        name="front",
    )(docs, tokens, gain, shift, bq, bv, w_query, w_fc, w_kv, w_out, cot)


def load_parts(parts, dst, local):
    copies, at = [], 0
    for i, part in enumerate(parts):
        rows = part.shape[0]
        copies.append(load(part, dst.at[pl.ds(at, rows), :], local.at[i]))
        at += rows
    return copies


def load_blocks(parts, dst, local):
    copies, at = [], 0
    for layer in range(parts[0].shape[0]):
        for part in parts:
            rows = part.shape[1]
            copies.append(load(part.at[layer], dst.at[pl.ds(at, rows), :], local.at[len(copies)]))
            at += rows
    return copies


def middle(
    mixed, wo, tokens, b_out, gain, shift, wf, piece, bf, cot_all, w_proj, layers, number
):
    total, depth = mixed.shape
    rows = total // PLANE
    wide = wo.shape[1]
    n_wf = len(wf)
    piece, first, last = piece
    piece_rows, hidden = piece.shape[1:]
    w_shape = (piece.shape[0], layers, piece_rows, hidden)
    out_wide = cot_all.shape[1]
    half, proj_half = rows // 2, w_proj.shape[0] // 2
    tiles, tile = 4, hidden // 4

    def kernel(mixed_ref, wo_ref, piece_ref, proj_ref, cot_ref, *refs):
        wf_refs, refs = refs[:n_wf], refs[n_wf:]
        late, refs = Late(refs[:5], refs[-6:]), refs[:-6]
        tok_ref, bias_ref, gain_ref, shift_ref, bf_ref = late.refs
        residual, all_ref, act_ref, slope_ref, dw_ref, piece_all, proj_all = refs[5:12]
        mean_out, inverse_out = refs[12:14]
        a_buf, wo_buf, proj_room, buf, w_buf, act, slope, cot, dw = refs[14:23]
        s, line_refs, residual_refs = refs[23:37], refs[37:43], refs[43:45]
        send, recv, local, store_sem = refs[45:]
        residual = Rows(residual, *residual_refs)
        acc = s[1]
        p = Place()
        piece_ref = piece_ref.at[pl.ds(first, last - first)]
        w_rest = w_buf.at[pl.ds(first, last - first)]
        loads = [load(mixed_ref, a_buf, local.at[0]), load(wo_ref, wo_buf, local.at[1])]
        own = Through(proj_ref, proj_room, proj_all.at[p.layer], local.at[2])
        loads_w, at = [load(piece_ref, w_rest.at[:, p.layer], local.at[3])], 0
        for i, ref in enumerate(wf_refs):
            loads_w.append(load(ref, w_buf.at[pl.ds(at, ref.shape[0])], local.at[4 + i]))
            at += ref.shape[0]
        line_fc = LineGather(p, piece_ref, lambda k: w_rest.at[:, k], layers, *line_refs[:2])
        lines_proj = [
            LineGather(
                p,
                proj_ref.at[pl.ds(i * proj_half, proj_half), :],
                lambda k, i=i: proj_all.at[k, pl.ds(i * proj_half, proj_half), :],
                layers,
                *line_refs[2 + 2 * i : 4 + 2 * i],
            )
            for i in range(2)
        ]
        p.greet(False, layers)
        line_fc.start()
        g = Gather(p, buf, rows, send, recv, 2)
        cots, stores = {}, []

        def fetch(k, dev):
            cots[k] = load(cot_ref.at[g.pair(dev), :], cot.at[k % 2], local.at[4 + n_wf + k % 2])

        def keep(src, dst):
            stores.append(load(src, dst, store_sem.at[len(stores)]))

        fetch(0, p.me)
        fetch(1, p.xn)
        for copy in loads:
            copy.wait()
        my_rows = [g.piece(p.me, k) for k in range(4)]

        def emit(line, value):
            values = tok_ref[line, :].astype(f32) + value + bias_ref[...]
            mean, inverse = norm_stats(values)
            residual.put(line, values)
            buf[rows_at(p.me * rows + line.start, line.size), :] = (
                (values - mean) * inverse * gain_ref[...] + shift_ref[...]
            ).astype(bf16)
            mean_out[line, :] = mean
            inverse_out[line, :] = inverse
            done = line.start + line.size - half
            if done > 0 and done % g.size == 0:
                g.start_piece(done // g.size - 1, my_rows)

        def poll_fc():
            line_fc.poll()
            if line_fc.step == 1:
                own.put()
            lines_proj[line_fc.step - 1].start()

        def idle():
            late.wait()
            lines_proj[0].poll()

        Scatter.take(p, rows, s).run(
            plain_product(a_buf, wo_buf), emit, idle, (poll_fc, None, poll_fc)
        )
        g.start_rest(my_rows)

        def work(dev):
            block = g.pair(dev)
            keep(buf.at[block, :], all_ref.at[block, :])

            @pl.loop(0, hidden // 512)
            def _(j):
                cols = rows_at(j * 512, 512)
                value = dot(buf[block, :], w_buf[:, :, :, cols].reshape(wide, 512))
                value = value + bf_ref[:, rows_at(p.me * hidden + j * 512, 512)]
                activated, gradient = gelu_pair(value)
                act[block, cols] = activated.astype(bf16)
                slope[block, cols] = gradient.astype(bf16)

            keep(act.at[block, :], act_ref.at[block, :])
            keep(slope.at[block, :], slope_ref.at[block, :])

        def grads(k, dev):
            block = g.pair(dev)
            cots[k].wait()
            for j in range(tiles):
                cols = pl.ds(j * tile, tile)
                term = dot_tn(act[block, cols], cot[k % 2])
                if k == 0:
                    acc[j] = term
                elif k < 3:
                    acc[j] += term
                else:
                    dw[j] = (acc[j] + term).astype(bf16)
                    keep(dw.at[j], dw_ref.at[cols, :])

        lines_proj[1].poll()
        line_fc.finish()
        for copy in loads_w:
            copy.wait()
        keep(w_rest, piece_all)
        g.have(p.sib)
        work(p.me)
        grads(0, p.me)
        fetch(2, p.yn)
        g.relay_first()
        lines_proj[0].poll()
        g.relay_rest()
        g.have(p.xs)
        work(p.xn)
        g.have(p.ys)
        work(p.yn)
        lines_proj[1].poll()
        grads(1, p.xn)
        fetch(3, p.dg)
        g.relay_corner()
        grads(2, p.yn)
        g.have(p.ds)
        work(p.dg)
        grads(3, p.dg)
        g.finish()
        for line in lines_proj:
            line.finish()
        own.wait()
        residual.finish()
        for copy in stores:
            copy.wait()

    return pl.pallas_call(
        kernel,
        out_shape=[
            jax.ShapeDtypeStruct((rows, wide), f32),
            jax.ShapeDtypeStruct((total, wide), bf16),
            jax.ShapeDtypeStruct((total, hidden), bf16),
            jax.ShapeDtypeStruct((total, hidden), bf16),
            jax.ShapeDtypeStruct((hidden, out_wide), bf16),
            jax.ShapeDtypeStruct((last - first, *w_shape[1:]), bf16),
            jax.ShapeDtypeStruct((layers, *w_proj.shape), bf16),
            jax.ShapeDtypeStruct((rows, 1), f32),
            jax.ShapeDtypeStruct((rows, 1), f32),
        ],
        in_specs=[ANY] * (10 + n_wf),
        out_specs=[ANY] * 7 + [WHOLE] * 2,
        scratch_shapes=[
            pltpu.VMEM(mixed.shape, bf16),
            pltpu.VMEM(wo.shape, bf16),
            pltpu.VMEM(w_proj.shape, bf16),
            pltpu.VMEM((total, wide), bf16),
            pltpu.VMEM(w_shape, bf16),
            pltpu.VMEM((total, hidden), bf16),
            pltpu.VMEM((total, hidden), bf16),
            pltpu.VMEM((2, 2 * rows, out_wide), bf16),
            pltpu.VMEM((tiles, tile, out_wide), bf16),
        ]
        + Scatter.scratch(rows, wide)
        + LineGather.scratch(layers) * 3
        + Rows.scratch(rows, wide, f32)
        + Gather.scratch(2)
        + [sems(6 + n_wf), sems(13 + tiles)]
        + Late.scratch(tokens, b_out, gain, shift, bf),
        compiler_params=params(number),
        cost_estimate=cost(4 * total * wide * hidden),
        name="middle",
    )(mixed, wo, piece, w_proj, cot_all, *wf, tokens, b_out, gain, shift, bf)


def gather_out(
    grad_attn, wo, mixed, hidden2, grad_pre, first_fc, grad_proj, proj_done, fc_part, layers, number
):
    rows, depth = grad_attn.shape
    wide = wo.shape[0]
    total = PLANE * rows
    hidden = grad_pre.shape[1]
    tile = 512
    steps = (depth - first_fc) // tile
    proj_cut = proj_done.shape[0]
    proj_shape = (grad_proj.shape[1] - proj_cut, grad_proj.shape[2])
    fc_shape = (fc_part.shape[0], *fc_part.shape[2:])

    def kernel(own_ref, w_ref, mixed_ref, h_ref, gp_ref, proj_ref, fc_ref, *refs):
        late, refs = Late(refs[:1], refs[-2:]), refs[1:-2]
        (done_ref,) = late.refs
        gm_ref, dw_ref, dwfc_ref, proj_out, fc_out = refs[:5]
        buf, w_buf, mixed_buf, gm, acc, dw, gp, h_buf, dwfc = refs[5:14]
        send, recv = refs[14:16]
        line_refs = refs[16:32]
        (local,) = refs[32:]
        p = Place()
        load_own = load(own_ref, buf.at[rows_at(p.me * rows, rows), :], local.at[0])
        loads = [load(w_ref, w_buf, local.at[1]), load(mixed_ref, mixed_buf, local.at[2])]
        load_gp = load(gp_ref, gp, local.at[3])
        proj = LineSum(p, lambda f: proj_ref.at[f, pl.ds(proj_cut, proj_shape[0]), :], layers, *line_refs[:8])
        fc = LineSum(p, lambda f: fc_ref.at[:, f], layers, *line_refs[8:])

        def h_fetch(i):
            here = pl.ds(first_fc + i * tile, tile)
            return load(h_ref.at[:, here], h_buf.at[i % 2], local.at[4 + i % 2])

        tiles = [h_fetch(0)]
        stores = []
        p.greet(False, layers)
        g = Gather(p, buf, rows, send, recv)
        g.start(own_ref)
        LineSum.start(proj, fc)

        def work(dev):
            block = g.pair(dev)
            gm[block, :] = dot_nt(buf[block, :], w_buf[...]).astype(bf16)

        def grads(k, dev):
            block = g.pair(dev)
            term = dot_tn(mixed_buf[block, :], buf[block, :])
            if k == 0:
                acc[...] = term
            elif k < 3:
                acc[...] += term
            else:
                dw[...] = (acc[...] + term).astype(bf16)

        def fc_grads(i):
            tiles[i].wait()
            if i + 1 < steps:
                tiles.append(h_fetch(i + 1))
            if i >= 2:
                stores[i - 2].wait()
            dwfc[i % 2] = dot_tn(h_buf[i % 2], gp[...]).astype(bf16)
            stores.append(
                load(dwfc.at[i % 2], dwfc_ref.at[pl.ds(i * tile, tile), :], local.at[6 + i % 2])
            )

        load_own.wait()
        for copy in loads:
            copy.wait()
        g.have(p.sib)
        work(p.me)
        grads(0, p.me)
        late.wait()
        for i in range(0, proj_cut, 32):
            proj_out[pl.ds(i, 32), :] = done_ref[pl.ds(i, 32), :].astype(f32)
        load_gp.wait()
        fc_grads(0)
        proj.poll()
        g.relay_first()
        fc_grads(1)
        fc.poll()
        for i in range(2, steps):
            fc_grads(i)
        proj.poll()
        g.relay_rest()
        fc.poll()
        g.have(p.xs)
        work(p.xn)
        g.have(p.ys)
        work(p.yn)
        grads(1, p.xn)
        g.relay_corner()
        grads(2, p.yn)
        g.have(p.ds)
        work(p.dg)
        store = load(gm, gm_ref, local.at[8])
        grads(3, p.dg)
        store_dw = load(dw, dw_ref, local.at[9])
        g.finish()

        def keep_proj(where, value):
            proj_out[pl.ds(proj_cut + where.start, where.size), :] = value

        def keep_fc(where, value):
            fc_out[where] = value.astype(bf16)

        proj.finish(keep_proj)
        fc.finish(keep_fc)
        store.wait()
        store_dw.wait()
        for copy in stores[-2:]:
            copy.wait()

    return pl.pallas_call(
        kernel,
        out_shape=[
            jax.ShapeDtypeStruct((total, wide), bf16),
            jax.ShapeDtypeStruct((wide, depth), bf16),
            jax.ShapeDtypeStruct((depth - first_fc, hidden), bf16),
            jax.ShapeDtypeStruct(grad_proj.shape[1:], f32),
            jax.ShapeDtypeStruct(fc_shape, bf16),
        ],
        in_specs=[ANY] * 8,
        out_specs=[ANY] * 3 + [WHOLE] * 2,
        scratch_shapes=[
            pltpu.VMEM((total, depth), bf16),
            pltpu.VMEM(wo.shape, bf16),
            pltpu.VMEM(mixed.shape, bf16),
            pltpu.VMEM((total, wide), bf16),
            pltpu.VMEM((wide, depth), f32),
            pltpu.VMEM((wide, depth), bf16),
            pltpu.VMEM(grad_pre.shape, bf16),
            pltpu.VMEM((2, total, tile), bf16),
            pltpu.VMEM((2, tile, hidden), bf16),
        ]
        + Gather.scratch()
        + LineSum.scratch(proj_shape, layers)
        + LineSum.scratch(fc_shape, layers)
        + [sems(10)]
        + Late.scratch(proj_done),
        compiler_params=params(number),
        cost_estimate=cost(4 * total * depth * wide),
        name="gather_out",
    )(grad_attn, wo, mixed, hidden2, grad_pre, grad_proj, fc_part, proj_done)


def plain_product(a_buf, w_buf):
    half = w_buf.shape[1] // 2

    def product(role, here, c):
        return dot(a_buf[here, :], w_buf[:, pl.ds(c * half, half)])

    return product


def scatter_fc(cot_all, slope, wp, wf, hidden2, back, grad_proj, proj_cut, layers, number):
    total, depth = cot_all.shape
    rows = total // PLANE
    wide = slope.shape[1]
    tile = 512
    n_wp, n_wf = len(wp), len(wf)
    proj_shape = (proj_cut, grad_proj.shape[2])
    cuts = (0, proj_cut // 64 * 32, proj_cut)

    def kernel(cot_ref, slope_ref, h_ref, proj_ref, *refs):
        wp_refs, wf_refs, refs = refs[:n_wp], refs[n_wp : n_wp + n_wf], refs[n_wp + n_wf :]
        late, refs = Late(refs[:5], refs[-6:]), refs[:-6]
        cot_own, residual_ref, mean_ref, inverse_ref, gain_ref = late.refs
        grad_residual, grad_attn, sums_ref, bias_ref, gp_ref, dw_ref, proj_out = refs[5:12]
        cot, slopes, wp_buf, wf_buf, gp, h_buf, dw_buf, folds = refs[12:20]
        s, line_refs = refs[20:34], refs[34:50]
        local, wlocal = refs[50:52]
        grad_residual, grad_attn = Rows(grad_residual, *refs[52:54]), Rows(grad_attn, *refs[54:56])
        p = Place()
        proj = [
            LineSum(
                p,
                lambda f, i=i: proj_ref.at[f, pl.ds(cuts[i], cuts[i + 1] - cuts[i]), :],
                layers,
                *line_refs[8 * i : 8 * i + 8],
            )
            for i in range(2)
        ]
        order = (p.dg, p.xn, p.yn, p.me)

        def chip(dev):
            return rows_at(lax.div(dev, 2) * (2 * rows), 2 * rows)

        def fetch(k):
            here = chip(order[k])
            return (
                load(cot_ref.at[here, :], cot.at[k % 2], local.at[k % 2]),
                load(slope_ref.at[here, :], slopes.at[k % 2], local.at[2 + k % 2]),
            )

        fetches = [fetch(0)]
        loads_wp = load_blocks(wp_refs, wp_buf, wlocal)
        loads_wf = load_parts(wf_refs, wf_buf, local.at[pl.ds(4, n_wf)])
        load_h = load(h_ref.at[:, pl.ds(0, tile)], h_buf, local.at[4 + n_wf])
        bias_ref[...] = jnp.zeros_like(bias_ref)
        p.greet(False, layers)
        LineSum.start(*proj)
        for copy in loads_wp:
            copy.wait()
        half = depth // 2

        def back_through_gelu(k):
            for copy in fetches[k]:
                copy.wait()
            if k < 3:
                fetches.append(fetch(k + 1))
            here = chip(order[k])

            @pl.loop(0, wide // 512)
            def _(j):
                cols = rows_at(j * 512, 512)
                grad_act = dot_nt(cot[k % 2], wp_buf[cols, :])
                grad_pre = (grad_act * slopes[k % 2, :, cols].astype(f32)).astype(bf16)
                gp[here, cols] = grad_pre
                bias_ref[:, cols] += jnp.sum(grad_pre.astype(f32), axis=0, keepdims=True)

            if k == 0:
                for copy in loads_wf:
                    copy.wait()

        def product(role, here, c):
            if c == 0:
                back_through_gelu(role)
            return dot_nt(gp[here, :], wf_buf[pl.ds(c * half, half), :])

        def emit(line, value):
            first = line.start == 0
            grad_out = cot_own[line, :].astype(f32)
            back = inverse_ref[line, :]
            normed = (residual_ref[line, :] - mean_ref[line, :]) * back
            result = grad_out + norm_back(value, normed, back, gain_ref[...])
            low = result.astype(bf16)
            grad_residual.put(line, result)
            grad_attn.put(line, low)
            for i, term in enumerate((value * normed, value, low.astype(f32), grad_out)):
                fold(folds.at[i], first, term)

        stores = []

        def last_poll():
            stores.append(load(gp, gp_ref, local.at[5 + n_wf]))
            proj[0].poll()

        def idle():
            late.wait()
            load_h.wait()
            dw_buf[...] = dot_tn(h_buf[...], gp[...]).astype(bf16)
            stores.append(load(dw_buf, dw_ref, local.at[6 + n_wf]))
            proj[1].poll()

        Scatter.take(p, rows, s).run(
            product, emit, idle, (proj[0].poll, proj[1].poll, last_poll)
        )
        sums_ref[...] = jnp.sum(folds[...], axis=1)
        for i in range(2):

            def keep(where, value, i=i):
                proj_out[pl.ds(cuts[i] + where.start, where.size), :] = value.astype(bf16)

            proj[i].finish(keep)
        for copy in stores:
            copy.wait()
        grad_residual.finish()
        grad_attn.finish()

    return pl.pallas_call(
        kernel,
        out_shape=[
            jax.ShapeDtypeStruct((rows, depth), f32),
            jax.ShapeDtypeStruct((rows, depth), bf16),
            jax.ShapeDtypeStruct((4, depth), f32),
            jax.ShapeDtypeStruct((1, wide), f32),
            jax.ShapeDtypeStruct((total, wide), bf16),
            jax.ShapeDtypeStruct((tile, wide), bf16),
            jax.ShapeDtypeStruct(proj_shape, bf16),
        ],
        in_specs=[ANY] * (9 + n_wp + n_wf),
        out_specs=[ANY] * 2 + [WHOLE] * 2 + [ANY] * 2 + [WHOLE],
        scratch_shapes=[
            pltpu.VMEM((2, 2 * rows, depth), bf16),
            pltpu.VMEM((2, 2 * rows, wide), bf16),
            pltpu.VMEM((wide, depth), bf16),
            pltpu.VMEM((depth, wide), bf16),
            pltpu.VMEM((total, wide), bf16),
            pltpu.VMEM((total, tile), bf16),
            pltpu.VMEM((tile, wide), bf16),
            pltpu.VMEM((4, 8, depth), f32),
        ]
        + Scatter.scratch(rows, depth)
        + LineSum.scratch((cuts[1], depth), layers)
        + LineSum.scratch((proj_cut - cuts[1], depth), layers)
        + [sems(7 + n_wf), sems(n_wp * layers)]
        + Rows.scratch(rows, depth, f32)
        + Rows.scratch(rows, depth, bf16)
        + Late.scratch(*back),
        compiler_params=params(number),
        cost_estimate=cost(6 * total * depth * wide),
        name="scatter_fc",
    )(cot_all, slope, hidden2, grad_proj, *wp, *wf, *back)


LANES = 128


def scatter_query(
    gq, gkv, wq, w_kv, grad_w_query, grad_w_kv, fc_done, fc_part, back, sums, layers, number
):
    total, cols = gq.shape
    kv_cols = gkv.shape[1]
    rows = total // PLANE
    depth = wq.shape[0]
    wide = depth + kv_cols
    q_shape = (grad_w_query.shape[0], *grad_w_query.shape[2:])
    fc_part, first, last = fc_part
    fc_shape = (last - first, *fc_part.shape[2:])
    my_hidden = sums[1].shape[1]
    places, lines_total = {}, 0
    for name, size in (
        ("ln1_gain", depth),
        ("ln1_bias", depth),
        ("b_query", PLANE * cols),
        ("b_value", kv_cols // 2),
        ("b_out", depth),
        ("ln2_gain", depth),
        ("ln2_bias", depth),
        ("b_fc", PLANE * my_hidden),
        ("b_proj", depth),
    ):
        places[name] = lines_total
        lines_total += size // LANES
    padded = -(-lines_total // (8 * PLANE)) * 8
    n_done = len(fc_done)
    done_cut = sum(a.shape[0] for a in fc_done)
    fc_rows, fc_cols = fc_shape[1:]
    kv_rows = rows // layers

    def kernel(gq_ref, gkv_ref, wq_ref, wkv_ref, dwq_ref, dwkv_ref, fc_ref, *refs):
        late, refs = Late(refs[:9], refs[-10:]), refs[:-10]
        tok_ref, mean_ref, inverse_ref, gain_ref, residual_ref = late.refs[:5]
        sums2_ref, sums_fc_ref, sums_q_ref, sums_kv_ref = late.refs[5:]
        done_refs, refs = refs[9 : 9 + n_done], refs[9 + n_done :]
        out_ref, vec_out, dwkv_out, fc_out, dwq_out = refs[:5]
        g_buf, wq_buf, wkv_buf, dwkv_buf, q_sum, folds = refs[5:11]
        vec, box, zbox, plane_sum, pieces, dwkv, kv_box = refs[11:18]
        s, line_refs = refs[18:32], refs[32:48]
        qsend, qrecv, local = refs[48:51]
        result = Rows(out_ref, *refs[51:53])
        vsend, vrecv, zsend, zrecv, gsend, grecv, fsend, frecv, ksend, krecv, flocal = refs[53:]
        p = Place()
        at, done_loads = 0, []
        for i, ref in enumerate(done_refs):
            done_loads.append(load(ref, pieces.at[pl.ds(at, ref.shape[0])], flocal.at[i]))
            at += ref.shape[0]

        def pack(at, row):
            for k in range(row.shape[1] // LANES):
                line = at + k
                vec[lax.div(line, padded), pl.ds(lax.rem(line, padded), 1), :] = row[
                    :, k * LANES : (k + 1) * LANES
                ]

        fc_spot = fc_out.at[:, rows_at(p.me * fc_cols, fc_cols)]

        def fc_copy(step):
            to = p.plane_peer(step)
            return push(pieces.at[to], fc_spot, fsend.at[step], frecv.at[step], {"seq": to})

        def spread_fc():
            for step in range(1, PLANE):
                fc_copy(step).start()

        q_side, kv_side = pl.ds(0, cols), pl.ds(cols, kv_cols)
        loads = [
            load(gq_ref, g_buf.at[:, q_side], local.at[0]),
            load(gkv_ref, g_buf.at[:, kv_side], local.at[1]),
            load(wq_ref, wq_buf, local.at[2]),
            load(wkv_ref, wkv_buf, local.at[3]),
            load(dwkv_ref, dwkv_buf, local.at[4]),
        ]
        line_q = LineSum(p, lambda f: dwq_ref.at[:, f], layers, *line_refs[:8])
        line_fc = LineSum(p, lambda f: fc_ref.at[pl.ds(first, last - first), f], layers, *line_refs[8:])
        p.greet(True, layers)
        LineSum.start(line_q, line_fc)
        for copy in loads:
            copy.wait()
        half = wide // 2

        def product(role, here, c):
            where = pl.ds(c * half, min(half, depth - c * half))
            value = dot_nt(g_buf[here, q_side], wq_buf[where, :]) + dot_nt(
                g_buf[here, kv_side], wkv_buf[where, :]
            )
            if c == 0:
                return value
            return jnp.concatenate([value, dwkv_buf[here, :].astype(f32)], axis=1)

        later = []

        def idle():
            def keep(where, value):
                q_sum[where] = value.astype(bf16)

            for copy in done_loads:
                copy.wait()
            late.wait()
            vec[...] = jnp.zeros_like(vec)
            for i, name in enumerate(("ln2_gain", "ln2_bias", "b_out", "b_proj")):
                pack(places[name], sums2_ref[i : i + 1, :])
            pack(places["b_fc"] + p.me * (my_hidden // LANES), sums_fc_ref[...])
            pack(places["b_query"] + p.me * (cols // LANES), sums_q_ref[...])
            pack(places["b_value"], sums_kv_ref[:, kv_cols // 2 :])
            line_fc.poll()
            line_q.finish(keep)
            later.append(Spread(p, q_sum, dwq_out, qsend, qrecv, local.at[5]))

        def emit(line, value):
            begin = line.start == 0
            grad = value[:, :depth]
            normed = (tok_ref[line, :].astype(f32) - mean_ref[line, :]) * inverse_ref[line, :]
            result.put(
                line,
                residual_ref[line, :]
                + norm_back(grad, normed, inverse_ref[line, :], gain_ref[...]),
            )
            fold(folds.at[0], begin, grad * normed)
            fold(folds.at[1], begin, grad)
            dwkv[line, :] = value[:, depth:].astype(bf16)

        def keep_fc(where, value):
            pieces[done_cut + where] = value.astype(bf16)

        polls = (line_q.poll, line_fc.poll, line_q.poll)
        Scatter.take(p, rows, s).run(product, emit, idle, polls)
        for i, name in enumerate(("ln1_gain", "ln1_bias")):
            pack(places[name], jnp.sum(folds[i], axis=0, keepdims=True))
        plane = PlaneSum(p, vec, box, vsend, vrecv)
        across = []

        def kv_block(layer):
            return dwkv.at[rows_at(layer * kv_rows, kv_rows), :]

        for step in range(1, layers):
            to = p.line_peer(step, layers)
            across.append(
                push(kv_block(to), kv_box.at[step], ksend.at[step], krecv.at[step], {"fsdp": to})
            )
            across[-1].start()
        line_fc.finish(keep_fc)
        spread_fc()
        my_fc = load(pieces.at[p.me], fc_spot, flocal.at[n_done])
        total_vec = plane.total()
        plane_sum[...] = total_vec
        zbox[0] = total_vec
        for step in range(1, layers):
            to = p.line_peer(step, layers)
            across.append(
                push(plane_sum, zbox.at[step], zsend.at[step], zrecv.at[step], {"fsdp": to})
            )
            across[-1].start()
        for copy in across:
            copy.wait_recv()
        total_vec = None
        for k in range(layers):
            term = zbox[lax.rem(p.layer - k + layers, layers)]
            total_vec = term if total_vec is None else total_vec + term
        vec_out[p.me] = total_vec
        for step in range(1, PLANE):
            to = p.plane_peer(step)
            mine = vec_out.at[p.me]
            later.append(push(mine, mine, gsend.at[step], grecv.at[step], {"seq": to}))
            later[-1].start()
        value = dwkv[rows_at(p.layer * kv_rows, kv_rows), :].astype(f32)
        for step in range(1, layers):
            value = value + kv_box[step].astype(f32)
        dwkv_out[...] = value
        for item in (*later, result):
            item.finish() if hasattr(item, "finish") else item.wait()
        for step in range(1, PLANE):
            fc_copy(step).wait()
        my_fc.wait()
        plane.finish()
        for copy in across:
            copy.wait_send()

    return pl.pallas_call(
        kernel,
        out_shape=[
            jax.ShapeDtypeStruct((rows, depth), f32),
            jax.ShapeDtypeStruct((PLANE, padded, LANES), f32),
            jax.ShapeDtypeStruct((kv_rows, kv_cols), f32),
            jax.ShapeDtypeStruct((fc_rows, PLANE * fc_cols), bf16),
            jax.ShapeDtypeStruct((q_shape[1], PLANE * q_shape[2]), bf16),
        ],
        in_specs=[ANY] * (16 + n_done),
        out_specs=[ANY, WHOLE, WHOLE, ANY, ANY],
        scratch_shapes=[
            pltpu.VMEM((total, cols + kv_cols), bf16),
            pltpu.VMEM(wq.shape, bf16),
            pltpu.VMEM(w_kv.shape, bf16),
            pltpu.VMEM(grad_w_kv.shape, bf16),
            pltpu.VMEM(q_shape, bf16),
            pltpu.VMEM((2, 8, depth), f32),
            pltpu.VMEM((PLANE, padded, LANES), f32),
            pltpu.VMEM((PLANE, padded, LANES), f32),
            pltpu.VMEM((layers, padded, LANES), f32),
            pltpu.VMEM((padded, LANES), f32),
            pltpu.VMEM((PLANE, fc_rows, fc_cols), bf16),
            pltpu.VMEM((rows, kv_cols), bf16),
            pltpu.VMEM((layers, kv_rows, kv_cols), bf16),
        ]
        + Scatter.scratch(rows, wide)
        + LineSum.scratch(q_shape, layers)
        + LineSum.scratch(fc_shape, layers)
        + [sems(PLANE)] * 2
        + [sems(6)]
        + Rows.scratch(rows, depth, f32)
        + [sems(PLANE)] * 2
        + [sems(layers)] * 2
        + [sems(PLANE)] * 4
        + [sems(layers)] * 2
        + [sems(n_done + 1)]
        + Late.scratch(*back, *sums),
        compiler_params=params(number),
        cost_estimate=cost(2 * total * depth * (cols + kv_cols)),
        name="scatter_query",
    )(gq, gkv, wq, w_kv, grad_w_query, grad_w_kv, fc_part, *back, *sums, *fc_done)


def starts_of(docs, stream, positions):
    start = jnp.zeros_like(positions)
    for j in range(docs.shape[1]):
        here = docs[stream, j]
        start = jnp.maximum(start, jnp.where(here <= positions, here, 0))
    return start


def masked_scores(docs, stream, keys, q, first, limit):
    scores = dot_nt(keys, q) * (HD**-0.5)
    t = first + lax.broadcasted_iota(jnp.int32, (1, q.shape[0]), 1)
    u = lax.broadcasted_iota(jnp.int32, scores.shape, 0)
    return scores, (u >= starts_of(docs, stream, t)) & (u <= t)


QROWS = 256


def attend_stream(docs, stream, q_ref, kv_ref, mixed_ref, lse_ref, block, heads):
    groups, rows, cols = q_ref.shape
    length = groups * rows
    kv = kv_ref[...].reshape(length, 2 * HD)
    keys = kv[:, :HD]
    values_t = kv[:, HD:].T
    per = block // rows
    for b in range(length // block):
        limit = (b + 1) * block
        q_rows = q_ref[b * per : (b + 1) * per].reshape(block, cols)
        for h in range(heads):
            q = q_rows[:, h * HD : (h + 1) * HD]
            scores, allowed = masked_scores(docs, stream, keys[:limit], q, b * block, limit)
            scores = jnp.where(allowed, scores, -1e30)
            top = jnp.max(scores, axis=0, keepdims=True)
            weights = jnp.exp(scores - top)
            total = jnp.sum(weights, axis=0, keepdims=True)
            mixed = dot(values_t[:, :limit], weights.astype(bf16)) / total
            mixed_ref[b * per : (b + 1) * per, :, h * HD : (h + 1) * HD] = (
                mixed.T.astype(bf16).reshape(per, rows, HD)
            )
            lse_ref[h : h + 1, b * block : (b + 1) * block] = top + jnp.log(total)


def attend_stream_back(docs, stream, q_ref, kv_ref, g_ref, lse_ref, gq_ref, gkv_ref, gk, gv, heads):
    groups, rows, cols = q_ref.shape
    length = groups * rows
    block = min(QROWS, length)
    kv = kv_ref[...].reshape(length, 2 * HD)
    keys, values = kv[:, :HD], kv[:, HD:]
    keys_t = keys.T
    per = block // rows
    gk[...] = jnp.zeros_like(gk)
    gv[...] = jnp.zeros_like(gv)
    for b in range(length // block):
        limit = (b + 1) * block
        q_rows = q_ref[b * per : (b + 1) * per].reshape(block, cols)
        g_rows = g_ref[b * per : (b + 1) * per].reshape(block, cols)
        for h in range(heads):
            q = q_rows[:, h * HD : (h + 1) * HD]
            g = g_rows[:, h * HD : (h + 1) * HD]
            scores, allowed = masked_scores(docs, stream, keys[:limit], q, b * block, limit)
            shift = lse_ref[h : h + 1, b * block : (b + 1) * block]
            probs = jnp.where(allowed, jnp.exp(scores - shift), 0.0)
            grad_probs = dot_nt(values[:limit], g)
            weighted = probs * grad_probs
            delta = jnp.sum(weighted, axis=0, keepdims=True)
            grad_scores = (weighted - probs * delta).astype(bf16)
            gq = dot(keys_t[:, :limit], grad_scores) * (HD**-0.5)
            gq_ref[b * per : (b + 1) * per, :, h * HD : (h + 1) * HD] = (
                gq.T.astype(bf16).reshape(per, rows, HD)
            )
            gk[:limit, :] += dot(grad_scores, q)
            gv[:limit, :] += dot(probs.astype(bf16), g)
    gkv_ref[:, :, :HD] = (gk[...] * (HD**-0.5)).astype(bf16).reshape(groups, rows, HD)
    gkv_ref[:, :, HD:] = gv[...].astype(bf16).reshape(groups, rows, HD)


def attend_back_scatter_proj(
    docs, queries, keyval, grads, lse, act, wp, hidden1, out_part, fc_part, residual, b_proj,
    layers, heads, number
):
    groups, streams, rows, cols = queries.shape
    kv_cols = keyval.shape[3]
    length = groups * rows
    total, depth = act.shape
    own = total // PLANE
    wide = hidden1.shape[1]
    part = hidden1.shape[1] // PLANE
    n_wp = len(wp)
    out_shape = out_part.shape[1:]
    fc_part, first, last = fc_part
    fc_shape = (last - first, *fc_part.shape[2:])

    def kernel(docs_ref, q_ref, kv_ref, g_ref, lse_in, act_ref, h_ref, dwo_ref, fc_ref, *refs):
        wp_refs, refs = refs[:n_wp], refs[n_wp:]
        late, refs = Late((*refs[:2], lse_in), refs[-4:]), refs[:-4]
        residual_ref, bias_ref, lse_ref = late.refs
        gq_out, gkv_out, gq_sum, gkv_sum, dwq_out, dwkv_out = refs[2:8]
        out_ref, dwo_out, fc_out = refs[8:11]
        a_buf, w_buf, q_buf, kv_buf, g_buf, grad_buf, gk, gv, h_buf = refs[11:20]
        dwq_buf, dwkv_buf = refs[20:22]
        s, line_refs = refs[22:36], refs[36:52]
        local, wlocal = refs[52:54]
        result = Rows(out_ref, *refs[54:])
        p = Place()
        loads = [load(act_ref, a_buf, local.at[0]), *load_blocks(wp_refs, w_buf, wlocal)]
        line_o = LineSum(p, lambda f: dwo_ref.at[f], layers, *line_refs[:8])
        line_fc = LineSum(p, lambda f: fc_ref.at[pl.ds(first, last - first), f], layers, *line_refs[8:])
        ins = [
            load(q_ref, q_buf, local.at[2]),
            load(kv_ref, kv_buf, local.at[3]),
            load(g_ref, g_buf, local.at[4]),
        ]

        def h_fetch(i):
            here = pl.ds(2 * i * part, 2 * part)
            return load(h_ref.at[:, here], h_buf.at[i % 2], local.at[5 + i % 2])

        tiles = [h_fetch(0)]
        p.greet(False, layers)
        LineSum.start(line_o, line_fc)
        for copy in loads:
            copy.wait()
        stores = []

        def idle():
            late.wait()
            for copy in ins:
                copy.wait()
            for stream in range(streams):
                attend_stream_back(
                    docs_ref,
                    stream,
                    q_buf.at[:, stream],
                    kv_buf.at[:, stream],
                    g_buf.at[:, stream],
                    lse_ref.at[stream],
                    grad_buf.at[:, stream, :, pl.ds(0, cols)],
                    grad_buf.at[:, stream, :, pl.ds(cols, kv_cols)],
                    gk,
                    gv,
                    heads,
                )
                if stream == 0:
                    line_fc.poll()
            stores.append(load(grad_buf.at[:, :, :, pl.ds(0, cols)], gq_out, local.at[7]))
            stores.append(load(grad_buf.at[:, :, :, pl.ds(cols, kv_cols)], gkv_out, local.at[8]))
            grad = grad_buf[...].reshape(total, cols + kv_cols)
            sums = jnp.sum(grad.astype(f32), axis=0, keepdims=True)
            gq_sum[...] = sums[:, :cols]
            gkv_sum[...] = sums[:, cols:]
            for i in range(PLANE // 2):
                tiles[i].wait()
                if i + 1 < PLANE // 2:
                    tiles.append(h_fetch(i + 1))
                term = dot_tn(h_buf[i % 2], grad).astype(bf16)
                for k in range(2):
                    lines = term[k * part : (k + 1) * part]
                    dwq_buf[2 * i + k] = lines[:, :cols].reshape(layers, part // layers, cols)
                    dwkv_buf[2 * i + k] = lines[:, cols:]
            stores.append(load(dwq_buf, dwq_out, local.at[9]))
            stores.append(load(dwkv_buf, dwkv_out, local.at[10]))

        def emit(line, value):
            result.put(line, residual_ref[line, :] + value + bias_ref[...])

        def keep_out(where, value):
            dwo_out[where, :] = value

        def keep_fc(where, value):
            fc_out[where] = value.astype(bf16)

        polls = (line_o.poll, line_fc.poll, line_o.poll)
        Scatter.take(p, own, s).run(plain_product(a_buf, w_buf), emit, idle, polls)
        line_o.finish(keep_out)
        line_fc.finish(keep_fc)
        for copy in stores:
            copy.wait()
        result.finish()

    return pl.pallas_call(
        kernel,
        out_shape=[
            jax.ShapeDtypeStruct(queries.shape, bf16),
            jax.ShapeDtypeStruct(keyval.shape, bf16),
            jax.ShapeDtypeStruct((1, cols), f32),
            jax.ShapeDtypeStruct((1, kv_cols), f32),
            jax.ShapeDtypeStruct((PLANE, layers, part // layers, cols), bf16),
            jax.ShapeDtypeStruct((PLANE, part, kv_cols), bf16),
            jax.ShapeDtypeStruct((own, wide), f32),
            jax.ShapeDtypeStruct(out_shape, f32),
            jax.ShapeDtypeStruct(fc_shape, bf16),
        ],
        in_specs=[pl.BlockSpec(memory_space=pltpu.SMEM)] + [ANY] * (10 + n_wp),
        out_specs=[ANY, ANY, WHOLE, WHOLE, ANY, ANY, ANY] + [WHOLE] * 2,
        scratch_shapes=[
            pltpu.VMEM(act.shape, bf16),
            pltpu.VMEM((depth, wide), bf16),
            pltpu.VMEM(queries.shape, bf16),
            pltpu.VMEM(keyval.shape, bf16),
            pltpu.VMEM(grads.shape, bf16),
            pltpu.VMEM((groups, streams, rows, cols + kv_cols), bf16),
            pltpu.VMEM((length, HD), f32),
            pltpu.VMEM((length, HD), f32),
            pltpu.VMEM((2, total, 2 * part), bf16),
            pltpu.VMEM((PLANE, layers, part // layers, cols), bf16),
            pltpu.VMEM((PLANE, part, kv_cols), bf16),
        ]
        + Scatter.scratch(own, wide)
        + LineSum.scratch(out_shape, layers)
        + LineSum.scratch(fc_shape, layers)
        + [sems(11), sems(n_wp * layers)]
        + Rows.scratch(own, wide, f32)
        + Late.scratch(residual, b_proj, lse),
        compiler_params=params(number),
        cost_estimate=cost(2 * total * depth * wide),
        name="attend_back_scatter_proj",
    )(docs, queries, keyval, grads, lse, act, hidden1, out_part, fc_part, *wp, residual, b_proj)


def finish(copied, cast, packed, vectors):
    n_copy, n_cast, n_vec = len(copied), len(cast), len(vectors)
    count = n_copy + n_cast

    def kernel(*refs):
        ins, packed_ref, refs = refs[:count], refs[count], refs[count + 1 :]
        outs, refs = refs[: count + n_vec], refs[count + n_vec :]
        rooms, wide, parts = refs[:count], refs[count : count + n_cast], refs[count + n_cast : -2]
        load_sem, store_sem = refs[-2:]
        loads = [load(src, room, load_sem.at[i]) for i, (src, room) in enumerate(zip(ins, rooms))]
        stores = []

        def store(src, dst):
            stores.append(load(src, dst, store_sem.at[len(stores)]))

        at = 0
        for part, out in zip(parts, outs[count:]):
            for k in range(part.shape[1] // LANES):
                part[:, k * LANES : (k + 1) * LANES] = packed_ref[at : at + 1, :]
                at += 1
            store(part, out)
        for i in range(n_copy):
            loads[i].wait()
            store(rooms[i], outs[i])
        for i in range(n_cast):
            loads[n_copy + i].wait()
            wide[i][...] = rooms[n_copy + i][...].astype(f32)
            store(wide[i], outs[n_copy + i])
        for copy in stores:
            copy.wait()

    shapes = [(a.shape, a.dtype) for a in copied] + [(a.shape, f32) for a in cast]
    shapes += [((1, size), f32) for size in vectors]
    return pl.pallas_call(
        kernel,
        out_shape=[jax.ShapeDtypeStruct(*shape) for shape in shapes],
        in_specs=[ANY] * count + [WHOLE],
        out_specs=[ANY] * (count + n_vec),
        scratch_shapes=[pltpu.VMEM(a.shape, a.dtype) for a in (*copied, *cast)]
        + [pltpu.VMEM(a.shape, f32) for a in cast]
        + [pltpu.VMEM((1, size), f32) for size in vectors]
        + [sems(count), sems(count + n_vec)],
        compiler_params=pltpu.CompilerParams(vmem_limit_bytes=VMEM_LIMIT),
        name="finish",
    )(*copied, *cast, packed)


def shards(
    tokens,
    doc_starts,
    w_query,
    w_kv,
    w_out,
    w_fc,
    w_proj,
    ln1_gain,
    ln1_bias,
    b_query,
    b_value,
    b_out,
    ln2_gain,
    ln2_bias,
    b_fc,
    b_proj,
    cotangent,
):
    layers = lax.axis_size("fsdp")
    streams, rows, width = tokens.shape
    own = streams * rows
    heads = HEADS // PLANE
    hidden = b_fc.shape[0]
    my_cols = heads * HD
    my_hidden = hidden // PLANE
    total = PLANE * own

    own_tokens = tokens.reshape(own, width)
    cot_low = cotangent.reshape(own, width)

    def row(vector):
        return vector.reshape(1, -1)

    fc_cut = PLANE * 6 // 8
    proj_rows = w_proj.shape[0]
    proj_cut = proj_rows * 5 // 8

    def rows_together(pieces):
        return pieces.reshape(-1, pieces.shape[-1])

    (
        hidden1,
        w_kv_all,
        cot_all,
        queries,
        keyval,
        mixed,
        wq,
        wo,
        wf_pieces,
        wf_a,
        wf_b,
        lse,
        mean1,
        inverse1,
    ) = front(
        doc_starts,
        own_tokens,
        row(ln1_gain),
        row(ln1_bias),
        w_query,
        w_fc,
        w_kv,
        w_out,
        cot_low,
        row(b_query),
        row(b_value),
        fc_cut,
        streams,
        heads,
        layers,
        1,
    )
    wq = rows_together(wq)
    mixed_rows = mixed.reshape(total, my_cols)
    residual, hidden2, act_low, slope, grad_w_proj, wf_c, wp, mean2, inverse2 = middle(
        mixed_rows,
        wo,
        own_tokens,
        row(b_out),
        row(ln2_gain),
        row(ln2_bias),
        (wf_a, wf_b),
        (wf_pieces, fc_cut, PLANE),
        row(b_fc),
        cot_all,
        w_proj,
        layers,
        2,
    )
    wf = [rows_together(w) for w in (wf_a, wf_b, wf_c)]
    wp = (wp,)
    grad_w_proj = grad_w_proj.reshape(layers, proj_rows, width)
    grad_residual, grad_attn, sums2, my_grad_b_fc, grad_pre, grad_fc_a, shard_proj_a = scatter_fc(
        cot_all,
        slope,
        wp,
        wf,
        hidden2,
        (cot_low, residual, mean2, inverse2, row(ln2_gain)),
        grad_w_proj,
        proj_cut,
        layers,
        6,
    )

    def by_layer(grad):
        return grad.reshape(-1, layers, width // PLANE // layers, my_hidden)

    first_fc = grad_fc_a.shape[0]
    grad_mixed, grad_w_out, grad_fc_rest, shard_proj, fc_a = gather_out(
        grad_attn,
        wo,
        mixed_rows,
        hidden2,
        grad_pre,
        first_fc,
        grad_w_proj,
        shard_proj_a,
        by_layer(grad_fc_a),
        layers,
        7,
    )
    grad_fc_rest = by_layer(grad_fc_rest)
    rest_cut = grad_fc_rest.shape[0] // 2
    (
        gq,
        gkv,
        my_grad_b_query,
        sums_kv,
        grad_w_query,
        grad_w_kv,
        output,
        shard_out,
        fc_b,
    ) = attend_back_scatter_proj(
        doc_starts,
        queries,
        keyval,
        grad_mixed.reshape(PLANE, streams, rows, my_cols),
        lse,
        act_low,
        wp,
        hidden1,
        grad_w_out.reshape(layers, -1, width),
        (grad_fc_rest, 0, rest_cut),
        residual,
        row(b_proj),
        layers,
        heads,
        8,
    )
    input_grad, packed, shard_kv, shard_fc, shard_query = scatter_query(
        gq.reshape(total, my_cols),
        gkv.reshape(total, 2 * HD),
        wq,
        w_kv_all,
        grad_w_query,
        grad_w_kv.reshape(width, 2 * HD),
        (fc_a, fc_b),
        (grad_fc_rest, rest_cut, grad_fc_rest.shape[0]),
        (own_tokens, mean1, inverse1, row(ln1_gain), grad_residual),
        (sums2, my_grad_b_fc, my_grad_b_query, sums_kv),
        layers,
        9,
    )
    vectors = (ln1_gain, ln1_bias, b_query, b_value, b_out, ln2_gain, ln2_bias, b_fc, b_proj)
    output, input_grad, shard_kv, shard_out, shard_proj, shard_query, shard_fc, *sums = finish(
        (output, input_grad, shard_kv, shard_out, shard_proj),
        (shard_query, shard_fc),
        packed.reshape(-1, LANES),
        [v.shape[0] for v in vectors],
    )
    return (
        output.reshape(streams, rows, width),
        input_grad.reshape(streams, rows, width),
        shard_query,
        shard_kv,
        shard_out,
        shard_fc,
        shard_proj,
        *[v.reshape(-1) for v in sums],
    )


def gather_seq(block):
    return lax.all_gather(block, "seq", axis=0, tiled=True)


def scatter_seq(partial):
    return lax.psum_scatter(partial.astype(bf16), "seq", scatter_dimension=0, tiled=True).astype(f32)


def columns_to_rows(part, groups):
    rows = part.shape[0]
    spread = part.reshape(rows, groups, part.shape[1] // groups).transpose(1, 0, 2)
    return lax.all_to_all(spread, "seq", split_axis=0, concat_axis=0, tiled=True)


def column_weight(shard, groups):
    pieces = columns_to_rows(shard, groups)
    full = lax.all_gather(pieces, "fsdp", axis=1, tiled=True)
    return full.reshape(-1, full.shape[2])


def plain_column_grad(grad, groups):
    rows, cols = grad.shape
    kept = lax.psum_scatter(
        grad.astype(bf16).reshape(groups, rows // groups, cols), "fsdp", scatter_dimension=1, tiled=True
    )
    moved = lax.all_to_all(kept, "seq", split_axis=0, concat_axis=0, tiled=True)
    return moved.transpose(1, 0, 2).reshape(moved.shape[1], groups * cols).astype(f32)


def row_weight_grad(grad):
    return lax.psum_scatter(grad.astype(bf16), "fsdp", scatter_dimension=0, tiled=True).astype(f32)


def plain_attend(queries, keyval, starts, groups, streams, rows, heads):
    length = groups * rows
    scale = HD ** (-0.5)
    position = jnp.arange(length, dtype=jnp.int32)
    mixed_list, lse_list = [], []
    for stream in range(streams):
        q = queries[:, stream].reshape(length, heads, HD)
        k = keyval[:, stream, :, :HD].reshape(length, HD)
        v = keyval[:, stream, :, HD:].reshape(length, HD)
        segment = jnp.sum((starts[stream][None, :] <= position[:, None]).astype(jnp.int32), axis=1)
        allowed = (position[None, :] <= position[:, None]) & (segment[None, :] == segment[:, None])
        scores = jnp.einsum("thd,ud->htu", q, k, preferred_element_type=f32) * scale
        scores = jnp.where(allowed[None], scores, -1e30)
        top = jnp.max(scores, axis=-1, keepdims=True)
        lse = top + jnp.log(jnp.sum(jnp.exp(scores - top), axis=-1, keepdims=True))
        probs = jnp.exp(scores - lse).astype(bf16)
        mixed = jnp.einsum("htu,ud->thd", probs, v, preferred_element_type=f32)
        mixed_list.append(mixed.astype(bf16).reshape(groups, rows, heads * HD))
        lse_list.append(lse)
    return jnp.stack(mixed_list, axis=1), lse_list


def plain_attend_back(queries, keyval, grads, lse_list, starts, groups, streams, rows, heads):
    length = groups * rows
    scale = HD ** (-0.5)
    position = jnp.arange(length, dtype=jnp.int32)
    gq_list, gkv_list = [], []
    for stream in range(streams):
        q = queries[:, stream].reshape(length, heads, HD)
        g = grads[:, stream].reshape(length, heads, HD)
        k = keyval[:, stream, :, :HD].reshape(length, HD)
        v = keyval[:, stream, :, HD:].reshape(length, HD)
        segment = jnp.sum((starts[stream][None, :] <= position[:, None]).astype(jnp.int32), axis=1)
        allowed = (position[None, :] <= position[:, None]) & (segment[None, :] == segment[:, None])
        scores = jnp.einsum("thd,ud->htu", q, k, preferred_element_type=f32) * scale
        probs = jnp.exp(jnp.where(allowed[None], scores, -1e30) - lse_list[stream])
        grad_probs = jnp.einsum("thd,ud->htu", g, v, preferred_element_type=f32)
        delta = jnp.sum(probs * grad_probs, axis=-1, keepdims=True)
        gs = (probs * (grad_probs - delta)).astype(bf16)
        gq = jnp.einsum("htu,ud->thd", gs, k, preferred_element_type=f32) * scale
        gk = jnp.einsum("htu,thd->ud", gs, q, preferred_element_type=f32) * scale
        gv = jnp.einsum("htu,thd->ud", probs.astype(bf16), g, preferred_element_type=f32)
        gq_list.append(gq.astype(bf16).reshape(groups, rows, heads * HD))
        gkv_list.append(jnp.concatenate([gk, gv], axis=1).reshape(groups, rows, 2 * HD))
    return jnp.stack(gq_list, axis=1), jnp.stack(gkv_list, axis=1)


def plain_shards(
    tokens,
    doc_starts,
    w_query,
    w_kv,
    w_out,
    w_fc,
    w_proj,
    ln1_gain,
    ln1_bias,
    b_query,
    b_value,
    b_out,
    ln2_gain,
    ln2_bias,
    b_fc,
    b_proj,
    cotangent,
):
    groups = lax.axis_size("seq")
    me = lax.axis_index("seq")
    streams, rows, width = tokens.shape
    own = streams * rows
    heads = HEADS // groups
    hidden = b_fc.shape[0]
    my_cols = heads * HD
    my_hidden = hidden // groups

    wq = column_weight(w_query, groups)
    w_kv_all = gather_seq(lax.all_gather(w_kv, "fsdp", axis=0, tiled=True))
    wo = lax.all_gather(w_out, "fsdp", axis=0, tiled=True)
    wf = column_weight(w_fc, groups)
    wp = lax.all_gather(w_proj, "fsdp", axis=0, tiled=True)
    my_bq = lax.dynamic_slice_in_dim(b_query, me * my_cols, my_cols, 0)
    my_bf = lax.dynamic_slice_in_dim(b_fc, me * my_hidden, my_hidden, 0)

    inputs = tokens.reshape(own, width).astype(f32)
    cot_low = cotangent.reshape(own, width)
    cot_full = cot_low.astype(f32)
    shifted1, normed1, inverse1 = normalize(inputs, ln1_gain, ln1_bias)
    hidden1 = gather_seq(shifted1.astype(bf16))
    queries = (dot(hidden1, wq) + my_bq).astype(bf16).reshape(groups, streams, rows, my_cols)
    value_shift = jnp.concatenate([jnp.zeros((HD,), f32), b_value])
    keyval = (dot(hidden1, w_kv_all) + value_shift).astype(bf16).reshape(groups, streams, rows, 2 * HD)
    mixed, lse = plain_attend(queries, keyval, doc_starts, groups, streams, rows, heads)
    mixed_rows = mixed.reshape(groups * own, my_cols)
    residual = inputs + scatter_seq(dot(mixed_rows, wo)) + b_out
    shifted2, normed2, inverse2 = normalize(residual, ln2_gain, ln2_bias)
    hidden2 = gather_seq(shifted2.astype(bf16))
    cot_all = gather_seq(cot_low)
    pre_act = dot(hidden2, wf) + my_bf
    activated, slope = gelu_pair(pre_act)
    act_low = activated.astype(bf16)
    output = residual + scatter_seq(dot(act_low, wp)) + b_proj

    grad_b_proj = jnp.sum(cot_full, axis=0)
    shard_proj = row_weight_grad(dot_tn(act_low, cot_all))
    grad_pre = (dot_nt(cot_all, wp) * slope).astype(bf16)
    my_grad_b_fc = jnp.sum(grad_pre.astype(f32), axis=0)
    shard_fc = plain_column_grad(dot_tn(hidden2, grad_pre), groups)
    grad_hidden2 = scatter_seq(dot_nt(grad_pre, wf))
    back_second, grad_ln2_gain, grad_ln2_bias = normalize_back(
        grad_hidden2, normed2, inverse2, ln2_gain
    )
    grad_residual = cot_full + back_second
    grad_attn = grad_residual.astype(bf16)
    grad_b_out = jnp.sum(grad_attn.astype(f32), axis=0)
    grad_attn_all = gather_seq(grad_attn)
    shard_out = row_weight_grad(dot_tn(mixed_rows, grad_attn_all))
    grad_mixed = dot_nt(grad_attn_all, wo).astype(bf16).reshape(groups, streams, rows, my_cols)
    gq, gkv = plain_attend_back(
        queries, keyval, grad_mixed, lse, doc_starts, groups, streams, rows, heads
    )
    gq_rows = gq.reshape(groups * own, my_cols)
    gkv_rows = gkv.reshape(groups * own, 2 * HD)
    my_grad_b_query = jnp.sum(gq_rows.astype(f32), axis=0)
    grad_b_value = jnp.sum(gkv_rows[:, HD:], axis=0)
    gkv_low = gkv_rows.astype(bf16)
    shard_query = plain_column_grad(dot_tn(hidden1, gq_rows), groups)
    shard_kv = row_weight_grad(scatter_seq(dot_tn(hidden1, gkv_low)))
    grad_hidden1 = scatter_seq(dot_nt(gq_rows, wq) + dot_nt(gkv_low, w_kv_all))
    back_first, grad_ln1_gain, grad_ln1_bias = normalize_back(
        grad_hidden1, normed1, inverse1, ln1_gain
    )
    input_grad = grad_residual + back_first

    zero = jnp.zeros_like
    grad_b_query = lax.dynamic_update_slice_in_dim(zero(b_query), my_grad_b_query, me * my_cols, 0)
    grad_b_fc = lax.dynamic_update_slice_in_dim(zero(b_fc), my_grad_b_fc, me * my_hidden, 0)
    vectors = (
        grad_ln1_gain,
        grad_ln1_bias,
        grad_b_query,
        grad_b_value,
        grad_b_out,
        grad_ln2_gain,
        grad_ln2_bias,
        grad_b_fc,
        grad_b_proj,
    )
    sums = lax.psum(vectors, ("seq", "fsdp"))
    return (
        output.reshape(streams, rows, width),
        input_grad.reshape(streams, rows, width),
        shard_query,
        shard_kv,
        shard_out,
        shard_fc,
        shard_proj,
        *sums,
    )


def solution(mesh):
    acts = P("fsdp", "seq", None)
    weight = P(("seq", "fsdp"), None)
    return jax.shard_map(
        shards if mesh.shape["seq"] == PLANE else plain_shards,
        mesh=mesh,
        in_specs=(acts, P("fsdp", None)) + (weight,) * 5 + (P(),) * 9 + (acts,),
        out_specs=(acts, acts) + (weight,) * 5 + (P(),) * 9,
        check_vma=False,
    )
```

```python
import functools

import jax
import jax.numpy as jnp
from jax import lax
from jax.experimental import pallas as pl
from jax.experimental.pallas import tpu as pltpu
from jax.sharding import PartitionSpec as P

HEADS = 16
HD = 128

root_two_pi = 0.7978845608028654
cubic_coef = 0.044715
epsilon = 1e-05
f32 = jnp.float32
bf16 = jnp.bfloat16
MESH = pl.DeviceIdType.MESH
ANY = pl.BlockSpec(memory_space=pl.ANY)
WHOLE = pl.BlockSpec(memory_space=pltpu.VMEM)
VMEM_LIMIT = 62 * 1024 * 1024
PLANE = 8


def normalize(values, gain_row, shift_row):
    center = values - jnp.mean(values, axis=-1, keepdims=True)
    inverse = lax.rsqrt(jnp.mean(center * center, axis=-1, keepdims=True) + epsilon)
    normed = center * inverse
    return (normed * gain_row + shift_row, normed, inverse)


def normalize_back(grad_out, normed, inverse, gain_row):
    scaled = grad_out * gain_row
    grad_in = inverse * (
        scaled
        - jnp.mean(scaled, axis=-1, keepdims=True)
        - normed * jnp.mean(scaled * normed, axis=-1, keepdims=True)
    )
    return (grad_in, jnp.sum(grad_out * normed, axis=0), jnp.sum(grad_out, axis=0))


def norm_stats(values):
    mean = jnp.mean(values, axis=-1, keepdims=True)
    center = values - mean
    return mean, lax.rsqrt(jnp.mean(center * center, axis=-1, keepdims=True) + epsilon)


def norm_back(grad_out, normed, inverse, gain_row):
    scaled = grad_out * gain_row
    return inverse * (
        scaled
        - jnp.mean(scaled, axis=-1, keepdims=True)
        - normed * jnp.mean(scaled * normed, axis=-1, keepdims=True)
    )


def gelu_pair(inputs):
    tangent = jnp.tanh(root_two_pi * (inputs + cubic_coef * inputs * inputs * inputs))
    activated = 0.5 * inputs * (1.0 + tangent)
    gradient_slope = 0.5 * (1.0 + tangent) + 0.5 * inputs * (
        1.0 - tangent * tangent
    ) * root_two_pi * (1.0 + 3.0 * cubic_coef * inputs * inputs)
    return (activated, gradient_slope)


def dot(a, b):
    return jnp.dot(a, b, preferred_element_type=f32)


def dot_nt(a, b):
    return lax.dot_general(a, b, (((1,), (1,)), ((), ())), preferred_element_type=f32)


def dot_tn(a, b):
    return lax.dot_general(a, b, (((0,), (0,)), ((), ())), preferred_element_type=f32)


def push(src, dst, send, recv, to):
    return pltpu.make_async_remote_copy(
        src_ref=src, dst_ref=dst, send_sem=send, recv_sem=recv, device_id=to, device_id_type=MESH
    )


def sems(*shape):
    return pltpu.SemaphoreType.DMA(shape)


def rows_at(start, size):
    return pl.ds(pl.multiple_of(start, size), size)


class Place:
    def __init__(self):
        me = lax.axis_index("seq")
        self.me = me
        self.core = lax.rem(me, 2)
        x = lax.rem(lax.div(me, 2), 2)
        y = lax.div(me, 4)
        self.sib = me + 1 - 2 * self.core
        self.xn = me + 2 - 4 * x
        self.yn = me + 4 - 8 * y
        self.dg = me + 2 - 4 * x + 4 - 8 * y
        turn = 1 - 2 * self.core
        self.xs, self.ys, self.ds = self.xn + turn, self.yn + turn, self.dg + turn
        self.layer = lax.axis_index("fsdp")

    def plane_peer(self, step):
        return lax.rem(self.me + step, PLANE)

    def line_peer(self, step, layers):
        return lax.rem(self.layer + step, layers)

    def greet(self, whole_plane=False, layers=1):
        barrier = pltpu.get_barrier_semaphore()
        if whole_plane:
            others = [self.plane_peer(step) for step in range(1, PLANE)]
        else:
            others = [self.sib, self.xn, self.yn]
        for other in others:
            pl.semaphore_signal(barrier, inc=1, device_id={"seq": other}, device_id_type=MESH)
        for step in range(1, layers):
            other = self.line_peer(step, layers)
            pl.semaphore_signal(barrier, inc=1, device_id={"fsdp": other}, device_id_type=MESH)
        pl.semaphore_wait(barrier, len(others) + layers - 1)


class Gather:
    @staticmethod
    def scratch(subs=1):
        return [sems(14 * subs), sems(PLANE, 2 * subs)]

    def __init__(self, place, buf, rows, send, recv, subs=1):
        self.p, self.buf, self.rows, self.subs = place, buf, rows, subs
        self.size = rows // (2 * subs)
        self.send_sem, self.recv_sem = send, recv
        self.copies = []
        self.low, self.high = range(subs), range(subs, 2 * subs)

    def piece(self, dev, k):
        return self.buf.at[rows_at(dev * self.rows + k * self.size, self.size), :]

    def pair(self, dev):
        return rows_at(lax.div(dev, 2) * (2 * self.rows), 2 * self.rows)

    def send(self, dev, k, to, src=None):
        piece = self.piece(dev, k)
        copy = push(
            piece if src is None else src,
            piece,
            self.send_sem.at[len(self.copies)],
            self.recv_sem.at[dev, k],
            {"seq": to},
        )
        copy.start()
        self.copies.append(copy)

    def arrived(self, dev, k):
        piece = self.piece(dev, k)
        push(
            piece, piece, self.send_sem.at[0], self.recv_sem.at[dev, k], {"seq": self.p.sib}
        ).wait_recv()

    def start(self, own):
        parts = [own.at[pl.ds(k * self.size, self.size), :] for k in range(2 * self.subs)]
        for k in self.low:
            self.start_piece(k, parts)
        self.start_rest(parts)

    def start_piece(self, k, parts):
        p, other = self.p, k + self.subs
        self.send(p.me, k, p.yn, parts[k])
        self.send(p.me, other, p.xn, parts[other])

    def start_rest(self, parts):
        p = self.p
        for k, other in zip(self.low, self.high):
            self.send(p.me, other, p.yn, parts[other])
            self.send(p.me, k, p.xn, parts[k])
        for k in range(2 * self.subs):
            self.send(p.me, k, p.sib, parts[k])

    def relay_first(self):
        p = self.p
        for k, other in zip(self.low, self.high):
            self.arrived(p.yn, k)
            self.send(p.yn, k, p.xn)
            self.arrived(p.xn, other)
            self.send(p.xn, other, p.yn)
            self.send(p.yn, k, p.sib)
            self.send(p.xn, other, p.sib)

    def relay_rest(self):
        p = self.p
        for k, other in zip(self.low, self.high):
            self.arrived(p.xn, k)
            self.send(p.xn, k, p.sib)
            self.arrived(p.yn, other)
            self.send(p.yn, other, p.sib)

    def relay(self):
        self.relay_first()
        self.relay_rest()

    def have(self, dev):
        for k in range(2 * self.subs):
            self.arrived(dev, k)

    def relay_corner(self):
        p = self.p
        for k in range(2 * self.subs):
            self.arrived(p.dg, k)
            self.send(p.dg, k, p.sib)

    def finish(self):
        for copy in self.copies:
            copy.wait_send()


class Scatter:
    LINES = 32
    CHUNKS = 4

    def __init__(
        self, place, rows, acc, part, sib_out, sib_in, boxes, sib_send, sib_recv, send, recv
    ):
        self.p, self.rows, self.half = place, rows, rows // 2
        self.wide = part.shape[2]
        self.acc, self.part, self.sib_out, self.sib_in = acc, part, sib_out, sib_in
        self.out_d, self.out_x, self.out_y, self.in_d, self.in_x, self.in_y = boxes
        self.sib_send, self.sib_recv, self.send, self.recv = sib_send, sib_recv, send, recv
        self.copies = []

    @staticmethod
    def scratch(rows, wide):
        return [
            pltpu.VMEM((2 * rows, wide // 2), f32),
            pltpu.VMEM((4, rows, wide), f32),
            pltpu.VMEM((4, rows, wide), bf16),
            pltpu.VMEM((4, rows, wide), bf16),
            *[pltpu.VMEM((rows, wide), bf16)] * 6,
            sems(4, 2),
            sems(4, 2),
            sems(14),
            sems(14),
        ]

    @classmethod
    def take(cls, place, rows, refs):
        return cls(place, rows, *refs[:4], refs[4:10], *refs[10:14])

    refs = 14

    def cols(self, c):
        return pl.ds(c * (self.wide // 2), self.wide // 2)

    def swap(self, role, dev, product, c):
        p = self.p
        self.acc[...] = product(role, rows_at(lax.div(dev, 2) * (2 * self.rows), 2 * self.rows), c)
        theirs = rows_at((1 - p.core) * self.rows, self.rows)
        ours = rows_at(p.core * self.rows, self.rows)
        self.sib_out[role, :, self.cols(c)] = self.acc[theirs, :].astype(bf16)
        copy = push(
            self.sib_out.at[role, :, self.cols(c)],
            self.sib_in.at[role, :, self.cols(c)],
            self.sib_send.at[role, c],
            self.sib_recv.at[role, c],
            {"seq": p.sib},
        )
        copy.start()
        self.copies.append(copy)
        self.part[role, :, self.cols(c)] = self.acc[ours, :]
        return copy

    def swap_all(self, role, dev, product):
        return [self.swap(role, dev, product, c) for c in range(2)]

    def add_into(self, dst, role, first, size, more=(), cols=slice(None)):
        lines = self.LINES

        @pl.loop(0, size // lines)
        def _(i):
            line = rows_at(first + i * lines, lines)
            value = self.part[role, line, cols] + self.sib_in[role, line, cols].astype(f32)
            for ref in more:
                value = value + ref[line, cols].astype(f32)
            dst[line, cols] = value.astype(dst.dtype)

    def final(self, start, size):
        line = pl.ds(start, size)
        value = self.part[3, line, :] + self.sib_in[3, line, :].astype(f32)
        return line, value + self.in_x[line, :].astype(f32) + self.in_y[line, :].astype(f32)

    def ship(self, src, dst, h, k, to, cols=slice(None), chunk=None):
        lines = pl.ds(h * self.half, self.half)
        if chunk is not None:
            size = self.half // self.CHUNKS
            lines = pl.ds(h * self.half + chunk * size, size)
        copy = push(
            src.at[lines, cols], dst.at[lines, cols], self.send.at[k], self.recv.at[k], {"seq": to}
        )
        copy.start()
        self.copies.append(copy)
        return copy

    def ship_corner(self, c):
        cols = self.cols(c)
        self.add_into(self.out_d, 0, 0, self.rows, (), cols)
        return (
            self.ship(self.out_d, self.in_d, 0, 2 * c, self.p.xn, cols),
            self.ship(self.out_d, self.in_d, 1, 2 * c + 1, self.p.yn, cols),
        )

    def run(self, product, emit, idle=None, polls=(None, None, None)):
        polls = [poll or (lambda: None) for poll in polls]
        p, rows, half = self.p, self.rows, self.half
        d0 = self.swap(0, p.dg, product, 0)
        d1 = self.swap(0, p.dg, product, 1)
        d0.wait_recv()
        dx0, dy0 = self.ship_corner(0)
        to_x = [self.swap(1, p.xn, product, 0)]
        d1.wait_recv()
        dx1, dy1 = self.ship_corner(1)
        to_x.append(self.swap(1, p.xn, product, 1))
        polls[0]()
        to_y = self.swap_all(2, p.yn, product)
        for copy in to_x:
            copy.wait_recv()
        self.add_into(self.out_x, 1, 0, half)
        x0 = self.ship(self.out_x, self.in_x, 0, 4, p.xn)
        for copy in to_y:
            copy.wait_recv()
        self.add_into(self.out_y, 2, half, half)
        y1 = self.ship(self.out_y, self.in_y, 1, 5, p.yn)
        polls[1]()
        to_me = self.swap_all(3, p.me, product)
        polls[2]()
        size = half // self.CHUNKS
        x1, y0 = [], []
        for copy in (dx0, dx1, dy0, dy1):
            copy.wait_recv()
        for k in range(self.CHUNKS):
            self.add_into(self.out_y, 2, k * size, size, (self.in_d,))
            y0.append(self.ship(self.out_y, self.in_y, 0, 6 + k, p.yn, chunk=k))
            self.add_into(self.out_x, 1, half + k * size, size, (self.in_d,))
            x1.append(
                self.ship(self.out_x, self.in_x, 1, 6 + self.CHUNKS + k, p.xn, chunk=k)
            )
        if idle is not None:
            idle()
        for copy in (*to_me, x0, y1):
            copy.wait_recv()
        for k in range(self.CHUNKS):
            y0[k].wait_recv()
            emit(*self.final(k * size, size))
            x1[k].wait_recv()
            emit(*self.final(half + k * size, size))
        for copy in self.copies:
            copy.wait_send()


class LineGather:
    def __init__(self, place, src, block, layers, send, recv):
        self.me, self.src, self.block, self.layers = place.layer, src, block, layers
        self.send, self.recv = send, recv
        self.step = 0

    @staticmethod
    def scratch(layers):
        return [sems(2 * layers), sems(layers)]

    def copy(self, src, layer, k, to):
        return push(src, self.block(layer), self.send.at[k], self.recv.at[layer], {"fsdp": to})

    def wait_from(self, layer):
        other = lax.rem(self.me + 1, self.layers)
        self.copy(self.block(layer), layer, 0, other).wait_recv()

    def start(self):
        me, top = self.me, self.layers - 1

        @pl.when(me < top)
        def _():
            self.copy(self.src, me, 0, me + 1).start()

        @pl.when(me > 0)
        def _():
            self.copy(self.src, me, self.layers, me - 1).start()

    def poll(self):
        me, top, hop = self.me, self.layers - 1, self.step
        self.step += 1
        below, above = me - 1 - hop, me + 1 + hop

        @pl.when((below >= 0) & (me < top))
        def _():
            self.wait_from(below)
            self.copy(self.block(below), below, hop + 1, me + 1).start()

        @pl.when((above <= top) & (me > 0))
        def _():
            self.wait_from(above)
            self.copy(self.block(above), above, self.layers + hop + 1, me - 1).start()

    def finish(self):
        while self.step < self.layers - 2:
            self.poll()
        me, top = self.me, self.layers - 1

        @pl.when(me == top)
        def _():
            for layer in range(top):
                self.wait_from(layer)

        @pl.when(me == 0)
        def _():
            for layer in range(1, top + 1):
                self.wait_from(layer)

        for hop in range(top):

            @pl.when((hop <= me) & (me < top))
            def _(hop=hop):
                self.copy(self.block(me), me, hop, me + 1).wait_send()

            @pl.when((hop <= top - me) & (me > 0))
            def _(hop=hop):
                self.copy(self.block(me), me, self.layers + hop, me - 1).wait_send()


class LineSum:
    def __init__(self, place, block, layers, own, up, down, us, ur, ds, dr, local):
        self.me, self.block, self.layers = place.layer, block, layers
        self.own, self.up, self.down = own, up, down
        self.us, self.ur, self.ds, self.dr, self.local = us, ur, ds, dr, local
        self.step = 0
        self.loads = [load(block(f), own.at[f], local.at[f]) for f in range(layers)]

    @staticmethod
    def scratch(shape, layers):
        return [
            pltpu.VMEM((layers, *shape), bf16),
            pltpu.VMEM((layers - 1, *shape), bf16),
            pltpu.VMEM((layers - 1, *shape), bf16),
            *[sems(layers)] * 5,
        ]

    refs = 8

    def up_copy(self, src, f, to):
        return push(src, self.up.at[f - 1], self.us.at[f], self.ur.at[f], {"fsdp": to})

    def down_copy(self, src, f, to):
        return push(src, self.down.at[f], self.ds.at[f], self.dr.at[f], {"fsdp": to})

    @staticmethod
    def start(*lines):
        me, top = lines[0].me, lines[0].layers - 1

        @pl.when(me == 0)
        def _():
            for f in range(top, 0, -1):
                for line in lines:
                    line.up_copy(line.block(f), f, 1).start()
            for line in lines:
                line.up[0] = jnp.zeros(line.up.shape[1:], bf16)

        @pl.when(me == top)
        def _():
            for f in range(top):
                for line in lines:
                    line.down_copy(line.block(f), f, top - 1).start()
            for line in lines:
                line.down[top - 1] = jnp.zeros(line.down.shape[1:], bf16)

    def chunks(self):
        shape = self.own.shape[1:]
        size = 1 if len(shape) == 3 else 32
        return shape[0] // size, lambda i: rows_at(i * size, size) if size > 1 else i

    def add(self, box, slot, f):
        count, where = self.chunks()

        @pl.loop(0, count)
        def _(i):
            here = where(i)
            value = box[slot, here].astype(f32) + self.own[f, here].astype(f32)
            box[slot, here] = value.astype(bf16)

    def poll(self):
        top, k = self.layers - 1, self.step
        self.step += 1
        if k == 0:
            for copy in self.loads:
                copy.wait()
        for f in range(2, top + 1):
            at = f - top + 1 + k
            if not 1 <= at < f:
                continue

            @pl.when(self.me == at)
            def _(f=f, at=at):
                self.up_copy(self.up.at[f - 1], f, at + 1).wait_recv()
                self.add(self.up, f - 1, f)
                self.up_copy(self.up.at[f - 1], f, at + 1).start()

            @pl.when(self.me == top - at)
            def _(f=top - f, at=top - at):
                self.down_copy(self.down.at[f], f, at - 1).wait_recv()
                self.add(self.down, f, f)
                self.down_copy(self.down.at[f], f, at - 1).start()

    def finish(self, emit):
        while self.step < self.layers - 2:
            self.poll()
        me, top = self.me, self.layers - 1

        @pl.when(me > 0)
        def _():
            self.up_copy(self.up.at[me - 1], me, me - 1).wait_recv()

        @pl.when(me < top)
        def _():
            self.down_copy(self.down.at[me], me, me + 1).wait_recv()

        count, where = self.chunks()
        below, above = jnp.maximum(me - 1, 0), jnp.minimum(me, top - 1)

        @pl.loop(0, count)
        def _(i):
            here = where(i)
            value = self.up[below, here].astype(f32) + self.down[above, here].astype(f32)
            emit(here, value + self.own[me, here].astype(f32))

        for f in range(1, top + 1):

            @pl.when(me < f)
            def _(f=f):
                self.up_copy(self.up.at[f - 1], f, me + 1).wait_send()

        for f in range(top):

            @pl.when(me > f)
            def _(f=f):
                self.down_copy(self.down.at[f], f, me - 1).wait_send()


class PlaneSum:
    def __init__(self, place, src, box, send, recv):
        self.p, self.src, self.box = place, src, box
        self.copies = []
        for step in range(1, PLANE):
            to = place.plane_peer(step)
            copy = push(src.at[to], box.at[step], send.at[step], recv.at[step], {"seq": to})
            copy.start()
            self.copies.append(copy)

    def total(self):
        value = self.src[self.p.me].astype(f32)
        for step, copy in enumerate(self.copies):
            copy.wait_recv()
            value = value + self.box[step + 1].astype(f32)
        return value

    def finish(self):
        for copy in self.copies:
            copy.wait_send()


class Spread:
    def __init__(self, place, src, out, send, recv, local, room=None):
        cols = src.shape[2]
        spot = out.at[:, rows_at(place.me * cols, cols)]
        if room is None:
            self.copies = [load(src.at[place.me], spot, local)]
        else:
            self.copies = [Through(src.at[place.me], room, spot, local)]
        for step in range(1, PLANE):
            to = place.plane_peer(step)
            copy = push(src.at[to], spot, send.at[step], recv.at[step], {"seq": to})
            copy.start()
            self.copies.append(copy)

    def finish(self):
        for copy in self.copies:
            copy.wait()


def fold(ref, first, value):
    rows, wide = value.shape
    total = jnp.sum(value.reshape(rows // 8, 8, wide), axis=0)
    ref[...] = total if first else ref[...] + total


class Rows:
    @staticmethod
    def scratch(rows, wide, dtype):
        return [pltpu.VMEM((rows, wide), dtype), sems(2 * Scatter.CHUNKS)]

    def __init__(self, out, stage, sem):
        self.out, self.stage, self.sem = out, stage, sem
        self.copies = []

    def put(self, line, value):
        self.stage[line, :] = value.astype(self.stage.dtype)
        self.copies.append(
            load(self.stage.at[line, :], self.out.at[line, :], self.sem.at[len(self.copies)])
        )

    def finish(self):
        for copy in self.copies:
            copy.wait()


def params(number, vmem=True):
    return pltpu.CompilerParams(
        collective_id=number,
        has_side_effects=True,
        vmem_limit_bytes=VMEM_LIMIT if vmem else None,
    )


def cost(flops, mib=40):
    return pl.CostEstimate(flops=flops, bytes_accessed=mib * 1024 * 1024, transcendentals=0)


def load(src, dst, sem):
    copy = pltpu.make_async_copy(src, dst, sem)
    copy.start()
    return copy


class Late:
    @staticmethod
    def scratch(*operands):
        return [pltpu.VMEM(a.shape, a.dtype) for a in operands] + [sems(len(operands))]

    def __init__(self, refs, room):
        self.refs = room[:-1]
        self.copies = [load(ref, buf, room[-1].at[i]) for i, (ref, buf) in enumerate(zip(refs, room))]

    def wait(self):
        for copy in self.copies:
            copy.wait()


class Through:
    def __init__(self, src, room, dst, sem):
        self.room, self.dst, self.sem = room, dst, sem
        self.copy = load(src, room, sem)

    def put(self):
        self.copy.wait()
        self.copy = load(self.room, self.dst, self.sem)

    def wait(self):
        self.copy.wait()


def rows_of(ref, rows):
    return lambda k: ref.at[rows_at(k * rows, rows), :]


def front(
    docs, tokens, gain, shift, w_query, w_fc, w_kv, w_out, cot, bq, bv, cut, streams, heads, layers, number
):
    own_rows, depth = tokens.shape
    total = PLANE * own_rows
    cols = w_query.shape[1] // PLANE
    kv_cols = w_kv.shape[1]
    rows = own_rows // streams
    length = PLANE * rows
    block = min(QROWS, length)
    piece_rows = w_query.shape[0]
    hidden = w_fc.shape[1] // PLANE
    wo_rows = w_out.shape[0]
    cuts = (0, cut // 2, cut)

    def kernel(docs_ref, *refs):
        late, refs = Late(refs[:5], refs[-6:]), refs[5:-6]
        tok_ref, gain_ref, shift_ref, bq_ref, bv_ref = late.refs
        (lse_ref, mean_out, inverse_out, out_sem), refs = refs[-4:], refs[:-4]
        wq_ref, wf_ref, wkv_ref, wo_ref, cot_ref = refs[:5]
        h_all, kv_all, cot_all, q_out, k_out, mixed_out = refs[5:11]
        wq_all, wo_all, wf_out, wfa_all, wfb_all, lse_hbm, mean_hbm, inverse_hbm = refs[11:19]
        h_buf, low_kv, kv_full, wq_own, wq_buf, wf_own, wo_room, cot_room = refs[19:27]
        q_buf, kv_buf, mixed_buf = refs[27:30]
        hs, hr, ks, kr, cs, cr = refs[30:36]
        line_refs, (qsend, qrecv, fsend, frecv, local) = refs[36:46], refs[46:]
        p = Place()

        def column_block(ref, dev):
            wide = ref.shape[1] // PLANE
            return ref.at[:, rows_at(dev * wide, wide)]

        my_pieces = [
            load(column_block(wq_ref, p.me), wq_own.at[p.me], local.at[0]),
            load(column_block(wf_ref, p.me), wf_own.at[p.me], local.at[1]),
        ]
        my_kv = load(wkv_ref, low_kv.at[rows_at(p.layer * piece_rows, piece_rows), :], local.at[2])
        own = [
            Through(wo_ref, wo_room, rows_of(wo_all, wo_rows)(p.layer), local.at[3]),
            Through(cot_ref, cot_room, rows_of(cot_all, own_rows)(p.me), local.at[4]),
        ]
        line_kv = LineGather(p, wkv_ref, rows_of(low_kv, piece_rows), layers, *line_refs[:2])
        line_wo = LineGather(p, wo_ref, rows_of(wo_all, wo_rows), layers, *line_refs[2:4])
        line_wq = LineGather(p, wq_own, lambda k: wq_buf.at[:, k], layers, *line_refs[4:6])
        wf_alls = (wfa_all, wfb_all)
        lines_wf = [
            LineGather(
                p,
                wf_own.at[pl.ds(cuts[i], cuts[i + 1] - cuts[i])],
                lambda k, i=i: wf_alls[i].at[:, k],
                layers,
                *line_refs[6 + 2 * i : 8 + 2 * i],
            )
            for i in range(2)
        ]
        p.greet(True, layers)
        line_kv.start()
        line_wo.start()

        def split(ref, out, send, recv):
            copies = []
            for step in range(1, PLANE):
                to = p.plane_peer(step)
                copies.append(
                    push(
                        column_block(ref, to),
                        out.at[p.me],
                        send.at[step],
                        recv.at[step],
                        {"seq": to},
                    )
                )
                copies[-1].start()
            return copies

        split_q = split(wq_ref, wq_own, qsend, qrecv)
        split_f = split(wf_ref, wf_own, fsend, frecv)
        late.wait()

        @pl.loop(0, own_rows // 32)
        def _(i):
            here = rows_at(i * 32, 32)
            values = tok_ref[here, :].astype(f32)
            mean, inverse = norm_stats(values)
            h_buf[rows_at(p.me * own_rows + i * 32, 32), :] = (
                (values - mean) * inverse * gain_ref[...] + shift_ref[...]
            ).astype(bf16)
            mean_out[here, :] = mean
            inverse_out[here, :] = inverse

        early = [
            load(mean_out, mean_hbm, out_sem.at[0]),
            load(inverse_out, inverse_hbm, out_sem.at[1]),
        ]
        g = Gather(p, h_buf, own_rows, hs, hr)
        g.start(h_buf.at[rows_at(p.me * own_rows, own_rows), :])
        for copy in own:
            copy.put()
        line_kv.poll()
        for copy in (*my_pieces, my_kv):
            copy.wait()
        for copy in split_q:
            copy.wait_recv()
        line_wq.start()
        stores = [load(wq_own, wq_buf.at[:, p.layer], local.at[5])]
        line_kv.poll()
        line_wo.poll()
        line_kv.finish()
        kv_rows = layers * piece_rows
        stores.append(load(low_kv, kv_full.at[rows_at(p.me * kv_rows, kv_rows), :], local.at[6]))
        gkv = Gather(p, kv_full, kv_rows, ks, kr)
        gkv.start(low_kv)
        line_wq.poll()
        for copy in split_f:
            copy.wait_recv()
        stores.append(load(wf_own, wf_out, local.at[7]))
        for i in range(2):
            here = pl.ds(cuts[i], cuts[i + 1] - cuts[i])
            stores.append(load(wf_own.at[here], wf_alls[i].at[:, p.layer], local.at[8 + i]))
        line_wo.poll()
        line_wq.poll()
        for line in lines_wf:
            line.start()
        g.relay_first()
        g.relay_rest()
        gkv.relay()
        gc = Gather(p, cot_all, own_rows, cs, cr)
        gc.start(cot_ref)
        lines_wf[0].poll()
        line_wq.finish()
        line_wo.finish()
        for copy in stores[:2]:
            copy.wait()
        stores.append(load(wq_buf, wq_all, local.at[10]))

        def project(dev, k):
            here = g.pair(dev)
            stores.append(load(h_buf.at[here, :], h_all.at[here, :], local.at[11 + k]))
            q = dot(h_buf[here, :], wq_buf[...].reshape(depth, cols))
            q = q + bq_ref[:, rows_at(p.me * cols, cols)]
            chip = rows_at(lax.div(dev, 2) * 2, 2)
            q_buf[chip] = q.astype(bf16).reshape(2, streams, rows, cols)

        g.have(p.sib)
        project(p.me, 0)
        g.have(p.xs)
        project(p.xn, 1)
        g.have(p.ys)
        project(p.yn, 2)
        lines_wf[1].poll()
        g.relay_corner()
        g.have(p.ds)
        project(p.dg, 3)
        stores.append(load(q_buf, q_out, local.at[15]))
        gkv.relay_corner()
        for dev in (p.sib, p.xs, p.ys, p.ds):
            gkv.have(dev)
        stores.append(load(kv_full, kv_all, local.at[16]))
        for k in range(4):
            kv = dot(h_buf[pl.ds(k * total // 4, total // 4), :], kv_full[...])
            kv = jnp.concatenate([kv[:, :HD], kv[:, HD:] + bv_ref[...]], axis=1)
            kv_buf[pl.ds(2 * k, 2)] = kv.astype(bf16).reshape(2, streams, rows, kv_cols)
        stores.append(load(kv_buf, k_out, local.at[17]))
        lines_wf[0].poll()
        for stream in range(streams):
            attend_stream(
                docs_ref,
                stream,
                q_buf.at[:, stream],
                kv_buf.at[:, stream],
                mixed_buf.at[:, stream],
                lse_ref.at[stream],
                block,
                heads,
            )
            if stream == 0:
                gc.relay_first()
                lines_wf[1].poll()
        stores.append(load(mixed_buf, mixed_out, local.at[18]))
        early.append(load(lse_ref, lse_hbm, out_sem.at[2]))
        gc.relay_rest()
        gc.relay_corner()
        for dev in (p.sib, p.xs, p.ys, p.ds):
            gc.have(dev)
        for item in (g, gkv, gc, *lines_wf):
            item.finish()
        for copy in (*split_q, *split_f):
            copy.wait_send()
        for copy in (*own, *stores[2:], *early):
            copy.wait()

    q_shape = (PLANE, streams, rows, cols)
    kv_shape = (PLANE, streams, rows, kv_cols)
    wq_shape = (PLANE, layers, piece_rows, cols)
    wf_shape = (PLANE, piece_rows, hidden)
    half = [(cuts[i + 1] - cuts[i], layers, piece_rows, hidden) for i in range(2)]
    return pl.pallas_call(
        kernel,
        out_shape=[
            jax.ShapeDtypeStruct((total, depth), bf16),
            jax.ShapeDtypeStruct((depth, kv_cols), bf16),
            jax.ShapeDtypeStruct((total, cot.shape[1]), bf16),
            jax.ShapeDtypeStruct(q_shape, bf16),
            jax.ShapeDtypeStruct(kv_shape, bf16),
            jax.ShapeDtypeStruct(q_shape, bf16),
            jax.ShapeDtypeStruct(wq_shape, bf16),
            jax.ShapeDtypeStruct((layers * wo_rows, w_out.shape[1]), bf16),
            jax.ShapeDtypeStruct(wf_shape, bf16),
            jax.ShapeDtypeStruct(half[0], bf16),
            jax.ShapeDtypeStruct(half[1], bf16),
            jax.ShapeDtypeStruct((streams, heads, length), f32),
            jax.ShapeDtypeStruct((own_rows, 1), f32),
            jax.ShapeDtypeStruct((own_rows, 1), f32),
        ],
        in_specs=[pl.BlockSpec(memory_space=pltpu.SMEM)] + [ANY] * 10,
        out_specs=[ANY] * 14,
        scratch_shapes=[
            pltpu.VMEM((total, depth), bf16),
            pltpu.VMEM((layers * piece_rows, kv_cols), bf16),
            pltpu.VMEM((depth, kv_cols), bf16),
            pltpu.VMEM((PLANE, piece_rows, cols), bf16),
            pltpu.VMEM(wq_shape, bf16),
            pltpu.VMEM(wf_shape, bf16),
            pltpu.VMEM(w_out.shape, bf16),
            pltpu.VMEM(cot.shape, bf16),
            pltpu.VMEM(q_shape, bf16),
            pltpu.VMEM(kv_shape, bf16),
            pltpu.VMEM(q_shape, bf16),
        ]
        + Gather.scratch() * 3
        + LineGather.scratch(layers) * 5
        + [sems(PLANE)] * 4
        + [sems(19)]
        + [pltpu.VMEM((streams, heads, length), f32)]
        + [pltpu.VMEM((own_rows, 1), f32)] * 2
        + [sems(3)]
        + Late.scratch(tokens, gain, shift, bq, bv),
        compiler_params=params(number),
        cost_estimate=cost(2 * total * depth * (cols + kv_cols)),
        name="front",
    )(docs, tokens, gain, shift, bq, bv, w_query, w_fc, w_kv, w_out, cot)


def load_parts(parts, dst, local):
    copies, at = [], 0
    for i, part in enumerate(parts):
        rows = part.shape[0]
        copies.append(load(part, dst.at[pl.ds(at, rows), :], local.at[i]))
        at += rows
    return copies


def load_blocks(parts, dst, local):
    copies, at = [], 0
    for layer in range(parts[0].shape[0]):
        for part in parts:
            rows = part.shape[1]
            copies.append(load(part.at[layer], dst.at[pl.ds(at, rows), :], local.at[len(copies)]))
            at += rows
    return copies


def middle(
    mixed, wo, tokens, b_out, gain, shift, wf, piece, bf, cot_all, w_proj, layers, number
):
    total, depth = mixed.shape
    rows = total // PLANE
    wide = wo.shape[1]
    n_wf = len(wf)
    piece, first, last = piece
    piece_rows, hidden = piece.shape[1:]
    w_shape = (piece.shape[0], layers, piece_rows, hidden)
    out_wide = cot_all.shape[1]
    half, proj_half = rows // 2, w_proj.shape[0] // 2
    tiles, tile = 4, hidden // 4

    def kernel(mixed_ref, wo_ref, piece_ref, proj_ref, cot_ref, *refs):
        wf_refs, refs = refs[:n_wf], refs[n_wf:]
        late, refs = Late(refs[:5], refs[-6:]), refs[:-6]
        tok_ref, bias_ref, gain_ref, shift_ref, bf_ref = late.refs
        (mean_out, inverse_out, out_sem), refs = refs[-3:], refs[:-3]
        residual, all_ref, act_ref, slope_ref, dw_ref, piece_all, proj_all = refs[5:12]
        mean_hbm, inverse_hbm = refs[12:14]
        a_buf, wo_buf, proj_room, buf, w_buf, act, slope, cot, dw = refs[14:23]
        s, line_refs, residual_refs = refs[23:37], refs[37:43], refs[43:45]
        send, recv, local, store_sem = refs[45:]
        residual = Rows(residual, *residual_refs)
        acc = s[1]
        p = Place()
        piece_ref = piece_ref.at[pl.ds(first, last - first)]
        w_rest = w_buf.at[pl.ds(first, last - first)]
        loads = [load(mixed_ref, a_buf, local.at[0]), load(wo_ref, wo_buf, local.at[1])]
        own = Through(proj_ref, proj_room, proj_all.at[p.layer], local.at[2])
        loads_w, at = [load(piece_ref, w_rest.at[:, p.layer], local.at[3])], 0
        for i, ref in enumerate(wf_refs):
            loads_w.append(load(ref, w_buf.at[pl.ds(at, ref.shape[0])], local.at[4 + i]))
            at += ref.shape[0]
        line_fc = LineGather(p, piece_ref, lambda k: w_rest.at[:, k], layers, *line_refs[:2])
        lines_proj = [
            LineGather(
                p,
                proj_ref.at[pl.ds(i * proj_half, proj_half), :],
                lambda k, i=i: proj_all.at[k, pl.ds(i * proj_half, proj_half), :],
                layers,
                *line_refs[2 + 2 * i : 4 + 2 * i],
            )
            for i in range(2)
        ]
        p.greet(False, layers)
        line_fc.start()
        g = Gather(p, buf, rows, send, recv, 2)
        cots, stores = {}, []

        def fetch(k, dev):
            cots[k] = load(cot_ref.at[g.pair(dev), :], cot.at[k % 2], local.at[4 + n_wf + k % 2])

        def keep(src, dst):
            stores.append(load(src, dst, store_sem.at[len(stores)]))

        fetch(0, p.me)
        fetch(1, p.xn)
        for copy in loads:
            copy.wait()
        my_rows = [g.piece(p.me, k) for k in range(4)]

        def emit(line, value):
            values = tok_ref[line, :].astype(f32) + value + bias_ref[...]
            mean, inverse = norm_stats(values)
            residual.put(line, values)
            buf[rows_at(p.me * rows + line.start, line.size), :] = (
                (values - mean) * inverse * gain_ref[...] + shift_ref[...]
            ).astype(bf16)
            mean_out[line, :] = mean
            inverse_out[line, :] = inverse
            done = line.start + line.size - half
            if done > 0 and done % g.size == 0:
                g.start_piece(done // g.size - 1, my_rows)

        def poll_fc():
            line_fc.poll()
            if line_fc.step == 1:
                own.put()
            lines_proj[line_fc.step - 1].start()

        def idle():
            late.wait()
            lines_proj[0].poll()

        Scatter.take(p, rows, s).run(
            plain_product(a_buf, wo_buf), emit, idle, (poll_fc, None, poll_fc)
        )
        g.start_rest(my_rows)
        early = [
            load(mean_out, mean_hbm, out_sem.at[0]),
            load(inverse_out, inverse_hbm, out_sem.at[1]),
        ]

        def work(dev):
            block = g.pair(dev)
            keep(buf.at[block, :], all_ref.at[block, :])

            @pl.loop(0, hidden // 512)
            def _(j):
                cols = rows_at(j * 512, 512)
                value = dot(buf[block, :], w_buf[:, :, :, cols].reshape(wide, 512))
                value = value + bf_ref[:, rows_at(p.me * hidden + j * 512, 512)]
                activated, gradient = gelu_pair(value)
                act[block, cols] = activated.astype(bf16)
                slope[block, cols] = gradient.astype(bf16)

            keep(act.at[block, :], act_ref.at[block, :])
            keep(slope.at[block, :], slope_ref.at[block, :])

        def grads(k, dev):
            block = g.pair(dev)
            cots[k].wait()
            for j in range(tiles):
                cols = pl.ds(j * tile, tile)
                term = dot_tn(act[block, cols], cot[k % 2])
                if k == 0:
                    acc[j] = term
                elif k < 3:
                    acc[j] += term
                else:
                    dw[j] = (acc[j] + term).astype(bf16)
                    keep(dw.at[j], dw_ref.at[cols, :])

        lines_proj[1].poll()
        line_fc.finish()
        for copy in loads_w:
            copy.wait()
        keep(w_rest, piece_all)
        g.have(p.sib)
        work(p.me)
        grads(0, p.me)
        fetch(2, p.yn)
        g.relay_first()
        lines_proj[0].poll()
        g.relay_rest()
        g.have(p.xs)
        work(p.xn)
        g.have(p.ys)
        work(p.yn)
        lines_proj[1].poll()
        grads(1, p.xn)
        fetch(3, p.dg)
        g.relay_corner()
        grads(2, p.yn)
        g.have(p.ds)
        work(p.dg)
        grads(3, p.dg)
        g.finish()
        for line in lines_proj:
            line.finish()
        own.wait()
        residual.finish()
        for copy in (*stores, *early):
            copy.wait()

    return pl.pallas_call(
        kernel,
        out_shape=[
            jax.ShapeDtypeStruct((rows, wide), f32),
            jax.ShapeDtypeStruct((total, wide), bf16),
            jax.ShapeDtypeStruct((total, hidden), bf16),
            jax.ShapeDtypeStruct((total, hidden), bf16),
            jax.ShapeDtypeStruct((hidden, out_wide), bf16),
            jax.ShapeDtypeStruct((last - first, *w_shape[1:]), bf16),
            jax.ShapeDtypeStruct((layers, *w_proj.shape), bf16),
            jax.ShapeDtypeStruct((rows, 1), f32),
            jax.ShapeDtypeStruct((rows, 1), f32),
        ],
        in_specs=[ANY] * (10 + n_wf),
        out_specs=[ANY] * 9,
        scratch_shapes=[
            pltpu.VMEM(mixed.shape, bf16),
            pltpu.VMEM(wo.shape, bf16),
            pltpu.VMEM(w_proj.shape, bf16),
            pltpu.VMEM((total, wide), bf16),
            pltpu.VMEM(w_shape, bf16),
            pltpu.VMEM((total, hidden), bf16),
            pltpu.VMEM((total, hidden), bf16),
            pltpu.VMEM((2, 2 * rows, out_wide), bf16),
            pltpu.VMEM((tiles, tile, out_wide), bf16),
        ]
        + Scatter.scratch(rows, wide)
        + LineGather.scratch(layers) * 3
        + Rows.scratch(rows, wide, f32)
        + Gather.scratch(2)
        + [sems(6 + n_wf), sems(13 + tiles)]
        + [pltpu.VMEM((rows, 1), f32)] * 2
        + [sems(2)]
        + Late.scratch(tokens, b_out, gain, shift, bf),
        compiler_params=params(number),
        cost_estimate=cost(4 * total * wide * hidden),
        name="middle",
    )(mixed, wo, piece, w_proj, cot_all, *wf, tokens, b_out, gain, shift, bf)


def gather_out(
    grad_attn, wo, mixed, hidden2, grad_pre, first_fc, grad_proj, proj_done, fc_part, layers, number
):
    rows, depth = grad_attn.shape
    wide = wo.shape[0]
    total = PLANE * rows
    hidden = grad_pre.shape[1]
    tile = 512
    steps = (depth - first_fc) // tile
    proj_cut = proj_done.shape[0]
    proj_shape = (grad_proj.shape[1] - proj_cut, grad_proj.shape[2])
    fc_shape = (fc_part.shape[0], *fc_part.shape[2:])

    def kernel(own_ref, w_ref, mixed_ref, h_ref, gp_ref, proj_ref, fc_ref, *refs):
        late, refs = Late(refs[:1], refs[-2:]), refs[1:-2]
        (done_ref,) = late.refs
        (proj_out, fc_out, out_sem), refs = refs[-3:], refs[:-3]
        gm_ref, dw_ref, dwfc_ref, proj_hbm, fc_hbm = refs[:5]
        buf, w_buf, mixed_buf, gm, acc, dw, gp, h_buf, dwfc = refs[5:14]
        send, recv = refs[14:16]
        line_refs = refs[16:32]
        (local,) = refs[32:]
        p = Place()
        load_own = load(own_ref, buf.at[rows_at(p.me * rows, rows), :], local.at[0])
        loads = [load(w_ref, w_buf, local.at[1]), load(mixed_ref, mixed_buf, local.at[2])]
        load_gp = load(gp_ref, gp, local.at[3])
        proj = LineSum(p, lambda f: proj_ref.at[f, pl.ds(proj_cut, proj_shape[0]), :], layers, *line_refs[:8])
        fc = LineSum(p, lambda f: fc_ref.at[:, f], layers, *line_refs[8:])

        def h_fetch(i):
            here = pl.ds(first_fc + i * tile, tile)
            return load(h_ref.at[:, here], h_buf.at[i % 2], local.at[4 + i % 2])

        tiles = [h_fetch(0)]
        stores = []
        p.greet(False, layers)
        g = Gather(p, buf, rows, send, recv)
        g.start(own_ref)
        LineSum.start(proj, fc)

        def work(dev):
            block = g.pair(dev)
            gm[block, :] = dot_nt(buf[block, :], w_buf[...]).astype(bf16)

        def grads(k, dev):
            block = g.pair(dev)
            term = dot_tn(mixed_buf[block, :], buf[block, :])
            if k == 0:
                acc[...] = term
            elif k < 3:
                acc[...] += term
            else:
                dw[...] = (acc[...] + term).astype(bf16)

        def fc_grads(i):
            tiles[i].wait()
            if i + 1 < steps:
                tiles.append(h_fetch(i + 1))
            if i >= 2:
                stores[i - 2].wait()
            dwfc[i % 2] = dot_tn(h_buf[i % 2], gp[...]).astype(bf16)
            stores.append(
                load(dwfc.at[i % 2], dwfc_ref.at[pl.ds(i * tile, tile), :], local.at[6 + i % 2])
            )

        load_own.wait()
        for copy in loads:
            copy.wait()
        g.have(p.sib)
        work(p.me)
        grads(0, p.me)
        late.wait()
        for i in range(0, proj_cut, 32):
            proj_out[pl.ds(i, 32), :] = done_ref[pl.ds(i, 32), :].astype(f32)
        before, rest = pl.ds(0, proj_cut), pl.ds(proj_cut, proj_shape[0])
        early = [load(proj_out.at[before, :], proj_hbm.at[before, :], out_sem.at[0])]
        load_gp.wait()
        fc_grads(0)
        proj.poll()
        g.relay_first()
        fc_grads(1)
        fc.poll()
        for i in range(2, steps):
            fc_grads(i)
        proj.poll()
        g.relay_rest()
        fc.poll()
        g.have(p.xs)
        work(p.xn)
        g.have(p.ys)
        work(p.yn)
        grads(1, p.xn)
        g.relay_corner()
        grads(2, p.yn)
        g.have(p.ds)
        work(p.dg)
        store = load(gm, gm_ref, local.at[8])
        grads(3, p.dg)
        store_dw = load(dw, dw_ref, local.at[9])
        g.finish()

        def keep_proj(where, value):
            proj_out[pl.ds(proj_cut + where.start, where.size), :] = value

        def keep_fc(where, value):
            fc_out[where] = value.astype(bf16)

        proj.finish(keep_proj)
        early.append(load(proj_out.at[rest, :], proj_hbm.at[rest, :], out_sem.at[1]))
        fc.finish(keep_fc)
        early.append(load(fc_out, fc_hbm, out_sem.at[2]))
        for copy in early:
            copy.wait()
        store.wait()
        store_dw.wait()
        for copy in stores[-2:]:
            copy.wait()

    return pl.pallas_call(
        kernel,
        out_shape=[
            jax.ShapeDtypeStruct((total, wide), bf16),
            jax.ShapeDtypeStruct((wide, depth), bf16),
            jax.ShapeDtypeStruct((depth - first_fc, hidden), bf16),
            jax.ShapeDtypeStruct(grad_proj.shape[1:], f32),
            jax.ShapeDtypeStruct(fc_shape, bf16),
        ],
        in_specs=[ANY] * 8,
        out_specs=[ANY] * 5,
        scratch_shapes=[
            pltpu.VMEM((total, depth), bf16),
            pltpu.VMEM(wo.shape, bf16),
            pltpu.VMEM(mixed.shape, bf16),
            pltpu.VMEM((total, wide), bf16),
            pltpu.VMEM((wide, depth), f32),
            pltpu.VMEM((wide, depth), bf16),
            pltpu.VMEM(grad_pre.shape, bf16),
            pltpu.VMEM((2, total, tile), bf16),
            pltpu.VMEM((2, tile, hidden), bf16),
        ]
        + Gather.scratch()
        + LineSum.scratch(proj_shape, layers)
        + LineSum.scratch(fc_shape, layers)
        + [sems(10)]
        + [pltpu.VMEM(grad_proj.shape[1:], f32), pltpu.VMEM(fc_shape, bf16), sems(3)]
        + Late.scratch(proj_done),
        compiler_params=params(number),
        cost_estimate=cost(4 * total * depth * wide),
        name="gather_out",
    )(grad_attn, wo, mixed, hidden2, grad_pre, grad_proj, fc_part, proj_done)


def plain_product(a_buf, w_buf):
    half = w_buf.shape[1] // 2

    def product(role, here, c):
        return dot(a_buf[here, :], w_buf[:, pl.ds(c * half, half)])

    return product


def scatter_fc(cot_all, slope, wp, wf, hidden2, back, grad_proj, proj_cut, layers, number):
    total, depth = cot_all.shape
    rows = total // PLANE
    wide = slope.shape[1]
    tile = 512
    n_wp, n_wf = len(wp), len(wf)
    proj_shape = (proj_cut, grad_proj.shape[2])
    cuts = (0, proj_cut // 64 * 32, proj_cut)

    def kernel(cot_ref, slope_ref, h_ref, proj_ref, *refs):
        wp_refs, wf_refs, refs = refs[:n_wp], refs[n_wp : n_wp + n_wf], refs[n_wp + n_wf :]
        late, refs = Late(refs[:5], refs[-6:]), refs[:-6]
        cot_own, residual_ref, mean_ref, inverse_ref, gain_ref = late.refs
        grad_residual, grad_attn, sums_ref, bias_ref, gp_ref, dw_ref, proj_out = refs[5:12]
        cot, slopes, wp_buf, wf_buf, gp, h_buf, dw_buf, folds = refs[12:20]
        s, line_refs = refs[20:34], refs[34:50]
        local, wlocal = refs[50:52]
        grad_residual, grad_attn = Rows(grad_residual, *refs[52:54]), Rows(grad_attn, *refs[54:56])
        p = Place()
        proj = [
            LineSum(
                p,
                lambda f, i=i: proj_ref.at[f, pl.ds(cuts[i], cuts[i + 1] - cuts[i]), :],
                layers,
                *line_refs[8 * i : 8 * i + 8],
            )
            for i in range(2)
        ]
        order = (p.dg, p.xn, p.yn, p.me)

        def chip(dev):
            return rows_at(lax.div(dev, 2) * (2 * rows), 2 * rows)

        def fetch(k):
            here = chip(order[k])
            return (
                load(cot_ref.at[here, :], cot.at[k % 2], local.at[k % 2]),
                load(slope_ref.at[here, :], slopes.at[k % 2], local.at[2 + k % 2]),
            )

        fetches = [fetch(0)]
        loads_wp = load_blocks(wp_refs, wp_buf, wlocal)
        loads_wf = load_parts(wf_refs, wf_buf, local.at[pl.ds(4, n_wf)])
        load_h = load(h_ref.at[:, pl.ds(0, tile)], h_buf, local.at[4 + n_wf])
        bias_ref[...] = jnp.zeros_like(bias_ref)
        p.greet(False, layers)
        LineSum.start(*proj)
        for copy in loads_wp:
            copy.wait()
        half = depth // 2

        def back_through_gelu(k):
            for copy in fetches[k]:
                copy.wait()
            if k < 3:
                fetches.append(fetch(k + 1))
            here = chip(order[k])

            @pl.loop(0, wide // 512)
            def _(j):
                cols = rows_at(j * 512, 512)
                grad_act = dot_nt(cot[k % 2], wp_buf[cols, :])
                grad_pre = (grad_act * slopes[k % 2, :, cols].astype(f32)).astype(bf16)
                gp[here, cols] = grad_pre
                bias_ref[:, cols] += jnp.sum(grad_pre.astype(f32), axis=0, keepdims=True)

            if k == 0:
                for copy in loads_wf:
                    copy.wait()

        def product(role, here, c):
            if c == 0:
                back_through_gelu(role)
            return dot_nt(gp[here, :], wf_buf[pl.ds(c * half, half), :])

        def emit(line, value):
            first = line.start == 0
            grad_out = cot_own[line, :].astype(f32)
            back = inverse_ref[line, :]
            normed = (residual_ref[line, :] - mean_ref[line, :]) * back
            result = grad_out + norm_back(value, normed, back, gain_ref[...])
            low = result.astype(bf16)
            grad_residual.put(line, result)
            grad_attn.put(line, low)
            for i, term in enumerate((value * normed, value, low.astype(f32), grad_out)):
                fold(folds.at[i], first, term)

        stores = []

        def last_poll():
            stores.append(load(gp, gp_ref, local.at[5 + n_wf]))
            proj[0].poll()

        def idle():
            late.wait()
            load_h.wait()
            dw_buf[...] = dot_tn(h_buf[...], gp[...]).astype(bf16)
            stores.append(load(dw_buf, dw_ref, local.at[6 + n_wf]))
            proj[1].poll()

        Scatter.take(p, rows, s).run(
            product, emit, idle, (proj[0].poll, proj[1].poll, last_poll)
        )
        sums_ref[...] = jnp.sum(folds[...], axis=1)
        for i in range(2):

            def keep(where, value, i=i):
                proj_out[pl.ds(cuts[i] + where.start, where.size), :] = value.astype(bf16)

            proj[i].finish(keep)
        for copy in stores:
            copy.wait()
        grad_residual.finish()
        grad_attn.finish()

    return pl.pallas_call(
        kernel,
        out_shape=[
            jax.ShapeDtypeStruct((rows, depth), f32),
            jax.ShapeDtypeStruct((rows, depth), bf16),
            jax.ShapeDtypeStruct((4, depth), f32),
            jax.ShapeDtypeStruct((1, wide), f32),
            jax.ShapeDtypeStruct((total, wide), bf16),
            jax.ShapeDtypeStruct((tile, wide), bf16),
            jax.ShapeDtypeStruct(proj_shape, bf16),
        ],
        in_specs=[ANY] * (9 + n_wp + n_wf),
        out_specs=[ANY] * 2 + [WHOLE] * 2 + [ANY] * 2 + [WHOLE],
        scratch_shapes=[
            pltpu.VMEM((2, 2 * rows, depth), bf16),
            pltpu.VMEM((2, 2 * rows, wide), bf16),
            pltpu.VMEM((wide, depth), bf16),
            pltpu.VMEM((depth, wide), bf16),
            pltpu.VMEM((total, wide), bf16),
            pltpu.VMEM((total, tile), bf16),
            pltpu.VMEM((tile, wide), bf16),
            pltpu.VMEM((4, 8, depth), f32),
        ]
        + Scatter.scratch(rows, depth)
        + LineSum.scratch((cuts[1], depth), layers)
        + LineSum.scratch((proj_cut - cuts[1], depth), layers)
        + [sems(7 + n_wf), sems(n_wp * layers)]
        + Rows.scratch(rows, depth, f32)
        + Rows.scratch(rows, depth, bf16)
        + Late.scratch(*back),
        compiler_params=params(number),
        cost_estimate=cost(6 * total * depth * wide),
        name="scatter_fc",
    )(cot_all, slope, hidden2, grad_proj, *wp, *wf, *back)


LANES = 128


def scatter_query(
    gq, gkv, wq, w_kv, grad_w_query, grad_w_kv, fc_done, fc_part, back, sums, layers, number
):
    total, cols = gq.shape
    kv_cols = gkv.shape[1]
    rows = total // PLANE
    depth = wq.shape[0]
    wide = depth + kv_cols
    q_shape = (grad_w_query.shape[0], *grad_w_query.shape[2:])
    fc_part, first, last = fc_part
    fc_shape = (last - first, *fc_part.shape[2:])
    my_hidden = sums[1].shape[1]
    places, lines_total = {}, 0
    for name, size in (
        ("ln1_gain", depth),
        ("ln1_bias", depth),
        ("b_query", PLANE * cols),
        ("b_value", kv_cols // 2),
        ("b_out", depth),
        ("ln2_gain", depth),
        ("ln2_bias", depth),
        ("b_fc", PLANE * my_hidden),
        ("b_proj", depth),
    ):
        places[name] = lines_total
        lines_total += size // LANES
    padded = -(-lines_total // (8 * PLANE)) * 8
    n_done = len(fc_done)
    done_cut = sum(a.shape[0] for a in fc_done)
    fc_rows, fc_cols = fc_shape[1:]
    kv_rows = rows // layers

    def kernel(gq_ref, gkv_ref, wq_ref, wkv_ref, dwq_ref, dwkv_ref, fc_ref, *refs):
        late, refs = Late(refs[:9], refs[-10:]), refs[:-10]
        tok_ref, mean_ref, inverse_ref, gain_ref, residual_ref = late.refs[:5]
        sums2_ref, sums_fc_ref, sums_q_ref, sums_kv_ref = late.refs[5:]
        done_refs, refs = refs[9 : 9 + n_done], refs[9 + n_done :]
        out_ref, vec_out, dwkv_out, fc_out, dwq_out = refs[:5]
        g_buf, wq_buf, wkv_buf, dwkv_buf, q_sum, folds = refs[5:11]
        vec, box, zbox, plane_sum, pieces, dwkv, kv_box = refs[11:18]
        s, line_refs = refs[18:32], refs[32:48]
        qsend, qrecv, local = refs[48:51]
        result = Rows(out_ref, *refs[51:53])
        vsend, vrecv, zsend, zrecv, gsend, grecv, fsend, frecv, ksend, krecv, flocal = refs[53:]
        p = Place()
        at, done_loads = 0, []
        for i, ref in enumerate(done_refs):
            done_loads.append(load(ref, pieces.at[pl.ds(at, ref.shape[0])], flocal.at[i]))
            at += ref.shape[0]

        def pack(at, row):
            for k in range(row.shape[1] // LANES):
                line = at + k
                vec[lax.div(line, padded), pl.ds(lax.rem(line, padded), 1), :] = row[
                    :, k * LANES : (k + 1) * LANES
                ]

        fc_spot = fc_out.at[:, rows_at(p.me * fc_cols, fc_cols)]

        def fc_copy(step):
            to = p.plane_peer(step)
            return push(pieces.at[to], fc_spot, fsend.at[step], frecv.at[step], {"seq": to})

        def spread_fc():
            for step in range(1, PLANE):
                fc_copy(step).start()

        q_side, kv_side = pl.ds(0, cols), pl.ds(cols, kv_cols)
        loads = [
            load(gq_ref, g_buf.at[:, q_side], local.at[0]),
            load(gkv_ref, g_buf.at[:, kv_side], local.at[1]),
            load(wq_ref, wq_buf, local.at[2]),
            load(wkv_ref, wkv_buf, local.at[3]),
            load(dwkv_ref, dwkv_buf, local.at[4]),
        ]
        line_q = LineSum(p, lambda f: dwq_ref.at[:, f], layers, *line_refs[:8])
        line_fc = LineSum(p, lambda f: fc_ref.at[pl.ds(first, last - first), f], layers, *line_refs[8:])
        p.greet(True, layers)
        LineSum.start(line_q, line_fc)
        for copy in loads:
            copy.wait()
        half = wide // 2

        def product(role, here, c):
            where = pl.ds(c * half, min(half, depth - c * half))
            value = dot_nt(g_buf[here, q_side], wq_buf[where, :]) + dot_nt(
                g_buf[here, kv_side], wkv_buf[where, :]
            )
            if c == 0:
                return value
            return jnp.concatenate([value, dwkv_buf[here, :].astype(f32)], axis=1)

        later = []

        def idle():
            def keep(where, value):
                q_sum[where] = value.astype(bf16)

            for copy in done_loads:
                copy.wait()
            late.wait()
            vec[...] = jnp.zeros_like(vec)
            for i, name in enumerate(("ln2_gain", "ln2_bias", "b_out", "b_proj")):
                pack(places[name], sums2_ref[i : i + 1, :])
            pack(places["b_fc"] + p.me * (my_hidden // LANES), sums_fc_ref[...])
            pack(places["b_query"] + p.me * (cols // LANES), sums_q_ref[...])
            pack(places["b_value"], sums_kv_ref[:, kv_cols // 2 :])
            line_fc.poll()
            line_q.finish(keep)
            later.append(Spread(p, q_sum, dwq_out, qsend, qrecv, local.at[5]))

        def emit(line, value):
            begin = line.start == 0
            grad = value[:, :depth]
            normed = (tok_ref[line, :].astype(f32) - mean_ref[line, :]) * inverse_ref[line, :]
            result.put(
                line,
                residual_ref[line, :]
                + norm_back(grad, normed, inverse_ref[line, :], gain_ref[...]),
            )
            fold(folds.at[0], begin, grad * normed)
            fold(folds.at[1], begin, grad)
            dwkv[line, :] = value[:, depth:].astype(bf16)

        def keep_fc(where, value):
            pieces[done_cut + where] = value.astype(bf16)

        polls = (line_q.poll, line_fc.poll, line_q.poll)
        Scatter.take(p, rows, s).run(product, emit, idle, polls)
        for i, name in enumerate(("ln1_gain", "ln1_bias")):
            pack(places[name], jnp.sum(folds[i], axis=0, keepdims=True))
        plane = PlaneSum(p, vec, box, vsend, vrecv)
        across = []

        def kv_block(layer):
            return dwkv.at[rows_at(layer * kv_rows, kv_rows), :]

        for step in range(1, layers):
            to = p.line_peer(step, layers)
            across.append(
                push(kv_block(to), kv_box.at[step], ksend.at[step], krecv.at[step], {"fsdp": to})
            )
            across[-1].start()
        line_fc.finish(keep_fc)
        spread_fc()
        my_fc = load(pieces.at[p.me], fc_spot, flocal.at[n_done])
        total_vec = plane.total()
        plane_sum[...] = total_vec
        zbox[0] = total_vec
        for step in range(1, layers):
            to = p.line_peer(step, layers)
            across.append(
                push(plane_sum, zbox.at[step], zsend.at[step], zrecv.at[step], {"fsdp": to})
            )
            across[-1].start()
        for copy in across:
            copy.wait_recv()
        total_vec = None
        for k in range(layers):
            term = zbox[lax.rem(p.layer - k + layers, layers)]
            total_vec = term if total_vec is None else total_vec + term
        vec_out[p.me] = total_vec
        for step in range(1, PLANE):
            to = p.plane_peer(step)
            mine = vec_out.at[p.me]
            later.append(push(mine, mine, gsend.at[step], grecv.at[step], {"seq": to}))
            later[-1].start()
        value = dwkv[rows_at(p.layer * kv_rows, kv_rows), :].astype(f32)
        for step in range(1, layers):
            value = value + kv_box[step].astype(f32)
        dwkv_out[...] = value
        for item in (*later, result):
            item.finish() if hasattr(item, "finish") else item.wait()
        for step in range(1, PLANE):
            fc_copy(step).wait()
        my_fc.wait()
        plane.finish()
        for copy in across:
            copy.wait_send()

    return pl.pallas_call(
        kernel,
        out_shape=[
            jax.ShapeDtypeStruct((rows, depth), f32),
            jax.ShapeDtypeStruct((PLANE, padded, LANES), f32),
            jax.ShapeDtypeStruct((kv_rows, kv_cols), f32),
            jax.ShapeDtypeStruct((fc_rows, PLANE * fc_cols), bf16),
            jax.ShapeDtypeStruct((q_shape[1], PLANE * q_shape[2]), bf16),
        ],
        in_specs=[ANY] * (16 + n_done),
        out_specs=[ANY, WHOLE, WHOLE, ANY, ANY],
        scratch_shapes=[
            pltpu.VMEM((total, cols + kv_cols), bf16),
            pltpu.VMEM(wq.shape, bf16),
            pltpu.VMEM(w_kv.shape, bf16),
            pltpu.VMEM(grad_w_kv.shape, bf16),
            pltpu.VMEM(q_shape, bf16),
            pltpu.VMEM((2, 8, depth), f32),
            pltpu.VMEM((PLANE, padded, LANES), f32),
            pltpu.VMEM((PLANE, padded, LANES), f32),
            pltpu.VMEM((layers, padded, LANES), f32),
            pltpu.VMEM((padded, LANES), f32),
            pltpu.VMEM((PLANE, fc_rows, fc_cols), bf16),
            pltpu.VMEM((rows, kv_cols), bf16),
            pltpu.VMEM((layers, kv_rows, kv_cols), bf16),
        ]
        + Scatter.scratch(rows, wide)
        + LineSum.scratch(q_shape, layers)
        + LineSum.scratch(fc_shape, layers)
        + [sems(PLANE)] * 2
        + [sems(6)]
        + Rows.scratch(rows, depth, f32)
        + [sems(PLANE)] * 2
        + [sems(layers)] * 2
        + [sems(PLANE)] * 4
        + [sems(layers)] * 2
        + [sems(n_done + 1)]
        + Late.scratch(*back, *sums),
        compiler_params=params(number),
        cost_estimate=cost(2 * total * depth * (cols + kv_cols)),
        name="scatter_query",
    )(gq, gkv, wq, w_kv, grad_w_query, grad_w_kv, fc_part, *back, *sums, *fc_done)


def starts_of(docs, stream, positions):
    start = jnp.zeros_like(positions)
    for j in range(docs.shape[1]):
        here = docs[stream, j]
        start = jnp.maximum(start, jnp.where(here <= positions, here, 0))
    return start


def masked_scores(docs, stream, keys, q, first, limit):
    scores = dot_nt(keys, q) * (HD**-0.5)
    t = first + lax.broadcasted_iota(jnp.int32, (1, q.shape[0]), 1)
    u = lax.broadcasted_iota(jnp.int32, scores.shape, 0)
    return scores, (u >= starts_of(docs, stream, t)) & (u <= t)


QROWS = 256


def attend_stream(docs, stream, q_ref, kv_ref, mixed_ref, lse_ref, block, heads):
    groups, rows, cols = q_ref.shape
    length = groups * rows
    kv = kv_ref[...].reshape(length, 2 * HD)
    keys = kv[:, :HD]
    values_t = kv[:, HD:].T
    per = block // rows
    for b in range(length // block):
        limit = (b + 1) * block
        q_rows = q_ref[b * per : (b + 1) * per].reshape(block, cols)
        for h in range(heads):
            q = q_rows[:, h * HD : (h + 1) * HD]
            scores, allowed = masked_scores(docs, stream, keys[:limit], q, b * block, limit)
            scores = jnp.where(allowed, scores, -1e30)
            top = jnp.max(scores, axis=0, keepdims=True)
            weights = jnp.exp(scores - top)
            total = jnp.sum(weights, axis=0, keepdims=True)
            mixed = dot(values_t[:, :limit], weights.astype(bf16)) / total
            mixed_ref[b * per : (b + 1) * per, :, h * HD : (h + 1) * HD] = (
                mixed.T.astype(bf16).reshape(per, rows, HD)
            )
            lse_ref[h : h + 1, b * block : (b + 1) * block] = top + jnp.log(total)


def attend_stream_back(docs, stream, q_ref, kv_ref, g_ref, lse_ref, gq_ref, gkv_ref, gk, gv, heads):
    groups, rows, cols = q_ref.shape
    length = groups * rows
    block = min(QROWS, length)
    kv = kv_ref[...].reshape(length, 2 * HD)
    keys, values = kv[:, :HD], kv[:, HD:]
    keys_t = keys.T
    per = block // rows
    gk[...] = jnp.zeros_like(gk)
    gv[...] = jnp.zeros_like(gv)
    for b in range(length // block):
        limit = (b + 1) * block
        q_rows = q_ref[b * per : (b + 1) * per].reshape(block, cols)
        g_rows = g_ref[b * per : (b + 1) * per].reshape(block, cols)
        for h in range(heads):
            q = q_rows[:, h * HD : (h + 1) * HD]
            g = g_rows[:, h * HD : (h + 1) * HD]
            scores, allowed = masked_scores(docs, stream, keys[:limit], q, b * block, limit)
            shift = lse_ref[h : h + 1, b * block : (b + 1) * block]
            probs = jnp.where(allowed, jnp.exp(scores - shift), 0.0)
            grad_probs = dot_nt(values[:limit], g)
            weighted = probs * grad_probs
            delta = jnp.sum(weighted, axis=0, keepdims=True)
            grad_scores = (weighted - probs * delta).astype(bf16)
            gq = dot(keys_t[:, :limit], grad_scores) * (HD**-0.5)
            gq_ref[b * per : (b + 1) * per, :, h * HD : (h + 1) * HD] = (
                gq.T.astype(bf16).reshape(per, rows, HD)
            )
            gk[:limit, :] += dot(grad_scores, q)
            gv[:limit, :] += dot(probs.astype(bf16), g)
    gkv_ref[:, :, :HD] = (gk[...] * (HD**-0.5)).astype(bf16).reshape(groups, rows, HD)
    gkv_ref[:, :, HD:] = gv[...].astype(bf16).reshape(groups, rows, HD)


def attend_back_scatter_proj(
    docs, queries, keyval, grads, lse, act, wp, hidden1, out_part, fc_part, residual, b_proj,
    layers, heads, number
):
    groups, streams, rows, cols = queries.shape
    kv_cols = keyval.shape[3]
    length = groups * rows
    total, depth = act.shape
    own = total // PLANE
    wide = hidden1.shape[1]
    part = hidden1.shape[1] // PLANE
    n_wp = len(wp)
    out_shape = out_part.shape[1:]
    fc_part, first, last = fc_part
    fc_shape = (last - first, *fc_part.shape[2:])

    def kernel(docs_ref, q_ref, kv_ref, g_ref, lse_in, act_ref, h_ref, dwo_ref, fc_ref, *refs):
        wp_refs, refs = refs[:n_wp], refs[n_wp:]
        late, refs = Late((*refs[:2], lse_in), refs[-4:]), refs[:-4]
        residual_ref, bias_ref, lse_ref = late.refs
        gq_out, gkv_out, gq_sum, gkv_sum, dwq_out, dwkv_out = refs[2:8]
        out_ref, dwo_out, fc_out = refs[8:11]
        a_buf, w_buf, q_buf, kv_buf, g_buf, grad_buf, gk, gv, h_buf = refs[11:20]
        dwq_buf, dwkv_buf = refs[20:22]
        s, line_refs = refs[22:36], refs[36:52]
        local, wlocal = refs[52:54]
        result = Rows(out_ref, *refs[54:])
        p = Place()
        loads = [load(act_ref, a_buf, local.at[0]), *load_blocks(wp_refs, w_buf, wlocal)]
        line_o = LineSum(p, lambda f: dwo_ref.at[f], layers, *line_refs[:8])
        line_fc = LineSum(p, lambda f: fc_ref.at[pl.ds(first, last - first), f], layers, *line_refs[8:])
        ins = [
            load(q_ref, q_buf, local.at[2]),
            load(kv_ref, kv_buf, local.at[3]),
            load(g_ref, g_buf, local.at[4]),
        ]

        def h_fetch(i):
            here = pl.ds(2 * i * part, 2 * part)
            return load(h_ref.at[:, here], h_buf.at[i % 2], local.at[5 + i % 2])

        tiles = [h_fetch(0)]
        p.greet(False, layers)
        LineSum.start(line_o, line_fc)
        for copy in loads:
            copy.wait()
        stores = []

        def idle():
            late.wait()
            for copy in ins:
                copy.wait()
            for stream in range(streams):
                attend_stream_back(
                    docs_ref,
                    stream,
                    q_buf.at[:, stream],
                    kv_buf.at[:, stream],
                    g_buf.at[:, stream],
                    lse_ref.at[stream],
                    grad_buf.at[:, stream, :, pl.ds(0, cols)],
                    grad_buf.at[:, stream, :, pl.ds(cols, kv_cols)],
                    gk,
                    gv,
                    heads,
                )
                if stream == 0:
                    line_fc.poll()
            stores.append(load(grad_buf.at[:, :, :, pl.ds(0, cols)], gq_out, local.at[7]))
            stores.append(load(grad_buf.at[:, :, :, pl.ds(cols, kv_cols)], gkv_out, local.at[8]))
            grad = grad_buf[...].reshape(total, cols + kv_cols)
            sums = jnp.sum(grad.astype(f32), axis=0, keepdims=True)
            gq_sum[...] = sums[:, :cols]
            gkv_sum[...] = sums[:, cols:]
            for i in range(PLANE // 2):
                tiles[i].wait()
                if i + 1 < PLANE // 2:
                    tiles.append(h_fetch(i + 1))
                term = dot_tn(h_buf[i % 2], grad).astype(bf16)
                for k in range(2):
                    lines = term[k * part : (k + 1) * part]
                    dwq_buf[2 * i + k] = lines[:, :cols].reshape(layers, part // layers, cols)
                    dwkv_buf[2 * i + k] = lines[:, cols:]
            stores.append(load(dwq_buf, dwq_out, local.at[9]))
            stores.append(load(dwkv_buf, dwkv_out, local.at[10]))

        def emit(line, value):
            result.put(line, residual_ref[line, :] + value + bias_ref[...])

        def keep_out(where, value):
            dwo_out[where, :] = value

        def keep_fc(where, value):
            fc_out[where] = value.astype(bf16)

        polls = (line_o.poll, line_fc.poll, line_o.poll)
        Scatter.take(p, own, s).run(plain_product(a_buf, w_buf), emit, idle, polls)
        line_o.finish(keep_out)
        line_fc.finish(keep_fc)
        for copy in stores:
            copy.wait()
        result.finish()

    return pl.pallas_call(
        kernel,
        out_shape=[
            jax.ShapeDtypeStruct(queries.shape, bf16),
            jax.ShapeDtypeStruct(keyval.shape, bf16),
            jax.ShapeDtypeStruct((1, cols), f32),
            jax.ShapeDtypeStruct((1, kv_cols), f32),
            jax.ShapeDtypeStruct((PLANE, layers, part // layers, cols), bf16),
            jax.ShapeDtypeStruct((PLANE, part, kv_cols), bf16),
            jax.ShapeDtypeStruct((own, wide), f32),
            jax.ShapeDtypeStruct(out_shape, f32),
            jax.ShapeDtypeStruct(fc_shape, bf16),
        ],
        in_specs=[pl.BlockSpec(memory_space=pltpu.SMEM)] + [ANY] * (10 + n_wp),
        out_specs=[ANY, ANY, WHOLE, WHOLE, ANY, ANY, ANY] + [WHOLE] * 2,
        scratch_shapes=[
            pltpu.VMEM(act.shape, bf16),
            pltpu.VMEM((depth, wide), bf16),
            pltpu.VMEM(queries.shape, bf16),
            pltpu.VMEM(keyval.shape, bf16),
            pltpu.VMEM(grads.shape, bf16),
            pltpu.VMEM((groups, streams, rows, cols + kv_cols), bf16),
            pltpu.VMEM((length, HD), f32),
            pltpu.VMEM((length, HD), f32),
            pltpu.VMEM((2, total, 2 * part), bf16),
            pltpu.VMEM((PLANE, layers, part // layers, cols), bf16),
            pltpu.VMEM((PLANE, part, kv_cols), bf16),
        ]
        + Scatter.scratch(own, wide)
        + LineSum.scratch(out_shape, layers)
        + LineSum.scratch(fc_shape, layers)
        + [sems(11), sems(n_wp * layers)]
        + Rows.scratch(own, wide, f32)
        + Late.scratch(residual, b_proj, lse),
        compiler_params=params(number),
        cost_estimate=cost(2 * total * depth * wide),
        name="attend_back_scatter_proj",
    )(docs, queries, keyval, grads, lse, act, hidden1, out_part, fc_part, *wp, residual, b_proj)


def finish(copied, cast, packed, vectors):
    n_copy, n_cast, n_vec = len(copied), len(cast), len(vectors)
    count = n_copy + n_cast

    def kernel(*refs):
        ins, packed_ref, refs = refs[:count], refs[count], refs[count + 1 :]
        outs, refs = refs[: count + n_vec], refs[count + n_vec :]
        rooms, wide, parts = refs[:count], refs[count : count + n_cast], refs[count + n_cast : -2]
        load_sem, store_sem = refs[-2:]
        loads = [load(src, room, load_sem.at[i]) for i, (src, room) in enumerate(zip(ins, rooms))]
        stores = []

        def store(src, dst):
            stores.append(load(src, dst, store_sem.at[len(stores)]))

        at = 0
        for part, out in zip(parts, outs[count:]):
            for k in range(part.shape[1] // LANES):
                part[:, k * LANES : (k + 1) * LANES] = packed_ref[at : at + 1, :]
                at += 1
            store(part, out)
        for i in range(n_copy):
            loads[i].wait()
            store(rooms[i], outs[i])
        for i in range(n_cast):
            loads[n_copy + i].wait()
            wide[i][...] = rooms[n_copy + i][...].astype(f32)
            store(wide[i], outs[n_copy + i])
        for copy in stores:
            copy.wait()

    shapes = [(a.shape, a.dtype) for a in copied] + [(a.shape, f32) for a in cast]
    shapes += [((1, size), f32) for size in vectors]
    return pl.pallas_call(
        kernel,
        out_shape=[jax.ShapeDtypeStruct(*shape) for shape in shapes],
        in_specs=[ANY] * count + [WHOLE],
        out_specs=[ANY] * (count + n_vec),
        scratch_shapes=[pltpu.VMEM(a.shape, a.dtype) for a in (*copied, *cast)]
        + [pltpu.VMEM(a.shape, f32) for a in cast]
        + [pltpu.VMEM((1, size), f32) for size in vectors]
        + [sems(count), sems(count + n_vec)],
        compiler_params=pltpu.CompilerParams(vmem_limit_bytes=VMEM_LIMIT),
        name="finish",
    )(*copied, *cast, packed)


def shards(
    tokens,
    doc_starts,
    w_query,
    w_kv,
    w_out,
    w_fc,
    w_proj,
    ln1_gain,
    ln1_bias,
    b_query,
    b_value,
    b_out,
    ln2_gain,
    ln2_bias,
    b_fc,
    b_proj,
    cotangent,
):
    layers = lax.axis_size("fsdp")
    streams, rows, width = tokens.shape
    own = streams * rows
    heads = HEADS // PLANE
    hidden = b_fc.shape[0]
    my_cols = heads * HD
    my_hidden = hidden // PLANE
    total = PLANE * own

    own_tokens = tokens.reshape(own, width)
    cot_low = cotangent.reshape(own, width)

    def row(vector):
        return vector.reshape(1, -1)

    fc_cut = PLANE * 6 // 8
    proj_rows = w_proj.shape[0]
    proj_cut = proj_rows * 5 // 8

    def rows_together(pieces):
        return pieces.reshape(-1, pieces.shape[-1])

    (
        hidden1,
        w_kv_all,
        cot_all,
        queries,
        keyval,
        mixed,
        wq,
        wo,
        wf_pieces,
        wf_a,
        wf_b,
        lse,
        mean1,
        inverse1,
    ) = front(
        doc_starts,
        own_tokens,
        row(ln1_gain),
        row(ln1_bias),
        w_query,
        w_fc,
        w_kv,
        w_out,
        cot_low,
        row(b_query),
        row(b_value),
        fc_cut,
        streams,
        heads,
        layers,
        1,
    )
    wq = rows_together(wq)
    mixed_rows = mixed.reshape(total, my_cols)
    residual, hidden2, act_low, slope, grad_w_proj, wf_c, wp, mean2, inverse2 = middle(
        mixed_rows,
        wo,
        own_tokens,
        row(b_out),
        row(ln2_gain),
        row(ln2_bias),
        (wf_a, wf_b),
        (wf_pieces, fc_cut, PLANE),
        row(b_fc),
        cot_all,
        w_proj,
        layers,
        2,
    )
    wf = [rows_together(w) for w in (wf_a, wf_b, wf_c)]
    wp = (wp,)
    grad_w_proj = grad_w_proj.reshape(layers, proj_rows, width)
    grad_residual, grad_attn, sums2, my_grad_b_fc, grad_pre, grad_fc_a, shard_proj_a = scatter_fc(
        cot_all,
        slope,
        wp,
        wf,
        hidden2,
        (cot_low, residual, mean2, inverse2, row(ln2_gain)),
        grad_w_proj,
        proj_cut,
        layers,
        6,
    )

    def by_layer(grad):
        return grad.reshape(-1, layers, width // PLANE // layers, my_hidden)

    first_fc = grad_fc_a.shape[0]
    grad_mixed, grad_w_out, grad_fc_rest, shard_proj, fc_a = gather_out(
        grad_attn,
        wo,
        mixed_rows,
        hidden2,
        grad_pre,
        first_fc,
        grad_w_proj,
        shard_proj_a,
        by_layer(grad_fc_a),
        layers,
        7,
    )
    grad_fc_rest = by_layer(grad_fc_rest)
    rest_cut = grad_fc_rest.shape[0] // 2
    (
        gq,
        gkv,
        my_grad_b_query,
        sums_kv,
        grad_w_query,
        grad_w_kv,
        output,
        shard_out,
        fc_b,
    ) = attend_back_scatter_proj(
        doc_starts,
        queries,
        keyval,
        grad_mixed.reshape(PLANE, streams, rows, my_cols),
        lse,
        act_low,
        wp,
        hidden1,
        grad_w_out.reshape(layers, -1, width),
        (grad_fc_rest, 0, rest_cut),
        residual,
        row(b_proj),
        layers,
        heads,
        8,
    )
    input_grad, packed, shard_kv, shard_fc, shard_query = scatter_query(
        gq.reshape(total, my_cols),
        gkv.reshape(total, 2 * HD),
        wq,
        w_kv_all,
        grad_w_query,
        grad_w_kv.reshape(width, 2 * HD),
        (fc_a, fc_b),
        (grad_fc_rest, rest_cut, grad_fc_rest.shape[0]),
        (own_tokens, mean1, inverse1, row(ln1_gain), grad_residual),
        (sums2, my_grad_b_fc, my_grad_b_query, sums_kv),
        layers,
        9,
    )
    vectors = (ln1_gain, ln1_bias, b_query, b_value, b_out, ln2_gain, ln2_bias, b_fc, b_proj)
    output, input_grad, shard_kv, shard_out, shard_proj, shard_query, shard_fc, *sums = finish(
        (output, input_grad, shard_kv, shard_out, shard_proj),
        (shard_query, shard_fc),
        packed.reshape(-1, LANES),
        [v.shape[0] for v in vectors],
    )
    return (
        output.reshape(streams, rows, width),
        input_grad.reshape(streams, rows, width),
        shard_query,
        shard_kv,
        shard_out,
        shard_fc,
        shard_proj,
        *[v.reshape(-1) for v in sums],
    )


def gather_seq(block):
    return lax.all_gather(block, "seq", axis=0, tiled=True)


def scatter_seq(partial):
    return lax.psum_scatter(partial.astype(bf16), "seq", scatter_dimension=0, tiled=True).astype(f32)


def columns_to_rows(part, groups):
    rows = part.shape[0]
    spread = part.reshape(rows, groups, part.shape[1] // groups).transpose(1, 0, 2)
    return lax.all_to_all(spread, "seq", split_axis=0, concat_axis=0, tiled=True)


def column_weight(shard, groups):
    pieces = columns_to_rows(shard, groups)
    full = lax.all_gather(pieces, "fsdp", axis=1, tiled=True)
    return full.reshape(-1, full.shape[2])


def plain_column_grad(grad, groups):
    rows, cols = grad.shape
    kept = lax.psum_scatter(
        grad.astype(bf16).reshape(groups, rows // groups, cols), "fsdp", scatter_dimension=1, tiled=True
    )
    moved = lax.all_to_all(kept, "seq", split_axis=0, concat_axis=0, tiled=True)
    return moved.transpose(1, 0, 2).reshape(moved.shape[1], groups * cols).astype(f32)


def row_weight_grad(grad):
    return lax.psum_scatter(grad.astype(bf16), "fsdp", scatter_dimension=0, tiled=True).astype(f32)


def plain_attend(queries, keyval, starts, groups, streams, rows, heads):
    length = groups * rows
    scale = HD ** (-0.5)
    position = jnp.arange(length, dtype=jnp.int32)
    mixed_list, lse_list = [], []
    for stream in range(streams):
        q = queries[:, stream].reshape(length, heads, HD)
        k = keyval[:, stream, :, :HD].reshape(length, HD)
        v = keyval[:, stream, :, HD:].reshape(length, HD)
        segment = jnp.sum((starts[stream][None, :] <= position[:, None]).astype(jnp.int32), axis=1)
        allowed = (position[None, :] <= position[:, None]) & (segment[None, :] == segment[:, None])
        scores = jnp.einsum("thd,ud->htu", q, k, preferred_element_type=f32) * scale
        scores = jnp.where(allowed[None], scores, -1e30)
        top = jnp.max(scores, axis=-1, keepdims=True)
        lse = top + jnp.log(jnp.sum(jnp.exp(scores - top), axis=-1, keepdims=True))
        probs = jnp.exp(scores - lse).astype(bf16)
        mixed = jnp.einsum("htu,ud->thd", probs, v, preferred_element_type=f32)
        mixed_list.append(mixed.astype(bf16).reshape(groups, rows, heads * HD))
        lse_list.append(lse)
    return jnp.stack(mixed_list, axis=1), lse_list


def plain_attend_back(queries, keyval, grads, lse_list, starts, groups, streams, rows, heads):
    length = groups * rows
    scale = HD ** (-0.5)
    position = jnp.arange(length, dtype=jnp.int32)
    gq_list, gkv_list = [], []
    for stream in range(streams):
        q = queries[:, stream].reshape(length, heads, HD)
        g = grads[:, stream].reshape(length, heads, HD)
        k = keyval[:, stream, :, :HD].reshape(length, HD)
        v = keyval[:, stream, :, HD:].reshape(length, HD)
        segment = jnp.sum((starts[stream][None, :] <= position[:, None]).astype(jnp.int32), axis=1)
        allowed = (position[None, :] <= position[:, None]) & (segment[None, :] == segment[:, None])
        scores = jnp.einsum("thd,ud->htu", q, k, preferred_element_type=f32) * scale
        probs = jnp.exp(jnp.where(allowed[None], scores, -1e30) - lse_list[stream])
        grad_probs = jnp.einsum("thd,ud->htu", g, v, preferred_element_type=f32)
        delta = jnp.sum(probs * grad_probs, axis=-1, keepdims=True)
        gs = (probs * (grad_probs - delta)).astype(bf16)
        gq = jnp.einsum("htu,ud->thd", gs, k, preferred_element_type=f32) * scale
        gk = jnp.einsum("htu,thd->ud", gs, q, preferred_element_type=f32) * scale
        gv = jnp.einsum("htu,thd->ud", probs.astype(bf16), g, preferred_element_type=f32)
        gq_list.append(gq.astype(bf16).reshape(groups, rows, heads * HD))
        gkv_list.append(jnp.concatenate([gk, gv], axis=1).reshape(groups, rows, 2 * HD))
    return jnp.stack(gq_list, axis=1), jnp.stack(gkv_list, axis=1)


def plain_shards(
    tokens,
    doc_starts,
    w_query,
    w_kv,
    w_out,
    w_fc,
    w_proj,
    ln1_gain,
    ln1_bias,
    b_query,
    b_value,
    b_out,
    ln2_gain,
    ln2_bias,
    b_fc,
    b_proj,
    cotangent,
):
    groups = lax.axis_size("seq")
    me = lax.axis_index("seq")
    streams, rows, width = tokens.shape
    own = streams * rows
    heads = HEADS // groups
    hidden = b_fc.shape[0]
    my_cols = heads * HD
    my_hidden = hidden // groups

    wq = column_weight(w_query, groups)
    w_kv_all = gather_seq(lax.all_gather(w_kv, "fsdp", axis=0, tiled=True))
    wo = lax.all_gather(w_out, "fsdp", axis=0, tiled=True)
    wf = column_weight(w_fc, groups)
    wp = lax.all_gather(w_proj, "fsdp", axis=0, tiled=True)
    my_bq = lax.dynamic_slice_in_dim(b_query, me * my_cols, my_cols, 0)
    my_bf = lax.dynamic_slice_in_dim(b_fc, me * my_hidden, my_hidden, 0)

    inputs = tokens.reshape(own, width).astype(f32)
    cot_low = cotangent.reshape(own, width)
    cot_full = cot_low.astype(f32)
    shifted1, normed1, inverse1 = normalize(inputs, ln1_gain, ln1_bias)
    hidden1 = gather_seq(shifted1.astype(bf16))
    queries = (dot(hidden1, wq) + my_bq).astype(bf16).reshape(groups, streams, rows, my_cols)
    value_shift = jnp.concatenate([jnp.zeros((HD,), f32), b_value])
    keyval = (dot(hidden1, w_kv_all) + value_shift).astype(bf16).reshape(groups, streams, rows, 2 * HD)
    mixed, lse = plain_attend(queries, keyval, doc_starts, groups, streams, rows, heads)
    mixed_rows = mixed.reshape(groups * own, my_cols)
    residual = inputs + scatter_seq(dot(mixed_rows, wo)) + b_out
    shifted2, normed2, inverse2 = normalize(residual, ln2_gain, ln2_bias)
    hidden2 = gather_seq(shifted2.astype(bf16))
    cot_all = gather_seq(cot_low)
    pre_act = dot(hidden2, wf) + my_bf
    activated, slope = gelu_pair(pre_act)
    act_low = activated.astype(bf16)
    output = residual + scatter_seq(dot(act_low, wp)) + b_proj

    grad_b_proj = jnp.sum(cot_full, axis=0)
    shard_proj = row_weight_grad(dot_tn(act_low, cot_all))
    grad_pre = (dot_nt(cot_all, wp) * slope).astype(bf16)
    my_grad_b_fc = jnp.sum(grad_pre.astype(f32), axis=0)
    shard_fc = plain_column_grad(dot_tn(hidden2, grad_pre), groups)
    grad_hidden2 = scatter_seq(dot_nt(grad_pre, wf))
    back_second, grad_ln2_gain, grad_ln2_bias = normalize_back(
        grad_hidden2, normed2, inverse2, ln2_gain
    )
    grad_residual = cot_full + back_second
    grad_attn = grad_residual.astype(bf16)
    grad_b_out = jnp.sum(grad_attn.astype(f32), axis=0)
    grad_attn_all = gather_seq(grad_attn)
    shard_out = row_weight_grad(dot_tn(mixed_rows, grad_attn_all))
    grad_mixed = dot_nt(grad_attn_all, wo).astype(bf16).reshape(groups, streams, rows, my_cols)
    gq, gkv = plain_attend_back(
        queries, keyval, grad_mixed, lse, doc_starts, groups, streams, rows, heads
    )
    gq_rows = gq.reshape(groups * own, my_cols)
    gkv_rows = gkv.reshape(groups * own, 2 * HD)
    my_grad_b_query = jnp.sum(gq_rows.astype(f32), axis=0)
    grad_b_value = jnp.sum(gkv_rows[:, HD:], axis=0)
    gkv_low = gkv_rows.astype(bf16)
    shard_query = plain_column_grad(dot_tn(hidden1, gq_rows), groups)
    shard_kv = row_weight_grad(scatter_seq(dot_tn(hidden1, gkv_low)))
    grad_hidden1 = scatter_seq(dot_nt(gq_rows, wq) + dot_nt(gkv_low, w_kv_all))
    back_first, grad_ln1_gain, grad_ln1_bias = normalize_back(
        grad_hidden1, normed1, inverse1, ln1_gain
    )
    input_grad = grad_residual + back_first

    zero = jnp.zeros_like
    grad_b_query = lax.dynamic_update_slice_in_dim(zero(b_query), my_grad_b_query, me * my_cols, 0)
    grad_b_fc = lax.dynamic_update_slice_in_dim(zero(b_fc), my_grad_b_fc, me * my_hidden, 0)
    vectors = (
        grad_ln1_gain,
        grad_ln1_bias,
        grad_b_query,
        grad_b_value,
        grad_b_out,
        grad_ln2_gain,
        grad_ln2_bias,
        grad_b_fc,
        grad_b_proj,
    )
    sums = lax.psum(vectors, ("seq", "fsdp"))
    return (
        output.reshape(streams, rows, width),
        input_grad.reshape(streams, rows, width),
        shard_query,
        shard_kv,
        shard_out,
        shard_fc,
        shard_proj,
        *sums,
    )


def solution(mesh):
    acts = P("fsdp", "seq", None)
    weight = P(("seq", "fsdp"), None)
    return jax.shard_map(
        shards if mesh.shape["seq"] == PLANE else plain_shards,
        mesh=mesh,
        in_specs=(acts, P("fsdp", None)) + (weight,) * 5 + (P(),) * 9 + (acts,),
        out_specs=(acts, acts) + (weight,) * 5 + (P(),) * 9,
        check_vma=False,
    )
```
